32 devices in a mesh: dp: 8 (over z, x), tensor: 4 (over y, core).
Axes of the slice: x: 2, y: 2, z: 4, core: 2. Of those that a mesh axis runs over, the one named last changes fastest.
Arguments:
- tokens: bfloat16 [4096, 2048], P('dp'), may hold values from -6 to 6
- segments: int32 [8, 512], P('dp'), may hold values from 0 to 2, as said below
- positions: int32 [8, 512], P('dp'), may hold values from 0 to 1789, as said below
- attn_gain: float32 [2048], replicated, may hold values from 0.5 to 1.5
- w_query: bfloat16 [2048, 2048], P(None, 'tensor'), may hold values from -0.125 to 0.125
- key_weight: bfloat16 [2048, 512], P(None, 'tensor'), may hold values from -0.125 to 0.125
- value_weight: bfloat16 [2048, 512], P(None, 'tensor'), may hold values from -0.125 to 0.125
- w_out: bfloat16 [2048, 2048], P('tensor'), may hold values from -1 to 1
- mlp_gain: float32 [2048], replicated, may hold values from 0.5 to 1.5
- w_gate: bfloat16 [2048, 8192], P(None, 'tensor'), may hold values from -0.125 to 0.125
- w_up: bfloat16 [2048, 8192], P(None, 'tensor'), may hold values from -0.125 to 0.125
- w_down: bfloat16 [8192, 2048], P('tensor'), may hold values from -0.0625 to 0.0625
- cotangent: bfloat16 [4096, 2048], P('dp'), may hold values from -6 to 6
Outputs:
- mixed: bfloat16 [4096, 2048], P('dp')
- grad_input: float32 [4096, 2048], P('dp')
- grad_attn_gain: float32 [2048], P('dp')
- grad_w_query: float32 [2048, 2048], P('dp', 'tensor')
- grad_w_key: float32 [2048, 512], P('dp', 'tensor')
- grad_w_value: float32 [2048, 512], P('dp', 'tensor')
- grad_w_out: float32 [2048, 2048], P('tensor', 'dp')
- grad_mlp_gain: float32 [2048], P('dp')
- grad_w_gate: float32 [2048, 8192], P('dp', 'tensor')
- grad_w_up: float32 [2048, 8192], P('dp', 'tensor')
- grad_w_down: float32 [8192, 2048], P('tensor', 'dp')
The draws below stay inside these ranges and needn't reach their ends.
Inputs may be any that keep to these rules, and one draw needn't show every extreme that they name: `segments`: within each sequence the segment numbers start at 0, never fall, and every sequence holds three documents. positions count up by one inside each document; the second and third documents of a sequence start at 0, the first may start higher.
All inputs are finite; a program needn't handle non-finite values.
Results may differ from the reference program's by a relative error of at most 0.014.
Values sent between devices are 32-bit elements; how exact they have to be, the bound alone decides.
A program may use at most 256 MiB of HBM per device.

```python
import jax
import jax.numpy as jnp
from jax import lax

MODEL_WIDTH = 2048
QUERY_HEAD_COUNT = 32
KEY_VALUE_HEADS = 8
HEAD_SIZE = 64
FF = 8192
PACKED_LENGTH = 512
SEQUENCE_TOTAL = 8
TOKENS = 4096


def document_cuts(key):
    early_key, late_key, pick_key = jax.random.split(key, 3)
    first_cut = jax.random.randint(early_key, (SEQUENCE_TOTAL, 1), PACKED_LENGTH // 8, PACKED_LENGTH // 2)
    second_cut = jax.random.randint(late_key, (SEQUENCE_TOTAL, 1), PACKED_LENGTH // 2 + PACKED_LENGTH // 16, PACKED_LENGTH - PACKED_LENGTH // 16)
    chosen = jax.random.randint(pick_key, (), 0, SEQUENCE_TOTAL)
    picked = jnp.arange(SEQUENCE_TOTAL, dtype=jnp.int32)[:, None] == chosen
    first_cut = jnp.where(picked, PACKED_LENGTH // 2 - 1, first_cut)
    return (first_cut, second_cut, picked)


def draw_segments(key, part):
    first_cut, second_cut, picked = document_cuts(key)
    places = jnp.arange(PACKED_LENGTH, dtype=jnp.int32)[None, :]
    return (places >= first_cut).astype(jnp.int32) + (places >= second_cut).astype(jnp.int32)


def draw_positions(key, part):
    first_cut, second_cut, picked = document_cuts(key)
    key = jax.random.fold_in(key, 12)
    offset = jax.random.randint(key, (SEQUENCE_TOTAL, 1), 0, 1536)
    offset = jnp.where(picked, 1535, offset)
    places = jnp.arange(PACKED_LENGTH, dtype=jnp.int32)[None, :]
    later = jnp.where(places < second_cut, places - first_cut, places - second_cut)
    return jnp.where(places < first_cut, places + offset, later).astype(jnp.int32)


def with_spikes(entries, key, source, target, blocks, factor):
    owner, partner = [(jnp.arange(entries.shape[position]) // (entries.shape[position] // blocks)).reshape([-1 if axis == position else 1 for axis in range(entries.ndim)]) for position in (source, target)]
    chosen = jax.random.permutation(key, blocks)[partner]
    strong = (owner == chosen) | (owner == (partner + blocks // 2) % blocks)
    return jnp.where(strong, factor * entries, entries)


def block_levels(rng, extent, cuts, least, high):
    loudness = 1.0
    for position, parts in cuts:
        heights = jax.random.uniform(jax.random.fold_in(jax.random.fold_in(rng, 6), position), (parts,), jnp.float32, least / len(cuts), high / len(cuts))
        loudness = loudness * jnp.repeat(jnp.exp(heights), extent[position] // parts).reshape((-1,) + (1,) * (len(extent) - 1 - position))
    return loudness


def scatter_about(key, dims, deviation, limit, pieces=(), held_as=jnp.bfloat16):
    factor_of = block_levels(key, dims, pieces, -0.22, 0.18) if pieces else 1.0
    drawn = jax.random.normal(key, dims, jnp.float32) * deviation * factor_of
    return jnp.minimum(jnp.maximum(drawn, -limit), limit).astype(held_as)


def bell_draw_with(stream_key, dims, spread, bound, cuts, heavy, kind=jnp.bfloat16):
    result = spread * jax.random.normal(stream_key, dims, jnp.float32)
    if cuts:
        result = result * block_levels(stream_key, dims, cuts, -0.22, 0.18)
    return jnp.clip(with_spikes(result, jax.random.fold_in(stream_key, 3), *heavy), -bound, bound).astype(kind)


def setup_inputs(seed: int = 0) -> dict:
    key_of = jax.random.split(jax.random.key(seed), 14)
    tokens = scatter_about(key_of[0], (TOKENS, MODEL_WIDTH), 1.0, 6.0, ((0, 8),))
    segments = draw_segments(jax.random.fold_in(key_of[13], 71), 0)
    positions = draw_positions(jax.random.fold_in(key_of[13], 71), 0)
    attn_gain = jnp.clip(1.0 + 0.1 * jax.random.normal(key_of[3], (MODEL_WIDTH,), jnp.float32), 0.5, 1.5)
    w_query = scatter_about(key_of[4], (MODEL_WIDTH, QUERY_HEAD_COUNT * HEAD_SIZE), MODEL_WIDTH ** -0.5, 0.125, ((1, 4),))
    key_weight = scatter_about(key_of[5], (MODEL_WIDTH, KEY_VALUE_HEADS * HEAD_SIZE), MODEL_WIDTH ** -0.5, 0.125, ((1, 4),))
    value_weight = scatter_about(key_of[6], (MODEL_WIDTH, KEY_VALUE_HEADS * HEAD_SIZE), MODEL_WIDTH ** -0.5, 0.125, ((1, 4),))
    w_out = scatter_about(key_of[7], (QUERY_HEAD_COUNT * HEAD_SIZE, MODEL_WIDTH), (max(QUERY_HEAD_COUNT * HEAD_SIZE // 64, 1)) ** -0.5, 1.0, ((0, 4),))
    mlp_gain = jnp.clip(1.0 + 0.1 * jax.random.normal(key_of[8], (MODEL_WIDTH,), jnp.float32), 0.5, 1.5)
    w_gate = scatter_about(key_of[9], (MODEL_WIDTH, FF), MODEL_WIDTH ** -0.5, 0.125, ((1, 4),))
    w_up = scatter_about(key_of[10], (MODEL_WIDTH, FF), MODEL_WIDTH ** -0.5, 0.125, ((1, 4),))
    w_down = scatter_about(key_of[11], (FF, MODEL_WIDTH), FF ** -0.5, 0.0625, ((0, 4),))
    cotangent = bell_draw_with(key_of[12], (TOKENS, MODEL_WIDTH), 1.0, 6.0, ((0, 8),), (0, 1, 8, 2.0))
    return dict(tokens=tokens, segments=segments, positions=positions, attn_gain=attn_gain, w_query=w_query, key_weight=key_weight, value_weight=value_weight, w_out=w_out, mlp_gain=mlp_gain, w_gate=w_gate, w_up=w_up, w_down=w_down, cotangent=cotangent)


@jax.custom_vjp
def lower_precision(v):
    return lax.optimization_barrier(v.astype(jnp.bfloat16)).astype(jnp.float32)

@jax.custom_vjp
def low_back(v):
    return v

def low_keep(v):
    return (lower_precision(v), None)

def low_pass(kept, grad):
    return (grad,)

def back_keep(v):
    return (v, None)

def back_low(kept, grad):
    return (lower_precision(grad),)
lower_precision.defvjp(low_keep, low_pass)
low_back.defvjp(back_keep, back_low)

def highest(left_matrix, right_matrix):
    return jnp.dot(left_matrix, right_matrix, precision=lax.Precision.HIGHEST, preferred_element_type=jnp.float32)

def norm_rows(values, gain):
    return values * lax.rsqrt(lax.optimization_barrier(jnp.mean(values * values, axis=-1, keepdims=True)) + 1e-05) * gain

def tables(places):
    half_dim = HEAD_SIZE // 2
    frequency = 500000.0 ** (-(jnp.arange(half_dim).astype(jnp.float32) * 2.0 / HEAD_SIZE))
    angles = places.astype(jnp.float32)[..., None] * frequency
    cosine_lookup = jnp.cos(angles)
    sine_lookup = jnp.sin(angles)
    return (jnp.concatenate([cosine_lookup, cosine_lookup], -1), jnp.concatenate([sine_lookup, sine_lookup], -1))

def apply_rotary(field, cosine_lookup, sine_lookup):
    half_dim = HEAD_SIZE // 2
    turned = jnp.concatenate([-field[..., half_dim:], field[..., :half_dim]], -1)
    return field * cosine_lookup + turned * sine_lookup

def attend_heads(block_args):
    query_projected, key_projected, value_projected, segment, places = block_args
    cosine_lookup, sine_lookup = tables(places)
    cosine_lookup = cosine_lookup[:, None, :]
    sine_lookup = sine_lookup[:, None, :]
    query_rotated = lower_precision(apply_rotary(query_projected.reshape(PACKED_LENGTH, QUERY_HEAD_COUNT, HEAD_SIZE), cosine_lookup, sine_lookup))
    query_rotated = query_rotated.reshape(PACKED_LENGTH, KEY_VALUE_HEADS, QUERY_HEAD_COUNT // KEY_VALUE_HEADS, HEAD_SIZE)
    key_rotated = lower_precision(apply_rotary(key_projected.reshape(PACKED_LENGTH, KEY_VALUE_HEADS, HEAD_SIZE), cosine_lookup, sine_lookup))
    raw_scores = jnp.einsum('qhgd,khd->hgqk', query_rotated, key_rotated, precision=lax.Precision.HIGHEST) * HEAD_SIZE ** (-0.5)
    raw_scores = low_back(raw_scores)
    spots = jnp.arange(PACKED_LENGTH)
    allowed = (spots[:, None] >= spots[None, :]) & (segment[:, None] == segment[None, :])
    masked = jnp.where(allowed, raw_scores, -1e+30)
    log_total = jax.nn.logsumexp(masked, axis=-1, keepdims=True)
    attention_probs = lower_precision(jnp.exp(masked - log_total))
    combined_heads = jnp.einsum('ojus,sov->uojv', attention_probs, value_projected.reshape(PACKED_LENGTH, KEY_VALUE_HEADS, HEAD_SIZE), precision=lax.Precision.HIGHEST)
    return combined_heads.reshape(PACKED_LENGTH, QUERY_HEAD_COUNT * HEAD_SIZE)

def reference(tokens, segments, positions, attn_gain, w_query, key_weight, value_weight, w_out, mlp_gain, w_gate, w_up, w_down, cotangent):

    def forward(inputs, gain_one, query_w, key_w, value_w, out_w, gain_two, gate_w, up_w, down_w):
        normed_one = lower_precision(norm_rows(inputs, gain_one))
        query_projected = low_back(highest(normed_one, query_w))
        key_projected = low_back(highest(normed_one, key_w))
        value_projected = lower_precision(low_back(highest(normed_one, value_w)))
        head_outputs = lax.map(jax.checkpoint(attend_heads), (query_projected.reshape(SEQUENCE_TOTAL, PACKED_LENGTH, QUERY_HEAD_COUNT * HEAD_SIZE), key_projected.reshape(SEQUENCE_TOTAL, PACKED_LENGTH, KEY_VALUE_HEADS * HEAD_SIZE), value_projected.reshape(SEQUENCE_TOTAL, PACKED_LENGTH, KEY_VALUE_HEADS * HEAD_SIZE), segments, positions))
        head_outputs = lower_precision(low_back(head_outputs.reshape(TOKENS, QUERY_HEAD_COUNT * HEAD_SIZE)))
        hidden = inputs + low_back(highest(head_outputs, out_w))
        normed_two = lower_precision(norm_rows(hidden, gain_two))
        gate_proj = low_back(highest(normed_two, gate_w))
        up_proj = low_back(highest(normed_two, up_w))
        activation = lower_precision(jax.nn.silu(gate_proj) * up_proj)
        return hidden + low_back(highest(activation, down_w))
    mixed, pull = jax.vjp(forward, tokens.astype(jnp.float32), attn_gain.astype(jnp.float32), w_query.astype(jnp.float32), key_weight.astype(jnp.float32), value_weight.astype(jnp.float32), w_out.astype(jnp.float32), mlp_gain.astype(jnp.float32), w_gate.astype(jnp.float32), w_up.astype(jnp.float32), w_down.astype(jnp.float32))
    grads = pull(cotangent.astype(jnp.float32))
    return (mixed.astype(jnp.bfloat16), grads[0], grads[1], grads[2], grads[3], grads[4], grads[5], grads[6], grads[7], grads[8], grads[9])
```

```python
import jax
import jax.numpy as jnp
from jax import lax
from jax.sharding import PartitionSpec as P

HEAD_SIZE = 64
EPSILON = 1e-05
MASKED = -1e30
F32 = jnp.float32
BF16 = jnp.bfloat16


def product(left_matrix, right_matrix):
    return jnp.dot(left_matrix, right_matrix, preferred_element_type=F32)


def over_rows(left_matrix, right_matrix):
    return lax.dot_general(
        left_matrix, right_matrix, (((0,), (0,)), ((), ())), preferred_element_type=F32
    )


def against(gradient, weight):
    return lax.dot_general(
        gradient, weight, (((1,), (1,)), ((), ())), preferred_element_type=F32
    )


def narrowed(value):
    return jnp.where(value == value, value, 0.0).astype(BF16)


def swap(value, axis, bit):
    size = lax.axis_size(axis)
    return lax.ppermute(value, axis, [(i, i ^ bit) for i in range(size)])


def half_of(value, which, dim=0):
    size = value.shape[dim] // 2
    return lax.dynamic_slice_in_dim(value, which * size, size, dim)


def joined(mine, other, which):
    first = jnp.where(which == 0, mine, other)
    second = jnp.where(which == 0, other, mine)
    return jnp.concatenate([first, second], axis=0)


def tensor_sum_half(partial, core):
    total = half_of(partial, core) + swap(half_of(partial, 1 - core), "tensor", 1)
    bit = 2
    while bit < lax.axis_size("tensor"):
        total = total + swap(total, "tensor", bit)
        bit *= 2
    return total


def tables(places):
    half_dim = HEAD_SIZE // 2
    frequency = 500000.0 ** (-(jnp.arange(half_dim).astype(F32) * 2.0 / HEAD_SIZE))
    angles = places.astype(F32)[..., None] * frequency
    cosine_lookup = jnp.cos(angles)
    sine_lookup = jnp.sin(angles)
    return (
        jnp.concatenate([cosine_lookup, cosine_lookup], -1),
        jnp.concatenate([sine_lookup, sine_lookup], -1),
    )


def apply_rotary(field, cosine_lookup, sine_lookup):
    half_dim = HEAD_SIZE // 2
    turned = jnp.concatenate([-field[..., half_dim:], field[..., :half_dim]], -1)
    return field * cosine_lookup + turned * sine_lookup


def unrotate(gradient, cosine_lookup, sine_lookup):
    half_dim = HEAD_SIZE // 2
    sined = gradient * sine_lookup
    return gradient * cosine_lookup + jnp.concatenate(
        [sined[..., half_dim:], -sined[..., :half_dim]], -1
    )


def allowed_pairs(segment):
    spots = jnp.arange(segment.shape[0])
    return (spots[:, None] >= spots[None, :]) & (segment[:, None] == segment[None, :])


def scores(query_rotated, key_rotated, segment):
    raw_scores = jnp.einsum(
        "qhgd,khd->hgqk", query_rotated, key_rotated, preferred_element_type=F32
    ) * HEAD_SIZE ** (-0.5)
    return jnp.where(allowed_pairs(segment), raw_scores, MASKED)


def attend_forward(query_rotated, key_rotated, value_seq, segment):
    masked = scores(query_rotated, key_rotated, segment)
    row_peak = jnp.max(masked, axis=-1, keepdims=True)
    log_total = row_peak + jnp.log(jnp.sum(jnp.exp(masked - row_peak), axis=-1, keepdims=True))
    attention_probs = jnp.exp(masked - log_total).astype(BF16)
    combined_heads = jnp.einsum(
        "ojus,sov->uojv", attention_probs, value_seq, preferred_element_type=F32
    )
    return (combined_heads, log_total)


def attend_backward(query_rotated, key_rotated, value_seq, segment, log_total, grad_heads):
    masked = scores(query_rotated, key_rotated, segment)
    attention_probs = jnp.exp(masked - log_total)
    grad_probs = jnp.einsum("qhgd,khd->hgqk", grad_heads, value_seq, preferred_element_type=F32)
    row_sum = jnp.sum(attention_probs * grad_probs, axis=-1, keepdims=True)
    grad_raw = jnp.where(
        allowed_pairs(segment), attention_probs * (grad_probs - row_sum), 0.0
    ).astype(BF16)
    factor = HEAD_SIZE ** (-0.5)
    grad_query_rot = (
        jnp.einsum("ojus,sov->uojv", grad_raw, key_rotated, preferred_element_type=F32) * factor
    )
    grad_key_rot = (
        jnp.einsum("hgqk,qhgd->khd", grad_raw, query_rotated, preferred_element_type=F32) * factor
    )
    grad_value_rot = jnp.einsum(
        "hgqk,qhgd->khd", attention_probs.astype(BF16), grad_heads, preferred_element_type=F32
    )
    return (grad_query_rot, grad_key_rot, grad_value_rot)


def per_sequence(step, *fields):
    results = [step(*[field[s] for field in fields]) for s in range(fields[0].shape[0])]
    return [jnp.stack(parts) for parts in zip(*results)]


def body(
    tokens,
    segments,
    positions,
    attn_gain,
    w_query,
    key_weight,
    value_weight,
    w_out,
    mlp_gain,
    w_gate,
    w_up,
    w_down,
    cotangent,
):
    groups = lax.axis_size("dp")
    place = lax.axis_index("dp")
    core = lax.axis_index("tensor") % 2
    all_bits = [1 << i for i in range(groups.bit_length() - 1)]
    shared_bits = [bit for bit in (4, 1) if bit < groups]
    split_bits = [bit for bit in all_bits if bit not in shared_bits]

    def gathered(half):
        parts = [half]
        for bit in shared_bits:
            parts = parts + [swap(part, "dp", bit) for part in parts]
        others = parts[1:]
        twins = [swap(part, "tensor", 1) for part in others]
        return jnp.concatenate([narrowed(part) for part in others + twins], axis=0)

    def blocks(matrix, offsets):
        width = matrix.shape[1] // groups
        return [
            lax.dynamic_slice_in_dim(matrix, (place ^ offset) * width, width, 1)
            for offset in offsets
        ]

    def offsets_of(bits):
        found = [0]
        for bit in bits:
            found = found + [offset + bit for offset in found]
        return found

    def reduced(matrix_of, bits):
        sent = None
        for bit in bits:
            rest = bits[bits.index(bit) + 1 :]
            offsets = offsets_of(rest)
            if sent is None:
                away = matrix_of([offset ^ bit for offset in offsets])
                home = matrix_of(offsets)
            else:
                away = [sent[offset ^ bit] for offset in offsets]
                home = [sent[offset] for offset in offsets]
            came = swap(away, "dp", bit)
            sent = {offset: h + c for offset, h, c in zip(offsets, home, came)}
        return sent[0]

    inputs = tokens.astype(F32)
    row_count, width = inputs.shape
    seq_count, seq_len = segments.shape
    query_heads = w_query.shape[1] // HEAD_SIZE
    kv_heads = key_weight.shape[1] // HEAD_SIZE
    group_size = query_heads // kv_heads
    query_width, kv_width = w_query.shape[1], key_weight.shape[1]

    cotangent_half = half_of(cotangent, core).astype(F32)
    cotangent_others = gathered(cotangent_half)

    scale_one = lax.rsqrt(jnp.mean(inputs * inputs, axis=-1, keepdims=True) + EPSILON)
    normed_one = (inputs * scale_one * attn_gain).astype(BF16)
    cosine_lookup, sine_lookup = tables(positions.reshape(row_count))
    cosine_lookup = cosine_lookup[:, None, :]
    sine_lookup = sine_lookup[:, None, :]
    query_projected = product(normed_one, w_query).reshape(row_count, query_heads, HEAD_SIZE)
    key_projected = product(normed_one, key_weight).reshape(row_count, kv_heads, HEAD_SIZE)
    query_rotated = (
        apply_rotary(query_projected, cosine_lookup, sine_lookup)
        .astype(BF16)
        .reshape(seq_count, seq_len, kv_heads, group_size, HEAD_SIZE)
    )
    key_rotated = (
        apply_rotary(key_projected, cosine_lookup, sine_lookup)
        .astype(BF16)
        .reshape(seq_count, seq_len, kv_heads, HEAD_SIZE)
    )
    value_projected = (
        product(normed_one, value_weight)
        .astype(BF16)
        .reshape(seq_count, seq_len, kv_heads, HEAD_SIZE)
    )
    combined_heads, log_totals = per_sequence(
        attend_forward, query_rotated, key_rotated, value_projected, segments
    )
    head_outputs = combined_heads.reshape(row_count, query_width).astype(BF16)

    inputs_half = half_of(inputs, core)
    hidden = inputs_half + tensor_sum_half(product(head_outputs, w_out), core)
    scale_two = lax.rsqrt(jnp.mean(hidden * hidden, axis=-1, keepdims=True) + EPSILON)
    normed_half = (hidden * scale_two * mlp_gain).astype(BF16)
    normed_sent = normed_half.astype(F32)
    normed_twin = narrowed(swap(normed_sent, "tensor", 1))
    normed_two = joined(normed_half, normed_twin, core)
    normed_others = gathered(normed_sent)

    def feed_forward(normed, incoming):
        gate_proj = product(normed, w_gate)
        up_proj = product(normed, w_up)
        grad_activation = against(incoming, w_down)
        sigmoid_gate = jax.nn.sigmoid(gate_proj)
        swish_gate = gate_proj * sigmoid_gate
        activation = (swish_gate * up_proj).astype(BF16)
        grad_gate_in = (
            grad_activation * up_proj * sigmoid_gate * (1.0 + gate_proj * (1.0 - sigmoid_gate))
        ).astype(BF16)
        grad_up_in = (grad_activation * swish_gate).astype(BF16)
        return activation, grad_gate_in, grad_up_in

    activation, grad_gate_in, grad_up_in = feed_forward(normed_two, cotangent)
    grad_normed_two = tensor_sum_half(
        against(grad_gate_in, w_gate) + against(grad_up_in, w_up), core
    )
    mixed_half = hidden + tensor_sum_half(product(activation, w_down), core)
    mixed = joined(mixed_half.astype(BF16), narrowed(swap(mixed_half, "tensor", 1)), core)

    weighted = grad_normed_two * mlp_gain
    inner_mean = jnp.mean(weighted * hidden, axis=-1, keepdims=True)
    back_two = scale_two * weighted - hidden * (scale_two * scale_two * scale_two) * inner_mean
    gain_two_half = jnp.sum(grad_normed_two * hidden * scale_two, axis=0)
    grad_hidden = cotangent_half + back_two
    attn_half = grad_hidden.astype(BF16)
    attn_twin = narrowed(swap(grad_hidden, "tensor", 1))
    grad_attn = joined(attn_half, attn_twin, core)

    grad_heads = (
        against(grad_attn, w_out)
        .astype(BF16)
        .reshape(seq_count, seq_len, kv_heads, group_size, HEAD_SIZE)
    )
    grad_query_rot, grad_key_rot, grad_value_rot = per_sequence(
        attend_backward,
        query_rotated,
        key_rotated,
        value_projected,
        segments,
        log_totals,
        grad_heads,
    )
    grad_query_in = (
        unrotate(
            grad_query_rot.reshape(row_count, query_heads, HEAD_SIZE), cosine_lookup, sine_lookup
        )
        .reshape(row_count, query_width)
        .astype(BF16)
    )
    grad_key_in = (
        unrotate(grad_key_rot.reshape(row_count, kv_heads, HEAD_SIZE), cosine_lookup, sine_lookup)
        .reshape(row_count, kv_width)
        .astype(BF16)
    )
    grad_value_in = grad_value_rot.reshape(row_count, kv_width).astype(BF16)
    partial_one = (
        against(grad_query_in, w_query)
        + against(grad_key_in, key_weight)
        + against(grad_value_in, value_weight)
    )
    grad_normed_one = tensor_sum_half(partial_one, core)
    scale_one = half_of(scale_one, core)
    weighted = grad_normed_one * attn_gain
    inner_mean = jnp.mean(weighted * inputs_half, axis=-1, keepdims=True)
    back_one = scale_one * weighted - inputs_half * (scale_one * scale_one * scale_one) * inner_mean
    gain_one_half = jnp.sum(grad_normed_one * inputs_half * scale_one, axis=0)
    input_half = grad_hidden + back_one
    grad_input = joined(input_half, swap(input_half, "tensor", 1), core)

    activation_o, grad_gate_o, grad_up_o = feed_forward(normed_others, cotangent_others)

    def rows_of(left, left_others, right, right_others):
        def term(offsets):
            ours = blocks(left, offsets)
            theirs = blocks(left_others, offsets)
            return [
                over_rows(a, right) + over_rows(b, right_others) for a, b in zip(ours, theirs)
            ]

        return reduced(term, split_bits)

    def columns_of(left, left_others, right, right_others):
        def term(offsets):
            ours = blocks(right, offsets)
            theirs = blocks(right_others, offsets)
            return [
                over_rows(left, a) + over_rows(left_others, b) for a, b in zip(ours, theirs)
            ]

        return reduced(term, split_bits)

    grad_w_down = columns_of(activation, activation_o, cotangent, cotangent_others)
    grad_w_gate = rows_of(normed_two, normed_others, grad_gate_in, grad_gate_o)
    grad_w_up = rows_of(normed_two, normed_others, grad_up_in, grad_up_o)

    grad_w_out = reduced(
        lambda offsets: [over_rows(head_outputs, b) for b in blocks(grad_attn, offsets)], all_bits
    )
    projected = jnp.concatenate([grad_query_in, grad_key_in, grad_value_in], axis=1)
    grad_w_proj = reduced(
        lambda offsets: [over_rows(b, projected) for b in blocks(normed_one, offsets)], all_bits
    )
    grad_w_query = grad_w_proj[:, :query_width]
    grad_w_key = grad_w_proj[:, query_width : query_width + kv_width]
    grad_w_value = grad_w_proj[:, query_width + kv_width :]

    gains = jnp.stack([gain_one_half, gain_two_half])
    gains = gains + swap(gains, "tensor", 1)
    gains = reduced(lambda offsets: blocks(gains, offsets), all_bits)
    grad_attn_gain, grad_mlp_gain = gains[0], gains[1]
    return (
        mixed,
        grad_input,
        grad_attn_gain,
        grad_w_query,
        grad_w_key,
        grad_w_value,
        grad_w_out,
        grad_mlp_gain,
        grad_w_gate,
        grad_w_up,
        grad_w_down,
    )


def solution(mesh):
    placed = (
        P("dp", None),
        P("dp", None),
        P("dp", None),
        P(),
        P(None, "tensor"),
        P(None, "tensor"),
        P(None, "tensor"),
        P("tensor", None),
        P(),
        P(None, "tensor"),
        P(None, "tensor"),
        P("tensor", None),
        P("dp", None),
    )
    return jax.shard_map(
        body,
        mesh=mesh,
        in_specs=placed,
        out_specs=(
            P("dp", None),
            P("dp", None),
            P("dp"),
            P("dp", "tensor"),
            P("dp", "tensor"),
            P("dp", "tensor"),
            P("tensor", "dp"),
            P("dp"),
            P("dp", "tensor"),
            P("dp", "tensor"),
            P("tensor", "dp"),
        ),
        check_vma=False,
    )
```

```python
import functools

import jax
import jax.numpy as jnp
from jax import lax
from jax.experimental import pallas as pl
from jax.experimental.pallas import tpu as pltpu
from jax.sharding import PartitionSpec as P

HEAD_SIZE = 64
EPSILON = 1e-05
MASKED = -1e30
F32 = jnp.float32
BF16 = jnp.bfloat16


def product(left_matrix, right_matrix):
    return jnp.dot(left_matrix, right_matrix, preferred_element_type=F32)


def over_rows(left_matrix, right_matrix):
    return lax.dot_general(
        left_matrix, right_matrix, (((0,), (0,)), ((), ())), preferred_element_type=F32
    )


def against(gradient, weight):
    return lax.dot_general(
        gradient, weight, (((1,), (1,)), ((), ())), preferred_element_type=F32
    )


def narrowed(value):
    return jnp.where(value == value, value, 0.0).astype(BF16)


def swap(value, axis, bit):
    size = lax.axis_size(axis)
    return lax.ppermute(value, axis, [(i, i ^ bit) for i in range(size)])


def half_of(value, which, dim=0):
    size = value.shape[dim] // 2
    return lax.dynamic_slice_in_dim(value, which * size, size, dim)


def joined(mine, other, which):
    first = jnp.where(which == 0, mine, other)
    second = jnp.where(which == 0, other, mine)
    return jnp.concatenate([first, second], axis=0)


def tensor_sum_half(partial, core):
    total = half_of(partial, core) + swap(half_of(partial, 1 - core), "tensor", 1)
    bit = 2
    while bit < lax.axis_size("tensor"):
        total = total + swap(total, "tensor", bit)
        bit *= 2
    return total


def tables(places):
    half_dim = HEAD_SIZE // 2
    frequency = 500000.0 ** (-(jnp.arange(half_dim).astype(F32) * 2.0 / HEAD_SIZE))
    angles = places.astype(F32)[..., None] * frequency
    cosine_lookup = jnp.cos(angles)
    sine_lookup = jnp.sin(angles)
    return (
        jnp.concatenate([cosine_lookup, cosine_lookup], -1),
        jnp.concatenate([sine_lookup, sine_lookup], -1),
    )


def apply_rotary(field, cosine_lookup, sine_lookup):
    half_dim = HEAD_SIZE // 2
    turned = jnp.concatenate([-field[..., half_dim:], field[..., :half_dim]], -1)
    return field * cosine_lookup + turned * sine_lookup


def unrotate(gradient, cosine_lookup, sine_lookup):
    half_dim = HEAD_SIZE // 2
    sined = gradient * sine_lookup
    return gradient * cosine_lookup + jnp.concatenate(
        [sined[..., half_dim:], -sined[..., :half_dim]], -1
    )


def allowed_pairs(segment):
    spots = jnp.arange(segment.shape[0])
    return (spots[:, None] >= spots[None, :]) & (segment[:, None] == segment[None, :])


def scores(query_rotated, key_rotated, segment):
    raw_scores = jnp.einsum(
        "qhgd,khd->hgqk", query_rotated, key_rotated, preferred_element_type=F32
    ) * HEAD_SIZE ** (-0.5)
    return jnp.where(allowed_pairs(segment), raw_scores, MASKED)


def attend_forward(query_rotated, key_rotated, value_seq, segment):
    masked = scores(query_rotated, key_rotated, segment)
    row_peak = jnp.max(masked, axis=-1, keepdims=True)
    log_total = row_peak + jnp.log(jnp.sum(jnp.exp(masked - row_peak), axis=-1, keepdims=True))
    attention_probs = jnp.exp(masked - log_total).astype(BF16)
    combined_heads = jnp.einsum(
        "ojus,sov->uojv", attention_probs, value_seq, preferred_element_type=F32
    )
    return (combined_heads, log_total)


def attend_backward(query_rotated, key_rotated, value_seq, segment, log_total, grad_heads):
    masked = scores(query_rotated, key_rotated, segment)
    attention_probs = jnp.exp(masked - log_total)
    grad_probs = jnp.einsum("qhgd,khd->hgqk", grad_heads, value_seq, preferred_element_type=F32)
    row_sum = jnp.sum(attention_probs * grad_probs, axis=-1, keepdims=True)
    grad_raw = jnp.where(
        allowed_pairs(segment), attention_probs * (grad_probs - row_sum), 0.0
    ).astype(BF16)
    factor = HEAD_SIZE ** (-0.5)
    grad_query_rot = (
        jnp.einsum("ojus,sov->uojv", grad_raw, key_rotated, preferred_element_type=F32) * factor
    )
    grad_key_rot = (
        jnp.einsum("hgqk,qhgd->khd", grad_raw, query_rotated, preferred_element_type=F32) * factor
    )
    grad_value_rot = jnp.einsum(
        "hgqk,qhgd->khd", attention_probs.astype(BF16), grad_heads, preferred_element_type=F32
    )
    return (grad_query_rot, grad_key_rot, grad_value_rot)


def per_sequence(step, *fields):
    results = [step(*[field[s] for field in fields]) for s in range(fields[0].shape[0])]
    return [jnp.stack(parts) for parts in zip(*results)]


MESH = pl.DeviceIdType.MESH
CHUNKS = 4
TILE = 256
ROWS = 16


def flip(index, bit):
    return index + bit * (1 - 2 * ((index // bit) % 2))


def loop(count, step):
    lax.fori_loop(0, count, lambda i, carry: (step(i), carry)[1], 0)


def middle_kernel(
    heads_ref,
    w_out_ref,
    tokens_ref,
    cot_ref,
    cot_half_ref,
    gain_ref,
    w_gate_ref,
    w_up_ref,
    w_down_ref,
    query_ref,
    keys_ref,
    values_ref,
    log_total_ref,
    segment_column_ref,
    segment_row_ref,
    cosine_ref,
    sine_ref,
    grad_hidden_out,
    grad_attn_out,
    projected_out,
    grad_attn_far,
    projected_far,
    mixed_half_out,
    mixed_twin_out,
    normed_out,
    activation_out,
    grad_gate_out,
    grad_up_out,
    gain_out,
    cot_others,
    normed_others,
    gate_w,
    up_w,
    down_w,
    cot,
    hidden,
    normed,
    normed_sent,
    normed_twin,
    act,
    gg,
    gu,
    away,
    mine,
    core_in,
    y_in,
    local_sem,
    core_send,
    core_recv,
    y_send,
    y_recv,
    cot_send,
    cot_recv,
    n_send,
    n_recv,
    twin_send,
    twin_recv,
    end_send,
    end_recv,
    hidden_send,
    hidden_recv,
    far_send,
    far_recv,
):
    dp, tensor = lax.axis_index("dp"), lax.axis_index("tensor")
    core = tensor % 2
    twin_id = (dp, flip(tensor, 1))
    y_id = (dp, flip(tensor, 2))
    x_id = (flip(dp, 1), tensor)
    z_id = (flip(dp, 4), tensor)
    far_id = (flip(dp, 2), tensor)
    heads = gg.at[:, pl.ds(0, heads_ref.shape[1])]
    tok = gu.at[pl.ds(0, hidden.shape[0])]
    half, width = hidden.shape
    hidden_units = gate_w.shape[1]
    chunk = half // CHUNKS
    my_row = pl.multiple_of(core * half, half)
    twin_row = pl.multiple_of((1 - core) * half, half)

    def remote(src, dst, send, recv, device):
        return pltpu.make_async_remote_copy(
            src_ref=src, dst_ref=dst, send_sem=send, recv_sem=recv,
            device_id=device, device_id_type=MESH,
        )

    loads = {
        "heads": pltpu.make_async_copy(heads_ref, heads, local_sem.at[0]),
        "w_out": pltpu.make_async_copy(w_out_ref, act, local_sem.at[1]),
        "tok": pltpu.make_async_copy(tokens_ref.at[pl.ds(my_row, half)], tok, local_sem.at[2]),
        "cot": pltpu.make_async_copy(cot_ref, cot, local_sem.at[3]),
        "gate": pltpu.make_async_copy(w_gate_ref, gate_w, local_sem.at[4]),
        "up": pltpu.make_async_copy(w_up_ref, up_w, local_sem.at[5]),
        "down": pltpu.make_async_copy(w_down_ref, down_w, local_sem.at[6]),
    }
    for name in loads:
        loads[name].start()

    barrier = pltpu.get_barrier_semaphore()
    for device in (twin_id, y_id, x_id, z_id, far_id):
        pl.semaphore_signal(barrier, inc=1, device_id=device, device_id_type=MESH)
    pl.semaphore_wait(barrier, 5)

    def rows(k):
        return pl.ds(pl.multiple_of(k * chunk, chunk), chunk)

    def from_x(source, slots, k, send, recv):
        return remote(source.at[rows(k)], slots.at[0, rows(k)], send.at[0, k], recv.at[0, k], x_id)

    def from_z(source, slots, k, send, recv):
        return remote(source.at[rows(k)], slots.at[1, rows(k)], send.at[1, k], recv.at[1, k], z_id)

    def from_zx(slots, k, send, recv):
        return remote(
            slots.at[1, rows(k)], slots.at[2, rows(k)], send.at[2, k], recv.at[2, k], x_id
        )

    def to_twin(slots, which, slot):
        return remote(
            slots.at[slot], slots.at[3 + slot],
            twin_send.at[which, slot], twin_recv.at[which, slot], twin_id,
        )

    def send_z(source, slots, k, send, recv):
        from_z(source, slots, k, send, recv).start()
        from_z(source, slots, k + 1, send, recv).start()

    def relay(source, slots, k, send, recv):
        for i in (k, k + 1):
            from_z(source, slots, i, send, recv).wait_recv()
            from_zx(slots, i, send, recv).start()
            from_z(source, slots, i, send, recv).wait_send()

    send_z(cot_half_ref, cot_others, 0, cot_send, cot_recv)
    for k in range(CHUNKS):
        from_x(cot_half_ref, cot_others, k, cot_send, cot_recv).start()

    loads["heads"].wait()
    loads["w_out"].wait()

    def project(into, first_row):
        def step(j):
            columns = pl.ds(pl.multiple_of(j * TILE, TILE), TILE)
            into[:, columns] = jnp.dot(
                heads[pl.ds(first_row, half), :], act[:, columns], preferred_element_type=F32
            )

        loop(width // TILE, step)

    def core_copy(which, window, k):
        return remote(
            away.at[window], core_in.at[which].at[window],
            core_send.at[which, k], core_recv.at[which, k], twin_id,
        )

    def y_copy(which, window, k):
        return remote(
            mine.at[which % 2].at[window], y_in.at[which % 2].at[window],
            y_send.at[which, k], y_recv.at[which, k], y_id,
        )

    everything = slice(None)
    row_windows = [(rows(k), everything) for k in range(CHUNKS)]

    def column_window(j):
        return (everything, pl.ds(pl.multiple_of(j * TILE, TILE), TILE))

    project(away, twin_row)
    for k in range(CHUNKS):
        core_copy(0, row_windows[k], k).start()
    project(mine.at[0], my_row)
    for k in range(CHUNKS):
        core_copy(0, row_windows[k], k).wait_recv()

        def add(i, k=k):
            window = pl.ds(pl.multiple_of(k * chunk + i * ROWS, ROWS), ROWS)
            mine[0, window, :] = mine[0, window, :] + core_in[0, window, :]

        loop(chunk // ROWS, add)
        y_copy(0, row_windows[k], k).start()

    loads["tok"].wait()
    gain = gain_ref[...]
    for k in range(CHUNKS):
        y_copy(0, row_windows[k], k).wait_recv()

        def normalize_rows(i, k=k):
            offset = pl.multiple_of(k * chunk + i * ROWS, ROWS)
            window = pl.ds(offset, ROWS)
            values = tok[window, :].astype(F32) + (mine[0, window, :] + y_in[0, window, :])
            scale = lax.rsqrt(jnp.mean(values * values, axis=-1, keepdims=True) + EPSILON)
            rounded = (values * scale * gain).astype(BF16)
            hidden[window, :] = values
            normed[pl.ds(pl.multiple_of(my_row + offset, ROWS), ROWS), :] = rounded
            normed_sent[window, :] = rounded.astype(F32)

        loop(chunk // ROWS, normalize_rows)
        remote(
            normed_sent.at[rows(k)], normed_twin.at[rows(k)],
            n_send.at[3, k], n_recv.at[3, k], twin_id,
        ).start()
        if k == 2:
            relay(cot_half_ref, cot_others, 0, cot_send, cot_recv)
            send_z(cot_half_ref, cot_others, 2, cot_send, cot_recv)
        from_x(normed_sent, normed_others, k, n_send, n_recv).start()
    for k in range(CHUNKS):
        remote(
            normed_sent.at[rows(k)], normed_twin.at[rows(k)],
            n_send.at[3, k], n_recv.at[3, k], twin_id,
        ).wait_recv()

        def take(i, k=k):
            offset = pl.multiple_of(k * chunk + i * ROWS, ROWS)
            normed[pl.ds(pl.multiple_of(twin_row + offset, ROWS), ROWS), :] = normed_twin[
                pl.ds(offset, ROWS), :
            ].astype(BF16)

        loop(chunk // ROWS, take)

    for name in ("cot", "gate", "up", "down"):
        loads[name].wait()

    def units(j):
        columns = pl.ds(pl.multiple_of(j * TILE, TILE), TILE)
        gate = jnp.dot(normed[...], gate_w[:, columns], preferred_element_type=F32)
        up = jnp.dot(normed[...], up_w[:, columns], preferred_element_type=F32)
        back = lax.dot_general(
            cot[...], down_w[columns, :], (((1,), (1,)), ((), ())), preferred_element_type=F32
        )
        sigmoid = jax.nn.sigmoid(gate)
        swish = gate * sigmoid
        act[:, columns] = (swish * up).astype(BF16)
        gg[:, columns] = (back * up * sigmoid * (1.0 + gate * (1.0 - sigmoid))).astype(BF16)
        gu[:, columns] = (back * swish).astype(BF16)

    loop(hidden_units // TILE, units)

    tiles = width // TILE
    for k in range(CHUNKS):
        core_copy(0, row_windows[k], k).wait_send()

    def column_sums(which, tile_product, forwarded=True):
        def produce(j):
            value = tile_product(j)
            columns = pl.ds(pl.multiple_of(j * TILE, TILE), TILE)
            away[:, columns] = value[0]
            mine[which % 2, :, columns] = value[1]
            core_copy(which, column_window(j), j).start()

        def forward(j):
            core_copy(which, column_window(j), j).wait_recv()
            columns = pl.ds(pl.multiple_of(j * TILE, TILE), TILE)
            mine[which % 2, :, columns] = (
                mine[which % 2, :, columns] + core_in[which, :, columns]
            )
            if forwarded:
                y_copy(which, column_window(j), j).start()

        produce(0)

        def step(j):
            produce(j + 1)
            forward(j)

        loop(tiles - 1, step)
        forward(tiles - 1)

    def halves(dot_of):
        return dot_of(pl.ds(twin_row, half)), dot_of(pl.ds(my_row, half))

    transposed = (((1,), (1,)), ((), ()))

    def back_tile(j):
        columns = pl.ds(pl.multiple_of(j * TILE, TILE), TILE)
        return halves(
            lambda part: lax.dot_general(
                gg[part, :], gate_w[columns, :], transposed, preferred_element_type=F32
            )
            + lax.dot_general(
                gu[part, :], up_w[columns, :], transposed, preferred_element_type=F32
            )
        )

    def branch_tile(j):
        columns = pl.ds(pl.multiple_of(j * TILE, TILE), TILE)
        return halves(
            lambda part: jnp.dot(act[part, :], down_w[:, columns], preferred_element_type=F32)
        )

    column_sums(1, back_tile)
    stores = [
        pltpu.make_async_copy(normed, normed_out, local_sem.at[7]),
        pltpu.make_async_copy(act, activation_out, local_sem.at[8]),
        pltpu.make_async_copy(gg, grad_gate_out, local_sem.at[9]),
        pltpu.make_async_copy(gu, grad_up_out, local_sem.at[10]),
    ]
    for store in stores:
        store.start()
    relay(cot_half_ref, cot_others, 2, cot_send, cot_recv)
    send_z(normed_sent, normed_others, 0, n_send, n_recv)
    loop(tiles, lambda j: core_copy(1, column_window(j), j).wait_send())
    for k in range(CHUNKS):
        y_copy(0, row_windows[k], k).wait_send()
    column_sums(2, branch_tile, forwarded=False)
    for k in range(CHUNKS):
        from_x(cot_half_ref, cot_others, k, cot_send, cot_recv).wait_recv()
    to_twin(cot_others, 0, 0).start()
    to_twin(cot_others, 0, 1).start()

    for store in stores:
        store.wait()
    operands = [
        pltpu.make_async_copy(query_ref, act.at[:, pl.ds(0, 512)], local_sem.at[0]),
        pltpu.make_async_copy(keys_ref, act.at[:, pl.ds(1024, 512)], local_sem.at[1]),
        pltpu.make_async_copy(values_ref, act.at[:, pl.ds(1536, 512)], local_sem.at[2]),
        pltpu.make_async_copy(w_out_ref, gate_w.at[pl.ds(0, 512)], local_sem.at[3]),
    ]
    for operand in operands:
        operand.start()

    loop(tiles, lambda j: y_copy(1, column_window(j), j).wait_recv())
    loop(tiles, lambda j: y_copy(2, column_window(j), j).start())
    gain_out[...] = jnp.zeros_like(gain_out)

    def hidden_copy(k):
        return remote(
            core_in.at[0, rows(k)], normed_twin.at[rows(k)],
            hidden_send.at[k], hidden_recv.at[k], twin_id,
        )

    for k in range(CHUNKS):

        def norm_rows(i, k=k):
            offset = pl.multiple_of(k * chunk + i * ROWS, ROWS)
            window = pl.ds(offset, ROWS)
            incoming = mine[1, window, :] + y_in[1, window, :]
            values = hidden[window, :]
            scale = lax.rsqrt(jnp.mean(values * values, axis=-1, keepdims=True) + EPSILON)
            weighted = incoming * gain
            inner = jnp.mean(weighted * values, axis=-1, keepdims=True)
            back = scale * weighted - values * (scale * scale * scale) * inner
            here = pl.ds(pl.multiple_of(my_row + offset, ROWS), ROWS)
            total = cot[here, :].astype(F32) + back
            core_in[0, window, :] = total
            normed[here, :] = total.astype(BF16)
            gain_out[...] = gain_out[...] + jnp.sum(
                incoming * values * scale, axis=0, keepdims=True
            )

        loop(chunk // ROWS, norm_rows)
        hidden_copy(k).start()
    hidden_store = pltpu.make_async_copy(core_in.at[0], grad_hidden_out, local_sem.at[4])
    hidden_store.start()
    relay(normed_sent, normed_others, 0, n_send, n_recv)
    send_z(normed_sent, normed_others, 2, n_send, n_recv)
    for k in range(CHUNKS):
        hidden_copy(k).wait_recv()

        def take_hidden(i, k=k):
            offset = pl.multiple_of(k * chunk + i * ROWS, ROWS)
            normed[pl.ds(pl.multiple_of(twin_row + offset, ROWS), ROWS), :] = normed_twin[
                pl.ds(offset, ROWS), :
            ].astype(BF16)

        loop(chunk // ROWS, take_hidden)
    grad_attn_store = pltpu.make_async_copy(normed, grad_attn_out, local_sem.at[5])
    grad_attn_store.start()

    def far_columns(b):
        z_low = (dp // 2) % 2
        return pl.ds(pl.multiple_of(b * 1024 + (1 - z_low) * 512, 512), 512)

    def far_copies():
        copies = []
        for b in range(2):
            kept = pl.ds(b * 512, 512)
            copies.append(remote(
                core_in.at[0, :, far_columns(b)], grad_attn_far.at[0, :, kept],
                far_send.at[b], far_recv.at[b], far_id,
            ))
            copies.append(remote(
                normed_twin.at[:, far_columns(b)], grad_attn_far.at[1, :, kept],
                far_send.at[2 + b], far_recv.at[2 + b], far_id,
            ))
        return copies

    for copy in far_copies():
        copy.start()

    for operand in operands:
        operand.wait()

    def head_tile(j):
        columns = pl.ds(pl.multiple_of(j * TILE, TILE), TILE)
        act[:, pl.ds(pl.multiple_of(512 + j * TILE, TILE), TILE)] = lax.dot_general(
            normed[...], gate_w[columns, :], transposed, preferred_element_type=F32
        ).astype(BF16)

    loop(512 // TILE, head_tile)
    sums = y_in.at[1]
    sums[:, pl.ds(0, 1024)] = jnp.zeros((TILE, 1024), F32)

    def gather_into(offset, kv, value):
        for part in range(value.shape[0] // TILE):
            columns = pl.ds(pl.multiple_of(offset + kv * 256 + part * 128, 128), 128)
            sums[:, columns] = sums[:, columns] + value[part * TILE : (part + 1) * TILE]

    factor = HEAD_SIZE ** (-0.5)
    lane = lax.broadcasted_iota(jnp.int32, (TILE, 128), 1)

    def unrotate_tile(value, window):
        turned = jnp.where(
            lane % 64 < 32, pltpu.roll(value, 96, 1), pltpu.roll(value, 32, 1)
        )
        return value * cosine_ref[window, :] + turned * sine_ref[window, :]

    def put(block, column, value):
        rounded = value.astype(BF16)
        gu[pl.ds(block * TILE, TILE), pl.ds(column, 128)] = rounded
        core_in[1, :, pl.ds(block * 1024 + column, 128)] = rounded.astype(F32)

    def pair(p):
        kv = p // 2
        column = pl.multiple_of(p * 128, 128)
        for block in range(2):
            keys_seen = (block + 1) * TILE
            window = pl.ds(block * TILE, TILE)
            seen = pl.ds(0, keys_seen)
            queries = act[window, pl.ds(column, 128)]
            upstream = act[window, pl.ds(pl.multiple_of(512 + column, 128), 128)]
            key_place = lax.broadcasted_iota(jnp.int32, (keys_seen, TILE), 0)
            query_place = lax.broadcasted_iota(jnp.int32, (keys_seen, TILE), 1) + block * TILE
            allowed = (key_place <= query_place) & (
                segment_column_ref[seen, :] == segment_row_ref[:, window]
            )
            query_grad = jnp.zeros((TILE, 128), F32)
            for side in range(2):
                padded = pl.multiple_of((kv * 2 + side) * 128, 128)
                keys = act[seen, pl.ds(pl.multiple_of(1024 + padded, 128), 128)]
                vals = act[seen, pl.ds(pl.multiple_of(1536 + padded, 128), 128)]
                raw = lax.dot_general(
                    keys, queries, transposed, preferred_element_type=F32
                ) * factor
                log_total = log_total_ref[pl.ds(2 * p + side, 1), window]
                probs = jnp.exp(jnp.where(allowed, raw - log_total, MASKED))
                grad_probs = lax.dot_general(
                    vals, upstream, transposed, preferred_element_type=F32
                )
                row_sum = jnp.sum(probs * grad_probs, axis=0, keepdims=True)
                grad_raw = (probs * (grad_probs - row_sum)).astype(BF16)
                query_grad = query_grad + lax.dot_general(
                    grad_raw, keys, (((0,), (0,)), ((), ())), preferred_element_type=F32
                )
                own = (lax.broadcasted_iota(jnp.int32, (keys_seen, 128), 1) // 64) == side
                gather_into(0, kv, jnp.where(
                    own, jnp.dot(grad_raw, queries, preferred_element_type=F32), 0.0
                ))
                gather_into(512, kv, jnp.where(
                    own, jnp.dot(probs.astype(BF16), upstream, preferred_element_type=F32), 0.0
                ))
            put(block, column, unrotate_tile(query_grad * factor, window))

    loop(4, pair)

    def both(offset, block):
        def folded(kv):
            value = sums[:, pl.ds(offset + kv * 256 + block * 128, 128)]
            return value + pltpu.roll(value, 64, 1)

        return jnp.where(lane < 64, folded(0), folded(1))

    for block in range(2):
        window = pl.ds(block * TILE, TILE)
        put(block, 512, unrotate_tile(both(0, block) * factor, window))
        put(block, 640, both(512, block))
    projected_store = pltpu.make_async_copy(
        gu.at[:, pl.ds(0, 768)], projected_out, local_sem.at[6]
    )
    projected_store.start()

    def projected_copy(b):
        window = (everything, pl.ds(b * 1024, 768))
        return remote(
            core_in.at[1].at[window], projected_far.at[window],
            far_send.at[4 + b], far_recv.at[4 + b], far_id,
        )

    projected_copy(0).start()
    projected_copy(1).start()

    for k in range(CHUNKS):
        from_x(normed_sent, normed_others, k, n_send, n_recv).wait_recv()
    to_twin(normed_others, 1, 0).start()
    for k in range(CHUNKS):
        from_zx(cot_others, k, cot_send, cot_recv).wait_recv()
    to_twin(cot_others, 0, 2).start()
    relay(normed_sent, normed_others, 2, n_send, n_recv)
    to_twin(normed_others, 1, 1).start()

    loop(tiles, lambda j: y_copy(2, column_window(j), j).wait_recv())
    loop(tiles, lambda j: y_copy(2, column_window(j), j).wait_send())

    def mixed_rows(i):
        window = pl.ds(pl.multiple_of(i * ROWS, ROWS), ROWS)
        mine[0, window, :] = hidden[window, :] + (mine[0, window, :] + y_in[0, window, :])

    loop(half // ROWS, mixed_rows)
    mixed_copy = remote(
        mine.at[0], mixed_twin_out, end_send.at[1], end_recv.at[1], twin_id
    )
    mixed_copy.start()
    mixed_store = pltpu.make_async_copy(mine.at[0], mixed_half_out, local_sem.at[12])
    mixed_store.start()
    for k in range(CHUNKS):
        from_zx(normed_others, k, n_send, n_recv).wait_recv()
    to_twin(normed_others, 1, 2).start()

    for store in (hidden_store, grad_attn_store, projected_store, mixed_store):
        store.wait()
    mixed_copy.wait()
    for copy in far_copies() + [projected_copy(0), projected_copy(1)]:
        copy.wait()
    for k in range(CHUNKS):
        hidden_copy(k).wait_send()
        from_x(cot_half_ref, cot_others, k, cot_send, cot_recv).wait_send()
        from_x(normed_sent, normed_others, k, n_send, n_recv).wait_send()
        from_zx(cot_others, k, cot_send, cot_recv).wait_send()
        from_zx(normed_others, k, n_send, n_recv).wait_send()
        remote(
            normed_sent.at[rows(k)], normed_twin.at[rows(k)],
            n_send.at[3, k], n_recv.at[3, k], twin_id,
        ).wait_send()
    loop(tiles, lambda j: y_copy(1, column_window(j), j).wait_send())
    loop(tiles, lambda j: core_copy(2, column_window(j), j).wait_send())
    for slot in range(3):
        to_twin(cot_others, 0, slot).wait()
        to_twin(normed_others, 1, slot).wait()


def middle(
    heads, w_out, tokens, cotangent, cotangent_half, gain, w_gate, w_up, w_down,
    query, keys, values, log_total, segment, cosine, sine,
):
    row_count, width = tokens.shape
    half = row_count // 2
    hidden_units = w_gate.shape[1]
    tiles = width // TILE
    hbm = pl.BlockSpec(memory_space=pl.ANY)
    vmem = pl.BlockSpec(memory_space=pltpu.VMEM)
    wide = jax.ShapeDtypeStruct((half, width), F32)
    units = jax.ShapeDtypeStruct((row_count, hidden_units), BF16)
    dma = pltpu.SemaphoreType.DMA
    return pl.pallas_call(
        middle_kernel,
        out_shape=(
            wide,
            jax.ShapeDtypeStruct((row_count, width), BF16),
            jax.ShapeDtypeStruct((row_count, 768), BF16),
            jax.ShapeDtypeStruct((2, half, width // 2), F32),
            wide,
            wide, wide,
            jax.ShapeDtypeStruct((row_count, width), BF16),
            units, units, units,
            jax.ShapeDtypeStruct((1, width), F32),
            jax.ShapeDtypeStruct((6, half, width), F32),
            jax.ShapeDtypeStruct((6, half, width), F32),
        ),
        in_specs=[hbm, hbm, hbm, hbm, hbm, vmem, hbm, hbm, hbm, hbm, hbm, hbm] + [vmem] * 5,
        out_specs=(hbm,) * 11 + (vmem,) + (hbm,) * 2,
        scratch_shapes=[
            pltpu.VMEM(w_gate.shape, BF16),
            pltpu.VMEM(w_up.shape, BF16),
            pltpu.VMEM(w_down.shape, BF16),
            pltpu.VMEM((row_count, width), BF16),
            pltpu.VMEM((half, width), F32),
            pltpu.VMEM((row_count, width), BF16),
            pltpu.VMEM((half, width), F32),
            pltpu.VMEM((half, width), F32),
            pltpu.VMEM((row_count, hidden_units), BF16),
            pltpu.VMEM((row_count, hidden_units), BF16),
            pltpu.VMEM((row_count, hidden_units), BF16),
            pltpu.VMEM((half, width), F32),
            pltpu.VMEM((2, half, width), F32),
            pltpu.VMEM((3, half, width), F32),
            pltpu.VMEM((2, half, width), F32),
            dma((13,)),
            dma((3, tiles)), dma((3, tiles)), dma((3, tiles)), dma((3, tiles)),
            dma((3, CHUNKS)), dma((3, CHUNKS)),
            dma((4, CHUNKS)), dma((4, CHUNKS)),
            dma((2, 3)), dma((2, 3)),
            dma((2,)), dma((2,)),
            dma((CHUNKS,)), dma((CHUNKS,)),
            dma((6,)), dma((6,)),
        ],
        compiler_params=pltpu.CompilerParams(
            collective_id=0, has_side_effects=True, vmem_limit_bytes=64 * 1024 * 1024
        ),
        name="feed_forward",
    )(
        heads, w_out, tokens, cotangent, cotangent_half, gain.reshape(1, width),
        w_gate, w_up, w_down, query, keys, values, log_total,
        segment.reshape(row_count, 1), segment.reshape(1, row_count), cosine, sine,
    )


def body(
    tokens,
    segments,
    positions,
    attn_gain,
    w_query,
    key_weight,
    value_weight,
    w_out,
    mlp_gain,
    w_gate,
    w_up,
    w_down,
    cotangent,
):
    groups = lax.axis_size("dp")
    place = lax.axis_index("dp")
    core = lax.axis_index("tensor") % 2
    all_bits = [1 << i for i in range(groups.bit_length() - 1)]
    shared_bits = [bit for bit in (4, 1) if bit < groups]
    split_bits = [bit for bit in all_bits if bit not in shared_bits]

    def blocks(matrix, offsets):
        width = matrix.shape[1] // groups
        return [
            lax.dynamic_slice_in_dim(matrix, (place ^ offset) * width, width, 1)
            for offset in offsets
        ]

    def offsets_of(bits):
        found = [0]
        for bit in bits:
            found = found + [offset + bit for offset in found]
        return found

    def reduced(matrix_of, bits):
        sent = None
        for bit in bits:
            rest = bits[bits.index(bit) + 1 :]
            offsets = offsets_of(rest)
            if sent is None:
                away = matrix_of([offset ^ bit for offset in offsets])
                home = matrix_of(offsets)
            else:
                away = [sent[offset ^ bit] for offset in offsets]
                home = [sent[offset] for offset in offsets]
            came = swap(away, "dp", bit)
            sent = {offset: h + c for offset, h, c in zip(offsets, home, came)}
        return sent[0]

    inputs = tokens.astype(F32)
    row_count, width = inputs.shape
    seq_count, seq_len = segments.shape
    query_heads = w_query.shape[1] // HEAD_SIZE
    kv_heads = key_weight.shape[1] // HEAD_SIZE
    group_size = query_heads // kv_heads
    query_width, kv_width = w_query.shape[1], key_weight.shape[1]

    scale_one = lax.rsqrt(jnp.mean(inputs * inputs, axis=-1, keepdims=True) + EPSILON)
    normed_one = (inputs * scale_one * attn_gain).astype(BF16)
    cosine_lookup, sine_lookup = tables(positions.reshape(row_count))
    cosine_lookup = cosine_lookup[:, None, :]
    sine_lookup = sine_lookup[:, None, :]
    query_projected = product(normed_one, w_query).reshape(row_count, query_heads, HEAD_SIZE)
    key_projected = product(normed_one, key_weight).reshape(row_count, kv_heads, HEAD_SIZE)
    query_rotated = (
        apply_rotary(query_projected, cosine_lookup, sine_lookup)
        .astype(BF16)
        .reshape(seq_count, seq_len, kv_heads, group_size, HEAD_SIZE)
    )
    key_rotated = (
        apply_rotary(key_projected, cosine_lookup, sine_lookup)
        .astype(BF16)
        .reshape(seq_count, seq_len, kv_heads, HEAD_SIZE)
    )
    value_projected = (
        product(normed_one, value_weight)
        .astype(BF16)
        .reshape(seq_count, seq_len, kv_heads, HEAD_SIZE)
    )
    combined_heads, log_totals = per_sequence(
        attend_forward, query_rotated, key_rotated, value_projected, segments
    )
    head_outputs = combined_heads.reshape(row_count, query_width).astype(BF16)

    inputs_half = half_of(inputs, core)
    cotangent_half = half_of(cotangent, core).astype(F32)
    def padded(heads):
        zeros = jnp.zeros((row_count, HEAD_SIZE), BF16)
        parts = []
        for h in range(kv_heads):
            parts += [heads[0, :, h], zeros, zeros, heads[0, :, h]]
        return jnp.concatenate(parts, axis=1)

    z_low = (place // 2) % 2

    def near(matrix, which):
        parts = matrix.reshape(matrix.shape[0], 2, 2, -1)
        return lax.dynamic_index_in_dim(parts, which, 2, False).reshape(matrix.shape[0], -1)

    heads_far = narrowed(swap(head_outputs.astype(F32), "dp", 2))
    normed_one_far = narrowed(swap(near(normed_one, 1 - z_low).astype(F32), "dp", 2))
    lanes = jnp.arange(128) % HEAD_SIZE
    cosine_tile = jnp.concatenate([cosine_lookup[:, 0], cosine_lookup[:, 0]], axis=1)
    sine_tile = jnp.concatenate([sine_lookup[:, 0], sine_lookup[:, 0]], axis=1)
    sine_tile = jnp.where(lanes < HEAD_SIZE // 2, sine_tile, -sine_tile)
    (
        grad_hidden,
        grad_attn,
        projected,
        grad_attn_far,
        projected_far,
        mixed_half,
        mixed_twin,
        normed_two,
        activation,
        grad_gate_in,
        grad_up_in,
        gain_two_half,
        cotangent_others,
        normed_others,
    ) = middle(
        head_outputs, w_out, tokens, cotangent, cotangent_half, mlp_gain, w_gate, w_up, w_down,
        query_rotated.reshape(row_count, query_width), padded(key_rotated),
        padded(value_projected), log_totals.reshape(query_heads, row_count), segments,
        cosine_tile, sine_tile,
    )
    gain_two_half = gain_two_half[0]
    mixed = joined(mixed_half, mixed_twin, core).astype(BF16)
    cotangent_others = cotangent_others.reshape(-1, width).astype(BF16)
    normed_others = normed_others.reshape(-1, width).astype(BF16)
    grad_attn_far = joined(grad_attn_far[0], grad_attn_far[1], core).astype(BF16)
    projected_far = jnp.concatenate(
        [projected_far[:, :768], projected_far[:, 1024:1792]], axis=0
    ).astype(BF16)

    def feed_forward(normed, incoming):
        gate_proj = product(normed, w_gate)
        up_proj = product(normed, w_up)
        grad_activation = against(incoming, w_down)
        sigmoid_gate = jax.nn.sigmoid(gate_proj)
        swish_gate = gate_proj * sigmoid_gate
        activation = (swish_gate * up_proj).astype(BF16)
        grad_gate_in = (
            grad_activation * up_proj * sigmoid_gate * (1.0 + gate_proj * (1.0 - sigmoid_gate))
        ).astype(BF16)
        grad_up_in = (grad_activation * swish_gate).astype(BF16)
        return activation, grad_gate_in, grad_up_in

    partial_one = against(
        projected, jnp.concatenate([w_query, key_weight, value_weight], axis=1)
    )
    grad_normed_one = tensor_sum_half(partial_one, core)
    scale_one = half_of(scale_one, core)
    weighted = grad_normed_one * attn_gain
    inner_mean = jnp.mean(weighted * inputs_half, axis=-1, keepdims=True)
    back_one = scale_one * weighted - inputs_half * (scale_one * scale_one * scale_one) * inner_mean
    gain_one_half = jnp.sum(grad_normed_one * inputs_half * scale_one, axis=0)
    input_half = grad_hidden + back_one
    grad_input = joined(input_half, swap(input_half, "tensor", 1), core)

    activation_o, grad_gate_o, grad_up_o = feed_forward(normed_others, cotangent_others)

    def rows_of(left, left_others, right, right_others):
        def term(offsets):
            ours = blocks(left, offsets)
            theirs = blocks(left_others, offsets)
            return [
                over_rows(a, right) + over_rows(b, right_others) for a, b in zip(ours, theirs)
            ]

        return reduced(term, split_bits)

    def columns_of(left, left_others, right, right_others):
        def term(offsets):
            ours = blocks(right, offsets)
            theirs = blocks(right_others, offsets)
            return [
                over_rows(left, a) + over_rows(left_others, b) for a, b in zip(ours, theirs)
            ]

        return reduced(term, split_bits)

    grad_w_down = columns_of(activation, activation_o, cotangent, cotangent_others)
    grad_w_gate = rows_of(normed_two, normed_others, grad_gate_in, grad_gate_o)
    grad_w_up = rows_of(normed_two, normed_others, grad_up_in, grad_up_o)

    out_part = over_rows(head_outputs, near(grad_attn, z_low)) + over_rows(
        heads_far, grad_attn_far
    )
    proj_part = over_rows(near(normed_one, z_low), projected) + over_rows(
        normed_one_far, projected_far
    )
    x_low, z_high = place % 2, place // 4
    width_out = width // groups

    def reduced_far(parts):
        column = lambda which: lax.dynamic_index_in_dim(parts, which, 1, False)
        parts = column(x_low) + swap(column(1 - x_low), "dp", 1)
        piece = lambda which: lax.dynamic_index_in_dim(parts, which, 0, False)
        return piece(z_high) + swap(piece(1 - z_high), "dp", 4)

    grad_w_out = reduced_far(
        out_part.reshape(query_width, 2, 2, width_out).transpose(1, 2, 0, 3)
    )
    grad_w_proj = reduced_far(proj_part.reshape(2, 2, width_out, -1))
    grad_w_query = grad_w_proj[:, :query_width]
    grad_w_key = grad_w_proj[:, query_width : query_width + kv_width]
    grad_w_value = grad_w_proj[:, query_width + kv_width :]

    gains = jnp.stack([gain_one_half, gain_two_half])
    gains = gains + swap(gains, "tensor", 1)
    gains = reduced(lambda offsets: blocks(gains, offsets), all_bits)
    grad_attn_gain, grad_mlp_gain = gains[0], gains[1]
    return (
        mixed,
        grad_input,
        grad_attn_gain,
        grad_w_query,
        grad_w_key,
        grad_w_value,
        grad_w_out,
        grad_mlp_gain,
        grad_w_gate,
        grad_w_up,
        grad_w_down,
    )


def general_body(
    tokens,
    segments,
    positions,
    attn_gain,
    w_query,
    key_weight,
    value_weight,
    w_out,
    mlp_gain,
    w_gate,
    w_up,
    w_down,
    cotangent,
):
    groups = lax.axis_size("dp")
    place = lax.axis_index("dp")
    core = lax.axis_index("tensor") % 2
    all_bits = [1 << i for i in range(groups.bit_length() - 1)]
    shared_bits = [bit for bit in (4, 1) if bit < groups]
    split_bits = [bit for bit in all_bits if bit not in shared_bits]

    def gathered(half):
        parts = [half]
        for bit in shared_bits:
            parts = parts + [swap(part, "dp", bit) for part in parts]
        others = parts[1:]
        twins = [swap(part, "tensor", 1) for part in others]
        return jnp.concatenate([narrowed(part) for part in others + twins], axis=0)

    def blocks(matrix, offsets):
        width = matrix.shape[1] // groups
        return [
            lax.dynamic_slice_in_dim(matrix, (place ^ offset) * width, width, 1)
            for offset in offsets
        ]

    def offsets_of(bits):
        found = [0]
        for bit in bits:
            found = found + [offset + bit for offset in found]
        return found

    def reduced(matrix_of, bits):
        sent = None
        for bit in bits:
            rest = bits[bits.index(bit) + 1 :]
            offsets = offsets_of(rest)
            if sent is None:
                away = matrix_of([offset ^ bit for offset in offsets])
                home = matrix_of(offsets)
            else:
                away = [sent[offset ^ bit] for offset in offsets]
                home = [sent[offset] for offset in offsets]
            came = swap(away, "dp", bit)
            sent = {offset: h + c for offset, h, c in zip(offsets, home, came)}
        return sent[0]

    inputs = tokens.astype(F32)
    row_count, width = inputs.shape
    seq_count, seq_len = segments.shape
    query_heads = w_query.shape[1] // HEAD_SIZE
    kv_heads = key_weight.shape[1] // HEAD_SIZE
    group_size = query_heads // kv_heads
    query_width, kv_width = w_query.shape[1], key_weight.shape[1]

    cotangent_half = half_of(cotangent, core).astype(F32)
    cotangent_others = gathered(cotangent_half)

    scale_one = lax.rsqrt(jnp.mean(inputs * inputs, axis=-1, keepdims=True) + EPSILON)
    normed_one = (inputs * scale_one * attn_gain).astype(BF16)
    cosine_lookup, sine_lookup = tables(positions.reshape(row_count))
    cosine_lookup = cosine_lookup[:, None, :]
    sine_lookup = sine_lookup[:, None, :]
    query_projected = product(normed_one, w_query).reshape(row_count, query_heads, HEAD_SIZE)
    key_projected = product(normed_one, key_weight).reshape(row_count, kv_heads, HEAD_SIZE)
    query_rotated = (
        apply_rotary(query_projected, cosine_lookup, sine_lookup)
        .astype(BF16)
        .reshape(seq_count, seq_len, kv_heads, group_size, HEAD_SIZE)
    )
    key_rotated = (
        apply_rotary(key_projected, cosine_lookup, sine_lookup)
        .astype(BF16)
        .reshape(seq_count, seq_len, kv_heads, HEAD_SIZE)
    )
    value_projected = (
        product(normed_one, value_weight)
        .astype(BF16)
        .reshape(seq_count, seq_len, kv_heads, HEAD_SIZE)
    )
    combined_heads, log_totals = per_sequence(
        attend_forward, query_rotated, key_rotated, value_projected, segments
    )
    head_outputs = combined_heads.reshape(row_count, query_width).astype(BF16)

    inputs_half = half_of(inputs, core)
    hidden = inputs_half + tensor_sum_half(product(head_outputs, w_out), core)
    scale_two = lax.rsqrt(jnp.mean(hidden * hidden, axis=-1, keepdims=True) + EPSILON)
    normed_half = (hidden * scale_two * mlp_gain).astype(BF16)
    normed_sent = normed_half.astype(F32)
    normed_twin = narrowed(swap(normed_sent, "tensor", 1))
    normed_two = joined(normed_half, normed_twin, core)
    normed_others = gathered(normed_sent)

    def feed_forward(normed, incoming):
        gate_proj = product(normed, w_gate)
        up_proj = product(normed, w_up)
        grad_activation = against(incoming, w_down)
        sigmoid_gate = jax.nn.sigmoid(gate_proj)
        swish_gate = gate_proj * sigmoid_gate
        activation = (swish_gate * up_proj).astype(BF16)
        grad_gate_in = (
            grad_activation * up_proj * sigmoid_gate * (1.0 + gate_proj * (1.0 - sigmoid_gate))
        ).astype(BF16)
        grad_up_in = (grad_activation * swish_gate).astype(BF16)
        return activation, grad_gate_in, grad_up_in

    activation, grad_gate_in, grad_up_in = feed_forward(normed_two, cotangent)
    grad_normed_two = tensor_sum_half(
        against(grad_gate_in, w_gate) + against(grad_up_in, w_up), core
    )
    mixed_half = hidden + tensor_sum_half(product(activation, w_down), core)
    mixed = joined(mixed_half.astype(BF16), narrowed(swap(mixed_half, "tensor", 1)), core)

    weighted = grad_normed_two * mlp_gain
    inner_mean = jnp.mean(weighted * hidden, axis=-1, keepdims=True)
    back_two = scale_two * weighted - hidden * (scale_two * scale_two * scale_two) * inner_mean
    gain_two_half = jnp.sum(grad_normed_two * hidden * scale_two, axis=0)
    grad_hidden = cotangent_half + back_two
    attn_half = grad_hidden.astype(BF16)
    attn_twin = narrowed(swap(grad_hidden, "tensor", 1))
    grad_attn = joined(attn_half, attn_twin, core)

    grad_heads = (
        against(grad_attn, w_out)
        .astype(BF16)
        .reshape(seq_count, seq_len, kv_heads, group_size, HEAD_SIZE)
    )
    grad_query_rot, grad_key_rot, grad_value_rot = per_sequence(
        attend_backward,
        query_rotated,
        key_rotated,
        value_projected,
        segments,
        log_totals,
        grad_heads,
    )
    grad_query_in = (
        unrotate(
            grad_query_rot.reshape(row_count, query_heads, HEAD_SIZE), cosine_lookup, sine_lookup
        )
        .reshape(row_count, query_width)
        .astype(BF16)
    )
    grad_key_in = (
        unrotate(grad_key_rot.reshape(row_count, kv_heads, HEAD_SIZE), cosine_lookup, sine_lookup)
        .reshape(row_count, kv_width)
        .astype(BF16)
    )
    grad_value_in = grad_value_rot.reshape(row_count, kv_width).astype(BF16)
    partial_one = (
        against(grad_query_in, w_query)
        + against(grad_key_in, key_weight)
        + against(grad_value_in, value_weight)
    )
    grad_normed_one = tensor_sum_half(partial_one, core)
    scale_one = half_of(scale_one, core)
    weighted = grad_normed_one * attn_gain
    inner_mean = jnp.mean(weighted * inputs_half, axis=-1, keepdims=True)
    back_one = scale_one * weighted - inputs_half * (scale_one * scale_one * scale_one) * inner_mean
    gain_one_half = jnp.sum(grad_normed_one * inputs_half * scale_one, axis=0)
    input_half = grad_hidden + back_one
    grad_input = joined(input_half, swap(input_half, "tensor", 1), core)

    activation_o, grad_gate_o, grad_up_o = feed_forward(normed_others, cotangent_others)

    def rows_of(left, left_others, right, right_others):
        def term(offsets):
            ours = blocks(left, offsets)
            theirs = blocks(left_others, offsets)
            return [
                over_rows(a, right) + over_rows(b, right_others) for a, b in zip(ours, theirs)
            ]

        return reduced(term, split_bits)

    def columns_of(left, left_others, right, right_others):
        def term(offsets):
            ours = blocks(right, offsets)
            theirs = blocks(right_others, offsets)
            return [
                over_rows(left, a) + over_rows(left_others, b) for a, b in zip(ours, theirs)
            ]

        return reduced(term, split_bits)

    grad_w_down = columns_of(activation, activation_o, cotangent, cotangent_others)
    grad_w_gate = rows_of(normed_two, normed_others, grad_gate_in, grad_gate_o)
    grad_w_up = rows_of(normed_two, normed_others, grad_up_in, grad_up_o)

    grad_w_out = reduced(
        lambda offsets: [over_rows(head_outputs, b) for b in blocks(grad_attn, offsets)], all_bits
    )
    projected = jnp.concatenate([grad_query_in, grad_key_in, grad_value_in], axis=1)
    grad_w_proj = reduced(
        lambda offsets: [over_rows(b, projected) for b in blocks(normed_one, offsets)], all_bits
    )
    grad_w_query = grad_w_proj[:, :query_width]
    grad_w_key = grad_w_proj[:, query_width : query_width + kv_width]
    grad_w_value = grad_w_proj[:, query_width + kv_width :]

    gains = jnp.stack([gain_one_half, gain_two_half])
    gains = gains + swap(gains, "tensor", 1)
    gains = reduced(lambda offsets: blocks(gains, offsets), all_bits)
    grad_attn_gain, grad_mlp_gain = gains[0], gains[1]
    return (
        mixed,
        grad_input,
        grad_attn_gain,
        grad_w_query,
        grad_w_key,
        grad_w_value,
        grad_w_out,
        grad_mlp_gain,
        grad_w_gate,
        grad_w_up,
        grad_w_down,
    )


def solution(mesh):
    placed = (
        P("dp", None),
        P("dp", None),
        P("dp", None),
        P(),
        P(None, "tensor"),
        P(None, "tensor"),
        P(None, "tensor"),
        P("tensor", None),
        P(),
        P(None, "tensor"),
        P(None, "tensor"),
        P("tensor", None),
        P("dp", None),
    )
    fits = mesh.shape["dp"] == 8 and mesh.shape["tensor"] == 4
    return jax.shard_map(
        body if fits else general_body,
        mesh=mesh,
        in_specs=placed,
        out_specs=(
            P("dp", None),
            P("dp", None),
            P("dp"),
            P("dp", "tensor"),
            P("dp", "tensor"),
            P("dp", "tensor"),
            P("tensor", "dp"),
            P("dp"),
            P("dp", "tensor"),
            P("dp", "tensor"),
            P("tensor", "dp"),
        ),
        check_vma=False,
    )
```

```python
import functools

import jax
import jax.numpy as jnp
from jax import lax
from jax.experimental import pallas as pl
from jax.experimental.pallas import tpu as pltpu
from jax.sharding import PartitionSpec as P

HEAD_SIZE = 64
EPSILON = 1e-05
MASKED = -1e30
F32 = jnp.float32
BF16 = jnp.bfloat16


def swap(value, axis, bit):
    size = lax.axis_size(axis)
    return lax.ppermute(value, axis, [(i, i ^ bit) for i in range(size)])


def half_of(value, which, dim=0):
    size = value.shape[dim] // 2
    return lax.dynamic_slice_in_dim(value, which * size, size, dim)


def joined(mine, other, which):
    first = jnp.where(which == 0, mine, other)
    second = jnp.where(which == 0, other, mine)
    return jnp.concatenate([first, second], axis=0)


MESH = pl.DeviceIdType.MESH
CHUNKS = 4
TILE = 256
ROWS = 16


def flip(index, bit):
    return index + bit * (1 - 2 * ((index // bit) % 2))


def loop(count, step):
    lax.fori_loop(0, count, lambda i, carry: (step(i), carry)[1], 0)


def middle_kernel(
    w_query_ref,
    w_key_ref,
    w_value_ref,
    w_out_ref,
    tokens_ref,
    cot_ref,
    cot_half_ref,
    gain_one_ref,
    gain_ref,
    w_gate_ref,
    w_up_ref,
    w_down_ref,
    segment_column_ref,
    segment_row_ref,
    cosine_ref,
    sine_ref,
    normed_one_out,
    heads_out,
    query_ref,
    keys_ref,
    values_ref,
    normed_one_far,
    heads_far,
    grad_hidden_out,
    grad_attn_out,
    projected_out,
    grad_attn_far,
    projected_far,
    mixed_half_out,
    mixed_twin_out,
    normed_out,
    activation_out,
    grad_gate_out,
    grad_up_out,
    gain_out,
    cot_others,
    normed_others,
    gate_w,
    up_w,
    down_w,
    cot,
    hidden,
    normed,
    normed_sent,
    normed_twin,
    act,
    gg,
    gu,
    away,
    mine,
    core_in,
    y_in,
    local_sem,
    core_send,
    core_recv,
    y_send,
    y_recv,
    cot_send,
    cot_recv,
    n_send,
    n_recv,
    twin_send,
    twin_recv,
    end_send,
    end_recv,
    hidden_send,
    hidden_recv,
    far_send,
    far_recv,
    log_total_ref,
):
    dp, tensor = lax.axis_index("dp"), lax.axis_index("tensor")
    core = tensor % 2
    twin_id = (dp, flip(tensor, 1))
    y_id = (dp, flip(tensor, 2))
    x_id = (flip(dp, 1), tensor)
    z_id = (flip(dp, 4), tensor)
    far_id = (flip(dp, 2), tensor)
    half, width = hidden.shape
    hidden_units = gate_w.shape[1]
    chunk = half // CHUNKS
    my_row = pl.multiple_of(core * half, half)
    twin_row = pl.multiple_of((1 - core) * half, half)
    row_count = 2 * half
    query_width = w_query_ref.shape[1]
    tiles = width // TILE
    transposed = (((1,), (1,)), ((), ()))
    z_low = (dp // 2) % 2
    heads = gg.at[:, pl.ds(0, query_width)]
    tok = gu

    def remote(src, dst, send, recv, device):
        return pltpu.make_async_remote_copy(
            src_ref=src, dst_ref=dst, send_sem=send, recv_sem=recv,
            device_id=device, device_id_type=MESH,
        )

    loads = {
        "tok": pltpu.make_async_copy(tokens_ref, tok, local_sem.at[0]),
        "query": pltpu.make_async_copy(
            w_query_ref, gate_w.at[:, pl.ds(0, query_width)], local_sem.at[1]
        ),
        "key": pltpu.make_async_copy(
            w_key_ref, gate_w.at[:, pl.ds(query_width, 128)], local_sem.at[2]
        ),
        "value": pltpu.make_async_copy(
            w_value_ref, gate_w.at[:, pl.ds(query_width + 128, 128)], local_sem.at[3]
        ),
        "w_out": pltpu.make_async_copy(w_out_ref, cot, local_sem.at[4]),
        "up": pltpu.make_async_copy(w_up_ref, up_w, local_sem.at[5]),
        "down": pltpu.make_async_copy(w_down_ref, down_w, local_sem.at[6]),
        "gate": pltpu.make_async_copy(w_gate_ref, gate_w, local_sem.at[7]),
        "cot": pltpu.make_async_copy(cot_ref, cot, local_sem.at[8]),
    }
    for name in ("tok", "query", "key", "value", "w_out", "up", "down"):
        loads[name].start()

    barrier = pltpu.get_barrier_semaphore()
    for device in (twin_id, y_id, x_id, z_id, far_id):
        pl.semaphore_signal(barrier, inc=1, device_id=device, device_id_type=MESH)
    pl.semaphore_wait(barrier, 5)

    def rows(k):
        return pl.ds(pl.multiple_of(k * chunk, chunk), chunk)

    def from_x(source, slots, k, send, recv):
        return remote(source.at[rows(k)], slots.at[0, rows(k)], send.at[0, k], recv.at[0, k], x_id)

    def from_z(source, slots, k, send, recv):
        return remote(source.at[rows(k)], slots.at[1, rows(k)], send.at[1, k], recv.at[1, k], z_id)

    def from_zx(slots, k, send, recv):
        return remote(
            slots.at[1, rows(k)], slots.at[2, rows(k)], send.at[2, k], recv.at[2, k], x_id
        )

    def to_twin(slots, which, slot):
        return remote(
            slots.at[slot], slots.at[3 + slot],
            twin_send.at[which, slot], twin_recv.at[which, slot], twin_id,
        )

    def send_z(source, slots, k, send, recv):
        from_z(source, slots, k, send, recv).start()
        from_z(source, slots, k + 1, send, recv).start()

    def relay(source, slots, k, send, recv):
        for i in (k, k + 1):
            from_z(source, slots, i, send, recv).wait_recv()
            from_zx(slots, i, send, recv).start()
            from_z(source, slots, i, send, recv).wait_send()

    send_z(cot_half_ref, cot_others, 0, cot_send, cot_recv)
    for k in range(CHUNKS):
        from_x(cot_half_ref, cot_others, k, cot_send, cot_recv).start()

    def far_columns(b):
        return pl.ds(pl.multiple_of(b * 1024 + (1 - z_low) * 512, 512), 512)

    gain_one = gain_one_ref[...]
    loads["tok"].wait()

    def first_norm(i):
        window = pl.ds(pl.multiple_of(i * ROWS, ROWS), ROWS)
        values = tok[window, :].astype(F32)
        scale = lax.rsqrt(jnp.mean(values * values, axis=-1, keepdims=True) + EPSILON)
        normed[window, :] = (values * scale * gain_one).astype(BF16)

    loop(row_count // ROWS, first_norm)
    normed_one_store = pltpu.make_async_copy(normed, normed_one_out, local_sem.at[9])
    normed_one_store.start()

    def stage_far(i):
        window = pl.ds(pl.multiple_of(i * ROWS, ROWS), ROWS)
        here = pl.ds(pl.multiple_of(my_row + i * ROWS, ROWS), ROWS)
        for b in range(2):
            core_in[2, window, pl.ds(b * 512, 512)] = normed[here, far_columns(b)].astype(F32)

    loop(half // ROWS, stage_far)
    early = pl.ds(0, 1024)
    normed_one_copy = remote(
        core_in.at[2, :, early], normed_one_far.at[0], far_send.at[0], far_recv.at[0], far_id
    )
    normed_one_copy.start()

    lane = lax.broadcasted_iota(jnp.int32, (TILE, 128), 1)
    factor = HEAD_SIZE ** (-0.5)
    everything = slice(None)

    def turn(value):
        return jnp.where(lane % 64 < 32, pltpu.roll(value, 96, 1), pltpu.roll(value, 32, 1))

    def rotate_tile(value, window):
        return value * cosine_ref[window, :] - turn(value) * sine_ref[window, :]

    def unrotate_tile(value, window):
        return value * cosine_ref[window, :] + turn(value) * sine_ref[window, :]

    for name in ("query", "key", "value"):
        loads[name].wait()
    for block in range(2):
        window = pl.ds(block * TILE, TILE)

        def query_tile(j, window=window):
            projection = jnp.dot(
                normed[window, :],
                gate_w[:, pl.ds(pl.multiple_of(j * TILE, TILE), TILE)],
                preferred_element_type=F32,
            )
            for part in range(2):
                act[window, pl.ds(pl.multiple_of(j * TILE + part * 128, 128), 128)] = rotate_tile(
                    projection[:, part * 128 : (part + 1) * 128], window
                ).astype(BF16)

        loop(query_width // TILE, query_tile)
        projection = jnp.dot(
            normed[window, :], gate_w[:, pl.ds(query_width, TILE)], preferred_element_type=F32
        )
        for base, value in (
            (1024, rotate_tile(projection[:, :128], window)),
            (1536, projection[:, 128:]),
        ):
            other = pltpu.roll(value, 64, 1)
            halves_of = (
                jnp.where(lane < 64, value, 0.0),
                jnp.where(lane >= 64, other, 0.0),
                jnp.where(lane < 64, other, 0.0),
                jnp.where(lane >= 64, value, 0.0),
            )
            for i, padded in enumerate(halves_of):
                act[window, pl.ds(base + i * 128, 128)] = padded.astype(BF16)
    normed_one_store.wait()
    loads["gate"].start()
    keeps = [
        pltpu.make_async_copy(act.at[:, pl.ds(0, 512)], query_ref, local_sem.at[0]),
        pltpu.make_async_copy(act.at[:, pl.ds(1024, 512)], keys_ref, local_sem.at[1]),
        pltpu.make_async_copy(act.at[:, pl.ds(1536, 512)], values_ref, local_sem.at[2]),
    ]
    for keep in keeps:
        keep.start()

    def allowed_of(block):
        keys_seen = (block + 1) * TILE
        window = pl.ds(block * TILE, TILE)
        key_place = lax.broadcasted_iota(jnp.int32, (keys_seen, TILE), 0)
        query_place = lax.broadcasted_iota(jnp.int32, (keys_seen, TILE), 1) + block * TILE
        return (key_place <= query_place) & (
            segment_column_ref[pl.ds(0, keys_seen), :] == segment_row_ref[:, window]
        )

    def forward_pair(p):
        kv = p // 2
        column = pl.multiple_of(p * 128, 128)
        for block in range(2):
            window = pl.ds(block * TILE, TILE)
            seen = pl.ds(0, (block + 1) * TILE)
            queries = act[window, pl.ds(column, 128)]
            allowed = allowed_of(block)
            result = jnp.zeros((TILE, 128), F32)
            for side in range(2):
                padded = pl.multiple_of((kv * 2 + side) * 128, 128)
                keys = act[seen, pl.ds(pl.multiple_of(1024 + padded, 128), 128)]
                vals = act[seen, pl.ds(pl.multiple_of(1536 + padded, 128), 128)]
                raw = jnp.where(
                    allowed,
                    lax.dot_general(keys, queries, transposed, preferred_element_type=F32)
                    * factor,
                    MASKED,
                )
                peak = jnp.max(raw, axis=0, keepdims=True)
                lifted = jnp.exp(raw - peak)
                summed = jnp.sum(lifted, axis=0, keepdims=True)
                log_total_ref[pl.ds(2 * p + side, 1), window] = peak + jnp.log(summed)
                result = result + lax.dot_general(
                    (lifted * (1.0 / summed)).astype(BF16), vals, (((0,), (0,)), ((), ())),
                    preferred_element_type=F32,
                )
            heads[window, pl.ds(column, 128)] = result.astype(BF16)

    loop(4, forward_pair)
    heads_store = pltpu.make_async_copy(heads, heads_out, local_sem.at[3])
    heads_store.start()

    loads["w_out"].wait()

    def project(into, first_row):
        def step(j):
            columns = pl.ds(pl.multiple_of(j * TILE, TILE), TILE)
            into[:, columns] = jnp.dot(
                heads[pl.ds(first_row, half), :], cot[:, columns], preferred_element_type=F32
            )

        loop(width // TILE, step)

    def core_copy(which, window, k):
        return remote(
            away.at[window], core_in.at[which].at[window],
            core_send.at[which, k], core_recv.at[which, k], twin_id,
        )

    def y_copy(which, window, k):
        return remote(
            mine.at[which % 2].at[window], y_in.at[which % 2].at[window],
            y_send.at[which, k], y_recv.at[which, k], y_id,
        )

    row_windows = [(rows(k), everything) for k in range(CHUNKS)]

    def column_window(j):
        return (everything, pl.ds(pl.multiple_of(j * TILE, TILE), TILE))

    project(away, twin_row)
    for k in range(CHUNKS):
        core_copy(0, row_windows[k], k).start()
    project(mine.at[0], my_row)
    loads["cot"].start()
    for k in range(CHUNKS):
        core_copy(0, row_windows[k], k).wait_recv()

        def add(i, k=k):
            window = pl.ds(pl.multiple_of(k * chunk + i * ROWS, ROWS), ROWS)
            mine[0, window, :] = mine[0, window, :] + core_in[0, window, :]

        loop(chunk // ROWS, add)
        y_copy(0, row_windows[k], k).start()

    def stage_heads(i):
        window = pl.ds(pl.multiple_of(i * ROWS, ROWS), ROWS)
        for b in range(2):
            here = pl.ds(pl.multiple_of(b * half + i * ROWS, ROWS), ROWS)
            mine[1, window, pl.ds(b * 512, 512)] = heads[here, :].astype(F32)

    loop(half // ROWS, stage_heads)
    heads_copy = remote(
        mine.at[1, :, early], heads_far, far_send.at[1], far_recv.at[1], far_id
    )
    heads_copy.start()
    gain = gain_ref[...]
    for k in range(CHUNKS):
        y_copy(0, row_windows[k], k).wait_recv()

        def normalize_rows(i, k=k):
            offset = pl.multiple_of(k * chunk + i * ROWS, ROWS)
            window = pl.ds(offset, ROWS)
            own = tok[pl.ds(pl.multiple_of(my_row + offset, ROWS), ROWS), :].astype(F32)
            values = own + (mine[0, window, :] + y_in[0, window, :])
            scale = lax.rsqrt(jnp.mean(values * values, axis=-1, keepdims=True) + EPSILON)
            rounded = (values * scale * gain).astype(BF16)
            hidden[window, :] = values
            normed[pl.ds(pl.multiple_of(my_row + offset, ROWS), ROWS), :] = rounded
            normed_sent[window, :] = rounded.astype(F32)

        loop(chunk // ROWS, normalize_rows)
        remote(
            normed_sent.at[rows(k)], normed_twin.at[rows(k)],
            n_send.at[3, k], n_recv.at[3, k], twin_id,
        ).start()
        if k == 2:
            relay(cot_half_ref, cot_others, 0, cot_send, cot_recv)
            send_z(cot_half_ref, cot_others, 2, cot_send, cot_recv)
        from_x(normed_sent, normed_others, k, n_send, n_recv).start()
    for k in range(CHUNKS):
        remote(
            normed_sent.at[rows(k)], normed_twin.at[rows(k)],
            n_send.at[3, k], n_recv.at[3, k], twin_id,
        ).wait_recv()

        def take(i, k=k):
            offset = pl.multiple_of(k * chunk + i * ROWS, ROWS)
            normed[pl.ds(pl.multiple_of(twin_row + offset, ROWS), ROWS), :] = normed_twin[
                pl.ds(offset, ROWS), :
            ].astype(BF16)

        loop(chunk // ROWS, take)

    for name in ("cot", "gate", "up", "down"):
        loads[name].wait()
    for keep in keeps + [heads_store]:
        keep.wait()

    def units(j):
        columns = pl.ds(pl.multiple_of(j * TILE, TILE), TILE)
        gate = jnp.dot(normed[...], gate_w[:, columns], preferred_element_type=F32)
        up = jnp.dot(normed[...], up_w[:, columns], preferred_element_type=F32)
        back = lax.dot_general(
            cot[...], down_w[columns, :], (((1,), (1,)), ((), ())), preferred_element_type=F32
        )
        sigmoid = jax.nn.sigmoid(gate)
        swish = gate * sigmoid
        act[:, columns] = (swish * up).astype(BF16)
        gg[:, columns] = (back * up * sigmoid * (1.0 + gate * (1.0 - sigmoid))).astype(BF16)
        gu[:, columns] = (back * swish).astype(BF16)

    loop(hidden_units // TILE, units)

    for k in range(CHUNKS):
        core_copy(0, row_windows[k], k).wait_send()
    normed_one_copy.wait()
    heads_copy.wait()
    normed_one_twin = remote(
        normed_one_far.at[0], normed_one_far.at[1], far_send.at[2], far_recv.at[2], twin_id
    )
    normed_one_twin.start()

    def column_sums(which, tile_product, forwarded=True):
        def produce(j):
            value = tile_product(j)
            columns = pl.ds(pl.multiple_of(j * TILE, TILE), TILE)
            away[:, columns] = value[0]
            mine[which % 2, :, columns] = value[1]
            core_copy(which, column_window(j), j).start()

        def forward(j):
            core_copy(which, column_window(j), j).wait_recv()
            columns = pl.ds(pl.multiple_of(j * TILE, TILE), TILE)
            mine[which % 2, :, columns] = (
                mine[which % 2, :, columns] + core_in[which, :, columns]
            )
            if forwarded:
                y_copy(which, column_window(j), j).start()

        produce(0)

        def step(j):
            produce(j + 1)
            forward(j)

        loop(tiles - 1, step)
        forward(tiles - 1)

    def halves(dot_of):
        return dot_of(pl.ds(twin_row, half)), dot_of(pl.ds(my_row, half))

    def back_tile(j):
        columns = pl.ds(pl.multiple_of(j * TILE, TILE), TILE)
        return halves(
            lambda part: lax.dot_general(
                gg[part, :], gate_w[columns, :], transposed, preferred_element_type=F32
            )
            + lax.dot_general(
                gu[part, :], up_w[columns, :], transposed, preferred_element_type=F32
            )
        )

    def branch_tile(j):
        columns = pl.ds(pl.multiple_of(j * TILE, TILE), TILE)
        return halves(
            lambda part: jnp.dot(act[part, :], down_w[:, columns], preferred_element_type=F32)
        )

    column_sums(1, back_tile)
    stores = [
        pltpu.make_async_copy(normed, normed_out, local_sem.at[7]),
        pltpu.make_async_copy(act, activation_out, local_sem.at[8]),
        pltpu.make_async_copy(gg, grad_gate_out, local_sem.at[9]),
        pltpu.make_async_copy(gu, grad_up_out, local_sem.at[10]),
    ]
    for store in stores:
        store.start()
    relay(cot_half_ref, cot_others, 2, cot_send, cot_recv)
    send_z(normed_sent, normed_others, 0, n_send, n_recv)
    loop(tiles, lambda j: core_copy(1, column_window(j), j).wait_send())
    for k in range(CHUNKS):
        y_copy(0, row_windows[k], k).wait_send()
    column_sums(2, branch_tile, forwarded=False)
    for k in range(CHUNKS):
        from_x(cot_half_ref, cot_others, k, cot_send, cot_recv).wait_recv()
    to_twin(cot_others, 0, 0).start()
    to_twin(cot_others, 0, 1).start()

    for store in stores:
        store.wait()
    operands = [
        pltpu.make_async_copy(query_ref, act.at[:, pl.ds(0, 512)], local_sem.at[0]),
        pltpu.make_async_copy(keys_ref, act.at[:, pl.ds(1024, 512)], local_sem.at[1]),
        pltpu.make_async_copy(values_ref, act.at[:, pl.ds(1536, 512)], local_sem.at[2]),
        pltpu.make_async_copy(w_out_ref, gate_w.at[pl.ds(0, 512)], local_sem.at[3]),
    ]
    for operand in operands:
        operand.start()

    loop(tiles, lambda j: y_copy(1, column_window(j), j).wait_recv())
    loop(tiles, lambda j: y_copy(2, column_window(j), j).start())
    gain_out[...] = jnp.zeros_like(gain_out)

    def hidden_copy(k):
        return remote(
            core_in.at[0, rows(k)], normed_twin.at[rows(k)],
            hidden_send.at[k], hidden_recv.at[k], twin_id,
        )

    for k in range(CHUNKS):

        def norm_rows(i, k=k):
            offset = pl.multiple_of(k * chunk + i * ROWS, ROWS)
            window = pl.ds(offset, ROWS)
            incoming = mine[1, window, :] + y_in[1, window, :]
            values = hidden[window, :]
            scale = lax.rsqrt(jnp.mean(values * values, axis=-1, keepdims=True) + EPSILON)
            weighted = incoming * gain
            inner = jnp.mean(weighted * values, axis=-1, keepdims=True)
            back = scale * weighted - values * (scale * scale * scale) * inner
            here = pl.ds(pl.multiple_of(my_row + offset, ROWS), ROWS)
            total = cot[here, :].astype(F32) + back
            core_in[0, window, :] = total
            normed[here, :] = total.astype(BF16)
            gain_out[...] = gain_out[...] + jnp.sum(
                incoming * values * scale, axis=0, keepdims=True
            )

        loop(chunk // ROWS, norm_rows)
        hidden_copy(k).start()
    hidden_store = pltpu.make_async_copy(core_in.at[0], grad_hidden_out, local_sem.at[4])
    hidden_store.start()
    relay(normed_sent, normed_others, 0, n_send, n_recv)
    send_z(normed_sent, normed_others, 2, n_send, n_recv)
    for k in range(CHUNKS):
        hidden_copy(k).wait_recv()

        def take_hidden(i, k=k):
            offset = pl.multiple_of(k * chunk + i * ROWS, ROWS)
            normed[pl.ds(pl.multiple_of(twin_row + offset, ROWS), ROWS), :] = normed_twin[
                pl.ds(offset, ROWS), :
            ].astype(BF16)

        loop(chunk // ROWS, take_hidden)
    grad_attn_store = pltpu.make_async_copy(normed, grad_attn_out, local_sem.at[5])
    grad_attn_store.start()

    hidden_far = [
        remote(
            core_in.at[0, :, far_columns(b)], grad_attn_far.at[0, :, pl.ds(b * 512, 512)],
            far_send.at[3 + b], far_recv.at[3 + b], far_id,
        )
        for b in range(2)
    ]
    for copy in hidden_far:
        copy.start()

    for operand in operands:
        operand.wait()

    def head_tile(j):
        columns = pl.ds(pl.multiple_of(j * TILE, TILE), TILE)
        act[:, pl.ds(pl.multiple_of(512 + j * TILE, TILE), TILE)] = lax.dot_general(
            normed[...], gate_w[columns, :], transposed, preferred_element_type=F32
        ).astype(BF16)

    loop(512 // TILE, head_tile)
    sums = y_in.at[1]
    sums[:, pl.ds(0, 1024)] = jnp.zeros((TILE, 1024), F32)

    def gather_into(offset, kv, value):
        for part in range(value.shape[0] // TILE):
            columns = pl.ds(pl.multiple_of(offset + kv * 256 + part * 128, 128), 128)
            sums[:, columns] = sums[:, columns] + value[part * TILE : (part + 1) * TILE]

    def put(block, column, value):
        rounded = value.astype(BF16)
        gu[pl.ds(block * TILE, TILE), pl.ds(column, 128)] = rounded
        core_in[1, :, pl.ds(block * 768 + column, 128)] = rounded.astype(F32)

    def pair(p):
        kv = p // 2
        column = pl.multiple_of(p * 128, 128)
        for block in range(2):
            keys_seen = (block + 1) * TILE
            window = pl.ds(block * TILE, TILE)
            seen = pl.ds(0, keys_seen)
            queries = act[window, pl.ds(column, 128)]
            upstream = act[window, pl.ds(pl.multiple_of(512 + column, 128), 128)]
            allowed = allowed_of(block)
            query_grad = jnp.zeros((TILE, 128), F32)
            for side in range(2):
                padded = pl.multiple_of((kv * 2 + side) * 128, 128)
                keys = act[seen, pl.ds(pl.multiple_of(1024 + padded, 128), 128)]
                vals = act[seen, pl.ds(pl.multiple_of(1536 + padded, 128), 128)]
                raw = lax.dot_general(
                    keys, queries, transposed, preferred_element_type=F32
                ) * factor
                log_total = log_total_ref[pl.ds(2 * p + side, 1), window]
                probs = jnp.exp(jnp.where(allowed, raw - log_total, MASKED))
                grad_probs = lax.dot_general(
                    vals, upstream, transposed, preferred_element_type=F32
                )
                row_sum = jnp.sum(probs * grad_probs, axis=0, keepdims=True)
                grad_raw = (probs * (grad_probs - row_sum)).astype(BF16)
                query_grad = query_grad + lax.dot_general(
                    grad_raw, keys, (((0,), (0,)), ((), ())), preferred_element_type=F32
                )
                own = (lax.broadcasted_iota(jnp.int32, (keys_seen, 128), 1) // 64) == side
                gather_into(0, kv, jnp.where(
                    own, jnp.dot(grad_raw, queries, preferred_element_type=F32), 0.0
                ))
                gather_into(512, kv, jnp.where(
                    own, jnp.dot(probs.astype(BF16), upstream, preferred_element_type=F32), 0.0
                ))
            put(block, column, unrotate_tile(query_grad * factor, window))

    loop(4, pair)

    def both(offset, block):
        def folded(kv):
            value = sums[:, pl.ds(offset + kv * 256 + block * 128, 128)]
            return value + pltpu.roll(value, 64, 1)

        return jnp.where(lane < 64, folded(0), folded(1))

    for block in range(2):
        window = pl.ds(block * TILE, TILE)
        put(block, 512, unrotate_tile(both(0, block) * factor, window))
        put(block, 640, both(512, block))
    projected_store = pltpu.make_async_copy(
        gu.at[:, pl.ds(0, 768)], projected_out, local_sem.at[6]
    )
    projected_store.start()

    projected_copy = remote(
        core_in.at[1, :, pl.ds(0, 1536)], projected_far, far_send.at[5], far_recv.at[5], far_id
    )
    projected_copy.start()
    for copy in hidden_far:
        copy.wait_recv()
    hidden_far_twin = remote(
        grad_attn_far.at[0], grad_attn_far.at[1], far_send.at[7], far_recv.at[7], twin_id
    )
    hidden_far_twin.start()

    for k in range(CHUNKS):
        from_x(normed_sent, normed_others, k, n_send, n_recv).wait_recv()
    to_twin(normed_others, 1, 0).start()
    for k in range(CHUNKS):
        from_zx(cot_others, k, cot_send, cot_recv).wait_recv()
    to_twin(cot_others, 0, 2).start()
    relay(normed_sent, normed_others, 2, n_send, n_recv)
    to_twin(normed_others, 1, 1).start()

    loop(tiles, lambda j: y_copy(2, column_window(j), j).wait_recv())
    loop(tiles, lambda j: y_copy(2, column_window(j), j).wait_send())

    def mixed_rows(i):
        window = pl.ds(pl.multiple_of(i * ROWS, ROWS), ROWS)
        mine[0, window, :] = hidden[window, :] + (mine[0, window, :] + y_in[0, window, :])

    loop(half // ROWS, mixed_rows)
    mixed_copy = remote(
        mine.at[0], mixed_twin_out, end_send.at[1], end_recv.at[1], twin_id
    )
    mixed_copy.start()
    mixed_store = pltpu.make_async_copy(mine.at[0], mixed_half_out, local_sem.at[12])
    mixed_store.start()
    for k in range(CHUNKS):
        from_zx(normed_others, k, n_send, n_recv).wait_recv()
    to_twin(normed_others, 1, 2).start()

    for store in (hidden_store, grad_attn_store, projected_store, mixed_store):
        store.wait()
    mixed_copy.wait()
    for copy in hidden_far:
        copy.wait_send()
    for copy in (hidden_far_twin, normed_one_twin, projected_copy):
        copy.wait()
    for k in range(CHUNKS):
        hidden_copy(k).wait_send()
        from_x(cot_half_ref, cot_others, k, cot_send, cot_recv).wait_send()
        from_x(normed_sent, normed_others, k, n_send, n_recv).wait_send()
        from_zx(cot_others, k, cot_send, cot_recv).wait_send()
        from_zx(normed_others, k, n_send, n_recv).wait_send()
        remote(
            normed_sent.at[rows(k)], normed_twin.at[rows(k)],
            n_send.at[3, k], n_recv.at[3, k], twin_id,
        ).wait_send()
    loop(tiles, lambda j: y_copy(1, column_window(j), j).wait_send())
    loop(tiles, lambda j: core_copy(2, column_window(j), j).wait_send())
    for slot in range(3):
        to_twin(cot_others, 0, slot).wait()
        to_twin(normed_others, 1, slot).wait()


def middle(
    w_query, w_key, w_value, w_out, tokens, cotangent, cotangent_half, gain_one, gain,
    w_gate, w_up, w_down, segment, cosine, sine,
):
    row_count, width = tokens.shape
    half = row_count // 2
    hidden_units = w_gate.shape[1]
    tiles = width // TILE
    hbm = pl.BlockSpec(memory_space=pl.ANY)
    vmem = pl.BlockSpec(memory_space=pltpu.VMEM)
    wide = jax.ShapeDtypeStruct((half, width), F32)
    units = jax.ShapeDtypeStruct((row_count, hidden_units), BF16)
    square = jax.ShapeDtypeStruct((row_count, 512), BF16)
    dma = pltpu.SemaphoreType.DMA
    return pl.pallas_call(
        middle_kernel,
        out_shape=(
            jax.ShapeDtypeStruct((row_count, width), BF16),
            square, square, square, square,
            jax.ShapeDtypeStruct((2, half, width // 2), F32),
            jax.ShapeDtypeStruct((half, width // 2), F32),
            wide,
            jax.ShapeDtypeStruct((row_count, width), BF16),
            jax.ShapeDtypeStruct((row_count, 768), BF16),
            jax.ShapeDtypeStruct((2, half, width // 2), F32),
            jax.ShapeDtypeStruct((half, 2 * 768), F32),
            wide, wide,
            jax.ShapeDtypeStruct((row_count, width), BF16),
            units, units, units,
            jax.ShapeDtypeStruct((1, width), F32),
            jax.ShapeDtypeStruct((6, half, width), F32),
            jax.ShapeDtypeStruct((6, half, width), F32),
        ),
        in_specs=[hbm] * 7 + [vmem] * 2 + [hbm] * 3 + [vmem] * 4,
        out_specs=(hbm,) * 18 + (vmem,) + (hbm,) * 2,
        scratch_shapes=[
            pltpu.VMEM(w_gate.shape, BF16),
            pltpu.VMEM(w_up.shape, BF16),
            pltpu.VMEM(w_down.shape, BF16),
            pltpu.VMEM((row_count, width), BF16),
            pltpu.VMEM((half, width), F32),
            pltpu.VMEM((row_count, width), BF16),
            pltpu.VMEM((half, width), F32),
            pltpu.VMEM((half, width), F32),
            pltpu.VMEM((row_count, hidden_units), BF16),
            pltpu.VMEM((row_count, hidden_units), BF16),
            pltpu.VMEM((row_count, hidden_units), BF16),
            pltpu.VMEM((half, width), F32),
            pltpu.VMEM((2, half, width), F32),
            pltpu.VMEM((3, half, width), F32),
            pltpu.VMEM((2, half, width), F32),
            dma((13,)),
            dma((3, tiles)), dma((3, tiles)), dma((3, tiles)), dma((3, tiles)),
            dma((3, CHUNKS)), dma((3, CHUNKS)),
            dma((4, CHUNKS)), dma((4, CHUNKS)),
            dma((2, 3)), dma((2, 3)),
            dma((2,)), dma((2,)),
            dma((CHUNKS,)), dma((CHUNKS,)),
            dma((8,)), dma((8,)),
            pltpu.VMEM((8, row_count), F32),
        ],
        compiler_params=pltpu.CompilerParams(
            collective_id=0, has_side_effects=True, vmem_limit_bytes=64 * 1024 * 1024
        ),
        name="feed_forward",
    )(
        w_query, w_key, w_value, w_out, tokens, cotangent, cotangent_half,
        gain_one.reshape(1, width), gain.reshape(1, width), w_gate, w_up, w_down,
        segment.reshape(row_count, 1), segment.reshape(1, row_count), cosine, sine,
    )


def last_kernel(
    normed_others_ref,
    cot_others_ref,
    normed_ref,
    cot_ref,
    act_ref,
    gg_ref,
    gu_ref,
    w_gate_ref,
    w_up_ref,
    w_down_ref,
    projected_ref,
    projected_far_ref,
    w_query_ref,
    w_key_ref,
    w_value_ref,
    heads_ref,
    grad_attn_ref,
    grad_attn_far_ref,
    normed_one_ref,
    normed_one_far_ref,
    heads_far_ref,
    grad_hidden_ref,
    tokens_ref,
    gain_ref,
    kept_out,
    sent_out,
    came_out,
    out_mine,
    out_came,
    proj_mine,
    proj_came,
    input_half_out,
    input_twin_out,
    gain_out,
    normed,
    cot,
    normed_t,
    cot_t,
    units,
    gate_w,
    up_w,
    down_w,
    total,
    staged,
    core_in,
    y_in,
    w_proj,
    tok,
    heads,
    grad_attn,
    normed_one,
    projected,
    out_part,
    proj_part,
    out_x,
    proj_x,
    own_columns,
    far_staged,
    far_heads,
    load_sem,
    piece_sem,
    weight_sem,
    unit_sem,
    store_sem,
    row_send,
    row_recv,
    core_send,
    core_recv,
    y_send,
    y_recv,
    x_send,
    x_recv,
    z_send,
    z_recv,
    end_send,
    end_recv,
):
    dp, tensor = lax.axis_index("dp"), lax.axis_index("tensor")
    core = tensor % 2
    x_low, z_low, z_high = dp % 2, (dp // 2) % 2, dp // 4
    twin_id = (dp, flip(tensor, 1))
    y_id = (dp, flip(tensor, 2))
    x_id = (flip(dp, 1), tensor)
    z_id = (flip(dp, 4), tensor)
    far_id = (flip(dp, 2), tensor)
    half, width = tok.shape
    row_count = 2 * half
    tiles = width // TILE
    my_row = pl.multiple_of(core * half, half)
    twin_row = pl.multiple_of((1 - core) * half, half)
    everything = slice(None)
    transposed = (((1,), (1,)), ((), ()))
    over = (((0,), (0,)), ((), ()))

    def remote(src, dst, send, recv, device):
        return pltpu.make_async_remote_copy(
            src_ref=src, dst_ref=dst, send_sem=send, recv_sem=recv,
            device_id=device, device_id_type=MESH,
        )

    def tile_of(j):
        return pl.ds(pl.multiple_of(j * TILE, TILE), TILE)

    away_block = tile_of(flip(dp, 2))
    home_block = tile_of(dp)
    near = [
        pl.ds(pl.multiple_of(b * 1024 + z_low * 512, 512), 512) for b in range(2)
    ]
    loads = [
        pltpu.make_async_copy(normed_ref.at[:, away_block], own_columns.at[0], load_sem.at[0]),
        pltpu.make_async_copy(normed_ref.at[:, home_block], own_columns.at[1], load_sem.at[1]),
        pltpu.make_async_copy(cot_ref.at[:, away_block], own_columns.at[2], load_sem.at[2]),
        pltpu.make_async_copy(cot_ref.at[:, home_block], own_columns.at[3], load_sem.at[3]),
        pltpu.make_async_copy(w_query_ref, w_proj.at[:, pl.ds(0, 512)], load_sem.at[4]),
        pltpu.make_async_copy(w_key_ref, w_proj.at[:, pl.ds(512, 128)], load_sem.at[5]),
        pltpu.make_async_copy(w_value_ref, w_proj.at[:, pl.ds(640, 128)], load_sem.at[6]),
        pltpu.make_async_copy(tokens_ref.at[pl.ds(my_row, half)], tok, load_sem.at[7]),
        pltpu.make_async_copy(heads_ref, heads.at[0], load_sem.at[8]),
        pltpu.make_async_copy(
            grad_attn_ref.at[:, near[0]], grad_attn.at[0, :, pl.ds(0, 512)], load_sem.at[9]
        ),
        pltpu.make_async_copy(
            grad_attn_ref.at[:, near[1]], grad_attn.at[0, :, pl.ds(512, 512)], load_sem.at[10]
        ),
        pltpu.make_async_copy(
            normed_one_ref.at[:, near[0]], normed_one.at[0, :, pl.ds(0, 512)], load_sem.at[11]
        ),
        pltpu.make_async_copy(
            normed_one_ref.at[:, near[1]], normed_one.at[0, :, pl.ds(512, 512)], load_sem.at[12]
        ),
        pltpu.make_async_copy(projected_ref, projected.at[0], load_sem.at[13]),
    ]

    def piece_load(i, slot):
        source = normed_others_ref.at[i] if i < 6 else cot_others_ref.at[i - 6]
        return pltpu.make_async_copy(source, staged.at[slot], piece_sem.at[slot])

    def weight_loads(j, slot):
        return [
            pltpu.make_async_copy(
                w_gate_ref.at[:, tile_of(j)], gate_w.at[slot], weight_sem.at[slot, 0]
            ),
            pltpu.make_async_copy(
                w_up_ref.at[:, tile_of(j)], up_w.at[slot], weight_sem.at[slot, 1]
            ),
            pltpu.make_async_copy(
                w_down_ref.at[tile_of(j), :], down_w.at[slot], weight_sem.at[slot, 2]
            ),
        ]

    piece_load(0, 0).start()
    piece_load(1, 1).start()
    for load in loads[:4]:
        load.start()
    for load in weight_loads(0, 0):
        load.start()

    barrier = pltpu.get_barrier_semaphore()
    for device in (twin_id, y_id, x_id, z_id, far_id):
        pl.semaphore_signal(barrier, inc=1, device_id=device, device_id_type=MESH)
    pl.semaphore_wait(barrier, 5)

    for i in range(12):
        piece_load(i, i % 2).wait()
        rows_to, turned_to = (normed, normed_t) if i < 6 else (cot, cot_t)
        base = (i % 6) * half

        def convert(r, i=i, rows_to=rows_to, base=base):
            window = pl.ds(pl.multiple_of(r * ROWS, ROWS), ROWS)
            rows_to[pl.ds(pl.multiple_of(base + r * ROWS, ROWS), ROWS), :] = staged[
                i % 2, window, :
            ].astype(BF16)

        loop(half // ROWS, convert)
        for part, block in enumerate((away_block, home_block)):
            turned_to[pl.ds(part * TILE, TILE), pl.ds(row_count + base, half)] = (
                staged[i % 2, :, block].T.astype(BF16)
            )
        if i + 2 < 12:
            piece_load(i + 2, i % 2).start()
    for part in range(4):
        loads[part].wait()
        turned_to = (normed_t, cot_t)[part // 2]
        turned_to[pl.ds((part % 2) * TILE, TILE), pl.ds(0, row_count)] = (
            own_columns[part].astype(F32).T.astype(BF16)
        )

    for load in loads[4:]:
        load.start()
    far_loads = (
        [
            pltpu.make_async_copy(
                grad_attn_far_ref.at[s], staged.at[0, :, pl.ds(s * 1024, 1024)], piece_sem.at[s]
            )
            for s in range(2)
        ]
        + [
            pltpu.make_async_copy(
                normed_one_far_ref.at[s], staged.at[1, :, pl.ds(s * 1024, 1024)],
                piece_sem.at[2 + s],
            )
            for s in range(2)
        ]
        + [
            pltpu.make_async_copy(projected_far_ref, far_staged, piece_sem.at[4]),
            pltpu.make_async_copy(heads_far_ref, far_heads, piece_sem.at[5]),
        ]
    )
    for load in far_loads:
        load.start()

    def row_copy(j):
        window = (everything, everything, tile_of(j))
        return remote(
            sent_out.at[window], came_out.at[window], row_send.at[j], row_recv.at[j], far_id
        )

    def stores(j, slot):
        return [
            pltpu.make_async_copy(
                total.at[slot, :, pl.ds(0, TILE)], sent_out.at[:, :, tile_of(j)],
                store_sem.at[slot, 0],
            ),
            pltpu.make_async_copy(
                total.at[slot, :, pl.ds(TILE, TILE)], kept_out.at[:, :, tile_of(j)],
                store_sem.at[slot, 1],
            ),
        ]

    def unit_loads(j):
        return [
            pltpu.make_async_copy(
                source.at[:, tile_of(j)], units.at[i, pl.ds(0, row_count)], unit_sem.at[i]
            )
            for i, source in enumerate((gg_ref, gu_ref, act_ref))
        ]

    def feed_forward_tile(j):
        slot = j % 2
        for load in weight_loads(j, slot):
            load.wait()

        @pl.when(j + 1 < tiles)
        def _():
            for load in weight_loads(j + 1, 1 - slot):
                load.start()

        for load in unit_loads(j):
            load.start()

        def block(m):
            rows = pl.ds(pl.multiple_of(m * 512, 512), 512)
            to = pl.ds(pl.multiple_of(row_count + m * 512, 512), 512)
            gate = jnp.dot(normed[rows, :], gate_w[slot], preferred_element_type=F32)
            up = jnp.dot(normed[rows, :], up_w[slot], preferred_element_type=F32)
            back = lax.dot_general(
                cot[rows, :], down_w[slot], transposed, preferred_element_type=F32
            )
            sigmoid = jax.nn.sigmoid(gate)
            swish = gate * sigmoid
            units[2, to, :] = (swish * up).astype(BF16)
            units[0, to, :] = (back * up * sigmoid * (1.0 + gate * (1.0 - sigmoid))).astype(BF16)
            units[1, to, :] = (back * swish).astype(BF16)

        loop(normed.shape[0] // 512, block)
        for load in unit_loads(j):
            load.wait()

        @pl.when(j >= 1)
        def _():
            for store in stores(j - 1, 1 - slot):
                store.wait()
            row_copy(j - 1).start()

        total[slot, 0] = jnp.dot(normed_t[...], units[0], preferred_element_type=F32)
        total[slot, 1] = jnp.dot(normed_t[...], units[1], preferred_element_type=F32)
        total[slot, 2] = jnp.dot(cot_t[...], units[2], preferred_element_type=F32)
        for store in stores(j, slot):
            store.start()

    def x_copies(slot):
        return [
            remote(out_part.at[0, slot], out_x.at[slot], x_send.at[0, slot],
                   x_recv.at[0, slot], x_id),
            remote(proj_part.at[0, slot], proj_x.at[slot], x_send.at[1, slot],
                   x_recv.at[1, slot], x_id),
        ]

    def attention_parts():
        for load in far_loads + loads[8:]:
            load.wait()

        def convert(r):
            window = pl.ds(pl.multiple_of(r * ROWS, ROWS), ROWS)
            for s in range(2):
                start = my_row if s == 0 else twin_row
                here = pl.ds(pl.multiple_of(start + r * ROWS, ROWS), ROWS)
                grad_attn[1, here, :] = staged[0, window, pl.ds(s * 1024, 1024)].astype(BF16)
                normed_one[1, here, :] = staged[1, window, pl.ds(s * 1024, 1024)].astype(BF16)
                there = pl.ds(pl.multiple_of(s * half + r * ROWS, ROWS), ROWS)
                projected[1, there, :] = far_staged[window, pl.ds(s * 768, 768)].astype(BF16)
                heads[1, there, :] = far_heads[window, pl.ds(s * 512, 512)].astype(BF16)

        loop(half // ROWS, convert)
        for side in range(2):
            x_at = 1 - x_low if side == 0 else x_low
            for slot in range(2):
                z_at = 1 - z_high if slot == 0 else z_high
                columns = pl.ds(pl.multiple_of(z_at * 512 + x_at * 256, 256), 256)
                out_part[side, slot] = lax.dot_general(
                    heads[0], grad_attn[0, :, columns], over, preferred_element_type=F32
                ) + lax.dot_general(
                    heads[1], grad_attn[1, :, columns], over, preferred_element_type=F32
                )
                proj_part[side, slot] = lax.dot_general(
                    normed_one[0, :, columns], projected[0], over, preferred_element_type=F32
                ) + lax.dot_general(
                    normed_one[1, :, columns], projected[1], over, preferred_element_type=F32
                )
                if side == 0:
                    for copy in x_copies(slot):
                        copy.start()

    def core_copy(j):
        window = (everything, tile_of(j))
        return remote(
            staged.at[0].at[window], core_in.at[window], core_send.at[j], core_recv.at[j], twin_id
        )

    def y_copy(j):
        window = (everything, tile_of(j))
        return remote(
            staged.at[1].at[window], y_in.at[window], y_send.at[j], y_recv.at[j], y_id
        )

    def attention_sums():
        for load in loads[4:8]:
            load.wait()

        def produce(j):
            weight = w_proj[tile_of(j), :]
            for slot, start in ((0, twin_row), (1, my_row)):
                staged[slot, :, tile_of(j)] = lax.dot_general(
                    projected[0, pl.ds(start, half), :], weight, transposed,
                    preferred_element_type=F32,
                )
            core_copy(j).start()

        def forward(j):
            core_copy(j).wait_recv()
            staged[1, :, tile_of(j)] = staged[1, :, tile_of(j)] + core_in[:, tile_of(j)]
            y_copy(j).start()

        produce(0)

        def step(j):
            produce(j + 1)
            forward(j)

        loop(tiles - 1, step)
        forward(tiles - 1)
        loop(tiles, lambda j: core_copy(j).wait_send())

    def step(j):
        feed_forward_tile(j)

        @pl.when(j == 1)
        def _():
            attention_parts()
            attention_sums()

    loop(tiles, step)
    hidden_load = pltpu.make_async_copy(grad_hidden_ref, core_in, load_sem.at[0])
    hidden_load.start()
    for store in stores(tiles - 1, (tiles - 1) % 2):
        store.wait()
    row_copy(tiles - 1).start()

    def z_copies():
        return [
            remote(out_part.at[1, 0], out_came, z_send.at[0], z_recv.at[0], z_id),
            remote(proj_part.at[1, 0], proj_came, z_send.at[1], z_recv.at[1], z_id),
        ]

    for slot in range(2):
        for copy in x_copies(slot):
            copy.wait_recv()
        out_part[1, slot] = out_part[1, slot] + out_x[slot]
        proj_part[1, slot] = proj_part[1, slot] + proj_x[slot]
        if slot == 0:
            for copy in z_copies():
                copy.start()
    part_stores = [
        pltpu.make_async_copy(out_part.at[1, 1], out_mine, load_sem.at[1]),
        pltpu.make_async_copy(proj_part.at[1, 1], proj_mine, load_sem.at[2]),
    ]
    for store in part_stores:
        store.start()

    gain = gain_ref[...]
    gain_out[...] = jnp.zeros_like(gain_out)
    hidden_load.wait()
    loop(tiles, lambda j: y_copy(j).wait_recv())

    def norm_rows(i):
        window = pl.ds(pl.multiple_of(i * ROWS, ROWS), ROWS)
        incoming = staged[1, window, :] + y_in[window, :]
        values = tok[window, :].astype(F32)
        scale = lax.rsqrt(jnp.mean(values * values, axis=-1, keepdims=True) + EPSILON)
        weighted = incoming * gain
        inner = jnp.mean(weighted * values, axis=-1, keepdims=True)
        back = scale * weighted - values * (scale * scale * scale) * inner
        staged[0, window, :] = core_in[window, :] + back
        gain_out[...] = gain_out[...] + jnp.sum(
            incoming * values * scale, axis=0, keepdims=True
        )

    loop(half // ROWS, norm_rows)
    input_copy = remote(
        staged.at[0], input_twin_out, end_send.at[0], end_recv.at[0], twin_id
    )
    input_copy.start()
    input_store = pltpu.make_async_copy(staged.at[0], input_half_out, load_sem.at[3])
    input_store.start()

    for store in part_stores + [input_store]:
        store.wait()
    input_copy.wait()
    for slot in range(2):
        for copy in x_copies(slot):
            copy.wait_send()
    loop(tiles, lambda j: y_copy(j).wait_send())
    for copy in z_copies():
        copy.wait()
    loop(tiles, lambda j: row_copy(j).wait())


def last(
    normed_others, cot_others, normed, cot, act, gg, gu, w_gate, w_up, w_down,
    projected, projected_far, w_query, w_key, w_value, heads, grad_attn, grad_attn_far,
    normed_one, normed_one_far, heads_far, grad_hidden, tokens, gain,
):
    row_count, width = tokens.shape
    half = row_count // 2
    tiles = width // TILE
    hidden_units = w_gate.shape[1]
    hbm = pl.BlockSpec(memory_space=pl.ANY)
    vmem = pl.BlockSpec(memory_space=pltpu.VMEM)
    wide = jax.ShapeDtypeStruct((half, width), F32)
    triple = jax.ShapeDtypeStruct((3, TILE, hidden_units), F32)
    out_block = jax.ShapeDtypeStruct((512, TILE), F32)
    proj_block = jax.ShapeDtypeStruct((TILE, 768), F32)
    dma = pltpu.SemaphoreType.DMA
    return pl.pallas_call(
        last_kernel,
        out_shape=(
            triple, triple, triple, out_block, out_block, proj_block, proj_block, wide, wide,
            jax.ShapeDtypeStruct((1, width), F32),
        ),
        in_specs=[hbm] * 23 + [vmem],
        out_specs=(hbm,) * 9 + (vmem,),
        scratch_shapes=[
            pltpu.VMEM((6 * half, width), BF16),
            pltpu.VMEM((6 * half, width), BF16),
            pltpu.VMEM((2 * TILE, row_count + 6 * half), BF16),
            pltpu.VMEM((2 * TILE, row_count + 6 * half), BF16),
            pltpu.VMEM((3, row_count + 6 * half, TILE), BF16),
            pltpu.VMEM((2, width, TILE), BF16),
            pltpu.VMEM((2, width, TILE), BF16),
            pltpu.VMEM((2, TILE, width), BF16),
            pltpu.VMEM((2, 3, 2 * TILE, TILE), F32),
            pltpu.VMEM((2, half, width), F32),
            pltpu.VMEM((half, width), F32),
            pltpu.VMEM((half, width), F32),
            pltpu.VMEM((width, 768), BF16),
            pltpu.VMEM((half, width), BF16),
            pltpu.VMEM((2, row_count, 512), BF16),
            pltpu.VMEM((2, row_count, 1024), BF16),
            pltpu.VMEM((2, row_count, 1024), BF16),
            pltpu.VMEM((2, row_count, 768), BF16),
            pltpu.VMEM((2, 2, 512, TILE), F32),
            pltpu.VMEM((2, 2, TILE, 768), F32),
            pltpu.VMEM((2, 512, TILE), F32),
            pltpu.VMEM((2, TILE, 768), F32),
            pltpu.VMEM((4, row_count, TILE), BF16),
            pltpu.VMEM((half, 2 * 768), F32),
            pltpu.VMEM((half, 1024), F32),
            dma((14,)), dma((6,)), dma((2, 3)), dma((3,)), dma((2, 2)),
            dma((tiles,)), dma((tiles,)),
            dma((tiles,)), dma((tiles,)), dma((tiles,)), dma((tiles,)),
            dma((2, 2)), dma((2, 2)), dma((2,)), dma((2,)), dma((1,)), dma((1,)),
        ],
        compiler_params=pltpu.CompilerParams(
            collective_id=1, has_side_effects=True, vmem_limit_bytes=64 * 1024 * 1024
        ),
        name="weight_gradients",
    )(
        normed_others, cot_others, normed, cot, act, gg, gu, w_gate, w_up, w_down,
        projected, projected_far, w_query, w_key, w_value, heads, grad_attn, grad_attn_far,
        normed_one, normed_one_far, heads_far, grad_hidden, tokens, gain.reshape(1, width),
    )


def body(
    tokens,
    segments,
    positions,
    attn_gain,
    w_query,
    key_weight,
    value_weight,
    w_out,
    mlp_gain,
    w_gate,
    w_up,
    w_down,
    cotangent,
):
    groups = lax.axis_size("dp")
    place = lax.axis_index("dp")
    core = lax.axis_index("tensor") % 2
    all_bits = [1 << i for i in range(groups.bit_length() - 1)]
    shared_bits = [bit for bit in (4, 1) if bit < groups]
    split_bits = [bit for bit in all_bits if bit not in shared_bits]

    def blocks(matrix, offsets):
        width = matrix.shape[1] // groups
        return [
            lax.dynamic_slice_in_dim(matrix, (place ^ offset) * width, width, 1)
            for offset in offsets
        ]

    def offsets_of(bits):
        found = [0]
        for bit in bits:
            found = found + [offset + bit for offset in found]
        return found

    def reduced(matrix_of, bits):
        sent = None
        for bit in bits:
            rest = bits[bits.index(bit) + 1 :]
            offsets = offsets_of(rest)
            if sent is None:
                away = matrix_of([offset ^ bit for offset in offsets])
                home = matrix_of(offsets)
            else:
                away = [sent[offset ^ bit] for offset in offsets]
                home = [sent[offset] for offset in offsets]
            came = swap(away, "dp", bit)
            sent = {offset: h + c for offset, h, c in zip(offsets, home, came)}
        return sent[0]

    row_count, width = tokens.shape
    query_width, kv_width = w_query.shape[1], key_weight.shape[1]
    half_dim = HEAD_SIZE // 2
    frequency = 500000.0 ** (-(jnp.arange(half_dim).astype(F32) * 2.0 / HEAD_SIZE))
    angles = positions.reshape(row_count, 1).astype(F32) * jnp.tile(frequency, 4)
    cosine_tile = jnp.cos(angles)
    sine_tile = jnp.sin(angles) * jnp.where(jnp.arange(128) % HEAD_SIZE < half_dim, 1.0, -1.0)
    (
        normed_one,
        head_outputs,
        _,
        _,
        _,
        normed_one_far,
        heads_far,
        grad_hidden,
        grad_attn,
        projected,
        grad_attn_far,
        projected_far,
        mixed_half,
        mixed_twin,
        normed_two,
        activation,
        grad_gate_in,
        grad_up_in,
        gain_two_half,
        cotangent_others,
        normed_others,
    ) = middle(
        w_query, key_weight, value_weight, w_out, tokens, cotangent,
        half_of(cotangent, core).astype(F32), attn_gain, mlp_gain, w_gate, w_up, w_down,
        segments, cosine_tile, sine_tile,
    )
    gain_two_half = gain_two_half[0]
    mixed = joined(mixed_half, mixed_twin, core).astype(BF16)
    (
        kept,
        _,
        came,
        out_mine,
        out_came,
        proj_mine,
        proj_came,
        input_half,
        input_twin,
        gain_one_half,
    ) = last(
        normed_others, cotangent_others, normed_two, cotangent, activation, grad_gate_in,
        grad_up_in, w_gate, w_up, w_down, projected, projected_far, w_query, key_weight,
        value_weight, head_outputs, grad_attn, grad_attn_far, normed_one, normed_one_far,
        heads_far, grad_hidden, tokens, attn_gain,
    )
    gain_one_half = gain_one_half[0]
    grad_input = joined(input_half, input_twin, core)
    grad_w_gate = kept[0] + came[0]
    grad_w_up = kept[1] + came[1]
    grad_w_down = (kept[2] + came[2]).T
    grad_w_out = out_mine + out_came
    grad_w_proj = proj_mine + proj_came
    grad_w_query = grad_w_proj[:, :query_width]
    grad_w_key = grad_w_proj[:, query_width : query_width + kv_width]
    grad_w_value = grad_w_proj[:, query_width + kv_width :]

    gains = jnp.stack([gain_one_half, gain_two_half])
    gains = gains + swap(gains, "tensor", 1)
    gains = reduced(lambda offsets: blocks(gains, offsets), all_bits)
    grad_attn_gain, grad_mlp_gain = gains[0], gains[1]
    return (
        mixed,
        grad_input,
        grad_attn_gain,
        grad_w_query,
        grad_w_key,
        grad_w_value,
        grad_w_out,
        grad_mlp_gain,
        grad_w_gate,
        grad_w_up,
        grad_w_down,
    )


def product(left_matrix, right_matrix):
    return jnp.dot(left_matrix, right_matrix, preferred_element_type=F32)


def over_rows(left_matrix, right_matrix):
    return lax.dot_general(
        left_matrix, right_matrix, (((0,), (0,)), ((), ())), preferred_element_type=F32
    )


def against(gradient, weight):
    return lax.dot_general(
        gradient, weight, (((1,), (1,)), ((), ())), preferred_element_type=F32
    )


def narrowed(value):
    return jnp.where(value == value, value, 0.0).astype(BF16)


def tensor_sum_half(partial, core):
    total = half_of(partial, core) + swap(half_of(partial, 1 - core), "tensor", 1)
    bit = 2
    while bit < lax.axis_size("tensor"):
        total = total + swap(total, "tensor", bit)
        bit *= 2
    return total


def tables(places):
    half_dim = HEAD_SIZE // 2
    frequency = 500000.0 ** (-(jnp.arange(half_dim).astype(F32) * 2.0 / HEAD_SIZE))
    angles = places.astype(F32)[..., None] * frequency
    cosine_lookup = jnp.cos(angles)
    sine_lookup = jnp.sin(angles)
    return (
        jnp.concatenate([cosine_lookup, cosine_lookup], -1),
        jnp.concatenate([sine_lookup, sine_lookup], -1),
    )


def apply_rotary(field, cosine_lookup, sine_lookup):
    half_dim = HEAD_SIZE // 2
    turned = jnp.concatenate([-field[..., half_dim:], field[..., :half_dim]], -1)
    return field * cosine_lookup + turned * sine_lookup


def unrotate(gradient, cosine_lookup, sine_lookup):
    half_dim = HEAD_SIZE // 2
    sined = gradient * sine_lookup
    return gradient * cosine_lookup + jnp.concatenate(
        [sined[..., half_dim:], -sined[..., :half_dim]], -1
    )


def allowed_pairs(segment):
    spots = jnp.arange(segment.shape[0])
    return (spots[:, None] >= spots[None, :]) & (segment[:, None] == segment[None, :])


def scores(query_rotated, key_rotated, segment):
    raw_scores = jnp.einsum(
        "qhgd,khd->hgqk", query_rotated, key_rotated, preferred_element_type=F32
    ) * HEAD_SIZE ** (-0.5)
    return jnp.where(allowed_pairs(segment), raw_scores, MASKED)


def attend_forward(query_rotated, key_rotated, value_seq, segment):
    masked = scores(query_rotated, key_rotated, segment)
    row_peak = jnp.max(masked, axis=-1, keepdims=True)
    log_total = row_peak + jnp.log(jnp.sum(jnp.exp(masked - row_peak), axis=-1, keepdims=True))
    attention_probs = jnp.exp(masked - log_total).astype(BF16)
    combined_heads = jnp.einsum(
        "ojus,sov->uojv", attention_probs, value_seq, preferred_element_type=F32
    )
    return (combined_heads, log_total)


def attend_backward(query_rotated, key_rotated, value_seq, segment, log_total, grad_heads):
    masked = scores(query_rotated, key_rotated, segment)
    attention_probs = jnp.exp(masked - log_total)
    grad_probs = jnp.einsum("qhgd,khd->hgqk", grad_heads, value_seq, preferred_element_type=F32)
    row_sum = jnp.sum(attention_probs * grad_probs, axis=-1, keepdims=True)
    grad_raw = jnp.where(
        allowed_pairs(segment), attention_probs * (grad_probs - row_sum), 0.0
    ).astype(BF16)
    factor = HEAD_SIZE ** (-0.5)
    grad_query_rot = (
        jnp.einsum("ojus,sov->uojv", grad_raw, key_rotated, preferred_element_type=F32) * factor
    )
    grad_key_rot = (
        jnp.einsum("hgqk,qhgd->khd", grad_raw, query_rotated, preferred_element_type=F32) * factor
    )
    grad_value_rot = jnp.einsum(
        "hgqk,qhgd->khd", attention_probs.astype(BF16), grad_heads, preferred_element_type=F32
    )
    return (grad_query_rot, grad_key_rot, grad_value_rot)


def per_sequence(step, *fields):
    results = [step(*[field[s] for field in fields]) for s in range(fields[0].shape[0])]
    return [jnp.stack(parts) for parts in zip(*results)]


def general_body(
    tokens,
    segments,
    positions,
    attn_gain,
    w_query,
    key_weight,
    value_weight,
    w_out,
    mlp_gain,
    w_gate,
    w_up,
    w_down,
    cotangent,
):
    groups = lax.axis_size("dp")
    place = lax.axis_index("dp")
    core = lax.axis_index("tensor") % 2
    all_bits = [1 << i for i in range(groups.bit_length() - 1)]
    shared_bits = [bit for bit in (4, 1) if bit < groups]
    split_bits = [bit for bit in all_bits if bit not in shared_bits]

    def gathered(half):
        parts = [half]
        for bit in shared_bits:
            parts = parts + [swap(part, "dp", bit) for part in parts]
        others = parts[1:]
        twins = [swap(part, "tensor", 1) for part in others]
        return jnp.concatenate([narrowed(part) for part in others + twins], axis=0)

    def blocks(matrix, offsets):
        width = matrix.shape[1] // groups
        return [
            lax.dynamic_slice_in_dim(matrix, (place ^ offset) * width, width, 1)
            for offset in offsets
        ]

    def offsets_of(bits):
        found = [0]
        for bit in bits:
            found = found + [offset + bit for offset in found]
        return found

    def reduced(matrix_of, bits):
        sent = None
        for bit in bits:
            rest = bits[bits.index(bit) + 1 :]
            offsets = offsets_of(rest)
            if sent is None:
                away = matrix_of([offset ^ bit for offset in offsets])
                home = matrix_of(offsets)
            else:
                away = [sent[offset ^ bit] for offset in offsets]
                home = [sent[offset] for offset in offsets]
            came = swap(away, "dp", bit)
            sent = {offset: h + c for offset, h, c in zip(offsets, home, came)}
        return sent[0]

    inputs = tokens.astype(F32)
    row_count, width = inputs.shape
    seq_count, seq_len = segments.shape
    query_heads = w_query.shape[1] // HEAD_SIZE
    kv_heads = key_weight.shape[1] // HEAD_SIZE
    group_size = query_heads // kv_heads
    query_width, kv_width = w_query.shape[1], key_weight.shape[1]

    cotangent_half = half_of(cotangent, core).astype(F32)
    cotangent_others = gathered(cotangent_half)

    scale_one = lax.rsqrt(jnp.mean(inputs * inputs, axis=-1, keepdims=True) + EPSILON)
    normed_one = (inputs * scale_one * attn_gain).astype(BF16)
    cosine_lookup, sine_lookup = tables(positions.reshape(row_count))
    cosine_lookup = cosine_lookup[:, None, :]
    sine_lookup = sine_lookup[:, None, :]
    query_projected = product(normed_one, w_query).reshape(row_count, query_heads, HEAD_SIZE)
    key_projected = product(normed_one, key_weight).reshape(row_count, kv_heads, HEAD_SIZE)
    query_rotated = (
        apply_rotary(query_projected, cosine_lookup, sine_lookup)
        .astype(BF16)
        .reshape(seq_count, seq_len, kv_heads, group_size, HEAD_SIZE)
    )
    key_rotated = (
        apply_rotary(key_projected, cosine_lookup, sine_lookup)
        .astype(BF16)
        .reshape(seq_count, seq_len, kv_heads, HEAD_SIZE)
    )
    value_projected = (
        product(normed_one, value_weight)
        .astype(BF16)
        .reshape(seq_count, seq_len, kv_heads, HEAD_SIZE)
    )
    combined_heads, log_totals = per_sequence(
        attend_forward, query_rotated, key_rotated, value_projected, segments
    )
    head_outputs = combined_heads.reshape(row_count, query_width).astype(BF16)

    inputs_half = half_of(inputs, core)
    hidden = inputs_half + tensor_sum_half(product(head_outputs, w_out), core)
    scale_two = lax.rsqrt(jnp.mean(hidden * hidden, axis=-1, keepdims=True) + EPSILON)
    normed_half = (hidden * scale_two * mlp_gain).astype(BF16)
    normed_sent = normed_half.astype(F32)
    normed_twin = narrowed(swap(normed_sent, "tensor", 1))
    normed_two = joined(normed_half, normed_twin, core)
    normed_others = gathered(normed_sent)

    def feed_forward(normed, incoming):
        gate_proj = product(normed, w_gate)
        up_proj = product(normed, w_up)
        grad_activation = against(incoming, w_down)
        sigmoid_gate = jax.nn.sigmoid(gate_proj)
        swish_gate = gate_proj * sigmoid_gate
        activation = (swish_gate * up_proj).astype(BF16)
        grad_gate_in = (
            grad_activation * up_proj * sigmoid_gate * (1.0 + gate_proj * (1.0 - sigmoid_gate))
        ).astype(BF16)
        grad_up_in = (grad_activation * swish_gate).astype(BF16)
        return activation, grad_gate_in, grad_up_in

    activation, grad_gate_in, grad_up_in = feed_forward(normed_two, cotangent)
    grad_normed_two = tensor_sum_half(
        against(grad_gate_in, w_gate) + against(grad_up_in, w_up), core
    )
    mixed_half = hidden + tensor_sum_half(product(activation, w_down), core)
    mixed = joined(mixed_half.astype(BF16), narrowed(swap(mixed_half, "tensor", 1)), core)

    weighted = grad_normed_two * mlp_gain
    inner_mean = jnp.mean(weighted * hidden, axis=-1, keepdims=True)
    back_two = scale_two * weighted - hidden * (scale_two * scale_two * scale_two) * inner_mean
    gain_two_half = jnp.sum(grad_normed_two * hidden * scale_two, axis=0)
    grad_hidden = cotangent_half + back_two
    attn_half = grad_hidden.astype(BF16)
    attn_twin = narrowed(swap(grad_hidden, "tensor", 1))
    grad_attn = joined(attn_half, attn_twin, core)

    grad_heads = (
        against(grad_attn, w_out)
        .astype(BF16)
        .reshape(seq_count, seq_len, kv_heads, group_size, HEAD_SIZE)
    )
    grad_query_rot, grad_key_rot, grad_value_rot = per_sequence(
        attend_backward,
        query_rotated,
        key_rotated,
        value_projected,
        segments,
        log_totals,
        grad_heads,
    )
    grad_query_in = (
        unrotate(
            grad_query_rot.reshape(row_count, query_heads, HEAD_SIZE), cosine_lookup, sine_lookup
        )
        .reshape(row_count, query_width)
        .astype(BF16)
    )
    grad_key_in = (
        unrotate(grad_key_rot.reshape(row_count, kv_heads, HEAD_SIZE), cosine_lookup, sine_lookup)
        .reshape(row_count, kv_width)
        .astype(BF16)
    )
    grad_value_in = grad_value_rot.reshape(row_count, kv_width).astype(BF16)
    partial_one = (
        against(grad_query_in, w_query)
        + against(grad_key_in, key_weight)
        + against(grad_value_in, value_weight)
    )
    grad_normed_one = tensor_sum_half(partial_one, core)
    scale_one = half_of(scale_one, core)
    weighted = grad_normed_one * attn_gain
    inner_mean = jnp.mean(weighted * inputs_half, axis=-1, keepdims=True)
    back_one = scale_one * weighted - inputs_half * (scale_one * scale_one * scale_one) * inner_mean
    gain_one_half = jnp.sum(grad_normed_one * inputs_half * scale_one, axis=0)
    input_half = grad_hidden + back_one
    grad_input = joined(input_half, swap(input_half, "tensor", 1), core)

    activation_o, grad_gate_o, grad_up_o = feed_forward(normed_others, cotangent_others)

    def rows_of(left, left_others, right, right_others):
        def term(offsets):
            ours = blocks(left, offsets)
            theirs = blocks(left_others, offsets)
            return [
                over_rows(a, right) + over_rows(b, right_others) for a, b in zip(ours, theirs)
            ]

        return reduced(term, split_bits)

    def columns_of(left, left_others, right, right_others):
        def term(offsets):
            ours = blocks(right, offsets)
            theirs = blocks(right_others, offsets)
            return [
                over_rows(left, a) + over_rows(left_others, b) for a, b in zip(ours, theirs)
            ]

        return reduced(term, split_bits)

    grad_w_down = columns_of(activation, activation_o, cotangent, cotangent_others)
    grad_w_gate = rows_of(normed_two, normed_others, grad_gate_in, grad_gate_o)
    grad_w_up = rows_of(normed_two, normed_others, grad_up_in, grad_up_o)

    grad_w_out = reduced(
        lambda offsets: [over_rows(head_outputs, b) for b in blocks(grad_attn, offsets)], all_bits
    )
    projected = jnp.concatenate([grad_query_in, grad_key_in, grad_value_in], axis=1)
    grad_w_proj = reduced(
        lambda offsets: [over_rows(b, projected) for b in blocks(normed_one, offsets)], all_bits
    )
    grad_w_query = grad_w_proj[:, :query_width]
    grad_w_key = grad_w_proj[:, query_width : query_width + kv_width]
    grad_w_value = grad_w_proj[:, query_width + kv_width :]

    gains = jnp.stack([gain_one_half, gain_two_half])
    gains = gains + swap(gains, "tensor", 1)
    gains = reduced(lambda offsets: blocks(gains, offsets), all_bits)
    grad_attn_gain, grad_mlp_gain = gains[0], gains[1]
    return (
        mixed,
        grad_input,
        grad_attn_gain,
        grad_w_query,
        grad_w_key,
        grad_w_value,
        grad_w_out,
        grad_mlp_gain,
        grad_w_gate,
        grad_w_up,
        grad_w_down,
    )


def solution(mesh):
    placed = (
        P("dp", None),
        P("dp", None),
        P("dp", None),
        P(),
        P(None, "tensor"),
        P(None, "tensor"),
        P(None, "tensor"),
        P("tensor", None),
        P(),
        P(None, "tensor"),
        P(None, "tensor"),
        P("tensor", None),
        P("dp", None),
    )
    fits = mesh.shape["dp"] == 8 and mesh.shape["tensor"] == 4
    return jax.shard_map(
        body if fits else general_body,
        mesh=mesh,
        in_specs=placed,
        out_specs=(
            P("dp", None),
            P("dp", None),
            P("dp"),
            P("dp", "tensor"),
            P("dp", "tensor"),
            P("dp", "tensor"),
            P("tensor", "dp"),
            P("dp"),
            P("dp", "tensor"),
            P("dp", "tensor"),
            P("tensor", "dp"),
        ),
        check_vma=False,
    )
```

```python
import functools

import jax
import jax.numpy as jnp
from jax import lax
from jax.experimental import pallas as pl
from jax.experimental.pallas import tpu as pltpu
from jax.sharding import PartitionSpec as P

HEAD_SIZE = 64
EPSILON = 1e-05
MASKED = -1e30
F32 = jnp.float32
BF16 = jnp.bfloat16


def swap(value, axis, bit):
    size = lax.axis_size(axis)
    return lax.ppermute(value, axis, [(i, i ^ bit) for i in range(size)])


def half_of(value, which, dim=0):
    size = value.shape[dim] // 2
    return lax.dynamic_slice_in_dim(value, which * size, size, dim)


def joined(mine, other, which):
    first = jnp.where(which == 0, mine, other)
    second = jnp.where(which == 0, other, mine)
    return jnp.concatenate([first, second], axis=0)


MESH = pl.DeviceIdType.MESH
CHUNKS = 4
TILE = 256
ROWS = 16


def flip(index, bit):
    return index + bit * (1 - 2 * ((index // bit) % 2))


def loop(count, step):
    lax.fori_loop(0, count, lambda i, carry: (step(i), carry)[1], 0)


def middle_kernel(
    w_query_ref,
    w_key_ref,
    w_value_ref,
    w_out_ref,
    tokens_ref,
    cot_ref,
    gain_one_ref,
    gain_ref,
    w_gate_ref,
    w_up_ref,
    w_down_ref,
    segment_column_ref,
    segment_row_ref,
    cosine_ref,
    sine_ref,
    normed_one_out,
    heads_out,
    query_ref,
    keys_ref,
    values_ref,
    normed_one_far,
    heads_far,
    grad_hidden_out,
    grad_attn_out,
    projected_out,
    grad_attn_far,
    branch_out,
    normed_out,
    activation_out,
    grad_gate_out,
    grad_up_out,
    gain_out,
    cot_others,
    normed_others,
    gate_w,
    up_w,
    down_w,
    cot,
    hidden,
    normed,
    normed_sent,
    normed_twin,
    act,
    gg,
    gu,
    away,
    mine,
    core_in,
    y_in,
    product,
    log_total_ref,
    local_sem,
    core_send,
    core_recv,
    y_send,
    y_recv,
    cot_send,
    cot_recv,
    n_send,
    n_recv,
    twin_send,
    twin_recv,
    hidden_send,
    hidden_recv,
    far_send,
    far_recv,
):
    dp, tensor = lax.axis_index("dp"), lax.axis_index("tensor")
    core, y_bit = tensor % 2, (tensor // 2) % 2
    z_low = (dp // 2) % 2
    twin_id = (dp, flip(tensor, 1))
    y_id = (dp, flip(tensor, 2))
    x_id = (flip(dp, 1), tensor)
    z_id = (flip(dp, 4), tensor)
    far_id = (flip(dp, 2), tensor)
    half, width = hidden.shape
    run = half // 2
    row_count = 2 * half
    hidden_units = gate_w.shape[1]
    query_width = w_query_ref.shape[1]
    tiles = width // TILE
    chunk = half // CHUNKS
    transposed = (((1,), (1,)), ((), ()))
    everything = slice(None)
    heads = gg.at[:, pl.ds(0, query_width)]
    tok = gu
    cot_half = mine.at[1]

    def own_row(block, which):
        return pl.multiple_of(block * half + which * run, run)

    def own_chunk(k, which):
        return own_row(k // 2, which) + (k % 2) * chunk

    def remote(src, dst, send, recv, device):
        return pltpu.make_async_remote_copy(
            src_ref=src, dst_ref=dst, send_sem=send, recv_sem=recv,
            device_id=device, device_id_type=MESH,
        )

    loads = {
        "tok": pltpu.make_async_copy(tokens_ref, tok, local_sem.at[0]),
        "query": pltpu.make_async_copy(
            w_query_ref, gate_w.at[:, pl.ds(0, query_width)], local_sem.at[1]
        ),
        "key": pltpu.make_async_copy(
            w_key_ref, gate_w.at[:, pl.ds(query_width, 128)], local_sem.at[2]
        ),
        "value": pltpu.make_async_copy(
            w_value_ref, gate_w.at[:, pl.ds(query_width + 128, 128)], local_sem.at[3]
        ),
        "w_out": pltpu.make_async_copy(w_out_ref, cot, local_sem.at[4]),
        "up": pltpu.make_async_copy(w_up_ref, up_w, local_sem.at[5]),
        "down": pltpu.make_async_copy(w_down_ref, down_w, local_sem.at[6]),
        "gate": pltpu.make_async_copy(w_gate_ref, gate_w, local_sem.at[7]),
        "cot": pltpu.make_async_copy(cot_ref, cot, local_sem.at[8]),
        "cot_0": pltpu.make_async_copy(
            cot_ref.at[pl.ds(own_row(0, core), run)], act.at[pl.ds(0, run)], local_sem.at[10]
        ),
        "cot_1": pltpu.make_async_copy(
            cot_ref.at[pl.ds(own_row(1, core), run)], act.at[pl.ds(run, run)], local_sem.at[11]
        ),
    }
    for name in ("cot_0", "cot_1", "tok", "query", "key", "value", "w_out", "up", "down"):
        loads[name].start()

    barrier = pltpu.get_barrier_semaphore()
    for device in (twin_id, y_id, x_id, z_id, far_id):
        pl.semaphore_signal(barrier, inc=1, device_id=device, device_id_type=MESH)
    loads["cot_0"].wait()
    loads["cot_1"].wait()

    def widen(i):
        window = pl.ds(pl.multiple_of(i * ROWS, ROWS), ROWS)
        cot_half[window, :] = act[window, :].astype(F32)

    loop(half // ROWS, widen)
    pl.semaphore_wait(barrier, 5)

    def rows(k):
        return pl.ds(pl.multiple_of(k * chunk, chunk), chunk)

    def from_x(source, slots, k, send, recv):
        return remote(source.at[rows(k)], slots.at[0, rows(k)], send.at[0, k], recv.at[0, k], x_id)

    def from_z(source, slots, k, send, recv):
        return remote(source.at[rows(k)], slots.at[1, rows(k)], send.at[1, k], recv.at[1, k], z_id)

    def from_zx(slots, k, send, recv):
        return remote(
            slots.at[1, rows(k)], slots.at[2, rows(k)], send.at[2, k], recv.at[2, k], x_id
        )

    def to_twin(slots, which, slot):
        return remote(
            slots.at[slot], slots.at[3 + slot],
            twin_send.at[which, slot], twin_recv.at[which, slot], twin_id,
        )

    half_chunk = pl.ds(pl.multiple_of((2 + y_bit) * chunk, chunk), chunk)

    def last_z():
        return remote(
            normed_sent.at[half_chunk], normed_others.at[1, half_chunk],
            n_send.at[1, 2], n_recv.at[1, 2], z_id,
        )

    def last_y():
        return remote(
            normed_others.at[1, half_chunk], normed_others.at[1, half_chunk],
            n_send.at[1, 3], n_recv.at[1, 3], y_id,
        )

    quarter = pl.ds(pl.multiple_of(y_bit * run, run), run)

    def quarter_z():
        return remote(
            cot_half.at[quarter], cot_others.at[1, quarter],
            cot_send.at[1, 0], cot_recv.at[1, 0], z_id,
        )

    def quarter_zx():
        return remote(
            cot_others.at[1, quarter], cot_others.at[2, quarter],
            cot_send.at[2, 0], cot_recv.at[2, 0], x_id,
        )

    def quarter_y():
        return remote(
            cot_others.at[1, quarter], cot_others.at[1, quarter],
            cot_send.at[1, 1], cot_recv.at[1, 1], y_id,
        )

    quarter_z().start()
    for k in range(CHUNKS):
        from_x(cot_half, cot_others, k, cot_send, cot_recv).start()

    def far_columns(b):
        return pl.ds(pl.multiple_of(b * 1024 + (1 - z_low) * 512, 512), 512)

    gain_one = gain_one_ref[...]
    loads["tok"].wait()

    def first_norm(i):
        window = pl.ds(pl.multiple_of(i * ROWS, ROWS), ROWS)
        values = tok[window, :].astype(F32)
        scale = lax.rsqrt(jnp.mean(values * values, axis=-1, keepdims=True) + EPSILON)
        normed[window, :] = (values * scale * gain_one).astype(BF16)

    loop(row_count // ROWS, first_norm)
    normed_one_store = pltpu.make_async_copy(normed, normed_one_out, local_sem.at[9])
    normed_one_store.start()

    for block in range(2):

        def stage_far(i, block=block):
            window = pl.ds(pl.multiple_of(block * run + i * ROWS, ROWS), ROWS)
            here = pl.ds(pl.multiple_of(own_row(block, core) + i * ROWS, ROWS), ROWS)
            for b in range(2):
                core_in[2, window, pl.ds(b * 512, 512)] = normed[here, far_columns(b)].astype(F32)

        loop(run // ROWS, stage_far)
    normed_one_copy = remote(
        core_in.at[2, :, pl.ds(0, 1024)], normed_one_far.at[0],
        far_send.at[0], far_recv.at[0], far_id,
    )
    normed_one_copy.start()

    lane = lax.broadcasted_iota(jnp.int32, (TILE, 128), 1)
    factor = HEAD_SIZE ** (-0.5)

    def turn(value):
        return jnp.where(lane % 64 < 32, pltpu.roll(value, 96, 1), pltpu.roll(value, 32, 1))

    def rotate_tile(value, window):
        return value * cosine_ref[window, :] - turn(value) * sine_ref[window, :]

    def unrotate_tile(value, window):
        return value * cosine_ref[window, :] + turn(value) * sine_ref[window, :]

    def project_in(block):
        window = pl.ds(block * TILE, TILE)

        def query_tile(j):
            projection = jnp.dot(
                normed[window, :],
                gate_w[:, pl.ds(pl.multiple_of(j * TILE, TILE), TILE)],
                preferred_element_type=F32,
            )
            for part in range(2):
                act[window, pl.ds(pl.multiple_of(j * TILE + part * 128, 128), 128)] = rotate_tile(
                    projection[:, part * 128 : (part + 1) * 128], window
                ).astype(BF16)

        loop(query_width // TILE, query_tile)
        projection = jnp.dot(
            normed[window, :], gate_w[:, pl.ds(query_width, TILE)], preferred_element_type=F32
        )
        for base, value in (
            (1024, rotate_tile(projection[:, :128], window)),
            (1536, projection[:, 128:]),
        ):
            other = pltpu.roll(value, 64, 1)
            halves_of = (
                jnp.where(lane < 64, value, 0.0),
                jnp.where(lane >= 64, other, 0.0),
                jnp.where(lane < 64, other, 0.0),
                jnp.where(lane >= 64, value, 0.0),
            )
            for i, padded in enumerate(halves_of):
                act[window, pl.ds(base + i * 128, 128)] = padded.astype(BF16)

    def allowed_of(block):
        keys_seen = (block + 1) * TILE
        window = pl.ds(block * TILE, TILE)
        key_place = lax.broadcasted_iota(jnp.int32, (keys_seen, TILE), 0)
        query_place = lax.broadcasted_iota(jnp.int32, (keys_seen, TILE), 1) + block * TILE
        return (key_place <= query_place) & (
            segment_column_ref[pl.ds(0, keys_seen), :] == segment_row_ref[:, window]
        )

    def attend(block, p):
        kv = p // 2
        column = pl.multiple_of(p * 128, 128)
        window = pl.ds(block * TILE, TILE)
        seen = pl.ds(0, (block + 1) * TILE)
        queries = act[window, pl.ds(column, 128)]
        allowed = allowed_of(block)
        result = jnp.zeros((TILE, 128), F32)
        for side in range(2):
            padded = pl.multiple_of((kv * 2 + side) * 128, 128)
            keys = act[seen, pl.ds(pl.multiple_of(1024 + padded, 128), 128)]
            vals = act[seen, pl.ds(pl.multiple_of(1536 + padded, 128), 128)]
            raw = jnp.where(
                allowed,
                lax.dot_general(keys, queries, transposed, preferred_element_type=F32) * factor,
                MASKED,
            )
            peak = jnp.max(raw, axis=0, keepdims=True)
            lifted = jnp.exp(raw - peak)
            summed = jnp.sum(lifted, axis=0, keepdims=True)
            log_total_ref[pl.ds(2 * p + side, 1), window] = peak + jnp.log(summed)
            result = result + lax.dot_general(
                (lifted * (1.0 / summed)).astype(BF16), vals, (((0,), (0,)), ((), ())),
                preferred_element_type=F32,
            )
        heads[window, pl.ds(column, 128)] = result.astype(BF16)

    def core_copy(which, window, k):
        return remote(
            away.at[window], core_in.at[which].at[window],
            core_send.at[which, k], core_recv.at[which, k], twin_id,
        )

    def y_copy(which, window, k):
        return remote(
            mine.at[which].at[window], y_in.at[which].at[window],
            y_send.at[which, k], y_recv.at[which, k], y_id,
        )

    def split_tile(which, block, columns, value):
        product[...] = value
        local = pl.ds(block * run, run)
        away[local, columns] = product[pl.ds(pl.multiple_of((1 - core) * run, run), run), :]
        mine[which, local, columns] = product[pl.ds(pl.multiple_of(core * run, run), run), :]

    row_windows = [(rows(k), everything) for k in range(CHUNKS)]

    def tile_of(j):
        return pl.ds(pl.multiple_of(j * TILE, TILE), TILE)

    for name in ("query", "key", "value", "w_out"):
        loads[name].wait()
    for block in range(2):
        project_in(block)
        loop(query_width // 128, functools.partial(attend, block))

        def project(j, block=block):
            split_tile(0, block, tile_of(j), jnp.dot(
                heads[pl.ds(block * TILE, TILE), :], cot[:, tile_of(j)],
                preferred_element_type=F32,
            ))

        loop(tiles, project)
        for k in (2 * block, 2 * block + 1):
            core_copy(0, row_windows[k], k).start()
        for k in (2 * block, 2 * block + 1):
            core_copy(0, row_windows[k], k).wait_recv()

            def add(i, k=k):
                window = pl.ds(pl.multiple_of(k * chunk + i * ROWS, ROWS), ROWS)
                mine[0, window, :] = mine[0, window, :] + core_in[0, window, :]

            loop(chunk // ROWS, add)
            y_copy(0, row_windows[k], k).start()
    normed_one_store.wait()
    loads["gate"].start()
    loads["cot"].start()
    keeps = [
        pltpu.make_async_copy(act.at[:, pl.ds(0, 512)], query_ref, local_sem.at[0]),
        pltpu.make_async_copy(act.at[:, pl.ds(1024, 512)], keys_ref, local_sem.at[1]),
        pltpu.make_async_copy(act.at[:, pl.ds(1536, 512)], values_ref, local_sem.at[2]),
        pltpu.make_async_copy(heads, heads_out, local_sem.at[3]),
    ]
    for keep in keeps:
        keep.start()

    def stage_heads(i):
        window = pl.ds(pl.multiple_of(i * ROWS, ROWS), ROWS)
        for b in range(2):
            here = pl.ds(pl.multiple_of(b * half + i * ROWS, ROWS), ROWS)
            core_in[2, window, pl.ds(1024 + b * 512, 512)] = heads[here, :].astype(F32)

    loop(half // ROWS, stage_heads)
    heads_copy = remote(
        core_in.at[2, :, pl.ds(1024, 1024)], heads_far, far_send.at[1], far_recv.at[1], far_id
    )
    heads_copy.start()
    for keep in keeps:
        keep.wait()

    for name in ("cot", "up", "down"):
        loads[name].wait()

    def activation_grad(j):
        gg[:, tile_of(j)] = lax.dot_general(
            cot[...], down_w[tile_of(j), :], transposed, preferred_element_type=F32
        ).astype(BF16)

    loop(hidden_units // TILE, activation_grad)
    loads["gate"].wait()
    gain = gain_ref[...]

    def twin_copy(k):
        return remote(
            normed_sent.at[rows(k)], normed_twin.at[rows(k)],
            n_send.at[3, k], n_recv.at[3, k], twin_id,
        )

    def block_window(block, j):
        return (pl.ds(block * run, run), tile_of(j))

    for block in range(2):
        chunks = (2 * block, 2 * block + 1)
        for k in chunks:
            y_copy(0, row_windows[k], k).wait_recv()

            def normalize_rows(i, k=k):
                window = pl.ds(pl.multiple_of(k * chunk + i * ROWS, ROWS), ROWS)
                here = pl.ds(pl.multiple_of(own_chunk(k, core) + i * ROWS, ROWS), ROWS)
                values = tok[here, :].astype(F32) + (mine[0, window, :] + y_in[0, window, :])
                scale = lax.rsqrt(jnp.mean(values * values, axis=-1, keepdims=True) + EPSILON)
                rounded = (values * scale * gain).astype(BF16)
                hidden[window, :] = values
                normed[here, :] = rounded
                normed_sent[window, :] = rounded.astype(F32)

            loop(chunk // ROWS, normalize_rows)
            twin_copy(k).start()
            if block == 0:
                from_z(normed_sent, normed_others, k, n_send, n_recv).start()
            elif k == 3:
                last_z().start()
            from_x(normed_sent, normed_others, k, n_send, n_recv).start()
        for k in chunks:
            twin_copy(k).wait_recv()

            def take(i, k=k):
                here = pl.ds(pl.multiple_of(own_chunk(k, 1 - core) + i * ROWS, ROWS), ROWS)
                normed[here, :] = normed_twin[
                    pl.ds(pl.multiple_of(k * chunk + i * ROWS, ROWS), ROWS), :
                ].astype(BF16)

            loop(chunk // ROWS, take)
        window = pl.ds(block * TILE, TILE)

        def units(j, window=window):
            columns = tile_of(j)
            gate = jnp.dot(normed[window, :], gate_w[:, columns], preferred_element_type=F32)
            up = jnp.dot(normed[window, :], up_w[:, columns], preferred_element_type=F32)
            back = gg[window, columns].astype(F32)
            sigmoid = jax.nn.sigmoid(gate)
            swish = gate * sigmoid
            act[window, columns] = (swish * up).astype(BF16)
            gg[window, columns] = (
                back * up * sigmoid * (1.0 + gate * (1.0 - sigmoid))
            ).astype(BF16)
            gu[window, columns] = (back * swish).astype(BF16)

        if block == 0:
            loop(hidden_units // TILE, units)
            quarter_z().wait()
            quarter_zx().start()
            for k in range(CHUNKS):
                from_x(cot_half, cot_others, k, cot_send, cot_recv).wait_send()
                core_copy(0, row_windows[k], k).wait_send()
        else:
            loop(hidden_units // TILE, units)
            normed_one_copy.wait()
            heads_copy.wait()

        def produce(j, block=block, window=window):
            split_tile(1, block, tile_of(j), lax.dot_general(
                gg[window, :], gate_w[tile_of(j), :], transposed, preferred_element_type=F32
            ) + lax.dot_general(
                gu[window, :], up_w[tile_of(j), :], transposed, preferred_element_type=F32
            ))
            core_copy(1, block_window(block, j), block * tiles + j).start()

        def forward(j, block=block):
            where = block_window(block, j)
            core_copy(1, where, block * tiles + j).wait_recv()
            mine[(1,) + where] = mine[(1,) + where] + core_in[(1,) + where]
            y_copy(1, where, block * tiles + j).start()

        def step(j, produce=produce, forward=forward):
            produce(j + 1)
            forward(j)

        produce(0)
        loop(tiles - 1, step)
        forward(tiles - 1)
    stores = [
        pltpu.make_async_copy(normed, normed_out, local_sem.at[7]),
        pltpu.make_async_copy(act, activation_out, local_sem.at[8]),
        pltpu.make_async_copy(gg, grad_gate_out, local_sem.at[9]),
        pltpu.make_async_copy(gu, grad_up_out, local_sem.at[10]),
    ]
    for store in stores:
        store.start()
    normed_one_twin = remote(
        normed_one_far.at[0], normed_one_far.at[1], far_send.at[2], far_recv.at[2], twin_id
    )
    normed_one_twin.start()

    for block in range(2):
        loop(tiles, lambda j: core_copy(1, block_window(block, j), block * tiles + j).wait_send())
    for k in range(CHUNKS):
        y_copy(0, row_windows[k], k).wait_send()

    def branch_produce(j):
        for block in range(2):
            split_tile(0, block, tile_of(j), jnp.dot(
                act[pl.ds(block * TILE, TILE), :], down_w[:, tile_of(j)],
                preferred_element_type=F32,
            ))
        core_copy(2, (everything, tile_of(j)), j).start()

    def branch_add(j):
        core_copy(2, (everything, tile_of(j)), j).wait_recv()
        mine[0, :, tile_of(j)] = mine[0, :, tile_of(j)] + core_in[2, :, tile_of(j)]

    def branch_step(j):
        branch_produce(j + 1)
        branch_add(j)

    branch_produce(0)
    loop(tiles - 1, branch_step)
    branch_add(tiles - 1)
    first_y = (1 - y_bit).astype(F32)

    def add_hidden(i):
        window = pl.ds(pl.multiple_of(i * ROWS, ROWS), ROWS)
        mine[0, window, :] = mine[0, window, :] + hidden[window, :] * first_y

    loop(half // ROWS, add_hidden)
    branch_store = pltpu.make_async_copy(mine.at[0], branch_out, local_sem.at[12])
    branch_store.start()

    for store in stores:
        store.wait()
    operands = [
        pltpu.make_async_copy(query_ref, act.at[:, pl.ds(0, 512)], local_sem.at[0]),
        pltpu.make_async_copy(keys_ref, act.at[:, pl.ds(1024, 512)], local_sem.at[1]),
        pltpu.make_async_copy(values_ref, act.at[:, pl.ds(1536, 512)], local_sem.at[2]),
        pltpu.make_async_copy(w_out_ref, gate_w.at[pl.ds(0, 512)], local_sem.at[3]),
    ]
    for operand in operands:
        operand.start()
    for k in (0, 1):
        from_z(normed_sent, normed_others, k, n_send, n_recv).wait_recv()
        from_zx(normed_others, k, n_send, n_recv).start()
    for k in range(CHUNKS):
        from_x(cot_half, cot_others, k, cot_send, cot_recv).wait_recv()
    to_twin(cot_others, 0, 0).start()
    for operand in operands:
        operand.wait()

    gain_out[...] = jnp.zeros_like(gain_out)
    sums = y_in.at[0]
    sums[:, pl.ds(0, 1024)] = jnp.zeros((TILE, 1024), F32)

    def hidden_copy(k):
        return remote(
            core_in.at[0, rows(k)], normed_twin.at[rows(k)],
            hidden_send.at[k], hidden_recv.at[k], twin_id,
        )

    def hidden_far(block, b):
        local = pl.ds(block * run, run)
        return remote(
            core_in.at[0, local, far_columns(b)],
            grad_attn_far.at[0, local, pl.ds(b * 512, 512)],
            far_send.at[3 + 2 * block + b], far_recv.at[3 + 2 * block + b], far_id,
        )

    def gather_into(offset, kv, value):
        for part in range(value.shape[0] // TILE):
            columns = pl.ds(pl.multiple_of(offset + kv * 256 + part * 128, 128), 128)
            sums[:, columns] = sums[:, columns] + value[part * TILE : (part + 1) * TILE]

    def put(block, column, value):
        gu[pl.ds(block * TILE, TILE), pl.ds(column, 128)] = value.astype(BF16)

    def attend_back(block, p):
        kv = p // 2
        column = pl.multiple_of(p * 128, 128)
        keys_seen = (block + 1) * TILE
        window = pl.ds(block * TILE, TILE)
        seen = pl.ds(0, keys_seen)
        queries = act[window, pl.ds(column, 128)]
        upstream = act[window, pl.ds(pl.multiple_of(512 + column, 128), 128)]
        allowed = allowed_of(block)
        query_grad = jnp.zeros((TILE, 128), F32)
        for side in range(2):
            padded = pl.multiple_of((kv * 2 + side) * 128, 128)
            keys = act[seen, pl.ds(pl.multiple_of(1024 + padded, 128), 128)]
            vals = act[seen, pl.ds(pl.multiple_of(1536 + padded, 128), 128)]
            raw = lax.dot_general(keys, queries, transposed, preferred_element_type=F32) * factor
            log_total = log_total_ref[pl.ds(2 * p + side, 1), window]
            probs = jnp.exp(jnp.where(allowed, raw - log_total, MASKED))
            grad_probs = lax.dot_general(
                vals, upstream, transposed, preferred_element_type=F32
            )
            row_sum = jnp.sum(probs * grad_probs, axis=0, keepdims=True)
            grad_raw = (probs * (grad_probs - row_sum)).astype(BF16)
            query_grad = query_grad + lax.dot_general(
                grad_raw, keys, (((0,), (0,)), ((), ())), preferred_element_type=F32
            )
            own = (lax.broadcasted_iota(jnp.int32, (keys_seen, 128), 1) // 64) == side
            gather_into(0, kv, jnp.where(
                own, jnp.dot(grad_raw, queries, preferred_element_type=F32), 0.0
            ))
            gather_into(512, kv, jnp.where(
                own, jnp.dot(probs.astype(BF16), upstream, preferred_element_type=F32), 0.0
            ))
        put(block, column, unrotate_tile(query_grad * factor, window))

    for block in range(2):
        loop(tiles, lambda j: y_copy(1, block_window(block, j), block * tiles + j).wait_recv())
        if block == 1:
            quarter_y().start()
        for k in (2 * block, 2 * block + 1):

            def norm_rows(i, k=k):
                window = pl.ds(pl.multiple_of(k * chunk + i * ROWS, ROWS), ROWS)
                here = pl.ds(pl.multiple_of(own_chunk(k, core) + i * ROWS, ROWS), ROWS)
                incoming = mine[1, window, :] + y_in[1, window, :]
                values = hidden[window, :]
                scale = lax.rsqrt(jnp.mean(values * values, axis=-1, keepdims=True) + EPSILON)
                weighted = incoming * gain
                inner = jnp.mean(weighted * values, axis=-1, keepdims=True)
                back = scale * weighted - values * (scale * scale * scale) * inner
                total = cot[here, :].astype(F32) + back
                core_in[0, window, :] = total
                normed[here, :] = total.astype(BF16)
                gain_out[...] = gain_out[...] + jnp.sum(
                    incoming * values * scale, axis=0, keepdims=True
                )

            loop(chunk // ROWS, norm_rows)
            hidden_copy(k).start()
        for b in range(2):
            hidden_far(block, b).start()
        for k in (2 * block, 2 * block + 1):
            hidden_copy(k).wait_recv()

            def take_hidden(i, k=k):
                here = pl.ds(pl.multiple_of(own_chunk(k, 1 - core) + i * ROWS, ROWS), ROWS)
                normed[here, :] = normed_twin[
                    pl.ds(pl.multiple_of(k * chunk + i * ROWS, ROWS), ROWS), :
                ].astype(BF16)

            loop(chunk // ROWS, take_hidden)

        def head_tile(j, block=block):
            window = pl.ds(block * TILE, TILE)
            act[window, pl.ds(pl.multiple_of(512 + j * TILE, TILE), TILE)] = lax.dot_general(
                normed[window, :], gate_w[tile_of(j), :], transposed, preferred_element_type=F32
            ).astype(BF16)

        loop(512 // TILE, head_tile)
        loop(query_width // 128, functools.partial(attend_back, block))

    grad_stores = [
        pltpu.make_async_copy(core_in.at[0], grad_hidden_out, local_sem.at[4]),
        pltpu.make_async_copy(normed, grad_attn_out, local_sem.at[5]),
    ]
    for store in grad_stores:
        store.start()

    def both(offset, block):
        def folded(kv):
            value = sums[:, pl.ds(offset + kv * 256 + block * 128, 128)]
            return value + pltpu.roll(value, 64, 1)

        return jnp.where(lane < 64, folded(0), folded(1))

    for block in range(2):
        window = pl.ds(block * TILE, TILE)
        put(block, 512, unrotate_tile(both(0, block) * factor, window))
        put(block, 640, both(512, block))
    projected_store = pltpu.make_async_copy(
        gu.at[:, pl.ds(0, 768)], projected_out, local_sem.at[6]
    )
    projected_store.start()

    last_z().wait()
    last_y().start()
    for block in range(2):
        for b in range(2):
            hidden_far(block, b).wait()
    hidden_far_twin = remote(
        grad_attn_far.at[0], grad_attn_far.at[1], far_send.at[7], far_recv.at[7], twin_id
    )
    hidden_far_twin.start()
    for k in range(CHUNKS):
        from_x(normed_sent, normed_others, k, n_send, n_recv).wait_recv()
    to_twin(normed_others, 1, 0).start()
    quarter_y().wait()
    to_twin(cot_others, 0, 1).start()
    last_y().wait()
    to_twin(normed_others, 1, 1).start()

    for store in grad_stores + [projected_store, branch_store]:
        store.wait()
    for copy in (hidden_far_twin, normed_one_twin, quarter_zx()):
        copy.wait()
    for k in range(CHUNKS):
        hidden_copy(k).wait_send()
        twin_copy(k).wait_send()
        from_x(normed_sent, normed_others, k, n_send, n_recv).wait_send()
    for k in (0, 1):
        from_z(normed_sent, normed_others, k, n_send, n_recv).wait_send()
        from_zx(normed_others, k, n_send, n_recv).wait()
    for block in range(2):
        loop(tiles, lambda j: y_copy(1, block_window(block, j), block * tiles + j).wait_send())
    loop(tiles, lambda j: core_copy(2, (everything, tile_of(j)), j).wait_send())
    for slot in range(2):
        to_twin(cot_others, 0, slot).wait()
        to_twin(normed_others, 1, slot).wait()


def middle(
    w_query, w_key, w_value, w_out, tokens, cotangent, gain_one, gain,
    w_gate, w_up, w_down, segment, cosine, sine,
):
    row_count, width = tokens.shape
    half = row_count // 2
    hidden_units = w_gate.shape[1]
    tiles = width // TILE
    hbm = pl.BlockSpec(memory_space=pl.ANY)
    vmem = pl.BlockSpec(memory_space=pltpu.VMEM)
    wide = jax.ShapeDtypeStruct((half, width), F32)
    units = jax.ShapeDtypeStruct((row_count, hidden_units), BF16)
    square = jax.ShapeDtypeStruct((row_count, 512), BF16)
    dma = pltpu.SemaphoreType.DMA
    return pl.pallas_call(
        middle_kernel,
        out_shape=(
            jax.ShapeDtypeStruct((row_count, width), BF16),
            square, square, square, square,
            jax.ShapeDtypeStruct((2, half, width // 2), F32),
            jax.ShapeDtypeStruct((half, width // 2), F32),
            wide,
            jax.ShapeDtypeStruct((row_count, width), BF16),
            jax.ShapeDtypeStruct((row_count, 768), BF16),
            jax.ShapeDtypeStruct((2, half, width // 2), F32),
            wide,
            jax.ShapeDtypeStruct((row_count, width), BF16),
            units, units, units,
            jax.ShapeDtypeStruct((1, width), F32),
            jax.ShapeDtypeStruct((5, half, width), F32),
            jax.ShapeDtypeStruct((5, half, width), F32),
        ),
        in_specs=[hbm] * 6 + [vmem] * 2 + [hbm] * 3 + [vmem] * 4,
        out_specs=(hbm,) * 16 + (vmem,) + (hbm,) * 2,
        scratch_shapes=[
            pltpu.VMEM(w_gate.shape, BF16),
            pltpu.VMEM(w_up.shape, BF16),
            pltpu.VMEM(w_down.shape, BF16),
            pltpu.VMEM((row_count, width), BF16),
            pltpu.VMEM((half, width), F32),
            pltpu.VMEM((row_count, width), BF16),
            pltpu.VMEM((half, width), F32),
            pltpu.VMEM((half, width), F32),
            pltpu.VMEM((row_count, hidden_units), BF16),
            pltpu.VMEM((row_count, hidden_units), BF16),
            pltpu.VMEM((row_count, hidden_units), BF16),
            pltpu.VMEM((half, width), F32),
            pltpu.VMEM((2, half, width), F32),
            pltpu.VMEM((3, half, width), F32),
            pltpu.VMEM((2, half, width), F32),
            pltpu.VMEM((half, TILE), F32),
            pltpu.VMEM((8, row_count), F32),
            dma((13,)),
            dma((3, 2 * tiles)), dma((3, 2 * tiles)), dma((2, 2 * tiles)), dma((2, 2 * tiles)),
            dma((3, CHUNKS)), dma((3, CHUNKS)),
            dma((4, CHUNKS)), dma((4, CHUNKS)),
            dma((2, 2)), dma((2, 2)),
            dma((CHUNKS,)), dma((CHUNKS,)),
            dma((8,)), dma((8,)),
        ],
        compiler_params=pltpu.CompilerParams(
            collective_id=0, has_side_effects=True, vmem_limit_bytes=64 * 1024 * 1024
        ),
        name="feed_forward",
    )(
        w_query, w_key, w_value, w_out, tokens, cotangent,
        gain_one.reshape(1, width), gain.reshape(1, width), w_gate, w_up, w_down,
        segment.reshape(row_count, 1), segment.reshape(1, row_count), cosine, sine,
    )


def last_kernel(
    normed_others_ref,
    cot_others_ref,
    normed_ref,
    cot_ref,
    act_ref,
    gg_ref,
    gu_ref,
    w_gate_ref,
    w_up_ref,
    w_down_ref,
    projected_ref,
    branch_ref,
    gain_two_ref,
    w_query_ref,
    w_key_ref,
    w_value_ref,
    heads_ref,
    grad_attn_ref,
    grad_attn_far_ref,
    normed_one_ref,
    normed_one_far_ref,
    heads_far_ref,
    grad_hidden_ref,
    tokens_ref,
    gain_ref,
    kept_out,
    sent_out,
    came_out,
    down_kept,
    down_sent,
    down_came,
    out_mine,
    out_came,
    proj_mine,
    proj_came,
    input_out,
    mixed_out,
    branch_came,
    normed_late,
    cot_late,
    gain_out,
    normed,
    cot,
    normed_t,
    cot_t,
    units,
    gate_w,
    up_w,
    down_w,
    total,
    staged,
    core_in,
    y_in,
    w_proj,
    tok,
    heads,
    grad_attn,
    normed_one,
    projected,
    out_part,
    proj_part,
    out_x,
    proj_x,
    far_staged,
    far_heads,
    gains,
    gains_came,
    load_sem,
    piece_sem,
    weight_sem,
    unit_sem,
    store_sem,
    row_send,
    row_recv,
    core_send,
    core_recv,
    y_send,
    y_recv,
    x_send,
    x_recv,
    z_send,
    z_recv,
    end_send,
    end_recv,
    gain_send,
    gain_recv,
    late_send,
    late_recv,
    product,
):
    dp, tensor = lax.axis_index("dp"), lax.axis_index("tensor")
    core = tensor % 2
    x_low, z_low, z_high = dp % 2, (dp // 2) % 2, dp // 4
    twin_id = (dp, flip(tensor, 1))
    y_id = (dp, flip(tensor, 2))
    x_id = (flip(dp, 1), tensor)
    z_id = (flip(dp, 4), tensor)
    far_id = (flip(dp, 2), tensor)
    half, width = tok.shape
    row_count = 2 * half
    tiles = width // TILE
    run = half // 2
    y_bit = (tensor // 2) % 2

    def own_row(block, which):
        return pl.multiple_of(block * half + which * run, run)

    everything = slice(None)
    transposed = (((1,), (1,)), ((), ()))
    over = (((0,), (0,)), ((), ()))

    def remote(src, dst, send, recv, device):
        return pltpu.make_async_remote_copy(
            src_ref=src, dst_ref=dst, send_sem=send, recv_sem=recv,
            device_id=device, device_id_type=MESH,
        )

    def tile_of(j):
        return pl.ds(pl.multiple_of(j * TILE, TILE), TILE)

    away_block = tile_of(flip(dp, 2))
    home_block = tile_of(dp)
    near = [
        pl.ds(pl.multiple_of(b * 1024 + z_low * 512, 512), 512) for b in range(2)
    ]
    own_columns = [units.at[0, pl.ds(i * row_count, row_count)] for i in range(4)]
    loads = [
        pltpu.make_async_copy(normed_ref.at[:, away_block], own_columns[0], load_sem.at[0]),
        pltpu.make_async_copy(normed_ref.at[:, home_block], own_columns[1], load_sem.at[1]),
        pltpu.make_async_copy(cot_ref.at[:, away_block], own_columns[2], load_sem.at[2]),
        pltpu.make_async_copy(cot_ref.at[:, home_block], own_columns[3], load_sem.at[3]),
        pltpu.make_async_copy(w_query_ref, w_proj.at[:, pl.ds(0, 512)], load_sem.at[4]),
        pltpu.make_async_copy(w_key_ref, w_proj.at[:, pl.ds(512, 128)], load_sem.at[5]),
        pltpu.make_async_copy(w_value_ref, w_proj.at[:, pl.ds(640, 128)], load_sem.at[6]),
        pltpu.make_async_copy(
            tokens_ref.at[pl.ds(own_row(0, core), run)], tok.at[pl.ds(0, run)], load_sem.at[7]
        ),
        pltpu.make_async_copy(heads_ref, heads.at[0], load_sem.at[8]),
        pltpu.make_async_copy(
            grad_attn_ref.at[:, near[0]], grad_attn.at[0, :, pl.ds(0, 512)], load_sem.at[9]
        ),
        pltpu.make_async_copy(
            grad_attn_ref.at[:, near[1]], grad_attn.at[0, :, pl.ds(512, 512)], load_sem.at[10]
        ),
        pltpu.make_async_copy(
            normed_one_ref.at[:, near[0]], normed_one.at[0, :, pl.ds(0, 512)], load_sem.at[11]
        ),
        pltpu.make_async_copy(
            normed_one_ref.at[:, near[1]], normed_one.at[0, :, pl.ds(512, 512)], load_sem.at[12]
        ),
        pltpu.make_async_copy(projected_ref, projected.at[0], load_sem.at[13]),
        pltpu.make_async_copy(
            tokens_ref.at[pl.ds(own_row(1, core), run)], tok.at[pl.ds(run, run)], load_sem.at[14]
        ),
    ]

    late_normed = pl.ds(run, run)
    early_normed = pl.ds(0, run)
    late_cot = pl.ds(pl.multiple_of((1 - y_bit) * run, run), run)
    early_cot = pl.ds(pl.multiple_of(y_bit * run, run), run)

    def piece_load(i, slot):
        which, part = i // 6, i % 6
        source = (normed_others_ref, cot_others_ref)[which]
        late = (normed_late, cot_late)[which]
        into = staged.at[slot]
        if part in (0, 1, 3, 4):
            return [pltpu.make_async_copy(source.at[part], into, piece_sem.at[slot])]
        if part == 5:
            return [pltpu.make_async_copy(late.at[1], into, piece_sem.at[slot])]
        early_rows = (early_normed, early_cot)[which]
        late_rows = (late_normed, late_cot)[which]
        return [
            pltpu.make_async_copy(
                source.at[2, early_rows], into.at[early_rows], piece_sem.at[slot]
            ),
            pltpu.make_async_copy(
                late.at[0, late_rows], into.at[late_rows], piece_sem.at[2 + slot]
            ),
        ]

    def weight_loads(j, slot):
        return [
            pltpu.make_async_copy(
                w_gate_ref.at[:, tile_of(j)], gate_w.at[slot], weight_sem.at[slot, 0]
            ),
            pltpu.make_async_copy(
                w_up_ref.at[:, tile_of(j)], up_w.at[slot], weight_sem.at[slot, 1]
            ),
            pltpu.make_async_copy(
                w_down_ref.at[tile_of(j), :], down_w.at[slot], weight_sem.at[slot, 2]
            ),
        ]

    order = [0, 1, 3, 4, 6, 7, 9, 10, 2, 5, 8, 11]
    for i in range(2):
        for load in piece_load(order[i], i):
            load.start()
    loads[13].start()
    for load in loads[:4]:
        load.start()
    for load in weight_loads(0, 0):
        load.start()

    barrier = pltpu.get_barrier_semaphore()
    peers = []
    for m in range(1, 8):
        peer = dp
        for bit in (1, 2, 4):
            peer = flip(peer, bit) if m & bit else peer
        peers.append(peer)
    for device in [twin_id, y_id] + [(peer, tensor) for peer in peers]:
        pl.semaphore_signal(barrier, inc=1, device_id=device, device_id_type=MESH)
    pl.semaphore_wait(barrier, 9)
    late_copies = [
        remote(normed_others_ref.at[1, late_normed], normed_late.at[0, late_normed],
               late_send.at[0], late_recv.at[0], x_id),
        remote(cot_others_ref.at[2, early_cot], cot_late.at[0, early_cot],
               late_send.at[1], late_recv.at[1], y_id),
        remote(normed_others_ref.at[2, early_normed], normed_late.at[1, early_normed],
               late_send.at[2], late_recv.at[2], twin_id),
        remote(cot_others_ref.at[2, early_cot], cot_late.at[1, early_cot],
               late_send.at[3], late_recv.at[3], twin_id),
    ]
    for copy in late_copies:
        copy.start()

    loads[13].wait()

    def widen(r):
        window = pl.ds(pl.multiple_of(r * ROWS, ROWS), ROWS)
        for s in range(2):
            there = pl.ds(pl.multiple_of(s * half + r * ROWS, ROWS), ROWS)
            proj_part[0, s, window, :] = projected[0, there, :].astype(F32)

    loop(half // ROWS, widen)
    projected_copy = remote(proj_part.at[0], far_staged, end_send.at[2], end_recv.at[2], far_id)
    projected_copy.start()
    branch_copy = remote(branch_ref, branch_came, end_send.at[1], end_recv.at[1], y_id)

    late_twins = [
        remote(normed_late.at[0, late_normed], normed_late.at[1, late_normed],
               late_send.at[4], late_recv.at[4], twin_id),
        remote(cot_late.at[0, late_cot], cot_late.at[1, late_cot],
               late_send.at[5], late_recv.at[5], twin_id),
    ]
    def take_piece(place):
        i, slot = order[place], place % 2
        for load in piece_load(i, slot):
            load.wait()
        rows_to, turned_to = (normed, normed_t) if i < 6 else (cot, cot_t)
        base = {0: 0, 1: 1, 3: 2, 4: 3, 2: 4, 5: 5}[i % 6] * half

        def convert(r, slot=slot, rows_to=rows_to, base=base):
            window = pl.ds(pl.multiple_of(r * ROWS, ROWS), ROWS)
            rows_to[pl.ds(pl.multiple_of(base + r * ROWS, ROWS), ROWS), :] = staged[
                slot, window, :
            ].astype(BF16)

        loop(half // ROWS, convert)
        for part, block in enumerate((away_block, home_block)):
            turned_to[pl.ds(part * TILE, TILE), pl.ds(row_count + base, half)] = (
                staged[slot, :, block].T.astype(BF16)
            )
        if place == 5:
            for copy, later in zip(late_copies[:2], late_twins):
                copy.wait()
                later.start()
            branch_copy.start()
        if place == 6:
            for copy in late_copies[2:]:
                copy.wait()
        if place == 7:
            for copy in late_twins:
                copy.wait()
        if place + 2 < 12:
            for load in piece_load(order[place + 2], slot):
                load.start()
    for place in range(8):
        take_piece(place)
    for part in range(4):
        loads[part].wait()
        turned_to = (normed_t, cot_t)[part // 2]
        turned_to[pl.ds((part % 2) * TILE, TILE), pl.ds(0, row_count)] = (
            own_columns[part][...].astype(F32).T.astype(BF16)
        )

    def row_copy(j):
        window = (everything, everything, tile_of(j))
        return [
            remote(
                sent_out.at[window], came_out.at[window],
                row_send.at[0, j], row_recv.at[0, j], far_id,
            ),
            remote(
                down_sent.at[tile_of(j)], down_came.at[tile_of(j)],
                row_send.at[1, j], row_recv.at[1, j], far_id,
            ),
        ]

    def stores(j, slot):
        return [
            pltpu.make_async_copy(
                total.at[slot, pl.ds(0, 2), pl.ds(0, TILE)], sent_out.at[:, :, tile_of(j)],
                store_sem.at[slot, 0],
            ),
            pltpu.make_async_copy(
                total.at[slot, pl.ds(0, 2), pl.ds(TILE, TILE)], kept_out.at[:, :, tile_of(j)],
                store_sem.at[slot, 1],
            ),
            pltpu.make_async_copy(
                total.at[slot, 2, pl.ds(0, TILE)], down_sent.at[tile_of(j)],
                store_sem.at[slot, 2],
            ),
            pltpu.make_async_copy(
                total.at[slot, 2, pl.ds(TILE, TILE)], down_kept.at[tile_of(j)],
                store_sem.at[slot, 3],
            ),
        ]

    def unit_loads(j):
        return [
            pltpu.make_async_copy(
                source.at[:, tile_of(j)], units.at[i, pl.ds(0, row_count)], unit_sem.at[i]
            )
            for i, source in enumerate((gg_ref, gu_ref, act_ref))
        ]

    def feed_forward_tile(j, first=False):
        slot = j % 2
        for load in weight_loads(j, slot):
            load.wait()

        if first:
            for load in weight_loads(1, 1):
                load.start()
        else:

            @pl.when(j + 1 < tiles)
            def _():
                for load in weight_loads(j + 1, 1 - slot):
                    load.start()

        for load in unit_loads(j):
            load.start()

        def block(m):
            rows = pl.ds(pl.multiple_of(m * 512, 512), 512)
            to = pl.ds(pl.multiple_of(row_count + m * 512, 512), 512)
            gate = jnp.dot(normed[rows, :], gate_w[slot], preferred_element_type=F32)
            up = jnp.dot(normed[rows, :], up_w[slot], preferred_element_type=F32)
            back = lax.dot_general(
                cot[rows, :], down_w[slot], transposed, preferred_element_type=F32
            )
            sigmoid = jax.nn.sigmoid(gate)
            swish = gate * sigmoid
            units[2, to, :] = (swish * up).astype(BF16)
            units[0, to, :] = (back * up * sigmoid * (1.0 + gate * (1.0 - sigmoid))).astype(BF16)
            units[1, to, :] = (back * swish).astype(BF16)

        if first:
            loop(2, block)
            for place in range(8, 12):
                take_piece(place)
            block(2)
        else:
            loop(normed.shape[0] // 512, block)
        for load in unit_loads(j):
            load.wait()

        total[slot, 0] = jnp.dot(normed_t[...], units[0], preferred_element_type=F32)
        total[slot, 1] = jnp.dot(normed_t[...], units[1], preferred_element_type=F32)
        turned = jnp.dot(cot_t[...], units[2], preferred_element_type=F32)
        for part in range(2):
            total[slot, 2, pl.ds(part * TILE, TILE)] = turned[part * TILE : (part + 1) * TILE].T
        for store in stores(j, slot):
            store.start()
        for store in stores(j, slot):
            store.wait()
        for copy in row_copy(j):
            copy.start()

    def x_copies(slot):
        return [
            remote(out_part.at[0, slot], out_x.at[slot], x_send.at[0, slot],
                   x_recv.at[0, slot], x_id),
            remote(proj_part.at[0, slot], proj_x.at[slot], x_send.at[1, slot],
                   x_recv.at[1, slot], x_id),
        ]

    def attention_parts():
        for load in far_loads + loads[8:13]:
            load.wait()
        projected_copy.wait()

        def convert(r):
            window = pl.ds(pl.multiple_of(r * ROWS, ROWS), ROWS)
            block, rest = r // (run // ROWS), r % (run // ROWS)
            for s in range(2):
                which = core if s == 0 else 1 - core
                here = pl.ds(
                    pl.multiple_of(block * half + which * run + rest * ROWS, ROWS), ROWS
                )
                grad_attn[1, here, :] = staged[0, window, pl.ds(s * 1024, 1024)].astype(BF16)
                normed_one[1, here, :] = staged[1, window, pl.ds(s * 1024, 1024)].astype(BF16)
                there = pl.ds(pl.multiple_of(s * half + r * ROWS, ROWS), ROWS)
                projected[1, there, :] = far_staged[s, window, :].astype(BF16)
                heads[1, there, :] = far_heads[window, pl.ds(s * 512, 512)].astype(BF16)

        loop(half // ROWS, convert)
        for side in range(2):
            x_at = 1 - x_low if side == 0 else x_low
            for slot in range(2):
                z_at = 1 - z_high if slot == 0 else z_high
                columns = pl.ds(pl.multiple_of(z_at * 512 + x_at * 256, 256), 256)
                out_part[side, slot] = lax.dot_general(
                    heads[0], grad_attn[0, :, columns], over, preferred_element_type=F32
                ) + lax.dot_general(
                    heads[1], grad_attn[1, :, columns], over, preferred_element_type=F32
                )
                proj_part[side, slot] = lax.dot_general(
                    normed_one[0, :, columns], projected[0], over, preferred_element_type=F32
                ) + lax.dot_general(
                    normed_one[1, :, columns], projected[1], over, preferred_element_type=F32
                )
                if side == 0:
                    for copy in x_copies(slot):
                        copy.start()

    def core_copy(j):
        window = (everything, tile_of(j))
        return remote(
            staged.at[0].at[window], core_in.at[window], core_send.at[j], core_recv.at[j], twin_id
        )

    def y_copy(j):
        window = (everything, tile_of(j))
        return remote(
            staged.at[1].at[window], y_in.at[window], y_send.at[j], y_recv.at[j], y_id
        )

    def attention_sums():
        for load in loads[4:8] + loads[14:]:
            load.wait()

        def produce(j):
            product[...] = lax.dot_general(
                projected[0], w_proj[tile_of(j), :], transposed, preferred_element_type=F32
            )
            for block in range(2):
                for slot, which in ((0, 1 - core), (1, core)):
                    staged[slot, pl.ds(block * run, run), tile_of(j)] = product[
                        pl.ds(own_row(block, which), run), :
                    ]
            core_copy(j).start()

        def forward(j):
            core_copy(j).wait_recv()
            staged[1, :, tile_of(j)] = staged[1, :, tile_of(j)] + core_in[:, tile_of(j)]
            y_copy(j).start()

        produce(0)

        def step(j):
            produce(j + 1)
            forward(j)

        loop(tiles - 1, step)
        forward(tiles - 1)
        loop(tiles, lambda j: core_copy(j).wait_send())

    feed_forward_tile(0, first=True)
    for load in loads[4:13] + loads[14:]:
        load.start()
    far_loads = (
        [
            pltpu.make_async_copy(
                grad_attn_far_ref.at[s], staged.at[0, :, pl.ds(s * 1024, 1024)], piece_sem.at[s]
            )
            for s in range(2)
        ]
        + [
            pltpu.make_async_copy(
                normed_one_far_ref.at[s], staged.at[1, :, pl.ds(s * 1024, 1024)],
                piece_sem.at[2 + s],
            )
            for s in range(2)
        ]
        + [
            pltpu.make_async_copy(heads_far_ref, far_heads, piece_sem.at[5]),
        ]
    )
    for load in far_loads:
        load.start()


    def step(j):
        feed_forward_tile(j + 1)

        @pl.when(j == 0)
        def _():
            attention_parts()
            attention_sums()

    loop(tiles - 1, step)
    hidden_load = pltpu.make_async_copy(grad_hidden_ref, core_in, load_sem.at[0])
    hidden_load.start()

    def z_copies():
        return [
            remote(out_part.at[1, 0], out_came, z_send.at[0], z_recv.at[0], z_id),
            remote(proj_part.at[1, 0], proj_came, z_send.at[1], z_recv.at[1], z_id),
        ]

    for slot in range(2):
        for copy in x_copies(slot):
            copy.wait_recv()
        out_part[1, slot] = out_part[1, slot] + out_x[slot]
        proj_part[1, slot] = proj_part[1, slot] + proj_x[slot]
        if slot == 0:
            for copy in z_copies():
                copy.start()
    part_stores = [
        pltpu.make_async_copy(out_part.at[1, 1], out_mine, load_sem.at[1]),
        pltpu.make_async_copy(proj_part.at[1, 1], proj_mine, load_sem.at[2]),
    ]
    for store in part_stores:
        store.start()

    gain = gain_ref[...]
    gains[pl.ds(0, 1), :] = jnp.zeros_like(gain)
    gains[pl.ds(1, 1), :] = gain_two_ref[...]
    hidden_load.wait()
    loop(tiles, lambda j: y_copy(j).wait_recv())

    def norm_rows(i):
        window = pl.ds(pl.multiple_of(i * ROWS, ROWS), ROWS)
        incoming = staged[1, window, :] + y_in[window, :]
        values = tok[window, :].astype(F32)
        scale = lax.rsqrt(jnp.mean(values * values, axis=-1, keepdims=True) + EPSILON)
        weighted = incoming * gain
        inner = jnp.mean(weighted * values, axis=-1, keepdims=True)
        back = scale * weighted - values * (scale * scale * scale) * inner
        staged[0, window, :] = core_in[window, :] + back
        gains[pl.ds(0, 1), :] = gains[pl.ds(0, 1), :] + jnp.sum(
            incoming * values * scale, axis=0, keepdims=True
        )

    loop(half // ROWS, norm_rows)

    def to_rows(slot, out, sems, first):
        copies, kept = [], []
        for block in range(2):
            local, here = pl.ds(block * run, run), pl.ds(own_row(block, core), run)
            copies.append(remote(
                staged.at[slot, local], out.at[here],
                end_send.at[sems + block], end_recv.at[sems + block], twin_id,
            ))
            kept.append(pltpu.make_async_copy(
                staged.at[slot, local], out.at[here], load_sem.at[first + block]
            ))
        for copy in copies + kept:
            copy.start()
        return copies, kept

    input_copies, input_stores = to_rows(0, input_out, 3, 3)

    gain_twin = remote(gains, gains_came, gain_send.at[7], gain_recv.at[7], twin_id)
    gain_twin.start()

    loop(tiles, lambda j: y_copy(j).wait_send())
    branch_copy.wait()
    branch_loads = [
        pltpu.make_async_copy(branch_ref, staged.at[1], load_sem.at[5]),
        pltpu.make_async_copy(branch_came, y_in, load_sem.at[6]),
    ]
    for load in branch_loads:
        load.start()
    gain_twin.wait()
    gains[...] = gains[...] + gains_came[...]

    def gain_copy(m):
        return remote(
            gains.at[:, tile_of(peers[m])], gain_out.at[m], gain_send.at[m], gain_recv.at[m],
            (peers[m], tensor),
        )

    for m in range(7):
        gain_copy(m).start()
    gain_out[7] = gains[:, tile_of(dp)]
    for load in branch_loads:
        load.wait()

    def mixed_rows(i):
        window = pl.ds(pl.multiple_of(i * ROWS, ROWS), ROWS)
        staged[1, window, :] = staged[1, window, :] + y_in[window, :]

    loop(half // ROWS, mixed_rows)
    mixed_copy = remote(staged.at[1], core_in, end_send.at[5], end_recv.at[5], twin_id)
    mixed_copy.start()

    def put_mixed(source, which, first):
        def narrow(i):
            window = pl.ds(pl.multiple_of(i * ROWS, ROWS), ROWS)
            tok[window, :] = source[window, :].astype(BF16)

        loop(half // ROWS, narrow)
        copies = [
            pltpu.make_async_copy(
                tok.at[pl.ds(block * run, run)], mixed_out.at[pl.ds(own_row(block, which), run)],
                load_sem.at[first + block],
            )
            for block in range(2)
        ]
        for copy in copies:
            copy.start()
        for copy in copies:
            copy.wait()

    put_mixed(staged.at[1], core, 7)
    mixed_copy.wait()
    put_mixed(core_in, 1 - core, 9)

    for copy in part_stores + input_stores + input_copies:
        copy.wait()
    for m in range(7):
        gain_copy(m).wait()
    for slot in range(2):
        for copy in x_copies(slot):
            copy.wait_send()
    for copy in z_copies():
        copy.wait()
    for part in range(2):
        loop(tiles, lambda j: row_copy(j)[part].wait())


def last(
    normed_others, cot_others, normed, cot, act, gg, gu, w_gate, w_up, w_down,
    projected, branch, gain_two, w_query, w_key, w_value, heads, grad_attn, grad_attn_far,
    normed_one, normed_one_far, heads_far, grad_hidden, tokens, gain,
):
    row_count, width = tokens.shape
    half = row_count // 2
    tiles = width // TILE
    hidden_units = w_gate.shape[1]
    hbm = pl.BlockSpec(memory_space=pl.ANY)
    vmem = pl.BlockSpec(memory_space=pltpu.VMEM)
    wide = jax.ShapeDtypeStruct((half, width), F32)
    rows_pair = jax.ShapeDtypeStruct((2, TILE, hidden_units), F32)
    columns = jax.ShapeDtypeStruct((hidden_units, TILE), F32)
    out_block = jax.ShapeDtypeStruct((512, TILE), F32)
    proj_block = jax.ShapeDtypeStruct((TILE, 768), F32)
    dma = pltpu.SemaphoreType.DMA
    return pl.pallas_call(
        last_kernel,
        out_shape=(
            rows_pair, rows_pair, rows_pair, columns, columns, columns, out_block, out_block, proj_block, proj_block,
            jax.ShapeDtypeStruct((row_count, width), F32),
            jax.ShapeDtypeStruct((row_count, width), BF16),
            wide,
            jax.ShapeDtypeStruct((2, half, width), F32),
            jax.ShapeDtypeStruct((2, half, width), F32),
            jax.ShapeDtypeStruct((8, 2, TILE), F32),
        ),
        in_specs=[hbm] * 12 + [vmem] + [hbm] * 11 + [vmem],
        out_specs=(hbm,) * 15 + (vmem,),
        scratch_shapes=[
            pltpu.VMEM((6 * half, width), BF16),
            pltpu.VMEM((6 * half, width), BF16),
            pltpu.VMEM((2 * TILE, row_count + 6 * half), BF16),
            pltpu.VMEM((2 * TILE, row_count + 6 * half), BF16),
            pltpu.VMEM((3, row_count + 6 * half, TILE), BF16),
            pltpu.VMEM((2, width, TILE), BF16),
            pltpu.VMEM((2, width, TILE), BF16),
            pltpu.VMEM((2, TILE, width), BF16),
            pltpu.VMEM((2, 3, 2 * TILE, TILE), F32),
            pltpu.VMEM((2, half, width), F32),
            pltpu.VMEM((half, width), F32),
            pltpu.VMEM((half, width), F32),
            pltpu.VMEM((width, 768), BF16),
            pltpu.VMEM((half, width), BF16),
            pltpu.VMEM((2, row_count, 512), BF16),
            pltpu.VMEM((2, row_count, 1024), BF16),
            pltpu.VMEM((2, row_count, 1024), BF16),
            pltpu.VMEM((2, row_count, 768), BF16),
            pltpu.VMEM((2, 2, 512, TILE), F32),
            pltpu.VMEM((2, 2, TILE, 768), F32),
            pltpu.VMEM((2, 512, TILE), F32),
            pltpu.VMEM((2, TILE, 768), F32),
            pltpu.VMEM((2, half, 768), F32),
            pltpu.VMEM((half, 1024), F32),
            pltpu.VMEM((2, width), F32),
            pltpu.VMEM((2, width), F32),
            dma((15,)), dma((6,)), dma((2, 3)), dma((3,)), dma((2, 4)),
            dma((2, tiles)), dma((2, tiles)),
            dma((tiles,)), dma((tiles,)), dma((tiles,)), dma((tiles,)),
            dma((2, 2)), dma((2, 2)), dma((2,)), dma((2,)), dma((7,)), dma((7,)), dma((8,)), dma((8,)),
            dma((6,)), dma((6,)), pltpu.VMEM((row_count, TILE), F32),
        ],
        compiler_params=pltpu.CompilerParams(
            collective_id=1, has_side_effects=True, vmem_limit_bytes=64 * 1024 * 1024
        ),
        name="weight_gradients",
    )(
        normed_others, cot_others, normed, cot, act, gg, gu, w_gate, w_up, w_down,
        projected, branch, gain_two, w_query, w_key, w_value, heads, grad_attn, grad_attn_far,
        normed_one, normed_one_far, heads_far, grad_hidden, tokens, gain.reshape(1, width),
    )


def body(
    tokens,
    segments,
    positions,
    attn_gain,
    w_query,
    key_weight,
    value_weight,
    w_out,
    mlp_gain,
    w_gate,
    w_up,
    w_down,
    cotangent,
):
    groups = lax.axis_size("dp")
    place = lax.axis_index("dp")
    core = lax.axis_index("tensor") % 2
    row_count, width = tokens.shape
    half = row_count // 2
    hidden_units = w_gate.shape[1]
    tiles = width // TILE
    hbm = pl.BlockSpec(memory_space=pl.ANY)
    vmem = pl.BlockSpec(memory_space=pltpu.VMEM)
    wide = jax.ShapeDtypeStruct((half, width), F32)
    units = jax.ShapeDtypeStruct((row_count, hidden_units), BF16)
    square = jax.ShapeDtypeStruct((row_count, 512), BF16)
    dma = pltpu.SemaphoreType.DMA
    return pl.pallas_call(
        middle_kernel,
        out_shape=(
            jax.ShapeDtypeStruct((row_count, width), BF16),
            square, square, square, square,
            jax.ShapeDtypeStruct((2, half, width // 2), F32),
            jax.ShapeDtypeStruct((half, width // 2), F32),
            wide,
            jax.ShapeDtypeStruct((row_count, width), BF16),
            jax.ShapeDtypeStruct((row_count, 768), BF16),
            jax.ShapeDtypeStruct((2, half, width // 2), F32),
            wide,
            jax.ShapeDtypeStruct((row_count, width), BF16),
            units, units, units,
            jax.ShapeDtypeStruct((1, width), F32),
            jax.ShapeDtypeStruct((5, half, width), F32),
            jax.ShapeDtypeStruct((5, half, width), F32),
        ),
        in_specs=[hbm] * 6 + [vmem] * 2 + [hbm] * 3 + [vmem] * 4,
        out_specs=(hbm,) * 16 + (vmem,) + (hbm,) * 2,
        scratch_shapes=[
            pltpu.VMEM(w_gate.shape, BF16),
            pltpu.VMEM(w_up.shape, BF16),
            pltpu.VMEM(w_down.shape, BF16),
            pltpu.VMEM((row_count, width), BF16),
            pltpu.VMEM((half, width), F32),
            pltpu.VMEM((row_count, width), BF16),
            pltpu.VMEM((half, width), F32),
            pltpu.VMEM((half, width), F32),
            pltpu.VMEM((row_count, hidden_units), BF16),
            pltpu.VMEM((row_count, hidden_units), BF16),
            pltpu.VMEM((row_count, hidden_units), BF16),
            pltpu.VMEM((half, width), F32),
            pltpu.VMEM((2, half, width), F32),
            pltpu.VMEM((3, half, width), F32),
            pltpu.VMEM((2, half, width), F32),
            pltpu.VMEM((half, TILE), F32),
            pltpu.VMEM((8, row_count), F32),
            dma((13,)),
            dma((3, 2 * tiles)), dma((3, 2 * tiles)), dma((2, 2 * tiles)), dma((2, 2 * tiles)),
            dma((3, CHUNKS)), dma((3, CHUNKS)),
            dma((4, CHUNKS)), dma((4, CHUNKS)),
            dma((2, 2)), dma((2, 2)),
            dma((CHUNKS,)), dma((CHUNKS,)),
            dma((8,)), dma((8,)),
        ],
        compiler_params=pltpu.CompilerParams(
            collective_id=0, has_side_effects=True, vmem_limit_bytes=64 * 1024 * 1024
        ),
        name="feed_forward",
    )(
        w_query, w_key, w_value, w_out, tokens, cotangent,
        gain_one.reshape(1, width), gain.reshape(1, width), w_gate, w_up, w_down,
        segment.reshape(row_count, 1), segment.reshape(1, row_count), cosine, sine,
    )


def last_kernel(
    normed_others_ref,
    cot_others_ref,
    normed_ref,
    cot_ref,
    act_ref,
    gg_ref,
    gu_ref,
    w_gate_ref,
    w_up_ref,
    w_down_ref,
    projected_ref,
    branch_ref,
    gain_two_ref,
    w_query_ref,
    w_key_ref,
    w_value_ref,
    heads_ref,
    grad_attn_ref,
    grad_attn_far_ref,
    normed_one_ref,
    normed_one_far_ref,
    heads_far_ref,
    grad_hidden_ref,
    tokens_ref,
    gain_ref,
    kept_out,
    sent_out,
    came_out,
    down_kept,
    down_sent,
    down_came,
    out_mine,
    out_came,
    proj_mine,
    proj_came,
    input_out,
    mixed_out,
    branch_came,
    normed_late,
    cot_late,
    gain_out,
    normed,
    cot,
    normed_t,
    cot_t,
    units,
    gate_w,
    up_w,
    down_w,
    total,
    staged,
    core_in,
    y_in,
    w_proj,
    tok,
    heads,
    grad_attn,
    normed_one,
    projected,
    out_part,
    proj_part,
    out_x,
    proj_x,
    far_staged,
    far_heads,
    gains,
    gains_came,
    load_sem,
    piece_sem,
    weight_sem,
    unit_sem,
    store_sem,
    row_send,
    row_recv,
    core_send,
    core_recv,
    y_send,
    y_recv,
    x_send,
    x_recv,
    z_send,
    z_recv,
    end_send,
    end_recv,
    gain_send,
    gain_recv,
    late_send,
    late_recv,
    product,
):
    dp, tensor = lax.axis_index("dp"), lax.axis_index("tensor")
    core = tensor % 2
    x_low, z_low, z_high = dp % 2, (dp // 2) % 2, dp // 4
    twin_id = (dp, flip(tensor, 1))
    y_id = (dp, flip(tensor, 2))
    x_id = (flip(dp, 1), tensor)
    z_id = (flip(dp, 4), tensor)
    far_id = (flip(dp, 2), tensor)
    half, width = tok.shape
    row_count = 2 * half
    tiles = width // TILE
    run = half // 2
    y_bit = (tensor // 2) % 2

    def own_row(block, which):
        return pl.multiple_of(block * half + which * run, run)

    everything = slice(None)
    transposed = (((1,), (1,)), ((), ()))
    over = (((0,), (0,)), ((), ()))

    def remote(src, dst, send, recv, device):
        return pltpu.make_async_remote_copy(
            src_ref=src, dst_ref=dst, send_sem=send, recv_sem=recv,
            device_id=device, device_id_type=MESH,
        )

    def tile_of(j):
        return pl.ds(pl.multiple_of(j * TILE, TILE), TILE)

    away_block = tile_of(flip(dp, 2))
    home_block = tile_of(dp)
    near = [
        pl.ds(pl.multiple_of(b * 1024 + z_low * 512, 512), 512) for b in range(2)
    ]
    own_columns = [units.at[0, pl.ds(i * row_count, row_count)] for i in range(4)]
    loads = [
        pltpu.make_async_copy(normed_ref.at[:, away_block], own_columns[0], load_sem.at[0]),
        pltpu.make_async_copy(normed_ref.at[:, home_block], own_columns[1], load_sem.at[1]),
        pltpu.make_async_copy(cot_ref.at[:, away_block], own_columns[2], load_sem.at[2]),
        pltpu.make_async_copy(cot_ref.at[:, home_block], own_columns[3], load_sem.at[3]),
        pltpu.make_async_copy(w_query_ref, w_proj.at[:, pl.ds(0, 512)], load_sem.at[4]),
        pltpu.make_async_copy(w_key_ref, w_proj.at[:, pl.ds(512, 128)], load_sem.at[5]),
        pltpu.make_async_copy(w_value_ref, w_proj.at[:, pl.ds(640, 128)], load_sem.at[6]),
        pltpu.make_async_copy(
            tokens_ref.at[pl.ds(own_row(0, core), run)], tok.at[pl.ds(0, run)], load_sem.at[7]
        ),
        pltpu.make_async_copy(heads_ref, heads.at[0], load_sem.at[8]),
        pltpu.make_async_copy(
            grad_attn_ref.at[:, near[0]], grad_attn.at[0, :, pl.ds(0, 512)], load_sem.at[9]
        ),
        pltpu.make_async_copy(
            grad_attn_ref.at[:, near[1]], grad_attn.at[0, :, pl.ds(512, 512)], load_sem.at[10]
        ),
        pltpu.make_async_copy(
            normed_one_ref.at[:, near[0]], normed_one.at[0, :, pl.ds(0, 512)], load_sem.at[11]
        ),
        pltpu.make_async_copy(
            normed_one_ref.at[:, near[1]], normed_one.at[0, :, pl.ds(512, 512)], load_sem.at[12]
        ),
        pltpu.make_async_copy(projected_ref, projected.at[0], load_sem.at[13]),
        pltpu.make_async_copy(
            tokens_ref.at[pl.ds(own_row(1, core), run)], tok.at[pl.ds(run, run)], load_sem.at[14]
        ),
    ]

    late_normed = pl.ds(run, run)
    early_normed = pl.ds(0, run)
    late_cot = pl.ds(pl.multiple_of((1 - y_bit) * run, run), run)
    early_cot = pl.ds(pl.multiple_of(y_bit * run, run), run)

    def piece_load(i, slot):
        which, part = i // 6, i % 6
        source = (normed_others_ref, cot_others_ref)[which]
        late = (normed_late, cot_late)[which]
        into = staged.at[slot]
        if part in (0, 1, 3, 4):
            return [pltpu.make_async_copy(source.at[part], into, piece_sem.at[slot])]
        if part == 5:
            return [pltpu.make_async_copy(late.at[1], into, piece_sem.at[slot])]
        early_rows = (early_normed, early_cot)[which]
        late_rows = (late_normed, late_cot)[which]
        return [
            pltpu.make_async_copy(
                source.at[2, early_rows], into.at[early_rows], piece_sem.at[slot]
            ),
            pltpu.make_async_copy(
                late.at[0, late_rows], into.at[late_rows], piece_sem.at[2 + slot]
            ),
        ]

    def weight_loads(j, slot):
        return [
            pltpu.make_async_copy(
                w_gate_ref.at[:, tile_of(j)], gate_w.at[slot], weight_sem.at[slot, 0]
            ),
            pltpu.make_async_copy(
                w_up_ref.at[:, tile_of(j)], up_w.at[slot], weight_sem.at[slot, 1]
            ),
            pltpu.make_async_copy(
                w_down_ref.at[tile_of(j), :], down_w.at[slot], weight_sem.at[slot, 2]
            ),
        ]

    order = [0, 1, 3, 4, 6, 7, 9, 10, 2, 5, 8, 11]
    for i in range(2):
        for load in piece_load(order[i], i):
            load.start()
    loads[13].start()
    for load in loads[:4]:
        load.start()
    for load in weight_loads(0, 0):
        load.start()

    barrier = pltpu.get_barrier_semaphore()
    peers = []
    for m in range(1, 8):
        peer = dp
        for bit in (1, 2, 4):
            peer = flip(peer, bit) if m & bit else peer
        peers.append(peer)
    for device in [twin_id, y_id] + [(peer, tensor) for peer in peers]:
        pl.semaphore_signal(barrier, inc=1, device_id=device, device_id_type=MESH)
    pl.semaphore_wait(barrier, 9)
    late_copies = [
        remote(normed_others_ref.at[1, late_normed], normed_late.at[0, late_normed],
               late_send.at[0], late_recv.at[0], x_id),
        remote(cot_others_ref.at[2, early_cot], cot_late.at[0, early_cot],
               late_send.at[1], late_recv.at[1], y_id),
        remote(normed_others_ref.at[2, early_normed], normed_late.at[1, early_normed],
               late_send.at[2], late_recv.at[2], twin_id),
        remote(cot_others_ref.at[2, early_cot], cot_late.at[1, early_cot],
               late_send.at[3], late_recv.at[3], twin_id),
    ]
    for copy in late_copies:
        copy.start()

    loads[13].wait()

    def widen(r):
        window = pl.ds(pl.multiple_of(r * ROWS, ROWS), ROWS)
        for s in range(2):
            there = pl.ds(pl.multiple_of(s * half + r * ROWS, ROWS), ROWS)
            proj_part[0, s, window, :] = projected[0, there, :].astype(F32)

    loop(half // ROWS, widen)
    projected_copy = remote(proj_part.at[0], far_staged, end_send.at[2], end_recv.at[2], far_id)
    projected_copy.start()
    branch_copy = remote(branch_ref, branch_came, end_send.at[1], end_recv.at[1], y_id)

    late_twins = [
        remote(normed_late.at[0, late_normed], normed_late.at[1, late_normed],
               late_send.at[4], late_recv.at[4], twin_id),
        remote(cot_late.at[0, late_cot], cot_late.at[1, late_cot],
               late_send.at[5], late_recv.at[5], twin_id),
    ]
    def take_piece(place):
        i, slot = order[place], place % 2
        for load in piece_load(i, slot):
            load.wait()
        rows_to, turned_to = (normed, normed_t) if i < 6 else (cot, cot_t)
        base = {0: 0, 1: 1, 3: 2, 4: 3, 2: 4, 5: 5}[i % 6] * half

        def convert(r, slot=slot, rows_to=rows_to, base=base):
            window = pl.ds(pl.multiple_of(r * ROWS, ROWS), ROWS)
            rows_to[pl.ds(pl.multiple_of(base + r * ROWS, ROWS), ROWS), :] = staged[
                slot, window, :
            ].astype(BF16)

        loop(half // ROWS, convert)
        for part, block in enumerate((away_block, home_block)):
            turned_to[pl.ds(part * TILE, TILE), pl.ds(row_count + base, half)] = (
                staged[slot, :, block].T.astype(BF16)
            )
        if place == 5:
            for copy, later in zip(late_copies[:2], late_twins):
                copy.wait()
                later.start()
            branch_copy.start()
        if place == 6:
            for copy in late_copies[2:]:
                copy.wait()
        if place == 7:
            for copy in late_twins:
                copy.wait()
        if place + 2 < 12:
            for load in piece_load(order[place + 2], slot):
                load.start()
    for place in range(8):
        take_piece(place)
    for part in range(4):
        loads[part].wait()
        turned_to = (normed_t, cot_t)[part // 2]
        turned_to[pl.ds((part % 2) * TILE, TILE), pl.ds(0, row_count)] = (
            own_columns[part][...].astype(F32).T.astype(BF16)
        )

    def row_copy(j):
        window = (everything, everything, tile_of(j))
        return [
            remote(
                sent_out.at[window], came_out.at[window],
                row_send.at[0, j], row_recv.at[0, j], far_id,
            ),
            remote(
                down_sent.at[tile_of(j)], down_came.at[tile_of(j)],
                row_send.at[1, j], row_recv.at[1, j], far_id,
            ),
        ]

    def stores(j, slot):
        return [
            pltpu.make_async_copy(
                total.at[slot, pl.ds(0, 2), pl.ds(0, TILE)], sent_out.at[:, :, tile_of(j)],
                store_sem.at[slot, 0],
            ),
            pltpu.make_async_copy(
                total.at[slot, pl.ds(0, 2), pl.ds(TILE, TILE)], kept_out.at[:, :, tile_of(j)],
                store_sem.at[slot, 1],
            ),
            pltpu.make_async_copy(
                total.at[slot, 2, pl.ds(0, TILE)], down_sent.at[tile_of(j)],
                store_sem.at[slot, 2],
            ),
            pltpu.make_async_copy(
                total.at[slot, 2, pl.ds(TILE, TILE)], down_kept.at[tile_of(j)],
                store_sem.at[slot, 3],
            ),
        ]

    def unit_loads(j):
        return [
            pltpu.make_async_copy(
                source.at[:, tile_of(j)], units.at[i, pl.ds(0, row_count)], unit_sem.at[i]
            )
            for i, source in enumerate((gg_ref, gu_ref, act_ref))
        ]

    def feed_forward_tile(j, first=False):
        slot = j % 2
        for load in weight_loads(j, slot):
            load.wait()

        if first:
            for load in weight_loads(1, 1):
                load.start()
        else:

            @pl.when(j + 1 < tiles)
            def _():
                for load in weight_loads(j + 1, 1 - slot):
                    load.start()

        for load in unit_loads(j):
            load.start()

        def block(m):
            rows = pl.ds(pl.multiple_of(m * 512, 512), 512)
            to = pl.ds(pl.multiple_of(row_count + m * 512, 512), 512)
            gate = jnp.dot(normed[rows, :], gate_w[slot], preferred_element_type=F32)
            up = jnp.dot(normed[rows, :], up_w[slot], preferred_element_type=F32)
            back = lax.dot_general(
                cot[rows, :], down_w[slot], transposed, preferred_element_type=F32
            )
            sigmoid = jax.nn.sigmoid(gate)
            swish = gate * sigmoid
            units[2, to, :] = (swish * up).astype(BF16)
            units[0, to, :] = (back * up * sigmoid * (1.0 + gate * (1.0 - sigmoid))).astype(BF16)
            units[1, to, :] = (back * swish).astype(BF16)

        if first:
            loop(2, block)
            for place in range(8, 12):
                take_piece(place)
            block(2)
        else:
            loop(normed.shape[0] // 512, block)
        for load in unit_loads(j):
            load.wait()

        total[slot, 0] = jnp.dot(normed_t[...], units[0], preferred_element_type=F32)
        total[slot, 1] = jnp.dot(normed_t[...], units[1], preferred_element_type=F32)
        turned = jnp.dot(cot_t[...], units[2], preferred_element_type=F32)
        for part in range(2):
            total[slot, 2, pl.ds(part * TILE, TILE)] = turned[part * TILE : (part + 1) * TILE].T
        for store in stores(j, slot):
            store.start()
        for store in stores(j, slot):
            store.wait()
        for copy in row_copy(j):
            copy.start()

    def x_copies(slot):
        return [
            remote(out_part.at[0, slot], out_x.at[slot], x_send.at[0, slot],
                   x_recv.at[0, slot], x_id),
            remote(proj_part.at[0, slot], proj_x.at[slot], x_send.at[1, slot],
                   x_recv.at[1, slot], x_id),
        ]

    def attention_parts():
        for load in far_loads + loads[8:13]:
            load.wait()
        projected_copy.wait()

        def convert(r):
            window = pl.ds(pl.multiple_of(r * ROWS, ROWS), ROWS)
            block, rest = r // (run // ROWS), r % (run // ROWS)
            for s in range(2):
                which = core if s == 0 else 1 - core
                here = pl.ds(
                    pl.multiple_of(block * half + which * run + rest * ROWS, ROWS), ROWS
                )
                grad_attn[1, here, :] = staged[0, window, pl.ds(s * 1024, 1024)].astype(BF16)
                normed_one[1, here, :] = staged[1, window, pl.ds(s * 1024, 1024)].astype(BF16)
                there = pl.ds(pl.multiple_of(s * half + r * ROWS, ROWS), ROWS)
                projected[1, there, :] = far_staged[s, window, :].astype(BF16)
                heads[1, there, :] = far_heads[window, pl.ds(s * 512, 512)].astype(BF16)

        loop(half // ROWS, convert)
        for side in range(2):
            x_at = 1 - x_low if side == 0 else x_low
            for slot in range(2):
                z_at = 1 - z_high if slot == 0 else z_high
                columns = pl.ds(pl.multiple_of(z_at * 512 + x_at * 256, 256), 256)
                out_part[side, slot] = lax.dot_general(
                    heads[0], grad_attn[0, :, columns], over, preferred_element_type=F32
                ) + lax.dot_general(
                    heads[1], grad_attn[1, :, columns], over, preferred_element_type=F32
                )
                proj_part[side, slot] = lax.dot_general(
                    normed_one[0, :, columns], projected[0], over, preferred_element_type=F32
                ) + lax.dot_general(
                    normed_one[1, :, columns], projected[1], over, preferred_element_type=F32
                )
                if side == 0:
                    for copy in x_copies(slot):
                        copy.start()

    def core_copy(j):
        window = (everything, tile_of(j))
        return remote(
            staged.at[0].at[window], core_in.at[window], core_send.at[j], core_recv.at[j], twin_id
        )

    def y_copy(j):
        window = (everything, tile_of(j))
        return remote(
            staged.at[1].at[window], y_in.at[window], y_send.at[j], y_recv.at[j], y_id
        )

    def attention_sums():
        for load in loads[4:8] + loads[14:]:
            load.wait()

        def produce(j):
            product[...] = lax.dot_general(
                projected[0], w_proj[tile_of(j), :], transposed, preferred_element_type=F32
            )
            for block in range(2):
                for slot, which in ((0, 1 - core), (1, core)):
                    staged[slot, pl.ds(block * run, run), tile_of(j)] = product[
                        pl.ds(own_row(block, which), run), :
                    ]
            core_copy(j).start()

        def forward(j):
            core_copy(j).wait_recv()
            staged[1, :, tile_of(j)] = staged[1, :, tile_of(j)] + core_in[:, tile_of(j)]
            y_copy(j).start()

        produce(0)

        def step(j):
            produce(j + 1)
            forward(j)

        loop(tiles - 1, step)
        forward(tiles - 1)
        loop(tiles, lambda j: core_copy(j).wait_send())

    feed_forward_tile(0, first=True)
    for load in loads[4:13] + loads[14:]:
        load.start()
    far_loads = (
        [
            pltpu.make_async_copy(
                grad_attn_far_ref.at[s], staged.at[0, :, pl.ds(s * 1024, 1024)], piece_sem.at[s]
            )
            for s in range(2)
        ]
        + [
            pltpu.make_async_copy(
                normed_one_far_ref.at[s], staged.at[1, :, pl.ds(s * 1024, 1024)],
                piece_sem.at[2 + s],
            )
            for s in range(2)
        ]
        + [
            pltpu.make_async_copy(heads_far_ref, far_heads, piece_sem.at[5]),
        ]
    )
    for load in far_loads:
        load.start()


    def step(j):
        feed_forward_tile(j + 1)

        @pl.when(j == 0)
        def _():
            attention_parts()
            attention_sums()

    loop(tiles - 1, step)
    hidden_load = pltpu.make_async_copy(grad_hidden_ref, core_in, load_sem.at[0])
    hidden_load.start()

    def z_copies():
        return [
            remote(out_part.at[1, 0], out_came, z_send.at[0], z_recv.at[0], z_id),
            remote(proj_part.at[1, 0], proj_came, z_send.at[1], z_recv.at[1], z_id),
        ]

    for slot in range(2):
        for copy in x_copies(slot):
            copy.wait_recv()
        out_part[1, slot] = out_part[1, slot] + out_x[slot]
        proj_part[1, slot] = proj_part[1, slot] + proj_x[slot]
        if slot == 0:
            for copy in z_copies():
                copy.start()
    part_stores = [
        pltpu.make_async_copy(out_part.at[1, 1], out_mine, load_sem.at[1]),
        pltpu.make_async_copy(proj_part.at[1, 1], proj_mine, load_sem.at[2]),
    ]
    for store in part_stores:
        store.start()

    gain = gain_ref[...]
    gains[pl.ds(0, 1), :] = jnp.zeros_like(gain)
    gains[pl.ds(1, 1), :] = gain_two_ref[...]
    hidden_load.wait()
    loop(tiles, lambda j: y_copy(j).wait_recv())

    def norm_rows(i):
        window = pl.ds(pl.multiple_of(i * ROWS, ROWS), ROWS)
        incoming = staged[1, window, :] + y_in[window, :]
        values = tok[window, :].astype(F32)
        scale = lax.rsqrt(jnp.mean(values * values, axis=-1, keepdims=True) + EPSILON)
        weighted = incoming * gain
        inner = jnp.mean(weighted * values, axis=-1, keepdims=True)
        back = scale * weighted - values * (scale * scale * scale) * inner
        staged[0, window, :] = core_in[window, :] + back
        gains[pl.ds(0, 1), :] = gains[pl.ds(0, 1), :] + jnp.sum(
            incoming * values * scale, axis=0, keepdims=True
        )

    loop(half // ROWS, norm_rows)

    def to_rows(slot, out, sems, first):
        copies, kept = [], []
        for block in range(2):
            local, here = pl.ds(block * run, run), pl.ds(own_row(block, core), run)
            copies.append(remote(
                staged.at[slot, local], out.at[here],
                end_send.at[sems + block], end_recv.at[sems + block], twin_id,
            ))
            kept.append(pltpu.make_async_copy(
                staged.at[slot, local], out.at[here], load_sem.at[first + block]
            ))
        for copy in copies + kept:
            copy.start()
        return copies, kept

    input_copies, input_stores = to_rows(0, input_out, 3, 3)

    gain_twin = remote(gains, gains_came, gain_send.at[7], gain_recv.at[7], twin_id)
    gain_twin.start()

    loop(tiles, lambda j: y_copy(j).wait_send())
    branch_copy.wait()
    branch_loads = [
        pltpu.make_async_copy(branch_ref, staged.at[1], load_sem.at[5]),
        pltpu.make_async_copy(branch_came, y_in, load_sem.at[6]),
    ]
    for load in branch_loads:
        load.start()
    gain_twin.wait()
    gains[...] = gains[...] + gains_came[...]

    def gain_copy(m):
        return remote(
            gains.at[:, tile_of(peers[m])], gain_out.at[m], gain_send.at[m], gain_recv.at[m],
            (peers[m], tensor),
        )

    for m in range(7):
        gain_copy(m).start()
    gain_out[7] = gains[:, tile_of(dp)]
    for load in branch_loads:
        load.wait()

    def mixed_rows(i):
        window = pl.ds(pl.multiple_of(i * ROWS, ROWS), ROWS)
        staged[1, window, :] = staged[1, window, :] + y_in[window, :]

    loop(half // ROWS, mixed_rows)
    mixed_copy = remote(staged.at[1], core_in, end_send.at[5], end_recv.at[5], twin_id)
    mixed_copy.start()

    def put_mixed(source, which, first):
        def narrow(i):
            window = pl.ds(pl.multiple_of(i * ROWS, ROWS), ROWS)
            tok[window, :] = source[window, :].astype(BF16)

        loop(half // ROWS, narrow)
        copies = [
            pltpu.make_async_copy(
                tok.at[pl.ds(block * run, run)], mixed_out.at[pl.ds(own_row(block, which), run)],
                load_sem.at[first + block],
            )
            for block in range(2)
        ]
        for copy in copies:
            copy.start()
        for copy in copies:
            copy.wait()

    put_mixed(staged.at[1], core, 7)
    mixed_copy.wait()
    put_mixed(core_in, 1 - core, 9)

    for copy in part_stores + input_stores + input_copies:
        copy.wait()
    for m in range(7):
        gain_copy(m).wait()
    for slot in range(2):
        for copy in x_copies(slot):
            copy.wait_send()
    for copy in z_copies():
        copy.wait()
    for part in range(2):
        loop(tiles, lambda j: row_copy(j)[part].wait())


def last(
    normed_others, cot_others, normed, cot, act, gg, gu, w_gate, w_up, w_down,
    projected, branch, gain_two, w_query, w_key, w_value, heads, grad_attn, grad_attn_far,
    normed_one, normed_one_far, heads_far, grad_hidden, tokens, gain,
):
    row_count, width = tokens.shape
    half = row_count // 2
    tiles = width // TILE
    hidden_units = w_gate.shape[1]
    hbm = pl.BlockSpec(memory_space=pl.ANY)
    vmem = pl.BlockSpec(memory_space=pltpu.VMEM)
    wide = jax.ShapeDtypeStruct((half, width), F32)
    rows_pair = jax.ShapeDtypeStruct((2, TILE, hidden_units), F32)
    columns = jax.ShapeDtypeStruct((hidden_units, TILE), F32)
    out_block = jax.ShapeDtypeStruct((512, TILE), F32)
    proj_block = jax.ShapeDtypeStruct((TILE, 768), F32)
    dma = pltpu.SemaphoreType.DMA
    return pl.pallas_call(
        last_kernel,
        out_shape=(
            rows_pair, rows_pair, rows_pair, columns, columns, columns, out_block, out_block, proj_block, proj_block,
            jax.ShapeDtypeStruct((row_count, width), F32),
            jax.ShapeDtypeStruct((row_count, width), BF16),
            wide,
            jax.ShapeDtypeStruct((2, half, width), F32),
            jax.ShapeDtypeStruct((2, half, width), F32),
            jax.ShapeDtypeStruct((8, 2, TILE), F32),
        ),
        in_specs=[hbm] * 12 + [vmem] + [hbm] * 11 + [vmem],
        out_specs=(hbm,) * 15 + (vmem,),
        scratch_shapes=[
            pltpu.VMEM((6 * half, width), BF16),
            pltpu.VMEM((6 * half, width), BF16),
            pltpu.VMEM((2 * TILE, row_count + 6 * half), BF16),
            pltpu.VMEM((2 * TILE, row_count + 6 * half), BF16),
            pltpu.VMEM((3, row_count + 6 * half, TILE), BF16),
            pltpu.VMEM((2, width, TILE), BF16),
            pltpu.VMEM((2, width, TILE), BF16),
            pltpu.VMEM((2, TILE, width), BF16),
            pltpu.VMEM((2, 3, 2 * TILE, TILE), F32),
            pltpu.VMEM((2, half, width), F32),
            pltpu.VMEM((half, width), F32),
            pltpu.VMEM((half, width), F32),
            pltpu.VMEM((width, 768), BF16),
            pltpu.VMEM((half, width), BF16),
            pltpu.VMEM((2, row_count, 512), BF16),
            pltpu.VMEM((2, row_count, 1024), BF16),
            pltpu.VMEM((2, row_count, 1024), BF16),
            pltpu.VMEM((2, row_count, 768), BF16),
            pltpu.VMEM((2, 2, 512, TILE), F32),
            pltpu.VMEM((2, 2, TILE, 768), F32),
            pltpu.VMEM((2, 512, TILE), F32),
            pltpu.VMEM((2, TILE, 768), F32),
            pltpu.VMEM((2, half, 768), F32),
            pltpu.VMEM((half, 1024), F32),
            pltpu.VMEM((2, width), F32),
            pltpu.VMEM((2, width), F32),
            dma((15,)), dma((6,)), dma((2, 3)), dma((3,)), dma((2, 4)),
            dma((2, tiles)), dma((2, tiles)),
            dma((tiles,)), dma((tiles,)), dma((tiles,)), dma((tiles,)),
            dma((2, 2)), dma((2, 2)), dma((2,)), dma((2,)), dma((7,)), dma((7,)), dma((8,)), dma((8,)),
            dma((6,)), dma((6,)), pltpu.VMEM((row_count, TILE), F32),
        ],
        compiler_params=pltpu.CompilerParams(
            collective_id=1, has_side_effects=True, vmem_limit_bytes=64 * 1024 * 1024
        ),
        name="weight_gradients",
    )(
        normed_others, cot_others, normed, cot, act, gg, gu, w_gate, w_up, w_down,
        projected, branch, gain_two, w_query, w_key, w_value, heads, grad_attn, grad_attn_far,
        normed_one, normed_one_far, heads_far, grad_hidden, tokens, gain.reshape(1, width),
    )


def body(
    tokens,
    segments,
    positions,
    attn_gain,
    w_query,
    key_weight,
    value_weight,
    w_out,
    mlp_gain,
    w_gate,
    w_up,
    w_down,
    cotangent,
):
    groups = lax.axis_size("dp")
    place = lax.axis_index("dp")
    core = lax.axis_index("tensor") % 2
    all_bits = [1 << i for i in range(groups.bit_length() - 1)]
    shared_bits = [bit for bit in (4, 1) if bit < groups]
    split_bits = [bit for bit in all_bits if bit not in shared_bits]

    def blocks(matrix, offsets):
        width = matrix.shape[1] // groups
        return [
            lax.dynamic_slice_in_dim(matrix, (place ^ offset) * width, width, 1)
            for offset in offsets
        ]

    def offsets_of(bits):
        found = [0]
        for bit in bits:
            found = found + [offset + bit for offset in found]
        return found

    def reduced(matrix_of, bits):
        sent = None
        for bit in bits:
            rest = bits[bits.index(bit) + 1 :]
            offsets = offsets_of(rest)
            if sent is None:
                away = matrix_of([offset ^ bit for offset in offsets])
                home = matrix_of(offsets)
            else:
                away = [sent[offset ^ bit] for offset in offsets]
                home = [sent[offset] for offset in offsets]
            came = swap(away, "dp", bit)
            sent = {offset: h + c for offset, h, c in zip(offsets, home, came)}
        return sent[0]

    row_count, width = tokens.shape
    query_width, kv_width = w_query.shape[1], key_weight.shape[1]
    half_dim = HEAD_SIZE // 2
    frequency = 500000.0 ** (-(jnp.arange(half_dim).astype(F32) * 2.0 / HEAD_SIZE))
    angles = positions.reshape(row_count, 1).astype(F32) * jnp.tile(frequency, 4)
    cosine_tile = jnp.cos(angles)
    sine_tile = jnp.sin(angles) * jnp.where(jnp.arange(128) % HEAD_SIZE < half_dim, 1.0, -1.0)
    (
        normed_one,
        head_outputs,
        _,
        _,
        _,
        normed_one_far,
        heads_far,
        grad_hidden,
        grad_attn,
        projected,
        grad_attn_far,
        branch,
        normed_two,
        activation,
        grad_gate_in,
        grad_up_in,
        gain_two_half,
        cotangent_others,
        normed_others,
    ) = middle(
        w_query, key_weight, value_weight, w_out, tokens, cotangent,
        attn_gain, mlp_gain, w_gate, w_up, w_down, segments, cosine_tile, sine_tile,
    )
    (
        kept,
        _,
        came,
        down_kept,
        _,
        down_came,
        out_mine,
        out_came,
        proj_mine,
        proj_came,
        grad_input,
        mixed,
        _,
        _,
        _,
        gains,
    ) = last(
        normed_others, cotangent_others, normed_two, cotangent, activation, grad_gate_in,
        grad_up_in, w_gate, w_up, w_down, projected, branch, gain_two_half, w_query, key_weight,
        value_weight, head_outputs, grad_attn, grad_attn_far, normed_one, normed_one_far,
        heads_far, grad_hidden, tokens, attn_gain,
    )
    grad_w_gate = kept[0] + came[0]
    grad_w_up = kept[1] + came[1]
    grad_w_down = down_kept + down_came
    grad_w_out = out_mine + out_came
    grad_w_proj = proj_mine + proj_came
    grad_w_query = grad_w_proj[:, :query_width]
    grad_w_key = grad_w_proj[:, query_width : query_width + kv_width]
    grad_w_value = grad_w_proj[:, query_width + kv_width :]

    gains = jnp.sum(gains, axis=0)
    grad_attn_gain, grad_mlp_gain = gains[0], gains[1]
    return (
        mixed,
        grad_input,
        grad_attn_gain,
        grad_w_query,
        grad_w_key,
        grad_w_value,
        grad_w_out,
        grad_mlp_gain,
        grad_w_gate,
        grad_w_up,
        grad_w_down,
    )


def product(left_matrix, right_matrix):
    return jnp.dot(left_matrix, right_matrix, preferred_element_type=F32)


def over_rows(left_matrix, right_matrix):
    return lax.dot_general(
        left_matrix, right_matrix, (((0,), (0,)), ((), ())), preferred_element_type=F32
    )


def against(gradient, weight):
    return lax.dot_general(
        gradient, weight, (((1,), (1,)), ((), ())), preferred_element_type=F32
    )


def narrowed(value):
    return jnp.where(value == value, value, 0.0).astype(BF16)


def tensor_sum_half(partial, core):
    total = half_of(partial, core) + swap(half_of(partial, 1 - core), "tensor", 1)
    bit = 2
    while bit < lax.axis_size("tensor"):
        total = total + swap(total, "tensor", bit)
        bit *= 2
    return total


def tables(places):
    half_dim = HEAD_SIZE // 2
    frequency = 500000.0 ** (-(jnp.arange(half_dim).astype(F32) * 2.0 / HEAD_SIZE))
    angles = places.astype(F32)[..., None] * frequency
    cosine_lookup = jnp.cos(angles)
    sine_lookup = jnp.sin(angles)
    return (
        jnp.concatenate([cosine_lookup, cosine_lookup], -1),
        jnp.concatenate([sine_lookup, sine_lookup], -1),
    )


def apply_rotary(field, cosine_lookup, sine_lookup):
    half_dim = HEAD_SIZE // 2
    turned = jnp.concatenate([-field[..., half_dim:], field[..., :half_dim]], -1)
    return field * cosine_lookup + turned * sine_lookup


def unrotate(gradient, cosine_lookup, sine_lookup):
    half_dim = HEAD_SIZE // 2
    sined = gradient * sine_lookup
    return gradient * cosine_lookup + jnp.concatenate(
        [sined[..., half_dim:], -sined[..., :half_dim]], -1
    )


def allowed_pairs(segment):
    spots = jnp.arange(segment.shape[0])
    return (spots[:, None] >= spots[None, :]) & (segment[:, None] == segment[None, :])


def scores(query_rotated, key_rotated, segment):
    raw_scores = jnp.einsum(
        "qhgd,khd->hgqk", query_rotated, key_rotated, preferred_element_type=F32
    ) * HEAD_SIZE ** (-0.5)
    return jnp.where(allowed_pairs(segment), raw_scores, MASKED)


def attend_forward(query_rotated, key_rotated, value_seq, segment):
    masked = scores(query_rotated, key_rotated, segment)
    row_peak = jnp.max(masked, axis=-1, keepdims=True)
    log_total = row_peak + jnp.log(jnp.sum(jnp.exp(masked - row_peak), axis=-1, keepdims=True))
    attention_probs = jnp.exp(masked - log_total).astype(BF16)
    combined_heads = jnp.einsum(
        "ojus,sov->uojv", attention_probs, value_seq, preferred_element_type=F32
    )
    return (combined_heads, log_total)


def attend_backward(query_rotated, key_rotated, value_seq, segment, log_total, grad_heads):
    masked = scores(query_rotated, key_rotated, segment)
    attention_probs = jnp.exp(masked - log_total)
    grad_probs = jnp.einsum("qhgd,khd->hgqk", grad_heads, value_seq, preferred_element_type=F32)
    row_sum = jnp.sum(attention_probs * grad_probs, axis=-1, keepdims=True)
    grad_raw = jnp.where(
        allowed_pairs(segment), attention_probs * (grad_probs - row_sum), 0.0
    ).astype(BF16)
    factor = HEAD_SIZE ** (-0.5)
    grad_query_rot = (
        jnp.einsum("ojus,sov->uojv", grad_raw, key_rotated, preferred_element_type=F32) * factor
    )
    grad_key_rot = (
        jnp.einsum("hgqk,qhgd->khd", grad_raw, query_rotated, preferred_element_type=F32) * factor
    )
    grad_value_rot = jnp.einsum(
        "hgqk,qhgd->khd", attention_probs.astype(BF16), grad_heads, preferred_element_type=F32
    )
    return (grad_query_rot, grad_key_rot, grad_value_rot)


def per_sequence(step, *fields):
    results = [step(*[field[s] for field in fields]) for s in range(fields[0].shape[0])]
    return [jnp.stack(parts) for parts in zip(*results)]


def general_body(
    tokens,
    segments,
    positions,
    attn_gain,
    w_query,
    key_weight,
    value_weight,
    w_out,
    mlp_gain,
    w_gate,
    w_up,
    w_down,
    cotangent,
):
    groups = lax.axis_size("dp")
    place = lax.axis_index("dp")
    core = lax.axis_index("tensor") % 2
    all_bits = [1 << i for i in range(groups.bit_length() - 1)]
    shared_bits = [bit for bit in (4, 1) if bit < groups]
    split_bits = [bit for bit in all_bits if bit not in shared_bits]

    def gathered(half):
        parts = [half]
        for bit in shared_bits:
            parts = parts + [swap(part, "dp", bit) for part in parts]
        others = parts[1:]
        twins = [swap(part, "tensor", 1) for part in others]
        return jnp.concatenate([narrowed(part) for part in others + twins], axis=0)

    def blocks(matrix, offsets):
        width = matrix.shape[1] // groups
        return [
            lax.dynamic_slice_in_dim(matrix, (place ^ offset) * width, width, 1)
            for offset in offsets
        ]

    def offsets_of(bits):
        found = [0]
        for bit in bits:
            found = found + [offset + bit for offset in found]
        return found

    def reduced(matrix_of, bits):
        sent = None
        for bit in bits:
            rest = bits[bits.index(bit) + 1 :]
            offsets = offsets_of(rest)
            if sent is None:
                away = matrix_of([offset ^ bit for offset in offsets])
                home = matrix_of(offsets)
            else:
                away = [sent[offset ^ bit] for offset in offsets]
                home = [sent[offset] for offset in offsets]
            came = swap(away, "dp", bit)
            sent = {offset: h + c for offset, h, c in zip(offsets, home, came)}
        return sent[0]

    inputs = tokens.astype(F32)
    row_count, width = inputs.shape
    seq_count, seq_len = segments.shape
    query_heads = w_query.shape[1] // HEAD_SIZE
    kv_heads = key_weight.shape[1] // HEAD_SIZE
    group_size = query_heads // kv_heads
    query_width, kv_width = w_query.shape[1], key_weight.shape[1]

    cotangent_half = half_of(cotangent, core).astype(F32)
    cotangent_others = gathered(cotangent_half)

    scale_one = lax.rsqrt(jnp.mean(inputs * inputs, axis=-1, keepdims=True) + EPSILON)
    normed_one = (inputs * scale_one * attn_gain).astype(BF16)
    cosine_lookup, sine_lookup = tables(positions.reshape(row_count))
    cosine_lookup = cosine_lookup[:, None, :]
    sine_lookup = sine_lookup[:, None, :]
    query_projected = product(normed_one, w_query).reshape(row_count, query_heads, HEAD_SIZE)
    key_projected = product(normed_one, key_weight).reshape(row_count, kv_heads, HEAD_SIZE)
    query_rotated = (
        apply_rotary(query_projected, cosine_lookup, sine_lookup)
        .astype(BF16)
        .reshape(seq_count, seq_len, kv_heads, group_size, HEAD_SIZE)
    )
    key_rotated = (
        apply_rotary(key_projected, cosine_lookup, sine_lookup)
        .astype(BF16)
        .reshape(seq_count, seq_len, kv_heads, HEAD_SIZE)
    )
    value_projected = (
        product(normed_one, value_weight)
        .astype(BF16)
        .reshape(seq_count, seq_len, kv_heads, HEAD_SIZE)
    )
    combined_heads, log_totals = per_sequence(
        attend_forward, query_rotated, key_rotated, value_projected, segments
    )
    head_outputs = combined_heads.reshape(row_count, query_width).astype(BF16)

    inputs_half = half_of(inputs, core)
    hidden = inputs_half + tensor_sum_half(product(head_outputs, w_out), core)
    scale_two = lax.rsqrt(jnp.mean(hidden * hidden, axis=-1, keepdims=True) + EPSILON)
    normed_half = (hidden * scale_two * mlp_gain).astype(BF16)
    normed_sent = normed_half.astype(F32)
    normed_twin = narrowed(swap(normed_sent, "tensor", 1))
    normed_two = joined(normed_half, normed_twin, core)
    normed_others = gathered(normed_sent)

    def feed_forward(normed, incoming):
        gate_proj = product(normed, w_gate)
        up_proj = product(normed, w_up)
        grad_activation = against(incoming, w_down)
        sigmoid_gate = jax.nn.sigmoid(gate_proj)
        swish_gate = gate_proj * sigmoid_gate
        activation = (swish_gate * up_proj).astype(BF16)
        grad_gate_in = (
            grad_activation * up_proj * sigmoid_gate * (1.0 + gate_proj * (1.0 - sigmoid_gate))
        ).astype(BF16)
        grad_up_in = (grad_activation * swish_gate).astype(BF16)
        return activation, grad_gate_in, grad_up_in

    activation, grad_gate_in, grad_up_in = feed_forward(normed_two, cotangent)
    grad_normed_two = tensor_sum_half(
        against(grad_gate_in, w_gate) + against(grad_up_in, w_up), core
    )
    mixed_half = hidden + tensor_sum_half(product(activation, w_down), core)
    mixed = joined(mixed_half.astype(BF16), narrowed(swap(mixed_half, "tensor", 1)), core)

    weighted = grad_normed_two * mlp_gain
    inner_mean = jnp.mean(weighted * hidden, axis=-1, keepdims=True)
    back_two = scale_two * weighted - hidden * (scale_two * scale_two * scale_two) * inner_mean
    gain_two_half = jnp.sum(grad_normed_two * hidden * scale_two, axis=0)
    grad_hidden = cotangent_half + back_two
    attn_half = grad_hidden.astype(BF16)
    attn_twin = narrowed(swap(grad_hidden, "tensor", 1))
    grad_attn = joined(attn_half, attn_twin, core)

    grad_heads = (
        against(grad_attn, w_out)
        .astype(BF16)
        .reshape(seq_count, seq_len, kv_heads, group_size, HEAD_SIZE)
    )
    grad_query_rot, grad_key_rot, grad_value_rot = per_sequence(
        attend_backward,
        query_rotated,
        key_rotated,
        value_projected,
        segments,
        log_totals,
        grad_heads,
    )
    grad_query_in = (
        unrotate(
            grad_query_rot.reshape(row_count, query_heads, HEAD_SIZE), cosine_lookup, sine_lookup
        )
        .reshape(row_count, query_width)
        .astype(BF16)
    )
    grad_key_in = (
        unrotate(grad_key_rot.reshape(row_count, kv_heads, HEAD_SIZE), cosine_lookup, sine_lookup)
        .reshape(row_count, kv_width)
        .astype(BF16)
    )
    grad_value_in = grad_value_rot.reshape(row_count, kv_width).astype(BF16)
    partial_one = (
        against(grad_query_in, w_query)
        + against(grad_key_in, key_weight)
        + against(grad_value_in, value_weight)
    )
    grad_normed_one = tensor_sum_half(partial_one, core)
    scale_one = half_of(scale_one, core)
    weighted = grad_normed_one * attn_gain
    inner_mean = jnp.mean(weighted * inputs_half, axis=-1, keepdims=True)
    back_one = scale_one * weighted - inputs_half * (scale_one * scale_one * scale_one) * inner_mean
    gain_one_half = jnp.sum(grad_normed_one * inputs_half * scale_one, axis=0)
    input_half = grad_hidden + back_one
    grad_input = joined(input_half, swap(input_half, "tensor", 1), core)

    activation_o, grad_gate_o, grad_up_o = feed_forward(normed_others, cotangent_others)

    def rows_of(left, left_others, right, right_others):
        def term(offsets):
            ours = blocks(left, offsets)
            theirs = blocks(left_others, offsets)
            return [
                over_rows(a, right) + over_rows(b, right_others) for a, b in zip(ours, theirs)
            ]

        return reduced(term, split_bits)

    def columns_of(left, left_others, right, right_others):
        def term(offsets):
            ours = blocks(right, offsets)
            theirs = blocks(right_others, offsets)
            return [
                over_rows(left, a) + over_rows(left_others, b) for a, b in zip(ours, theirs)
            ]

        return reduced(term, split_bits)

    grad_w_down = columns_of(activation, activation_o, cotangent, cotangent_others)
    grad_w_gate = rows_of(normed_two, normed_others, grad_gate_in, grad_gate_o)
    grad_w_up = rows_of(normed_two, normed_others, grad_up_in, grad_up_o)

    grad_w_out = reduced(
        lambda offsets: [over_rows(head_outputs, b) for b in blocks(grad_attn, offsets)], all_bits
    )
    projected = jnp.concatenate([grad_query_in, grad_key_in, grad_value_in], axis=1)
    grad_w_proj = reduced(
        lambda offsets: [over_rows(b, projected) for b in blocks(normed_one, offsets)], all_bits
    )
    grad_w_query = grad_w_proj[:, :query_width]
    grad_w_key = grad_w_proj[:, query_width : query_width + kv_width]
    grad_w_value = grad_w_proj[:, query_width + kv_width :]

    gains = jnp.stack([gain_one_half, gain_two_half])
    gains = gains + swap(gains, "tensor", 1)
    gains = reduced(lambda offsets: blocks(gains, offsets), all_bits)
    grad_attn_gain, grad_mlp_gain = gains[0], gains[1]
    return (
        mixed,
        grad_input,
        grad_attn_gain,
        grad_w_query,
        grad_w_key,
        grad_w_value,
        grad_w_out,
        grad_mlp_gain,
        grad_w_gate,
        grad_w_up,
        grad_w_down,
    )


def solution(mesh):
    placed = (
        P("dp", None),
        P("dp", None),
        P("dp", None),
        P(),
        P(None, "tensor"),
        P(None, "tensor"),
        P(None, "tensor"),
        P("tensor", None),
        P(),
        P(None, "tensor"),
        P(None, "tensor"),
        P("tensor", None),
        P("dp", None),
    )
    fits = mesh.shape["dp"] == 8 and mesh.shape["tensor"] == 4
    return jax.shard_map(
        body if fits else general_body,
        mesh=mesh,
        in_specs=placed,
        out_specs=(
            P("dp", None),
            P("dp", None),
            P("dp"),
            P("dp", "tensor"),
            P("dp", "tensor"),
            P("dp", "tensor"),
            P("tensor", "dp"),
            P("dp"),
            P("dp", "tensor"),
            P("dp", "tensor"),
            P("tensor", "dp"),
        ),
        check_vma=False,
    )
```

```python
import functools

import jax
import jax.numpy as jnp
from jax import lax
from jax.experimental import pallas as pl
from jax.experimental.pallas import tpu as pltpu
from jax.sharding import PartitionSpec as P

HEAD_SIZE = 64
EPSILON = 1e-05
MASKED = -1e30
F32 = jnp.float32
BF16 = jnp.bfloat16


MESH = pl.DeviceIdType.MESH
CHUNKS = 4
TILE = 256
ROWS = 16


def flip(index, bit):
    return index + bit * (1 - 2 * ((index // bit) % 2))


def loop(count, step):
    lax.fori_loop(0, count, lambda i, carry: (step(i), carry)[1], 0)


def middle_kernel(
    w_query_ref,
    w_key_ref,
    w_value_ref,
    w_out_ref,
    tokens_ref,
    cot_ref,
    gain_one_ref,
    gain_ref,
    w_gate_ref,
    w_up_ref,
    w_down_ref,
    segment_ref,
    cosine_ref,
    sine_ref,
    normed_one_out,
    heads_out,
    query_ref,
    keys_ref,
    values_ref,
    normed_one_far,
    heads_far,
    grad_hidden_out,
    grad_attn_out,
    projected_out,
    grad_attn_far,
    branch_out,
    normed_out,
    activation_out,
    grad_gate_out,
    grad_up_out,
    gain_out,
    cot_others,
    normed_others,
    gate_w,
    up_w,
    down_w,
    cot,
    cot_half,
    normed,
    normed_sent,
    normed_twin,
    act,
    gg,
    gu,
    away,
    mine,
    core_in,
    y_in,
    product,
    log_total_ref,
    segment_column,
    local_sem,
    core_send,
    core_recv,
    y_send,
    y_recv,
    cot_send,
    cot_recv,
    n_send,
    n_recv,
    twin_send,
    twin_recv,
    hidden_send,
    hidden_recv,
    far_send,
    far_recv,
    free_sem,
):
    dp, tensor = lax.axis_index("dp"), lax.axis_index("tensor")
    core, y_bit = tensor % 2, (tensor // 2) % 2
    z_low = (dp // 2) % 2
    twin_id = (dp, flip(tensor, 1))
    y_id = (dp, flip(tensor, 2))
    x_id = (flip(dp, 1), tensor)
    z_id = (flip(dp, 4), tensor)
    far_id = (flip(dp, 2), tensor)
    half, width = cot_half.shape
    run = half // 2
    row_count = 2 * half
    hidden_units = gate_w.shape[1]
    query_width = w_query_ref.shape[1]
    tiles = width // TILE
    chunk = half // CHUNKS
    transposed = (((1,), (1,)), ((), ()))
    everything = slice(None)
    heads = gg.at[:, pl.ds(0, query_width)]
    tok = gu
    hidden = core_in.at[0]

    def own_row(block, which):
        return pl.multiple_of(block * half + which * run, run)

    def own_chunk(k, which):
        return own_row(k // 2, which) + (k % 2) * chunk

    def remote(src, dst, send, recv, device):
        return pltpu.make_async_remote_copy(
            src_ref=src, dst_ref=dst, send_sem=send, recv_sem=recv,
            device_id=device, device_id_type=MESH,
        )

    loads = {
        "tok": pltpu.make_async_copy(tokens_ref, tok, local_sem.at[0]),
        "query": pltpu.make_async_copy(
            w_query_ref, gate_w.at[:, pl.ds(0, query_width)], local_sem.at[1]
        ),
        "key": pltpu.make_async_copy(
            w_key_ref, gate_w.at[:, pl.ds(query_width, 128)], local_sem.at[2]
        ),
        "value": pltpu.make_async_copy(
            w_value_ref, gate_w.at[:, pl.ds(query_width + 128, 128)], local_sem.at[3]
        ),
        "w_out": pltpu.make_async_copy(w_out_ref, cot, local_sem.at[4]),
        "up": pltpu.make_async_copy(w_up_ref, up_w, local_sem.at[5]),
        "down": pltpu.make_async_copy(w_down_ref, down_w, local_sem.at[6]),
        "gate": pltpu.make_async_copy(w_gate_ref, gate_w, local_sem.at[7]),
        "cot": pltpu.make_async_copy(cot_ref, cot, local_sem.at[8]),
        "cot_0": pltpu.make_async_copy(
            cot_ref.at[pl.ds(own_row(0, core), run)], act.at[pl.ds(0, run)], local_sem.at[10]
        ),
        "cot_1": pltpu.make_async_copy(
            cot_ref.at[pl.ds(own_row(1, core), run)], act.at[pl.ds(run, run)], local_sem.at[11]
        ),
    }
    for name in ("cot_0", "cot_1", "tok", "query", "key", "value", "w_out", "up", "down"):
        loads[name].start()

    barrier = pltpu.get_barrier_semaphore()
    for device in (twin_id, y_id, x_id, z_id, far_id):
        pl.semaphore_signal(barrier, inc=1, device_id=device, device_id_type=MESH)
    loads["cot_0"].wait()
    loads["cot_1"].wait()

    def widen(i):
        window = pl.ds(pl.multiple_of(i * ROWS, ROWS), ROWS)
        cot_half[window, :] = act[window, :].astype(F32)

    loop(half // ROWS, widen)
    pl.semaphore_wait(barrier, 5)

    def rows(k):
        return pl.ds(pl.multiple_of(k * chunk, chunk), chunk)

    def from_x(source, slots, k, send, recv):
        return remote(source.at[rows(k)], slots.at[0, rows(k)], send.at[0, k], recv.at[0, k], x_id)

    def from_z(source, slots, k, send, recv):
        return remote(source.at[rows(k)], slots.at[1, rows(k)], send.at[1, k], recv.at[1, k], z_id)

    def from_zx(slots, k, send, recv):
        return remote(
            slots.at[1, rows(k)], slots.at[2, rows(k)], send.at[2, k], recv.at[2, k], x_id
        )

    def to_twin(slots, which, slot):
        return remote(
            slots.at[slot], slots.at[3 + slot],
            twin_send.at[which, slot], twin_recv.at[which, slot], twin_id,
        )

    half_chunk = pl.ds(pl.multiple_of((2 + y_bit) * chunk, chunk), chunk)

    def last_z():
        return remote(
            normed_sent.at[half_chunk], normed_others.at[1, half_chunk],
            n_send.at[1, 2], n_recv.at[1, 2], z_id,
        )

    def last_y():
        return remote(
            normed_others.at[1, half_chunk], normed_others.at[1, half_chunk],
            n_send.at[1, 3], n_recv.at[1, 3], y_id,
        )

    quarter = pl.ds(pl.multiple_of(y_bit * run, run), run)

    def quarter_z():
        return remote(
            cot_half.at[quarter], cot_others.at[1, quarter],
            cot_send.at[1, 0], cot_recv.at[1, 0], z_id,
        )

    def quarter_zx():
        return remote(
            cot_others.at[1, quarter], cot_others.at[2, quarter],
            cot_send.at[2, 0], cot_recv.at[2, 0], x_id,
        )

    def quarter_y():
        return remote(
            cot_others.at[1, quarter], cot_others.at[1, quarter],
            cot_send.at[1, 1], cot_recv.at[1, 1], y_id,
        )

    quarter_z().start()
    for k in range(CHUNKS):
        from_x(cot_half, cot_others, k, cot_send, cot_recv).start()

    def far_columns(b):
        return pl.ds(pl.multiple_of(b * 1024 + (1 - z_low) * 512, 512), 512)

    gain_one = gain_one_ref[...]
    segments = segment_ref[...].astype(F32)
    segment_column[...] = jnp.broadcast_to(segments, (8, row_count)).T
    loads["tok"].wait()

    def first_norm(block):
        def step(i):
            window = pl.ds(pl.multiple_of(block * half + i * ROWS, ROWS), ROWS)
            values = tok[window, :].astype(F32)
            scale = lax.rsqrt(jnp.mean(values * values, axis=-1, keepdims=True) + EPSILON)
            normed[window, :] = (values * scale * gain_one).astype(BF16)

        loop(half // ROWS, step)

    normed_one_store = pltpu.make_async_copy(normed, normed_one_out, local_sem.at[9])

    def stage_far(block):
        def step(i):
            window = pl.ds(pl.multiple_of(block * run + i * ROWS, ROWS), ROWS)
            here = pl.ds(pl.multiple_of(own_row(block, core) + i * ROWS, ROWS), ROWS)
            for b in range(2):
                core_in[2, window, pl.ds(b * 512, 512)] = normed[here, far_columns(b)].astype(F32)

        loop(run // ROWS, step)

    normed_one_copy = remote(
        core_in.at[2, :, pl.ds(0, 1024)], normed_one_far.at[0],
        far_send.at[0], far_recv.at[0], far_id,
    )

    lane = lax.broadcasted_iota(jnp.int32, (TILE, 128), 1)
    factor = HEAD_SIZE ** (-0.5)

    def turn(value):
        return jnp.where(lane % 64 < 32, pltpu.roll(value, 96, 1), pltpu.roll(value, 32, 1))

    def rotate_tile(value, window):
        return value * cosine_ref[window, :] - turn(value) * sine_ref[window, :]

    def unrotate_tile(value, window):
        return value * cosine_ref[window, :] + turn(value) * sine_ref[window, :]

    def project_in(block):
        window = pl.ds(block * TILE, TILE)

        def query_tile(j):
            projection = jnp.dot(
                normed[window, :],
                gate_w[:, pl.ds(pl.multiple_of(j * TILE, TILE), TILE)],
                preferred_element_type=F32,
            )
            for part in range(2):
                act[window, pl.ds(pl.multiple_of(j * TILE + part * 128, 128), 128)] = rotate_tile(
                    projection[:, part * 128 : (part + 1) * 128], window
                ).astype(BF16)

        loop(query_width // TILE, query_tile)
        projection = jnp.dot(
            normed[window, :], gate_w[:, pl.ds(query_width, TILE)], preferred_element_type=F32
        )
        for base, value in (
            (1024, rotate_tile(projection[:, :128], window)),
            (1536, projection[:, 128:]),
        ):
            other = pltpu.roll(value, 64, 1)
            halves_of = (
                jnp.where(lane < 64, value, 0.0),
                jnp.where(lane >= 64, other, 0.0),
                jnp.where(lane < 64, other, 0.0),
                jnp.where(lane >= 64, value, 0.0),
            )
            for i, padded in enumerate(halves_of):
                act[window, pl.ds(base + i * 128, 128)] = padded.astype(BF16)

    def allowed_of(block):
        keys_seen = (block + 1) * TILE
        window = pl.ds(block * TILE, TILE)
        key_place = lax.broadcasted_iota(jnp.int32, (keys_seen, TILE), 0)
        query_place = lax.broadcasted_iota(jnp.int32, (keys_seen, TILE), 1) + block * TILE
        return (key_place <= query_place) & (
            segment_column[pl.ds(0, keys_seen), pl.ds(0, 1)] == segments[:, block * TILE : (block + 1) * TILE]
        )

    def attend(block, p):
        kv = p // 2
        column = pl.multiple_of(p * 128, 128)
        window = pl.ds(block * TILE, TILE)
        seen = pl.ds(0, (block + 1) * TILE)
        queries = act[window, pl.ds(column, 128)]
        allowed = allowed_of(block)
        result = jnp.zeros((TILE, 128), F32)
        for side in range(2):
            padded = pl.multiple_of((kv * 2 + side) * 128, 128)
            keys = act[seen, pl.ds(pl.multiple_of(1024 + padded, 128), 128)]
            vals = act[seen, pl.ds(pl.multiple_of(1536 + padded, 128), 128)]
            raw = jnp.where(
                allowed,
                lax.dot_general(keys, queries, transposed, preferred_element_type=F32) * factor,
                MASKED,
            )
            peak = jnp.max(raw, axis=0, keepdims=True)
            lifted = jnp.exp(raw - peak)
            summed = jnp.sum(lifted, axis=0, keepdims=True)
            log_total_ref[pl.ds(2 * p + side, 1), window] = peak + jnp.log(summed)
            result = result + lax.dot_general(
                (lifted * (1.0 / summed)).astype(BF16), vals, (((0,), (0,)), ((), ())),
                preferred_element_type=F32,
            )
        heads[window, pl.ds(column, 128)] = result.astype(BF16)

    def core_copy(which, window, k):
        return remote(
            away.at[window], core_in.at[min(which, 1)].at[window],
            core_send.at[which, k], core_recv.at[which, k], twin_id,
        )

    def y_copy(which, window, k):
        return remote(
            mine.at[which].at[window], y_in.at[which].at[window],
            y_send.at[which, k], y_recv.at[which, k], y_id,
        )

    def split_tile(which, block, columns, value):
        product[...] = value
        local = pl.ds(block * run, run)
        away[local, columns] = product[pl.ds(pl.multiple_of((1 - core) * run, run), run), :]
        mine[which, local, columns] = product[pl.ds(pl.multiple_of(core * run, run), run), :]

    row_windows = [(rows(k), everything) for k in range(CHUNKS)]

    def tile_of(j):
        return pl.ds(pl.multiple_of(j * TILE, TILE), TILE)

    first_norm(0)
    first_norm(1)
    normed_one_store.start()
    stage_far(0)
    stage_far(1)
    normed_one_copy.start()
    for name in ("query", "key", "value", "w_out"):
        loads[name].wait()
    for block in range(2):
        project_in(block)
        loop(query_width // 128, functools.partial(attend, block))

        def project(j, block=block):
            split_tile(0, block, tile_of(j), jnp.dot(
                heads[pl.ds(block * TILE, TILE), :], cot[:, tile_of(j)],
                preferred_element_type=F32,
            ))

        loop(tiles, project)
        for k in (2 * block, 2 * block + 1):
            core_copy(0, row_windows[k], k).start()
        for k in (2 * block, 2 * block + 1):
            core_copy(0, row_windows[k], k).wait_recv()

            def add(i, k=k):
                window = pl.ds(pl.multiple_of(k * chunk + i * ROWS, ROWS), ROWS)
                mine[0, window, :] = mine[0, window, :] + core_in[0, window, :]

            loop(chunk // ROWS, add)
            y_copy(0, row_windows[k], k).start()
    normed_one_store.wait()
    loads["gate"].start()
    loads["cot"].start()
    keeps = [
        pltpu.make_async_copy(act.at[:, pl.ds(0, 512)], query_ref, local_sem.at[0]),
        pltpu.make_async_copy(act.at[:, pl.ds(1024, 512)], keys_ref, local_sem.at[1]),
        pltpu.make_async_copy(act.at[:, pl.ds(1536, 512)], values_ref, local_sem.at[2]),
        pltpu.make_async_copy(heads, heads_out, local_sem.at[3]),
    ]
    for keep in keeps:
        keep.start()

    def stage_heads(i):
        window = pl.ds(pl.multiple_of(i * ROWS, ROWS), ROWS)
        for b in range(2):
            here = pl.ds(pl.multiple_of(b * half + i * ROWS, ROWS), ROWS)
            core_in[2, window, pl.ds(1024 + b * 512, 512)] = heads[here, :].astype(F32)

    loop(half // ROWS, stage_heads)
    heads_copy = remote(
        core_in.at[2, :, pl.ds(1024, 1024)], heads_far, far_send.at[1], far_recv.at[1], far_id
    )
    heads_copy.start()
    for keep in keeps:
        keep.wait()

    for name in ("cot", "up", "down"):
        loads[name].wait()

    def activation_grad(j):
        gg[:, tile_of(j)] = lax.dot_general(
            cot[...], down_w[tile_of(j), :], transposed, preferred_element_type=F32
        ).astype(BF16)

    loop(hidden_units // TILE, activation_grad)
    loads["gate"].wait()
    gain = gain_ref[...]

    def twin_copy(k):
        return remote(
            normed_sent.at[rows(k)], normed_twin.at[rows(k)],
            n_send.at[3, k], n_recv.at[3, k], twin_id,
        )

    def block_window(block, j):
        return (pl.ds(block * run, run), tile_of(j))

    for block in range(2):
        chunks = (2 * block, 2 * block + 1)
        for k in chunks:
            y_copy(0, row_windows[k], k).wait_recv()

            def normalize_rows(i, k=k):
                window = pl.ds(pl.multiple_of(k * chunk + i * ROWS, ROWS), ROWS)
                here = pl.ds(pl.multiple_of(own_chunk(k, core) + i * ROWS, ROWS), ROWS)
                values = tok[here, :].astype(F32) + (mine[0, window, :] + y_in[0, window, :])
                scale = lax.rsqrt(jnp.mean(values * values, axis=-1, keepdims=True) + EPSILON)
                rounded = (values * scale * gain).astype(BF16)
                hidden[window, :] = values
                normed[here, :] = rounded
                normed_sent[window, :] = rounded.astype(F32)

            loop(chunk // ROWS, normalize_rows)
            twin_copy(k).start()
            if block == 0:
                from_z(normed_sent, normed_others, k, n_send, n_recv).start()
            elif k == 3:
                last_z().start()
            from_x(normed_sent, normed_others, k, n_send, n_recv).start()
        for k in chunks:
            twin_copy(k).wait_recv()

            def take(i, k=k):
                here = pl.ds(pl.multiple_of(own_chunk(k, 1 - core) + i * ROWS, ROWS), ROWS)
                normed[here, :] = normed_twin[
                    pl.ds(pl.multiple_of(k * chunk + i * ROWS, ROWS), ROWS), :
                ].astype(BF16)

            loop(chunk // ROWS, take)
        window = pl.ds(block * TILE, TILE)

        def units(j, window=window):
            columns = tile_of(j)
            gate = jnp.dot(normed[window, :], gate_w[:, columns], preferred_element_type=F32)
            up = jnp.dot(normed[window, :], up_w[:, columns], preferred_element_type=F32)
            back = gg[window, columns].astype(F32)
            sigmoid = jax.nn.sigmoid(gate)
            swish = gate * sigmoid
            act[window, columns] = (swish * up).astype(BF16)
            gg[window, columns] = (
                back * up * sigmoid * (1.0 + gate * (1.0 - sigmoid))
            ).astype(BF16)
            gu[window, columns] = (back * swish).astype(BF16)

        if block == 0:
            loop(hidden_units // TILE, units)
            for k in range(CHUNKS):
                core_copy(0, row_windows[k], k).wait_send()
        else:
            loop(hidden_units // TILE, units)

        def produce(j, block=block, window=window):
            split_tile(1, block, tile_of(j), lax.dot_general(
                gg[window, :], gate_w[tile_of(j), :], transposed, preferred_element_type=F32
            ) + lax.dot_general(
                gu[window, :], up_w[tile_of(j), :], transposed, preferred_element_type=F32
            ))
            core_copy(1, block_window(block, j), block * tiles + j).start()

        def forward(j, block=block):
            where = block_window(block, j)
            core_copy(1, where, block * tiles + j).wait_recv()
            mine[(1,) + where] = mine[(1,) + where] + core_in[(1,) + where]
            y_copy(1, where, block * tiles + j).start()

        def step(j, produce=produce, forward=forward):
            produce(j + 1)
            forward(j)

        produce(0)
        loop(tiles - 1, step)
        forward(tiles - 1)
    stores = [
        pltpu.make_async_copy(normed, normed_out, local_sem.at[7]),
        pltpu.make_async_copy(act, activation_out, local_sem.at[8]),
        pltpu.make_async_copy(gg, grad_gate_out, local_sem.at[9]),
        pltpu.make_async_copy(gu, grad_up_out, local_sem.at[10]),
    ]
    for store in stores:
        store.start()
    pl.semaphore_signal(free_sem, inc=1, device_id=twin_id, device_id_type=MESH)
    quarter_z().wait()
    quarter_zx().start()

    for block in range(2):
        loop(tiles, lambda j: core_copy(1, block_window(block, j), block * tiles + j).wait_send())
    for k in range(CHUNKS):
        y_copy(0, row_windows[k], k).wait_send()

    def branch_produce(j):
        for block in range(2):
            split_tile(0, block, tile_of(j), jnp.dot(
                act[pl.ds(block * TILE, TILE), :], down_w[:, tile_of(j)],
                preferred_element_type=F32,
            ))
        core_copy(2, (everything, tile_of(j)), j).start()

    def branch_add(j):
        core_copy(2, (everything, tile_of(j)), j).wait_recv()
        mine[0, :, tile_of(j)] = mine[0, :, tile_of(j)] + core_in[1, :, tile_of(j)]

    def branch_step(j):
        branch_produce(j + 1)
        branch_add(j)

    pl.semaphore_wait(free_sem, 1)
    branch_produce(0)
    loop(tiles - 1, branch_step)
    branch_add(tiles - 1)
    first_y = (1 - y_bit).astype(F32)

    def add_hidden(i):
        window = pl.ds(pl.multiple_of(i * ROWS, ROWS), ROWS)
        mine[0, window, :] = mine[0, window, :] + hidden[window, :] * first_y

    loop(half // ROWS, add_hidden)
    branch_store = pltpu.make_async_copy(mine.at[0], branch_out, local_sem.at[12])
    branch_store.start()

    for store in stores:
        store.wait()
    operands = [
        pltpu.make_async_copy(query_ref, act.at[:, pl.ds(0, 512)], local_sem.at[0]),
        pltpu.make_async_copy(keys_ref, act.at[:, pl.ds(1024, 512)], local_sem.at[1]),
        pltpu.make_async_copy(values_ref, act.at[:, pl.ds(1536, 512)], local_sem.at[2]),
        pltpu.make_async_copy(w_out_ref, gate_w.at[pl.ds(0, 512)], local_sem.at[3]),
    ]
    for operand in operands:
        operand.start()
    for operand in operands:
        operand.wait()

    gain_out[...] = jnp.zeros_like(gain_out)
    sums = y_in.at[0]
    sums[:, pl.ds(0, 1024)] = jnp.zeros((TILE, 1024), F32)

    def hidden_copy(k):
        return remote(
            core_in.at[0, rows(k)], normed_twin.at[rows(k)],
            hidden_send.at[k], hidden_recv.at[k], twin_id,
        )

    def hidden_far(block, b):
        local = pl.ds(block * run, run)
        return remote(
            core_in.at[0, local, far_columns(b)],
            grad_attn_far.at[0, local, pl.ds(b * 512, 512)],
            far_send.at[3 + 2 * block + b], far_recv.at[3 + 2 * block + b], far_id,
        )

    def gather_into(offset, kv, value):
        for part in range(value.shape[0] // TILE):
            columns = pl.ds(pl.multiple_of(offset + kv * 256 + part * 128, 128), 128)
            sums[:, columns] = sums[:, columns] + value[part * TILE : (part + 1) * TILE]

    def put(block, column, value):
        gu[pl.ds(block * TILE, TILE), pl.ds(column, 128)] = value.astype(BF16)

    def attend_back(block, p):
        kv = p // 2
        column = pl.multiple_of(p * 128, 128)
        keys_seen = (block + 1) * TILE
        window = pl.ds(block * TILE, TILE)
        seen = pl.ds(0, keys_seen)
        queries = act[window, pl.ds(column, 128)]
        upstream = act[window, pl.ds(pl.multiple_of(512 + column, 128), 128)]
        allowed = allowed_of(block)
        query_grad = jnp.zeros((TILE, 128), F32)
        for side in range(2):
            padded = pl.multiple_of((kv * 2 + side) * 128, 128)
            keys = act[seen, pl.ds(pl.multiple_of(1024 + padded, 128), 128)]
            vals = act[seen, pl.ds(pl.multiple_of(1536 + padded, 128), 128)]
            raw = lax.dot_general(keys, queries, transposed, preferred_element_type=F32) * factor
            log_total = log_total_ref[pl.ds(2 * p + side, 1), window]
            probs = jnp.exp(jnp.where(allowed, raw - log_total, MASKED))
            grad_probs = lax.dot_general(
                vals, upstream, transposed, preferred_element_type=F32
            )
            row_sum = jnp.sum(probs * grad_probs, axis=0, keepdims=True)
            grad_raw = (probs * (grad_probs - row_sum)).astype(BF16)
            query_grad = query_grad + lax.dot_general(
                grad_raw, keys, (((0,), (0,)), ((), ())), preferred_element_type=F32
            )
            own = (lax.broadcasted_iota(jnp.int32, (keys_seen, 128), 1) // 64) == side
            gather_into(0, kv, jnp.where(
                own, jnp.dot(grad_raw, queries, preferred_element_type=F32), 0.0
            ))
            gather_into(512, kv, jnp.where(
                own, jnp.dot(probs.astype(BF16), upstream, preferred_element_type=F32), 0.0
            ))
        put(block, column, unrotate_tile(query_grad * factor, window))

    for block in range(2):
        loop(tiles, lambda j: y_copy(1, block_window(block, j), block * tiles + j).wait_recv())
        if block == 1:
            quarter_y().start()
        for k in (2 * block, 2 * block + 1):

            def norm_rows(i, k=k):
                window = pl.ds(pl.multiple_of(k * chunk + i * ROWS, ROWS), ROWS)
                here = pl.ds(pl.multiple_of(own_chunk(k, core) + i * ROWS, ROWS), ROWS)
                incoming = mine[1, window, :] + y_in[1, window, :]
                values = hidden[window, :]
                scale = lax.rsqrt(jnp.mean(values * values, axis=-1, keepdims=True) + EPSILON)
                weighted = incoming * gain
                inner = jnp.mean(weighted * values, axis=-1, keepdims=True)
                back = scale * weighted - values * (scale * scale * scale) * inner
                total = cot[here, :].astype(F32) + back
                core_in[0, window, :] = total
                normed[here, :] = total.astype(BF16)
                gain_out[...] = gain_out[...] + jnp.sum(
                    incoming * values * scale, axis=0, keepdims=True
                )

            loop(chunk // ROWS, norm_rows)
            hidden_copy(k).start()
        for b in range(2):
            hidden_far(block, b).start()
        for k in (2 * block, 2 * block + 1):
            hidden_copy(k).wait_recv()

            def take_hidden(i, k=k):
                here = pl.ds(pl.multiple_of(own_chunk(k, 1 - core) + i * ROWS, ROWS), ROWS)
                normed[here, :] = normed_twin[
                    pl.ds(pl.multiple_of(k * chunk + i * ROWS, ROWS), ROWS), :
                ].astype(BF16)

            loop(chunk // ROWS, take_hidden)

        def head_tile(j, block=block):
            window = pl.ds(block * TILE, TILE)
            act[window, pl.ds(pl.multiple_of(512 + j * TILE, TILE), TILE)] = lax.dot_general(
                normed[window, :], gate_w[tile_of(j), :], transposed, preferred_element_type=F32
            ).astype(BF16)

        loop(512 // TILE, head_tile)
        loop(query_width // 128, functools.partial(attend_back, block))
        if block == 0:
            for k in (0, 1):
                from_z(normed_sent, normed_others, k, n_send, n_recv).wait_recv()
                from_zx(normed_others, k, n_send, n_recv).start()
            for k in range(CHUNKS):
                from_x(cot_half, cot_others, k, cot_send, cot_recv).wait()
            to_twin(cot_others, 0, 0).start()

    grad_stores = [
        pltpu.make_async_copy(core_in.at[0], grad_hidden_out, local_sem.at[4]),
        pltpu.make_async_copy(normed, grad_attn_out, local_sem.at[5]),
    ]
    for store in grad_stores:
        store.start()

    def both(offset, block):
        def folded(kv):
            value = sums[:, pl.ds(offset + kv * 256 + block * 128, 128)]
            return value + pltpu.roll(value, 64, 1)

        return jnp.where(lane < 64, folded(0), folded(1))

    for block in range(2):
        window = pl.ds(block * TILE, TILE)
        put(block, 512, unrotate_tile(both(0, block) * factor, window))
        put(block, 640, both(512, block))
    projected_store = pltpu.make_async_copy(
        gu.at[:, pl.ds(0, 768)], projected_out, local_sem.at[6]
    )
    projected_store.start()

    last_z().wait()
    last_y().start()
    normed_one_copy.wait()
    normed_one_twin = remote(
        normed_one_far.at[0], normed_one_far.at[1], far_send.at[2], far_recv.at[2], twin_id
    )
    normed_one_twin.start()
    heads_copy.wait()
    for block in range(2):
        for b in range(2):
            hidden_far(block, b).wait()
    hidden_far_twin = remote(
        grad_attn_far.at[0], grad_attn_far.at[1], far_send.at[7], far_recv.at[7], twin_id
    )
    hidden_far_twin.start()
    for k in range(CHUNKS):
        from_x(normed_sent, normed_others, k, n_send, n_recv).wait_recv()
    to_twin(normed_others, 1, 0).start()
    quarter_y().wait()
    to_twin(cot_others, 0, 1).start()
    last_y().wait()
    to_twin(normed_others, 1, 1).start()

    for store in grad_stores + [projected_store, branch_store]:
        store.wait()
    for copy in (hidden_far_twin, normed_one_twin, quarter_zx()):
        copy.wait()
    for k in range(CHUNKS):
        hidden_copy(k).wait_send()
        twin_copy(k).wait_send()
        from_x(normed_sent, normed_others, k, n_send, n_recv).wait_send()
    for k in (0, 1):
        from_z(normed_sent, normed_others, k, n_send, n_recv).wait_send()
        from_zx(normed_others, k, n_send, n_recv).wait()
    for block in range(2):
        loop(tiles, lambda j: y_copy(1, block_window(block, j), block * tiles + j).wait_send())
    loop(tiles, lambda j: core_copy(2, (everything, tile_of(j)), j).wait_send())
    for slot in range(2):
        to_twin(cot_others, 0, slot).wait()
        to_twin(normed_others, 1, slot).wait()


def middle(
    w_query, w_key, w_value, w_out, tokens, cotangent, gain_one, gain,
    w_gate, w_up, w_down, segment, cosine, sine,
):
    row_count, width = tokens.shape
    half = row_count // 2
    hidden_units = w_gate.shape[1]
    tiles = width // TILE
    hbm = pl.BlockSpec(memory_space=pl.ANY)
    vmem = pl.BlockSpec(memory_space=pltpu.VMEM)
    wide = jax.ShapeDtypeStruct((half, width), F32)
    units = jax.ShapeDtypeStruct((row_count, hidden_units), BF16)
    square = jax.ShapeDtypeStruct((row_count, 512), BF16)
    dma = pltpu.SemaphoreType.DMA
    return pl.pallas_call(
        middle_kernel,
        out_shape=(
            jax.ShapeDtypeStruct((row_count, width), BF16),
            square, square, square, square,
            jax.ShapeDtypeStruct((2, half, width // 2), F32),
            jax.ShapeDtypeStruct((half, width // 2), F32),
            wide,
            jax.ShapeDtypeStruct((row_count, width), BF16),
            jax.ShapeDtypeStruct((row_count, 768), BF16),
            jax.ShapeDtypeStruct((2, half, width // 2), F32),
            wide,
            jax.ShapeDtypeStruct((row_count, width), BF16),
            units, units, units,
            jax.ShapeDtypeStruct((1, width), F32),
            jax.ShapeDtypeStruct((5, half, width), F32),
            jax.ShapeDtypeStruct((5, half, width), F32),
        ),
        in_specs=[hbm] * 6 + [vmem] * 2 + [hbm] * 3 + [vmem] * 3,
        out_specs=(hbm,) * 16 + (vmem,) + (hbm,) * 2,
        scratch_shapes=[
            pltpu.VMEM(w_gate.shape, BF16),
            pltpu.VMEM(w_up.shape, BF16),
            pltpu.VMEM(w_down.shape, BF16),
            pltpu.VMEM((row_count, width), BF16),
            pltpu.VMEM((half, width), F32),
            pltpu.VMEM((row_count, width), BF16),
            pltpu.VMEM((half, width), F32),
            pltpu.VMEM((half, width), F32),
            pltpu.VMEM((row_count, hidden_units), BF16),
            pltpu.VMEM((row_count, hidden_units), BF16),
            pltpu.VMEM((row_count, hidden_units), BF16),
            pltpu.VMEM((half, width), F32),
            pltpu.VMEM((2, half, width), F32),
            pltpu.VMEM((3, half, width), F32),
            pltpu.VMEM((2, half, width), F32),
            pltpu.VMEM((half, TILE), F32),
            pltpu.VMEM((8, row_count), F32),
            pltpu.VMEM((row_count, 8), F32),
            dma((13,)),
            dma((3, 2 * tiles)), dma((3, 2 * tiles)), dma((2, 2 * tiles)), dma((2, 2 * tiles)),
            dma((3, CHUNKS)), dma((3, CHUNKS)),
            dma((4, CHUNKS)), dma((4, CHUNKS)),
            dma((2, 2)), dma((2, 2)),
            dma((CHUNKS,)), dma((CHUNKS,)),
            dma((8,)), dma((8,)),
            pltpu.SemaphoreType.REGULAR,
        ],
        compiler_params=pltpu.CompilerParams(
            collective_id=0, has_side_effects=True, vmem_limit_bytes=64 * 1024 * 1024
        ),
        name="feed_forward",
    )(
        w_query, w_key, w_value, w_out, tokens, cotangent,
        gain_one.reshape(1, width), gain.reshape(1, width), w_gate, w_up, w_down,
        segment.reshape(1, row_count), cosine, sine,
    )


def last_kernel(
    normed_others_ref,
    cot_others_ref,
    normed_ref,
    cot_ref,
    act_ref,
    gg_ref,
    gu_ref,
    w_gate_ref,
    w_up_ref,
    w_down_ref,
    projected_ref,
    branch_ref,
    gain_two_ref,
    w_query_ref,
    w_key_ref,
    w_value_ref,
    heads_ref,
    grad_attn_ref,
    grad_attn_far_ref,
    normed_one_ref,
    normed_one_far_ref,
    heads_far_ref,
    grad_hidden_ref,
    tokens_ref,
    gain_ref,
    kept_out,
    sent_out,
    came_out,
    down_kept,
    down_sent,
    down_came,
    out_mine,
    out_came,
    proj_mine,
    proj_came,
    input_out,
    mixed_out,
    branch_came,
    normed_late,
    cot_late,
    gain_out,
    normed,
    cot,
    normed_t,
    cot_t,
    units,
    gate_w,
    up_w,
    down_w,
    total,
    staged,
    core_in,
    y_in,
    w_proj,
    tok,
    heads,
    grad_attn,
    normed_one,
    projected,
    out_part,
    proj_part,
    out_x,
    proj_x,
    far_staged,
    far_heads,
    gains,
    gains_came,
    load_sem,
    piece_sem,
    weight_sem,
    unit_sem,
    store_sem,
    row_send,
    row_recv,
    core_send,
    core_recv,
    y_send,
    y_recv,
    x_send,
    x_recv,
    z_send,
    z_recv,
    end_send,
    end_recv,
    gain_send,
    gain_recv,
    late_send,
    late_recv,
    product,
):
    dp, tensor = lax.axis_index("dp"), lax.axis_index("tensor")
    core = tensor % 2
    x_low, z_low, z_high = dp % 2, (dp // 2) % 2, dp // 4
    twin_id = (dp, flip(tensor, 1))
    y_id = (dp, flip(tensor, 2))
    x_id = (flip(dp, 1), tensor)
    z_id = (flip(dp, 4), tensor)
    far_id = (flip(dp, 2), tensor)
    half, width = tok.shape
    row_count = 2 * half
    tiles = width // TILE
    run = half // 2
    y_bit = (tensor // 2) % 2

    def own_row(block, which):
        return pl.multiple_of(block * half + which * run, run)

    everything = slice(None)
    transposed = (((1,), (1,)), ((), ()))
    over = (((0,), (0,)), ((), ()))

    def remote(src, dst, send, recv, device):
        return pltpu.make_async_remote_copy(
            src_ref=src, dst_ref=dst, send_sem=send, recv_sem=recv,
            device_id=device, device_id_type=MESH,
        )

    def tile_of(j):
        return pl.ds(pl.multiple_of(j * TILE, TILE), TILE)

    away_block = tile_of(flip(dp, 2))
    home_block = tile_of(dp)
    near = [
        pl.ds(pl.multiple_of(b * 1024 + z_low * 512, 512), 512) for b in range(2)
    ]
    own_columns = [units.at[0, pl.ds(i * row_count, row_count)] for i in range(4)]
    loads = [
        pltpu.make_async_copy(normed_ref.at[:, away_block], own_columns[0], load_sem.at[0]),
        pltpu.make_async_copy(normed_ref.at[:, home_block], own_columns[1], load_sem.at[1]),
        pltpu.make_async_copy(cot_ref.at[:, away_block], own_columns[2], load_sem.at[2]),
        pltpu.make_async_copy(cot_ref.at[:, home_block], own_columns[3], load_sem.at[3]),
        pltpu.make_async_copy(w_query_ref, w_proj.at[:, pl.ds(0, 512)], load_sem.at[4]),
        pltpu.make_async_copy(w_key_ref, w_proj.at[:, pl.ds(512, 128)], load_sem.at[5]),
        pltpu.make_async_copy(w_value_ref, w_proj.at[:, pl.ds(640, 128)], load_sem.at[6]),
        pltpu.make_async_copy(
            tokens_ref.at[pl.ds(own_row(0, core), run)], tok.at[pl.ds(0, run)], load_sem.at[7]
        ),
        pltpu.make_async_copy(heads_ref, heads.at[0], load_sem.at[8]),
        pltpu.make_async_copy(
            grad_attn_ref.at[:, near[0]], grad_attn.at[0, :, pl.ds(0, 512)], load_sem.at[9]
        ),
        pltpu.make_async_copy(
            grad_attn_ref.at[:, near[1]], grad_attn.at[0, :, pl.ds(512, 512)], load_sem.at[10]
        ),
        pltpu.make_async_copy(
            normed_one_ref.at[:, near[0]], normed_one.at[0, :, pl.ds(0, 512)], load_sem.at[11]
        ),
        pltpu.make_async_copy(
            normed_one_ref.at[:, near[1]], normed_one.at[0, :, pl.ds(512, 512)], load_sem.at[12]
        ),
        pltpu.make_async_copy(projected_ref, projected.at[0], load_sem.at[13]),
        pltpu.make_async_copy(
            tokens_ref.at[pl.ds(own_row(1, core), run)], tok.at[pl.ds(run, run)], load_sem.at[14]
        ),
    ]

    late_normed = pl.ds(run, run)
    early_normed = pl.ds(0, run)
    late_cot = pl.ds(pl.multiple_of((1 - y_bit) * run, run), run)
    early_cot = pl.ds(pl.multiple_of(y_bit * run, run), run)

    def piece_load(i, slot):
        which, part = i // 6, i % 6
        source = (normed_others_ref, cot_others_ref)[which]
        late = (normed_late, cot_late)[which]
        into = staged.at[slot]
        if part in (0, 1, 3, 4):
            return [pltpu.make_async_copy(source.at[part], into, piece_sem.at[slot])]
        if part == 5:
            return [pltpu.make_async_copy(late.at[1], into, piece_sem.at[slot])]
        early_rows = (early_normed, early_cot)[which]
        late_rows = (late_normed, late_cot)[which]
        return [
            pltpu.make_async_copy(
                source.at[2, early_rows], into.at[early_rows], piece_sem.at[slot]
            ),
            pltpu.make_async_copy(
                late.at[0, late_rows], into.at[late_rows], piece_sem.at[2 + slot]
            ),
        ]

    def weight_loads(j, slot):
        return [
            pltpu.make_async_copy(
                w_gate_ref.at[:, tile_of(j)], gate_w.at[slot], weight_sem.at[slot, 0]
            ),
            pltpu.make_async_copy(
                w_up_ref.at[:, tile_of(j)], up_w.at[slot], weight_sem.at[slot, 1]
            ),
            pltpu.make_async_copy(
                w_down_ref.at[tile_of(j), :], down_w.at[slot], weight_sem.at[slot, 2]
            ),
        ]

    order = [0, 1, 3, 4, 6, 7, 9, 10, 2, 5, 8, 11]
    for i in range(2):
        for load in piece_load(order[i], i):
            load.start()
    loads[13].start()
    for load in loads[:4]:
        load.start()
    for load in weight_loads(0, 0):
        load.start()

    barrier = pltpu.get_barrier_semaphore()
    peers = []
    for m in range(1, 8):
        peer = dp
        for bit in (1, 2, 4):
            peer = flip(peer, bit) if m & bit else peer
        peers.append(peer)
    for device in [twin_id, y_id] + [(peer, tensor) for peer in peers]:
        pl.semaphore_signal(barrier, inc=1, device_id=device, device_id_type=MESH)
    pl.semaphore_wait(barrier, 9)
    late_copies = [
        remote(normed_others_ref.at[1, late_normed], normed_late.at[0, late_normed],
               late_send.at[0], late_recv.at[0], x_id),
        remote(cot_others_ref.at[2, early_cot], cot_late.at[0, early_cot],
               late_send.at[1], late_recv.at[1], y_id),
        remote(normed_others_ref.at[2, early_normed], normed_late.at[1, early_normed],
               late_send.at[2], late_recv.at[2], twin_id),
        remote(cot_others_ref.at[2, early_cot], cot_late.at[1, early_cot],
               late_send.at[3], late_recv.at[3], twin_id),
    ]
    for copy in late_copies:
        copy.start()

    loads[13].wait()

    def widen(r):
        window = pl.ds(pl.multiple_of(r * ROWS, ROWS), ROWS)
        for s in range(2):
            there = pl.ds(pl.multiple_of(s * half + r * ROWS, ROWS), ROWS)
            proj_part[0, s, window, :] = projected[0, there, :].astype(F32)

    loop(half // ROWS, widen)
    projected_copy = remote(proj_part.at[0], far_staged, end_send.at[2], end_recv.at[2], far_id)
    projected_copy.start()
    branch_copy = remote(branch_ref, branch_came, end_send.at[1], end_recv.at[1], y_id)

    late_twins = [
        remote(normed_late.at[0, late_normed], normed_late.at[1, late_normed],
               late_send.at[4], late_recv.at[4], twin_id),
        remote(cot_late.at[0, late_cot], cot_late.at[1, late_cot],
               late_send.at[5], late_recv.at[5], twin_id),
    ]
    def take_piece(place):
        i, slot = order[place], place % 2
        for load in piece_load(i, slot):
            load.wait()
        rows_to, turned_to = (normed, normed_t) if i < 6 else (cot, cot_t)
        base = {0: 0, 1: 1, 3: 2, 4: 3, 2: 4, 5: 5}[i % 6] * half

        def convert(r, slot=slot, rows_to=rows_to, base=base):
            window = pl.ds(pl.multiple_of(r * ROWS, ROWS), ROWS)
            rows_to[pl.ds(pl.multiple_of(base + r * ROWS, ROWS), ROWS), :] = staged[
                slot, window, :
            ].astype(BF16)

        loop(half // ROWS, convert)
        for part, block in enumerate((away_block, home_block)):
            turned_to[pl.ds(part * TILE, TILE), pl.ds(row_count + base, half)] = (
                staged[slot, :, block].T.astype(BF16)
            )
        if place == 5:
            for copy, later in zip(late_copies[:2], late_twins):
                copy.wait()
                later.start()
            branch_copy.start()
        if place == 6:
            for copy in late_copies[2:]:
                copy.wait()
        if place == 7:
            for copy in late_twins:
                copy.wait()
        if place + 2 < 12:
            for load in piece_load(order[place + 2], slot):
                load.start()
    for place in range(8):
        take_piece(place)
    for part in range(4):
        loads[part].wait()
        turned_to = (normed_t, cot_t)[part // 2]
        turned_to[pl.ds((part % 2) * TILE, TILE), pl.ds(0, row_count)] = (
            own_columns[part][...].astype(F32).T.astype(BF16)
        )

    def row_copy(j):
        window = (everything, everything, tile_of(j))
        return [
            remote(
                sent_out.at[window], came_out.at[window],
                row_send.at[0, j], row_recv.at[0, j], far_id,
            ),
            remote(
                down_sent.at[tile_of(j)], down_came.at[tile_of(j)],
                row_send.at[1, j], row_recv.at[1, j], far_id,
            ),
        ]

    def stores(j, slot):
        return [
            pltpu.make_async_copy(
                total.at[slot, pl.ds(0, 2), pl.ds(0, TILE)], sent_out.at[:, :, tile_of(j)],
                store_sem.at[slot, 0],
            ),
            pltpu.make_async_copy(
                total.at[slot, pl.ds(0, 2), pl.ds(TILE, TILE)], kept_out.at[:, :, tile_of(j)],
                store_sem.at[slot, 1],
            ),
            pltpu.make_async_copy(
                total.at[slot, 2, pl.ds(0, TILE)], down_sent.at[tile_of(j)],
                store_sem.at[slot, 2],
            ),
            pltpu.make_async_copy(
                total.at[slot, 2, pl.ds(TILE, TILE)], down_kept.at[tile_of(j)],
                store_sem.at[slot, 3],
            ),
        ]

    def unit_loads(j):
        return [
            pltpu.make_async_copy(
                source.at[:, tile_of(j)], units.at[i, pl.ds(0, row_count)], unit_sem.at[i]
            )
            for i, source in enumerate((gg_ref, gu_ref, act_ref))
        ]

    def feed_forward_tile(j, first=False):
        slot = j % 2
        for load in weight_loads(j, slot):
            load.wait()

        if first:
            for load in weight_loads(1, 1):
                load.start()
        else:

            @pl.when(j + 1 < tiles)
            def _():
                for load in weight_loads(j + 1, 1 - slot):
                    load.start()

        for load in unit_loads(j):
            load.start()

        def block(m):
            rows = pl.ds(pl.multiple_of(m * 512, 512), 512)
            to = pl.ds(pl.multiple_of(row_count + m * 512, 512), 512)
            gate = jnp.dot(normed[rows, :], gate_w[slot], preferred_element_type=F32)
            up = jnp.dot(normed[rows, :], up_w[slot], preferred_element_type=F32)
            back = lax.dot_general(
                cot[rows, :], down_w[slot], transposed, preferred_element_type=F32
            )
            sigmoid = jax.nn.sigmoid(gate)
            swish = gate * sigmoid
            units[2, to, :] = (swish * up).astype(BF16)
            units[0, to, :] = (back * up * sigmoid * (1.0 + gate * (1.0 - sigmoid))).astype(BF16)
            units[1, to, :] = (back * swish).astype(BF16)

        if first:
            loop(2, block)
            for place in range(8, 12):
                take_piece(place)
            block(2)
        else:
            loop(normed.shape[0] // 512, block)
        for load in unit_loads(j):
            load.wait()

        total[slot, 0] = jnp.dot(normed_t[...], units[0], preferred_element_type=F32)
        total[slot, 1] = jnp.dot(normed_t[...], units[1], preferred_element_type=F32)
        turned = jnp.dot(cot_t[...], units[2], preferred_element_type=F32)
        for part in range(2):
            total[slot, 2, pl.ds(part * TILE, TILE)] = turned[part * TILE : (part + 1) * TILE].T
        for store in stores(j, slot):
            store.start()
        for store in stores(j, slot):
            store.wait()
        for copy in row_copy(j):
            copy.start()

    def x_copies(slot):
        return [
            remote(out_part.at[0, slot], out_x.at[slot], x_send.at[0, slot],
                   x_recv.at[0, slot], x_id),
            remote(proj_part.at[0, slot], proj_x.at[slot], x_send.at[1, slot],
                   x_recv.at[1, slot], x_id),
        ]

    def attention_parts():
        for load in far_loads + loads[8:13]:
            load.wait()
        projected_copy.wait()

        def convert(r):
            window = pl.ds(pl.multiple_of(r * ROWS, ROWS), ROWS)
            block, rest = r // (run // ROWS), r % (run // ROWS)
            for s in range(2):
                which = core if s == 0 else 1 - core
                here = pl.ds(
                    pl.multiple_of(block * half + which * run + rest * ROWS, ROWS), ROWS
                )
                grad_attn[1, here, :] = staged[0, window, pl.ds(s * 1024, 1024)].astype(BF16)
                normed_one[1, here, :] = staged[1, window, pl.ds(s * 1024, 1024)].astype(BF16)
                there = pl.ds(pl.multiple_of(s * half + r * ROWS, ROWS), ROWS)
                projected[1, there, :] = far_staged[s, window, :].astype(BF16)
                heads[1, there, :] = far_heads[window, pl.ds(s * 512, 512)].astype(BF16)

        loop(half // ROWS, convert)
        for side in range(2):
            x_at = 1 - x_low if side == 0 else x_low
            for slot in range(2):
                z_at = 1 - z_high if slot == 0 else z_high
                columns = pl.ds(pl.multiple_of(z_at * 512 + x_at * 256, 256), 256)
                out_part[side, slot] = lax.dot_general(
                    heads[0], grad_attn[0, :, columns], over, preferred_element_type=F32
                ) + lax.dot_general(
                    heads[1], grad_attn[1, :, columns], over, preferred_element_type=F32
                )
                proj_part[side, slot] = lax.dot_general(
                    normed_one[0, :, columns], projected[0], over, preferred_element_type=F32
                ) + lax.dot_general(
                    normed_one[1, :, columns], projected[1], over, preferred_element_type=F32
                )
                if side == 0:
                    for copy in x_copies(slot):
                        copy.start()

    def core_copy(j):
        window = (everything, tile_of(j))
        return remote(
            staged.at[0].at[window], core_in.at[window], core_send.at[j], core_recv.at[j], twin_id
        )

    def y_copy(j):
        window = (everything, tile_of(j))
        return remote(
            staged.at[1].at[window], y_in.at[window], y_send.at[j], y_recv.at[j], y_id
        )

    def attention_sums():
        for load in loads[4:8] + loads[14:]:
            load.wait()

        def produce(j):
            product[...] = lax.dot_general(
                projected[0], w_proj[tile_of(j), :], transposed, preferred_element_type=F32
            )
            for block in range(2):
                for slot, which in ((0, 1 - core), (1, core)):
                    staged[slot, pl.ds(block * run, run), tile_of(j)] = product[
                        pl.ds(own_row(block, which), run), :
                    ]
            core_copy(j).start()

        def forward(j):
            core_copy(j).wait_recv()
            staged[1, :, tile_of(j)] = staged[1, :, tile_of(j)] + core_in[:, tile_of(j)]
            y_copy(j).start()

        produce(0)

        def step(j):
            produce(j + 1)
            forward(j)

        loop(tiles - 1, step)
        forward(tiles - 1)
        loop(tiles, lambda j: core_copy(j).wait_send())

    feed_forward_tile(0, first=True)
    for load in loads[4:13] + loads[14:]:
        load.start()
    far_loads = (
        [
            pltpu.make_async_copy(
                grad_attn_far_ref.at[s], staged.at[0, :, pl.ds(s * 1024, 1024)], piece_sem.at[s]
            )
            for s in range(2)
        ]
        + [
            pltpu.make_async_copy(
                normed_one_far_ref.at[s], staged.at[1, :, pl.ds(s * 1024, 1024)],
                piece_sem.at[2 + s],
            )
            for s in range(2)
        ]
        + [
            pltpu.make_async_copy(heads_far_ref, far_heads, piece_sem.at[5]),
        ]
    )
    for load in far_loads:
        load.start()


    def step(j):
        feed_forward_tile(j + 1)

        @pl.when(j == 0)
        def _():
            attention_parts()
            attention_sums()

    loop(tiles - 1, step)
    hidden_load = pltpu.make_async_copy(grad_hidden_ref, core_in, load_sem.at[0])
    hidden_load.start()

    def z_copies():
        return [
            remote(out_part.at[1, 0], out_came, z_send.at[0], z_recv.at[0], z_id),
            remote(proj_part.at[1, 0], proj_came, z_send.at[1], z_recv.at[1], z_id),
        ]

    for slot in range(2):
        for copy in x_copies(slot):
            copy.wait_recv()
        out_part[1, slot] = out_part[1, slot] + out_x[slot]
        proj_part[1, slot] = proj_part[1, slot] + proj_x[slot]
        if slot == 0:
            for copy in z_copies():
                copy.start()
    part_stores = [
        pltpu.make_async_copy(out_part.at[1, 1], out_mine, load_sem.at[1]),
        pltpu.make_async_copy(proj_part.at[1, 1], proj_mine, load_sem.at[2]),
    ]
    for store in part_stores:
        store.start()

    gain = gain_ref[...]
    gains[pl.ds(0, 1), :] = jnp.zeros_like(gain)
    gains[pl.ds(1, 1), :] = gain_two_ref[...]
    hidden_load.wait()
    loop(tiles, lambda j: y_copy(j).wait_recv())

    def norm_rows(i):
        window = pl.ds(pl.multiple_of(i * ROWS, ROWS), ROWS)
        incoming = staged[1, window, :] + y_in[window, :]
        values = tok[window, :].astype(F32)
        scale = lax.rsqrt(jnp.mean(values * values, axis=-1, keepdims=True) + EPSILON)
        weighted = incoming * gain
        inner = jnp.mean(weighted * values, axis=-1, keepdims=True)
        back = scale * weighted - values * (scale * scale * scale) * inner
        staged[0, window, :] = core_in[window, :] + back
        gains[pl.ds(0, 1), :] = gains[pl.ds(0, 1), :] + jnp.sum(
            incoming * values * scale, axis=0, keepdims=True
        )

    loop(half // ROWS, norm_rows)

    def to_rows(slot, out, sems, first):
        copies, kept = [], []
        for block in range(2):
            local, here = pl.ds(block * run, run), pl.ds(own_row(block, core), run)
            copies.append(remote(
                staged.at[slot, local], out.at[here],
                end_send.at[sems + block], end_recv.at[sems + block], twin_id,
            ))
            kept.append(pltpu.make_async_copy(
                staged.at[slot, local], out.at[here], load_sem.at[first + block]
            ))
        for copy in copies + kept:
            copy.start()
        return copies, kept

    input_copies, input_stores = to_rows(0, input_out, 3, 3)

    gain_twin = remote(gains, gains_came, gain_send.at[7], gain_recv.at[7], twin_id)
    gain_twin.start()

    loop(tiles, lambda j: y_copy(j).wait_send())
    branch_copy.wait()
    branch_loads = [
        pltpu.make_async_copy(branch_ref, staged.at[1], load_sem.at[5]),
        pltpu.make_async_copy(branch_came, y_in, load_sem.at[6]),
    ]
    for load in branch_loads:
        load.start()
    gain_twin.wait()
    gains[...] = gains[...] + gains_came[...]

    def gain_copy(m):
        return remote(
            gains.at[:, tile_of(peers[m])], gain_out.at[m], gain_send.at[m], gain_recv.at[m],
            (peers[m], tensor),
        )

    for m in range(7):
        gain_copy(m).start()
    gain_out[7] = gains[:, tile_of(dp)]
    for load in branch_loads:
        load.wait()

    def mixed_rows(i):
        window = pl.ds(pl.multiple_of(i * ROWS, ROWS), ROWS)
        staged[1, window, :] = staged[1, window, :] + y_in[window, :]

    loop(half // ROWS, mixed_rows)
    mixed_copy = remote(staged.at[1], core_in, end_send.at[5], end_recv.at[5], twin_id)
    mixed_copy.start()

    def put_mixed(source, which, first):
        def narrow(i):
            window = pl.ds(pl.multiple_of(i * ROWS, ROWS), ROWS)
            tok[window, :] = source[window, :].astype(BF16)

        loop(half // ROWS, narrow)
        copies = [
            pltpu.make_async_copy(
                tok.at[pl.ds(block * run, run)], mixed_out.at[pl.ds(own_row(block, which), run)],
                load_sem.at[first + block],
            )
            for block in range(2)
        ]
        for copy in copies:
            copy.start()
        for copy in copies:
            copy.wait()

    put_mixed(staged.at[1], core, 7)
    mixed_copy.wait()
    put_mixed(core_in, 1 - core, 9)

    for copy in part_stores + input_stores + input_copies:
        copy.wait()
    for m in range(7):
        gain_copy(m).wait()
    for slot in range(2):
        for copy in x_copies(slot):
            copy.wait_send()
    for copy in z_copies():
        copy.wait()
    for part in range(2):
        loop(tiles, lambda j: row_copy(j)[part].wait())


def last(
    normed_others, cot_others, normed, cot, act, gg, gu, w_gate, w_up, w_down,
    projected, branch, gain_two, w_query, w_key, w_value, heads, grad_attn, grad_attn_far,
    normed_one, normed_one_far, heads_far, grad_hidden, tokens, gain,
):
    row_count, width = tokens.shape
    half = row_count // 2
    tiles = width // TILE
    hidden_units = w_gate.shape[1]
    hbm = pl.BlockSpec(memory_space=pl.ANY)
    vmem = pl.BlockSpec(memory_space=pltpu.VMEM)
    wide = jax.ShapeDtypeStruct((half, width), F32)
    rows_pair = jax.ShapeDtypeStruct((2, TILE, hidden_units), F32)
    columns = jax.ShapeDtypeStruct((hidden_units, TILE), F32)
    out_block = jax.ShapeDtypeStruct((512, TILE), F32)
    proj_block = jax.ShapeDtypeStruct((TILE, 768), F32)
    dma = pltpu.SemaphoreType.DMA
    return pl.pallas_call(
        last_kernel,
        out_shape=(
            rows_pair, rows_pair, rows_pair, columns, columns, columns, out_block, out_block, proj_block, proj_block,
            jax.ShapeDtypeStruct((row_count, width), F32),
            jax.ShapeDtypeStruct((row_count, width), BF16),
            wide,
            jax.ShapeDtypeStruct((2, half, width), F32),
            jax.ShapeDtypeStruct((2, half, width), F32),
            jax.ShapeDtypeStruct((8, 2, TILE), F32),
        ),
        in_specs=[hbm] * 12 + [vmem] + [hbm] * 11 + [vmem],
        out_specs=(hbm,) * 15 + (vmem,),
        scratch_shapes=[
            pltpu.VMEM((6 * half, width), BF16),
            pltpu.VMEM((6 * half, width), BF16),
            pltpu.VMEM((2 * TILE, row_count + 6 * half), BF16),
            pltpu.VMEM((2 * TILE, row_count + 6 * half), BF16),
            pltpu.VMEM((3, row_count + 6 * half, TILE), BF16),
            pltpu.VMEM((2, width, TILE), BF16),
            pltpu.VMEM((2, width, TILE), BF16),
            pltpu.VMEM((2, TILE, width), BF16),
            pltpu.VMEM((2, 3, 2 * TILE, TILE), F32),
            pltpu.VMEM((2, half, width), F32),
            pltpu.VMEM((half, width), F32),
            pltpu.VMEM((half, width), F32),
            pltpu.VMEM((width, 768), BF16),
            pltpu.VMEM((half, width), BF16),
            pltpu.VMEM((2, row_count, 512), BF16),
            pltpu.VMEM((2, row_count, 1024), BF16),
            pltpu.VMEM((2, row_count, 1024), BF16),
            pltpu.VMEM((2, row_count, 768), BF16),
            pltpu.VMEM((2, 2, 512, TILE), F32),
            pltpu.VMEM((2, 2, TILE, 768), F32),
            pltpu.VMEM((2, 512, TILE), F32),
            pltpu.VMEM((2, TILE, 768), F32),
            pltpu.VMEM((2, half, 768), F32),
            pltpu.VMEM((half, 1024), F32),
            pltpu.VMEM((2, width), F32),
            pltpu.VMEM((2, width), F32),
            dma((15,)), dma((6,)), dma((2, 3)), dma((3,)), dma((2, 4)),
            dma((2, tiles)), dma((2, tiles)),
            dma((tiles,)), dma((tiles,)), dma((tiles,)), dma((tiles,)),
            dma((2, 2)), dma((2, 2)), dma((2,)), dma((2,)), dma((7,)), dma((7,)), dma((8,)), dma((8,)),
            dma((6,)), dma((6,)), pltpu.VMEM((row_count, TILE), F32),
        ],
        compiler_params=pltpu.CompilerParams(
            collective_id=1, has_side_effects=True, vmem_limit_bytes=64 * 1024 * 1024
        ),
        name="weight_gradients",
    )(
        normed_others, cot_others, normed, cot, act, gg, gu, w_gate, w_up, w_down,
        projected, branch, gain_two, w_query, w_key, w_value, heads, grad_attn, grad_attn_far,
        normed_one, normed_one_far, heads_far, grad_hidden, tokens, gain.reshape(1, width),
    )


def finish_kernel(
    kept, came, down_kept, down_came, out_mine, out_came, proj_mine, proj_came, input_in,
    mixed_in, gains, w_gate, w_up, w_down, w_out, w_query, w_key, w_value, grad_input, mixed,
    gain_sums,
):
    w_gate[...] = kept[0] + came[0]
    w_up[...] = kept[1] + came[1]
    w_down[...] = down_kept[...] + down_came[...]
    w_out[...] = out_mine[...] + out_came[...]
    queries, keys = w_query.shape[1], w_key.shape[1]
    w_query[...] = proj_mine[:, :queries] + proj_came[:, :queries]
    w_key[...] = proj_mine[:, queries : queries + keys] + proj_came[:, queries : queries + keys]
    w_value[...] = proj_mine[:, queries + keys :] + proj_came[:, queries + keys :]
    grad_input[...] = input_in[...]
    mixed[...] = mixed_in[...]
    gain_sums[...] = jnp.sum(gains[...], axis=0)


def finish(*parts):
    steps = 8
    kept, down, out, proj, whole, gains = (parts[i] for i in (0, 2, 4, 6, 8, 10))
    rows, units = kept.shape[1:]

    def block(array, lead=()):
        size = array[len(lead) :]
        shape = lead + (size[0] // steps,) + size[1:]
        return pl.BlockSpec(shape, lambda i: (0,) * len(lead) + (i,) + (0,) * (len(size) - 1))

    fixed = lambda shape: pl.BlockSpec(shape, lambda i: (0,) * len(shape))
    outs = [
        (rows, units), (rows, units), down.shape, out.shape,
        (proj.shape[0], 512), (proj.shape[0], 128), (proj.shape[0], 128), whole.shape,
    ]
    return pl.pallas_call(
        finish_kernel,
        grid=(steps,),
        out_shape=[jax.ShapeDtypeStruct(shape, F32) for shape in outs]
        + [
            jax.ShapeDtypeStruct(whole.shape, BF16),
            jax.ShapeDtypeStruct(gains.shape[1:], F32),
        ],
        in_specs=[block(kept.shape, (2,))] * 2
        + [block(part.shape) for part in parts[2:10]]
        + [fixed(gains.shape)],
        out_specs=[block(shape) for shape in outs]
        + [block(whole.shape), fixed(gains.shape[1:])],
        compiler_params=pltpu.CompilerParams(vmem_limit_bytes=64 * 1024 * 1024),
        name="last_sums",
    )(*parts)


def body(
    tokens,
    segments,
    positions,
    attn_gain,
    w_query,
    key_weight,
    value_weight,
    w_out,
    mlp_gain,
    w_gate,
    w_up,
    w_down,
    cotangent,
):
    row_count, width = tokens.shape
    half = row_count // 2
    hidden_units = w_gate.shape[1]
    tiles = width // TILE
    hbm = pl.BlockSpec(memory_space=pl.ANY)
    vmem = pl.BlockSpec(memory_space=pltpu.VMEM)
    wide = jax.ShapeDtypeStruct((half, width), F32)
    units = jax.ShapeDtypeStruct((row_count, hidden_units), BF16)
    square = jax.ShapeDtypeStruct((row_count, 512), BF16)
    dma = pltpu.SemaphoreType.DMA
    return pl.pallas_call(
        middle_kernel,
        out_shape=(
            jax.ShapeDtypeStruct((row_count, width), BF16),
            square, square, square, square,
            jax.ShapeDtypeStruct((2, half, width // 2), F32),
            jax.ShapeDtypeStruct((half, width // 2), F32),
            wide,
            jax.ShapeDtypeStruct((row_count, width), BF16),
            jax.ShapeDtypeStruct((row_count, 768), BF16),
            jax.ShapeDtypeStruct((2, half, width // 2), F32),
            wide,
            jax.ShapeDtypeStruct((row_count, width), BF16),
            units, units, units,
            jax.ShapeDtypeStruct((1, width), F32),
            jax.ShapeDtypeStruct((5, half, width), F32),
            jax.ShapeDtypeStruct((5, half, width), F32),
        ),
        in_specs=[hbm] * 6 + [vmem] * 2 + [hbm] * 3 + [vmem] * 3,
        out_specs=(hbm,) * 16 + (vmem,) + (hbm,) * 2,
        scratch_shapes=[
            pltpu.VMEM(w_gate.shape, BF16),
            pltpu.VMEM(w_up.shape, BF16),
            pltpu.VMEM(w_down.shape, BF16),
            pltpu.VMEM((row_count, width), BF16),
            pltpu.VMEM((half, width), F32),
            pltpu.VMEM((row_count, width), BF16),
            pltpu.VMEM((half, width), F32),
            pltpu.VMEM((half, width), F32),
            pltpu.VMEM((row_count, hidden_units), BF16),
            pltpu.VMEM((row_count, hidden_units), BF16),
            pltpu.VMEM((row_count, hidden_units), BF16),
            pltpu.VMEM((half, width), F32),
            pltpu.VMEM((2, half, width), F32),
            pltpu.VMEM((3, half, width), F32),
            pltpu.VMEM((2, half, width), F32),
            pltpu.VMEM((half, TILE), F32),
            pltpu.VMEM((8, row_count), F32),
            pltpu.VMEM((row_count, 8), F32),
            dma((13,)),
            dma((3, 2 * tiles)), dma((3, 2 * tiles)), dma((2, 2 * tiles)), dma((2, 2 * tiles)),
            dma((3, CHUNKS)), dma((3, CHUNKS)),
            dma((4, CHUNKS)), dma((4, CHUNKS)),
            dma((2, 2)), dma((2, 2)),
            dma((CHUNKS,)), dma((CHUNKS,)),
            dma((8,)), dma((8,)),
            pltpu.SemaphoreType.REGULAR,
        ],
        compiler_params=pltpu.CompilerParams(
            collective_id=0, has_side_effects=True, vmem_limit_bytes=64 * 1024 * 1024
        ),
        name="feed_forward",
    )(
        w_query, w_key, w_value, w_out, tokens, cotangent,
        gain_one.reshape(1, width), gain.reshape(1, width), w_gate, w_up, w_down,
        segment.reshape(1, row_count), cosine, sine,
    )


def last_kernel(
    normed_others_ref,
    cot_others_ref,
    normed_ref,
    cot_ref,
    act_ref,
    gg_ref,
    gu_ref,
    w_gate_ref,
    w_up_ref,
    w_down_ref,
    projected_ref,
    branch_ref,
    gain_two_ref,
    w_query_ref,
    w_key_ref,
    w_value_ref,
    heads_ref,
    grad_attn_ref,
    grad_attn_far_ref,
    normed_one_ref,
    normed_one_far_ref,
    heads_far_ref,
    grad_hidden_ref,
    tokens_ref,
    gain_ref,
    kept_out,
    sent_out,
    came_out,
    down_kept,
    down_sent,
    down_came,
    out_mine,
    out_came,
    proj_mine,
    proj_came,
    input_out,
    mixed_out,
    branch_came,
    normed_late,
    cot_late,
    gain_out,
    normed,
    cot,
    normed_t,
    cot_t,
    units,
    gate_w,
    up_w,
    down_w,
    total,
    staged,
    core_in,
    y_in,
    w_proj,
    tok,
    heads,
    grad_attn,
    normed_one,
    projected,
    out_part,
    proj_part,
    out_x,
    proj_x,
    far_staged,
    far_heads,
    gains,
    gains_came,
    load_sem,
    piece_sem,
    weight_sem,
    unit_sem,
    store_sem,
    row_send,
    row_recv,
    core_send,
    core_recv,
    y_send,
    y_recv,
    x_send,
    x_recv,
    z_send,
    z_recv,
    end_send,
    end_recv,
    gain_send,
    gain_recv,
    late_send,
    late_recv,
    product,
):
    dp, tensor = lax.axis_index("dp"), lax.axis_index("tensor")
    core = tensor % 2
    x_low, z_low, z_high = dp % 2, (dp // 2) % 2, dp // 4
    twin_id = (dp, flip(tensor, 1))
    y_id = (dp, flip(tensor, 2))
    x_id = (flip(dp, 1), tensor)
    z_id = (flip(dp, 4), tensor)
    far_id = (flip(dp, 2), tensor)
    half, width = tok.shape
    row_count = 2 * half
    tiles = width // TILE
    run = half // 2
    y_bit = (tensor // 2) % 2

    def own_row(block, which):
        return pl.multiple_of(block * half + which * run, run)

    everything = slice(None)
    transposed = (((1,), (1,)), ((), ()))
    over = (((0,), (0,)), ((), ()))

    def remote(src, dst, send, recv, device):
        return pltpu.make_async_remote_copy(
            src_ref=src, dst_ref=dst, send_sem=send, recv_sem=recv,
            device_id=device, device_id_type=MESH,
        )

    def tile_of(j):
        return pl.ds(pl.multiple_of(j * TILE, TILE), TILE)

    away_block = tile_of(flip(dp, 2))
    home_block = tile_of(dp)
    near = [
        pl.ds(pl.multiple_of(b * 1024 + z_low * 512, 512), 512) for b in range(2)
    ]
    own_columns = [units.at[0, pl.ds(i * row_count, row_count)] for i in range(4)]
    loads = [
        pltpu.make_async_copy(normed_ref.at[:, away_block], own_columns[0], load_sem.at[0]),
        pltpu.make_async_copy(normed_ref.at[:, home_block], own_columns[1], load_sem.at[1]),
        pltpu.make_async_copy(cot_ref.at[:, away_block], own_columns[2], load_sem.at[2]),
        pltpu.make_async_copy(cot_ref.at[:, home_block], own_columns[3], load_sem.at[3]),
        pltpu.make_async_copy(w_query_ref, w_proj.at[:, pl.ds(0, 512)], load_sem.at[4]),
        pltpu.make_async_copy(w_key_ref, w_proj.at[:, pl.ds(512, 128)], load_sem.at[5]),
        pltpu.make_async_copy(w_value_ref, w_proj.at[:, pl.ds(640, 128)], load_sem.at[6]),
        pltpu.make_async_copy(
            tokens_ref.at[pl.ds(own_row(0, core), run)], tok.at[pl.ds(0, run)], load_sem.at[7]
        ),
        pltpu.make_async_copy(heads_ref, heads.at[0], load_sem.at[8]),
        pltpu.make_async_copy(
            grad_attn_ref.at[:, near[0]], grad_attn.at[0, :, pl.ds(0, 512)], load_sem.at[9]
        ),
        pltpu.make_async_copy(
            grad_attn_ref.at[:, near[1]], grad_attn.at[0, :, pl.ds(512, 512)], load_sem.at[10]
        ),
        pltpu.make_async_copy(
            normed_one_ref.at[:, near[0]], normed_one.at[0, :, pl.ds(0, 512)], load_sem.at[11]
        ),
        pltpu.make_async_copy(
            normed_one_ref.at[:, near[1]], normed_one.at[0, :, pl.ds(512, 512)], load_sem.at[12]
        ),
        pltpu.make_async_copy(projected_ref, projected.at[0], load_sem.at[13]),
        pltpu.make_async_copy(
            tokens_ref.at[pl.ds(own_row(1, core), run)], tok.at[pl.ds(run, run)], load_sem.at[14]
        ),
    ]

    late_normed = pl.ds(run, run)
    early_normed = pl.ds(0, run)
    late_cot = pl.ds(pl.multiple_of((1 - y_bit) * run, run), run)
    early_cot = pl.ds(pl.multiple_of(y_bit * run, run), run)

    def piece_load(i, slot):
        which, part = i // 6, i % 6
        source = (normed_others_ref, cot_others_ref)[which]
        late = (normed_late, cot_late)[which]
        into = staged.at[slot]
        if part in (0, 1, 3, 4):
            return [pltpu.make_async_copy(source.at[part], into, piece_sem.at[slot])]
        if part == 5:
            return [pltpu.make_async_copy(late.at[1], into, piece_sem.at[slot])]
        early_rows = (early_normed, early_cot)[which]
        late_rows = (late_normed, late_cot)[which]
        return [
            pltpu.make_async_copy(
                source.at[2, early_rows], into.at[early_rows], piece_sem.at[slot]
            ),
            pltpu.make_async_copy(
                late.at[0, late_rows], into.at[late_rows], piece_sem.at[2 + slot]
            ),
        ]

    def weight_loads(j, slot):
        return [
            pltpu.make_async_copy(
                w_gate_ref.at[:, tile_of(j)], gate_w.at[slot], weight_sem.at[slot, 0]
            ),
            pltpu.make_async_copy(
                w_up_ref.at[:, tile_of(j)], up_w.at[slot], weight_sem.at[slot, 1]
            ),
            pltpu.make_async_copy(
                w_down_ref.at[tile_of(j), :], down_w.at[slot], weight_sem.at[slot, 2]
            ),
        ]

    order = [0, 1, 3, 4, 6, 7, 9, 10, 2, 5, 8, 11]
    for i in range(2):
        for load in piece_load(order[i], i):
            load.start()
    loads[13].start()
    for load in loads[:4]:
        load.start()
    for load in weight_loads(0, 0):
        load.start()

    barrier = pltpu.get_barrier_semaphore()
    peers = []
    for m in range(1, 8):
        peer = dp
        for bit in (1, 2, 4):
            peer = flip(peer, bit) if m & bit else peer
        peers.append(peer)
    for device in [twin_id, y_id] + [(peer, tensor) for peer in peers]:
        pl.semaphore_signal(barrier, inc=1, device_id=device, device_id_type=MESH)
    pl.semaphore_wait(barrier, 9)
    late_copies = [
        remote(normed_others_ref.at[1, late_normed], normed_late.at[0, late_normed],
               late_send.at[0], late_recv.at[0], x_id),
        remote(cot_others_ref.at[2, early_cot], cot_late.at[0, early_cot],
               late_send.at[1], late_recv.at[1], y_id),
        remote(normed_others_ref.at[2, early_normed], normed_late.at[1, early_normed],
               late_send.at[2], late_recv.at[2], twin_id),
        remote(cot_others_ref.at[2, early_cot], cot_late.at[1, early_cot],
               late_send.at[3], late_recv.at[3], twin_id),
    ]
    for copy in late_copies:
        copy.start()

    loads[13].wait()

    def widen(r):
        window = pl.ds(pl.multiple_of(r * ROWS, ROWS), ROWS)
        for s in range(2):
            there = pl.ds(pl.multiple_of(s * half + r * ROWS, ROWS), ROWS)
            proj_part[0, s, window, :] = projected[0, there, :].astype(F32)

    loop(half // ROWS, widen)
    projected_copy = remote(proj_part.at[0], far_staged, end_send.at[2], end_recv.at[2], far_id)
    projected_copy.start()
    branch_copy = remote(branch_ref, branch_came, end_send.at[1], end_recv.at[1], y_id)

    late_twins = [
        remote(normed_late.at[0, late_normed], normed_late.at[1, late_normed],
               late_send.at[4], late_recv.at[4], twin_id),
        remote(cot_late.at[0, late_cot], cot_late.at[1, late_cot],
               late_send.at[5], late_recv.at[5], twin_id),
    ]
    def take_piece(place):
        i, slot = order[place], place % 2
        for load in piece_load(i, slot):
            load.wait()
        rows_to, turned_to = (normed, normed_t) if i < 6 else (cot, cot_t)
        base = {0: 0, 1: 1, 3: 2, 4: 3, 2: 4, 5: 5}[i % 6] * half

        def convert(r, slot=slot, rows_to=rows_to, base=base):
            window = pl.ds(pl.multiple_of(r * ROWS, ROWS), ROWS)
            rows_to[pl.ds(pl.multiple_of(base + r * ROWS, ROWS), ROWS), :] = staged[
                slot, window, :
            ].astype(BF16)

        loop(half // ROWS, convert)
        for part, block in enumerate((away_block, home_block)):
            turned_to[pl.ds(part * TILE, TILE), pl.ds(row_count + base, half)] = (
                staged[slot, :, block].T.astype(BF16)
            )
        if place == 5:
            for copy, later in zip(late_copies[:2], late_twins):
                copy.wait()
                later.start()
            branch_copy.start()
        if place == 6:
            for copy in late_copies[2:]:
                copy.wait()
        if place == 7:
            for copy in late_twins:
                copy.wait()
        if place + 2 < 12:
            for load in piece_load(order[place + 2], slot):
                load.start()
    for place in range(8):
        take_piece(place)
    for part in range(4):
        loads[part].wait()
        turned_to = (normed_t, cot_t)[part // 2]
        turned_to[pl.ds((part % 2) * TILE, TILE), pl.ds(0, row_count)] = (
            own_columns[part][...].astype(F32).T.astype(BF16)
        )

    def row_copy(j):
        window = (everything, everything, tile_of(j))
        return [
            remote(
                sent_out.at[window], came_out.at[window],
                row_send.at[0, j], row_recv.at[0, j], far_id,
            ),
            remote(
                down_sent.at[tile_of(j)], down_came.at[tile_of(j)],
                row_send.at[1, j], row_recv.at[1, j], far_id,
            ),
        ]

    def stores(j, slot):
        return [
            pltpu.make_async_copy(
                total.at[slot, pl.ds(0, 2), pl.ds(0, TILE)], sent_out.at[:, :, tile_of(j)],
                store_sem.at[slot, 0],
            ),
            pltpu.make_async_copy(
                total.at[slot, pl.ds(0, 2), pl.ds(TILE, TILE)], kept_out.at[:, :, tile_of(j)],
                store_sem.at[slot, 1],
            ),
            pltpu.make_async_copy(
                total.at[slot, 2, pl.ds(0, TILE)], down_sent.at[tile_of(j)],
                store_sem.at[slot, 2],
            ),
            pltpu.make_async_copy(
                total.at[slot, 2, pl.ds(TILE, TILE)], down_kept.at[tile_of(j)],
                store_sem.at[slot, 3],
            ),
        ]

    def unit_loads(j):
        return [
            pltpu.make_async_copy(
                source.at[:, tile_of(j)], units.at[i, pl.ds(0, row_count)], unit_sem.at[i]
            )
            for i, source in enumerate((gg_ref, gu_ref, act_ref))
        ]

    def feed_forward_tile(j, first=False):
        slot = j % 2
        for load in weight_loads(j, slot):
            load.wait()

        if first:
            for load in weight_loads(1, 1):
                load.start()
        else:

            @pl.when(j + 1 < tiles)
            def _():
                for load in weight_loads(j + 1, 1 - slot):
                    load.start()

        for load in unit_loads(j):
            load.start()

        def block(m):
            rows = pl.ds(pl.multiple_of(m * 512, 512), 512)
            to = pl.ds(pl.multiple_of(row_count + m * 512, 512), 512)
            gate = jnp.dot(normed[rows, :], gate_w[slot], preferred_element_type=F32)
            up = jnp.dot(normed[rows, :], up_w[slot], preferred_element_type=F32)
            back = lax.dot_general(
                cot[rows, :], down_w[slot], transposed, preferred_element_type=F32
            )
            sigmoid = jax.nn.sigmoid(gate)
            swish = gate * sigmoid
            units[2, to, :] = (swish * up).astype(BF16)
            units[0, to, :] = (back * up * sigmoid * (1.0 + gate * (1.0 - sigmoid))).astype(BF16)
            units[1, to, :] = (back * swish).astype(BF16)

        if first:
            loop(2, block)
            for place in range(8, 12):
                take_piece(place)
            block(2)
        else:
            loop(normed.shape[0] // 512, block)
        for load in unit_loads(j):
            load.wait()

        total[slot, 0] = jnp.dot(normed_t[...], units[0], preferred_element_type=F32)
        total[slot, 1] = jnp.dot(normed_t[...], units[1], preferred_element_type=F32)
        turned = jnp.dot(cot_t[...], units[2], preferred_element_type=F32)
        for part in range(2):
            total[slot, 2, pl.ds(part * TILE, TILE)] = turned[part * TILE : (part + 1) * TILE].T
        for store in stores(j, slot):
            store.start()
        for store in stores(j, slot):
            store.wait()
        for copy in row_copy(j):
            copy.start()

    def x_copies(slot):
        return [
            remote(out_part.at[0, slot], out_x.at[slot], x_send.at[0, slot],
                   x_recv.at[0, slot], x_id),
            remote(proj_part.at[0, slot], proj_x.at[slot], x_send.at[1, slot],
                   x_recv.at[1, slot], x_id),
        ]

    def attention_parts():
        for load in far_loads + loads[8:13]:
            load.wait()
        projected_copy.wait()

        def convert(r):
            window = pl.ds(pl.multiple_of(r * ROWS, ROWS), ROWS)
            block, rest = r // (run // ROWS), r % (run // ROWS)
            for s in range(2):
                which = core if s == 0 else 1 - core
                here = pl.ds(
                    pl.multiple_of(block * half + which * run + rest * ROWS, ROWS), ROWS
                )
                grad_attn[1, here, :] = staged[0, window, pl.ds(s * 1024, 1024)].astype(BF16)
                normed_one[1, here, :] = staged[1, window, pl.ds(s * 1024, 1024)].astype(BF16)
                there = pl.ds(pl.multiple_of(s * half + r * ROWS, ROWS), ROWS)
                projected[1, there, :] = far_staged[s, window, :].astype(BF16)
                heads[1, there, :] = far_heads[window, pl.ds(s * 512, 512)].astype(BF16)

        loop(half // ROWS, convert)
        for side in range(2):
            x_at = 1 - x_low if side == 0 else x_low
            for slot in range(2):
                z_at = 1 - z_high if slot == 0 else z_high
                columns = pl.ds(pl.multiple_of(z_at * 512 + x_at * 256, 256), 256)
                out_part[side, slot] = lax.dot_general(
                    heads[0], grad_attn[0, :, columns], over, preferred_element_type=F32
                ) + lax.dot_general(
                    heads[1], grad_attn[1, :, columns], over, preferred_element_type=F32
                )
                proj_part[side, slot] = lax.dot_general(
                    normed_one[0, :, columns], projected[0], over, preferred_element_type=F32
                ) + lax.dot_general(
                    normed_one[1, :, columns], projected[1], over, preferred_element_type=F32
                )
                if side == 0:
                    for copy in x_copies(slot):
                        copy.start()

    def core_copy(j):
        window = (everything, tile_of(j))
        return remote(
            staged.at[0].at[window], core_in.at[window], core_send.at[j], core_recv.at[j], twin_id
        )

    def y_copy(j):
        window = (everything, tile_of(j))
        return remote(
            staged.at[1].at[window], y_in.at[window], y_send.at[j], y_recv.at[j], y_id
        )

    def attention_sums():
        for load in loads[4:8] + loads[14:]:
            load.wait()

        def produce(j):
            product[...] = lax.dot_general(
                projected[0], w_proj[tile_of(j), :], transposed, preferred_element_type=F32
            )
            for block in range(2):
                for slot, which in ((0, 1 - core), (1, core)):
                    staged[slot, pl.ds(block * run, run), tile_of(j)] = product[
                        pl.ds(own_row(block, which), run), :
                    ]
            core_copy(j).start()

        def forward(j):
            core_copy(j).wait_recv()
            staged[1, :, tile_of(j)] = staged[1, :, tile_of(j)] + core_in[:, tile_of(j)]
            y_copy(j).start()

        produce(0)

        def step(j):
            produce(j + 1)
            forward(j)

        loop(tiles - 1, step)
        forward(tiles - 1)
        loop(tiles, lambda j: core_copy(j).wait_send())

    feed_forward_tile(0, first=True)
    for load in loads[4:13] + loads[14:]:
        load.start()
    far_loads = (
        [
            pltpu.make_async_copy(
                grad_attn_far_ref.at[s], staged.at[0, :, pl.ds(s * 1024, 1024)], piece_sem.at[s]
            )
            for s in range(2)
        ]
        + [
            pltpu.make_async_copy(
                normed_one_far_ref.at[s], staged.at[1, :, pl.ds(s * 1024, 1024)],
                piece_sem.at[2 + s],
            )
            for s in range(2)
        ]
        + [
            pltpu.make_async_copy(heads_far_ref, far_heads, piece_sem.at[5]),
        ]
    )
    for load in far_loads:
        load.start()


    def step(j):
        feed_forward_tile(j + 1)

        @pl.when(j == 0)
        def _():
            attention_parts()
            attention_sums()

    loop(tiles - 1, step)
    hidden_load = pltpu.make_async_copy(grad_hidden_ref, core_in, load_sem.at[0])
    hidden_load.start()

    def z_copies():
        return [
            remote(out_part.at[1, 0], out_came, z_send.at[0], z_recv.at[0], z_id),
            remote(proj_part.at[1, 0], proj_came, z_send.at[1], z_recv.at[1], z_id),
        ]

    for slot in range(2):
        for copy in x_copies(slot):
            copy.wait_recv()
        out_part[1, slot] = out_part[1, slot] + out_x[slot]
        proj_part[1, slot] = proj_part[1, slot] + proj_x[slot]
        if slot == 0:
            for copy in z_copies():
                copy.start()
    part_stores = [
        pltpu.make_async_copy(out_part.at[1, 1], out_mine, load_sem.at[1]),
        pltpu.make_async_copy(proj_part.at[1, 1], proj_mine, load_sem.at[2]),
    ]
    for store in part_stores:
        store.start()

    gain = gain_ref[...]
    gains[pl.ds(0, 1), :] = jnp.zeros_like(gain)
    gains[pl.ds(1, 1), :] = gain_two_ref[...]
    hidden_load.wait()
    loop(tiles, lambda j: y_copy(j).wait_recv())

    def norm_rows(i):
        window = pl.ds(pl.multiple_of(i * ROWS, ROWS), ROWS)
        incoming = staged[1, window, :] + y_in[window, :]
        values = tok[window, :].astype(F32)
        scale = lax.rsqrt(jnp.mean(values * values, axis=-1, keepdims=True) + EPSILON)
        weighted = incoming * gain
        inner = jnp.mean(weighted * values, axis=-1, keepdims=True)
        back = scale * weighted - values * (scale * scale * scale) * inner
        staged[0, window, :] = core_in[window, :] + back
        gains[pl.ds(0, 1), :] = gains[pl.ds(0, 1), :] + jnp.sum(
            incoming * values * scale, axis=0, keepdims=True
        )

    loop(half // ROWS, norm_rows)

    def to_rows(slot, out, sems, first):
        copies, kept = [], []
        for block in range(2):
            local, here = pl.ds(block * run, run), pl.ds(own_row(block, core), run)
            copies.append(remote(
                staged.at[slot, local], out.at[here],
                end_send.at[sems + block], end_recv.at[sems + block], twin_id,
            ))
            kept.append(pltpu.make_async_copy(
                staged.at[slot, local], out.at[here], load_sem.at[first + block]
            ))
        for copy in copies + kept:
            copy.start()
        return copies, kept

    input_copies, input_stores = to_rows(0, input_out, 3, 3)

    gain_twin = remote(gains, gains_came, gain_send.at[7], gain_recv.at[7], twin_id)
    gain_twin.start()

    loop(tiles, lambda j: y_copy(j).wait_send())
    branch_copy.wait()
    branch_loads = [
        pltpu.make_async_copy(branch_ref, staged.at[1], load_sem.at[5]),
        pltpu.make_async_copy(branch_came, y_in, load_sem.at[6]),
    ]
    for load in branch_loads:
        load.start()
    gain_twin.wait()
    gains[...] = gains[...] + gains_came[...]

    def gain_copy(m):
        return remote(
            gains.at[:, tile_of(peers[m])], gain_out.at[m], gain_send.at[m], gain_recv.at[m],
            (peers[m], tensor),
        )

    for m in range(7):
        gain_copy(m).start()
    gain_out[7] = gains[:, tile_of(dp)]
    for load in branch_loads:
        load.wait()

    def mixed_rows(i):
        window = pl.ds(pl.multiple_of(i * ROWS, ROWS), ROWS)
        staged[1, window, :] = staged[1, window, :] + y_in[window, :]

    loop(half // ROWS, mixed_rows)
    mixed_copy = remote(staged.at[1], core_in, end_send.at[5], end_recv.at[5], twin_id)
    mixed_copy.start()

    def put_mixed(source, which, first):
        def narrow(i):
            window = pl.ds(pl.multiple_of(i * ROWS, ROWS), ROWS)
            tok[window, :] = source[window, :].astype(BF16)

        loop(half // ROWS, narrow)
        copies = [
            pltpu.make_async_copy(
                tok.at[pl.ds(block * run, run)], mixed_out.at[pl.ds(own_row(block, which), run)],
                load_sem.at[first + block],
            )
            for block in range(2)
        ]
        for copy in copies:
            copy.start()
        for copy in copies:
            copy.wait()

    put_mixed(staged.at[1], core, 7)
    mixed_copy.wait()
    put_mixed(core_in, 1 - core, 9)

    for copy in part_stores + input_stores + input_copies:
        copy.wait()
    for m in range(7):
        gain_copy(m).wait()
    for slot in range(2):
        for copy in x_copies(slot):
            copy.wait_send()
    for copy in z_copies():
        copy.wait()
    for part in range(2):
        loop(tiles, lambda j: row_copy(j)[part].wait())


def last(
    normed_others, cot_others, normed, cot, act, gg, gu, w_gate, w_up, w_down,
    projected, branch, gain_two, w_query, w_key, w_value, heads, grad_attn, grad_attn_far,
    normed_one, normed_one_far, heads_far, grad_hidden, tokens, gain,
):
    row_count, width = tokens.shape
    half = row_count // 2
    tiles = width // TILE
    hidden_units = w_gate.shape[1]
    hbm = pl.BlockSpec(memory_space=pl.ANY)
    vmem = pl.BlockSpec(memory_space=pltpu.VMEM)
    wide = jax.ShapeDtypeStruct((half, width), F32)
    rows_pair = jax.ShapeDtypeStruct((2, TILE, hidden_units), F32)
    columns = jax.ShapeDtypeStruct((hidden_units, TILE), F32)
    out_block = jax.ShapeDtypeStruct((512, TILE), F32)
    proj_block = jax.ShapeDtypeStruct((TILE, 768), F32)
    dma = pltpu.SemaphoreType.DMA
    return pl.pallas_call(
        last_kernel,
        out_shape=(
            rows_pair, rows_pair, rows_pair, columns, columns, columns, out_block, out_block, proj_block, proj_block,
            jax.ShapeDtypeStruct((row_count, width), F32),
            jax.ShapeDtypeStruct((row_count, width), BF16),
            wide,
            jax.ShapeDtypeStruct((2, half, width), F32),
            jax.ShapeDtypeStruct((2, half, width), F32),
            jax.ShapeDtypeStruct((8, 2, TILE), F32),
        ),
        in_specs=[hbm] * 12 + [vmem] + [hbm] * 11 + [vmem],
        out_specs=(hbm,) * 15 + (vmem,),
        scratch_shapes=[
            pltpu.VMEM((6 * half, width), BF16),
            pltpu.VMEM((6 * half, width), BF16),
            pltpu.VMEM((2 * TILE, row_count + 6 * half), BF16),
            pltpu.VMEM((2 * TILE, row_count + 6 * half), BF16),
            pltpu.VMEM((3, row_count + 6 * half, TILE), BF16),
            pltpu.VMEM((2, width, TILE), BF16),
            pltpu.VMEM((2, width, TILE), BF16),
            pltpu.VMEM((2, TILE, width), BF16),
            pltpu.VMEM((2, 3, 2 * TILE, TILE), F32),
            pltpu.VMEM((2, half, width), F32),
            pltpu.VMEM((half, width), F32),
            pltpu.VMEM((half, width), F32),
            pltpu.VMEM((width, 768), BF16),
            pltpu.VMEM((half, width), BF16),
            pltpu.VMEM((2, row_count, 512), BF16),
            pltpu.VMEM((2, row_count, 1024), BF16),
            pltpu.VMEM((2, row_count, 1024), BF16),
            pltpu.VMEM((2, row_count, 768), BF16),
            pltpu.VMEM((2, 2, 512, TILE), F32),
            pltpu.VMEM((2, 2, TILE, 768), F32),
            pltpu.VMEM((2, 512, TILE), F32),
            pltpu.VMEM((2, TILE, 768), F32),
            pltpu.VMEM((2, half, 768), F32),
            pltpu.VMEM((half, 1024), F32),
            pltpu.VMEM((2, width), F32),
            pltpu.VMEM((2, width), F32),
            dma((15,)), dma((6,)), dma((2, 3)), dma((3,)), dma((2, 4)),
            dma((2, tiles)), dma((2, tiles)),
            dma((tiles,)), dma((tiles,)), dma((tiles,)), dma((tiles,)),
            dma((2, 2)), dma((2, 2)), dma((2,)), dma((2,)), dma((7,)), dma((7,)), dma((8,)), dma((8,)),
            dma((6,)), dma((6,)), pltpu.VMEM((row_count, TILE), F32),
        ],
        compiler_params=pltpu.CompilerParams(
            collective_id=1, has_side_effects=True, vmem_limit_bytes=64 * 1024 * 1024
        ),
        name="weight_gradients",
    )(
        normed_others, cot_others, normed, cot, act, gg, gu, w_gate, w_up, w_down,
        projected, branch, gain_two, w_query, w_key, w_value, heads, grad_attn, grad_attn_far,
        normed_one, normed_one_far, heads_far, grad_hidden, tokens, gain.reshape(1, width),
    )


def finish_kernel(
    kept, came, down_kept, down_came, out_mine, out_came, proj_mine, proj_came, input_in,
    mixed_in, gains, w_gate, w_up, w_down, w_out, w_query, w_key, w_value, grad_input, mixed,
    gain_sums,
):
    w_gate[...] = kept[0] + came[0]
    w_up[...] = kept[1] + came[1]
    w_down[...] = down_kept[...] + down_came[...]
    w_out[...] = out_mine[...] + out_came[...]
    queries, keys = w_query.shape[1], w_key.shape[1]
    w_query[...] = proj_mine[:, :queries] + proj_came[:, :queries]
    w_key[...] = proj_mine[:, queries : queries + keys] + proj_came[:, queries : queries + keys]
    w_value[...] = proj_mine[:, queries + keys :] + proj_came[:, queries + keys :]
    grad_input[...] = input_in[...]
    mixed[...] = mixed_in[...]
    gain_sums[...] = jnp.sum(gains[...], axis=0)


def finish(*parts):
    steps = 8
    kept, down, out, proj, whole, gains = (parts[i] for i in (0, 2, 4, 6, 8, 10))
    rows, units = kept.shape[1:]

    def block(array, lead=()):
        size = array[len(lead) :]
        shape = lead + (size[0] // steps,) + size[1:]
        return pl.BlockSpec(shape, lambda i: (0,) * len(lead) + (i,) + (0,) * (len(size) - 1))

    fixed = lambda shape: pl.BlockSpec(shape, lambda i: (0,) * len(shape))
    outs = [
        (rows, units), (rows, units), down.shape, out.shape,
        (proj.shape[0], 512), (proj.shape[0], 128), (proj.shape[0], 128), whole.shape,
    ]
    return pl.pallas_call(
        finish_kernel,
        grid=(steps,),
        out_shape=[jax.ShapeDtypeStruct(shape, F32) for shape in outs]
        + [
            jax.ShapeDtypeStruct(whole.shape, BF16),
            jax.ShapeDtypeStruct(gains.shape[1:], F32),
        ],
        in_specs=[block(kept.shape, (2,))] * 2
        + [block(part.shape) for part in parts[2:10]]
        + [fixed(gains.shape)],
        out_specs=[block(shape) for shape in outs]
        + [block(whole.shape), fixed(gains.shape[1:])],
        compiler_params=pltpu.CompilerParams(vmem_limit_bytes=64 * 1024 * 1024),
        name="last_sums",
    )(*parts)


def body(
    tokens,
    segments,
    positions,
    attn_gain,
    w_query,
    key_weight,
    value_weight,
    w_out,
    mlp_gain,
    w_gate,
    w_up,
    w_down,
    cotangent,
):
    groups = lax.axis_size("dp")
    place = lax.axis_index("dp")
    core = lax.axis_index("tensor") % 2
    all_bits = [1 << i for i in range(groups.bit_length() - 1)]
    shared_bits = [bit for bit in (4, 1) if bit < groups]
    split_bits = [bit for bit in all_bits if bit not in shared_bits]

    def blocks(matrix, offsets):
        width = matrix.shape[1] // groups
        return [
            lax.dynamic_slice_in_dim(matrix, (place ^ offset) * width, width, 1)
            for offset in offsets
        ]

    def offsets_of(bits):
        found = [0]
        for bit in bits:
            found = found + [offset + bit for offset in found]
        return found

    def reduced(matrix_of, bits):
        sent = None
        for bit in bits:
            rest = bits[bits.index(bit) + 1 :]
            offsets = offsets_of(rest)
            if sent is None:
                away = matrix_of([offset ^ bit for offset in offsets])
                home = matrix_of(offsets)
            else:
                away = [sent[offset ^ bit] for offset in offsets]
                home = [sent[offset] for offset in offsets]
            came = swap(away, "dp", bit)
            sent = {offset: h + c for offset, h, c in zip(offsets, home, came)}
        return sent[0]

    row_count, width = tokens.shape
    query_width, kv_width = w_query.shape[1], key_weight.shape[1]
    half_dim = HEAD_SIZE // 2
    frequency = 500000.0 ** (-(jnp.arange(half_dim).astype(F32) * 2.0 / HEAD_SIZE))
    angles = positions.reshape(row_count, 1).astype(F32) * jnp.tile(frequency, 4)
    cosine_tile = jnp.cos(angles)
    sine_tile = jnp.sin(angles) * jnp.where(jnp.arange(128) % HEAD_SIZE < half_dim, 1.0, -1.0)
    (
        normed_one,
        head_outputs,
        _,
        _,
        _,
        normed_one_far,
        heads_far,
        grad_hidden,
        grad_attn,
        projected,
        grad_attn_far,
        branch,
        normed_two,
        activation,
        grad_gate_in,
        grad_up_in,
        gain_two_half,
        cotangent_others,
        normed_others,
    ) = middle(
        w_query, key_weight, value_weight, w_out, tokens, cotangent,
        attn_gain, mlp_gain, w_gate, w_up, w_down, segments, cosine_tile, sine_tile,
    )
    (
        kept,
        _,
        came,
        down_kept,
        _,
        down_came,
        out_mine,
        out_came,
        proj_mine,
        proj_came,
        grad_input,
        mixed,
        _,
        _,
        _,
        gains,
    ) = last(
        normed_others, cotangent_others, normed_two, cotangent, activation, grad_gate_in,
        grad_up_in, w_gate, w_up, w_down, projected, branch, gain_two_half, w_query, key_weight,
        value_weight, head_outputs, grad_attn, grad_attn_far, normed_one, normed_one_far,
        heads_far, grad_hidden, tokens, attn_gain,
    )
    (
        grad_w_gate,
        grad_w_up,
        grad_w_down,
        grad_w_out,
        grad_w_query,
        grad_w_key,
        grad_w_value,
        grad_input,
        mixed,
        gains,
    ) = finish(
        kept, came, down_kept, down_came, out_mine, out_came, proj_mine, proj_came, grad_input,
        mixed, gains,
    )
    grad_attn_gain, grad_mlp_gain = gains[0], gains[1]
    return (
        mixed,
        grad_input,
        grad_attn_gain,
        grad_w_query,
        grad_w_key,
        grad_w_value,
        grad_w_out,
        grad_mlp_gain,
        grad_w_gate,
        grad_w_up,
        grad_w_down,
    )


def product(left_matrix, right_matrix):
    return jnp.dot(left_matrix, right_matrix, preferred_element_type=F32)


def over_rows(left_matrix, right_matrix):
    return lax.dot_general(
        left_matrix, right_matrix, (((0,), (0,)), ((), ())), preferred_element_type=F32
    )


def against(gradient, weight):
    return lax.dot_general(
        gradient, weight, (((1,), (1,)), ((), ())), preferred_element_type=F32
    )


def narrowed(value):
    return jnp.where(value == value, value, 0.0).astype(BF16)


def swap(value, axis, bit):
    size = lax.axis_size(axis)
    return lax.ppermute(value, axis, [(i, i ^ bit) for i in range(size)])


def half_of(value, which, dim=0):
    size = value.shape[dim] // 2
    return lax.dynamic_slice_in_dim(value, which * size, size, dim)


def joined(mine, other, which):
    first = jnp.where(which == 0, mine, other)
    second = jnp.where(which == 0, other, mine)
    return jnp.concatenate([first, second], axis=0)


def tensor_sum_half(partial, core):
    total = half_of(partial, core) + swap(half_of(partial, 1 - core), "tensor", 1)
    bit = 2
    while bit < lax.axis_size("tensor"):
        total = total + swap(total, "tensor", bit)
        bit *= 2
    return total


def tables(places):
    half_dim = HEAD_SIZE // 2
    frequency = 500000.0 ** (-(jnp.arange(half_dim).astype(F32) * 2.0 / HEAD_SIZE))
    angles = places.astype(F32)[..., None] * frequency
    cosine_lookup = jnp.cos(angles)
    sine_lookup = jnp.sin(angles)
    return (
        jnp.concatenate([cosine_lookup, cosine_lookup], -1),
        jnp.concatenate([sine_lookup, sine_lookup], -1),
    )


def apply_rotary(field, cosine_lookup, sine_lookup):
    half_dim = HEAD_SIZE // 2
    turned = jnp.concatenate([-field[..., half_dim:], field[..., :half_dim]], -1)
    return field * cosine_lookup + turned * sine_lookup


def unrotate(gradient, cosine_lookup, sine_lookup):
    half_dim = HEAD_SIZE // 2
    sined = gradient * sine_lookup
    return gradient * cosine_lookup + jnp.concatenate(
        [sined[..., half_dim:], -sined[..., :half_dim]], -1
    )


def allowed_pairs(segment):
    spots = jnp.arange(segment.shape[0])
    return (spots[:, None] >= spots[None, :]) & (segment[:, None] == segment[None, :])


def scores(query_rotated, key_rotated, segment):
    raw_scores = jnp.einsum(
        "qhgd,khd->hgqk", query_rotated, key_rotated, preferred_element_type=F32
    ) * HEAD_SIZE ** (-0.5)
    return jnp.where(allowed_pairs(segment), raw_scores, MASKED)


def attend_forward(query_rotated, key_rotated, value_seq, segment):
    masked = scores(query_rotated, key_rotated, segment)
    row_peak = jnp.max(masked, axis=-1, keepdims=True)
    log_total = row_peak + jnp.log(jnp.sum(jnp.exp(masked - row_peak), axis=-1, keepdims=True))
    attention_probs = jnp.exp(masked - log_total).astype(BF16)
    combined_heads = jnp.einsum(
        "ojus,sov->uojv", attention_probs, value_seq, preferred_element_type=F32
    )
    return (combined_heads, log_total)


def attend_backward(query_rotated, key_rotated, value_seq, segment, log_total, grad_heads):
    masked = scores(query_rotated, key_rotated, segment)
    attention_probs = jnp.exp(masked - log_total)
    grad_probs = jnp.einsum("qhgd,khd->hgqk", grad_heads, value_seq, preferred_element_type=F32)
    row_sum = jnp.sum(attention_probs * grad_probs, axis=-1, keepdims=True)
    grad_raw = jnp.where(
        allowed_pairs(segment), attention_probs * (grad_probs - row_sum), 0.0
    ).astype(BF16)
    factor = HEAD_SIZE ** (-0.5)
    grad_query_rot = (
        jnp.einsum("ojus,sov->uojv", grad_raw, key_rotated, preferred_element_type=F32) * factor
    )
    grad_key_rot = (
        jnp.einsum("hgqk,qhgd->khd", grad_raw, query_rotated, preferred_element_type=F32) * factor
    )
    grad_value_rot = jnp.einsum(
        "hgqk,qhgd->khd", attention_probs.astype(BF16), grad_heads, preferred_element_type=F32
    )
    return (grad_query_rot, grad_key_rot, grad_value_rot)


def per_sequence(step, *fields):
    results = [step(*[field[s] for field in fields]) for s in range(fields[0].shape[0])]
    return [jnp.stack(parts) for parts in zip(*results)]


def general_body(
    tokens,
    segments,
    positions,
    attn_gain,
    w_query,
    key_weight,
    value_weight,
    w_out,
    mlp_gain,
    w_gate,
    w_up,
    w_down,
    cotangent,
):
    groups = lax.axis_size("dp")
    place = lax.axis_index("dp")
    core = lax.axis_index("tensor") % 2
    all_bits = [1 << i for i in range(groups.bit_length() - 1)]
    shared_bits = [bit for bit in (4, 1) if bit < groups]
    split_bits = [bit for bit in all_bits if bit not in shared_bits]

    def gathered(half):
        parts = [half]
        for bit in shared_bits:
            parts = parts + [swap(part, "dp", bit) for part in parts]
        others = parts[1:]
        twins = [swap(part, "tensor", 1) for part in others]
        return jnp.concatenate([narrowed(part) for part in others + twins], axis=0)

    def blocks(matrix, offsets):
        width = matrix.shape[1] // groups
        return [
            lax.dynamic_slice_in_dim(matrix, (place ^ offset) * width, width, 1)
            for offset in offsets
        ]

    def offsets_of(bits):
        found = [0]
        for bit in bits:
            found = found + [offset + bit for offset in found]
        return found

    def reduced(matrix_of, bits):
        sent = None
        for bit in bits:
            rest = bits[bits.index(bit) + 1 :]
            offsets = offsets_of(rest)
            if sent is None:
                away = matrix_of([offset ^ bit for offset in offsets])
                home = matrix_of(offsets)
            else:
                away = [sent[offset ^ bit] for offset in offsets]
                home = [sent[offset] for offset in offsets]
            came = swap(away, "dp", bit)
            sent = {offset: h + c for offset, h, c in zip(offsets, home, came)}
        return sent[0]

    inputs = tokens.astype(F32)
    row_count, width = inputs.shape
    seq_count, seq_len = segments.shape
    query_heads = w_query.shape[1] // HEAD_SIZE
    kv_heads = key_weight.shape[1] // HEAD_SIZE
    group_size = query_heads // kv_heads
    query_width, kv_width = w_query.shape[1], key_weight.shape[1]

    cotangent_half = half_of(cotangent, core).astype(F32)
    cotangent_others = gathered(cotangent_half)

    scale_one = lax.rsqrt(jnp.mean(inputs * inputs, axis=-1, keepdims=True) + EPSILON)
    normed_one = (inputs * scale_one * attn_gain).astype(BF16)
    cosine_lookup, sine_lookup = tables(positions.reshape(row_count))
    cosine_lookup = cosine_lookup[:, None, :]
    sine_lookup = sine_lookup[:, None, :]
    query_projected = product(normed_one, w_query).reshape(row_count, query_heads, HEAD_SIZE)
    key_projected = product(normed_one, key_weight).reshape(row_count, kv_heads, HEAD_SIZE)
    query_rotated = (
        apply_rotary(query_projected, cosine_lookup, sine_lookup)
        .astype(BF16)
        .reshape(seq_count, seq_len, kv_heads, group_size, HEAD_SIZE)
    )
    key_rotated = (
        apply_rotary(key_projected, cosine_lookup, sine_lookup)
        .astype(BF16)
        .reshape(seq_count, seq_len, kv_heads, HEAD_SIZE)
    )
    value_projected = (
        product(normed_one, value_weight)
        .astype(BF16)
        .reshape(seq_count, seq_len, kv_heads, HEAD_SIZE)
    )
    combined_heads, log_totals = per_sequence(
        attend_forward, query_rotated, key_rotated, value_projected, segments
    )
    head_outputs = combined_heads.reshape(row_count, query_width).astype(BF16)

    inputs_half = half_of(inputs, core)
    hidden = inputs_half + tensor_sum_half(product(head_outputs, w_out), core)
    scale_two = lax.rsqrt(jnp.mean(hidden * hidden, axis=-1, keepdims=True) + EPSILON)
    normed_half = (hidden * scale_two * mlp_gain).astype(BF16)
    normed_sent = normed_half.astype(F32)
    normed_twin = narrowed(swap(normed_sent, "tensor", 1))
    normed_two = joined(normed_half, normed_twin, core)
    normed_others = gathered(normed_sent)

    def feed_forward(normed, incoming):
        gate_proj = product(normed, w_gate)
        up_proj = product(normed, w_up)
        grad_activation = against(incoming, w_down)
        sigmoid_gate = jax.nn.sigmoid(gate_proj)
        swish_gate = gate_proj * sigmoid_gate
        activation = (swish_gate * up_proj).astype(BF16)
        grad_gate_in = (
            grad_activation * up_proj * sigmoid_gate * (1.0 + gate_proj * (1.0 - sigmoid_gate))
        ).astype(BF16)
        grad_up_in = (grad_activation * swish_gate).astype(BF16)
        return activation, grad_gate_in, grad_up_in

    activation, grad_gate_in, grad_up_in = feed_forward(normed_two, cotangent)
    grad_normed_two = tensor_sum_half(
        against(grad_gate_in, w_gate) + against(grad_up_in, w_up), core
    )
    mixed_half = hidden + tensor_sum_half(product(activation, w_down), core)
    mixed = joined(mixed_half.astype(BF16), narrowed(swap(mixed_half, "tensor", 1)), core)

    weighted = grad_normed_two * mlp_gain
    inner_mean = jnp.mean(weighted * hidden, axis=-1, keepdims=True)
    back_two = scale_two * weighted - hidden * (scale_two * scale_two * scale_two) * inner_mean
    gain_two_half = jnp.sum(grad_normed_two * hidden * scale_two, axis=0)
    grad_hidden = cotangent_half + back_two
    attn_half = grad_hidden.astype(BF16)
    attn_twin = narrowed(swap(grad_hidden, "tensor", 1))
    grad_attn = joined(attn_half, attn_twin, core)

    grad_heads = (
        against(grad_attn, w_out)
        .astype(BF16)
        .reshape(seq_count, seq_len, kv_heads, group_size, HEAD_SIZE)
    )
    grad_query_rot, grad_key_rot, grad_value_rot = per_sequence(
        attend_backward,
        query_rotated,
        key_rotated,
        value_projected,
        segments,
        log_totals,
        grad_heads,
    )
    grad_query_in = (
        unrotate(
            grad_query_rot.reshape(row_count, query_heads, HEAD_SIZE), cosine_lookup, sine_lookup
        )
        .reshape(row_count, query_width)
        .astype(BF16)
    )
    grad_key_in = (
        unrotate(grad_key_rot.reshape(row_count, kv_heads, HEAD_SIZE), cosine_lookup, sine_lookup)
        .reshape(row_count, kv_width)
        .astype(BF16)
    )
    grad_value_in = grad_value_rot.reshape(row_count, kv_width).astype(BF16)
    partial_one = (
        against(grad_query_in, w_query)
        + against(grad_key_in, key_weight)
        + against(grad_value_in, value_weight)
    )
    grad_normed_one = tensor_sum_half(partial_one, core)
    scale_one = half_of(scale_one, core)
    weighted = grad_normed_one * attn_gain
    inner_mean = jnp.mean(weighted * inputs_half, axis=-1, keepdims=True)
    back_one = scale_one * weighted - inputs_half * (scale_one * scale_one * scale_one) * inner_mean
    gain_one_half = jnp.sum(grad_normed_one * inputs_half * scale_one, axis=0)
    input_half = grad_hidden + back_one
    grad_input = joined(input_half, swap(input_half, "tensor", 1), core)

    activation_o, grad_gate_o, grad_up_o = feed_forward(normed_others, cotangent_others)

    def rows_of(left, left_others, right, right_others):
        def term(offsets):
            ours = blocks(left, offsets)
            theirs = blocks(left_others, offsets)
            return [
                over_rows(a, right) + over_rows(b, right_others) for a, b in zip(ours, theirs)
            ]

        return reduced(term, split_bits)

    def columns_of(left, left_others, right, right_others):
        def term(offsets):
            ours = blocks(right, offsets)
            theirs = blocks(right_others, offsets)
            return [
                over_rows(left, a) + over_rows(left_others, b) for a, b in zip(ours, theirs)
            ]

        return reduced(term, split_bits)

    grad_w_down = columns_of(activation, activation_o, cotangent, cotangent_others)
    grad_w_gate = rows_of(normed_two, normed_others, grad_gate_in, grad_gate_o)
    grad_w_up = rows_of(normed_two, normed_others, grad_up_in, grad_up_o)

    grad_w_out = reduced(
        lambda offsets: [over_rows(head_outputs, b) for b in blocks(grad_attn, offsets)], all_bits
    )
    projected = jnp.concatenate([grad_query_in, grad_key_in, grad_value_in], axis=1)
    grad_w_proj = reduced(
        lambda offsets: [over_rows(b, projected) for b in blocks(normed_one, offsets)], all_bits
    )
    grad_w_query = grad_w_proj[:, :query_width]
    grad_w_key = grad_w_proj[:, query_width : query_width + kv_width]
    grad_w_value = grad_w_proj[:, query_width + kv_width :]

    gains = jnp.stack([gain_one_half, gain_two_half])
    gains = gains + swap(gains, "tensor", 1)
    gains = reduced(lambda offsets: blocks(gains, offsets), all_bits)
    grad_attn_gain, grad_mlp_gain = gains[0], gains[1]
    return (
        mixed,
        grad_input,
        grad_attn_gain,
        grad_w_query,
        grad_w_key,
        grad_w_value,
        grad_w_out,
        grad_mlp_gain,
        grad_w_gate,
        grad_w_up,
        grad_w_down,
    )


def solution(mesh):
    placed = (
        P("dp", None),
        P("dp", None),
        P("dp", None),
        P(),
        P(None, "tensor"),
        P(None, "tensor"),
        P(None, "tensor"),
        P("tensor", None),
        P(),
        P(None, "tensor"),
        P(None, "tensor"),
        P("tensor", None),
        P("dp", None),
    )
    fits = mesh.shape["dp"] == 8 and mesh.shape["tensor"] == 4
    return jax.shard_map(
        body if fits else general_body,
        mesh=mesh,
        in_specs=placed,
        out_specs=(
            P("dp", None),
            P("dp", None),
            P("dp"),
            P("dp", "tensor"),
            P("dp", "tensor"),
            P("dp", "tensor"),
            P("tensor", "dp"),
            P("dp"),
            P("dp", "tensor"),
            P("dp", "tensor"),
            P("tensor", "dp"),
        ),
        check_vma=False,
    )
```

```python
import functools

import jax
import jax.numpy as jnp
from jax import lax
from jax.experimental import pallas as pl
from jax.experimental.pallas import tpu as pltpu
from jax.sharding import PartitionSpec as P

HEAD_SIZE = 64
EPSILON = 1e-05
MASKED = -1e30
F32 = jnp.float32
BF16 = jnp.bfloat16


MESH = pl.DeviceIdType.MESH
CHUNKS = 4
TILE = 256
ROWS = 16


def flip(index, bit):
    return index + bit * (1 - 2 * ((index // bit) % 2))


def loop(count, step):
    lax.fori_loop(0, count, lambda i, carry: (step(i), carry)[1], 0)


def middle_kernel(
    w_query_ref,
    w_key_ref,
    w_value_ref,
    w_out_ref,
    tokens_ref,
    cot_ref,
    gain_one_ref,
    gain_ref,
    w_gate_ref,
    w_up_ref,
    w_down_ref,
    segment_ref,
    position_ref,
    frequency_ref,
    normed_one_out,
    heads_out,
    query_ref,
    keys_ref,
    values_ref,
    normed_one_far,
    heads_far,
    grad_hidden_out,
    grad_attn_out,
    projected_out,
    grad_attn_far,
    branch_out,
    normed_out,
    activation_out,
    grad_gate_out,
    grad_up_out,
    gain_out,
    cot_others,
    normed_others,
    gate_w,
    up_w,
    down_w,
    cot,
    cot_half,
    normed,
    normed_sent,
    normed_twin,
    act,
    gg,
    gu,
    away,
    mine,
    core_in,
    y_in,
    product,
    log_total_ref,
    segment_column,
    cosine_ref,
    sine_ref,
    local_sem,
    core_send,
    core_recv,
    y_send,
    y_recv,
    cot_send,
    cot_recv,
    n_send,
    n_recv,
    twin_send,
    twin_recv,
    hidden_send,
    hidden_recv,
    far_send,
    far_recv,
    free_sem,
):
    dp, tensor = lax.axis_index("dp"), lax.axis_index("tensor")
    core, y_bit = tensor % 2, (tensor // 2) % 2
    z_low = (dp // 2) % 2
    twin_id = (dp, flip(tensor, 1))
    y_id = (dp, flip(tensor, 2))
    x_id = (flip(dp, 1), tensor)
    z_id = (flip(dp, 4), tensor)
    far_id = (flip(dp, 2), tensor)
    half, width = cot_half.shape
    run = half // 2
    row_count = 2 * half
    hidden_units = gate_w.shape[1]
    query_width = w_query_ref.shape[1]
    tiles = width // TILE
    chunk = half // CHUNKS
    transposed = (((1,), (1,)), ((), ()))
    everything = slice(None)
    heads = gg.at[:, pl.ds(0, query_width)]
    tok = gu
    hidden = core_in.at[0]

    def own_row(block, which):
        return pl.multiple_of(block * half + which * run, run)

    def own_chunk(k, which):
        return own_row(k // 2, which) + (k % 2) * chunk

    def remote(src, dst, send, recv, device):
        return pltpu.make_async_remote_copy(
            src_ref=src, dst_ref=dst, send_sem=send, recv_sem=recv,
            device_id=device, device_id_type=MESH,
        )

    loads = {
        "tok": pltpu.make_async_copy(tokens_ref, tok, local_sem.at[0]),
        "query": pltpu.make_async_copy(
            w_query_ref, gate_w.at[:, pl.ds(0, query_width)], local_sem.at[1]
        ),
        "key": pltpu.make_async_copy(
            w_key_ref, gate_w.at[:, pl.ds(query_width, 128)], local_sem.at[2]
        ),
        "value": pltpu.make_async_copy(
            w_value_ref, gate_w.at[:, pl.ds(query_width + 128, 128)], local_sem.at[3]
        ),
        "w_out": pltpu.make_async_copy(w_out_ref, cot, local_sem.at[4]),
        "up": pltpu.make_async_copy(w_up_ref, up_w, local_sem.at[5]),
        "down": pltpu.make_async_copy(w_down_ref, down_w, local_sem.at[6]),
        "gate": pltpu.make_async_copy(w_gate_ref, gate_w, local_sem.at[7]),
        "cot": pltpu.make_async_copy(cot_ref, cot, local_sem.at[8]),
        "cot_0": pltpu.make_async_copy(
            cot_ref.at[pl.ds(own_row(0, core), run)], act.at[pl.ds(0, run)], local_sem.at[10]
        ),
        "cot_1": pltpu.make_async_copy(
            cot_ref.at[pl.ds(own_row(1, core), run)], act.at[pl.ds(run, run)], local_sem.at[11]
        ),
    }
    for name in ("cot_0", "cot_1", "tok", "query", "key", "value", "w_out", "up", "down"):
        loads[name].start()

    barrier = pltpu.get_barrier_semaphore()
    for device in (twin_id, y_id, x_id, z_id, far_id):
        pl.semaphore_signal(barrier, inc=1, device_id=device, device_id_type=MESH)
    loads["cot_0"].wait()
    loads["cot_1"].wait()

    def widen(i):
        window = pl.ds(pl.multiple_of(i * ROWS, ROWS), ROWS)
        cot_half[window, :] = act[window, :].astype(F32)

    loop(half // ROWS, widen)
    pl.semaphore_wait(barrier, 5)

    def rows(k):
        return pl.ds(pl.multiple_of(k * chunk, chunk), chunk)

    def from_x(source, slots, k, send, recv):
        return remote(source.at[rows(k)], slots.at[0, rows(k)], send.at[0, k], recv.at[0, k], x_id)

    def from_z(source, slots, k, send, recv):
        return remote(source.at[rows(k)], slots.at[1, rows(k)], send.at[1, k], recv.at[1, k], z_id)

    def from_zx(slots, k, send, recv):
        return remote(
            slots.at[1, rows(k)], slots.at[2, rows(k)], send.at[2, k], recv.at[2, k], x_id
        )

    def to_twin(slots, which, slot):
        return remote(
            slots.at[slot], slots.at[3 + slot],
            twin_send.at[which, slot], twin_recv.at[which, slot], twin_id,
        )

    half_chunk = pl.ds(pl.multiple_of((2 + y_bit) * chunk, chunk), chunk)

    def last_z():
        return remote(
            normed_sent.at[half_chunk], normed_others.at[1, half_chunk],
            n_send.at[1, 2], n_recv.at[1, 2], z_id,
        )

    def last_y():
        return remote(
            normed_others.at[1, half_chunk], normed_others.at[1, half_chunk],
            n_send.at[1, 3], n_recv.at[1, 3], y_id,
        )

    quarter = pl.ds(pl.multiple_of(y_bit * run, run), run)

    def quarter_z():
        return remote(
            cot_half.at[quarter], cot_others.at[1, quarter],
            cot_send.at[1, 0], cot_recv.at[1, 0], z_id,
        )

    def quarter_zx():
        return remote(
            cot_others.at[1, quarter], cot_others.at[2, quarter],
            cot_send.at[2, 0], cot_recv.at[2, 0], x_id,
        )

    def quarter_y():
        return remote(
            cot_others.at[1, quarter], cot_others.at[1, quarter],
            cot_send.at[1, 1], cot_recv.at[1, 1], y_id,
        )

    quarter_z().start()
    for k in range(CHUNKS):
        from_x(cot_half, cot_others, k, cot_send, cot_recv).start()

    def far_columns(b):
        return pl.ds(pl.multiple_of(b * 1024 + (1 - z_low) * 512, 512), 512)

    gain_one = gain_one_ref[...]
    segments = segment_ref[...].astype(F32)
    segment_column[...] = jnp.broadcast_to(segments, (8, row_count)).T
    loads["tok"].wait()

    def first_norm(block):
        def step(i):
            window = pl.ds(pl.multiple_of(block * half + i * ROWS, ROWS), ROWS)
            values = tok[window, :].astype(F32)
            scale = lax.rsqrt(jnp.mean(values * values, axis=-1, keepdims=True) + EPSILON)
            normed[window, :] = (values * scale * gain_one).astype(BF16)

        loop(half // ROWS, step)

    normed_one_store = pltpu.make_async_copy(normed, normed_one_out, local_sem.at[9])

    def stage_far(block):
        def step(i):
            window = pl.ds(pl.multiple_of(block * run + i * ROWS, ROWS), ROWS)
            here = pl.ds(pl.multiple_of(own_row(block, core) + i * ROWS, ROWS), ROWS)
            for b in range(2):
                core_in[2, window, pl.ds(b * 512, 512)] = normed[here, far_columns(b)].astype(F32)

        loop(run // ROWS, step)

    normed_one_copy = remote(
        core_in.at[2, :, pl.ds(0, 1024)], normed_one_far.at[0],
        far_send.at[0], far_recv.at[0], far_id,
    )

    places = jnp.broadcast_to(position_ref[...].astype(F32), (8, row_count)).T
    angles = places[:, 0:1] * frequency_ref[...]
    cosine_ref[...] = jnp.cos(angles)
    signs = lax.broadcasted_iota(jnp.int32, (row_count, 128), 1) % 64 < 32
    sines = jnp.sin(angles)
    sine_ref[...] = jnp.where(signs, sines, -sines)

    lane = lax.broadcasted_iota(jnp.int32, (TILE, 128), 1)
    factor = HEAD_SIZE ** (-0.5)

    def turn(value):
        return jnp.where(lane % 64 < 32, pltpu.roll(value, 96, 1), pltpu.roll(value, 32, 1))

    def rotate_tile(value, window):
        return value * cosine_ref[window, :] - turn(value) * sine_ref[window, :]

    def unrotate_tile(value, window):
        return value * cosine_ref[window, :] + turn(value) * sine_ref[window, :]

    def project_in(block):
        window = pl.ds(block * TILE, TILE)

        def query_tile(j):
            projection = jnp.dot(
                normed[window, :],
                gate_w[:, pl.ds(pl.multiple_of(j * TILE, TILE), TILE)],
                preferred_element_type=F32,
            )
            for part in range(2):
                act[window, pl.ds(pl.multiple_of(j * TILE + part * 128, 128), 128)] = rotate_tile(
                    projection[:, part * 128 : (part + 1) * 128], window
                ).astype(BF16)

        loop(query_width // TILE, query_tile)
        projection = jnp.dot(
            normed[window, :], gate_w[:, pl.ds(query_width, TILE)], preferred_element_type=F32
        )
        for base, value in (
            (1024, rotate_tile(projection[:, :128], window)),
            (1536, projection[:, 128:]),
        ):
            other = pltpu.roll(value, 64, 1)
            halves_of = (
                jnp.where(lane < 64, value, 0.0),
                jnp.where(lane >= 64, other, 0.0),
                jnp.where(lane < 64, other, 0.0),
                jnp.where(lane >= 64, value, 0.0),
            )
            for i, padded in enumerate(halves_of):
                act[window, pl.ds(base + i * 128, 128)] = padded.astype(BF16)

    def allowed_of(block):
        keys_seen = (block + 1) * TILE
        window = pl.ds(block * TILE, TILE)
        key_place = lax.broadcasted_iota(jnp.int32, (keys_seen, TILE), 0)
        query_place = lax.broadcasted_iota(jnp.int32, (keys_seen, TILE), 1) + block * TILE
        return (key_place <= query_place) & (
            segment_column[pl.ds(0, keys_seen), pl.ds(0, 1)] == segments[:, block * TILE : (block + 1) * TILE]
        )

    def attend(block, p):
        kv = p // 2
        column = pl.multiple_of(p * 128, 128)
        window = pl.ds(block * TILE, TILE)
        seen = pl.ds(0, (block + 1) * TILE)
        queries = act[window, pl.ds(column, 128)]
        allowed = allowed_of(block)
        result = jnp.zeros((TILE, 128), F32)
        for side in range(2):
            padded = pl.multiple_of((kv * 2 + side) * 128, 128)
            keys = act[seen, pl.ds(pl.multiple_of(1024 + padded, 128), 128)]
            vals = act[seen, pl.ds(pl.multiple_of(1536 + padded, 128), 128)]
            raw = jnp.where(
                allowed,
                lax.dot_general(keys, queries, transposed, preferred_element_type=F32) * factor,
                MASKED,
            )
            peak = jnp.max(raw, axis=0, keepdims=True)
            lifted = jnp.exp(raw - peak)
            summed = jnp.sum(lifted, axis=0, keepdims=True)
            log_total_ref[pl.ds(2 * p + side, 1), window] = peak + jnp.log(summed)
            result = result + lax.dot_general(
                (lifted * (1.0 / summed)).astype(BF16), vals, (((0,), (0,)), ((), ())),
                preferred_element_type=F32,
            )
        heads[window, pl.ds(column, 128)] = result.astype(BF16)

    def core_copy(which, window, k):
        return remote(
            away.at[window], core_in.at[min(which, 1)].at[window],
            core_send.at[which, k], core_recv.at[which, k], twin_id,
        )

    def y_copy(which, window, k):
        return remote(
            mine.at[which].at[window], y_in.at[which].at[window],
            y_send.at[which, k], y_recv.at[which, k], y_id,
        )

    def split_tile(which, block, columns, value):
        product[...] = value
        local = pl.ds(block * run, run)
        away[local, columns] = product[pl.ds(pl.multiple_of((1 - core) * run, run), run), :]
        mine[which, local, columns] = product[pl.ds(pl.multiple_of(core * run, run), run), :]

    row_windows = [(rows(k), everything) for k in range(CHUNKS)]

    def tile_of(j):
        return pl.ds(pl.multiple_of(j * TILE, TILE), TILE)

    first_norm(0)
    first_norm(1)
    normed_one_store.start()
    stage_far(0)
    stage_far(1)
    normed_one_copy.start()
    for name in ("query", "key", "value", "w_out"):
        loads[name].wait()
    for block in range(2):
        project_in(block)
        loop(query_width // 128, functools.partial(attend, block))

        def project(j, block=block):
            split_tile(0, block, tile_of(j), jnp.dot(
                heads[pl.ds(block * TILE, TILE), :], cot[:, tile_of(j)],
                preferred_element_type=F32,
            ))

        loop(tiles, project)
        for k in (2 * block, 2 * block + 1):
            core_copy(0, row_windows[k], k).start()
        for k in (2 * block, 2 * block + 1):
            core_copy(0, row_windows[k], k).wait_recv()

            def add(i, k=k):
                window = pl.ds(pl.multiple_of(k * chunk + i * ROWS, ROWS), ROWS)
                mine[0, window, :] = mine[0, window, :] + core_in[0, window, :]

            loop(chunk // ROWS, add)
            y_copy(0, row_windows[k], k).start()
    normed_one_store.wait()
    loads["gate"].start()
    loads["cot"].start()
    keeps = [
        pltpu.make_async_copy(act.at[:, pl.ds(0, 512)], query_ref, local_sem.at[0]),
        pltpu.make_async_copy(act.at[:, pl.ds(1024, 512)], keys_ref, local_sem.at[1]),
        pltpu.make_async_copy(act.at[:, pl.ds(1536, 512)], values_ref, local_sem.at[2]),
        pltpu.make_async_copy(heads, heads_out, local_sem.at[3]),
    ]
    for keep in keeps:
        keep.start()

    def stage_heads(i):
        window = pl.ds(pl.multiple_of(i * ROWS, ROWS), ROWS)
        for b in range(2):
            here = pl.ds(pl.multiple_of(b * half + i * ROWS, ROWS), ROWS)
            core_in[2, window, pl.ds(1024 + b * 512, 512)] = heads[here, :].astype(F32)

    loop(half // ROWS, stage_heads)
    heads_copy = remote(
        core_in.at[2, :, pl.ds(1024, 1024)], heads_far, far_send.at[1], far_recv.at[1], far_id
    )
    heads_copy.start()
    for keep in keeps:
        keep.wait()

    for name in ("cot", "up", "down"):
        loads[name].wait()

    def activation_grad(j):
        gg[:, tile_of(j)] = lax.dot_general(
            cot[...], down_w[tile_of(j), :], transposed, preferred_element_type=F32
        ).astype(BF16)

    loop(hidden_units // TILE, activation_grad)
    loads["gate"].wait()
    gain = gain_ref[...]

    def twin_copy(k):
        return remote(
            normed_sent.at[rows(k)], normed_twin.at[rows(k)],
            n_send.at[3, k], n_recv.at[3, k], twin_id,
        )

    def block_window(block, j):
        return (pl.ds(block * run, run), tile_of(j))

    for block in range(2):
        chunks = (2 * block, 2 * block + 1)
        for k in chunks:
            y_copy(0, row_windows[k], k).wait_recv()

            def normalize_rows(i, k=k):
                window = pl.ds(pl.multiple_of(k * chunk + i * ROWS, ROWS), ROWS)
                here = pl.ds(pl.multiple_of(own_chunk(k, core) + i * ROWS, ROWS), ROWS)
                values = tok[here, :].astype(F32) + (mine[0, window, :] + y_in[0, window, :])
                scale = lax.rsqrt(jnp.mean(values * values, axis=-1, keepdims=True) + EPSILON)
                rounded = (values * scale * gain).astype(BF16)
                hidden[window, :] = values
                normed[here, :] = rounded
                normed_sent[window, :] = rounded.astype(F32)

            loop(chunk // ROWS, normalize_rows)
            twin_copy(k).start()
            if block == 0:
                from_z(normed_sent, normed_others, k, n_send, n_recv).start()
            elif k == 3:
                last_z().start()
            from_x(normed_sent, normed_others, k, n_send, n_recv).start()
        for k in chunks:
            twin_copy(k).wait_recv()

            def take(i, k=k):
                here = pl.ds(pl.multiple_of(own_chunk(k, 1 - core) + i * ROWS, ROWS), ROWS)
                normed[here, :] = normed_twin[
                    pl.ds(pl.multiple_of(k * chunk + i * ROWS, ROWS), ROWS), :
                ].astype(BF16)

            loop(chunk // ROWS, take)
        window = pl.ds(block * TILE, TILE)

        def units(j, window=window):
            columns = tile_of(j)
            gate = jnp.dot(normed[window, :], gate_w[:, columns], preferred_element_type=F32)
            up = jnp.dot(normed[window, :], up_w[:, columns], preferred_element_type=F32)
            back = gg[window, columns].astype(F32)
            sigmoid = jax.nn.sigmoid(gate)
            swish = gate * sigmoid
            act[window, columns] = (swish * up).astype(BF16)
            gg[window, columns] = (
                back * up * sigmoid * (1.0 + gate * (1.0 - sigmoid))
            ).astype(BF16)
            gu[window, columns] = (back * swish).astype(BF16)

        if block == 0:
            loop(hidden_units // TILE, units)
            for k in range(CHUNKS):
                core_copy(0, row_windows[k], k).wait_send()
        else:
            loop(hidden_units // TILE, units)

        def produce(j, block=block, window=window):
            split_tile(1, block, tile_of(j), lax.dot_general(
                gg[window, :], gate_w[tile_of(j), :], transposed, preferred_element_type=F32
            ) + lax.dot_general(
                gu[window, :], up_w[tile_of(j), :], transposed, preferred_element_type=F32
            ))
            core_copy(1, block_window(block, j), block * tiles + j).start()

        def forward(j, block=block):
            where = block_window(block, j)
            core_copy(1, where, block * tiles + j).wait_recv()
            mine[(1,) + where] = mine[(1,) + where] + core_in[(1,) + where]
            y_copy(1, where, block * tiles + j).start()

        def step(j, produce=produce, forward=forward):
            produce(j + 1)
            forward(j)

        produce(0)
        loop(tiles - 1, step)
        forward(tiles - 1)
    stores = [
        pltpu.make_async_copy(normed, normed_out, local_sem.at[7]),
        pltpu.make_async_copy(act, activation_out, local_sem.at[8]),
        pltpu.make_async_copy(gg, grad_gate_out, local_sem.at[9]),
        pltpu.make_async_copy(gu, grad_up_out, local_sem.at[10]),
    ]
    for store in stores:
        store.start()
    pl.semaphore_signal(free_sem, inc=1, device_id=twin_id, device_id_type=MESH)
    quarter_z().wait()
    quarter_zx().start()

    for block in range(2):
        loop(tiles, lambda j: core_copy(1, block_window(block, j), block * tiles + j).wait_send())
    for k in range(CHUNKS):
        y_copy(0, row_windows[k], k).wait_send()

    def branch_produce(j):
        for block in range(2):
            split_tile(0, block, tile_of(j), jnp.dot(
                act[pl.ds(block * TILE, TILE), :], down_w[:, tile_of(j)],
                preferred_element_type=F32,
            ))
        core_copy(2, (everything, tile_of(j)), j).start()

    def branch_add(j):
        core_copy(2, (everything, tile_of(j)), j).wait_recv()
        mine[0, :, tile_of(j)] = mine[0, :, tile_of(j)] + core_in[1, :, tile_of(j)]

    def branch_step(j):
        branch_produce(j + 1)
        branch_add(j)

    pl.semaphore_wait(free_sem, 1)
    branch_produce(0)
    loop(tiles - 1, branch_step)
    branch_add(tiles - 1)
    first_y = (1 - y_bit).astype(F32)

    def add_hidden(i):
        window = pl.ds(pl.multiple_of(i * ROWS, ROWS), ROWS)
        mine[0, window, :] = mine[0, window, :] + hidden[window, :] * first_y

    loop(half // ROWS, add_hidden)
    branch_store = pltpu.make_async_copy(mine.at[0], branch_out, local_sem.at[12])
    branch_store.start()

    for store in stores:
        store.wait()
    operands = [
        pltpu.make_async_copy(query_ref, act.at[:, pl.ds(0, 512)], local_sem.at[0]),
        pltpu.make_async_copy(keys_ref, act.at[:, pl.ds(1024, 512)], local_sem.at[1]),
        pltpu.make_async_copy(values_ref, act.at[:, pl.ds(1536, 512)], local_sem.at[2]),
        pltpu.make_async_copy(w_out_ref, gate_w.at[pl.ds(0, 512)], local_sem.at[3]),
    ]
    for operand in operands:
        operand.start()
    for operand in operands:
        operand.wait()

    gain_out[...] = jnp.zeros_like(gain_out)
    sums = y_in.at[0]
    sums[:, pl.ds(0, 1024)] = jnp.zeros((TILE, 1024), F32)

    def hidden_copy(k):
        return remote(
            core_in.at[0, rows(k)], normed_twin.at[rows(k)],
            hidden_send.at[k], hidden_recv.at[k], twin_id,
        )

    def hidden_far(block, b):
        local = pl.ds(block * run, run)
        return remote(
            core_in.at[0, local, far_columns(b)],
            grad_attn_far.at[0, local, pl.ds(b * 512, 512)],
            far_send.at[3 + 2 * block + b], far_recv.at[3 + 2 * block + b], far_id,
        )

    def gather_into(offset, kv, value):
        for part in range(value.shape[0] // TILE):
            columns = pl.ds(pl.multiple_of(offset + kv * 256 + part * 128, 128), 128)
            sums[:, columns] = sums[:, columns] + value[part * TILE : (part + 1) * TILE]

    def put(block, column, value):
        gu[pl.ds(block * TILE, TILE), pl.ds(column, 128)] = value.astype(BF16)

    def attend_back(block, p):
        kv = p // 2
        column = pl.multiple_of(p * 128, 128)
        keys_seen = (block + 1) * TILE
        window = pl.ds(block * TILE, TILE)
        seen = pl.ds(0, keys_seen)
        queries = act[window, pl.ds(column, 128)]
        upstream = act[window, pl.ds(pl.multiple_of(512 + column, 128), 128)]
        allowed = allowed_of(block)
        query_grad = jnp.zeros((TILE, 128), F32)
        for side in range(2):
            padded = pl.multiple_of((kv * 2 + side) * 128, 128)
            keys = act[seen, pl.ds(pl.multiple_of(1024 + padded, 128), 128)]
            vals = act[seen, pl.ds(pl.multiple_of(1536 + padded, 128), 128)]
            raw = lax.dot_general(keys, queries, transposed, preferred_element_type=F32) * factor
            log_total = log_total_ref[pl.ds(2 * p + side, 1), window]
            probs = jnp.exp(jnp.where(allowed, raw - log_total, MASKED))
            grad_probs = lax.dot_general(
                vals, upstream, transposed, preferred_element_type=F32
            )
            row_sum = jnp.sum(probs * grad_probs, axis=0, keepdims=True)
            grad_raw = (probs * (grad_probs - row_sum)).astype(BF16)
            query_grad = query_grad + lax.dot_general(
                grad_raw, keys, (((0,), (0,)), ((), ())), preferred_element_type=F32
            )
            own = (lax.broadcasted_iota(jnp.int32, (keys_seen, 128), 1) // 64) == side
            gather_into(0, kv, jnp.where(
                own, jnp.dot(grad_raw, queries, preferred_element_type=F32), 0.0
            ))
            gather_into(512, kv, jnp.where(
                own, jnp.dot(probs.astype(BF16), upstream, preferred_element_type=F32), 0.0
            ))
        put(block, column, unrotate_tile(query_grad * factor, window))

    for block in range(2):
        loop(tiles, lambda j: y_copy(1, block_window(block, j), block * tiles + j).wait_recv())
        if block == 1:
            quarter_y().start()
        for k in (2 * block, 2 * block + 1):

            def norm_rows(i, k=k):
                window = pl.ds(pl.multiple_of(k * chunk + i * ROWS, ROWS), ROWS)
                here = pl.ds(pl.multiple_of(own_chunk(k, core) + i * ROWS, ROWS), ROWS)
                incoming = mine[1, window, :] + y_in[1, window, :]
                values = hidden[window, :]
                scale = lax.rsqrt(jnp.mean(values * values, axis=-1, keepdims=True) + EPSILON)
                weighted = incoming * gain
                inner = jnp.mean(weighted * values, axis=-1, keepdims=True)
                back = scale * weighted - values * (scale * scale * scale) * inner
                total = cot[here, :].astype(F32) + back
                core_in[0, window, :] = total
                normed[here, :] = total.astype(BF16)
                gain_out[...] = gain_out[...] + jnp.sum(
                    incoming * values * scale, axis=0, keepdims=True
                )

            loop(chunk // ROWS, norm_rows)
            hidden_copy(k).start()
        for b in range(2):
            hidden_far(block, b).start()
        for k in (2 * block, 2 * block + 1):
            hidden_copy(k).wait_recv()

            def take_hidden(i, k=k):
                here = pl.ds(pl.multiple_of(own_chunk(k, 1 - core) + i * ROWS, ROWS), ROWS)
                normed[here, :] = normed_twin[
                    pl.ds(pl.multiple_of(k * chunk + i * ROWS, ROWS), ROWS), :
                ].astype(BF16)

            loop(chunk // ROWS, take_hidden)

        def head_tile(j, block=block):
            window = pl.ds(block * TILE, TILE)
            act[window, pl.ds(pl.multiple_of(512 + j * TILE, TILE), TILE)] = lax.dot_general(
                normed[window, :], gate_w[tile_of(j), :], transposed, preferred_element_type=F32
            ).astype(BF16)

        loop(512 // TILE, head_tile)
        loop(query_width // 128, functools.partial(attend_back, block))
        if block == 0:
            for k in (0, 1):
                from_z(normed_sent, normed_others, k, n_send, n_recv).wait_recv()
                from_zx(normed_others, k, n_send, n_recv).start()
            for k in range(CHUNKS):
                from_x(cot_half, cot_others, k, cot_send, cot_recv).wait()
            to_twin(cot_others, 0, 0).start()

    grad_stores = [
        pltpu.make_async_copy(core_in.at[0], grad_hidden_out, local_sem.at[4]),
        pltpu.make_async_copy(normed, grad_attn_out, local_sem.at[5]),
    ]
    for store in grad_stores:
        store.start()

    def both(offset, block):
        def folded(kv):
            value = sums[:, pl.ds(offset + kv * 256 + block * 128, 128)]
            return value + pltpu.roll(value, 64, 1)

        return jnp.where(lane < 64, folded(0), folded(1))

    for block in range(2):
        window = pl.ds(block * TILE, TILE)
        put(block, 512, unrotate_tile(both(0, block) * factor, window))
        put(block, 640, both(512, block))
    projected_store = pltpu.make_async_copy(
        gu.at[:, pl.ds(0, 768)], projected_out, local_sem.at[6]
    )
    projected_store.start()

    last_z().wait()
    last_y().start()
    normed_one_copy.wait()
    normed_one_twin = remote(
        normed_one_far.at[0], normed_one_far.at[1], far_send.at[2], far_recv.at[2], twin_id
    )
    normed_one_twin.start()
    heads_copy.wait()
    for block in range(2):
        for b in range(2):
            hidden_far(block, b).wait()
    hidden_far_twin = remote(
        grad_attn_far.at[0], grad_attn_far.at[1], far_send.at[7], far_recv.at[7], twin_id
    )
    hidden_far_twin.start()
    for k in range(CHUNKS):
        from_x(normed_sent, normed_others, k, n_send, n_recv).wait_recv()
    to_twin(normed_others, 1, 0).start()
    quarter_y().wait()
    to_twin(cot_others, 0, 1).start()
    last_y().wait()
    to_twin(normed_others, 1, 1).start()

    for store in grad_stores + [projected_store, branch_store]:
        store.wait()
    for copy in (hidden_far_twin, normed_one_twin, quarter_zx()):
        copy.wait()
    for k in range(CHUNKS):
        hidden_copy(k).wait_send()
        twin_copy(k).wait_send()
        from_x(normed_sent, normed_others, k, n_send, n_recv).wait_send()
    for k in (0, 1):
        from_z(normed_sent, normed_others, k, n_send, n_recv).wait_send()
        from_zx(normed_others, k, n_send, n_recv).wait()
    for block in range(2):
        loop(tiles, lambda j: y_copy(1, block_window(block, j), block * tiles + j).wait_send())
    loop(tiles, lambda j: core_copy(2, (everything, tile_of(j)), j).wait_send())
    for slot in range(2):
        to_twin(cot_others, 0, slot).wait()
        to_twin(normed_others, 1, slot).wait()


def middle(
    w_query, w_key, w_value, w_out, tokens, cotangent, gain_one, gain,
    w_gate, w_up, w_down, segment, position, frequency,
):
    row_count, width = tokens.shape
    half = row_count // 2
    hidden_units = w_gate.shape[1]
    tiles = width // TILE
    hbm = pl.BlockSpec(memory_space=pl.ANY)
    vmem = pl.BlockSpec(memory_space=pltpu.VMEM)
    wide = jax.ShapeDtypeStruct((half, width), F32)
    units = jax.ShapeDtypeStruct((row_count, hidden_units), BF16)
    square = jax.ShapeDtypeStruct((row_count, 512), BF16)
    dma = pltpu.SemaphoreType.DMA
    return pl.pallas_call(
        middle_kernel,
        out_shape=(
            jax.ShapeDtypeStruct((row_count, width), BF16),
            square, square, square, square,
            jax.ShapeDtypeStruct((2, half, width // 2), F32),
            jax.ShapeDtypeStruct((half, width // 2), F32),
            wide,
            jax.ShapeDtypeStruct((row_count, width), BF16),
            jax.ShapeDtypeStruct((row_count, 768), BF16),
            jax.ShapeDtypeStruct((2, half, width // 2), F32),
            wide,
            jax.ShapeDtypeStruct((row_count, width), BF16),
            units, units, units,
            jax.ShapeDtypeStruct((1, width), F32),
            jax.ShapeDtypeStruct((5, half, width), F32),
            jax.ShapeDtypeStruct((5, half, width), F32),
        ),
        in_specs=[hbm] * 6 + [vmem] * 2 + [hbm] * 3 + [vmem] * 3,
        out_specs=(hbm,) * 16 + (vmem,) + (hbm,) * 2,
        scratch_shapes=[
            pltpu.VMEM(w_gate.shape, BF16),
            pltpu.VMEM(w_up.shape, BF16),
            pltpu.VMEM(w_down.shape, BF16),
            pltpu.VMEM((row_count, width), BF16),
            pltpu.VMEM((half, width), F32),
            pltpu.VMEM((row_count, width), BF16),
            pltpu.VMEM((half, width), F32),
            pltpu.VMEM((half, width), F32),
            pltpu.VMEM((row_count, hidden_units), BF16),
            pltpu.VMEM((row_count, hidden_units), BF16),
            pltpu.VMEM((row_count, hidden_units), BF16),
            pltpu.VMEM((half, width), F32),
            pltpu.VMEM((2, half, width), F32),
            pltpu.VMEM((3, half, width), F32),
            pltpu.VMEM((2, half, width), F32),
            pltpu.VMEM((half, TILE), F32),
            pltpu.VMEM((8, row_count), F32),
            pltpu.VMEM((row_count, 8), F32),
            pltpu.VMEM((row_count, 128), F32),
            pltpu.VMEM((row_count, 128), F32),
            dma((13,)),
            dma((3, 2 * tiles)), dma((3, 2 * tiles)), dma((2, 2 * tiles)), dma((2, 2 * tiles)),
            dma((3, CHUNKS)), dma((3, CHUNKS)),
            dma((4, CHUNKS)), dma((4, CHUNKS)),
            dma((2, 2)), dma((2, 2)),
            dma((CHUNKS,)), dma((CHUNKS,)),
            dma((8,)), dma((8,)),
            pltpu.SemaphoreType.REGULAR,
        ],
        compiler_params=pltpu.CompilerParams(
            collective_id=0, has_side_effects=True, vmem_limit_bytes=64 * 1024 * 1024
        ),
        name="feed_forward",
    )(
        w_query, w_key, w_value, w_out, tokens, cotangent,
        gain_one.reshape(1, width), gain.reshape(1, width), w_gate, w_up, w_down,
        segment.reshape(1, row_count), position.reshape(1, row_count), frequency.reshape(1, 128),
    )


LAST = 2


def last_kernel(
    normed_others_ref,
    cot_others_ref,
    normed_ref,
    cot_ref,
    act_ref,
    gg_ref,
    gu_ref,
    w_gate_ref,
    w_up_ref,
    w_down_ref,
    projected_ref,
    branch_ref,
    gain_two_ref,
    w_query_ref,
    w_key_ref,
    w_value_ref,
    heads_ref,
    grad_attn_ref,
    grad_attn_far_ref,
    normed_one_ref,
    normed_one_far_ref,
    heads_far_ref,
    grad_hidden_ref,
    tokens_ref,
    gain_ref,
    kept_out,
    sent_out,
    came_out,
    down_kept,
    down_sent,
    down_came,
    down_last,
    out_mine,
    out_came,
    proj_mine,
    proj_came,
    input_out,
    mixed_out,
    branch_came,
    normed_late,
    cot_late,
    gain_out,
    normed,
    cot,
    normed_t,
    cot_t,
    units,
    gate_w,
    up_w,
    down_w,
    total,
    staged,
    core_in,
    y_in,
    w_proj,
    tok,
    heads,
    grad_attn,
    normed_one,
    projected,
    out_part,
    proj_part,
    out_x,
    proj_x,
    far_staged,
    far_heads,
    gains,
    gains_came,
    load_sem,
    piece_sem,
    weight_sem,
    unit_sem,
    store_sem,
    row_send,
    row_recv,
    core_send,
    core_recv,
    y_send,
    y_recv,
    x_send,
    x_recv,
    z_send,
    z_recv,
    end_send,
    end_recv,
    gain_send,
    gain_recv,
    late_send,
    late_recv,
    product,
):
    dp, tensor = lax.axis_index("dp"), lax.axis_index("tensor")
    core = tensor % 2
    x_low, z_low, z_high = dp % 2, (dp // 2) % 2, dp // 4
    twin_id = (dp, flip(tensor, 1))
    y_id = (dp, flip(tensor, 2))
    x_id = (flip(dp, 1), tensor)
    z_id = (flip(dp, 4), tensor)
    far_id = (flip(dp, 2), tensor)
    half, width = tok.shape
    row_count = 2 * half
    tiles = width // TILE
    run = half // 2
    y_bit = (tensor // 2) % 2

    def own_row(block, which):
        return pl.multiple_of(block * half + which * run, run)

    everything = slice(None)
    transposed = (((1,), (1,)), ((), ()))
    over = (((0,), (0,)), ((), ()))

    def remote(src, dst, send, recv, device):
        return pltpu.make_async_remote_copy(
            src_ref=src, dst_ref=dst, send_sem=send, recv_sem=recv,
            device_id=device, device_id_type=MESH,
        )

    def tile_of(j):
        return pl.ds(pl.multiple_of(j * TILE, TILE), TILE)

    away_block = tile_of(flip(dp, 2))
    home_block = tile_of(dp)
    near = [
        pl.ds(pl.multiple_of(b * 1024 + z_low * 512, 512), 512) for b in range(2)
    ]
    own_columns = [units.at[0, pl.ds(i * row_count, row_count)] for i in range(4)]
    loads = [
        pltpu.make_async_copy(normed_ref.at[:, away_block], own_columns[0], load_sem.at[0]),
        pltpu.make_async_copy(normed_ref.at[:, home_block], own_columns[1], load_sem.at[1]),
        pltpu.make_async_copy(cot_ref.at[:, away_block], own_columns[2], load_sem.at[2]),
        pltpu.make_async_copy(cot_ref.at[:, home_block], own_columns[3], load_sem.at[3]),
        pltpu.make_async_copy(w_query_ref, w_proj.at[:, pl.ds(0, 512)], load_sem.at[4]),
        pltpu.make_async_copy(w_key_ref, w_proj.at[:, pl.ds(512, 128)], load_sem.at[5]),
        pltpu.make_async_copy(w_value_ref, w_proj.at[:, pl.ds(640, 128)], load_sem.at[6]),
        pltpu.make_async_copy(
            tokens_ref.at[pl.ds(own_row(0, core), run)], tok.at[pl.ds(0, run)], load_sem.at[7]
        ),
        pltpu.make_async_copy(heads_ref, heads.at[0], load_sem.at[8]),
        pltpu.make_async_copy(
            grad_attn_ref.at[:, near[0]], grad_attn.at[0, :, pl.ds(0, 512)], load_sem.at[9]
        ),
        pltpu.make_async_copy(
            grad_attn_ref.at[:, near[1]], grad_attn.at[0, :, pl.ds(512, 512)], load_sem.at[10]
        ),
        pltpu.make_async_copy(
            normed_one_ref.at[:, near[0]], normed_one.at[0, :, pl.ds(0, 512)], load_sem.at[11]
        ),
        pltpu.make_async_copy(
            normed_one_ref.at[:, near[1]], normed_one.at[0, :, pl.ds(512, 512)], load_sem.at[12]
        ),
        pltpu.make_async_copy(projected_ref, projected.at[0], load_sem.at[13]),
        pltpu.make_async_copy(
            tokens_ref.at[pl.ds(own_row(1, core), run)], tok.at[pl.ds(run, run)], load_sem.at[14]
        ),
    ]

    late_normed = pl.ds(run, run)
    early_normed = pl.ds(0, run)
    late_cot = pl.ds(pl.multiple_of((1 - y_bit) * run, run), run)
    early_cot = pl.ds(pl.multiple_of(y_bit * run, run), run)

    def piece_load(i, slot):
        which, part = i // 6, i % 6
        source = (normed_others_ref, cot_others_ref)[which]
        late = (normed_late, cot_late)[which]
        into = staged.at[slot]
        if part in (0, 1, 3, 4):
            return [pltpu.make_async_copy(source.at[part], into, piece_sem.at[slot])]
        if part == 5:
            return [pltpu.make_async_copy(late.at[1], into, piece_sem.at[slot])]
        early_rows = (early_normed, early_cot)[which]
        late_rows = (late_normed, late_cot)[which]
        return [
            pltpu.make_async_copy(
                source.at[2, early_rows], into.at[early_rows], piece_sem.at[slot]
            ),
            pltpu.make_async_copy(
                late.at[0, late_rows], into.at[late_rows], piece_sem.at[2 + slot]
            ),
        ]

    def weight_loads(j, slot):
        return [
            pltpu.make_async_copy(
                w_gate_ref.at[:, tile_of(j)], gate_w.at[slot], weight_sem.at[slot, 0]
            ),
            pltpu.make_async_copy(
                w_up_ref.at[:, tile_of(j)], up_w.at[slot], weight_sem.at[slot, 1]
            ),
            pltpu.make_async_copy(
                w_down_ref.at[tile_of(j), :], down_w.at[slot], weight_sem.at[slot, 2]
            ),
        ]

    order = [0, 1, 3, 4, 6, 7, 9, 10, 2, 5, 8, 11]
    for i in range(2):
        for load in piece_load(order[i], i):
            load.start()
    loads[13].start()
    for load in loads[:4]:
        load.start()
    for load in weight_loads(0, 0):
        load.start()

    barrier = pltpu.get_barrier_semaphore()
    peers = []
    for m in range(1, 8):
        peer = dp
        for bit in (1, 2, 4):
            peer = flip(peer, bit) if m & bit else peer
        peers.append(peer)
    for device in [twin_id, y_id] + [(peer, tensor) for peer in peers]:
        pl.semaphore_signal(barrier, inc=1, device_id=device, device_id_type=MESH)
    pl.semaphore_wait(barrier, 9)
    late_copies = [
        remote(normed_others_ref.at[1, late_normed], normed_late.at[0, late_normed],
               late_send.at[0], late_recv.at[0], x_id),
        remote(cot_others_ref.at[2, early_cot], cot_late.at[0, early_cot],
               late_send.at[1], late_recv.at[1], y_id),
        remote(normed_others_ref.at[2, early_normed], normed_late.at[1, early_normed],
               late_send.at[2], late_recv.at[2], twin_id),
        remote(cot_others_ref.at[2, early_cot], cot_late.at[1, early_cot],
               late_send.at[3], late_recv.at[3], twin_id),
    ]
    for copy in late_copies:
        copy.start()

    loads[13].wait()

    def widen(r):
        window = pl.ds(pl.multiple_of(r * ROWS, ROWS), ROWS)
        for s in range(2):
            there = pl.ds(pl.multiple_of(s * half + r * ROWS, ROWS), ROWS)
            proj_part[0, s, window, :] = projected[0, there, :].astype(F32)

    loop(half // ROWS, widen)
    projected_copy = remote(proj_part.at[0], far_staged, end_send.at[2], end_recv.at[2], far_id)
    projected_copy.start()
    branch_copy = remote(branch_ref, branch_came, end_send.at[1], end_recv.at[1], y_id)

    late_twins = [
        remote(normed_late.at[0, late_normed], normed_late.at[1, late_normed],
               late_send.at[4], late_recv.at[4], twin_id),
        remote(cot_late.at[0, late_cot], cot_late.at[1, late_cot],
               late_send.at[5], late_recv.at[5], twin_id),
    ]
    def take_piece(place):
        i, slot = order[place], place % 2
        for load in piece_load(i, slot):
            load.wait()
        rows_to, turned_to = (normed, normed_t) if i < 6 else (cot, cot_t)
        base = {0: 0, 1: 1, 3: 2, 4: 3, 2: 4, 5: 5}[i % 6] * half

        def convert(r, slot=slot, rows_to=rows_to, base=base):
            window = pl.ds(pl.multiple_of(r * ROWS, ROWS), ROWS)
            rows_to[pl.ds(pl.multiple_of(base + r * ROWS, ROWS), ROWS), :] = staged[
                slot, window, :
            ].astype(BF16)

        loop(half // ROWS, convert)
        for part, block in enumerate((away_block, home_block)):
            turned_to[pl.ds(part * TILE, TILE), pl.ds(row_count + base, half)] = (
                staged[slot, :, block].T.astype(BF16)
            )
        if place == 5:
            for copy, later in zip(late_copies[:2], late_twins):
                copy.wait()
                later.start()
            branch_copy.start()
        if place == 6:
            for copy in late_copies[2:]:
                copy.wait()
        if place == 7:
            for copy in late_twins:
                copy.wait()
        if place + 2 < 12:
            for load in piece_load(order[place + 2], slot):
                load.start()
    for place in range(8):
        take_piece(place)
    for part in range(4):
        loads[part].wait()
        turned_to = (normed_t, cot_t)[part // 2]
        turned_to[pl.ds((part % 2) * TILE, TILE), pl.ds(0, row_count)] = (
            own_columns[part][...].astype(F32).T.astype(BF16)
        )

    def row_copy(j):
        window = (everything, everything, tile_of(j))
        return [
            remote(
                sent_out.at[window], came_out.at[window],
                row_send.at[0, j], row_recv.at[0, j], far_id,
            ),
            remote(
                down_sent.at[tile_of(j)], down_came.at[tile_of(j)],
                row_send.at[1, j], row_recv.at[1, j], far_id,
            ),
        ]

    def stores(j, slot):
        return [
            pltpu.make_async_copy(
                total.at[slot, pl.ds(0, 2), pl.ds(0, TILE)], sent_out.at[:, :, tile_of(j)],
                store_sem.at[slot, 0],
            ),
            pltpu.make_async_copy(
                total.at[slot, pl.ds(0, 2), pl.ds(TILE, TILE)], kept_out.at[:, :, tile_of(j)],
                store_sem.at[slot, 1],
            ),
            pltpu.make_async_copy(
                total.at[slot, 2, pl.ds(TILE, TILE)], down_kept.at[tile_of(j)],
                store_sem.at[slot, 3],
            ),
        ]

    def down_store(slot, into):
        return pltpu.make_async_copy(
            total.at[slot, 2, pl.ds(0, TILE)], into, store_sem.at[slot, 2]
        )

    def unit_loads(j):
        return [
            pltpu.make_async_copy(
                source.at[:, tile_of(j)], units.at[i, pl.ds(0, row_count)], unit_sem.at[i]
            )
            for i, source in enumerate((gg_ref, gu_ref, act_ref))
        ]

    def feed_forward_tile(j, first=False):
        slot = j % 2
        for load in weight_loads(j, slot):
            load.wait()

        if first:
            for load in weight_loads(1, 1):
                load.start()
        else:

            @pl.when(j + 1 < tiles)
            def _():
                for load in weight_loads(j + 1, 1 - slot):
                    load.start()

        for load in unit_loads(j):
            load.start()

        def block(m):
            rows = pl.ds(pl.multiple_of(m * 512, 512), 512)
            to = pl.ds(pl.multiple_of(row_count + m * 512, 512), 512)
            gate = jnp.dot(normed[rows, :], gate_w[slot], preferred_element_type=F32)
            up = jnp.dot(normed[rows, :], up_w[slot], preferred_element_type=F32)
            back = lax.dot_general(
                cot[rows, :], down_w[slot], transposed, preferred_element_type=F32
            )
            sigmoid = jax.nn.sigmoid(gate)
            swish = gate * sigmoid
            units[2, to, :] = (swish * up).astype(BF16)
            units[0, to, :] = (back * up * sigmoid * (1.0 + gate * (1.0 - sigmoid))).astype(BF16)
            units[1, to, :] = (back * swish).astype(BF16)

        if first:
            loop(2, block)
            for place in range(8, 12):
                take_piece(place)
            block(2)
        else:
            loop(normed.shape[0] // 512, block)
        for load in unit_loads(j):
            load.wait()

        total[slot, 0] = jnp.dot(normed_t[...], units[0], preferred_element_type=F32)
        total[slot, 1] = jnp.dot(normed_t[...], units[1], preferred_element_type=F32)
        turned = jnp.dot(cot_t[...], units[2], preferred_element_type=F32)
        for part in range(2):
            total[slot, 2, pl.ds(part * TILE, TILE)] = turned[part * TILE : (part + 1) * TILE].T
        for store in stores(j, slot):
            store.start()
        here = j < tiles - LAST

        @pl.when(here)
        def _():
            store = down_store(slot, down_sent.at[tile_of(j)])
            store.start()
            store.wait()
            row_copy(j)[1].start()

        @pl.when(jnp.logical_not(here))
        def _():
            store = down_store(slot, down_last.at[tile_of(j - (tiles - LAST))])
            store.start()
            store.wait()

        for store in stores(j, slot):
            store.wait()
        row_copy(j)[0].start()

    def x_copies(slot):
        return [
            remote(out_part.at[0, slot], out_x.at[slot], x_send.at[0, slot],
                   x_recv.at[0, slot], x_id),
            remote(proj_part.at[0, slot], proj_x.at[slot], x_send.at[1, slot],
                   x_recv.at[1, slot], x_id),
        ]

    def attention_parts():
        for load in far_loads + loads[8:13]:
            load.wait()
        projected_copy.wait()

        def convert(r):
            window = pl.ds(pl.multiple_of(r * ROWS, ROWS), ROWS)
            block, rest = r // (run // ROWS), r % (run // ROWS)
            for s in range(2):
                which = core if s == 0 else 1 - core
                here = pl.ds(
                    pl.multiple_of(block * half + which * run + rest * ROWS, ROWS), ROWS
                )
                grad_attn[1, here, :] = staged[0, window, pl.ds(s * 1024, 1024)].astype(BF16)
                normed_one[1, here, :] = staged[1, window, pl.ds(s * 1024, 1024)].astype(BF16)
                there = pl.ds(pl.multiple_of(s * half + r * ROWS, ROWS), ROWS)
                projected[1, there, :] = far_staged[s, window, :].astype(BF16)
                heads[1, there, :] = far_heads[window, pl.ds(s * 512, 512)].astype(BF16)

        loop(half // ROWS, convert)
        for side in range(2):
            x_at = 1 - x_low if side == 0 else x_low
            for slot in range(2):
                z_at = 1 - z_high if slot == 0 else z_high
                columns = pl.ds(pl.multiple_of(z_at * 512 + x_at * 256, 256), 256)
                out_part[side, slot] = lax.dot_general(
                    heads[0], grad_attn[0, :, columns], over, preferred_element_type=F32
                ) + lax.dot_general(
                    heads[1], grad_attn[1, :, columns], over, preferred_element_type=F32
                )
                proj_part[side, slot] = lax.dot_general(
                    normed_one[0, :, columns], projected[0], over, preferred_element_type=F32
                ) + lax.dot_general(
                    normed_one[1, :, columns], projected[1], over, preferred_element_type=F32
                )
                if side == 0:
                    for copy in x_copies(slot):
                        copy.start()

    def core_copy(j):
        window = (everything, tile_of(j))
        return remote(
            staged.at[0].at[window], core_in.at[window], core_send.at[j], core_recv.at[j], twin_id
        )

    def y_copy(j):
        window = (everything, tile_of(j))
        return remote(
            staged.at[1].at[window], y_in.at[window], y_send.at[j], y_recv.at[j], y_id
        )

    def attention_sums():
        for load in loads[4:8] + loads[14:]:
            load.wait()

        def produce(j):
            product[...] = lax.dot_general(
                projected[0], w_proj[tile_of(j), :], transposed, preferred_element_type=F32
            )
            for block in range(2):
                for slot, which in ((0, 1 - core), (1, core)):
                    staged[slot, pl.ds(block * run, run), tile_of(j)] = product[
                        pl.ds(own_row(block, which), run), :
                    ]
            core_copy(j).start()

        def forward(j):
            core_copy(j).wait_recv()
            staged[1, :, tile_of(j)] = staged[1, :, tile_of(j)] + core_in[:, tile_of(j)]
            y_copy(j).start()

        produce(0)

        def step(j):
            produce(j + 1)
            forward(j)

        loop(tiles - 1, step)
        forward(tiles - 1)
        loop(tiles, lambda j: core_copy(j).wait_send())

    feed_forward_tile(0, first=True)
    for load in loads[4:13] + loads[14:]:
        load.start()
    far_loads = (
        [
            pltpu.make_async_copy(
                grad_attn_far_ref.at[s], staged.at[0, :, pl.ds(s * 1024, 1024)], piece_sem.at[s]
            )
            for s in range(2)
        ]
        + [
            pltpu.make_async_copy(
                normed_one_far_ref.at[s], staged.at[1, :, pl.ds(s * 1024, 1024)],
                piece_sem.at[2 + s],
            )
            for s in range(2)
        ]
        + [
            pltpu.make_async_copy(heads_far_ref, far_heads, piece_sem.at[5]),
        ]
    )
    for load in far_loads:
        load.start()


    def step(j):
        feed_forward_tile(j + 1)

        @pl.when(j == 0)
        def _():
            attention_parts()
            attention_sums()

    loop(tiles - 1, step)
    hidden_load = pltpu.make_async_copy(grad_hidden_ref, core_in, load_sem.at[0])
    hidden_load.start()

    def z_copies():
        return [
            remote(out_part.at[1, 0], out_came, z_send.at[0], z_recv.at[0], z_id),
            remote(proj_part.at[1, 0], proj_came, z_send.at[1], z_recv.at[1], z_id),
        ]

    for slot in range(2):
        for copy in x_copies(slot):
            copy.wait_recv()
        out_part[1, slot] = out_part[1, slot] + out_x[slot]
        proj_part[1, slot] = proj_part[1, slot] + proj_x[slot]
        if slot == 0:
            for copy in z_copies():
                copy.start()
    part_stores = [
        pltpu.make_async_copy(out_part.at[1, 1], out_mine, load_sem.at[1]),
        pltpu.make_async_copy(proj_part.at[1, 1], proj_mine, load_sem.at[2]),
    ]
    for store in part_stores:
        store.start()

    gain = gain_ref[...]
    gains[pl.ds(0, 1), :] = jnp.zeros_like(gain)
    gains[pl.ds(1, 1), :] = gain_two_ref[...]
    hidden_load.wait()
    loop(tiles, lambda j: y_copy(j).wait_recv())

    def norm_rows(i):
        window = pl.ds(pl.multiple_of(i * ROWS, ROWS), ROWS)
        incoming = staged[1, window, :] + y_in[window, :]
        values = tok[window, :].astype(F32)
        scale = lax.rsqrt(jnp.mean(values * values, axis=-1, keepdims=True) + EPSILON)
        weighted = incoming * gain
        inner = jnp.mean(weighted * values, axis=-1, keepdims=True)
        back = scale * weighted - values * (scale * scale * scale) * inner
        staged[0, window, :] = core_in[window, :] + back
        gains[pl.ds(0, 1), :] = gains[pl.ds(0, 1), :] + jnp.sum(
            incoming * values * scale, axis=0, keepdims=True
        )

    loop(half // ROWS, norm_rows)

    def to_rows(slot, out, sems, first):
        copies, kept = [], []
        for block in range(2):
            local, here = pl.ds(block * run, run), pl.ds(own_row(block, core), run)
            copies.append(remote(
                staged.at[slot, local], out.at[here],
                end_send.at[sems + block], end_recv.at[sems + block], twin_id,
            ))
            kept.append(pltpu.make_async_copy(
                staged.at[slot, local], out.at[here], load_sem.at[first + block]
            ))
        for copy in copies + kept:
            copy.start()
        return copies, kept

    input_copies, input_stores = to_rows(0, input_out, 3, 3)

    gain_twin = remote(gains, gains_came, gain_send.at[7], gain_recv.at[7], twin_id)
    gain_twin.start()

    loop(tiles, lambda j: y_copy(j).wait_send())
    branch_copy.wait()
    branch_loads = [
        pltpu.make_async_copy(branch_ref, staged.at[1], load_sem.at[5]),
        pltpu.make_async_copy(branch_came, y_in, load_sem.at[6]),
    ]
    for load in branch_loads:
        load.start()
    gain_twin.wait()
    gains[...] = gains[...] + gains_came[...]

    def gain_copy(m):
        return remote(
            gains.at[:, tile_of(peers[m])], gain_out.at[m], gain_send.at[m], gain_recv.at[m],
            (peers[m], tensor),
        )

    for m in range(7):
        gain_copy(m).start()
    gain_out[7] = gains[:, tile_of(dp)]
    for load in branch_loads:
        load.wait()

    def mixed_rows(i):
        window = pl.ds(pl.multiple_of(i * ROWS, ROWS), ROWS)
        staged[1, window, :] = staged[1, window, :] + y_in[window, :]

    loop(half // ROWS, mixed_rows)
    mixed_copy = remote(staged.at[1], core_in, end_send.at[5], end_recv.at[5], twin_id)
    mixed_copy.start()

    def put_mixed(source, which, first):
        def narrow(i):
            window = pl.ds(pl.multiple_of(i * ROWS, ROWS), ROWS)
            tok[window, :] = source[window, :].astype(BF16)

        loop(half // ROWS, narrow)
        copies = [
            pltpu.make_async_copy(
                tok.at[pl.ds(block * run, run)], mixed_out.at[pl.ds(own_row(block, which), run)],
                load_sem.at[first + block],
            )
            for block in range(2)
        ]
        for copy in copies:
            copy.start()
        for copy in copies:
            copy.wait()

    put_mixed(staged.at[1], core, 7)
    mixed_copy.wait()
    put_mixed(core_in, 1 - core, 9)

    for copy in part_stores + input_stores + input_copies:
        copy.wait()
    for m in range(7):
        gain_copy(m).wait()
    for slot in range(2):
        for copy in x_copies(slot):
            copy.wait_send()
    for copy in z_copies():
        copy.wait()
    loop(tiles, lambda j: row_copy(j)[0].wait())
    loop(tiles - LAST, lambda j: row_copy(j)[1].wait())


def last(
    normed_others, cot_others, normed, cot, act, gg, gu, w_gate, w_up, w_down,
    projected, branch, gain_two, w_query, w_key, w_value, heads, grad_attn, grad_attn_far,
    normed_one, normed_one_far, heads_far, grad_hidden, tokens, gain,
):
    row_count, width = tokens.shape
    half = row_count // 2
    tiles = width // TILE
    hidden_units = w_gate.shape[1]
    hbm = pl.BlockSpec(memory_space=pl.ANY)
    vmem = pl.BlockSpec(memory_space=pltpu.VMEM)
    wide = jax.ShapeDtypeStruct((half, width), F32)
    rows_pair = jax.ShapeDtypeStruct((2, TILE, hidden_units), F32)
    columns = jax.ShapeDtypeStruct((hidden_units, TILE), F32)
    out_block = jax.ShapeDtypeStruct((512, TILE), F32)
    proj_block = jax.ShapeDtypeStruct((TILE, 768), F32)
    dma = pltpu.SemaphoreType.DMA
    return pl.pallas_call(
        last_kernel,
        out_shape=(
            rows_pair, rows_pair, rows_pair, columns, columns, columns,
            jax.ShapeDtypeStruct((LAST * TILE, TILE), F32), out_block, out_block, proj_block, proj_block,
            jax.ShapeDtypeStruct((row_count, width), F32),
            jax.ShapeDtypeStruct((row_count, width), BF16),
            wide,
            jax.ShapeDtypeStruct((2, half, width), F32),
            jax.ShapeDtypeStruct((2, half, width), F32),
            jax.ShapeDtypeStruct((8, 2, TILE), F32),
        ),
        in_specs=[hbm] * 12 + [vmem] + [hbm] * 11 + [vmem],
        out_specs=(hbm,) * 16 + (vmem,),
        scratch_shapes=[
            pltpu.VMEM((6 * half, width), BF16),
            pltpu.VMEM((6 * half, width), BF16),
            pltpu.VMEM((2 * TILE, row_count + 6 * half), BF16),
            pltpu.VMEM((2 * TILE, row_count + 6 * half), BF16),
            pltpu.VMEM((3, row_count + 6 * half, TILE), BF16),
            pltpu.VMEM((2, width, TILE), BF16),
            pltpu.VMEM((2, width, TILE), BF16),
            pltpu.VMEM((2, TILE, width), BF16),
            pltpu.VMEM((2, 3, 2 * TILE, TILE), F32),
            pltpu.VMEM((2, half, width), F32),
            pltpu.VMEM((half, width), F32),
            pltpu.VMEM((half, width), F32),
            pltpu.VMEM((width, 768), BF16),
            pltpu.VMEM((half, width), BF16),
            pltpu.VMEM((2, row_count, 512), BF16),
            pltpu.VMEM((2, row_count, 1024), BF16),
            pltpu.VMEM((2, row_count, 1024), BF16),
            pltpu.VMEM((2, row_count, 768), BF16),
            pltpu.VMEM((2, 2, 512, TILE), F32),
            pltpu.VMEM((2, 2, TILE, 768), F32),
            pltpu.VMEM((2, 512, TILE), F32),
            pltpu.VMEM((2, TILE, 768), F32),
            pltpu.VMEM((2, half, 768), F32),
            pltpu.VMEM((half, 1024), F32),
            pltpu.VMEM((2, width), F32),
            pltpu.VMEM((2, width), F32),
            dma((15,)), dma((6,)), dma((2, 3)), dma((3,)), dma((2, 4)),
            dma((2, tiles)), dma((2, tiles)),
            dma((tiles,)), dma((tiles,)), dma((tiles,)), dma((tiles,)),
            dma((2, 2)), dma((2, 2)), dma((2,)), dma((2,)), dma((7,)), dma((7,)), dma((8,)), dma((8,)),
            dma((6,)), dma((6,)), pltpu.VMEM((row_count, TILE), F32),
        ],
        compiler_params=pltpu.CompilerParams(
            collective_id=1, has_side_effects=True, vmem_limit_bytes=64 * 1024 * 1024
        ),
        name="weight_gradients",
    )(
        normed_others, cot_others, normed, cot, act, gg, gu, w_gate, w_up, w_down,
        projected, branch, gain_two, w_query, w_key, w_value, heads, grad_attn, grad_attn_far,
        normed_one, normed_one_far, heads_far, grad_hidden, tokens, gain.reshape(1, width),
    )


def finish_kernel(
    kept, came, down_kept, down_came, out_mine, out_came, proj_mine, proj_came, input_in,
    mixed_in, gains, w_gate, w_up, w_down, w_out, w_query, w_key, w_value, grad_input, mixed,
    gain_one, gain_two,
):
    w_gate[...] = kept[0] + came[0]
    w_up[...] = kept[1] + came[1]
    w_down[...] = down_kept[...] + down_came[...]
    w_out[...] = out_mine[...] + out_came[...]
    queries, keys = w_query.shape[1], w_key.shape[1]
    w_query[...] = proj_mine[:, :queries] + proj_came[:, :queries]
    w_key[...] = proj_mine[:, queries : queries + keys] + proj_came[:, queries : queries + keys]
    w_value[...] = proj_mine[:, queries + keys :] + proj_came[:, queries + keys :]
    grad_input[...] = input_in[...]
    mixed[...] = mixed_in[...]
    total = jnp.sum(gains[...], axis=0)
    gain_one[...] = total[0:1]
    gain_two[...] = total[1:2]


def finish(*parts):
    steps = 8
    kept, down, out, proj, whole, gains = (parts[i] for i in (0, 2, 4, 6, 8, 10))
    rows, units = kept.shape[1:]

    def block(array, lead=()):
        size = array[len(lead) :]
        shape = lead + (size[0] // steps,) + size[1:]
        return pl.BlockSpec(shape, lambda i: (0,) * len(lead) + (i,) + (0,) * (len(size) - 1))

    fixed = lambda shape: pl.BlockSpec(shape, lambda i: (0,) * len(shape))
    outs = [
        (rows, units), (rows, units), down.shape, out.shape,
        (proj.shape[0], 512), (proj.shape[0], 128), (proj.shape[0], 128), whole.shape,
    ]
    return pl.pallas_call(
        finish_kernel,
        grid=(steps,),
        out_shape=[jax.ShapeDtypeStruct(shape, F32) for shape in outs]
        + [
            jax.ShapeDtypeStruct(whole.shape, BF16),
            jax.ShapeDtypeStruct((1, gains.shape[2]), F32),
            jax.ShapeDtypeStruct((1, gains.shape[2]), F32),
        ],
        in_specs=[block(kept.shape, (2,))] * 2
        + [block(part.shape) for part in parts[2:10]]
        + [fixed(gains.shape)],
        out_specs=[block(shape) for shape in outs]
        + [block(whole.shape)] + [fixed((1, gains.shape[2]))] * 2,
        compiler_params=pltpu.CompilerParams(vmem_limit_bytes=64 * 1024 * 1024),
        cost_estimate=pl.CostEstimate(
            flops=2_000_000, bytes_accessed=34_000_000, transcendentals=0
        ),
        name="last_sums",
    )(*parts)


def body(
    tokens,
    segments,
    positions,
    attn_gain,
    w_query,
    key_weight,
    value_weight,
    w_out,
    mlp_gain,
    w_gate,
    w_up,
    w_down,
    cotangent,
):
    row_count, width = tokens.shape
    half = row_count // 2
    hidden_units = w_gate.shape[1]
    tiles = width // TILE
    hbm = pl.BlockSpec(memory_space=pl.ANY)
    vmem = pl.BlockSpec(memory_space=pltpu.VMEM)
    wide = jax.ShapeDtypeStruct((half, width), F32)
    units = jax.ShapeDtypeStruct((row_count, hidden_units), BF16)
    square = jax.ShapeDtypeStruct((row_count, 512), BF16)
    dma = pltpu.SemaphoreType.DMA
    return pl.pallas_call(
        middle_kernel,
        out_shape=(
            jax.ShapeDtypeStruct((row_count, width), BF16),
            square, square, square, square,
            jax.ShapeDtypeStruct((2, half, width // 2), F32),
            jax.ShapeDtypeStruct((half, width // 2), F32),
            wide,
            jax.ShapeDtypeStruct((row_count, width), BF16),
            jax.ShapeDtypeStruct((row_count, 768), BF16),
            jax.ShapeDtypeStruct((2, half, width // 2), F32),
            wide,
            jax.ShapeDtypeStruct((row_count, width), BF16),
            units, units, units,
            jax.ShapeDtypeStruct((1, width), F32),
            jax.ShapeDtypeStruct((5, half, width), F32),
            jax.ShapeDtypeStruct((5, half, width), F32),
        ),
        in_specs=[hbm] * 6 + [vmem] * 2 + [hbm] * 3 + [vmem] * 3,
        out_specs=(hbm,) * 16 + (vmem,) + (hbm,) * 2,
        scratch_shapes=[
            pltpu.VMEM(w_gate.shape, BF16),
            pltpu.VMEM(w_up.shape, BF16),
            pltpu.VMEM(w_down.shape, BF16),
            pltpu.VMEM((row_count, width), BF16),
            pltpu.VMEM((half, width), F32),
            pltpu.VMEM((row_count, width), BF16),
            pltpu.VMEM((half, width), F32),
            pltpu.VMEM((half, width), F32),
            pltpu.VMEM((row_count, hidden_units), BF16),
            pltpu.VMEM((row_count, hidden_units), BF16),
            pltpu.VMEM((row_count, hidden_units), BF16),
            pltpu.VMEM((half, width), F32),
            pltpu.VMEM((2, half, width), F32),
            pltpu.VMEM((3, half, width), F32),
            pltpu.VMEM((2, half, width), F32),
            pltpu.VMEM((half, TILE), F32),
            pltpu.VMEM((8, row_count), F32),
            pltpu.VMEM((row_count, 8), F32),
            pltpu.VMEM((row_count, 128), F32),
            pltpu.VMEM((row_count, 128), F32),
            dma((13,)),
            dma((3, 2 * tiles)), dma((3, 2 * tiles)), dma((2, 2 * tiles)), dma((2, 2 * tiles)),
            dma((3, CHUNKS)), dma((3, CHUNKS)),
            dma((4, CHUNKS)), dma((4, CHUNKS)),
            dma((2, 2)), dma((2, 2)),
            dma((CHUNKS,)), dma((CHUNKS,)),
            dma((8,)), dma((8,)),
            pltpu.SemaphoreType.REGULAR,
        ],
        compiler_params=pltpu.CompilerParams(
            collective_id=0, has_side_effects=True, vmem_limit_bytes=64 * 1024 * 1024
        ),
        name="feed_forward",
    )(
        w_query, w_key, w_value, w_out, tokens, cotangent,
        gain_one.reshape(1, width), gain.reshape(1, width), w_gate, w_up, w_down,
        segment.reshape(1, row_count), position.reshape(1, row_count), frequency.reshape(1, 128),
    )


LAST = 2


def last_kernel(
    normed_others_ref,
    cot_others_ref,
    normed_ref,
    cot_ref,
    act_ref,
    gg_ref,
    gu_ref,
    w_gate_ref,
    w_up_ref,
    w_down_ref,
    projected_ref,
    branch_ref,
    gain_two_ref,
    w_query_ref,
    w_key_ref,
    w_value_ref,
    heads_ref,
    grad_attn_ref,
    grad_attn_far_ref,
    normed_one_ref,
    normed_one_far_ref,
    heads_far_ref,
    grad_hidden_ref,
    tokens_ref,
    gain_ref,
    kept_out,
    sent_out,
    came_out,
    down_kept,
    down_sent,
    down_came,
    down_last,
    out_mine,
    out_came,
    proj_mine,
    proj_came,
    input_out,
    mixed_out,
    branch_came,
    normed_late,
    cot_late,
    gain_out,
    normed,
    cot,
    normed_t,
    cot_t,
    units,
    gate_w,
    up_w,
    down_w,
    total,
    staged,
    core_in,
    y_in,
    w_proj,
    tok,
    heads,
    grad_attn,
    normed_one,
    projected,
    out_part,
    proj_part,
    out_x,
    proj_x,
    far_staged,
    far_heads,
    gains,
    gains_came,
    load_sem,
    piece_sem,
    weight_sem,
    unit_sem,
    store_sem,
    row_send,
    row_recv,
    core_send,
    core_recv,
    y_send,
    y_recv,
    x_send,
    x_recv,
    z_send,
    z_recv,
    end_send,
    end_recv,
    gain_send,
    gain_recv,
    late_send,
    late_recv,
    product,
):
    dp, tensor = lax.axis_index("dp"), lax.axis_index("tensor")
    core = tensor % 2
    x_low, z_low, z_high = dp % 2, (dp // 2) % 2, dp // 4
    twin_id = (dp, flip(tensor, 1))
    y_id = (dp, flip(tensor, 2))
    x_id = (flip(dp, 1), tensor)
    z_id = (flip(dp, 4), tensor)
    far_id = (flip(dp, 2), tensor)
    half, width = tok.shape
    row_count = 2 * half
    tiles = width // TILE
    run = half // 2
    y_bit = (tensor // 2) % 2

    def own_row(block, which):
        return pl.multiple_of(block * half + which * run, run)

    everything = slice(None)
    transposed = (((1,), (1,)), ((), ()))
    over = (((0,), (0,)), ((), ()))

    def remote(src, dst, send, recv, device):
        return pltpu.make_async_remote_copy(
            src_ref=src, dst_ref=dst, send_sem=send, recv_sem=recv,
            device_id=device, device_id_type=MESH,
        )

    def tile_of(j):
        return pl.ds(pl.multiple_of(j * TILE, TILE), TILE)

    away_block = tile_of(flip(dp, 2))
    home_block = tile_of(dp)
    near = [
        pl.ds(pl.multiple_of(b * 1024 + z_low * 512, 512), 512) for b in range(2)
    ]
    own_columns = [units.at[0, pl.ds(i * row_count, row_count)] for i in range(4)]
    loads = [
        pltpu.make_async_copy(normed_ref.at[:, away_block], own_columns[0], load_sem.at[0]),
        pltpu.make_async_copy(normed_ref.at[:, home_block], own_columns[1], load_sem.at[1]),
        pltpu.make_async_copy(cot_ref.at[:, away_block], own_columns[2], load_sem.at[2]),
        pltpu.make_async_copy(cot_ref.at[:, home_block], own_columns[3], load_sem.at[3]),
        pltpu.make_async_copy(w_query_ref, w_proj.at[:, pl.ds(0, 512)], load_sem.at[4]),
        pltpu.make_async_copy(w_key_ref, w_proj.at[:, pl.ds(512, 128)], load_sem.at[5]),
        pltpu.make_async_copy(w_value_ref, w_proj.at[:, pl.ds(640, 128)], load_sem.at[6]),
        pltpu.make_async_copy(
            tokens_ref.at[pl.ds(own_row(0, core), run)], tok.at[pl.ds(0, run)], load_sem.at[7]
        ),
        pltpu.make_async_copy(heads_ref, heads.at[0], load_sem.at[8]),
        pltpu.make_async_copy(
            grad_attn_ref.at[:, near[0]], grad_attn.at[0, :, pl.ds(0, 512)], load_sem.at[9]
        ),
        pltpu.make_async_copy(
            grad_attn_ref.at[:, near[1]], grad_attn.at[0, :, pl.ds(512, 512)], load_sem.at[10]
        ),
        pltpu.make_async_copy(
            normed_one_ref.at[:, near[0]], normed_one.at[0, :, pl.ds(0, 512)], load_sem.at[11]
        ),
        pltpu.make_async_copy(
            normed_one_ref.at[:, near[1]], normed_one.at[0, :, pl.ds(512, 512)], load_sem.at[12]
        ),
        pltpu.make_async_copy(projected_ref, projected.at[0], load_sem.at[13]),
        pltpu.make_async_copy(
            tokens_ref.at[pl.ds(own_row(1, core), run)], tok.at[pl.ds(run, run)], load_sem.at[14]
        ),
    ]

    late_normed = pl.ds(run, run)
    early_normed = pl.ds(0, run)
    late_cot = pl.ds(pl.multiple_of((1 - y_bit) * run, run), run)
    early_cot = pl.ds(pl.multiple_of(y_bit * run, run), run)

    def piece_load(i, slot):
        which, part = i // 6, i % 6
        source = (normed_others_ref, cot_others_ref)[which]
        late = (normed_late, cot_late)[which]
        into = staged.at[slot]
        if part in (0, 1, 3, 4):
            return [pltpu.make_async_copy(source.at[part], into, piece_sem.at[slot])]
        if part == 5:
            return [pltpu.make_async_copy(late.at[1], into, piece_sem.at[slot])]
        early_rows = (early_normed, early_cot)[which]
        late_rows = (late_normed, late_cot)[which]
        return [
            pltpu.make_async_copy(
                source.at[2, early_rows], into.at[early_rows], piece_sem.at[slot]
            ),
            pltpu.make_async_copy(
                late.at[0, late_rows], into.at[late_rows], piece_sem.at[2 + slot]
            ),
        ]

    def weight_loads(j, slot):
        return [
            pltpu.make_async_copy(
                w_gate_ref.at[:, tile_of(j)], gate_w.at[slot], weight_sem.at[slot, 0]
            ),
            pltpu.make_async_copy(
                w_up_ref.at[:, tile_of(j)], up_w.at[slot], weight_sem.at[slot, 1]
            ),
            pltpu.make_async_copy(
                w_down_ref.at[tile_of(j), :], down_w.at[slot], weight_sem.at[slot, 2]
            ),
        ]

    order = [0, 1, 3, 4, 6, 7, 9, 10, 2, 5, 8, 11]
    for i in range(2):
        for load in piece_load(order[i], i):
            load.start()
    loads[13].start()
    for load in loads[:4]:
        load.start()
    for load in weight_loads(0, 0):
        load.start()

    barrier = pltpu.get_barrier_semaphore()
    peers = []
    for m in range(1, 8):
        peer = dp
        for bit in (1, 2, 4):
            peer = flip(peer, bit) if m & bit else peer
        peers.append(peer)
    for device in [twin_id, y_id] + [(peer, tensor) for peer in peers]:
        pl.semaphore_signal(barrier, inc=1, device_id=device, device_id_type=MESH)
    pl.semaphore_wait(barrier, 9)
    late_copies = [
        remote(normed_others_ref.at[1, late_normed], normed_late.at[0, late_normed],
               late_send.at[0], late_recv.at[0], x_id),
        remote(cot_others_ref.at[2, early_cot], cot_late.at[0, early_cot],
               late_send.at[1], late_recv.at[1], y_id),
        remote(normed_others_ref.at[2, early_normed], normed_late.at[1, early_normed],
               late_send.at[2], late_recv.at[2], twin_id),
        remote(cot_others_ref.at[2, early_cot], cot_late.at[1, early_cot],
               late_send.at[3], late_recv.at[3], twin_id),
    ]
    for copy in late_copies:
        copy.start()

    loads[13].wait()

    def widen(r):
        window = pl.ds(pl.multiple_of(r * ROWS, ROWS), ROWS)
        for s in range(2):
            there = pl.ds(pl.multiple_of(s * half + r * ROWS, ROWS), ROWS)
            proj_part[0, s, window, :] = projected[0, there, :].astype(F32)

    loop(half // ROWS, widen)
    projected_copy = remote(proj_part.at[0], far_staged, end_send.at[2], end_recv.at[2], far_id)
    projected_copy.start()
    branch_copy = remote(branch_ref, branch_came, end_send.at[1], end_recv.at[1], y_id)

    late_twins = [
        remote(normed_late.at[0, late_normed], normed_late.at[1, late_normed],
               late_send.at[4], late_recv.at[4], twin_id),
        remote(cot_late.at[0, late_cot], cot_late.at[1, late_cot],
               late_send.at[5], late_recv.at[5], twin_id),
    ]
    def take_piece(place):
        i, slot = order[place], place % 2
        for load in piece_load(i, slot):
            load.wait()
        rows_to, turned_to = (normed, normed_t) if i < 6 else (cot, cot_t)
        base = {0: 0, 1: 1, 3: 2, 4: 3, 2: 4, 5: 5}[i % 6] * half

        def convert(r, slot=slot, rows_to=rows_to, base=base):
            window = pl.ds(pl.multiple_of(r * ROWS, ROWS), ROWS)
            rows_to[pl.ds(pl.multiple_of(base + r * ROWS, ROWS), ROWS), :] = staged[
                slot, window, :
            ].astype(BF16)

        loop(half // ROWS, convert)
        for part, block in enumerate((away_block, home_block)):
            turned_to[pl.ds(part * TILE, TILE), pl.ds(row_count + base, half)] = (
                staged[slot, :, block].T.astype(BF16)
            )
        if place == 5:
            for copy, later in zip(late_copies[:2], late_twins):
                copy.wait()
                later.start()
            branch_copy.start()
        if place == 6:
            for copy in late_copies[2:]:
                copy.wait()
        if place == 7:
            for copy in late_twins:
                copy.wait()
        if place + 2 < 12:
            for load in piece_load(order[place + 2], slot):
                load.start()
    for place in range(8):
        take_piece(place)
    for part in range(4):
        loads[part].wait()
        turned_to = (normed_t, cot_t)[part // 2]
        turned_to[pl.ds((part % 2) * TILE, TILE), pl.ds(0, row_count)] = (
            own_columns[part][...].astype(F32).T.astype(BF16)
        )

    def row_copy(j):
        window = (everything, everything, tile_of(j))
        return [
            remote(
                sent_out.at[window], came_out.at[window],
                row_send.at[0, j], row_recv.at[0, j], far_id,
            ),
            remote(
                down_sent.at[tile_of(j)], down_came.at[tile_of(j)],
                row_send.at[1, j], row_recv.at[1, j], far_id,
            ),
        ]

    def stores(j, slot):
        return [
            pltpu.make_async_copy(
                total.at[slot, pl.ds(0, 2), pl.ds(0, TILE)], sent_out.at[:, :, tile_of(j)],
                store_sem.at[slot, 0],
            ),
            pltpu.make_async_copy(
                total.at[slot, pl.ds(0, 2), pl.ds(TILE, TILE)], kept_out.at[:, :, tile_of(j)],
                store_sem.at[slot, 1],
            ),
            pltpu.make_async_copy(
                total.at[slot, 2, pl.ds(TILE, TILE)], down_kept.at[tile_of(j)],
                store_sem.at[slot, 3],
            ),
        ]

    def down_store(slot, into):
        return pltpu.make_async_copy(
            total.at[slot, 2, pl.ds(0, TILE)], into, store_sem.at[slot, 2]
        )

    def unit_loads(j):
        return [
            pltpu.make_async_copy(
                source.at[:, tile_of(j)], units.at[i, pl.ds(0, row_count)], unit_sem.at[i]
            )
            for i, source in enumerate((gg_ref, gu_ref, act_ref))
        ]

    def feed_forward_tile(j, first=False):
        slot = j % 2
        for load in weight_loads(j, slot):
            load.wait()

        if first:
            for load in weight_loads(1, 1):
                load.start()
        else:

            @pl.when(j + 1 < tiles)
            def _():
                for load in weight_loads(j + 1, 1 - slot):
                    load.start()

        for load in unit_loads(j):
            load.start()

        def block(m):
            rows = pl.ds(pl.multiple_of(m * 512, 512), 512)
            to = pl.ds(pl.multiple_of(row_count + m * 512, 512), 512)
            gate = jnp.dot(normed[rows, :], gate_w[slot], preferred_element_type=F32)
            up = jnp.dot(normed[rows, :], up_w[slot], preferred_element_type=F32)
            back = lax.dot_general(
                cot[rows, :], down_w[slot], transposed, preferred_element_type=F32
            )
            sigmoid = jax.nn.sigmoid(gate)
            swish = gate * sigmoid
            units[2, to, :] = (swish * up).astype(BF16)
            units[0, to, :] = (back * up * sigmoid * (1.0 + gate * (1.0 - sigmoid))).astype(BF16)
            units[1, to, :] = (back * swish).astype(BF16)

        if first:
            loop(2, block)
            for place in range(8, 12):
                take_piece(place)
            block(2)
        else:
            loop(normed.shape[0] // 512, block)
        for load in unit_loads(j):
            load.wait()

        total[slot, 0] = jnp.dot(normed_t[...], units[0], preferred_element_type=F32)
        total[slot, 1] = jnp.dot(normed_t[...], units[1], preferred_element_type=F32)
        turned = jnp.dot(cot_t[...], units[2], preferred_element_type=F32)
        for part in range(2):
            total[slot, 2, pl.ds(part * TILE, TILE)] = turned[part * TILE : (part + 1) * TILE].T
        for store in stores(j, slot):
            store.start()
        here = j < tiles - LAST

        @pl.when(here)
        def _():
            store = down_store(slot, down_sent.at[tile_of(j)])
            store.start()
            store.wait()
            row_copy(j)[1].start()

        @pl.when(jnp.logical_not(here))
        def _():
            store = down_store(slot, down_last.at[tile_of(j - (tiles - LAST))])
            store.start()
            store.wait()

        for store in stores(j, slot):
            store.wait()
        row_copy(j)[0].start()

    def x_copies(slot):
        return [
            remote(out_part.at[0, slot], out_x.at[slot], x_send.at[0, slot],
                   x_recv.at[0, slot], x_id),
            remote(proj_part.at[0, slot], proj_x.at[slot], x_send.at[1, slot],
                   x_recv.at[1, slot], x_id),
        ]

    def attention_parts():
        for load in far_loads + loads[8:13]:
            load.wait()
        projected_copy.wait()

        def convert(r):
            window = pl.ds(pl.multiple_of(r * ROWS, ROWS), ROWS)
            block, rest = r // (run // ROWS), r % (run // ROWS)
            for s in range(2):
                which = core if s == 0 else 1 - core
                here = pl.ds(
                    pl.multiple_of(block * half + which * run + rest * ROWS, ROWS), ROWS
                )
                grad_attn[1, here, :] = staged[0, window, pl.ds(s * 1024, 1024)].astype(BF16)
                normed_one[1, here, :] = staged[1, window, pl.ds(s * 1024, 1024)].astype(BF16)
                there = pl.ds(pl.multiple_of(s * half + r * ROWS, ROWS), ROWS)
                projected[1, there, :] = far_staged[s, window, :].astype(BF16)
                heads[1, there, :] = far_heads[window, pl.ds(s * 512, 512)].astype(BF16)

        loop(half // ROWS, convert)
        for side in range(2):
            x_at = 1 - x_low if side == 0 else x_low
            for slot in range(2):
                z_at = 1 - z_high if slot == 0 else z_high
                columns = pl.ds(pl.multiple_of(z_at * 512 + x_at * 256, 256), 256)
                out_part[side, slot] = lax.dot_general(
                    heads[0], grad_attn[0, :, columns], over, preferred_element_type=F32
                ) + lax.dot_general(
                    heads[1], grad_attn[1, :, columns], over, preferred_element_type=F32
                )
                proj_part[side, slot] = lax.dot_general(
                    normed_one[0, :, columns], projected[0], over, preferred_element_type=F32
                ) + lax.dot_general(
                    normed_one[1, :, columns], projected[1], over, preferred_element_type=F32
                )
                if side == 0:
                    for copy in x_copies(slot):
                        copy.start()

    def core_copy(j):
        window = (everything, tile_of(j))
        return remote(
            staged.at[0].at[window], core_in.at[window], core_send.at[j], core_recv.at[j], twin_id
        )

    def y_copy(j):
        window = (everything, tile_of(j))
        return remote(
            staged.at[1].at[window], y_in.at[window], y_send.at[j], y_recv.at[j], y_id
        )

    def attention_sums():
        for load in loads[4:8] + loads[14:]:
            load.wait()

        def produce(j):
            product[...] = lax.dot_general(
                projected[0], w_proj[tile_of(j), :], transposed, preferred_element_type=F32
            )
            for block in range(2):
                for slot, which in ((0, 1 - core), (1, core)):
                    staged[slot, pl.ds(block * run, run), tile_of(j)] = product[
                        pl.ds(own_row(block, which), run), :
                    ]
            core_copy(j).start()

        def forward(j):
            core_copy(j).wait_recv()
            staged[1, :, tile_of(j)] = staged[1, :, tile_of(j)] + core_in[:, tile_of(j)]
            y_copy(j).start()

        produce(0)

        def step(j):
            produce(j + 1)
            forward(j)

        loop(tiles - 1, step)
        forward(tiles - 1)
        loop(tiles, lambda j: core_copy(j).wait_send())

    feed_forward_tile(0, first=True)
    for load in loads[4:13] + loads[14:]:
        load.start()
    far_loads = (
        [
            pltpu.make_async_copy(
                grad_attn_far_ref.at[s], staged.at[0, :, pl.ds(s * 1024, 1024)], piece_sem.at[s]
            )
            for s in range(2)
        ]
        + [
            pltpu.make_async_copy(
                normed_one_far_ref.at[s], staged.at[1, :, pl.ds(s * 1024, 1024)],
                piece_sem.at[2 + s],
            )
            for s in range(2)
        ]
        + [
            pltpu.make_async_copy(heads_far_ref, far_heads, piece_sem.at[5]),
        ]
    )
    for load in far_loads:
        load.start()


    def step(j):
        feed_forward_tile(j + 1)

        @pl.when(j == 0)
        def _():
            attention_parts()
            attention_sums()

    loop(tiles - 1, step)
    hidden_load = pltpu.make_async_copy(grad_hidden_ref, core_in, load_sem.at[0])
    hidden_load.start()

    def z_copies():
        return [
            remote(out_part.at[1, 0], out_came, z_send.at[0], z_recv.at[0], z_id),
            remote(proj_part.at[1, 0], proj_came, z_send.at[1], z_recv.at[1], z_id),
        ]

    for slot in range(2):
        for copy in x_copies(slot):
            copy.wait_recv()
        out_part[1, slot] = out_part[1, slot] + out_x[slot]
        proj_part[1, slot] = proj_part[1, slot] + proj_x[slot]
        if slot == 0:
            for copy in z_copies():
                copy.start()
    part_stores = [
        pltpu.make_async_copy(out_part.at[1, 1], out_mine, load_sem.at[1]),
        pltpu.make_async_copy(proj_part.at[1, 1], proj_mine, load_sem.at[2]),
    ]
    for store in part_stores:
        store.start()

    gain = gain_ref[...]
    gains[pl.ds(0, 1), :] = jnp.zeros_like(gain)
    gains[pl.ds(1, 1), :] = gain_two_ref[...]
    hidden_load.wait()
    loop(tiles, lambda j: y_copy(j).wait_recv())

    def norm_rows(i):
        window = pl.ds(pl.multiple_of(i * ROWS, ROWS), ROWS)
        incoming = staged[1, window, :] + y_in[window, :]
        values = tok[window, :].astype(F32)
        scale = lax.rsqrt(jnp.mean(values * values, axis=-1, keepdims=True) + EPSILON)
        weighted = incoming * gain
        inner = jnp.mean(weighted * values, axis=-1, keepdims=True)
        back = scale * weighted - values * (scale * scale * scale) * inner
        staged[0, window, :] = core_in[window, :] + back
        gains[pl.ds(0, 1), :] = gains[pl.ds(0, 1), :] + jnp.sum(
            incoming * values * scale, axis=0, keepdims=True
        )

    loop(half // ROWS, norm_rows)

    def to_rows(slot, out, sems, first):
        copies, kept = [], []
        for block in range(2):
            local, here = pl.ds(block * run, run), pl.ds(own_row(block, core), run)
            copies.append(remote(
                staged.at[slot, local], out.at[here],
                end_send.at[sems + block], end_recv.at[sems + block], twin_id,
            ))
            kept.append(pltpu.make_async_copy(
                staged.at[slot, local], out.at[here], load_sem.at[first + block]
            ))
        for copy in copies + kept:
            copy.start()
        return copies, kept

    input_copies, input_stores = to_rows(0, input_out, 3, 3)

    gain_twin = remote(gains, gains_came, gain_send.at[7], gain_recv.at[7], twin_id)
    gain_twin.start()

    loop(tiles, lambda j: y_copy(j).wait_send())
    branch_copy.wait()
    branch_loads = [
        pltpu.make_async_copy(branch_ref, staged.at[1], load_sem.at[5]),
        pltpu.make_async_copy(branch_came, y_in, load_sem.at[6]),
    ]
    for load in branch_loads:
        load.start()
    gain_twin.wait()
    gains[...] = gains[...] + gains_came[...]

    def gain_copy(m):
        return remote(
            gains.at[:, tile_of(peers[m])], gain_out.at[m], gain_send.at[m], gain_recv.at[m],
            (peers[m], tensor),
        )

    for m in range(7):
        gain_copy(m).start()
    gain_out[7] = gains[:, tile_of(dp)]
    for load in branch_loads:
        load.wait()

    def mixed_rows(i):
        window = pl.ds(pl.multiple_of(i * ROWS, ROWS), ROWS)
        staged[1, window, :] = staged[1, window, :] + y_in[window, :]

    loop(half // ROWS, mixed_rows)
    mixed_copy = remote(staged.at[1], core_in, end_send.at[5], end_recv.at[5], twin_id)
    mixed_copy.start()

    def put_mixed(source, which, first):
        def narrow(i):
            window = pl.ds(pl.multiple_of(i * ROWS, ROWS), ROWS)
            tok[window, :] = source[window, :].astype(BF16)

        loop(half // ROWS, narrow)
        copies = [
            pltpu.make_async_copy(
                tok.at[pl.ds(block * run, run)], mixed_out.at[pl.ds(own_row(block, which), run)],
                load_sem.at[first + block],
            )
            for block in range(2)
        ]
        for copy in copies:
            copy.start()
        for copy in copies:
            copy.wait()

    put_mixed(staged.at[1], core, 7)
    mixed_copy.wait()
    put_mixed(core_in, 1 - core, 9)

    for copy in part_stores + input_stores + input_copies:
        copy.wait()
    for m in range(7):
        gain_copy(m).wait()
    for slot in range(2):
        for copy in x_copies(slot):
            copy.wait_send()
    for copy in z_copies():
        copy.wait()
    loop(tiles, lambda j: row_copy(j)[0].wait())
    loop(tiles - LAST, lambda j: row_copy(j)[1].wait())


def last(
    normed_others, cot_others, normed, cot, act, gg, gu, w_gate, w_up, w_down,
    projected, branch, gain_two, w_query, w_key, w_value, heads, grad_attn, grad_attn_far,
    normed_one, normed_one_far, heads_far, grad_hidden, tokens, gain,
):
    row_count, width = tokens.shape
    half = row_count // 2
    tiles = width // TILE
    hidden_units = w_gate.shape[1]
    hbm = pl.BlockSpec(memory_space=pl.ANY)
    vmem = pl.BlockSpec(memory_space=pltpu.VMEM)
    wide = jax.ShapeDtypeStruct((half, width), F32)
    rows_pair = jax.ShapeDtypeStruct((2, TILE, hidden_units), F32)
    columns = jax.ShapeDtypeStruct((hidden_units, TILE), F32)
    out_block = jax.ShapeDtypeStruct((512, TILE), F32)
    proj_block = jax.ShapeDtypeStruct((TILE, 768), F32)
    dma = pltpu.SemaphoreType.DMA
    return pl.pallas_call(
        last_kernel,
        out_shape=(
            rows_pair, rows_pair, rows_pair, columns, columns, columns,
            jax.ShapeDtypeStruct((LAST * TILE, TILE), F32), out_block, out_block, proj_block, proj_block,
            jax.ShapeDtypeStruct((row_count, width), F32),
            jax.ShapeDtypeStruct((row_count, width), BF16),
            wide,
            jax.ShapeDtypeStruct((2, half, width), F32),
            jax.ShapeDtypeStruct((2, half, width), F32),
            jax.ShapeDtypeStruct((8, 2, TILE), F32),
        ),
        in_specs=[hbm] * 12 + [vmem] + [hbm] * 11 + [vmem],
        out_specs=(hbm,) * 16 + (vmem,),
        scratch_shapes=[
            pltpu.VMEM((6 * half, width), BF16),
            pltpu.VMEM((6 * half, width), BF16),
            pltpu.VMEM((2 * TILE, row_count + 6 * half), BF16),
            pltpu.VMEM((2 * TILE, row_count + 6 * half), BF16),
            pltpu.VMEM((3, row_count + 6 * half, TILE), BF16),
            pltpu.VMEM((2, width, TILE), BF16),
            pltpu.VMEM((2, width, TILE), BF16),
            pltpu.VMEM((2, TILE, width), BF16),
            pltpu.VMEM((2, 3, 2 * TILE, TILE), F32),
            pltpu.VMEM((2, half, width), F32),
            pltpu.VMEM((half, width), F32),
            pltpu.VMEM((half, width), F32),
            pltpu.VMEM((width, 768), BF16),
            pltpu.VMEM((half, width), BF16),
            pltpu.VMEM((2, row_count, 512), BF16),
            pltpu.VMEM((2, row_count, 1024), BF16),
            pltpu.VMEM((2, row_count, 1024), BF16),
            pltpu.VMEM((2, row_count, 768), BF16),
            pltpu.VMEM((2, 2, 512, TILE), F32),
            pltpu.VMEM((2, 2, TILE, 768), F32),
            pltpu.VMEM((2, 512, TILE), F32),
            pltpu.VMEM((2, TILE, 768), F32),
            pltpu.VMEM((2, half, 768), F32),
            pltpu.VMEM((half, 1024), F32),
            pltpu.VMEM((2, width), F32),
            pltpu.VMEM((2, width), F32),
            dma((15,)), dma((6,)), dma((2, 3)), dma((3,)), dma((2, 4)),
            dma((2, tiles)), dma((2, tiles)),
            dma((tiles,)), dma((tiles,)), dma((tiles,)), dma((tiles,)),
            dma((2, 2)), dma((2, 2)), dma((2,)), dma((2,)), dma((7,)), dma((7,)), dma((8,)), dma((8,)),
            dma((6,)), dma((6,)), pltpu.VMEM((row_count, TILE), F32),
        ],
        compiler_params=pltpu.CompilerParams(
            collective_id=1, has_side_effects=True, vmem_limit_bytes=64 * 1024 * 1024
        ),
        name="weight_gradients",
    )(
        normed_others, cot_others, normed, cot, act, gg, gu, w_gate, w_up, w_down,
        projected, branch, gain_two, w_query, w_key, w_value, heads, grad_attn, grad_attn_far,
        normed_one, normed_one_far, heads_far, grad_hidden, tokens, gain.reshape(1, width),
    )


def finish_kernel(
    kept, came, down_kept, down_came, out_mine, out_came, proj_mine, proj_came, input_in,
    mixed_in, gains, w_gate, w_up, w_down, w_out, w_query, w_key, w_value, grad_input, mixed,
    gain_one, gain_two,
):
    w_gate[...] = kept[0] + came[0]
    w_up[...] = kept[1] + came[1]
    w_down[...] = down_kept[...] + down_came[...]
    w_out[...] = out_mine[...] + out_came[...]
    queries, keys = w_query.shape[1], w_key.shape[1]
    w_query[...] = proj_mine[:, :queries] + proj_came[:, :queries]
    w_key[...] = proj_mine[:, queries : queries + keys] + proj_came[:, queries : queries + keys]
    w_value[...] = proj_mine[:, queries + keys :] + proj_came[:, queries + keys :]
    grad_input[...] = input_in[...]
    mixed[...] = mixed_in[...]
    total = jnp.sum(gains[...], axis=0)
    gain_one[...] = total[0:1]
    gain_two[...] = total[1:2]


def finish(*parts):
    steps = 8
    kept, down, out, proj, whole, gains = (parts[i] for i in (0, 2, 4, 6, 8, 10))
    rows, units = kept.shape[1:]

    def block(array, lead=()):
        size = array[len(lead) :]
        shape = lead + (size[0] // steps,) + size[1:]
        return pl.BlockSpec(shape, lambda i: (0,) * len(lead) + (i,) + (0,) * (len(size) - 1))

    fixed = lambda shape: pl.BlockSpec(shape, lambda i: (0,) * len(shape))
    outs = [
        (rows, units), (rows, units), down.shape, out.shape,
        (proj.shape[0], 512), (proj.shape[0], 128), (proj.shape[0], 128), whole.shape,
    ]
    return pl.pallas_call(
        finish_kernel,
        grid=(steps,),
        out_shape=[jax.ShapeDtypeStruct(shape, F32) for shape in outs]
        + [
            jax.ShapeDtypeStruct(whole.shape, BF16),
            jax.ShapeDtypeStruct((1, gains.shape[2]), F32),
            jax.ShapeDtypeStruct((1, gains.shape[2]), F32),
        ],
        in_specs=[block(kept.shape, (2,))] * 2
        + [block(part.shape) for part in parts[2:10]]
        + [fixed(gains.shape)],
        out_specs=[block(shape) for shape in outs]
        + [block(whole.shape)] + [fixed((1, gains.shape[2]))] * 2,
        compiler_params=pltpu.CompilerParams(vmem_limit_bytes=64 * 1024 * 1024),
        cost_estimate=pl.CostEstimate(
            flops=2_000_000, bytes_accessed=34_000_000, transcendentals=0
        ),
        name="last_sums",
    )(*parts)


def body(
    tokens,
    segments,
    positions,
    attn_gain,
    w_query,
    key_weight,
    value_weight,
    w_out,
    mlp_gain,
    w_gate,
    w_up,
    w_down,
    cotangent,
):
    groups = lax.axis_size("dp")
    place = lax.axis_index("dp")
    core = lax.axis_index("tensor") % 2
    all_bits = [1 << i for i in range(groups.bit_length() - 1)]
    shared_bits = [bit for bit in (4, 1) if bit < groups]
    split_bits = [bit for bit in all_bits if bit not in shared_bits]

    def blocks(matrix, offsets):
        width = matrix.shape[1] // groups
        return [
            lax.dynamic_slice_in_dim(matrix, (place ^ offset) * width, width, 1)
            for offset in offsets
        ]

    def offsets_of(bits):
        found = [0]
        for bit in bits:
            found = found + [offset + bit for offset in found]
        return found

    def reduced(matrix_of, bits):
        sent = None
        for bit in bits:
            rest = bits[bits.index(bit) + 1 :]
            offsets = offsets_of(rest)
            if sent is None:
                away = matrix_of([offset ^ bit for offset in offsets])
                home = matrix_of(offsets)
            else:
                away = [sent[offset ^ bit] for offset in offsets]
                home = [sent[offset] for offset in offsets]
            came = swap(away, "dp", bit)
            sent = {offset: h + c for offset, h, c in zip(offsets, home, came)}
        return sent[0]

    row_count, width = tokens.shape
    query_width, kv_width = w_query.shape[1], key_weight.shape[1]
    half_dim = HEAD_SIZE // 2
    frequency = 500000.0 ** (-(jnp.arange(half_dim).astype(F32) * 2.0 / HEAD_SIZE))
    frequency = jnp.tile(frequency, 4)
    (
        normed_one,
        head_outputs,
        _,
        _,
        _,
        normed_one_far,
        heads_far,
        grad_hidden,
        grad_attn,
        projected,
        grad_attn_far,
        branch,
        normed_two,
        activation,
        grad_gate_in,
        grad_up_in,
        gain_two_half,
        cotangent_others,
        normed_others,
    ) = middle(
        w_query, key_weight, value_weight, w_out, tokens, cotangent,
        attn_gain, mlp_gain, w_gate, w_up, w_down, segments, positions, frequency,
    )
    (
        kept,
        _,
        came,
        down_kept,
        _,
        down_came,
        down_last,
        out_mine,
        out_came,
        proj_mine,
        proj_came,
        grad_input,
        mixed,
        _,
        _,
        _,
        gains,
    ) = last(
        normed_others, cotangent_others, normed_two, cotangent, activation, grad_gate_in,
        grad_up_in, w_gate, w_up, w_down, projected, branch, gain_two_half, w_query, key_weight,
        value_weight, head_outputs, grad_attn, grad_attn_far, normed_one, normed_one_far,
        heads_far, grad_hidden, tokens, attn_gain,
    )
    pairs = [(i, i ^ 2) for i in range(lax.axis_size("dp"))]
    last_came = lax.ppermute(down_last, "dp", pairs)
    (
        grad_w_gate,
        grad_w_up,
        grad_w_down,
        grad_w_out,
        grad_w_query,
        grad_w_key,
        grad_w_value,
        grad_input,
        mixed,
        grad_attn_gain,
        grad_mlp_gain,
    ) = finish(
        kept, came, down_kept, down_came, out_mine, out_came, proj_mine, proj_came, grad_input,
        mixed, gains,
    )
    done = grad_w_down.shape[0] - LAST * TILE
    grad_w_down = lax.dynamic_update_slice(grad_w_down, down_kept[done:] + last_came, (done, 0))
    grad_attn_gain, grad_mlp_gain = grad_attn_gain[0], grad_mlp_gain[0]
    return (
        mixed,
        grad_input,
        grad_attn_gain,
        grad_w_query,
        grad_w_key,
        grad_w_value,
        grad_w_out,
        grad_mlp_gain,
        grad_w_gate,
        grad_w_up,
        grad_w_down,
    )


def product(left_matrix, right_matrix):
    return jnp.dot(left_matrix, right_matrix, preferred_element_type=F32)


def over_rows(left_matrix, right_matrix):
    return lax.dot_general(
        left_matrix, right_matrix, (((0,), (0,)), ((), ())), preferred_element_type=F32
    )


def against(gradient, weight):
    return lax.dot_general(
        gradient, weight, (((1,), (1,)), ((), ())), preferred_element_type=F32
    )


def narrowed(value):
    return jnp.where(value == value, value, 0.0).astype(BF16)


def swap(value, axis, bit):
    size = lax.axis_size(axis)
    return lax.ppermute(value, axis, [(i, i ^ bit) for i in range(size)])


def half_of(value, which, dim=0):
    size = value.shape[dim] // 2
    return lax.dynamic_slice_in_dim(value, which * size, size, dim)


def joined(mine, other, which):
    first = jnp.where(which == 0, mine, other)
    second = jnp.where(which == 0, other, mine)
    return jnp.concatenate([first, second], axis=0)


def tensor_sum_half(partial, core):
    total = half_of(partial, core) + swap(half_of(partial, 1 - core), "tensor", 1)
    bit = 2
    while bit < lax.axis_size("tensor"):
        total = total + swap(total, "tensor", bit)
        bit *= 2
    return total


def tables(places):
    half_dim = HEAD_SIZE // 2
    frequency = 500000.0 ** (-(jnp.arange(half_dim).astype(F32) * 2.0 / HEAD_SIZE))
    angles = places.astype(F32)[..., None] * frequency
    cosine_lookup = jnp.cos(angles)
    sine_lookup = jnp.sin(angles)
    return (
        jnp.concatenate([cosine_lookup, cosine_lookup], -1),
        jnp.concatenate([sine_lookup, sine_lookup], -1),
    )


def apply_rotary(field, cosine_lookup, sine_lookup):
    half_dim = HEAD_SIZE // 2
    turned = jnp.concatenate([-field[..., half_dim:], field[..., :half_dim]], -1)
    return field * cosine_lookup + turned * sine_lookup


def unrotate(gradient, cosine_lookup, sine_lookup):
    half_dim = HEAD_SIZE // 2
    sined = gradient * sine_lookup
    return gradient * cosine_lookup + jnp.concatenate(
        [sined[..., half_dim:], -sined[..., :half_dim]], -1
    )


def allowed_pairs(segment):
    spots = jnp.arange(segment.shape[0])
    return (spots[:, None] >= spots[None, :]) & (segment[:, None] == segment[None, :])


def scores(query_rotated, key_rotated, segment):
    raw_scores = jnp.einsum(
        "qhgd,khd->hgqk", query_rotated, key_rotated, preferred_element_type=F32
    ) * HEAD_SIZE ** (-0.5)
    return jnp.where(allowed_pairs(segment), raw_scores, MASKED)


def attend_forward(query_rotated, key_rotated, value_seq, segment):
    masked = scores(query_rotated, key_rotated, segment)
    row_peak = jnp.max(masked, axis=-1, keepdims=True)
    log_total = row_peak + jnp.log(jnp.sum(jnp.exp(masked - row_peak), axis=-1, keepdims=True))
    attention_probs = jnp.exp(masked - log_total).astype(BF16)
    combined_heads = jnp.einsum(
        "ojus,sov->uojv", attention_probs, value_seq, preferred_element_type=F32
    )
    return (combined_heads, log_total)


def attend_backward(query_rotated, key_rotated, value_seq, segment, log_total, grad_heads):
    masked = scores(query_rotated, key_rotated, segment)
    attention_probs = jnp.exp(masked - log_total)
    grad_probs = jnp.einsum("qhgd,khd->hgqk", grad_heads, value_seq, preferred_element_type=F32)
    row_sum = jnp.sum(attention_probs * grad_probs, axis=-1, keepdims=True)
    grad_raw = jnp.where(
        allowed_pairs(segment), attention_probs * (grad_probs - row_sum), 0.0
    ).astype(BF16)
    factor = HEAD_SIZE ** (-0.5)
    grad_query_rot = (
        jnp.einsum("ojus,sov->uojv", grad_raw, key_rotated, preferred_element_type=F32) * factor
    )
    grad_key_rot = (
        jnp.einsum("hgqk,qhgd->khd", grad_raw, query_rotated, preferred_element_type=F32) * factor
    )
    grad_value_rot = jnp.einsum(
        "hgqk,qhgd->khd", attention_probs.astype(BF16), grad_heads, preferred_element_type=F32
    )
    return (grad_query_rot, grad_key_rot, grad_value_rot)


def per_sequence(step, *fields):
    results = [step(*[field[s] for field in fields]) for s in range(fields[0].shape[0])]
    return [jnp.stack(parts) for parts in zip(*results)]


def general_body(
    tokens,
    segments,
    positions,
    attn_gain,
    w_query,
    key_weight,
    value_weight,
    w_out,
    mlp_gain,
    w_gate,
    w_up,
    w_down,
    cotangent,
):
    groups = lax.axis_size("dp")
    place = lax.axis_index("dp")
    core = lax.axis_index("tensor") % 2
    all_bits = [1 << i for i in range(groups.bit_length() - 1)]
    shared_bits = [bit for bit in (4, 1) if bit < groups]
    split_bits = [bit for bit in all_bits if bit not in shared_bits]

    def gathered(half):
        parts = [half]
        for bit in shared_bits:
            parts = parts + [swap(part, "dp", bit) for part in parts]
        others = parts[1:]
        twins = [swap(part, "tensor", 1) for part in others]
        return jnp.concatenate([narrowed(part) for part in others + twins], axis=0)

    def blocks(matrix, offsets):
        width = matrix.shape[1] // groups
        return [
            lax.dynamic_slice_in_dim(matrix, (place ^ offset) * width, width, 1)
            for offset in offsets
        ]

    def offsets_of(bits):
        found = [0]
        for bit in bits:
            found = found + [offset + bit for offset in found]
        return found

    def reduced(matrix_of, bits):
        sent = None
        for bit in bits:
            rest = bits[bits.index(bit) + 1 :]
            offsets = offsets_of(rest)
            if sent is None:
                away = matrix_of([offset ^ bit for offset in offsets])
                home = matrix_of(offsets)
            else:
                away = [sent[offset ^ bit] for offset in offsets]
                home = [sent[offset] for offset in offsets]
            came = swap(away, "dp", bit)
            sent = {offset: h + c for offset, h, c in zip(offsets, home, came)}
        return sent[0]

    inputs = tokens.astype(F32)
    row_count, width = inputs.shape
    seq_count, seq_len = segments.shape
    query_heads = w_query.shape[1] // HEAD_SIZE
    kv_heads = key_weight.shape[1] // HEAD_SIZE
    group_size = query_heads // kv_heads
    query_width, kv_width = w_query.shape[1], key_weight.shape[1]

    cotangent_half = half_of(cotangent, core).astype(F32)
    cotangent_others = gathered(cotangent_half)

    scale_one = lax.rsqrt(jnp.mean(inputs * inputs, axis=-1, keepdims=True) + EPSILON)
    normed_one = (inputs * scale_one * attn_gain).astype(BF16)
    cosine_lookup, sine_lookup = tables(positions.reshape(row_count))
    cosine_lookup = cosine_lookup[:, None, :]
    sine_lookup = sine_lookup[:, None, :]
    query_projected = product(normed_one, w_query).reshape(row_count, query_heads, HEAD_SIZE)
    key_projected = product(normed_one, key_weight).reshape(row_count, kv_heads, HEAD_SIZE)
    query_rotated = (
        apply_rotary(query_projected, cosine_lookup, sine_lookup)
        .astype(BF16)
        .reshape(seq_count, seq_len, kv_heads, group_size, HEAD_SIZE)
    )
    key_rotated = (
        apply_rotary(key_projected, cosine_lookup, sine_lookup)
        .astype(BF16)
        .reshape(seq_count, seq_len, kv_heads, HEAD_SIZE)
    )
    value_projected = (
        product(normed_one, value_weight)
        .astype(BF16)
        .reshape(seq_count, seq_len, kv_heads, HEAD_SIZE)
    )
    combined_heads, log_totals = per_sequence(
        attend_forward, query_rotated, key_rotated, value_projected, segments
    )
    head_outputs = combined_heads.reshape(row_count, query_width).astype(BF16)

    inputs_half = half_of(inputs, core)
    hidden = inputs_half + tensor_sum_half(product(head_outputs, w_out), core)
    scale_two = lax.rsqrt(jnp.mean(hidden * hidden, axis=-1, keepdims=True) + EPSILON)
    normed_half = (hidden * scale_two * mlp_gain).astype(BF16)
    normed_sent = normed_half.astype(F32)
    normed_twin = narrowed(swap(normed_sent, "tensor", 1))
    normed_two = joined(normed_half, normed_twin, core)
    normed_others = gathered(normed_sent)

    def feed_forward(normed, incoming):
        gate_proj = product(normed, w_gate)
        up_proj = product(normed, w_up)
        grad_activation = against(incoming, w_down)
        sigmoid_gate = jax.nn.sigmoid(gate_proj)
        swish_gate = gate_proj * sigmoid_gate
        activation = (swish_gate * up_proj).astype(BF16)
        grad_gate_in = (
            grad_activation * up_proj * sigmoid_gate * (1.0 + gate_proj * (1.0 - sigmoid_gate))
        ).astype(BF16)
        grad_up_in = (grad_activation * swish_gate).astype(BF16)
        return activation, grad_gate_in, grad_up_in

    activation, grad_gate_in, grad_up_in = feed_forward(normed_two, cotangent)
    grad_normed_two = tensor_sum_half(
        against(grad_gate_in, w_gate) + against(grad_up_in, w_up), core
    )
    mixed_half = hidden + tensor_sum_half(product(activation, w_down), core)
    mixed = joined(mixed_half.astype(BF16), narrowed(swap(mixed_half, "tensor", 1)), core)

    weighted = grad_normed_two * mlp_gain
    inner_mean = jnp.mean(weighted * hidden, axis=-1, keepdims=True)
    back_two = scale_two * weighted - hidden * (scale_two * scale_two * scale_two) * inner_mean
    gain_two_half = jnp.sum(grad_normed_two * hidden * scale_two, axis=0)
    grad_hidden = cotangent_half + back_two
    attn_half = grad_hidden.astype(BF16)
    attn_twin = narrowed(swap(grad_hidden, "tensor", 1))
    grad_attn = joined(attn_half, attn_twin, core)

    grad_heads = (
        against(grad_attn, w_out)
        .astype(BF16)
        .reshape(seq_count, seq_len, kv_heads, group_size, HEAD_SIZE)
    )
    grad_query_rot, grad_key_rot, grad_value_rot = per_sequence(
        attend_backward,
        query_rotated,
        key_rotated,
        value_projected,
        segments,
        log_totals,
        grad_heads,
    )
    grad_query_in = (
        unrotate(
            grad_query_rot.reshape(row_count, query_heads, HEAD_SIZE), cosine_lookup, sine_lookup
        )
        .reshape(row_count, query_width)
        .astype(BF16)
    )
    grad_key_in = (
        unrotate(grad_key_rot.reshape(row_count, kv_heads, HEAD_SIZE), cosine_lookup, sine_lookup)
        .reshape(row_count, kv_width)
        .astype(BF16)
    )
    grad_value_in = grad_value_rot.reshape(row_count, kv_width).astype(BF16)
    partial_one = (
        against(grad_query_in, w_query)
        + against(grad_key_in, key_weight)
        + against(grad_value_in, value_weight)
    )
    grad_normed_one = tensor_sum_half(partial_one, core)
    scale_one = half_of(scale_one, core)
    weighted = grad_normed_one * attn_gain
    inner_mean = jnp.mean(weighted * inputs_half, axis=-1, keepdims=True)
    back_one = scale_one * weighted - inputs_half * (scale_one * scale_one * scale_one) * inner_mean
    gain_one_half = jnp.sum(grad_normed_one * inputs_half * scale_one, axis=0)
    input_half = grad_hidden + back_one
    grad_input = joined(input_half, swap(input_half, "tensor", 1), core)

    activation_o, grad_gate_o, grad_up_o = feed_forward(normed_others, cotangent_others)

    def rows_of(left, left_others, right, right_others):
        def term(offsets):
            ours = blocks(left, offsets)
            theirs = blocks(left_others, offsets)
            return [
                over_rows(a, right) + over_rows(b, right_others) for a, b in zip(ours, theirs)
            ]

        return reduced(term, split_bits)

    def columns_of(left, left_others, right, right_others):
        def term(offsets):
            ours = blocks(right, offsets)
            theirs = blocks(right_others, offsets)
            return [
                over_rows(left, a) + over_rows(left_others, b) for a, b in zip(ours, theirs)
            ]

        return reduced(term, split_bits)

    grad_w_down = columns_of(activation, activation_o, cotangent, cotangent_others)
    grad_w_gate = rows_of(normed_two, normed_others, grad_gate_in, grad_gate_o)
    grad_w_up = rows_of(normed_two, normed_others, grad_up_in, grad_up_o)

    grad_w_out = reduced(
        lambda offsets: [over_rows(head_outputs, b) for b in blocks(grad_attn, offsets)], all_bits
    )
    projected = jnp.concatenate([grad_query_in, grad_key_in, grad_value_in], axis=1)
    grad_w_proj = reduced(
        lambda offsets: [over_rows(b, projected) for b in blocks(normed_one, offsets)], all_bits
    )
    grad_w_query = grad_w_proj[:, :query_width]
    grad_w_key = grad_w_proj[:, query_width : query_width + kv_width]
    grad_w_value = grad_w_proj[:, query_width + kv_width :]

    gains = jnp.stack([gain_one_half, gain_two_half])
    gains = gains + swap(gains, "tensor", 1)
    gains = reduced(lambda offsets: blocks(gains, offsets), all_bits)
    grad_attn_gain, grad_mlp_gain = gains[0], gains[1]
    return (
        mixed,
        grad_input,
        grad_attn_gain,
        grad_w_query,
        grad_w_key,
        grad_w_value,
        grad_w_out,
        grad_mlp_gain,
        grad_w_gate,
        grad_w_up,
        grad_w_down,
    )


def solution(mesh):
    placed = (
        P("dp", None),
        P("dp", None),
        P("dp", None),
        P(),
        P(None, "tensor"),
        P(None, "tensor"),
        P(None, "tensor"),
        P("tensor", None),
        P(),
        P(None, "tensor"),
        P(None, "tensor"),
        P("tensor", None),
        P("dp", None),
    )
    fits = mesh.shape["dp"] == 8 and mesh.shape["tensor"] == 4
    return jax.shard_map(
        body if fits else general_body,
        mesh=mesh,
        in_specs=placed,
        out_specs=(
            P("dp", None),
            P("dp", None),
            P("dp"),
            P("dp", "tensor"),
            P("dp", "tensor"),
            P("dp", "tensor"),
            P("tensor", "dp"),
            P("dp"),
            P("dp", "tensor"),
            P("dp", "tensor"),
            P("tensor", "dp"),
        ),
        check_vma=False,
    )
```

```python
import functools

import jax
import jax.numpy as jnp
from jax import lax
from jax.experimental import pallas as pl
from jax.experimental.pallas import tpu as pltpu
from jax.sharding import PartitionSpec as P

HEAD_SIZE = 64
EPSILON = 1e-05
MASKED = -1e30
F32 = jnp.float32
BF16 = jnp.bfloat16


MESH = pl.DeviceIdType.MESH
CHUNKS = 4
TILE = 256
ROWS = 16


def flip(index, bit):
    return index + bit * (1 - 2 * ((index // bit) % 2))


def loop(count, step):
    lax.fori_loop(0, count, lambda i, carry: (step(i), carry)[1], 0)


def middle_kernel(
    w_query_ref,
    w_key_ref,
    w_value_ref,
    w_out_ref,
    tokens_ref,
    cot_ref,
    gain_one_ref,
    gain_ref,
    w_gate_ref,
    w_up_ref,
    w_down_ref,
    segment_ref,
    position_ref,
    frequency_ref,
    normed_one_out,
    heads_out,
    query_ref,
    keys_ref,
    values_ref,
    normed_one_far,
    heads_far,
    grad_hidden_out,
    grad_attn_out,
    projected_out,
    grad_attn_far,
    branch_out,
    normed_out,
    activation_out,
    grad_gate_out,
    grad_up_out,
    gain_out,
    cot_others,
    normed_others,
    gate_w,
    up_w,
    down_w,
    cot,
    cot_half,
    normed,
    normed_sent,
    normed_twin,
    act,
    gg,
    gu,
    away,
    mine,
    core_in,
    y_in,
    product,
    log_total_ref,
    segment_column,
    cosine_ref,
    sine_ref,
    local_sem,
    core_send,
    core_recv,
    y_send,
    y_recv,
    cot_send,
    cot_recv,
    n_send,
    n_recv,
    twin_send,
    twin_recv,
    hidden_send,
    hidden_recv,
    far_send,
    far_recv,
    free_sem,
):
    dp, tensor = lax.axis_index("dp"), lax.axis_index("tensor")
    core, y_bit = tensor % 2, (tensor // 2) % 2
    z_low = (dp // 2) % 2
    twin_id = (dp, flip(tensor, 1))
    y_id = (dp, flip(tensor, 2))
    x_id = (flip(dp, 1), tensor)
    z_id = (flip(dp, 4), tensor)
    far_id = (flip(dp, 2), tensor)
    half, width = cot_half.shape
    run = half // 2
    row_count = 2 * half
    hidden_units = gate_w.shape[1]
    query_width = w_query_ref.shape[1]
    tiles = width // TILE
    chunk = half // CHUNKS
    transposed = (((1,), (1,)), ((), ()))
    everything = slice(None)
    heads = gg.at[:, pl.ds(0, query_width)]
    tok = gu
    hidden = core_in.at[0]

    def own_row(block, which):
        return pl.multiple_of(block * half + which * run, run)

    def own_chunk(k, which):
        return own_row(k // 2, which) + (k % 2) * chunk

    def remote(src, dst, send, recv, device):
        return pltpu.make_async_remote_copy(
            src_ref=src, dst_ref=dst, send_sem=send, recv_sem=recv,
            device_id=device, device_id_type=MESH,
        )

    loads = {
        "tok": pltpu.make_async_copy(tokens_ref, tok, local_sem.at[0]),
        "query": pltpu.make_async_copy(
            w_query_ref, gate_w.at[:, pl.ds(0, query_width)], local_sem.at[1]
        ),
        "key": pltpu.make_async_copy(
            w_key_ref, gate_w.at[:, pl.ds(query_width, 128)], local_sem.at[2]
        ),
        "value": pltpu.make_async_copy(
            w_value_ref, gate_w.at[:, pl.ds(query_width + 128, 128)], local_sem.at[3]
        ),
        "w_out": pltpu.make_async_copy(w_out_ref, cot, local_sem.at[4]),
        "up": pltpu.make_async_copy(w_up_ref, up_w, local_sem.at[5]),
        "down": pltpu.make_async_copy(w_down_ref, down_w, local_sem.at[6]),
        "gate": pltpu.make_async_copy(w_gate_ref, gate_w, local_sem.at[7]),
        "cot": pltpu.make_async_copy(cot_ref, cot, local_sem.at[8]),
        "cot_0": pltpu.make_async_copy(
            cot_ref.at[pl.ds(own_row(0, core), run)], act.at[pl.ds(0, run)], local_sem.at[10]
        ),
        "cot_1": pltpu.make_async_copy(
            cot_ref.at[pl.ds(own_row(1, core), run)], act.at[pl.ds(run, run)], local_sem.at[11]
        ),
    }
    for name in ("cot_0", "cot_1", "tok", "query", "key", "value", "w_out", "up", "down"):
        loads[name].start()

    barrier = pltpu.get_barrier_semaphore()
    for device in (twin_id, y_id, x_id, z_id, far_id):
        pl.semaphore_signal(barrier, inc=1, device_id=device, device_id_type=MESH)
    loads["cot_0"].wait()
    loads["cot_1"].wait()

    def widen(i):
        window = pl.ds(pl.multiple_of(i * ROWS, ROWS), ROWS)
        cot_half[window, :] = act[window, :].astype(F32)

    loop(half // ROWS, widen)
    pl.semaphore_wait(barrier, 5)

    def rows(k):
        return pl.ds(pl.multiple_of(k * chunk, chunk), chunk)

    def from_x(source, slots, k, send, recv):
        return remote(source.at[rows(k)], slots.at[0, rows(k)], send.at[0, k], recv.at[0, k], x_id)

    def from_z(source, slots, k, send, recv):
        return remote(source.at[rows(k)], slots.at[1, rows(k)], send.at[1, k], recv.at[1, k], z_id)

    def from_zx(slots, k, send, recv):
        return remote(
            slots.at[1, rows(k)], slots.at[2, rows(k)], send.at[2, k], recv.at[2, k], x_id
        )

    def to_twin(slots, which, slot):
        return remote(
            slots.at[slot], slots.at[3 + slot],
            twin_send.at[which, slot], twin_recv.at[which, slot], twin_id,
        )

    half_chunk = pl.ds(pl.multiple_of((2 + y_bit) * chunk, chunk), chunk)

    def last_z():
        return remote(
            normed_sent.at[half_chunk], normed_others.at[1, half_chunk],
            n_send.at[1, 2], n_recv.at[1, 2], z_id,
        )

    def last_y():
        return remote(
            normed_others.at[1, half_chunk], normed_others.at[1, half_chunk],
            n_send.at[1, 3], n_recv.at[1, 3], y_id,
        )

    def half_to_twin(slots, which, part, window):
        return remote(
            slots.at[1, window], slots.at[4, window],
            twin_send.at[which, 1 + part], twin_recv.at[which, 1 + part], twin_id,
        )

    first_run, last_run = pl.ds(0, run), pl.ds(run, run)
    other_quarter = pl.ds(pl.multiple_of((1 - y_bit) * run, run), run)
    quarter = pl.ds(pl.multiple_of(y_bit * run, run), run)

    def quarter_z():
        return remote(
            cot_half.at[quarter], cot_others.at[1, quarter],
            cot_send.at[1, 0], cot_recv.at[1, 0], z_id,
        )

    def quarter_zx():
        return remote(
            cot_others.at[1, quarter], cot_others.at[2, quarter],
            cot_send.at[2, 0], cot_recv.at[2, 0], x_id,
        )

    def quarter_y():
        return remote(
            cot_others.at[1, quarter], cot_others.at[1, quarter],
            cot_send.at[1, 1], cot_recv.at[1, 1], y_id,
        )

    quarter_z().start()
    for k in range(CHUNKS):
        from_x(cot_half, cot_others, k, cot_send, cot_recv).start()

    def far_columns(b):
        return pl.ds(pl.multiple_of(b * 1024 + (1 - z_low) * 512, 512), 512)

    gain_one = gain_one_ref[...]
    segments = segment_ref[...].astype(F32)
    segment_column[...] = jnp.broadcast_to(segments, (8, row_count)).T
    loads["tok"].wait()

    def first_norm(block):
        def step(i):
            window = pl.ds(pl.multiple_of(block * half + i * ROWS, ROWS), ROWS)
            values = tok[window, :].astype(F32)
            scale = lax.rsqrt(jnp.mean(values * values, axis=-1, keepdims=True) + EPSILON)
            normed[window, :] = (values * scale * gain_one).astype(BF16)

        loop(half // ROWS, step)

    normed_one_store = pltpu.make_async_copy(normed, normed_one_out, local_sem.at[9])

    def stage_far(block):
        def step(i):
            window = pl.ds(pl.multiple_of(block * run + i * ROWS, ROWS), ROWS)
            here = pl.ds(pl.multiple_of(own_row(block, core) + i * ROWS, ROWS), ROWS)
            for b in range(2):
                core_in[2, window, pl.ds(b * 512, 512)] = normed[here, far_columns(b)].astype(F32)

        loop(run // ROWS, step)

    normed_one_copy = remote(
        core_in.at[2, :, pl.ds(0, 1024)], normed_one_far.at[0],
        far_send.at[0], far_recv.at[0], far_id,
    )

    places = jnp.broadcast_to(position_ref[...].astype(F32), (8, row_count)).T
    angles = places[:, 0:1] * frequency_ref[...]
    cosine_ref[...] = jnp.cos(angles)
    signs = lax.broadcasted_iota(jnp.int32, (row_count, 128), 1) % 64 < 32
    sines = jnp.sin(angles)
    sine_ref[...] = jnp.where(signs, sines, -sines)

    lane = lax.broadcasted_iota(jnp.int32, (TILE, 128), 1)
    factor = HEAD_SIZE ** (-0.5)

    def turn(value):
        return jnp.where(lane % 64 < 32, pltpu.roll(value, 96, 1), pltpu.roll(value, 32, 1))

    def rotate_tile(value, window):
        return value * cosine_ref[window, :] - turn(value) * sine_ref[window, :]

    def unrotate_tile(value, window):
        return value * cosine_ref[window, :] + turn(value) * sine_ref[window, :]

    def project_in(block):
        window = pl.ds(block * TILE, TILE)

        def query_tile(j):
            projection = jnp.dot(
                normed[window, :],
                gate_w[:, pl.ds(pl.multiple_of(j * TILE, TILE), TILE)],
                preferred_element_type=F32,
            )
            for part in range(2):
                act[window, pl.ds(pl.multiple_of(j * TILE + part * 128, 128), 128)] = rotate_tile(
                    projection[:, part * 128 : (part + 1) * 128], window
                ).astype(BF16)

        loop(query_width // TILE, query_tile)
        projection = jnp.dot(
            normed[window, :], gate_w[:, pl.ds(query_width, TILE)], preferred_element_type=F32
        )
        for base, value in (
            (1024, rotate_tile(projection[:, :128], window)),
            (1536, projection[:, 128:]),
        ):
            other = pltpu.roll(value, 64, 1)
            halves_of = (
                jnp.where(lane < 64, value, 0.0),
                jnp.where(lane >= 64, other, 0.0),
                jnp.where(lane < 64, other, 0.0),
                jnp.where(lane >= 64, value, 0.0),
            )
            for i, padded in enumerate(halves_of):
                act[window, pl.ds(base + i * 128, 128)] = padded.astype(BF16)

    def allowed_of(block):
        keys_seen = (block + 1) * TILE
        window = pl.ds(block * TILE, TILE)
        key_place = lax.broadcasted_iota(jnp.int32, (keys_seen, TILE), 0)
        query_place = lax.broadcasted_iota(jnp.int32, (keys_seen, TILE), 1) + block * TILE
        return (key_place <= query_place) & (
            segment_column[pl.ds(0, keys_seen), pl.ds(0, 1)] == segments[:, block * TILE : (block + 1) * TILE]
        )

    def attend(block, p):
        kv = p // 2
        column = pl.multiple_of(p * 128, 128)
        window = pl.ds(block * TILE, TILE)
        seen = pl.ds(0, (block + 1) * TILE)
        queries = act[window, pl.ds(column, 128)]
        allowed = allowed_of(block)
        result = jnp.zeros((TILE, 128), F32)
        for side in range(2):
            padded = pl.multiple_of((kv * 2 + side) * 128, 128)
            keys = act[seen, pl.ds(pl.multiple_of(1024 + padded, 128), 128)]
            vals = act[seen, pl.ds(pl.multiple_of(1536 + padded, 128), 128)]
            raw = jnp.where(
                allowed,
                lax.dot_general(keys, queries, transposed, preferred_element_type=F32) * factor,
                MASKED,
            )
            peak = jnp.max(raw, axis=0, keepdims=True)
            lifted = jnp.exp(raw - peak)
            summed = jnp.sum(lifted, axis=0, keepdims=True)
            log_total_ref[pl.ds(2 * p + side, 1), window] = peak + jnp.log(summed)
            result = result + lax.dot_general(
                (lifted * (1.0 / summed)).astype(BF16), vals, (((0,), (0,)), ((), ())),
                preferred_element_type=F32,
            )
        heads[window, pl.ds(column, 128)] = result.astype(BF16)

    def core_copy(which, window, k):
        return remote(
            away.at[window], core_in.at[min(which, 1)].at[window],
            core_send.at[which, k], core_recv.at[which, k], twin_id,
        )

    def y_copy(which, window, k):
        return remote(
            mine.at[which].at[window], y_in.at[which].at[window],
            y_send.at[which, k], y_recv.at[which, k], y_id,
        )

    def split_tile(which, block, columns, value):
        product[...] = value
        local = pl.ds(block * run, run)
        away[local, columns] = product[pl.ds(pl.multiple_of((1 - core) * run, run), run), :]
        mine[which, local, columns] = product[pl.ds(pl.multiple_of(core * run, run), run), :]

    row_windows = [(rows(k), everything) for k in range(CHUNKS)]

    def tile_of(j):
        return pl.ds(pl.multiple_of(j * TILE, TILE), TILE)

    first_norm(0)
    first_norm(1)
    normed_one_store.start()
    stage_far(0)
    stage_far(1)
    normed_one_copy.start()
    for name in ("query", "key", "value", "w_out"):
        loads[name].wait()
    for block in range(2):
        project_in(block)
        loop(query_width // 128, functools.partial(attend, block))

        def project(j, block=block):
            split_tile(0, block, tile_of(j), jnp.dot(
                heads[pl.ds(block * TILE, TILE), :], cot[:, tile_of(j)],
                preferred_element_type=F32,
            ))

        loop(tiles, project)
        for k in (2 * block, 2 * block + 1):
            core_copy(0, row_windows[k], k).start()
        for k in (2 * block, 2 * block + 1):
            core_copy(0, row_windows[k], k).wait_recv()

            def add(i, k=k):
                window = pl.ds(pl.multiple_of(k * chunk + i * ROWS, ROWS), ROWS)
                mine[0, window, :] = mine[0, window, :] + core_in[0, window, :]

            loop(chunk // ROWS, add)
            y_copy(0, row_windows[k], k).start()
    normed_one_store.wait()
    loads["gate"].start()
    loads["cot"].start()
    keeps = [
        pltpu.make_async_copy(act.at[:, pl.ds(0, 512)], query_ref, local_sem.at[0]),
        pltpu.make_async_copy(act.at[:, pl.ds(1024, 512)], keys_ref, local_sem.at[1]),
        pltpu.make_async_copy(act.at[:, pl.ds(1536, 512)], values_ref, local_sem.at[2]),
        pltpu.make_async_copy(heads, heads_out, local_sem.at[3]),
    ]
    for keep in keeps:
        keep.start()

    def stage_heads(i):
        window = pl.ds(pl.multiple_of(i * ROWS, ROWS), ROWS)
        for b in range(2):
            here = pl.ds(pl.multiple_of(b * half + i * ROWS, ROWS), ROWS)
            core_in[2, window, pl.ds(1024 + b * 512, 512)] = heads[here, :].astype(F32)

    loop(half // ROWS, stage_heads)
    heads_copy = remote(
        core_in.at[2, :, pl.ds(1024, 1024)], heads_far, far_send.at[1], far_recv.at[1], far_id
    )
    heads_copy.start()
    for keep in keeps:
        keep.wait()

    for name in ("cot", "up", "down"):
        loads[name].wait()

    def activation_grad(j):
        gg[:, tile_of(j)] = lax.dot_general(
            cot[...], down_w[tile_of(j), :], transposed, preferred_element_type=F32
        ).astype(BF16)

    loop(hidden_units // TILE, activation_grad)
    loads["gate"].wait()
    gain = gain_ref[...]

    def twin_copy(k):
        return remote(
            normed_sent.at[rows(k)], normed_twin.at[rows(k)],
            n_send.at[3, k], n_recv.at[3, k], twin_id,
        )

    def block_window(block, j):
        return (pl.ds(block * run, run), tile_of(j))

    for block in range(2):
        chunks = (2 * block, 2 * block + 1)
        for k in chunks:
            y_copy(0, row_windows[k], k).wait_recv()

            def normalize_rows(i, k=k):
                window = pl.ds(pl.multiple_of(k * chunk + i * ROWS, ROWS), ROWS)
                here = pl.ds(pl.multiple_of(own_chunk(k, core) + i * ROWS, ROWS), ROWS)
                values = tok[here, :].astype(F32) + (mine[0, window, :] + y_in[0, window, :])
                scale = lax.rsqrt(jnp.mean(values * values, axis=-1, keepdims=True) + EPSILON)
                rounded = (values * scale * gain).astype(BF16)
                hidden[window, :] = values
                normed[here, :] = rounded
                normed_sent[window, :] = rounded.astype(F32)

            loop(chunk // ROWS, normalize_rows)
            twin_copy(k).start()
            if block == 0:
                from_z(normed_sent, normed_others, k, n_send, n_recv).start()
            elif k == 3:
                last_z().start()
            from_x(normed_sent, normed_others, k, n_send, n_recv).start()
        for k in chunks:
            twin_copy(k).wait_recv()

            def take(i, k=k):
                here = pl.ds(pl.multiple_of(own_chunk(k, 1 - core) + i * ROWS, ROWS), ROWS)
                normed[here, :] = normed_twin[
                    pl.ds(pl.multiple_of(k * chunk + i * ROWS, ROWS), ROWS), :
                ].astype(BF16)

            loop(chunk // ROWS, take)
        window = pl.ds(block * TILE, TILE)

        def units(j, window=window):
            columns = tile_of(j)
            gate = jnp.dot(normed[window, :], gate_w[:, columns], preferred_element_type=F32)
            up = jnp.dot(normed[window, :], up_w[:, columns], preferred_element_type=F32)
            back = gg[window, columns].astype(F32)
            sigmoid = jax.nn.sigmoid(gate)
            swish = gate * sigmoid
            act[window, columns] = (swish * up).astype(BF16)
            gg[window, columns] = (
                back * up * sigmoid * (1.0 + gate * (1.0 - sigmoid))
            ).astype(BF16)
            gu[window, columns] = (back * swish).astype(BF16)

        if block == 0:
            loop(hidden_units // TILE, units)
            for k in range(CHUNKS):
                core_copy(0, row_windows[k], k).wait_send()
        else:
            loop(hidden_units // TILE, units)

        def produce(j, block=block, window=window):
            split_tile(1, block, tile_of(j), lax.dot_general(
                gg[window, :], gate_w[tile_of(j), :], transposed, preferred_element_type=F32
            ) + lax.dot_general(
                gu[window, :], up_w[tile_of(j), :], transposed, preferred_element_type=F32
            ))
            core_copy(1, block_window(block, j), block * tiles + j).start()

        def forward(j, block=block):
            where = block_window(block, j)
            core_copy(1, where, block * tiles + j).wait_recv()
            mine[(1,) + where] = mine[(1,) + where] + core_in[(1,) + where]
            y_copy(1, where, block * tiles + j).start()

        def step(j, produce=produce, forward=forward):
            produce(j + 1)
            forward(j)

        produce(0)
        loop(tiles - 1, step)
        forward(tiles - 1)
    stores = [
        pltpu.make_async_copy(normed, normed_out, local_sem.at[7]),
        pltpu.make_async_copy(act, activation_out, local_sem.at[8]),
        pltpu.make_async_copy(gg, grad_gate_out, local_sem.at[9]),
        pltpu.make_async_copy(gu, grad_up_out, local_sem.at[10]),
    ]
    for store in stores:
        store.start()
    pl.semaphore_signal(free_sem, inc=1, device_id=twin_id, device_id_type=MESH)
    quarter_z().wait()
    quarter_zx().start()
    half_to_twin(cot_others, 0, 0, quarter).start()

    for block in range(2):
        loop(tiles, lambda j: core_copy(1, block_window(block, j), block * tiles + j).wait_send())
    for k in range(CHUNKS):
        y_copy(0, row_windows[k], k).wait_send()

    def branch_produce(j):
        for block in range(2):
            split_tile(0, block, tile_of(j), jnp.dot(
                act[pl.ds(block * TILE, TILE), :], down_w[:, tile_of(j)],
                preferred_element_type=F32,
            ))
        core_copy(2, (everything, tile_of(j)), j).start()

    def branch_add(j):
        core_copy(2, (everything, tile_of(j)), j).wait_recv()
        mine[0, :, tile_of(j)] = mine[0, :, tile_of(j)] + core_in[1, :, tile_of(j)]

    def branch_step(j):
        branch_produce(j + 1)
        branch_add(j)

    pl.semaphore_wait(free_sem, 1)
    branch_produce(0)
    loop(tiles - 1, branch_step)
    branch_add(tiles - 1)
    first_y = (1 - y_bit).astype(F32)

    def add_hidden(i):
        window = pl.ds(pl.multiple_of(i * ROWS, ROWS), ROWS)
        mine[0, window, :] = mine[0, window, :] + hidden[window, :] * first_y

    loop(half // ROWS, add_hidden)
    branch_store = pltpu.make_async_copy(mine.at[0], branch_out, local_sem.at[12])
    branch_store.start()

    for store in stores:
        store.wait()
    operands = [
        pltpu.make_async_copy(query_ref, act.at[:, pl.ds(0, 512)], local_sem.at[0]),
        pltpu.make_async_copy(keys_ref, act.at[:, pl.ds(1024, 512)], local_sem.at[1]),
        pltpu.make_async_copy(values_ref, act.at[:, pl.ds(1536, 512)], local_sem.at[2]),
        pltpu.make_async_copy(w_out_ref, gate_w.at[pl.ds(0, 512)], local_sem.at[3]),
    ]
    for operand in operands:
        operand.start()
    for operand in operands:
        operand.wait()

    gain_out[...] = jnp.zeros_like(gain_out)
    sums = y_in.at[0]
    sums[:, pl.ds(0, 1024)] = jnp.zeros((TILE, 1024), F32)

    def hidden_copy(k):
        return remote(
            core_in.at[0, rows(k)], normed_twin.at[rows(k)],
            hidden_send.at[k], hidden_recv.at[k], twin_id,
        )

    def hidden_far(block, b):
        local = pl.ds(block * run, run)
        return remote(
            core_in.at[0, local, far_columns(b)],
            grad_attn_far.at[0, local, pl.ds(b * 512, 512)],
            far_send.at[3 + 2 * block + b], far_recv.at[3 + 2 * block + b], far_id,
        )

    def gather_into(offset, kv, value):
        for part in range(value.shape[0] // TILE):
            columns = pl.ds(pl.multiple_of(offset + kv * 256 + part * 128, 128), 128)
            sums[:, columns] = sums[:, columns] + value[part * TILE : (part + 1) * TILE]

    def put(block, column, value):
        gu[pl.ds(block * TILE, TILE), pl.ds(column, 128)] = value.astype(BF16)

    def attend_back(block, p):
        kv = p // 2
        column = pl.multiple_of(p * 128, 128)
        keys_seen = (block + 1) * TILE
        window = pl.ds(block * TILE, TILE)
        seen = pl.ds(0, keys_seen)
        queries = act[window, pl.ds(column, 128)]
        upstream = act[window, pl.ds(pl.multiple_of(512 + column, 128), 128)]
        allowed = allowed_of(block)
        query_grad = jnp.zeros((TILE, 128), F32)
        for side in range(2):
            padded = pl.multiple_of((kv * 2 + side) * 128, 128)
            keys = act[seen, pl.ds(pl.multiple_of(1024 + padded, 128), 128)]
            vals = act[seen, pl.ds(pl.multiple_of(1536 + padded, 128), 128)]
            raw = lax.dot_general(keys, queries, transposed, preferred_element_type=F32) * factor
            log_total = log_total_ref[pl.ds(2 * p + side, 1), window]
            probs = jnp.exp(jnp.where(allowed, raw - log_total, MASKED))
            grad_probs = lax.dot_general(
                vals, upstream, transposed, preferred_element_type=F32
            )
            row_sum = jnp.sum(probs * grad_probs, axis=0, keepdims=True)
            grad_raw = (probs * (grad_probs - row_sum)).astype(BF16)
            query_grad = query_grad + lax.dot_general(
                grad_raw, keys, (((0,), (0,)), ((), ())), preferred_element_type=F32
            )
            own = (lax.broadcasted_iota(jnp.int32, (keys_seen, 128), 1) // 64) == side
            gather_into(0, kv, jnp.where(
                own, jnp.dot(grad_raw, queries, preferred_element_type=F32), 0.0
            ))
            gather_into(512, kv, jnp.where(
                own, jnp.dot(probs.astype(BF16), upstream, preferred_element_type=F32), 0.0
            ))
        put(block, column, unrotate_tile(query_grad * factor, window))

    for block in range(2):
        loop(tiles, lambda j: y_copy(1, block_window(block, j), block * tiles + j).wait_recv())
        if block == 1:
            quarter_y().start()
        for k in (2 * block, 2 * block + 1):

            def norm_rows(i, k=k):
                window = pl.ds(pl.multiple_of(k * chunk + i * ROWS, ROWS), ROWS)
                here = pl.ds(pl.multiple_of(own_chunk(k, core) + i * ROWS, ROWS), ROWS)
                incoming = mine[1, window, :] + y_in[1, window, :]
                values = hidden[window, :]
                scale = lax.rsqrt(jnp.mean(values * values, axis=-1, keepdims=True) + EPSILON)
                weighted = incoming * gain
                inner = jnp.mean(weighted * values, axis=-1, keepdims=True)
                back = scale * weighted - values * (scale * scale * scale) * inner
                total = cot[here, :].astype(F32) + back
                core_in[0, window, :] = total
                normed[here, :] = total.astype(BF16)
                gain_out[...] = gain_out[...] + jnp.sum(
                    incoming * values * scale, axis=0, keepdims=True
                )

            loop(chunk // ROWS, norm_rows)
            hidden_copy(k).start()
        for b in range(2):
            hidden_far(block, b).start()
        for k in (2 * block, 2 * block + 1):
            hidden_copy(k).wait_recv()

            def take_hidden(i, k=k):
                here = pl.ds(pl.multiple_of(own_chunk(k, 1 - core) + i * ROWS, ROWS), ROWS)
                normed[here, :] = normed_twin[
                    pl.ds(pl.multiple_of(k * chunk + i * ROWS, ROWS), ROWS), :
                ].astype(BF16)

            loop(chunk // ROWS, take_hidden)

        def head_tile(j, block=block):
            window = pl.ds(block * TILE, TILE)
            act[window, pl.ds(pl.multiple_of(512 + j * TILE, TILE), TILE)] = lax.dot_general(
                normed[window, :], gate_w[tile_of(j), :], transposed, preferred_element_type=F32
            ).astype(BF16)

        loop(512 // TILE, head_tile)
        loop(query_width // 128, functools.partial(attend_back, block))
        if block == 0:
            for k in (0, 1):
                from_z(normed_sent, normed_others, k, n_send, n_recv).wait_recv()
                from_zx(normed_others, k, n_send, n_recv).start()
            half_to_twin(normed_others, 1, 0, first_run).start()
            for k in range(CHUNKS):
                from_x(cot_half, cot_others, k, cot_send, cot_recv).wait()
            to_twin(cot_others, 0, 0).start()

    grad_stores = [
        pltpu.make_async_copy(core_in.at[0], grad_hidden_out, local_sem.at[4]),
        pltpu.make_async_copy(normed, grad_attn_out, local_sem.at[5]),
    ]
    for store in grad_stores:
        store.start()

    def both(offset, block):
        def folded(kv):
            value = sums[:, pl.ds(offset + kv * 256 + block * 128, 128)]
            return value + pltpu.roll(value, 64, 1)

        return jnp.where(lane < 64, folded(0), folded(1))

    for block in range(2):
        window = pl.ds(block * TILE, TILE)
        put(block, 512, unrotate_tile(both(0, block) * factor, window))
        put(block, 640, both(512, block))
    projected_store = pltpu.make_async_copy(
        gu.at[:, pl.ds(0, 768)], projected_out, local_sem.at[6]
    )
    projected_store.start()

    last_z().wait()
    last_y().start()
    normed_one_copy.wait()
    normed_one_twin = remote(
        normed_one_far.at[0], normed_one_far.at[1], far_send.at[2], far_recv.at[2], twin_id
    )
    normed_one_twin.start()
    heads_copy.wait()
    for block in range(2):
        for b in range(2):
            hidden_far(block, b).wait()
    hidden_far_twin = remote(
        grad_attn_far.at[0], grad_attn_far.at[1], far_send.at[7], far_recv.at[7], twin_id
    )
    hidden_far_twin.start()
    for k in range(CHUNKS):
        from_x(normed_sent, normed_others, k, n_send, n_recv).wait_recv()
    to_twin(normed_others, 1, 0).start()
    quarter_y().wait()
    half_to_twin(cot_others, 0, 1, other_quarter).start()
    last_y().wait()
    half_to_twin(normed_others, 1, 1, last_run).start()

    for store in grad_stores + [projected_store, branch_store]:
        store.wait()
    for copy in (hidden_far_twin, normed_one_twin, quarter_zx()):
        copy.wait()
    for k in range(CHUNKS):
        hidden_copy(k).wait_send()
        twin_copy(k).wait_send()
        from_x(normed_sent, normed_others, k, n_send, n_recv).wait_send()
    for k in (0, 1):
        from_z(normed_sent, normed_others, k, n_send, n_recv).wait_send()
        from_zx(normed_others, k, n_send, n_recv).wait()
    for block in range(2):
        loop(tiles, lambda j: y_copy(1, block_window(block, j), block * tiles + j).wait_send())
    loop(tiles, lambda j: core_copy(2, (everything, tile_of(j)), j).wait_send())
    to_twin(cot_others, 0, 0).wait()
    to_twin(normed_others, 1, 0).wait()
    half_to_twin(cot_others, 0, 0, quarter).wait()
    half_to_twin(cot_others, 0, 1, other_quarter).wait()
    half_to_twin(normed_others, 1, 0, first_run).wait()
    half_to_twin(normed_others, 1, 1, last_run).wait()


def middle(
    w_query, w_key, w_value, w_out, tokens, cotangent, gain_one, gain,
    w_gate, w_up, w_down, segment, position, frequency,
):
    row_count, width = tokens.shape
    half = row_count // 2
    hidden_units = w_gate.shape[1]
    tiles = width // TILE
    hbm = pl.BlockSpec(memory_space=pl.ANY)
    vmem = pl.BlockSpec(memory_space=pltpu.VMEM)
    wide = jax.ShapeDtypeStruct((half, width), F32)
    units = jax.ShapeDtypeStruct((row_count, hidden_units), BF16)
    square = jax.ShapeDtypeStruct((row_count, 512), BF16)
    dma = pltpu.SemaphoreType.DMA
    return pl.pallas_call(
        middle_kernel,
        out_shape=(
            jax.ShapeDtypeStruct((row_count, width), BF16),
            square, square, square, square,
            jax.ShapeDtypeStruct((2, half, width // 2), F32),
            jax.ShapeDtypeStruct((half, width // 2), F32),
            wide,
            jax.ShapeDtypeStruct((row_count, width), BF16),
            jax.ShapeDtypeStruct((row_count, 768), BF16),
            jax.ShapeDtypeStruct((2, half, width // 2), F32),
            wide,
            jax.ShapeDtypeStruct((row_count, width), BF16),
            units, units, units,
            jax.ShapeDtypeStruct((1, width), F32),
            jax.ShapeDtypeStruct((5, half, width), F32),
            jax.ShapeDtypeStruct((5, half, width), F32),
        ),
        in_specs=[hbm] * 6 + [vmem] * 2 + [hbm] * 3 + [vmem] * 3,
        out_specs=(hbm,) * 16 + (vmem,) + (hbm,) * 2,
        scratch_shapes=[
            pltpu.VMEM(w_gate.shape, BF16),
            pltpu.VMEM(w_up.shape, BF16),
            pltpu.VMEM(w_down.shape, BF16),
            pltpu.VMEM((row_count, width), BF16),
            pltpu.VMEM((half, width), F32),
            pltpu.VMEM((row_count, width), BF16),
            pltpu.VMEM((half, width), F32),
            pltpu.VMEM((half, width), F32),
            pltpu.VMEM((row_count, hidden_units), BF16),
            pltpu.VMEM((row_count, hidden_units), BF16),
            pltpu.VMEM((row_count, hidden_units), BF16),
            pltpu.VMEM((half, width), F32),
            pltpu.VMEM((2, half, width), F32),
            pltpu.VMEM((3, half, width), F32),
            pltpu.VMEM((2, half, width), F32),
            pltpu.VMEM((half, TILE), F32),
            pltpu.VMEM((8, row_count), F32),
            pltpu.VMEM((row_count, 8), F32),
            pltpu.VMEM((row_count, 128), F32),
            pltpu.VMEM((row_count, 128), F32),
            dma((13,)),
            dma((3, 2 * tiles)), dma((3, 2 * tiles)), dma((2, 2 * tiles)), dma((2, 2 * tiles)),
            dma((3, CHUNKS)), dma((3, CHUNKS)),
            dma((4, CHUNKS)), dma((4, CHUNKS)),
            dma((2, 3)), dma((2, 3)),
            dma((CHUNKS,)), dma((CHUNKS,)),
            dma((8,)), dma((8,)),
            pltpu.SemaphoreType.REGULAR,
        ],
        compiler_params=pltpu.CompilerParams(
            collective_id=0, has_side_effects=True, vmem_limit_bytes=64 * 1024 * 1024
        ),
        name="feed_forward",
    )(
        w_query, w_key, w_value, w_out, tokens, cotangent,
        gain_one.reshape(1, width), gain.reshape(1, width), w_gate, w_up, w_down,
        segment.reshape(1, row_count), position.reshape(1, row_count), frequency.reshape(1, 128),
    )


LAST = 2


def last_kernel(
    normed_others_ref,
    cot_others_ref,
    normed_ref,
    cot_ref,
    act_ref,
    gg_ref,
    gu_ref,
    w_gate_ref,
    w_up_ref,
    w_down_ref,
    projected_ref,
    branch_ref,
    gain_two_ref,
    w_query_ref,
    w_key_ref,
    w_value_ref,
    heads_ref,
    grad_attn_ref,
    grad_attn_far_ref,
    normed_one_ref,
    normed_one_far_ref,
    heads_far_ref,
    grad_hidden_ref,
    tokens_ref,
    gain_ref,
    kept_out,
    sent_out,
    came_out,
    down_kept,
    down_sent,
    down_came,
    down_last,
    out_mine,
    out_came,
    proj_mine,
    proj_came,
    input_out,
    mixed_out,
    branch_came,
    normed_late,
    cot_late,
    gain_out,
    normed,
    cot,
    normed_t,
    cot_t,
    units,
    gate_w,
    up_w,
    down_w,
    total,
    staged,
    core_in,
    y_in,
    w_proj,
    tok,
    heads,
    grad_attn,
    normed_one,
    projected,
    out_part,
    proj_part,
    out_x,
    proj_x,
    far_staged,
    far_heads,
    gains,
    gains_came,
    load_sem,
    piece_sem,
    weight_sem,
    unit_sem,
    store_sem,
    row_send,
    row_recv,
    core_send,
    core_recv,
    y_send,
    y_recv,
    x_send,
    x_recv,
    z_send,
    z_recv,
    end_send,
    end_recv,
    gain_send,
    gain_recv,
    late_send,
    late_recv,
    product,
):
    dp, tensor = lax.axis_index("dp"), lax.axis_index("tensor")
    core = tensor % 2
    x_low, z_low, z_high = dp % 2, (dp // 2) % 2, dp // 4
    twin_id = (dp, flip(tensor, 1))
    y_id = (dp, flip(tensor, 2))
    x_id = (flip(dp, 1), tensor)
    z_id = (flip(dp, 4), tensor)
    far_id = (flip(dp, 2), tensor)
    half, width = tok.shape
    row_count = 2 * half
    tiles = width // TILE
    run = half // 2
    y_bit = (tensor // 2) % 2

    def own_row(block, which):
        return pl.multiple_of(block * half + which * run, run)

    everything = slice(None)
    transposed = (((1,), (1,)), ((), ()))
    over = (((0,), (0,)), ((), ()))

    def remote(src, dst, send, recv, device):
        return pltpu.make_async_remote_copy(
            src_ref=src, dst_ref=dst, send_sem=send, recv_sem=recv,
            device_id=device, device_id_type=MESH,
        )

    def tile_of(j):
        return pl.ds(pl.multiple_of(j * TILE, TILE), TILE)

    away_block = tile_of(flip(dp, 2))
    home_block = tile_of(dp)
    near = [
        pl.ds(pl.multiple_of(b * 1024 + z_low * 512, 512), 512) for b in range(2)
    ]
    own_columns = [units.at[0, pl.ds(i * row_count, row_count)] for i in range(4)]
    loads = [
        pltpu.make_async_copy(normed_ref.at[:, away_block], own_columns[0], load_sem.at[0]),
        pltpu.make_async_copy(normed_ref.at[:, home_block], own_columns[1], load_sem.at[1]),
        pltpu.make_async_copy(cot_ref.at[:, away_block], own_columns[2], load_sem.at[2]),
        pltpu.make_async_copy(cot_ref.at[:, home_block], own_columns[3], load_sem.at[3]),
        pltpu.make_async_copy(w_query_ref, w_proj.at[:, pl.ds(0, 512)], load_sem.at[4]),
        pltpu.make_async_copy(w_key_ref, w_proj.at[:, pl.ds(512, 128)], load_sem.at[5]),
        pltpu.make_async_copy(w_value_ref, w_proj.at[:, pl.ds(640, 128)], load_sem.at[6]),
        pltpu.make_async_copy(
            tokens_ref.at[pl.ds(own_row(0, core), run)], tok.at[pl.ds(0, run)], load_sem.at[7]
        ),
        pltpu.make_async_copy(heads_ref, heads.at[0], load_sem.at[8]),
        pltpu.make_async_copy(
            grad_attn_ref.at[:, near[0]], grad_attn.at[0, :, pl.ds(0, 512)], load_sem.at[9]
        ),
        pltpu.make_async_copy(
            grad_attn_ref.at[:, near[1]], grad_attn.at[0, :, pl.ds(512, 512)], load_sem.at[10]
        ),
        pltpu.make_async_copy(
            normed_one_ref.at[:, near[0]], normed_one.at[0, :, pl.ds(0, 512)], load_sem.at[11]
        ),
        pltpu.make_async_copy(
            normed_one_ref.at[:, near[1]], normed_one.at[0, :, pl.ds(512, 512)], load_sem.at[12]
        ),
        pltpu.make_async_copy(projected_ref, projected.at[0], load_sem.at[13]),
        pltpu.make_async_copy(
            tokens_ref.at[pl.ds(own_row(1, core), run)], tok.at[pl.ds(run, run)], load_sem.at[14]
        ),
    ]

    late_normed = pl.ds(run, run)
    early_normed = pl.ds(0, run)
    late_cot = pl.ds(pl.multiple_of((1 - y_bit) * run, run), run)
    early_cot = pl.ds(pl.multiple_of(y_bit * run, run), run)

    def piece_load(i, slot):
        which, part = i // 6, i % 6
        source = (normed_others_ref, cot_others_ref)[which]
        late = (normed_late, cot_late)[which]
        into = staged.at[slot]
        if part in (0, 1, 3, 4):
            return [pltpu.make_async_copy(source.at[part], into, piece_sem.at[slot])]
        if part == 5:
            return [pltpu.make_async_copy(late.at[1], into, piece_sem.at[slot])]
        early_rows = (early_normed, early_cot)[which]
        late_rows = (late_normed, late_cot)[which]
        return [
            pltpu.make_async_copy(
                source.at[2, early_rows], into.at[early_rows], piece_sem.at[slot]
            ),
            pltpu.make_async_copy(
                late.at[0, late_rows], into.at[late_rows], piece_sem.at[2 + slot]
            ),
        ]

    def weight_loads(j, slot):
        return [
            pltpu.make_async_copy(
                w_gate_ref.at[:, tile_of(j)], gate_w.at[slot], weight_sem.at[slot, 0]
            ),
            pltpu.make_async_copy(
                w_up_ref.at[:, tile_of(j)], up_w.at[slot], weight_sem.at[slot, 1]
            ),
            pltpu.make_async_copy(
                w_down_ref.at[tile_of(j), :], down_w.at[slot], weight_sem.at[slot, 2]
            ),
        ]

    order = [0, 1, 3, 4, 6, 7, 9, 10, 2, 8, 5, 11]
    for i in range(2):
        for load in piece_load(order[i], i):
            load.start()
    loads[13].start()
    for load in loads[:4]:
        load.start()
    for load in weight_loads(0, 0):
        load.start()

    barrier = pltpu.get_barrier_semaphore()
    peers = []
    for m in range(1, 8):
        peer = dp
        for bit in (1, 2, 4):
            peer = flip(peer, bit) if m & bit else peer
        peers.append(peer)
    for device in [twin_id, y_id] + [(peer, tensor) for peer in peers]:
        pl.semaphore_signal(barrier, inc=1, device_id=device, device_id_type=MESH)
    pl.semaphore_wait(barrier, 9)
    late_copies = [
        remote(normed_others_ref.at[1, late_normed], normed_late.at[0, late_normed],
               late_send.at[0], late_recv.at[0], x_id),
        remote(cot_others_ref.at[2, early_cot], cot_late.at[0, early_cot],
               late_send.at[1], late_recv.at[1], y_id),
        remote(normed_others_ref.at[2, early_normed], normed_late.at[1, early_normed],
               late_send.at[2], late_recv.at[2], twin_id),
        remote(cot_others_ref.at[2, early_cot], cot_late.at[1, early_cot],
               late_send.at[3], late_recv.at[3], twin_id),
    ]
    for copy in late_copies:
        copy.start()

    loads[13].wait()

    def widen(r):
        window = pl.ds(pl.multiple_of(r * ROWS, ROWS), ROWS)
        for s in range(2):
            there = pl.ds(pl.multiple_of(s * half + r * ROWS, ROWS), ROWS)
            proj_part[0, s, window, :] = projected[0, there, :].astype(F32)

    loop(half // ROWS, widen)
    projected_copy = remote(proj_part.at[0], far_staged, end_send.at[2], end_recv.at[2], far_id)
    projected_copy.start()
    branch_copy = remote(branch_ref, branch_came, end_send.at[1], end_recv.at[1], y_id)

    late_twins = [
        remote(normed_late.at[0, late_normed], normed_late.at[1, late_normed],
               late_send.at[4], late_recv.at[4], twin_id),
        remote(cot_late.at[0, late_cot], cot_late.at[1, late_cot],
               late_send.at[5], late_recv.at[5], twin_id),
    ]
    def take_piece(place):
        i, slot = order[place], place % 2
        for load in piece_load(i, slot):
            load.wait()
        rows_to, turned_to = (normed, normed_t) if i < 6 else (cot, cot_t)
        base = {0: 0, 1: 1, 3: 2, 4: 3, 2: 4, 5: 5}[i % 6] * half

        def convert(r, slot=slot, rows_to=rows_to, base=base):
            window = pl.ds(pl.multiple_of(r * ROWS, ROWS), ROWS)
            rows_to[pl.ds(pl.multiple_of(base + r * ROWS, ROWS), ROWS), :] = staged[
                slot, window, :
            ].astype(BF16)

        loop(half // ROWS, convert)
        for part, block in enumerate((away_block, home_block)):
            turned_to[pl.ds(part * TILE, TILE), pl.ds(row_count + base, half)] = (
                staged[slot, :, block].T.astype(BF16)
            )
        if place == 8:
            for copy in late_copies[2:] + late_twins:
                copy.wait()
        if place + 2 < 8 or 8 <= place < 10:
            for load in piece_load(order[place + 2], slot):
                load.start()
    for place in range(8):
        take_piece(place)
    for part in range(4):
        loads[part].wait()
        turned_to = (normed_t, cot_t)[part // 2]
        turned_to[pl.ds((part % 2) * TILE, TILE), pl.ds(0, row_count)] = (
            own_columns[part][...].astype(F32).T.astype(BF16)
        )

    def row_copy(j):
        window = (everything, everything, tile_of(j))
        return [
            remote(
                sent_out.at[window], came_out.at[window],
                row_send.at[0, j], row_recv.at[0, j], far_id,
            ),
            remote(
                down_sent.at[tile_of(j)], down_came.at[tile_of(j)],
                row_send.at[1, j], row_recv.at[1, j], far_id,
            ),
        ]

    def stores(j, slot):
        return [
            pltpu.make_async_copy(
                total.at[slot, pl.ds(0, 2), pl.ds(0, TILE)], sent_out.at[:, :, tile_of(j)],
                store_sem.at[slot, 0],
            ),
            pltpu.make_async_copy(
                total.at[slot, pl.ds(0, 2), pl.ds(TILE, TILE)], kept_out.at[:, :, tile_of(j)],
                store_sem.at[slot, 1],
            ),
            pltpu.make_async_copy(
                total.at[slot, 2, pl.ds(TILE, TILE)], down_kept.at[tile_of(j)],
                store_sem.at[slot, 3],
            ),
        ]

    def down_store(slot, into):
        return pltpu.make_async_copy(
            total.at[slot, 2, pl.ds(0, TILE)], into, store_sem.at[slot, 2]
        )

    def unit_loads(j):
        return [
            pltpu.make_async_copy(
                source.at[:, tile_of(j)], units.at[i, pl.ds(0, row_count)], unit_sem.at[i]
            )
            for i, source in enumerate((gg_ref, gu_ref, act_ref))
        ]

    def feed_forward_tile(j, first=False):
        slot = j % 2
        for load in weight_loads(j, slot):
            load.wait()

        if first:
            for load in weight_loads(1, 1):
                load.start()
        else:

            @pl.when(j + 1 < tiles)
            def _():
                for load in weight_loads(j + 1, 1 - slot):
                    load.start()

        for load in unit_loads(j):
            load.start()

        def block(m):
            rows = pl.ds(pl.multiple_of(m * 512, 512), 512)
            to = pl.ds(pl.multiple_of(row_count + m * 512, 512), 512)
            gate = jnp.dot(normed[rows, :], gate_w[slot], preferred_element_type=F32)
            up = jnp.dot(normed[rows, :], up_w[slot], preferred_element_type=F32)
            back = lax.dot_general(
                cot[rows, :], down_w[slot], transposed, preferred_element_type=F32
            )
            sigmoid = jax.nn.sigmoid(gate)
            swish = gate * sigmoid
            units[2, to, :] = (swish * up).astype(BF16)
            units[0, to, :] = (back * up * sigmoid * (1.0 + gate * (1.0 - sigmoid))).astype(BF16)
            units[1, to, :] = (back * swish).astype(BF16)

        if first:
            loop(2, block)
            for copy, later in zip(late_copies[:2], late_twins):
                copy.wait()
                later.start()
            branch_copy.start()
            for place in (8, 9):
                for load in piece_load(order[place], place % 2):
                    load.start()
            for place in range(8, 12):
                take_piece(place)
            block(2)
        else:
            loop(normed.shape[0] // 512, block)
        for load in unit_loads(j):
            load.wait()

        total[slot, 0] = jnp.dot(normed_t[...], units[0], preferred_element_type=F32)
        total[slot, 1] = jnp.dot(normed_t[...], units[1], preferred_element_type=F32)
        turned = jnp.dot(cot_t[...], units[2], preferred_element_type=F32)
        for part in range(2):
            total[slot, 2, pl.ds(part * TILE, TILE)] = turned[part * TILE : (part + 1) * TILE].T
        for store in stores(j, slot):
            store.start()
        here = j < tiles - LAST

        @pl.when(here)
        def _():
            store = down_store(slot, down_sent.at[tile_of(j)])
            store.start()
            store.wait()
            row_copy(j)[1].start()

        @pl.when(jnp.logical_not(here))
        def _():
            store = down_store(slot, down_last.at[tile_of(j - (tiles - LAST))])
            store.start()
            store.wait()

        for store in stores(j, slot):
            store.wait()
        row_copy(j)[0].start()

    def x_copies(slot):
        return [
            remote(out_part.at[0, slot], out_x.at[slot], x_send.at[0, slot],
                   x_recv.at[0, slot], x_id),
            remote(proj_part.at[0, slot], proj_x.at[slot], x_send.at[1, slot],
                   x_recv.at[1, slot], x_id),
        ]

    def attention_parts():
        for load in far_loads + loads[8:13]:
            load.wait()
        projected_copy.wait()

        def convert(r):
            window = pl.ds(pl.multiple_of(r * ROWS, ROWS), ROWS)
            block, rest = r // (run // ROWS), r % (run // ROWS)
            for s in range(2):
                which = core if s == 0 else 1 - core
                here = pl.ds(
                    pl.multiple_of(block * half + which * run + rest * ROWS, ROWS), ROWS
                )
                grad_attn[1, here, :] = staged[0, window, pl.ds(s * 1024, 1024)].astype(BF16)
                normed_one[1, here, :] = staged[1, window, pl.ds(s * 1024, 1024)].astype(BF16)
                there = pl.ds(pl.multiple_of(s * half + r * ROWS, ROWS), ROWS)
                projected[1, there, :] = far_staged[s, window, :].astype(BF16)
                heads[1, there, :] = far_heads[window, pl.ds(s * 512, 512)].astype(BF16)

        loop(half // ROWS, convert)
        for side in range(2):
            x_at = 1 - x_low if side == 0 else x_low
            for slot in range(2):
                z_at = 1 - z_high if slot == 0 else z_high
                columns = pl.ds(pl.multiple_of(z_at * 512 + x_at * 256, 256), 256)
                out_part[side, slot] = lax.dot_general(
                    heads[0], grad_attn[0, :, columns], over, preferred_element_type=F32
                ) + lax.dot_general(
                    heads[1], grad_attn[1, :, columns], over, preferred_element_type=F32
                )
                proj_part[side, slot] = lax.dot_general(
                    normed_one[0, :, columns], projected[0], over, preferred_element_type=F32
                ) + lax.dot_general(
                    normed_one[1, :, columns], projected[1], over, preferred_element_type=F32
                )
                if side == 0:
                    for copy in x_copies(slot):
                        copy.start()

    def core_copy(j):
        window = (everything, tile_of(j))
        return remote(
            staged.at[0].at[window], core_in.at[window], core_send.at[j], core_recv.at[j], twin_id
        )

    def y_copy(j):
        window = (everything, tile_of(j))
        return remote(
            staged.at[1].at[window], y_in.at[window], y_send.at[j], y_recv.at[j], y_id
        )

    def attention_sums():
        for load in loads[4:8] + loads[14:]:
            load.wait()

        def produce(j):
            product[...] = lax.dot_general(
                projected[0], w_proj[tile_of(j), :], transposed, preferred_element_type=F32
            )
            for block in range(2):
                for slot, which in ((0, 1 - core), (1, core)):
                    staged[slot, pl.ds(block * run, run), tile_of(j)] = product[
                        pl.ds(own_row(block, which), run), :
                    ]
            core_copy(j).start()

        def forward(j):
            core_copy(j).wait_recv()
            staged[1, :, tile_of(j)] = staged[1, :, tile_of(j)] + core_in[:, tile_of(j)]
            y_copy(j).start()

        produce(0)

        def step(j):
            produce(j + 1)
            forward(j)

        loop(tiles - 1, step)
        forward(tiles - 1)
        loop(tiles, lambda j: core_copy(j).wait_send())

    feed_forward_tile(0, first=True)
    for load in loads[4:13] + loads[14:]:
        load.start()
    far_loads = (
        [
            pltpu.make_async_copy(
                grad_attn_far_ref.at[s], staged.at[0, :, pl.ds(s * 1024, 1024)], piece_sem.at[s]
            )
            for s in range(2)
        ]
        + [
            pltpu.make_async_copy(
                normed_one_far_ref.at[s], staged.at[1, :, pl.ds(s * 1024, 1024)],
                piece_sem.at[2 + s],
            )
            for s in range(2)
        ]
        + [
            pltpu.make_async_copy(heads_far_ref, far_heads, piece_sem.at[5]),
        ]
    )
    for load in far_loads:
        load.start()


    def step(j):
        feed_forward_tile(j + 1)

        @pl.when(j == 0)
        def _():
            attention_parts()
            attention_sums()

    loop(tiles - 1, step)
    hidden_load = pltpu.make_async_copy(grad_hidden_ref, core_in, load_sem.at[0])
    hidden_load.start()

    def z_copies():
        return [
            remote(out_part.at[1, 0], out_came, z_send.at[0], z_recv.at[0], z_id),
            remote(proj_part.at[1, 0], proj_came, z_send.at[1], z_recv.at[1], z_id),
        ]

    for slot in range(2):
        for copy in x_copies(slot):
            copy.wait_recv()
        out_part[1, slot] = out_part[1, slot] + out_x[slot]
        proj_part[1, slot] = proj_part[1, slot] + proj_x[slot]
        if slot == 0:
            for copy in z_copies():
                copy.start()
    part_stores = [
        pltpu.make_async_copy(out_part.at[1, 1], out_mine, load_sem.at[1]),
        pltpu.make_async_copy(proj_part.at[1, 1], proj_mine, load_sem.at[2]),
    ]
    for store in part_stores:
        store.start()

    gain = gain_ref[...]
    gains[pl.ds(0, 1), :] = jnp.zeros_like(gain)
    gains[pl.ds(1, 1), :] = gain_two_ref[...]
    hidden_load.wait()
    loop(tiles, lambda j: y_copy(j).wait_recv())

    def norm_rows(i):
        window = pl.ds(pl.multiple_of(i * ROWS, ROWS), ROWS)
        incoming = staged[1, window, :] + y_in[window, :]
        values = tok[window, :].astype(F32)
        scale = lax.rsqrt(jnp.mean(values * values, axis=-1, keepdims=True) + EPSILON)
        weighted = incoming * gain
        inner = jnp.mean(weighted * values, axis=-1, keepdims=True)
        back = scale * weighted - values * (scale * scale * scale) * inner
        staged[0, window, :] = core_in[window, :] + back
        gains[pl.ds(0, 1), :] = gains[pl.ds(0, 1), :] + jnp.sum(
            incoming * values * scale, axis=0, keepdims=True
        )

    loop(half // ROWS, norm_rows)

    def to_rows(slot, out, sems, first):
        copies, kept = [], []
        for block in range(2):
            local, here = pl.ds(block * run, run), pl.ds(own_row(block, core), run)
            copies.append(remote(
                staged.at[slot, local], out.at[here],
                end_send.at[sems + block], end_recv.at[sems + block], twin_id,
            ))
            kept.append(pltpu.make_async_copy(
                staged.at[slot, local], out.at[here], load_sem.at[first + block]
            ))
        for copy in copies + kept:
            copy.start()
        return copies, kept

    input_copies, input_stores = to_rows(0, input_out, 3, 3)

    gain_twin = remote(gains, gains_came, gain_send.at[7], gain_recv.at[7], twin_id)
    gain_twin.start()

    loop(tiles, lambda j: y_copy(j).wait_send())
    branch_copy.wait()
    branch_loads = [
        pltpu.make_async_copy(branch_ref, staged.at[1], load_sem.at[5]),
        pltpu.make_async_copy(branch_came, y_in, load_sem.at[6]),
    ]
    for load in branch_loads:
        load.start()
    gain_twin.wait()
    gains[...] = gains[...] + gains_came[...]

    def gain_copy(m):
        return remote(
            gains.at[:, tile_of(peers[m])], gain_out.at[m], gain_send.at[m], gain_recv.at[m],
            (peers[m], tensor),
        )

    for m in range(7):
        gain_copy(m).start()
    gain_out[7] = gains[:, tile_of(dp)]
    for load in branch_loads:
        load.wait()

    def mixed_rows(i):
        window = pl.ds(pl.multiple_of(i * ROWS, ROWS), ROWS)
        staged[1, window, :] = staged[1, window, :] + y_in[window, :]

    loop(half // ROWS, mixed_rows)
    mixed_copy = remote(staged.at[1], core_in, end_send.at[5], end_recv.at[5], twin_id)
    mixed_copy.start()

    def put_mixed(source, which, first):
        def narrow(i):
            window = pl.ds(pl.multiple_of(i * ROWS, ROWS), ROWS)
            tok[window, :] = source[window, :].astype(BF16)

        loop(half // ROWS, narrow)
        copies = [
            pltpu.make_async_copy(
                tok.at[pl.ds(block * run, run)], mixed_out.at[pl.ds(own_row(block, which), run)],
                load_sem.at[first + block],
            )
            for block in range(2)
        ]
        for copy in copies:
            copy.start()
        for copy in copies:
            copy.wait()

    put_mixed(staged.at[1], core, 7)
    mixed_copy.wait()
    put_mixed(core_in, 1 - core, 9)

    for copy in part_stores + input_stores + input_copies:
        copy.wait()
    for m in range(7):
        gain_copy(m).wait()
    for slot in range(2):
        for copy in x_copies(slot):
            copy.wait_send()
    for copy in z_copies():
        copy.wait()
    loop(tiles, lambda j: row_copy(j)[0].wait())
    loop(tiles - LAST, lambda j: row_copy(j)[1].wait())


def last(
    normed_others, cot_others, normed, cot, act, gg, gu, w_gate, w_up, w_down,
    projected, branch, gain_two, w_query, w_key, w_value, heads, grad_attn, grad_attn_far,
    normed_one, normed_one_far, heads_far, grad_hidden, tokens, gain,
):
    row_count, width = tokens.shape
    half = row_count // 2
    tiles = width // TILE
    hidden_units = w_gate.shape[1]
    hbm = pl.BlockSpec(memory_space=pl.ANY)
    vmem = pl.BlockSpec(memory_space=pltpu.VMEM)
    wide = jax.ShapeDtypeStruct((half, width), F32)
    rows_pair = jax.ShapeDtypeStruct((2, TILE, hidden_units), F32)
    columns = jax.ShapeDtypeStruct((hidden_units, TILE), F32)
    out_block = jax.ShapeDtypeStruct((512, TILE), F32)
    proj_block = jax.ShapeDtypeStruct((TILE, 768), F32)
    dma = pltpu.SemaphoreType.DMA
    return pl.pallas_call(
        last_kernel,
        out_shape=(
            rows_pair, rows_pair, rows_pair, columns, columns, columns,
            jax.ShapeDtypeStruct((LAST * TILE, TILE), F32), out_block, out_block, proj_block, proj_block,
            jax.ShapeDtypeStruct((row_count, width), F32),
            jax.ShapeDtypeStruct((row_count, width), BF16),
            wide,
            jax.ShapeDtypeStruct((2, half, width), F32),
            jax.ShapeDtypeStruct((2, half, width), F32),
            jax.ShapeDtypeStruct((8, 2, TILE), F32),
        ),
        in_specs=[hbm] * 12 + [vmem] + [hbm] * 11 + [vmem],
        out_specs=(hbm,) * 16 + (vmem,),
        scratch_shapes=[
            pltpu.VMEM((6 * half, width), BF16),
            pltpu.VMEM((6 * half, width), BF16),
            pltpu.VMEM((2 * TILE, row_count + 6 * half), BF16),
            pltpu.VMEM((2 * TILE, row_count + 6 * half), BF16),
            pltpu.VMEM((3, row_count + 6 * half, TILE), BF16),
            pltpu.VMEM((2, width, TILE), BF16),
            pltpu.VMEM((2, width, TILE), BF16),
            pltpu.VMEM((2, TILE, width), BF16),
            pltpu.VMEM((2, 3, 2 * TILE, TILE), F32),
            pltpu.VMEM((2, half, width), F32),
            pltpu.VMEM((half, width), F32),
            pltpu.VMEM((half, width), F32),
            pltpu.VMEM((width, 768), BF16),
            pltpu.VMEM((half, width), BF16),
            pltpu.VMEM((2, row_count, 512), BF16),
            pltpu.VMEM((2, row_count, 1024), BF16),
            pltpu.VMEM((2, row_count, 1024), BF16),
            pltpu.VMEM((2, row_count, 768), BF16),
            pltpu.VMEM((2, 2, 512, TILE), F32),
            pltpu.VMEM((2, 2, TILE, 768), F32),
            pltpu.VMEM((2, 512, TILE), F32),
            pltpu.VMEM((2, TILE, 768), F32),
            pltpu.VMEM((2, half, 768), F32),
            pltpu.VMEM((half, 1024), F32),
            pltpu.VMEM((2, width), F32),
            pltpu.VMEM((2, width), F32),
            dma((15,)), dma((6,)), dma((2, 3)), dma((3,)), dma((2, 4)),
            dma((2, tiles)), dma((2, tiles)),
            dma((tiles,)), dma((tiles,)), dma((tiles,)), dma((tiles,)),
            dma((2, 2)), dma((2, 2)), dma((2,)), dma((2,)), dma((7,)), dma((7,)), dma((8,)), dma((8,)),
            dma((6,)), dma((6,)), pltpu.VMEM((row_count, TILE), F32),
        ],
        compiler_params=pltpu.CompilerParams(
            collective_id=1, has_side_effects=True, vmem_limit_bytes=64 * 1024 * 1024
        ),
        name="weight_gradients",
    )(
        normed_others, cot_others, normed, cot, act, gg, gu, w_gate, w_up, w_down,
        projected, branch, gain_two, w_query, w_key, w_value, heads, grad_attn, grad_attn_far,
        normed_one, normed_one_far, heads_far, grad_hidden, tokens, gain.reshape(1, width),
    )


def finish_kernel(
    kept, came, down_kept, down_came, out_mine, out_came, proj_mine, proj_came, input_in,
    mixed_in, gains, w_gate, w_up, w_down, w_out, w_query, w_key, w_value, grad_input, mixed,
    gain_one, gain_two,
):
    w_gate[...] = kept[0] + came[0]
    w_up[...] = kept[1] + came[1]
    w_down[...] = down_kept[...] + down_came[...]
    w_out[...] = out_mine[...] + out_came[...]
    queries, keys = w_query.shape[1], w_key.shape[1]
    w_query[...] = proj_mine[:, :queries] + proj_came[:, :queries]
    w_key[...] = proj_mine[:, queries : queries + keys] + proj_came[:, queries : queries + keys]
    w_value[...] = proj_mine[:, queries + keys :] + proj_came[:, queries + keys :]
    grad_input[...] = input_in[...]
    mixed[...] = mixed_in[...]
    total = jnp.sum(gains[...], axis=0)
    gain_one[...] = total[0:1]
    gain_two[...] = total[1:2]


def finish(*parts):
    steps = 8
    kept, down, out, proj, whole, gains = (parts[i] for i in (0, 2, 4, 6, 8, 10))
    rows, units = kept.shape[1:]

    def block(array, lead=()):
        size = array[len(lead) :]
        shape = lead + (size[0] // steps,) + size[1:]
        return pl.BlockSpec(shape, lambda i: (0,) * len(lead) + (i,) + (0,) * (len(size) - 1))

    fixed = lambda shape: pl.BlockSpec(shape, lambda i: (0,) * len(shape))
    outs = [
        (rows, units), (rows, units), down.shape, out.shape,
        (proj.shape[0], 512), (proj.shape[0], 128), (proj.shape[0], 128), whole.shape,
    ]
    return pl.pallas_call(
        finish_kernel,
        grid=(steps,),
        out_shape=[jax.ShapeDtypeStruct(shape, F32) for shape in outs]
        + [
            jax.ShapeDtypeStruct(whole.shape, BF16),
            jax.ShapeDtypeStruct((1, gains.shape[2]), F32),
            jax.ShapeDtypeStruct((1, gains.shape[2]), F32),
        ],
        in_specs=[block(kept.shape, (2,))] * 2
        + [block(part.shape) for part in parts[2:10]]
        + [fixed(gains.shape)],
        out_specs=[block(shape) for shape in outs]
        + [block(whole.shape)] + [fixed((1, gains.shape[2]))] * 2,
        compiler_params=pltpu.CompilerParams(vmem_limit_bytes=64 * 1024 * 1024),
        cost_estimate=pl.CostEstimate(
            flops=2_000_000, bytes_accessed=34_000_000, transcendentals=0
        ),
        name="last_sums",
    )(*parts)


def body(
    tokens,
    segments,
    positions,
    attn_gain,
    w_query,
    key_weight,
    value_weight,
    w_out,
    mlp_gain,
    w_gate,
    w_up,
    w_down,
    cotangent,
):
    row_count, width = tokens.shape
    half = row_count // 2
    hidden_units = w_gate.shape[1]
    tiles = width // TILE
    hbm = pl.BlockSpec(memory_space=pl.ANY)
    vmem = pl.BlockSpec(memory_space=pltpu.VMEM)
    wide = jax.ShapeDtypeStruct((half, width), F32)
    units = jax.ShapeDtypeStruct((row_count, hidden_units), BF16)
    square = jax.ShapeDtypeStruct((row_count, 512), BF16)
    dma = pltpu.SemaphoreType.DMA
    return pl.pallas_call(
        middle_kernel,
        out_shape=(
            jax.ShapeDtypeStruct((row_count, width), BF16),
            square, square, square, square,
            jax.ShapeDtypeStruct((2, half, width // 2), F32),
            jax.ShapeDtypeStruct((half, width // 2), F32),
            wide,
            jax.ShapeDtypeStruct((row_count, width), BF16),
            jax.ShapeDtypeStruct((row_count, 768), BF16),
            jax.ShapeDtypeStruct((2, half, width // 2), F32),
            wide,
            jax.ShapeDtypeStruct((row_count, width), BF16),
            units, units, units,
            jax.ShapeDtypeStruct((1, width), F32),
            jax.ShapeDtypeStruct((5, half, width), F32),
            jax.ShapeDtypeStruct((5, half, width), F32),
        ),
        in_specs=[hbm] * 6 + [vmem] * 2 + [hbm] * 3 + [vmem] * 3,
        out_specs=(hbm,) * 16 + (vmem,) + (hbm,) * 2,
        scratch_shapes=[
            pltpu.VMEM(w_gate.shape, BF16),
            pltpu.VMEM(w_up.shape, BF16),
            pltpu.VMEM(w_down.shape, BF16),
            pltpu.VMEM((row_count, width), BF16),
            pltpu.VMEM((half, width), F32),
            pltpu.VMEM((row_count, width), BF16),
            pltpu.VMEM((half, width), F32),
            pltpu.VMEM((half, width), F32),
            pltpu.VMEM((row_count, hidden_units), BF16),
            pltpu.VMEM((row_count, hidden_units), BF16),
            pltpu.VMEM((row_count, hidden_units), BF16),
            pltpu.VMEM((half, width), F32),
            pltpu.VMEM((2, half, width), F32),
            pltpu.VMEM((3, half, width), F32),
            pltpu.VMEM((2, half, width), F32),
            pltpu.VMEM((half, TILE), F32),
            pltpu.VMEM((8, row_count), F32),
            pltpu.VMEM((row_count, 8), F32),
            pltpu.VMEM((row_count, 128), F32),
            pltpu.VMEM((row_count, 128), F32),
            dma((13,)),
            dma((3, 2 * tiles)), dma((3, 2 * tiles)), dma((2, 2 * tiles)), dma((2, 2 * tiles)),
            dma((3, CHUNKS)), dma((3, CHUNKS)),
            dma((4, CHUNKS)), dma((4, CHUNKS)),
            dma((2, 3)), dma((2, 3)),
            dma((CHUNKS,)), dma((CHUNKS,)),
            dma((8,)), dma((8,)),
            pltpu.SemaphoreType.REGULAR,
        ],
        compiler_params=pltpu.CompilerParams(
            collective_id=0, has_side_effects=True, vmem_limit_bytes=64 * 1024 * 1024
        ),
        name="feed_forward",
    )(
        w_query, w_key, w_value, w_out, tokens, cotangent,
        gain_one.reshape(1, width), gain.reshape(1, width), w_gate, w_up, w_down,
        segment.reshape(1, row_count), position.reshape(1, row_count), frequency.reshape(1, 128),
    )


LAST = 2


def last_kernel(
    normed_others_ref,
    cot_others_ref,
    normed_ref,
    cot_ref,
    act_ref,
    gg_ref,
    gu_ref,
    w_gate_ref,
    w_up_ref,
    w_down_ref,
    projected_ref,
    branch_ref,
    gain_two_ref,
    w_query_ref,
    w_key_ref,
    w_value_ref,
    heads_ref,
    grad_attn_ref,
    grad_attn_far_ref,
    normed_one_ref,
    normed_one_far_ref,
    heads_far_ref,
    grad_hidden_ref,
    tokens_ref,
    gain_ref,
    kept_out,
    sent_out,
    came_out,
    down_kept,
    down_sent,
    down_came,
    down_last,
    out_mine,
    out_came,
    proj_mine,
    proj_came,
    input_out,
    mixed_out,
    branch_came,
    normed_late,
    cot_late,
    gain_out,
    normed,
    cot,
    normed_t,
    cot_t,
    units,
    gate_w,
    up_w,
    down_w,
    total,
    staged,
    core_in,
    y_in,
    w_proj,
    tok,
    heads,
    grad_attn,
    normed_one,
    projected,
    out_part,
    proj_part,
    out_x,
    proj_x,
    far_staged,
    far_heads,
    gains,
    gains_came,
    load_sem,
    piece_sem,
    weight_sem,
    unit_sem,
    store_sem,
    row_send,
    row_recv,
    core_send,
    core_recv,
    y_send,
    y_recv,
    x_send,
    x_recv,
    z_send,
    z_recv,
    end_send,
    end_recv,
    gain_send,
    gain_recv,
    late_send,
    late_recv,
    product,
):
    dp, tensor = lax.axis_index("dp"), lax.axis_index("tensor")
    core = tensor % 2
    x_low, z_low, z_high = dp % 2, (dp // 2) % 2, dp // 4
    twin_id = (dp, flip(tensor, 1))
    y_id = (dp, flip(tensor, 2))
    x_id = (flip(dp, 1), tensor)
    z_id = (flip(dp, 4), tensor)
    far_id = (flip(dp, 2), tensor)
    half, width = tok.shape
    row_count = 2 * half
    tiles = width // TILE
    run = half // 2
    y_bit = (tensor // 2) % 2

    def own_row(block, which):
        return pl.multiple_of(block * half + which * run, run)

    everything = slice(None)
    transposed = (((1,), (1,)), ((), ()))
    over = (((0,), (0,)), ((), ()))

    def remote(src, dst, send, recv, device):
        return pltpu.make_async_remote_copy(
            src_ref=src, dst_ref=dst, send_sem=send, recv_sem=recv,
            device_id=device, device_id_type=MESH,
        )

    def tile_of(j):
        return pl.ds(pl.multiple_of(j * TILE, TILE), TILE)

    away_block = tile_of(flip(dp, 2))
    home_block = tile_of(dp)
    near = [
        pl.ds(pl.multiple_of(b * 1024 + z_low * 512, 512), 512) for b in range(2)
    ]
    own_columns = [units.at[0, pl.ds(i * row_count, row_count)] for i in range(4)]
    loads = [
        pltpu.make_async_copy(normed_ref.at[:, away_block], own_columns[0], load_sem.at[0]),
        pltpu.make_async_copy(normed_ref.at[:, home_block], own_columns[1], load_sem.at[1]),
        pltpu.make_async_copy(cot_ref.at[:, away_block], own_columns[2], load_sem.at[2]),
        pltpu.make_async_copy(cot_ref.at[:, home_block], own_columns[3], load_sem.at[3]),
        pltpu.make_async_copy(w_query_ref, w_proj.at[:, pl.ds(0, 512)], load_sem.at[4]),
        pltpu.make_async_copy(w_key_ref, w_proj.at[:, pl.ds(512, 128)], load_sem.at[5]),
        pltpu.make_async_copy(w_value_ref, w_proj.at[:, pl.ds(640, 128)], load_sem.at[6]),
        pltpu.make_async_copy(
            tokens_ref.at[pl.ds(own_row(0, core), run)], tok.at[pl.ds(0, run)], load_sem.at[7]
        ),
        pltpu.make_async_copy(heads_ref, heads.at[0], load_sem.at[8]),
        pltpu.make_async_copy(
            grad_attn_ref.at[:, near[0]], grad_attn.at[0, :, pl.ds(0, 512)], load_sem.at[9]
        ),
        pltpu.make_async_copy(
            grad_attn_ref.at[:, near[1]], grad_attn.at[0, :, pl.ds(512, 512)], load_sem.at[10]
        ),
        pltpu.make_async_copy(
            normed_one_ref.at[:, near[0]], normed_one.at[0, :, pl.ds(0, 512)], load_sem.at[11]
        ),
        pltpu.make_async_copy(
            normed_one_ref.at[:, near[1]], normed_one.at[0, :, pl.ds(512, 512)], load_sem.at[12]
        ),
        pltpu.make_async_copy(projected_ref, projected.at[0], load_sem.at[13]),
        pltpu.make_async_copy(
            tokens_ref.at[pl.ds(own_row(1, core), run)], tok.at[pl.ds(run, run)], load_sem.at[14]
        ),
    ]

    late_normed = pl.ds(run, run)
    early_normed = pl.ds(0, run)
    late_cot = pl.ds(pl.multiple_of((1 - y_bit) * run, run), run)
    early_cot = pl.ds(pl.multiple_of(y_bit * run, run), run)

    def piece_load(i, slot):
        which, part = i // 6, i % 6
        source = (normed_others_ref, cot_others_ref)[which]
        late = (normed_late, cot_late)[which]
        into = staged.at[slot]
        if part in (0, 1, 3, 4):
            return [pltpu.make_async_copy(source.at[part], into, piece_sem.at[slot])]
        if part == 5:
            return [pltpu.make_async_copy(late.at[1], into, piece_sem.at[slot])]
        early_rows = (early_normed, early_cot)[which]
        late_rows = (late_normed, late_cot)[which]
        return [
            pltpu.make_async_copy(
                source.at[2, early_rows], into.at[early_rows], piece_sem.at[slot]
            ),
            pltpu.make_async_copy(
                late.at[0, late_rows], into.at[late_rows], piece_sem.at[2 + slot]
            ),
        ]

    def weight_loads(j, slot):
        return [
            pltpu.make_async_copy(
                w_gate_ref.at[:, tile_of(j)], gate_w.at[slot], weight_sem.at[slot, 0]
            ),
            pltpu.make_async_copy(
                w_up_ref.at[:, tile_of(j)], up_w.at[slot], weight_sem.at[slot, 1]
            ),
            pltpu.make_async_copy(
                w_down_ref.at[tile_of(j), :], down_w.at[slot], weight_sem.at[slot, 2]
            ),
        ]

    order = [0, 1, 3, 4, 6, 7, 9, 10, 2, 8, 5, 11]
    for i in range(2):
        for load in piece_load(order[i], i):
            load.start()
    loads[13].start()
    for load in loads[:4]:
        load.start()
    for load in weight_loads(0, 0):
        load.start()

    barrier = pltpu.get_barrier_semaphore()
    peers = []
    for m in range(1, 8):
        peer = dp
        for bit in (1, 2, 4):
            peer = flip(peer, bit) if m & bit else peer
        peers.append(peer)
    for device in [twin_id, y_id] + [(peer, tensor) for peer in peers]:
        pl.semaphore_signal(barrier, inc=1, device_id=device, device_id_type=MESH)
    pl.semaphore_wait(barrier, 9)
    late_copies = [
        remote(normed_others_ref.at[1, late_normed], normed_late.at[0, late_normed],
               late_send.at[0], late_recv.at[0], x_id),
        remote(cot_others_ref.at[2, early_cot], cot_late.at[0, early_cot],
               late_send.at[1], late_recv.at[1], y_id),
        remote(normed_others_ref.at[2, early_normed], normed_late.at[1, early_normed],
               late_send.at[2], late_recv.at[2], twin_id),
        remote(cot_others_ref.at[2, early_cot], cot_late.at[1, early_cot],
               late_send.at[3], late_recv.at[3], twin_id),
    ]
    for copy in late_copies:
        copy.start()

    loads[13].wait()

    def widen(r):
        window = pl.ds(pl.multiple_of(r * ROWS, ROWS), ROWS)
        for s in range(2):
            there = pl.ds(pl.multiple_of(s * half + r * ROWS, ROWS), ROWS)
            proj_part[0, s, window, :] = projected[0, there, :].astype(F32)

    loop(half // ROWS, widen)
    projected_copy = remote(proj_part.at[0], far_staged, end_send.at[2], end_recv.at[2], far_id)
    projected_copy.start()
    branch_copy = remote(branch_ref, branch_came, end_send.at[1], end_recv.at[1], y_id)

    late_twins = [
        remote(normed_late.at[0, late_normed], normed_late.at[1, late_normed],
               late_send.at[4], late_recv.at[4], twin_id),
        remote(cot_late.at[0, late_cot], cot_late.at[1, late_cot],
               late_send.at[5], late_recv.at[5], twin_id),
    ]
    def take_piece(place):
        i, slot = order[place], place % 2
        for load in piece_load(i, slot):
            load.wait()
        rows_to, turned_to = (normed, normed_t) if i < 6 else (cot, cot_t)
        base = {0: 0, 1: 1, 3: 2, 4: 3, 2: 4, 5: 5}[i % 6] * half

        def convert(r, slot=slot, rows_to=rows_to, base=base):
            window = pl.ds(pl.multiple_of(r * ROWS, ROWS), ROWS)
            rows_to[pl.ds(pl.multiple_of(base + r * ROWS, ROWS), ROWS), :] = staged[
                slot, window, :
            ].astype(BF16)

        loop(half // ROWS, convert)
        for part, block in enumerate((away_block, home_block)):
            turned_to[pl.ds(part * TILE, TILE), pl.ds(row_count + base, half)] = (
                staged[slot, :, block].T.astype(BF16)
            )
        if place == 8:
            for copy in late_copies[2:] + late_twins:
                copy.wait()
        if place + 2 < 8 or 8 <= place < 10:
            for load in piece_load(order[place + 2], slot):
                load.start()
    for place in range(8):
        take_piece(place)
    for part in range(4):
        loads[part].wait()
        turned_to = (normed_t, cot_t)[part // 2]
        turned_to[pl.ds((part % 2) * TILE, TILE), pl.ds(0, row_count)] = (
            own_columns[part][...].astype(F32).T.astype(BF16)
        )

    def row_copy(j):
        window = (everything, everything, tile_of(j))
        return [
            remote(
                sent_out.at[window], came_out.at[window],
                row_send.at[0, j], row_recv.at[0, j], far_id,
            ),
            remote(
                down_sent.at[tile_of(j)], down_came.at[tile_of(j)],
                row_send.at[1, j], row_recv.at[1, j], far_id,
            ),
        ]

    def stores(j, slot):
        return [
            pltpu.make_async_copy(
                total.at[slot, pl.ds(0, 2), pl.ds(0, TILE)], sent_out.at[:, :, tile_of(j)],
                store_sem.at[slot, 0],
            ),
            pltpu.make_async_copy(
                total.at[slot, pl.ds(0, 2), pl.ds(TILE, TILE)], kept_out.at[:, :, tile_of(j)],
                store_sem.at[slot, 1],
            ),
            pltpu.make_async_copy(
                total.at[slot, 2, pl.ds(TILE, TILE)], down_kept.at[tile_of(j)],
                store_sem.at[slot, 3],
            ),
        ]

    def down_store(slot, into):
        return pltpu.make_async_copy(
            total.at[slot, 2, pl.ds(0, TILE)], into, store_sem.at[slot, 2]
        )

    def unit_loads(j):
        return [
            pltpu.make_async_copy(
                source.at[:, tile_of(j)], units.at[i, pl.ds(0, row_count)], unit_sem.at[i]
            )
            for i, source in enumerate((gg_ref, gu_ref, act_ref))
        ]

    def feed_forward_tile(j, first=False):
        slot = j % 2
        for load in weight_loads(j, slot):
            load.wait()

        if first:
            for load in weight_loads(1, 1):
                load.start()
        else:

            @pl.when(j + 1 < tiles)
            def _():
                for load in weight_loads(j + 1, 1 - slot):
                    load.start()

        for load in unit_loads(j):
            load.start()

        def block(m):
            rows = pl.ds(pl.multiple_of(m * 512, 512), 512)
            to = pl.ds(pl.multiple_of(row_count + m * 512, 512), 512)
            gate = jnp.dot(normed[rows, :], gate_w[slot], preferred_element_type=F32)
            up = jnp.dot(normed[rows, :], up_w[slot], preferred_element_type=F32)
            back = lax.dot_general(
                cot[rows, :], down_w[slot], transposed, preferred_element_type=F32
            )
            sigmoid = jax.nn.sigmoid(gate)
            swish = gate * sigmoid
            units[2, to, :] = (swish * up).astype(BF16)
            units[0, to, :] = (back * up * sigmoid * (1.0 + gate * (1.0 - sigmoid))).astype(BF16)
            units[1, to, :] = (back * swish).astype(BF16)

        if first:
            loop(2, block)
            for copy, later in zip(late_copies[:2], late_twins):
                copy.wait()
                later.start()
            branch_copy.start()
            for place in (8, 9):
                for load in piece_load(order[place], place % 2):
                    load.start()
            for place in range(8, 12):
                take_piece(place)
            block(2)
        else:
            loop(normed.shape[0] // 512, block)
        for load in unit_loads(j):
            load.wait()

        total[slot, 0] = jnp.dot(normed_t[...], units[0], preferred_element_type=F32)
        total[slot, 1] = jnp.dot(normed_t[...], units[1], preferred_element_type=F32)
        turned = jnp.dot(cot_t[...], units[2], preferred_element_type=F32)
        for part in range(2):
            total[slot, 2, pl.ds(part * TILE, TILE)] = turned[part * TILE : (part + 1) * TILE].T
        for store in stores(j, slot):
            store.start()
        here = j < tiles - LAST

        @pl.when(here)
        def _():
            store = down_store(slot, down_sent.at[tile_of(j)])
            store.start()
            store.wait()
            row_copy(j)[1].start()

        @pl.when(jnp.logical_not(here))
        def _():
            store = down_store(slot, down_last.at[tile_of(j - (tiles - LAST))])
            store.start()
            store.wait()

        for store in stores(j, slot):
            store.wait()
        row_copy(j)[0].start()

    def x_copies(slot):
        return [
            remote(out_part.at[0, slot], out_x.at[slot], x_send.at[0, slot],
                   x_recv.at[0, slot], x_id),
            remote(proj_part.at[0, slot], proj_x.at[slot], x_send.at[1, slot],
                   x_recv.at[1, slot], x_id),
        ]

    def attention_parts():
        for load in far_loads + loads[8:13]:
            load.wait()
        projected_copy.wait()

        def convert(r):
            window = pl.ds(pl.multiple_of(r * ROWS, ROWS), ROWS)
            block, rest = r // (run // ROWS), r % (run // ROWS)
            for s in range(2):
                which = core if s == 0 else 1 - core
                here = pl.ds(
                    pl.multiple_of(block * half + which * run + rest * ROWS, ROWS), ROWS
                )
                grad_attn[1, here, :] = staged[0, window, pl.ds(s * 1024, 1024)].astype(BF16)
                normed_one[1, here, :] = staged[1, window, pl.ds(s * 1024, 1024)].astype(BF16)
                there = pl.ds(pl.multiple_of(s * half + r * ROWS, ROWS), ROWS)
                projected[1, there, :] = far_staged[s, window, :].astype(BF16)
                heads[1, there, :] = far_heads[window, pl.ds(s * 512, 512)].astype(BF16)

        loop(half // ROWS, convert)
        for side in range(2):
            x_at = 1 - x_low if side == 0 else x_low
            for slot in range(2):
                z_at = 1 - z_high if slot == 0 else z_high
                columns = pl.ds(pl.multiple_of(z_at * 512 + x_at * 256, 256), 256)
                out_part[side, slot] = lax.dot_general(
                    heads[0], grad_attn[0, :, columns], over, preferred_element_type=F32
                ) + lax.dot_general(
                    heads[1], grad_attn[1, :, columns], over, preferred_element_type=F32
                )
                proj_part[side, slot] = lax.dot_general(
                    normed_one[0, :, columns], projected[0], over, preferred_element_type=F32
                ) + lax.dot_general(
                    normed_one[1, :, columns], projected[1], over, preferred_element_type=F32
                )
                if side == 0:
                    for copy in x_copies(slot):
                        copy.start()

    def core_copy(j):
        window = (everything, tile_of(j))
        return remote(
            staged.at[0].at[window], core_in.at[window], core_send.at[j], core_recv.at[j], twin_id
        )

    def y_copy(j):
        window = (everything, tile_of(j))
        return remote(
            staged.at[1].at[window], y_in.at[window], y_send.at[j], y_recv.at[j], y_id
        )

    def attention_sums():
        for load in loads[4:8] + loads[14:]:
            load.wait()

        def produce(j):
            product[...] = lax.dot_general(
                projected[0], w_proj[tile_of(j), :], transposed, preferred_element_type=F32
            )
            for block in range(2):
                for slot, which in ((0, 1 - core), (1, core)):
                    staged[slot, pl.ds(block * run, run), tile_of(j)] = product[
                        pl.ds(own_row(block, which), run), :
                    ]
            core_copy(j).start()

        def forward(j):
            core_copy(j).wait_recv()
            staged[1, :, tile_of(j)] = staged[1, :, tile_of(j)] + core_in[:, tile_of(j)]
            y_copy(j).start()

        produce(0)

        def step(j):
            produce(j + 1)
            forward(j)

        loop(tiles - 1, step)
        forward(tiles - 1)
        loop(tiles, lambda j: core_copy(j).wait_send())

    feed_forward_tile(0, first=True)
    for load in loads[4:13] + loads[14:]:
        load.start()
    far_loads = (
        [
            pltpu.make_async_copy(
                grad_attn_far_ref.at[s], staged.at[0, :, pl.ds(s * 1024, 1024)], piece_sem.at[s]
            )
            for s in range(2)
        ]
        + [
            pltpu.make_async_copy(
                normed_one_far_ref.at[s], staged.at[1, :, pl.ds(s * 1024, 1024)],
                piece_sem.at[2 + s],
            )
            for s in range(2)
        ]
        + [
            pltpu.make_async_copy(heads_far_ref, far_heads, piece_sem.at[5]),
        ]
    )
    for load in far_loads:
        load.start()


    def step(j):
        feed_forward_tile(j + 1)

        @pl.when(j == 0)
        def _():
            attention_parts()
            attention_sums()

    loop(tiles - 1, step)
    hidden_load = pltpu.make_async_copy(grad_hidden_ref, core_in, load_sem.at[0])
    hidden_load.start()

    def z_copies():
        return [
            remote(out_part.at[1, 0], out_came, z_send.at[0], z_recv.at[0], z_id),
            remote(proj_part.at[1, 0], proj_came, z_send.at[1], z_recv.at[1], z_id),
        ]

    for slot in range(2):
        for copy in x_copies(slot):
            copy.wait_recv()
        out_part[1, slot] = out_part[1, slot] + out_x[slot]
        proj_part[1, slot] = proj_part[1, slot] + proj_x[slot]
        if slot == 0:
            for copy in z_copies():
                copy.start()
    part_stores = [
        pltpu.make_async_copy(out_part.at[1, 1], out_mine, load_sem.at[1]),
        pltpu.make_async_copy(proj_part.at[1, 1], proj_mine, load_sem.at[2]),
    ]
    for store in part_stores:
        store.start()

    gain = gain_ref[...]
    gains[pl.ds(0, 1), :] = jnp.zeros_like(gain)
    gains[pl.ds(1, 1), :] = gain_two_ref[...]
    hidden_load.wait()
    loop(tiles, lambda j: y_copy(j).wait_recv())

    def norm_rows(i):
        window = pl.ds(pl.multiple_of(i * ROWS, ROWS), ROWS)
        incoming = staged[1, window, :] + y_in[window, :]
        values = tok[window, :].astype(F32)
        scale = lax.rsqrt(jnp.mean(values * values, axis=-1, keepdims=True) + EPSILON)
        weighted = incoming * gain
        inner = jnp.mean(weighted * values, axis=-1, keepdims=True)
        back = scale * weighted - values * (scale * scale * scale) * inner
        staged[0, window, :] = core_in[window, :] + back
        gains[pl.ds(0, 1), :] = gains[pl.ds(0, 1), :] + jnp.sum(
            incoming * values * scale, axis=0, keepdims=True
        )

    loop(half // ROWS, norm_rows)

    def to_rows(slot, out, sems, first):
        copies, kept = [], []
        for block in range(2):
            local, here = pl.ds(block * run, run), pl.ds(own_row(block, core), run)
            copies.append(remote(
                staged.at[slot, local], out.at[here],
                end_send.at[sems + block], end_recv.at[sems + block], twin_id,
            ))
            kept.append(pltpu.make_async_copy(
                staged.at[slot, local], out.at[here], load_sem.at[first + block]
            ))
        for copy in copies + kept:
            copy.start()
        return copies, kept

    input_copies, input_stores = to_rows(0, input_out, 3, 3)

    gain_twin = remote(gains, gains_came, gain_send.at[7], gain_recv.at[7], twin_id)
    gain_twin.start()

    loop(tiles, lambda j: y_copy(j).wait_send())
    branch_copy.wait()
    branch_loads = [
        pltpu.make_async_copy(branch_ref, staged.at[1], load_sem.at[5]),
        pltpu.make_async_copy(branch_came, y_in, load_sem.at[6]),
    ]
    for load in branch_loads:
        load.start()
    gain_twin.wait()
    gains[...] = gains[...] + gains_came[...]

    def gain_copy(m):
        return remote(
            gains.at[:, tile_of(peers[m])], gain_out.at[m], gain_send.at[m], gain_recv.at[m],
            (peers[m], tensor),
        )

    for m in range(7):
        gain_copy(m).start()
    gain_out[7] = gains[:, tile_of(dp)]
    for load in branch_loads:
        load.wait()

    def mixed_rows(i):
        window = pl.ds(pl.multiple_of(i * ROWS, ROWS), ROWS)
        staged[1, window, :] = staged[1, window, :] + y_in[window, :]

    loop(half // ROWS, mixed_rows)
    mixed_copy = remote(staged.at[1], core_in, end_send.at[5], end_recv.at[5], twin_id)
    mixed_copy.start()

    def put_mixed(source, which, first):
        def narrow(i):
            window = pl.ds(pl.multiple_of(i * ROWS, ROWS), ROWS)
            tok[window, :] = source[window, :].astype(BF16)

        loop(half // ROWS, narrow)
        copies = [
            pltpu.make_async_copy(
                tok.at[pl.ds(block * run, run)], mixed_out.at[pl.ds(own_row(block, which), run)],
                load_sem.at[first + block],
            )
            for block in range(2)
        ]
        for copy in copies:
            copy.start()
        for copy in copies:
            copy.wait()

    put_mixed(staged.at[1], core, 7)
    mixed_copy.wait()
    put_mixed(core_in, 1 - core, 9)

    for copy in part_stores + input_stores + input_copies:
        copy.wait()
    for m in range(7):
        gain_copy(m).wait()
    for slot in range(2):
        for copy in x_copies(slot):
            copy.wait_send()
    for copy in z_copies():
        copy.wait()
    loop(tiles, lambda j: row_copy(j)[0].wait())
    loop(tiles - LAST, lambda j: row_copy(j)[1].wait())


def last(
    normed_others, cot_others, normed, cot, act, gg, gu, w_gate, w_up, w_down,
    projected, branch, gain_two, w_query, w_key, w_value, heads, grad_attn, grad_attn_far,
    normed_one, normed_one_far, heads_far, grad_hidden, tokens, gain,
):
    row_count, width = tokens.shape
    half = row_count // 2
    tiles = width // TILE
    hidden_units = w_gate.shape[1]
    hbm = pl.BlockSpec(memory_space=pl.ANY)
    vmem = pl.BlockSpec(memory_space=pltpu.VMEM)
    wide = jax.ShapeDtypeStruct((half, width), F32)
    rows_pair = jax.ShapeDtypeStruct((2, TILE, hidden_units), F32)
    columns = jax.ShapeDtypeStruct((hidden_units, TILE), F32)
    out_block = jax.ShapeDtypeStruct((512, TILE), F32)
    proj_block = jax.ShapeDtypeStruct((TILE, 768), F32)
    dma = pltpu.SemaphoreType.DMA
    return pl.pallas_call(
        last_kernel,
        out_shape=(
            rows_pair, rows_pair, rows_pair, columns, columns, columns,
            jax.ShapeDtypeStruct((LAST * TILE, TILE), F32), out_block, out_block, proj_block, proj_block,
            jax.ShapeDtypeStruct((row_count, width), F32),
            jax.ShapeDtypeStruct((row_count, width), BF16),
            wide,
            jax.ShapeDtypeStruct((2, half, width), F32),
            jax.ShapeDtypeStruct((2, half, width), F32),
            jax.ShapeDtypeStruct((8, 2, TILE), F32),
        ),
        in_specs=[hbm] * 12 + [vmem] + [hbm] * 11 + [vmem],
        out_specs=(hbm,) * 16 + (vmem,),
        scratch_shapes=[
            pltpu.VMEM((6 * half, width), BF16),
            pltpu.VMEM((6 * half, width), BF16),
            pltpu.VMEM((2 * TILE, row_count + 6 * half), BF16),
            pltpu.VMEM((2 * TILE, row_count + 6 * half), BF16),
            pltpu.VMEM((3, row_count + 6 * half, TILE), BF16),
            pltpu.VMEM((2, width, TILE), BF16),
            pltpu.VMEM((2, width, TILE), BF16),
            pltpu.VMEM((2, TILE, width), BF16),
            pltpu.VMEM((2, 3, 2 * TILE, TILE), F32),
            pltpu.VMEM((2, half, width), F32),
            pltpu.VMEM((half, width), F32),
            pltpu.VMEM((half, width), F32),
            pltpu.VMEM((width, 768), BF16),
            pltpu.VMEM((half, width), BF16),
            pltpu.VMEM((2, row_count, 512), BF16),
            pltpu.VMEM((2, row_count, 1024), BF16),
            pltpu.VMEM((2, row_count, 1024), BF16),
            pltpu.VMEM((2, row_count, 768), BF16),
            pltpu.VMEM((2, 2, 512, TILE), F32),
            pltpu.VMEM((2, 2, TILE, 768), F32),
            pltpu.VMEM((2, 512, TILE), F32),
            pltpu.VMEM((2, TILE, 768), F32),
            pltpu.VMEM((2, half, 768), F32),
            pltpu.VMEM((half, 1024), F32),
            pltpu.VMEM((2, width), F32),
            pltpu.VMEM((2, width), F32),
            dma((15,)), dma((6,)), dma((2, 3)), dma((3,)), dma((2, 4)),
            dma((2, tiles)), dma((2, tiles)),
            dma((tiles,)), dma((tiles,)), dma((tiles,)), dma((tiles,)),
            dma((2, 2)), dma((2, 2)), dma((2,)), dma((2,)), dma((7,)), dma((7,)), dma((8,)), dma((8,)),
            dma((6,)), dma((6,)), pltpu.VMEM((row_count, TILE), F32),
        ],
        compiler_params=pltpu.CompilerParams(
            collective_id=1, has_side_effects=True, vmem_limit_bytes=64 * 1024 * 1024
        ),
        name="weight_gradients",
    )(
        normed_others, cot_others, normed, cot, act, gg, gu, w_gate, w_up, w_down,
        projected, branch, gain_two, w_query, w_key, w_value, heads, grad_attn, grad_attn_far,
        normed_one, normed_one_far, heads_far, grad_hidden, tokens, gain.reshape(1, width),
    )


def finish_kernel(
    kept, came, down_kept, down_came, out_mine, out_came, proj_mine, proj_came, input_in,
    mixed_in, gains, w_gate, w_up, w_down, w_out, w_query, w_key, w_value, grad_input, mixed,
    gain_one, gain_two,
):
    w_gate[...] = kept[0] + came[0]
    w_up[...] = kept[1] + came[1]
    w_down[...] = down_kept[...] + down_came[...]
    w_out[...] = out_mine[...] + out_came[...]
    queries, keys = w_query.shape[1], w_key.shape[1]
    w_query[...] = proj_mine[:, :queries] + proj_came[:, :queries]
    w_key[...] = proj_mine[:, queries : queries + keys] + proj_came[:, queries : queries + keys]
    w_value[...] = proj_mine[:, queries + keys :] + proj_came[:, queries + keys :]
    grad_input[...] = input_in[...]
    mixed[...] = mixed_in[...]
    total = jnp.sum(gains[...], axis=0)
    gain_one[...] = total[0:1]
    gain_two[...] = total[1:2]


def finish(*parts):
    steps = 8
    kept, down, out, proj, whole, gains = (parts[i] for i in (0, 2, 4, 6, 8, 10))
    rows, units = kept.shape[1:]

    def block(array, lead=()):
        size = array[len(lead) :]
        shape = lead + (size[0] // steps,) + size[1:]
        return pl.BlockSpec(shape, lambda i: (0,) * len(lead) + (i,) + (0,) * (len(size) - 1))

    fixed = lambda shape: pl.BlockSpec(shape, lambda i: (0,) * len(shape))
    outs = [
        (rows, units), (rows, units), down.shape, out.shape,
        (proj.shape[0], 512), (proj.shape[0], 128), (proj.shape[0], 128), whole.shape,
    ]
    return pl.pallas_call(
        finish_kernel,
        grid=(steps,),
        out_shape=[jax.ShapeDtypeStruct(shape, F32) for shape in outs]
        + [
            jax.ShapeDtypeStruct(whole.shape, BF16),
            jax.ShapeDtypeStruct((1, gains.shape[2]), F32),
            jax.ShapeDtypeStruct((1, gains.shape[2]), F32),
        ],
        in_specs=[block(kept.shape, (2,))] * 2
        + [block(part.shape) for part in parts[2:10]]
        + [fixed(gains.shape)],
        out_specs=[block(shape) for shape in outs]
        + [block(whole.shape)] + [fixed((1, gains.shape[2]))] * 2,
        compiler_params=pltpu.CompilerParams(vmem_limit_bytes=64 * 1024 * 1024),
        cost_estimate=pl.CostEstimate(
            flops=2_000_000, bytes_accessed=34_000_000, transcendentals=0
        ),
        name="last_sums",
    )(*parts)


def body(
    tokens,
    segments,
    positions,
    attn_gain,
    w_query,
    key_weight,
    value_weight,
    w_out,
    mlp_gain,
    w_gate,
    w_up,
    w_down,
    cotangent,
):
    groups = lax.axis_size("dp")
    place = lax.axis_index("dp")
    core = lax.axis_index("tensor") % 2
    all_bits = [1 << i for i in range(groups.bit_length() - 1)]
    shared_bits = [bit for bit in (4, 1) if bit < groups]
    split_bits = [bit for bit in all_bits if bit not in shared_bits]

    def blocks(matrix, offsets):
        width = matrix.shape[1] // groups
        return [
            lax.dynamic_slice_in_dim(matrix, (place ^ offset) * width, width, 1)
            for offset in offsets
        ]

    def offsets_of(bits):
        found = [0]
        for bit in bits:
            found = found + [offset + bit for offset in found]
        return found

    def reduced(matrix_of, bits):
        sent = None
        for bit in bits:
            rest = bits[bits.index(bit) + 1 :]
            offsets = offsets_of(rest)
            if sent is None:
                away = matrix_of([offset ^ bit for offset in offsets])
                home = matrix_of(offsets)
            else:
                away = [sent[offset ^ bit] for offset in offsets]
                home = [sent[offset] for offset in offsets]
            came = swap(away, "dp", bit)
            sent = {offset: h + c for offset, h, c in zip(offsets, home, came)}
        return sent[0]

    row_count, width = tokens.shape
    query_width, kv_width = w_query.shape[1], key_weight.shape[1]
    half_dim = HEAD_SIZE // 2
    frequency = 500000.0 ** (-(jnp.arange(half_dim).astype(F32) * 2.0 / HEAD_SIZE))
    frequency = jnp.tile(frequency, 4)
    (
        normed_one,
        head_outputs,
        _,
        _,
        _,
        normed_one_far,
        heads_far,
        grad_hidden,
        grad_attn,
        projected,
        grad_attn_far,
        branch,
        normed_two,
        activation,
        grad_gate_in,
        grad_up_in,
        gain_two_half,
        cotangent_others,
        normed_others,
    ) = middle(
        w_query, key_weight, value_weight, w_out, tokens, cotangent,
        attn_gain, mlp_gain, w_gate, w_up, w_down, segments, positions, frequency,
    )
    (
        kept,
        _,
        came,
        down_kept,
        _,
        down_came,
        down_last,
        out_mine,
        out_came,
        proj_mine,
        proj_came,
        grad_input,
        mixed,
        _,
        _,
        _,
        gains,
    ) = last(
        normed_others, cotangent_others, normed_two, cotangent, activation, grad_gate_in,
        grad_up_in, w_gate, w_up, w_down, projected, branch, gain_two_half, w_query, key_weight,
        value_weight, head_outputs, grad_attn, grad_attn_far, normed_one, normed_one_far,
        heads_far, grad_hidden, tokens, attn_gain,
    )
    pairs = [(i, i ^ 2) for i in range(lax.axis_size("dp"))]
    last_came = lax.ppermute(down_last, "dp", pairs)
    (
        grad_w_gate,
        grad_w_up,
        grad_w_down,
        grad_w_out,
        grad_w_query,
        grad_w_key,
        grad_w_value,
        grad_input,
        mixed,
        grad_attn_gain,
        grad_mlp_gain,
    ) = finish(
        kept, came, down_kept, down_came, out_mine, out_came, proj_mine, proj_came, grad_input,
        mixed, gains,
    )
    done = grad_w_down.shape[0] - LAST * TILE
    grad_w_down = lax.dynamic_update_slice(grad_w_down, down_kept[done:] + last_came, (done, 0))
    grad_attn_gain, grad_mlp_gain = grad_attn_gain[0], grad_mlp_gain[0]
    return (
        mixed,
        grad_input,
        grad_attn_gain,
        grad_w_query,
        grad_w_key,
        grad_w_value,
        grad_w_out,
        grad_mlp_gain,
        grad_w_gate,
        grad_w_up,
        grad_w_down,
    )


def product(left_matrix, right_matrix):
    return jnp.dot(left_matrix, right_matrix, preferred_element_type=F32)


def over_rows(left_matrix, right_matrix):
    return lax.dot_general(
        left_matrix, right_matrix, (((0,), (0,)), ((), ())), preferred_element_type=F32
    )


def against(gradient, weight):
    return lax.dot_general(
        gradient, weight, (((1,), (1,)), ((), ())), preferred_element_type=F32
    )


def narrowed(value):
    return jnp.where(value == value, value, 0.0).astype(BF16)


def swap(value, axis, bit):
    size = lax.axis_size(axis)
    return lax.ppermute(value, axis, [(i, i ^ bit) for i in range(size)])


def half_of(value, which, dim=0):
    size = value.shape[dim] // 2
    return lax.dynamic_slice_in_dim(value, which * size, size, dim)


def joined(mine, other, which):
    first = jnp.where(which == 0, mine, other)
    second = jnp.where(which == 0, other, mine)
    return jnp.concatenate([first, second], axis=0)


def tensor_sum_half(partial, core):
    total = half_of(partial, core) + swap(half_of(partial, 1 - core), "tensor", 1)
    bit = 2
    while bit < lax.axis_size("tensor"):
        total = total + swap(total, "tensor", bit)
        bit *= 2
    return total


def tables(places):
    half_dim = HEAD_SIZE // 2
    frequency = 500000.0 ** (-(jnp.arange(half_dim).astype(F32) * 2.0 / HEAD_SIZE))
    angles = places.astype(F32)[..., None] * frequency
    cosine_lookup = jnp.cos(angles)
    sine_lookup = jnp.sin(angles)
    return (
        jnp.concatenate([cosine_lookup, cosine_lookup], -1),
        jnp.concatenate([sine_lookup, sine_lookup], -1),
    )


def apply_rotary(field, cosine_lookup, sine_lookup):
    half_dim = HEAD_SIZE // 2
    turned = jnp.concatenate([-field[..., half_dim:], field[..., :half_dim]], -1)
    return field * cosine_lookup + turned * sine_lookup


def unrotate(gradient, cosine_lookup, sine_lookup):
    half_dim = HEAD_SIZE // 2
    sined = gradient * sine_lookup
    return gradient * cosine_lookup + jnp.concatenate(
        [sined[..., half_dim:], -sined[..., :half_dim]], -1
    )


def allowed_pairs(segment):
    spots = jnp.arange(segment.shape[0])
    return (spots[:, None] >= spots[None, :]) & (segment[:, None] == segment[None, :])


def scores(query_rotated, key_rotated, segment):
    raw_scores = jnp.einsum(
        "qhgd,khd->hgqk", query_rotated, key_rotated, preferred_element_type=F32
    ) * HEAD_SIZE ** (-0.5)
    return jnp.where(allowed_pairs(segment), raw_scores, MASKED)


def attend_forward(query_rotated, key_rotated, value_seq, segment):
    masked = scores(query_rotated, key_rotated, segment)
    row_peak = jnp.max(masked, axis=-1, keepdims=True)
    log_total = row_peak + jnp.log(jnp.sum(jnp.exp(masked - row_peak), axis=-1, keepdims=True))
    attention_probs = jnp.exp(masked - log_total).astype(BF16)
    combined_heads = jnp.einsum(
        "ojus,sov->uojv", attention_probs, value_seq, preferred_element_type=F32
    )
    return (combined_heads, log_total)


def attend_backward(query_rotated, key_rotated, value_seq, segment, log_total, grad_heads):
    masked = scores(query_rotated, key_rotated, segment)
    attention_probs = jnp.exp(masked - log_total)
    grad_probs = jnp.einsum("qhgd,khd->hgqk", grad_heads, value_seq, preferred_element_type=F32)
    row_sum = jnp.sum(attention_probs * grad_probs, axis=-1, keepdims=True)
    grad_raw = jnp.where(
        allowed_pairs(segment), attention_probs * (grad_probs - row_sum), 0.0
    ).astype(BF16)
    factor = HEAD_SIZE ** (-0.5)
    grad_query_rot = (
        jnp.einsum("ojus,sov->uojv", grad_raw, key_rotated, preferred_element_type=F32) * factor
    )
    grad_key_rot = (
        jnp.einsum("hgqk,qhgd->khd", grad_raw, query_rotated, preferred_element_type=F32) * factor
    )
    grad_value_rot = jnp.einsum(
        "hgqk,qhgd->khd", attention_probs.astype(BF16), grad_heads, preferred_element_type=F32
    )
    return (grad_query_rot, grad_key_rot, grad_value_rot)


def per_sequence(step, *fields):
    results = [step(*[field[s] for field in fields]) for s in range(fields[0].shape[0])]
    return [jnp.stack(parts) for parts in zip(*results)]


def general_body(
    tokens,
    segments,
    positions,
    attn_gain,
    w_query,
    key_weight,
    value_weight,
    w_out,
    mlp_gain,
    w_gate,
    w_up,
    w_down,
    cotangent,
):
    groups = lax.axis_size("dp")
    place = lax.axis_index("dp")
    core = lax.axis_index("tensor") % 2
    all_bits = [1 << i for i in range(groups.bit_length() - 1)]
    shared_bits = [bit for bit in (4, 1) if bit < groups]
    split_bits = [bit for bit in all_bits if bit not in shared_bits]

    def gathered(half):
        parts = [half]
        for bit in shared_bits:
            parts = parts + [swap(part, "dp", bit) for part in parts]
        others = parts[1:]
        twins = [swap(part, "tensor", 1) for part in others]
        return jnp.concatenate([narrowed(part) for part in others + twins], axis=0)

    def blocks(matrix, offsets):
        width = matrix.shape[1] // groups
        return [
            lax.dynamic_slice_in_dim(matrix, (place ^ offset) * width, width, 1)
            for offset in offsets
        ]

    def offsets_of(bits):
        found = [0]
        for bit in bits:
            found = found + [offset + bit for offset in found]
        return found

    def reduced(matrix_of, bits):
        sent = None
        for bit in bits:
            rest = bits[bits.index(bit) + 1 :]
            offsets = offsets_of(rest)
            if sent is None:
                away = matrix_of([offset ^ bit for offset in offsets])
                home = matrix_of(offsets)
            else:
                away = [sent[offset ^ bit] for offset in offsets]
                home = [sent[offset] for offset in offsets]
            came = swap(away, "dp", bit)
            sent = {offset: h + c for offset, h, c in zip(offsets, home, came)}
        return sent[0]

    inputs = tokens.astype(F32)
    row_count, width = inputs.shape
    seq_count, seq_len = segments.shape
    query_heads = w_query.shape[1] // HEAD_SIZE
    kv_heads = key_weight.shape[1] // HEAD_SIZE
    group_size = query_heads // kv_heads
    query_width, kv_width = w_query.shape[1], key_weight.shape[1]

    cotangent_half = half_of(cotangent, core).astype(F32)
    cotangent_others = gathered(cotangent_half)

    scale_one = lax.rsqrt(jnp.mean(inputs * inputs, axis=-1, keepdims=True) + EPSILON)
    normed_one = (inputs * scale_one * attn_gain).astype(BF16)
    cosine_lookup, sine_lookup = tables(positions.reshape(row_count))
    cosine_lookup = cosine_lookup[:, None, :]
    sine_lookup = sine_lookup[:, None, :]
    query_projected = product(normed_one, w_query).reshape(row_count, query_heads, HEAD_SIZE)
    key_projected = product(normed_one, key_weight).reshape(row_count, kv_heads, HEAD_SIZE)
    query_rotated = (
        apply_rotary(query_projected, cosine_lookup, sine_lookup)
        .astype(BF16)
        .reshape(seq_count, seq_len, kv_heads, group_size, HEAD_SIZE)
    )
    key_rotated = (
        apply_rotary(key_projected, cosine_lookup, sine_lookup)
        .astype(BF16)
        .reshape(seq_count, seq_len, kv_heads, HEAD_SIZE)
    )
    value_projected = (
        product(normed_one, value_weight)
        .astype(BF16)
        .reshape(seq_count, seq_len, kv_heads, HEAD_SIZE)
    )
    combined_heads, log_totals = per_sequence(
        attend_forward, query_rotated, key_rotated, value_projected, segments
    )
    head_outputs = combined_heads.reshape(row_count, query_width).astype(BF16)

    inputs_half = half_of(inputs, core)
    hidden = inputs_half + tensor_sum_half(product(head_outputs, w_out), core)
    scale_two = lax.rsqrt(jnp.mean(hidden * hidden, axis=-1, keepdims=True) + EPSILON)
    normed_half = (hidden * scale_two * mlp_gain).astype(BF16)
    normed_sent = normed_half.astype(F32)
    normed_twin = narrowed(swap(normed_sent, "tensor", 1))
    normed_two = joined(normed_half, normed_twin, core)
    normed_others = gathered(normed_sent)

    def feed_forward(normed, incoming):
        gate_proj = product(normed, w_gate)
        up_proj = product(normed, w_up)
        grad_activation = against(incoming, w_down)
        sigmoid_gate = jax.nn.sigmoid(gate_proj)
        swish_gate = gate_proj * sigmoid_gate
        activation = (swish_gate * up_proj).astype(BF16)
        grad_gate_in = (
            grad_activation * up_proj * sigmoid_gate * (1.0 + gate_proj * (1.0 - sigmoid_gate))
        ).astype(BF16)
        grad_up_in = (grad_activation * swish_gate).astype(BF16)
        return activation, grad_gate_in, grad_up_in

    activation, grad_gate_in, grad_up_in = feed_forward(normed_two, cotangent)
    grad_normed_two = tensor_sum_half(
        against(grad_gate_in, w_gate) + against(grad_up_in, w_up), core
    )
    mixed_half = hidden + tensor_sum_half(product(activation, w_down), core)
    mixed = joined(mixed_half.astype(BF16), narrowed(swap(mixed_half, "tensor", 1)), core)

    weighted = grad_normed_two * mlp_gain
    inner_mean = jnp.mean(weighted * hidden, axis=-1, keepdims=True)
    back_two = scale_two * weighted - hidden * (scale_two * scale_two * scale_two) * inner_mean
    gain_two_half = jnp.sum(grad_normed_two * hidden * scale_two, axis=0)
    grad_hidden = cotangent_half + back_two
    attn_half = grad_hidden.astype(BF16)
    attn_twin = narrowed(swap(grad_hidden, "tensor", 1))
    grad_attn = joined(attn_half, attn_twin, core)

    grad_heads = (
        against(grad_attn, w_out)
        .astype(BF16)
        .reshape(seq_count, seq_len, kv_heads, group_size, HEAD_SIZE)
    )
    grad_query_rot, grad_key_rot, grad_value_rot = per_sequence(
        attend_backward,
        query_rotated,
        key_rotated,
        value_projected,
        segments,
        log_totals,
        grad_heads,
    )
    grad_query_in = (
        unrotate(
            grad_query_rot.reshape(row_count, query_heads, HEAD_SIZE), cosine_lookup, sine_lookup
        )
        .reshape(row_count, query_width)
        .astype(BF16)
    )
    grad_key_in = (
        unrotate(grad_key_rot.reshape(row_count, kv_heads, HEAD_SIZE), cosine_lookup, sine_lookup)
        .reshape(row_count, kv_width)
        .astype(BF16)
    )
    grad_value_in = grad_value_rot.reshape(row_count, kv_width).astype(BF16)
    partial_one = (
        against(grad_query_in, w_query)
        + against(grad_key_in, key_weight)
        + against(grad_value_in, value_weight)
    )
    grad_normed_one = tensor_sum_half(partial_one, core)
    scale_one = half_of(scale_one, core)
    weighted = grad_normed_one * attn_gain
    inner_mean = jnp.mean(weighted * inputs_half, axis=-1, keepdims=True)
    back_one = scale_one * weighted - inputs_half * (scale_one * scale_one * scale_one) * inner_mean
    gain_one_half = jnp.sum(grad_normed_one * inputs_half * scale_one, axis=0)
    input_half = grad_hidden + back_one
    grad_input = joined(input_half, swap(input_half, "tensor", 1), core)

    activation_o, grad_gate_o, grad_up_o = feed_forward(normed_others, cotangent_others)

    def rows_of(left, left_others, right, right_others):
        def term(offsets):
            ours = blocks(left, offsets)
            theirs = blocks(left_others, offsets)
            return [
                over_rows(a, right) + over_rows(b, right_others) for a, b in zip(ours, theirs)
            ]

        return reduced(term, split_bits)

    def columns_of(left, left_others, right, right_others):
        def term(offsets):
            ours = blocks(right, offsets)
            theirs = blocks(right_others, offsets)
            return [
                over_rows(left, a) + over_rows(left_others, b) for a, b in zip(ours, theirs)
            ]

        return reduced(term, split_bits)

    grad_w_down = columns_of(activation, activation_o, cotangent, cotangent_others)
    grad_w_gate = rows_of(normed_two, normed_others, grad_gate_in, grad_gate_o)
    grad_w_up = rows_of(normed_two, normed_others, grad_up_in, grad_up_o)

    grad_w_out = reduced(
        lambda offsets: [over_rows(head_outputs, b) for b in blocks(grad_attn, offsets)], all_bits
    )
    projected = jnp.concatenate([grad_query_in, grad_key_in, grad_value_in], axis=1)
    grad_w_proj = reduced(
        lambda offsets: [over_rows(b, projected) for b in blocks(normed_one, offsets)], all_bits
    )
    grad_w_query = grad_w_proj[:, :query_width]
    grad_w_key = grad_w_proj[:, query_width : query_width + kv_width]
    grad_w_value = grad_w_proj[:, query_width + kv_width :]

    gains = jnp.stack([gain_one_half, gain_two_half])
    gains = gains + swap(gains, "tensor", 1)
    gains = reduced(lambda offsets: blocks(gains, offsets), all_bits)
    grad_attn_gain, grad_mlp_gain = gains[0], gains[1]
    return (
        mixed,
        grad_input,
        grad_attn_gain,
        grad_w_query,
        grad_w_key,
        grad_w_value,
        grad_w_out,
        grad_mlp_gain,
        grad_w_gate,
        grad_w_up,
        grad_w_down,
    )


def solution(mesh):
    placed = (
        P("dp", None),
        P("dp", None),
        P("dp", None),
        P(),
        P(None, "tensor"),
        P(None, "tensor"),
        P(None, "tensor"),
        P("tensor", None),
        P(),
        P(None, "tensor"),
        P(None, "tensor"),
        P("tensor", None),
        P("dp", None),
    )
    fits = mesh.shape["dp"] == 8 and mesh.shape["tensor"] == 4
    return jax.shard_map(
        body if fits else general_body,
        mesh=mesh,
        in_specs=placed,
        out_specs=(
            P("dp", None),
            P("dp", None),
            P("dp"),
            P("dp", "tensor"),
            P("dp", "tensor"),
            P("dp", "tensor"),
            P("tensor", "dp"),
            P("dp"),
            P("dp", "tensor"),
            P("dp", "tensor"),
            P("tensor", "dp"),
        ),
        check_vma=False,
    )
```

```python
import functools

import jax
import jax.numpy as jnp
from jax import lax
from jax.experimental import pallas as pl
from jax.experimental.pallas import tpu as pltpu
from jax.sharding import PartitionSpec as P

HEAD_SIZE = 64
EPSILON = 1e-05
MASKED = -1e30
F32 = jnp.float32
BF16 = jnp.bfloat16


MESH = pl.DeviceIdType.MESH
CHUNKS = 4
TILE = 256
ROWS = 16


def flip(index, bit):
    return index + bit * (1 - 2 * ((index // bit) % 2))


def loop(count, step):
    lax.fori_loop(0, count, lambda i, carry: (step(i), carry)[1], 0)


def middle_kernel(
    w_query_ref,
    w_key_ref,
    w_value_ref,
    w_out_ref,
    tokens_ref,
    cot_ref,
    gain_one_ref,
    gain_ref,
    w_gate_ref,
    w_up_ref,
    w_down_ref,
    segment_ref,
    position_ref,
    frequency_ref,
    normed_one_out,
    heads_out,
    query_ref,
    keys_ref,
    values_ref,
    normed_one_far,
    heads_far,
    grad_hidden_out,
    grad_attn_out,
    projected_out,
    grad_attn_far,
    branch_out,
    normed_out,
    activation_out,
    grad_gate_out,
    grad_up_out,
    gain_out,
    cot_others,
    normed_others,
    gate_w,
    up_w,
    down_w,
    cot,
    cot_half,
    normed,
    normed_sent,
    normed_twin,
    act,
    gg,
    gu,
    away,
    mine,
    core_in,
    y_in,
    product,
    log_total_ref,
    segment_column,
    cosine_ref,
    sine_ref,
    local_sem,
    core_send,
    core_recv,
    y_send,
    y_recv,
    cot_send,
    cot_recv,
    n_send,
    n_recv,
    twin_send,
    twin_recv,
    hidden_send,
    hidden_recv,
    far_send,
    far_recv,
    free_sem,
):
    dp, tensor = lax.axis_index("dp"), lax.axis_index("tensor")
    core, y_bit = tensor % 2, (tensor // 2) % 2
    z_low = (dp // 2) % 2
    twin_id = (dp, flip(tensor, 1))
    y_id = (dp, flip(tensor, 2))
    x_id = (flip(dp, 1), tensor)
    z_id = (flip(dp, 4), tensor)
    far_id = (flip(dp, 2), tensor)
    half, width = cot_half.shape
    run = half // 2
    row_count = 2 * half
    hidden_units = gate_w.shape[1]
    query_width = w_query_ref.shape[1]
    tiles = width // TILE
    chunk = half // CHUNKS
    transposed = (((1,), (1,)), ((), ()))
    everything = slice(None)
    heads = gg.at[:, pl.ds(0, query_width)]
    tok = gu
    hidden = core_in.at[0]

    def own_row(block, which):
        return pl.multiple_of(block * half + which * run, run)

    def own_chunk(k, which):
        return own_row(k // 2, which) + (k % 2) * chunk

    def remote(src, dst, send, recv, device):
        return pltpu.make_async_remote_copy(
            src_ref=src, dst_ref=dst, send_sem=send, recv_sem=recv,
            device_id=device, device_id_type=MESH,
        )

    loads = {
        "tok": pltpu.make_async_copy(tokens_ref, tok, local_sem.at[0]),
        "query": pltpu.make_async_copy(
            w_query_ref, gate_w.at[:, pl.ds(0, query_width)], local_sem.at[1]
        ),
        "key": pltpu.make_async_copy(
            w_key_ref, gate_w.at[:, pl.ds(query_width, 128)], local_sem.at[2]
        ),
        "value": pltpu.make_async_copy(
            w_value_ref, gate_w.at[:, pl.ds(query_width + 128, 128)], local_sem.at[3]
        ),
        "w_out": pltpu.make_async_copy(w_out_ref, cot, local_sem.at[4]),
        "up": pltpu.make_async_copy(w_up_ref, up_w, local_sem.at[5]),
        "down": pltpu.make_async_copy(w_down_ref, down_w, local_sem.at[6]),
        "gate": pltpu.make_async_copy(w_gate_ref, gate_w, local_sem.at[7]),
        "cot": pltpu.make_async_copy(cot_ref, cot, local_sem.at[8]),
        "cot_0": pltpu.make_async_copy(
            cot_ref.at[pl.ds(own_row(0, core), run)], act.at[pl.ds(0, run)], local_sem.at[10]
        ),
        "cot_1": pltpu.make_async_copy(
            cot_ref.at[pl.ds(own_row(1, core), run)], act.at[pl.ds(run, run)], local_sem.at[11]
        ),
    }
    for name in ("cot_0", "cot_1", "tok", "query", "key", "value", "w_out", "up", "down"):
        loads[name].start()

    barrier = pltpu.get_barrier_semaphore()
    for device in (twin_id, y_id, x_id, z_id, far_id):
        pl.semaphore_signal(barrier, inc=1, device_id=device, device_id_type=MESH)
    loads["cot_0"].wait()
    loads["cot_1"].wait()

    def widen(i):
        window = pl.ds(pl.multiple_of(i * ROWS, ROWS), ROWS)
        cot_half[window, :] = act[window, :].astype(F32)

    loop(half // ROWS, widen)
    pl.semaphore_wait(barrier, 5)

    def rows(k):
        return pl.ds(pl.multiple_of(k * chunk, chunk), chunk)

    def from_x(source, slots, k, send, recv):
        return remote(source.at[rows(k)], slots.at[0, rows(k)], send.at[0, k], recv.at[0, k], x_id)

    def from_z(source, slots, k, send, recv):
        return remote(source.at[rows(k)], slots.at[1, rows(k)], send.at[1, k], recv.at[1, k], z_id)

    def from_zx(slots, k, send, recv):
        return remote(
            slots.at[1, rows(k)], slots.at[2, rows(k)], send.at[2, k], recv.at[2, k], x_id
        )

    def to_twin(slots, which, slot):
        return remote(
            slots.at[slot], slots.at[3 + slot],
            twin_send.at[which, slot], twin_recv.at[which, slot], twin_id,
        )

    half_chunk = pl.ds(pl.multiple_of((2 + y_bit) * chunk, chunk), chunk)

    def last_z():
        return remote(
            normed_sent.at[half_chunk], normed_others.at[1, half_chunk],
            n_send.at[1, 2], n_recv.at[1, 2], z_id,
        )

    def last_y():
        return remote(
            normed_others.at[1, half_chunk], normed_others.at[1, half_chunk],
            n_send.at[1, 3], n_recv.at[1, 3], y_id,
        )

    def half_to_twin(slots, which, part, window):
        return remote(
            slots.at[1, window], slots.at[4, window],
            twin_send.at[which, 1 + part], twin_recv.at[which, 1 + part], twin_id,
        )

    first_run, last_run = pl.ds(0, run), pl.ds(run, run)
    other_quarter = pl.ds(pl.multiple_of((1 - y_bit) * run, run), run)
    quarter = pl.ds(pl.multiple_of(y_bit * run, run), run)

    def quarter_z():
        return remote(
            cot_half.at[quarter], cot_others.at[1, quarter],
            cot_send.at[1, 0], cot_recv.at[1, 0], z_id,
        )

    def quarter_zx():
        return remote(
            cot_others.at[1, quarter], cot_others.at[2, quarter],
            cot_send.at[2, 0], cot_recv.at[2, 0], x_id,
        )

    def quarter_y():
        return remote(
            cot_others.at[1, quarter], cot_others.at[1, quarter],
            cot_send.at[1, 1], cot_recv.at[1, 1], y_id,
        )

    quarter_z().start()
    for k in range(CHUNKS):
        from_x(cot_half, cot_others, k, cot_send, cot_recv).start()

    def far_columns(b):
        return pl.ds(pl.multiple_of(b * 1024 + (1 - z_low) * 512, 512), 512)

    gain_one = gain_one_ref[...]
    segments = segment_ref[...].astype(F32)
    segment_column[...] = jnp.broadcast_to(segments, (8, row_count)).T
    loads["tok"].wait()

    def first_norm(block):
        def step(i):
            window = pl.ds(pl.multiple_of(block * half + i * ROWS, ROWS), ROWS)
            values = tok[window, :].astype(F32)
            scale = lax.rsqrt(jnp.mean(values * values, axis=-1, keepdims=True) + EPSILON)
            normed[window, :] = (values * scale * gain_one).astype(BF16)

        loop(half // ROWS, step)

    normed_one_store = pltpu.make_async_copy(normed, normed_one_out, local_sem.at[9])

    def stage_far(block):
        def step(i):
            window = pl.ds(pl.multiple_of(block * run + i * ROWS, ROWS), ROWS)
            here = pl.ds(pl.multiple_of(own_row(block, core) + i * ROWS, ROWS), ROWS)
            for b in range(2):
                core_in[2, window, pl.ds(b * 512, 512)] = normed[here, far_columns(b)].astype(F32)

        loop(run // ROWS, step)

    normed_one_copy = remote(
        core_in.at[2, :, pl.ds(0, 1024)], normed_one_far.at[0],
        far_send.at[0], far_recv.at[0], far_id,
    )

    places = jnp.broadcast_to(position_ref[...].astype(F32), (8, row_count)).T

    def make_tables(block):
        window = pl.ds(block * half, half)
        angles = places[block * half : (block + 1) * half, 0:1] * frequency_ref[...]
        cosine_ref[window, :] = jnp.cos(angles)
        sines = jnp.sin(angles)
        signs = lax.broadcasted_iota(jnp.int32, (half, 128), 1) % 64 < 32
        sine_ref[window, :] = jnp.where(signs, sines, -sines)

    lane = lax.broadcasted_iota(jnp.int32, (TILE, 128), 1)
    factor = HEAD_SIZE ** (-0.5)

    def turn(value):
        return jnp.where(lane % 64 < 32, pltpu.roll(value, 96, 1), pltpu.roll(value, 32, 1))

    def rotate_tile(value, window):
        return value * cosine_ref[window, :] - turn(value) * sine_ref[window, :]

    def unrotate_tile(value, window):
        return value * cosine_ref[window, :] + turn(value) * sine_ref[window, :]

    def project_in(block):
        window = pl.ds(block * TILE, TILE)

        def query_tile(j):
            projection = jnp.dot(
                normed[window, :],
                gate_w[:, pl.ds(pl.multiple_of(j * TILE, TILE), TILE)],
                preferred_element_type=F32,
            )
            for part in range(2):
                act[window, pl.ds(pl.multiple_of(j * TILE + part * 128, 128), 128)] = rotate_tile(
                    projection[:, part * 128 : (part + 1) * 128], window
                ).astype(BF16)

        loop(query_width // TILE, query_tile)
        projection = jnp.dot(
            normed[window, :], gate_w[:, pl.ds(query_width, TILE)], preferred_element_type=F32
        )
        for base, value in (
            (1024, rotate_tile(projection[:, :128], window)),
            (1536, projection[:, 128:]),
        ):
            other = pltpu.roll(value, 64, 1)
            halves_of = (
                jnp.where(lane < 64, value, 0.0),
                jnp.where(lane >= 64, other, 0.0),
                jnp.where(lane < 64, other, 0.0),
                jnp.where(lane >= 64, value, 0.0),
            )
            for i, padded in enumerate(halves_of):
                act[window, pl.ds(base + i * 128, 128)] = padded.astype(BF16)

    def allowed_of(block):
        keys_seen = (block + 1) * TILE
        window = pl.ds(block * TILE, TILE)
        key_place = lax.broadcasted_iota(jnp.int32, (keys_seen, TILE), 0)
        query_place = lax.broadcasted_iota(jnp.int32, (keys_seen, TILE), 1) + block * TILE
        return (key_place <= query_place) & (
            segment_column[pl.ds(0, keys_seen), pl.ds(0, 1)] == segments[:, block * TILE : (block + 1) * TILE]
        )

    def attend(block, p):
        kv = p // 2
        column = pl.multiple_of(p * 128, 128)
        window = pl.ds(block * TILE, TILE)
        seen = pl.ds(0, (block + 1) * TILE)
        queries = act[window, pl.ds(column, 128)]
        allowed = allowed_of(block)
        result = jnp.zeros((TILE, 128), F32)
        for side in range(2):
            padded = pl.multiple_of((kv * 2 + side) * 128, 128)
            keys = act[seen, pl.ds(pl.multiple_of(1024 + padded, 128), 128)]
            vals = act[seen, pl.ds(pl.multiple_of(1536 + padded, 128), 128)]
            raw = jnp.where(
                allowed,
                lax.dot_general(keys, queries, transposed, preferred_element_type=F32) * factor,
                MASKED,
            )
            peak = jnp.max(raw, axis=0, keepdims=True)
            lifted = jnp.exp(raw - peak)
            summed = jnp.sum(lifted, axis=0, keepdims=True)
            log_total_ref[pl.ds(2 * p + side, 1), window] = peak + jnp.log(summed)
            result = result + lax.dot_general(
                (lifted * (1.0 / summed)).astype(BF16), vals, (((0,), (0,)), ((), ())),
                preferred_element_type=F32,
            )
        heads[window, pl.ds(column, 128)] = result.astype(BF16)

    def core_copy(which, window, k):
        return remote(
            away.at[window], core_in.at[min(which, 1)].at[window],
            core_send.at[which, k], core_recv.at[which, k], twin_id,
        )

    def y_copy(which, window, k):
        return remote(
            mine.at[which].at[window], y_in.at[which].at[window],
            y_send.at[which, k], y_recv.at[which, k], y_id,
        )

    def split_tile(which, block, columns, value):
        product[...] = value
        local = pl.ds(block * run, run)
        away[local, columns] = product[pl.ds(pl.multiple_of((1 - core) * run, run), run), :]
        mine[which, local, columns] = product[pl.ds(pl.multiple_of(core * run, run), run), :]

    row_windows = [(rows(k), everything) for k in range(CHUNKS)]

    def tile_of(j):
        return pl.ds(pl.multiple_of(j * TILE, TILE), TILE)

    first_norm(0)
    first_norm(1)
    normed_one_store.start()
    stage_far(0)
    stage_far(1)
    normed_one_copy.start()
    for name in ("query", "key", "value", "w_out"):
        loads[name].wait()
    for block in range(2):
        make_tables(block)
        project_in(block)
        loop(query_width // 128, functools.partial(attend, block))

        def project(j, block=block):
            split_tile(0, block, tile_of(j), jnp.dot(
                heads[pl.ds(block * TILE, TILE), :], cot[:, tile_of(j)],
                preferred_element_type=F32,
            ))

        loop(tiles, project)
        for k in (2 * block, 2 * block + 1):
            core_copy(0, row_windows[k], k).start()
        for k in (2 * block, 2 * block + 1):
            core_copy(0, row_windows[k], k).wait_recv()

            def add(i, k=k):
                window = pl.ds(pl.multiple_of(k * chunk + i * ROWS, ROWS), ROWS)
                mine[0, window, :] = mine[0, window, :] + core_in[0, window, :]

            loop(chunk // ROWS, add)
            y_copy(0, row_windows[k], k).start()
    normed_one_store.wait()
    loads["gate"].start()
    loads["cot"].start()
    keeps = [
        pltpu.make_async_copy(act.at[:, pl.ds(0, 512)], query_ref, local_sem.at[0]),
        pltpu.make_async_copy(act.at[:, pl.ds(1024, 512)], keys_ref, local_sem.at[1]),
        pltpu.make_async_copy(act.at[:, pl.ds(1536, 512)], values_ref, local_sem.at[2]),
        pltpu.make_async_copy(heads, heads_out, local_sem.at[3]),
    ]
    for keep in keeps:
        keep.start()

    def stage_heads(i):
        window = pl.ds(pl.multiple_of(i * ROWS, ROWS), ROWS)
        for b in range(2):
            here = pl.ds(pl.multiple_of(b * half + i * ROWS, ROWS), ROWS)
            core_in[2, window, pl.ds(1024 + b * 512, 512)] = heads[here, :].astype(F32)

    loop(half // ROWS, stage_heads)
    heads_copy = remote(
        core_in.at[2, :, pl.ds(1024, 1024)], heads_far, far_send.at[1], far_recv.at[1], far_id
    )
    heads_copy.start()
    for keep in keeps:
        keep.wait()

    for name in ("cot", "up", "down"):
        loads[name].wait()

    def activation_grad(j):
        gg[:, tile_of(j)] = lax.dot_general(
            cot[...], down_w[tile_of(j), :], transposed, preferred_element_type=F32
        ).astype(BF16)

    loop(hidden_units // TILE, activation_grad)
    loads["gate"].wait()
    gain = gain_ref[...]

    def twin_copy(k):
        return remote(
            normed_sent.at[rows(k)], normed_twin.at[rows(k)],
            n_send.at[3, k], n_recv.at[3, k], twin_id,
        )

    def block_window(block, j):
        return (pl.ds(block * run, run), tile_of(j))

    for block in range(2):
        chunks = (2 * block, 2 * block + 1)
        for k in chunks:
            y_copy(0, row_windows[k], k).wait_recv()

            def normalize_rows(i, k=k):
                window = pl.ds(pl.multiple_of(k * chunk + i * ROWS, ROWS), ROWS)
                here = pl.ds(pl.multiple_of(own_chunk(k, core) + i * ROWS, ROWS), ROWS)
                values = tok[here, :].astype(F32) + (mine[0, window, :] + y_in[0, window, :])
                scale = lax.rsqrt(jnp.mean(values * values, axis=-1, keepdims=True) + EPSILON)
                rounded = (values * scale * gain).astype(BF16)
                hidden[window, :] = values
                normed[here, :] = rounded
                normed_sent[window, :] = rounded.astype(F32)

            loop(chunk // ROWS, normalize_rows)
            twin_copy(k).start()
            if block == 0:
                from_z(normed_sent, normed_others, k, n_send, n_recv).start()
            elif k == 3:
                last_z().start()
            from_x(normed_sent, normed_others, k, n_send, n_recv).start()
        for k in chunks:
            twin_copy(k).wait_recv()

            def take(i, k=k):
                here = pl.ds(pl.multiple_of(own_chunk(k, 1 - core) + i * ROWS, ROWS), ROWS)
                normed[here, :] = normed_twin[
                    pl.ds(pl.multiple_of(k * chunk + i * ROWS, ROWS), ROWS), :
                ].astype(BF16)

            loop(chunk // ROWS, take)
        window = pl.ds(block * TILE, TILE)

        def units(j, window=window):
            columns = tile_of(j)
            gate = jnp.dot(normed[window, :], gate_w[:, columns], preferred_element_type=F32)
            up = jnp.dot(normed[window, :], up_w[:, columns], preferred_element_type=F32)
            back = gg[window, columns].astype(F32)
            sigmoid = jax.nn.sigmoid(gate)
            swish = gate * sigmoid
            act[window, columns] = (swish * up).astype(BF16)
            gg[window, columns] = (
                back * up * sigmoid * (1.0 + gate * (1.0 - sigmoid))
            ).astype(BF16)
            gu[window, columns] = (back * swish).astype(BF16)

        if block == 0:
            loop(hidden_units // TILE, units)
            for k in range(CHUNKS):
                core_copy(0, row_windows[k], k).wait_send()
        else:
            loop(hidden_units // TILE, units)

        def produce(j, block=block, window=window):
            split_tile(1, block, tile_of(j), lax.dot_general(
                gg[window, :], gate_w[tile_of(j), :], transposed, preferred_element_type=F32
            ) + lax.dot_general(
                gu[window, :], up_w[tile_of(j), :], transposed, preferred_element_type=F32
            ))
            core_copy(1, block_window(block, j), block * tiles + j).start()

        def forward(j, block=block):
            where = block_window(block, j)
            core_copy(1, where, block * tiles + j).wait_recv()
            mine[(1,) + where] = mine[(1,) + where] + core_in[(1,) + where]
            y_copy(1, where, block * tiles + j).start()

        def step(j, produce=produce, forward=forward):
            produce(j + 1)
            forward(j)

        produce(0)
        loop(tiles - 1, step)
        forward(tiles - 1)
    stores = [
        pltpu.make_async_copy(normed, normed_out, local_sem.at[7]),
        pltpu.make_async_copy(act, activation_out, local_sem.at[8]),
        pltpu.make_async_copy(gg, grad_gate_out, local_sem.at[9]),
        pltpu.make_async_copy(gu, grad_up_out, local_sem.at[10]),
    ]
    for store in stores:
        store.start()
    pl.semaphore_signal(free_sem, inc=1, device_id=twin_id, device_id_type=MESH)
    quarter_z().wait()
    quarter_zx().start()
    half_to_twin(cot_others, 0, 0, quarter).start()

    for block in range(2):
        loop(tiles, lambda j: core_copy(1, block_window(block, j), block * tiles + j).wait_send())
    for k in range(CHUNKS):
        y_copy(0, row_windows[k], k).wait_send()

    def branch_produce(j):
        for block in range(2):
            split_tile(0, block, tile_of(j), jnp.dot(
                act[pl.ds(block * TILE, TILE), :], down_w[:, tile_of(j)],
                preferred_element_type=F32,
            ))
        core_copy(2, (everything, tile_of(j)), j).start()

    def branch_add(j):
        core_copy(2, (everything, tile_of(j)), j).wait_recv()
        mine[0, :, tile_of(j)] = mine[0, :, tile_of(j)] + core_in[1, :, tile_of(j)]

    def branch_step(j):
        branch_produce(j + 1)
        branch_add(j)

    pl.semaphore_wait(free_sem, 1)
    branch_produce(0)
    loop(tiles - 1, branch_step)
    branch_add(tiles - 1)
    first_y = (1 - y_bit).astype(F32)

    def add_hidden(i):
        window = pl.ds(pl.multiple_of(i * ROWS, ROWS), ROWS)
        mine[0, window, :] = mine[0, window, :] + hidden[window, :] * first_y

    loop(half // ROWS, add_hidden)
    branch_store = pltpu.make_async_copy(mine.at[0], branch_out, local_sem.at[12])
    branch_store.start()

    for store in stores:
        store.wait()
    operands = [
        pltpu.make_async_copy(query_ref, act.at[:, pl.ds(0, 512)], local_sem.at[0]),
        pltpu.make_async_copy(keys_ref, act.at[:, pl.ds(1024, 512)], local_sem.at[1]),
        pltpu.make_async_copy(values_ref, act.at[:, pl.ds(1536, 512)], local_sem.at[2]),
        pltpu.make_async_copy(w_out_ref, gate_w.at[pl.ds(0, 512)], local_sem.at[3]),
    ]
    for operand in operands:
        operand.start()
    for operand in operands:
        operand.wait()

    gain_out[...] = jnp.zeros_like(gain_out)
    sums = y_in.at[0]
    sums[:, pl.ds(0, 1024)] = jnp.zeros((TILE, 1024), F32)

    def hidden_copy(k):
        return remote(
            core_in.at[0, rows(k)], normed_twin.at[rows(k)],
            hidden_send.at[k], hidden_recv.at[k], twin_id,
        )

    def hidden_far(block, b):
        local = pl.ds(block * run, run)
        return remote(
            core_in.at[0, local, far_columns(b)],
            grad_attn_far.at[0, local, pl.ds(b * 512, 512)],
            far_send.at[3 + 2 * block + b], far_recv.at[3 + 2 * block + b], far_id,
        )

    def gather_into(offset, kv, value):
        for part in range(value.shape[0] // TILE):
            columns = pl.ds(pl.multiple_of(offset + kv * 256 + part * 128, 128), 128)
            sums[:, columns] = sums[:, columns] + value[part * TILE : (part + 1) * TILE]

    def put(block, column, value):
        gu[pl.ds(block * TILE, TILE), pl.ds(column, 128)] = value.astype(BF16)

    def attend_back(block, p):
        kv = p // 2
        column = pl.multiple_of(p * 128, 128)
        keys_seen = (block + 1) * TILE
        window = pl.ds(block * TILE, TILE)
        seen = pl.ds(0, keys_seen)
        queries = act[window, pl.ds(column, 128)]
        upstream = act[window, pl.ds(pl.multiple_of(512 + column, 128), 128)]
        allowed = allowed_of(block)
        query_grad = jnp.zeros((TILE, 128), F32)
        for side in range(2):
            padded = pl.multiple_of((kv * 2 + side) * 128, 128)
            keys = act[seen, pl.ds(pl.multiple_of(1024 + padded, 128), 128)]
            vals = act[seen, pl.ds(pl.multiple_of(1536 + padded, 128), 128)]
            raw = lax.dot_general(keys, queries, transposed, preferred_element_type=F32) * factor
            log_total = log_total_ref[pl.ds(2 * p + side, 1), window]
            probs = jnp.exp(jnp.where(allowed, raw - log_total, MASKED))
            grad_probs = lax.dot_general(
                vals, upstream, transposed, preferred_element_type=F32
            )
            row_sum = jnp.sum(probs * grad_probs, axis=0, keepdims=True)
            grad_raw = (probs * (grad_probs - row_sum)).astype(BF16)
            query_grad = query_grad + lax.dot_general(
                grad_raw, keys, (((0,), (0,)), ((), ())), preferred_element_type=F32
            )
            own = (lax.broadcasted_iota(jnp.int32, (keys_seen, 128), 1) // 64) == side
            gather_into(0, kv, jnp.where(
                own, jnp.dot(grad_raw, queries, preferred_element_type=F32), 0.0
            ))
            gather_into(512, kv, jnp.where(
                own, jnp.dot(probs.astype(BF16), upstream, preferred_element_type=F32), 0.0
            ))
        put(block, column, unrotate_tile(query_grad * factor, window))

    for block in range(2):
        loop(tiles, lambda j: y_copy(1, block_window(block, j), block * tiles + j).wait_recv())
        if block == 1:
            quarter_y().start()
        for k in (2 * block, 2 * block + 1):

            def norm_rows(i, k=k):
                window = pl.ds(pl.multiple_of(k * chunk + i * ROWS, ROWS), ROWS)
                here = pl.ds(pl.multiple_of(own_chunk(k, core) + i * ROWS, ROWS), ROWS)
                incoming = mine[1, window, :] + y_in[1, window, :]
                values = hidden[window, :]
                scale = lax.rsqrt(jnp.mean(values * values, axis=-1, keepdims=True) + EPSILON)
                weighted = incoming * gain
                inner = jnp.mean(weighted * values, axis=-1, keepdims=True)
                back = scale * weighted - values * (scale * scale * scale) * inner
                total = cot[here, :].astype(F32) + back
                core_in[0, window, :] = total
                normed[here, :] = total.astype(BF16)
                gain_out[...] = gain_out[...] + jnp.sum(
                    incoming * values * scale, axis=0, keepdims=True
                )

            loop(chunk // ROWS, norm_rows)
            hidden_copy(k).start()
        for b in range(2):
            hidden_far(block, b).start()
        for k in (2 * block, 2 * block + 1):
            hidden_copy(k).wait_recv()

            def take_hidden(i, k=k):
                here = pl.ds(pl.multiple_of(own_chunk(k, 1 - core) + i * ROWS, ROWS), ROWS)
                normed[here, :] = normed_twin[
                    pl.ds(pl.multiple_of(k * chunk + i * ROWS, ROWS), ROWS), :
                ].astype(BF16)

            loop(chunk // ROWS, take_hidden)

        def head_tile(j, block=block):
            window = pl.ds(block * TILE, TILE)
            act[window, pl.ds(pl.multiple_of(512 + j * TILE, TILE), TILE)] = lax.dot_general(
                normed[window, :], gate_w[tile_of(j), :], transposed, preferred_element_type=F32
            ).astype(BF16)

        loop(512 // TILE, head_tile)
        loop(query_width // 128, functools.partial(attend_back, block))
        if block == 0:
            for k in (0, 1):
                from_z(normed_sent, normed_others, k, n_send, n_recv).wait_recv()
                from_zx(normed_others, k, n_send, n_recv).start()
            half_to_twin(normed_others, 1, 0, first_run).start()
            for k in range(CHUNKS):
                from_x(cot_half, cot_others, k, cot_send, cot_recv).wait()
            to_twin(cot_others, 0, 0).start()

    grad_stores = [
        pltpu.make_async_copy(core_in.at[0], grad_hidden_out, local_sem.at[4]),
        pltpu.make_async_copy(normed, grad_attn_out, local_sem.at[5]),
    ]
    for store in grad_stores:
        store.start()

    def both(offset, block):
        def folded(kv):
            value = sums[:, pl.ds(offset + kv * 256 + block * 128, 128)]
            return value + pltpu.roll(value, 64, 1)

        return jnp.where(lane < 64, folded(0), folded(1))

    for block in range(2):
        window = pl.ds(block * TILE, TILE)
        put(block, 512, unrotate_tile(both(0, block) * factor, window))
        put(block, 640, both(512, block))
    projected_store = pltpu.make_async_copy(
        gu.at[:, pl.ds(0, 768)], projected_out, local_sem.at[6]
    )
    projected_store.start()

    last_z().wait()
    last_y().start()
    normed_one_copy.wait()
    normed_one_twin = remote(
        normed_one_far.at[0], normed_one_far.at[1], far_send.at[2], far_recv.at[2], twin_id
    )
    normed_one_twin.start()
    heads_copy.wait()
    for block in range(2):
        for b in range(2):
            hidden_far(block, b).wait()
    hidden_far_twin = remote(
        grad_attn_far.at[0], grad_attn_far.at[1], far_send.at[7], far_recv.at[7], twin_id
    )
    hidden_far_twin.start()
    for k in range(CHUNKS):
        from_x(normed_sent, normed_others, k, n_send, n_recv).wait_recv()
    to_twin(normed_others, 1, 0).start()
    quarter_y().wait()
    half_to_twin(cot_others, 0, 1, other_quarter).start()
    last_y().wait()
    half_to_twin(normed_others, 1, 1, last_run).start()

    for store in grad_stores + [projected_store, branch_store]:
        store.wait()
    for copy in (hidden_far_twin, normed_one_twin, quarter_zx()):
        copy.wait()
    for k in range(CHUNKS):
        hidden_copy(k).wait_send()
        twin_copy(k).wait_send()
        from_x(normed_sent, normed_others, k, n_send, n_recv).wait_send()
    for k in (0, 1):
        from_z(normed_sent, normed_others, k, n_send, n_recv).wait_send()
        from_zx(normed_others, k, n_send, n_recv).wait()
    for block in range(2):
        loop(tiles, lambda j: y_copy(1, block_window(block, j), block * tiles + j).wait_send())
    loop(tiles, lambda j: core_copy(2, (everything, tile_of(j)), j).wait_send())
    to_twin(cot_others, 0, 0).wait()
    to_twin(normed_others, 1, 0).wait()
    half_to_twin(cot_others, 0, 0, quarter).wait()
    half_to_twin(cot_others, 0, 1, other_quarter).wait()
    half_to_twin(normed_others, 1, 0, first_run).wait()
    half_to_twin(normed_others, 1, 1, last_run).wait()


def middle(
    w_query, w_key, w_value, w_out, tokens, cotangent, gain_one, gain,
    w_gate, w_up, w_down, segment, position, frequency,
):
    row_count, width = tokens.shape
    half = row_count // 2
    hidden_units = w_gate.shape[1]
    tiles = width // TILE
    hbm = pl.BlockSpec(memory_space=pl.ANY)
    vmem = pl.BlockSpec(memory_space=pltpu.VMEM)
    wide = jax.ShapeDtypeStruct((half, width), F32)
    units = jax.ShapeDtypeStruct((row_count, hidden_units), BF16)
    square = jax.ShapeDtypeStruct((row_count, 512), BF16)
    dma = pltpu.SemaphoreType.DMA
    return pl.pallas_call(
        middle_kernel,
        out_shape=(
            jax.ShapeDtypeStruct((row_count, width), BF16),
            square, square, square, square,
            jax.ShapeDtypeStruct((2, half, width // 2), F32),
            jax.ShapeDtypeStruct((half, width // 2), F32),
            wide,
            jax.ShapeDtypeStruct((row_count, width), BF16),
            jax.ShapeDtypeStruct((row_count, 768), BF16),
            jax.ShapeDtypeStruct((2, half, width // 2), F32),
            wide,
            jax.ShapeDtypeStruct((row_count, width), BF16),
            units, units, units,
            jax.ShapeDtypeStruct((1, width), F32),
            jax.ShapeDtypeStruct((5, half, width), F32),
            jax.ShapeDtypeStruct((5, half, width), F32),
        ),
        in_specs=[hbm] * 6 + [vmem] * 2 + [hbm] * 3 + [vmem] * 3,
        out_specs=(hbm,) * 16 + (vmem,) + (hbm,) * 2,
        scratch_shapes=[
            pltpu.VMEM(w_gate.shape, BF16),
            pltpu.VMEM(w_up.shape, BF16),
            pltpu.VMEM(w_down.shape, BF16),
            pltpu.VMEM((row_count, width), BF16),
            pltpu.VMEM((half, width), F32),
            pltpu.VMEM((row_count, width), BF16),
            pltpu.VMEM((half, width), F32),
            pltpu.VMEM((half, width), F32),
            pltpu.VMEM((row_count, hidden_units), BF16),
            pltpu.VMEM((row_count, hidden_units), BF16),
            pltpu.VMEM((row_count, hidden_units), BF16),
            pltpu.VMEM((half, width), F32),
            pltpu.VMEM((2, half, width), F32),
            pltpu.VMEM((3, half, width), F32),
            pltpu.VMEM((2, half, width), F32),
            pltpu.VMEM((half, TILE), F32),
            pltpu.VMEM((8, row_count), F32),
            pltpu.VMEM((row_count, 8), F32),
            pltpu.VMEM((row_count, 128), F32),
            pltpu.VMEM((row_count, 128), F32),
            dma((13,)),
            dma((3, 2 * tiles)), dma((3, 2 * tiles)), dma((2, 2 * tiles)), dma((2, 2 * tiles)),
            dma((3, CHUNKS)), dma((3, CHUNKS)),
            dma((4, CHUNKS)), dma((4, CHUNKS)),
            dma((2, 3)), dma((2, 3)),
            dma((CHUNKS,)), dma((CHUNKS,)),
            dma((8,)), dma((8,)),
            pltpu.SemaphoreType.REGULAR,
        ],
        compiler_params=pltpu.CompilerParams(
            collective_id=0, has_side_effects=True, vmem_limit_bytes=64 * 1024 * 1024
        ),
        name="feed_forward",
    )(
        w_query, w_key, w_value, w_out, tokens, cotangent,
        gain_one.reshape(1, width), gain.reshape(1, width), w_gate, w_up, w_down,
        segment.reshape(1, row_count), position.reshape(1, row_count), frequency.reshape(1, 128),
    )


LAST = 2


def last_kernel(
    normed_others_ref,
    cot_others_ref,
    normed_ref,
    cot_ref,
    act_ref,
    gg_ref,
    gu_ref,
    w_gate_ref,
    w_up_ref,
    w_down_ref,
    projected_ref,
    branch_ref,
    gain_two_ref,
    w_query_ref,
    w_key_ref,
    w_value_ref,
    heads_ref,
    grad_attn_ref,
    grad_attn_far_ref,
    normed_one_ref,
    normed_one_far_ref,
    heads_far_ref,
    grad_hidden_ref,
    tokens_ref,
    gain_ref,
    kept_out,
    sent_out,
    came_out,
    down_kept,
    down_sent,
    down_came,
    down_last,
    out_mine,
    out_came,
    proj_mine,
    proj_came,
    input_out,
    mixed_out,
    branch_came,
    normed_late,
    cot_late,
    gain_out,
    normed,
    cot,
    normed_t,
    cot_t,
    units,
    gate_w,
    up_w,
    down_w,
    total,
    staged,
    core_in,
    y_in,
    w_proj,
    tok,
    heads,
    grad_attn,
    normed_one,
    projected,
    out_part,
    proj_part,
    out_x,
    proj_x,
    far_staged,
    far_heads,
    gains,
    gains_came,
    load_sem,
    piece_sem,
    weight_sem,
    unit_sem,
    store_sem,
    row_send,
    row_recv,
    core_send,
    core_recv,
    y_send,
    y_recv,
    x_send,
    x_recv,
    z_send,
    z_recv,
    end_send,
    end_recv,
    gain_send,
    gain_recv,
    late_send,
    late_recv,
    product,
):
    dp, tensor = lax.axis_index("dp"), lax.axis_index("tensor")
    core = tensor % 2
    x_low, z_low, z_high = dp % 2, (dp // 2) % 2, dp // 4
    twin_id = (dp, flip(tensor, 1))
    y_id = (dp, flip(tensor, 2))
    x_id = (flip(dp, 1), tensor)
    z_id = (flip(dp, 4), tensor)
    far_id = (flip(dp, 2), tensor)
    half, width = tok.shape
    row_count = 2 * half
    tiles = width // TILE
    run = half // 2
    y_bit = (tensor // 2) % 2

    def own_row(block, which):
        return pl.multiple_of(block * half + which * run, run)

    everything = slice(None)
    transposed = (((1,), (1,)), ((), ()))
    over = (((0,), (0,)), ((), ()))

    def remote(src, dst, send, recv, device):
        return pltpu.make_async_remote_copy(
            src_ref=src, dst_ref=dst, send_sem=send, recv_sem=recv,
            device_id=device, device_id_type=MESH,
        )

    def tile_of(j):
        return pl.ds(pl.multiple_of(j * TILE, TILE), TILE)

    away_block = tile_of(flip(dp, 2))
    home_block = tile_of(dp)
    near = [
        pl.ds(pl.multiple_of(b * 1024 + z_low * 512, 512), 512) for b in range(2)
    ]
    own_columns = [units.at[0, pl.ds(i * row_count, row_count)] for i in range(4)]
    loads = [
        pltpu.make_async_copy(normed_ref.at[:, away_block], own_columns[0], load_sem.at[0]),
        pltpu.make_async_copy(normed_ref.at[:, home_block], own_columns[1], load_sem.at[1]),
        pltpu.make_async_copy(cot_ref.at[:, away_block], own_columns[2], load_sem.at[2]),
        pltpu.make_async_copy(cot_ref.at[:, home_block], own_columns[3], load_sem.at[3]),
        pltpu.make_async_copy(w_query_ref, w_proj.at[:, pl.ds(0, 512)], load_sem.at[4]),
        pltpu.make_async_copy(w_key_ref, w_proj.at[:, pl.ds(512, 128)], load_sem.at[5]),
        pltpu.make_async_copy(w_value_ref, w_proj.at[:, pl.ds(640, 128)], load_sem.at[6]),
        pltpu.make_async_copy(
            tokens_ref.at[pl.ds(own_row(0, core), run)], tok.at[pl.ds(0, run)], load_sem.at[7]
        ),
        pltpu.make_async_copy(heads_ref, heads.at[0], load_sem.at[8]),
        pltpu.make_async_copy(
            grad_attn_ref.at[:, near[0]], grad_attn.at[0, :, pl.ds(0, 512)], load_sem.at[9]
        ),
        pltpu.make_async_copy(
            grad_attn_ref.at[:, near[1]], grad_attn.at[0, :, pl.ds(512, 512)], load_sem.at[10]
        ),
        pltpu.make_async_copy(
            normed_one_ref.at[:, near[0]], normed_one.at[0, :, pl.ds(0, 512)], load_sem.at[11]
        ),
        pltpu.make_async_copy(
            normed_one_ref.at[:, near[1]], normed_one.at[0, :, pl.ds(512, 512)], load_sem.at[12]
        ),
        pltpu.make_async_copy(projected_ref, projected.at[0], load_sem.at[13]),
        pltpu.make_async_copy(
            tokens_ref.at[pl.ds(own_row(1, core), run)], tok.at[pl.ds(run, run)], load_sem.at[14]
        ),
    ]

    late_normed = pl.ds(run, run)
    early_normed = pl.ds(0, run)
    late_cot = pl.ds(pl.multiple_of((1 - y_bit) * run, run), run)
    early_cot = pl.ds(pl.multiple_of(y_bit * run, run), run)

    def piece_load(i, slot):
        which, part = i // 6, i % 6
        source = (normed_others_ref, cot_others_ref)[which]
        late = (normed_late, cot_late)[which]
        into = staged.at[slot]
        if part in (0, 1, 3, 4):
            return [pltpu.make_async_copy(source.at[part], into, piece_sem.at[slot])]
        if part == 5:
            return [pltpu.make_async_copy(late.at[1], into, piece_sem.at[slot])]
        early_rows = (early_normed, early_cot)[which]
        late_rows = (late_normed, late_cot)[which]
        return [
            pltpu.make_async_copy(
                source.at[2, early_rows], into.at[early_rows], piece_sem.at[slot]
            ),
            pltpu.make_async_copy(
                late.at[0, late_rows], into.at[late_rows], piece_sem.at[2 + slot]
            ),
        ]

    def weight_loads(j, slot):
        return [
            pltpu.make_async_copy(
                w_gate_ref.at[:, tile_of(j)], gate_w.at[slot], weight_sem.at[slot, 0]
            ),
            pltpu.make_async_copy(
                w_up_ref.at[:, tile_of(j)], up_w.at[slot], weight_sem.at[slot, 1]
            ),
            pltpu.make_async_copy(
                w_down_ref.at[tile_of(j), :], down_w.at[slot], weight_sem.at[slot, 2]
            ),
        ]

    order = [0, 1, 3, 4, 6, 7, 9, 10, 2, 8, 5, 11]
    for i in range(2):
        for load in piece_load(order[i], i):
            load.start()
    loads[13].start()
    for load in loads[:4]:
        load.start()
    for load in weight_loads(0, 0):
        load.start()

    barrier = pltpu.get_barrier_semaphore()
    peers = []
    for m in range(1, 8):
        peer = dp
        for bit in (1, 2, 4):
            peer = flip(peer, bit) if m & bit else peer
        peers.append(peer)
    for device in [twin_id, y_id] + [(peer, tensor) for peer in peers]:
        pl.semaphore_signal(barrier, inc=1, device_id=device, device_id_type=MESH)
    pl.semaphore_wait(barrier, 9)
    late_copies = [
        remote(normed_others_ref.at[1, late_normed], normed_late.at[0, late_normed],
               late_send.at[0], late_recv.at[0], x_id),
        remote(cot_others_ref.at[2, early_cot], cot_late.at[0, early_cot],
               late_send.at[1], late_recv.at[1], y_id),
        remote(normed_others_ref.at[2, early_normed], normed_late.at[1, early_normed],
               late_send.at[2], late_recv.at[2], twin_id),
        remote(cot_others_ref.at[2, early_cot], cot_late.at[1, early_cot],
               late_send.at[3], late_recv.at[3], twin_id),
    ]
    for copy in late_copies:
        copy.start()

    loads[13].wait()

    def widen(r):
        window = pl.ds(pl.multiple_of(r * ROWS, ROWS), ROWS)
        for s in range(2):
            there = pl.ds(pl.multiple_of(s * half + r * ROWS, ROWS), ROWS)
            proj_part[0, s, window, :] = projected[0, there, :].astype(F32)

    loop(half // ROWS, widen)
    projected_copy = remote(proj_part.at[0], far_staged, end_send.at[2], end_recv.at[2], far_id)
    projected_copy.start()
    branch_copy = remote(branch_ref, branch_came, end_send.at[1], end_recv.at[1], y_id)

    late_twins = [
        remote(normed_late.at[0, late_normed], normed_late.at[1, late_normed],
               late_send.at[4], late_recv.at[4], twin_id),
        remote(cot_late.at[0, late_cot], cot_late.at[1, late_cot],
               late_send.at[5], late_recv.at[5], twin_id),
    ]
    def take_piece(place):
        i, slot = order[place], place % 2
        for load in piece_load(i, slot):
            load.wait()
        rows_to, turned_to = (normed, normed_t) if i < 6 else (cot, cot_t)
        base = {0: 0, 1: 1, 3: 2, 4: 3, 2: 4, 5: 5}[i % 6] * half

        def convert(r, slot=slot, rows_to=rows_to, base=base):
            window = pl.ds(pl.multiple_of(r * ROWS, ROWS), ROWS)
            rows_to[pl.ds(pl.multiple_of(base + r * ROWS, ROWS), ROWS), :] = staged[
                slot, window, :
            ].astype(BF16)

        loop(half // ROWS, convert)
        for part, block in enumerate((away_block, home_block)):
            turned_to[pl.ds(part * TILE, TILE), pl.ds(row_count + base, half)] = (
                staged[slot, :, block].T.astype(BF16)
            )
        if place == 8:
            for copy in late_copies[2:] + late_twins:
                copy.wait()
        if place + 2 < 8 or 8 <= place < 10:
            for load in piece_load(order[place + 2], slot):
                load.start()
    for place in range(8):
        take_piece(place)
    for part in range(4):
        loads[part].wait()
        turned_to = (normed_t, cot_t)[part // 2]
        turned_to[pl.ds((part % 2) * TILE, TILE), pl.ds(0, row_count)] = (
            own_columns[part][...].astype(F32).T.astype(BF16)
        )

    def row_copy(j):
        window = (everything, everything, tile_of(j))
        return [
            remote(
                sent_out.at[window], came_out.at[window],
                row_send.at[0, j], row_recv.at[0, j], far_id,
            ),
            remote(
                down_sent.at[tile_of(j)], down_came.at[tile_of(j)],
                row_send.at[1, j], row_recv.at[1, j], far_id,
            ),
        ]

    def stores(j, slot):
        return [
            pltpu.make_async_copy(
                total.at[slot, pl.ds(0, 2), pl.ds(0, TILE)], sent_out.at[:, :, tile_of(j)],
                store_sem.at[slot, 0],
            ),
            pltpu.make_async_copy(
                total.at[slot, pl.ds(0, 2), pl.ds(TILE, TILE)], kept_out.at[:, :, tile_of(j)],
                store_sem.at[slot, 1],
            ),
            pltpu.make_async_copy(
                total.at[slot, 2, pl.ds(TILE, TILE)], down_kept.at[tile_of(j)],
                store_sem.at[slot, 3],
            ),
        ]

    def down_store(slot, into):
        return pltpu.make_async_copy(
            total.at[slot, 2, pl.ds(0, TILE)], into, store_sem.at[slot, 2]
        )

    def unit_loads(j):
        return [
            pltpu.make_async_copy(
                source.at[:, tile_of(j)], units.at[i, pl.ds(0, row_count)], unit_sem.at[i]
            )
            for i, source in enumerate((gg_ref, gu_ref, act_ref))
        ]

    def feed_forward_tile(j, first=False):
        slot = j % 2
        for load in weight_loads(j, slot):
            load.wait()

        if first:
            for load in weight_loads(1, 1):
                load.start()
        else:

            @pl.when(j + 1 < tiles)
            def _():
                for load in weight_loads(j + 1, 1 - slot):
                    load.start()

        for load in unit_loads(j):
            load.start()

        def block(m):
            rows = pl.ds(pl.multiple_of(m * 512, 512), 512)
            to = pl.ds(pl.multiple_of(row_count + m * 512, 512), 512)
            gate = jnp.dot(normed[rows, :], gate_w[slot], preferred_element_type=F32)
            up = jnp.dot(normed[rows, :], up_w[slot], preferred_element_type=F32)
            back = lax.dot_general(
                cot[rows, :], down_w[slot], transposed, preferred_element_type=F32
            )
            sigmoid = jax.nn.sigmoid(gate)
            swish = gate * sigmoid
            units[2, to, :] = (swish * up).astype(BF16)
            units[0, to, :] = (back * up * sigmoid * (1.0 + gate * (1.0 - sigmoid))).astype(BF16)
            units[1, to, :] = (back * swish).astype(BF16)

        if first:
            loop(2, block)
            for copy, later in zip(late_copies[:2], late_twins):
                copy.wait()
                later.start()
            branch_copy.start()
            for place in (8, 9):
                for load in piece_load(order[place], place % 2):
                    load.start()
            for place in range(8, 12):
                take_piece(place)
            block(2)
        else:
            loop(normed.shape[0] // 512, block)
        for load in unit_loads(j):
            load.wait()

        total[slot, 0] = jnp.dot(normed_t[...], units[0], preferred_element_type=F32)
        total[slot, 1] = jnp.dot(normed_t[...], units[1], preferred_element_type=F32)
        turned = jnp.dot(cot_t[...], units[2], preferred_element_type=F32)
        for part in range(2):
            total[slot, 2, pl.ds(part * TILE, TILE)] = turned[part * TILE : (part + 1) * TILE].T
        for store in stores(j, slot):
            store.start()
        here = j < tiles - LAST

        @pl.when(here)
        def _():
            store = down_store(slot, down_sent.at[tile_of(j)])
            store.start()
            store.wait()
            row_copy(j)[1].start()

        @pl.when(jnp.logical_not(here))
        def _():
            store = down_store(slot, down_last.at[tile_of(j - (tiles - LAST))])
            store.start()
            store.wait()

        for store in stores(j, slot):
            store.wait()
        row_copy(j)[0].start()

    def x_copies(slot):
        return [
            remote(out_part.at[0, slot], out_x.at[slot], x_send.at[0, slot],
                   x_recv.at[0, slot], x_id),
            remote(proj_part.at[0, slot], proj_x.at[slot], x_send.at[1, slot],
                   x_recv.at[1, slot], x_id),
        ]

    def attention_parts():
        for load in far_loads + loads[8:13]:
            load.wait()
        projected_copy.wait()

        def convert(r):
            window = pl.ds(pl.multiple_of(r * ROWS, ROWS), ROWS)
            block, rest = r // (run // ROWS), r % (run // ROWS)
            for s in range(2):
                which = core if s == 0 else 1 - core
                here = pl.ds(
                    pl.multiple_of(block * half + which * run + rest * ROWS, ROWS), ROWS
                )
                grad_attn[1, here, :] = staged[0, window, pl.ds(s * 1024, 1024)].astype(BF16)
                normed_one[1, here, :] = staged[1, window, pl.ds(s * 1024, 1024)].astype(BF16)
                there = pl.ds(pl.multiple_of(s * half + r * ROWS, ROWS), ROWS)
                projected[1, there, :] = far_staged[s, window, :].astype(BF16)
                heads[1, there, :] = far_heads[window, pl.ds(s * 512, 512)].astype(BF16)

        loop(half // ROWS, convert)
        for side in range(2):
            x_at = 1 - x_low if side == 0 else x_low
            for slot in range(2):
                z_at = 1 - z_high if slot == 0 else z_high
                columns = pl.ds(pl.multiple_of(z_at * 512 + x_at * 256, 256), 256)
                out_part[side, slot] = lax.dot_general(
                    heads[0], grad_attn[0, :, columns], over, preferred_element_type=F32
                ) + lax.dot_general(
                    heads[1], grad_attn[1, :, columns], over, preferred_element_type=F32
                )
                proj_part[side, slot] = lax.dot_general(
                    normed_one[0, :, columns], projected[0], over, preferred_element_type=F32
                ) + lax.dot_general(
                    normed_one[1, :, columns], projected[1], over, preferred_element_type=F32
                )
                if side == 0:
                    for copy in x_copies(slot):
                        copy.start()

    def core_copy(j):
        window = (everything, tile_of(j))
        return remote(
            staged.at[0].at[window], core_in.at[window], core_send.at[j], core_recv.at[j], twin_id
        )

    def y_copy(j):
        window = (everything, tile_of(j))
        return remote(
            staged.at[1].at[window], y_in.at[window], y_send.at[j], y_recv.at[j], y_id
        )

    def attention_sums():
        for load in loads[4:8] + loads[14:]:
            load.wait()

        def produce(j):
            product[...] = lax.dot_general(
                projected[0], w_proj[tile_of(j), :], transposed, preferred_element_type=F32
            )
            for block in range(2):
                for slot, which in ((0, 1 - core), (1, core)):
                    staged[slot, pl.ds(block * run, run), tile_of(j)] = product[
                        pl.ds(own_row(block, which), run), :
                    ]
            core_copy(j).start()

        def forward(j):
            core_copy(j).wait_recv()
            staged[1, :, tile_of(j)] = staged[1, :, tile_of(j)] + core_in[:, tile_of(j)]
            y_copy(j).start()

        produce(0)

        def step(j):
            produce(j + 1)
            forward(j)

        loop(tiles - 1, step)
        forward(tiles - 1)
        loop(tiles, lambda j: core_copy(j).wait_send())

    feed_forward_tile(0, first=True)
    for load in loads[4:13] + loads[14:]:
        load.start()
    far_loads = (
        [
            pltpu.make_async_copy(
                grad_attn_far_ref.at[s], staged.at[0, :, pl.ds(s * 1024, 1024)], piece_sem.at[s]
            )
            for s in range(2)
        ]
        + [
            pltpu.make_async_copy(
                normed_one_far_ref.at[s], staged.at[1, :, pl.ds(s * 1024, 1024)],
                piece_sem.at[2 + s],
            )
            for s in range(2)
        ]
        + [
            pltpu.make_async_copy(heads_far_ref, far_heads, piece_sem.at[5]),
        ]
    )
    for load in far_loads:
        load.start()


    def step(j):
        feed_forward_tile(j + 1)

        @pl.when(j == 0)
        def _():
            attention_parts()
            attention_sums()

    loop(tiles - 1, step)
    hidden_load = pltpu.make_async_copy(grad_hidden_ref, core_in, load_sem.at[0])
    hidden_load.start()

    def z_copies():
        return [
            remote(out_part.at[1, 0], out_came, z_send.at[0], z_recv.at[0], z_id),
            remote(proj_part.at[1, 0], proj_came, z_send.at[1], z_recv.at[1], z_id),
        ]

    for slot in range(2):
        for copy in x_copies(slot):
            copy.wait_recv()
        out_part[1, slot] = out_part[1, slot] + out_x[slot]
        proj_part[1, slot] = proj_part[1, slot] + proj_x[slot]
        if slot == 0:
            for copy in z_copies():
                copy.start()
    part_stores = [
        pltpu.make_async_copy(out_part.at[1, 1], out_mine, load_sem.at[1]),
        pltpu.make_async_copy(proj_part.at[1, 1], proj_mine, load_sem.at[2]),
    ]
    for store in part_stores:
        store.start()

    gain = gain_ref[...]
    gains[pl.ds(0, 1), :] = jnp.zeros_like(gain)
    gains[pl.ds(1, 1), :] = gain_two_ref[...]
    hidden_load.wait()
    loop(tiles, lambda j: y_copy(j).wait_recv())

    def norm_rows(i):
        window = pl.ds(pl.multiple_of(i * ROWS, ROWS), ROWS)
        incoming = staged[1, window, :] + y_in[window, :]
        values = tok[window, :].astype(F32)
        scale = lax.rsqrt(jnp.mean(values * values, axis=-1, keepdims=True) + EPSILON)
        weighted = incoming * gain
        inner = jnp.mean(weighted * values, axis=-1, keepdims=True)
        back = scale * weighted - values * (scale * scale * scale) * inner
        staged[0, window, :] = core_in[window, :] + back
        gains[pl.ds(0, 1), :] = gains[pl.ds(0, 1), :] + jnp.sum(
            incoming * values * scale, axis=0, keepdims=True
        )

    loop(half // ROWS, norm_rows)

    def to_rows(slot, out, sems, first):
        copies, kept = [], []
        for block in range(2):
            local, here = pl.ds(block * run, run), pl.ds(own_row(block, core), run)
            copies.append(remote(
                staged.at[slot, local], out.at[here],
                end_send.at[sems + block], end_recv.at[sems + block], twin_id,
            ))
            kept.append(pltpu.make_async_copy(
                staged.at[slot, local], out.at[here], load_sem.at[first + block]
            ))
        for copy in copies + kept:
            copy.start()
        return copies, kept

    input_copies, input_stores = to_rows(0, input_out, 3, 3)

    gain_twin = remote(gains, gains_came, gain_send.at[7], gain_recv.at[7], twin_id)
    gain_twin.start()

    loop(tiles, lambda j: y_copy(j).wait_send())
    branch_copy.wait()
    branch_loads = [
        pltpu.make_async_copy(branch_ref, staged.at[1], load_sem.at[5]),
        pltpu.make_async_copy(branch_came, y_in, load_sem.at[6]),
    ]
    for load in branch_loads:
        load.start()
    gain_twin.wait()
    gains[...] = gains[...] + gains_came[...]

    def gain_copy(m):
        return remote(
            gains.at[:, tile_of(peers[m])], gain_out.at[m], gain_send.at[m], gain_recv.at[m],
            (peers[m], tensor),
        )

    for m in range(7):
        gain_copy(m).start()
    gain_out[7] = gains[:, tile_of(dp)]
    for load in branch_loads:
        load.wait()

    def mixed_rows(i):
        window = pl.ds(pl.multiple_of(i * ROWS, ROWS), ROWS)
        staged[1, window, :] = staged[1, window, :] + y_in[window, :]

    loop(half // ROWS, mixed_rows)
    mixed_copy = remote(staged.at[1], core_in, end_send.at[5], end_recv.at[5], twin_id)
    mixed_copy.start()

    def put_mixed(source, which, first):
        def narrow(i):
            window = pl.ds(pl.multiple_of(i * ROWS, ROWS), ROWS)
            tok[window, :] = source[window, :].astype(BF16)

        loop(half // ROWS, narrow)
        copies = [
            pltpu.make_async_copy(
                tok.at[pl.ds(block * run, run)], mixed_out.at[pl.ds(own_row(block, which), run)],
                load_sem.at[first + block],
            )
            for block in range(2)
        ]
        for copy in copies:
            copy.start()
        for copy in copies:
            copy.wait()

    put_mixed(staged.at[1], core, 7)
    mixed_copy.wait()
    put_mixed(core_in, 1 - core, 9)

    for copy in part_stores + input_stores + input_copies:
        copy.wait()
    for m in range(7):
        gain_copy(m).wait()
    for slot in range(2):
        for copy in x_copies(slot):
            copy.wait_send()
    for copy in z_copies():
        copy.wait()
    loop(tiles, lambda j: row_copy(j)[0].wait())
    loop(tiles - LAST, lambda j: row_copy(j)[1].wait())


def last(
    normed_others, cot_others, normed, cot, act, gg, gu, w_gate, w_up, w_down,
    projected, branch, gain_two, w_query, w_key, w_value, heads, grad_attn, grad_attn_far,
    normed_one, normed_one_far, heads_far, grad_hidden, tokens, gain,
):
    row_count, width = tokens.shape
    half = row_count // 2
    tiles = width // TILE
    hidden_units = w_gate.shape[1]
    hbm = pl.BlockSpec(memory_space=pl.ANY)
    vmem = pl.BlockSpec(memory_space=pltpu.VMEM)
    wide = jax.ShapeDtypeStruct((half, width), F32)
    rows_pair = jax.ShapeDtypeStruct((2, TILE, hidden_units), F32)
    columns = jax.ShapeDtypeStruct((hidden_units, TILE), F32)
    out_block = jax.ShapeDtypeStruct((512, TILE), F32)
    proj_block = jax.ShapeDtypeStruct((TILE, 768), F32)
    dma = pltpu.SemaphoreType.DMA
    return pl.pallas_call(
        last_kernel,
        out_shape=(
            rows_pair, rows_pair, rows_pair, columns, columns, columns,
            jax.ShapeDtypeStruct((LAST * TILE, TILE), F32), out_block, out_block, proj_block, proj_block,
            jax.ShapeDtypeStruct((row_count, width), F32),
            jax.ShapeDtypeStruct((row_count, width), BF16),
            wide,
            jax.ShapeDtypeStruct((2, half, width), F32),
            jax.ShapeDtypeStruct((2, half, width), F32),
            jax.ShapeDtypeStruct((8, 2, TILE), F32),
        ),
        in_specs=[hbm] * 12 + [vmem] + [hbm] * 11 + [vmem],
        out_specs=(hbm,) * 16 + (vmem,),
        scratch_shapes=[
            pltpu.VMEM((6 * half, width), BF16),
            pltpu.VMEM((6 * half, width), BF16),
            pltpu.VMEM((2 * TILE, row_count + 6 * half), BF16),
            pltpu.VMEM((2 * TILE, row_count + 6 * half), BF16),
            pltpu.VMEM((3, row_count + 6 * half, TILE), BF16),
            pltpu.VMEM((2, width, TILE), BF16),
            pltpu.VMEM((2, width, TILE), BF16),
            pltpu.VMEM((2, TILE, width), BF16),
            pltpu.VMEM((2, 3, 2 * TILE, TILE), F32),
            pltpu.VMEM((2, half, width), F32),
            pltpu.VMEM((half, width), F32),
            pltpu.VMEM((half, width), F32),
            pltpu.VMEM((width, 768), BF16),
            pltpu.VMEM((half, width), BF16),
            pltpu.VMEM((2, row_count, 512), BF16),
            pltpu.VMEM((2, row_count, 1024), BF16),
            pltpu.VMEM((2, row_count, 1024), BF16),
            pltpu.VMEM((2, row_count, 768), BF16),
            pltpu.VMEM((2, 2, 512, TILE), F32),
            pltpu.VMEM((2, 2, TILE, 768), F32),
            pltpu.VMEM((2, 512, TILE), F32),
            pltpu.VMEM((2, TILE, 768), F32),
            pltpu.VMEM((2, half, 768), F32),
            pltpu.VMEM((half, 1024), F32),
            pltpu.VMEM((2, width), F32),
            pltpu.VMEM((2, width), F32),
            dma((15,)), dma((6,)), dma((2, 3)), dma((3,)), dma((2, 4)),
            dma((2, tiles)), dma((2, tiles)),
            dma((tiles,)), dma((tiles,)), dma((tiles,)), dma((tiles,)),
            dma((2, 2)), dma((2, 2)), dma((2,)), dma((2,)), dma((7,)), dma((7,)), dma((8,)), dma((8,)),
            dma((6,)), dma((6,)), pltpu.VMEM((row_count, TILE), F32),
        ],
        compiler_params=pltpu.CompilerParams(
            collective_id=1, has_side_effects=True, vmem_limit_bytes=64 * 1024 * 1024
        ),
        name="weight_gradients",
    )(
        normed_others, cot_others, normed, cot, act, gg, gu, w_gate, w_up, w_down,
        projected, branch, gain_two, w_query, w_key, w_value, heads, grad_attn, grad_attn_far,
        normed_one, normed_one_far, heads_far, grad_hidden, tokens, gain.reshape(1, width),
    )


def finish_kernel(
    kept, came, down_kept, down_came, out_mine, out_came, proj_mine, proj_came, input_in,
    mixed_in, gains, w_gate, w_up, w_down, w_out, w_query, w_key, w_value, grad_input, mixed,
    gain_one, gain_two,
):
    w_gate[...] = kept[0] + came[0]
    w_up[...] = kept[1] + came[1]
    w_down[...] = down_kept[...] + down_came[...]
    w_out[...] = out_mine[...] + out_came[...]
    queries, keys = w_query.shape[1], w_key.shape[1]
    w_query[...] = proj_mine[:, :queries] + proj_came[:, :queries]
    w_key[...] = proj_mine[:, queries : queries + keys] + proj_came[:, queries : queries + keys]
    w_value[...] = proj_mine[:, queries + keys :] + proj_came[:, queries + keys :]
    grad_input[...] = input_in[...]
    mixed[...] = mixed_in[...]
    total = jnp.sum(gains[...], axis=0)
    gain_one[...] = total[0:1]
    gain_two[...] = total[1:2]


def finish(*parts):
    steps = 4
    kept, down, out, proj, whole, gains = (parts[i] for i in (0, 2, 4, 6, 8, 10))
    rows, units = kept.shape[1:]

    def block(array, lead=()):
        size = array[len(lead) :]
        shape = lead + (size[0] // steps,) + size[1:]
        return pl.BlockSpec(shape, lambda i: (0,) * len(lead) + (i,) + (0,) * (len(size) - 1))

    fixed = lambda shape: pl.BlockSpec(shape, lambda i: (0,) * len(shape))
    outs = [
        (rows, units), (rows, units), down.shape, out.shape,
        (proj.shape[0], 512), (proj.shape[0], 128), (proj.shape[0], 128), whole.shape,
    ]
    return pl.pallas_call(
        finish_kernel,
        grid=(steps,),
        out_shape=[jax.ShapeDtypeStruct(shape, F32) for shape in outs]
        + [
            jax.ShapeDtypeStruct(whole.shape, BF16),
            jax.ShapeDtypeStruct((1, gains.shape[2]), F32),
            jax.ShapeDtypeStruct((1, gains.shape[2]), F32),
        ],
        in_specs=[block(kept.shape, (2,))] * 2
        + [block(part.shape) for part in parts[2:10]]
        + [fixed(gains.shape)],
        out_specs=[block(shape) for shape in outs]
        + [block(whole.shape)] + [fixed((1, gains.shape[2]))] * 2,
        compiler_params=pltpu.CompilerParams(vmem_limit_bytes=64 * 1024 * 1024),
        cost_estimate=pl.CostEstimate(
            flops=2_000_000, bytes_accessed=34_000_000, transcendentals=0
        ),
        name="last_sums",
    )(*parts)


def body(
    tokens,
    segments,
    positions,
    attn_gain,
    w_query,
    key_weight,
    value_weight,
    w_out,
    mlp_gain,
    w_gate,
    w_up,
    w_down,
    cotangent,
):
    row_count, width = tokens.shape
    half = row_count // 2
    hidden_units = w_gate.shape[1]
    tiles = width // TILE
    hbm = pl.BlockSpec(memory_space=pl.ANY)
    vmem = pl.BlockSpec(memory_space=pltpu.VMEM)
    wide = jax.ShapeDtypeStruct((half, width), F32)
    units = jax.ShapeDtypeStruct((row_count, hidden_units), BF16)
    square = jax.ShapeDtypeStruct((row_count, 512), BF16)
    dma = pltpu.SemaphoreType.DMA
    return pl.pallas_call(
        middle_kernel,
        out_shape=(
            jax.ShapeDtypeStruct((row_count, width), BF16),
            square, square, square, square,
            jax.ShapeDtypeStruct((2, half, width // 2), F32),
            jax.ShapeDtypeStruct((half, width // 2), F32),
            wide,
            jax.ShapeDtypeStruct((row_count, width), BF16),
            jax.ShapeDtypeStruct((row_count, 768), BF16),
            jax.ShapeDtypeStruct((2, half, width // 2), F32),
            wide,
            jax.ShapeDtypeStruct((row_count, width), BF16),
            units, units, units,
            jax.ShapeDtypeStruct((1, width), F32),
            jax.ShapeDtypeStruct((5, half, width), F32),
            jax.ShapeDtypeStruct((5, half, width), F32),
        ),
        in_specs=[hbm] * 6 + [vmem] * 2 + [hbm] * 3 + [vmem] * 3,
        out_specs=(hbm,) * 16 + (vmem,) + (hbm,) * 2,
        scratch_shapes=[
            pltpu.VMEM(w_gate.shape, BF16),
            pltpu.VMEM(w_up.shape, BF16),
            pltpu.VMEM(w_down.shape, BF16),
            pltpu.VMEM((row_count, width), BF16),
            pltpu.VMEM((half, width), F32),
            pltpu.VMEM((row_count, width), BF16),
            pltpu.VMEM((half, width), F32),
            pltpu.VMEM((half, width), F32),
            pltpu.VMEM((row_count, hidden_units), BF16),
            pltpu.VMEM((row_count, hidden_units), BF16),
            pltpu.VMEM((row_count, hidden_units), BF16),
            pltpu.VMEM((half, width), F32),
            pltpu.VMEM((2, half, width), F32),
            pltpu.VMEM((3, half, width), F32),
            pltpu.VMEM((2, half, width), F32),
            pltpu.VMEM((half, TILE), F32),
            pltpu.VMEM((8, row_count), F32),
            pltpu.VMEM((row_count, 8), F32),
            pltpu.VMEM((row_count, 128), F32),
            pltpu.VMEM((row_count, 128), F32),
            dma((13,)),
            dma((3, 2 * tiles)), dma((3, 2 * tiles)), dma((2, 2 * tiles)), dma((2, 2 * tiles)),
            dma((3, CHUNKS)), dma((3, CHUNKS)),
            dma((4, CHUNKS)), dma((4, CHUNKS)),
            dma((2, 3)), dma((2, 3)),
            dma((CHUNKS,)), dma((CHUNKS,)),
            dma((8,)), dma((8,)),
            pltpu.SemaphoreType.REGULAR,
        ],
        compiler_params=pltpu.CompilerParams(
            collective_id=0, has_side_effects=True, vmem_limit_bytes=64 * 1024 * 1024
        ),
        name="feed_forward",
    )(
        w_query, w_key, w_value, w_out, tokens, cotangent,
        gain_one.reshape(1, width), gain.reshape(1, width), w_gate, w_up, w_down,
        segment.reshape(1, row_count), position.reshape(1, row_count), frequency.reshape(1, 128),
    )


LAST = 2


def last_kernel(
    normed_others_ref,
    cot_others_ref,
    normed_ref,
    cot_ref,
    act_ref,
    gg_ref,
    gu_ref,
    w_gate_ref,
    w_up_ref,
    w_down_ref,
    projected_ref,
    branch_ref,
    gain_two_ref,
    w_query_ref,
    w_key_ref,
    w_value_ref,
    heads_ref,
    grad_attn_ref,
    grad_attn_far_ref,
    normed_one_ref,
    normed_one_far_ref,
    heads_far_ref,
    grad_hidden_ref,
    tokens_ref,
    gain_ref,
    kept_out,
    sent_out,
    came_out,
    down_kept,
    down_sent,
    down_came,
    down_last,
    out_mine,
    out_came,
    proj_mine,
    proj_came,
    input_out,
    mixed_out,
    branch_came,
    normed_late,
    cot_late,
    gain_out,
    normed,
    cot,
    normed_t,
    cot_t,
    units,
    gate_w,
    up_w,
    down_w,
    total,
    staged,
    core_in,
    y_in,
    w_proj,
    tok,
    heads,
    grad_attn,
    normed_one,
    projected,
    out_part,
    proj_part,
    out_x,
    proj_x,
    far_staged,
    far_heads,
    gains,
    gains_came,
    load_sem,
    piece_sem,
    weight_sem,
    unit_sem,
    store_sem,
    row_send,
    row_recv,
    core_send,
    core_recv,
    y_send,
    y_recv,
    x_send,
    x_recv,
    z_send,
    z_recv,
    end_send,
    end_recv,
    gain_send,
    gain_recv,
    late_send,
    late_recv,
    product,
):
    dp, tensor = lax.axis_index("dp"), lax.axis_index("tensor")
    core = tensor % 2
    x_low, z_low, z_high = dp % 2, (dp // 2) % 2, dp // 4
    twin_id = (dp, flip(tensor, 1))
    y_id = (dp, flip(tensor, 2))
    x_id = (flip(dp, 1), tensor)
    z_id = (flip(dp, 4), tensor)
    far_id = (flip(dp, 2), tensor)
    half, width = tok.shape
    row_count = 2 * half
    tiles = width // TILE
    run = half // 2
    y_bit = (tensor // 2) % 2

    def own_row(block, which):
        return pl.multiple_of(block * half + which * run, run)

    everything = slice(None)
    transposed = (((1,), (1,)), ((), ()))
    over = (((0,), (0,)), ((), ()))

    def remote(src, dst, send, recv, device):
        return pltpu.make_async_remote_copy(
            src_ref=src, dst_ref=dst, send_sem=send, recv_sem=recv,
            device_id=device, device_id_type=MESH,
        )

    def tile_of(j):
        return pl.ds(pl.multiple_of(j * TILE, TILE), TILE)

    away_block = tile_of(flip(dp, 2))
    home_block = tile_of(dp)
    near = [
        pl.ds(pl.multiple_of(b * 1024 + z_low * 512, 512), 512) for b in range(2)
    ]
    own_columns = [units.at[0, pl.ds(i * row_count, row_count)] for i in range(4)]
    loads = [
        pltpu.make_async_copy(normed_ref.at[:, away_block], own_columns[0], load_sem.at[0]),
        pltpu.make_async_copy(normed_ref.at[:, home_block], own_columns[1], load_sem.at[1]),
        pltpu.make_async_copy(cot_ref.at[:, away_block], own_columns[2], load_sem.at[2]),
        pltpu.make_async_copy(cot_ref.at[:, home_block], own_columns[3], load_sem.at[3]),
        pltpu.make_async_copy(w_query_ref, w_proj.at[:, pl.ds(0, 512)], load_sem.at[4]),
        pltpu.make_async_copy(w_key_ref, w_proj.at[:, pl.ds(512, 128)], load_sem.at[5]),
        pltpu.make_async_copy(w_value_ref, w_proj.at[:, pl.ds(640, 128)], load_sem.at[6]),
        pltpu.make_async_copy(
            tokens_ref.at[pl.ds(own_row(0, core), run)], tok.at[pl.ds(0, run)], load_sem.at[7]
        ),
        pltpu.make_async_copy(heads_ref, heads.at[0], load_sem.at[8]),
        pltpu.make_async_copy(
            grad_attn_ref.at[:, near[0]], grad_attn.at[0, :, pl.ds(0, 512)], load_sem.at[9]
        ),
        pltpu.make_async_copy(
            grad_attn_ref.at[:, near[1]], grad_attn.at[0, :, pl.ds(512, 512)], load_sem.at[10]
        ),
        pltpu.make_async_copy(
            normed_one_ref.at[:, near[0]], normed_one.at[0, :, pl.ds(0, 512)], load_sem.at[11]
        ),
        pltpu.make_async_copy(
            normed_one_ref.at[:, near[1]], normed_one.at[0, :, pl.ds(512, 512)], load_sem.at[12]
        ),
        pltpu.make_async_copy(projected_ref, projected.at[0], load_sem.at[13]),
        pltpu.make_async_copy(
            tokens_ref.at[pl.ds(own_row(1, core), run)], tok.at[pl.ds(run, run)], load_sem.at[14]
        ),
    ]

    late_normed = pl.ds(run, run)
    early_normed = pl.ds(0, run)
    late_cot = pl.ds(pl.multiple_of((1 - y_bit) * run, run), run)
    early_cot = pl.ds(pl.multiple_of(y_bit * run, run), run)

    def piece_load(i, slot):
        which, part = i // 6, i % 6
        source = (normed_others_ref, cot_others_ref)[which]
        late = (normed_late, cot_late)[which]
        into = staged.at[slot]
        if part in (0, 1, 3, 4):
            return [pltpu.make_async_copy(source.at[part], into, piece_sem.at[slot])]
        if part == 5:
            return [pltpu.make_async_copy(late.at[1], into, piece_sem.at[slot])]
        early_rows = (early_normed, early_cot)[which]
        late_rows = (late_normed, late_cot)[which]
        return [
            pltpu.make_async_copy(
                source.at[2, early_rows], into.at[early_rows], piece_sem.at[slot]
            ),
            pltpu.make_async_copy(
                late.at[0, late_rows], into.at[late_rows], piece_sem.at[2 + slot]
            ),
        ]

    def weight_loads(j, slot):
        return [
            pltpu.make_async_copy(
                w_gate_ref.at[:, tile_of(j)], gate_w.at[slot], weight_sem.at[slot, 0]
            ),
            pltpu.make_async_copy(
                w_up_ref.at[:, tile_of(j)], up_w.at[slot], weight_sem.at[slot, 1]
            ),
            pltpu.make_async_copy(
                w_down_ref.at[tile_of(j), :], down_w.at[slot], weight_sem.at[slot, 2]
            ),
        ]

    order = [0, 1, 3, 4, 6, 7, 9, 10, 2, 8, 5, 11]
    for i in range(2):
        for load in piece_load(order[i], i):
            load.start()
    loads[13].start()
    for load in loads[:4]:
        load.start()
    for load in weight_loads(0, 0):
        load.start()

    barrier = pltpu.get_barrier_semaphore()
    peers = []
    for m in range(1, 8):
        peer = dp
        for bit in (1, 2, 4):
            peer = flip(peer, bit) if m & bit else peer
        peers.append(peer)
    for device in [twin_id, y_id] + [(peer, tensor) for peer in peers]:
        pl.semaphore_signal(barrier, inc=1, device_id=device, device_id_type=MESH)
    pl.semaphore_wait(barrier, 9)
    late_copies = [
        remote(normed_others_ref.at[1, late_normed], normed_late.at[0, late_normed],
               late_send.at[0], late_recv.at[0], x_id),
        remote(cot_others_ref.at[2, early_cot], cot_late.at[0, early_cot],
               late_send.at[1], late_recv.at[1], y_id),
        remote(normed_others_ref.at[2, early_normed], normed_late.at[1, early_normed],
               late_send.at[2], late_recv.at[2], twin_id),
        remote(cot_others_ref.at[2, early_cot], cot_late.at[1, early_cot],
               late_send.at[3], late_recv.at[3], twin_id),
    ]
    for copy in late_copies:
        copy.start()

    loads[13].wait()

    def widen(r):
        window = pl.ds(pl.multiple_of(r * ROWS, ROWS), ROWS)
        for s in range(2):
            there = pl.ds(pl.multiple_of(s * half + r * ROWS, ROWS), ROWS)
            proj_part[0, s, window, :] = projected[0, there, :].astype(F32)

    loop(half // ROWS, widen)
    projected_copy = remote(proj_part.at[0], far_staged, end_send.at[2], end_recv.at[2], far_id)
    projected_copy.start()
    branch_copy = remote(branch_ref, branch_came, end_send.at[1], end_recv.at[1], y_id)

    late_twins = [
        remote(normed_late.at[0, late_normed], normed_late.at[1, late_normed],
               late_send.at[4], late_recv.at[4], twin_id),
        remote(cot_late.at[0, late_cot], cot_late.at[1, late_cot],
               late_send.at[5], late_recv.at[5], twin_id),
    ]
    def take_piece(place):
        i, slot = order[place], place % 2
        for load in piece_load(i, slot):
            load.wait()
        rows_to, turned_to = (normed, normed_t) if i < 6 else (cot, cot_t)
        base = {0: 0, 1: 1, 3: 2, 4: 3, 2: 4, 5: 5}[i % 6] * half

        def convert(r, slot=slot, rows_to=rows_to, base=base):
            window = pl.ds(pl.multiple_of(r * ROWS, ROWS), ROWS)
            rows_to[pl.ds(pl.multiple_of(base + r * ROWS, ROWS), ROWS), :] = staged[
                slot, window, :
            ].astype(BF16)

        loop(half // ROWS, convert)
        for part, block in enumerate((away_block, home_block)):
            turned_to[pl.ds(part * TILE, TILE), pl.ds(row_count + base, half)] = (
                staged[slot, :, block].T.astype(BF16)
            )
        if place == 8:
            for copy in late_copies[2:] + late_twins:
                copy.wait()
        if place + 2 < 8 or 8 <= place < 10:
            for load in piece_load(order[place + 2], slot):
                load.start()
    for place in range(8):
        take_piece(place)
    for part in range(4):
        loads[part].wait()
        turned_to = (normed_t, cot_t)[part // 2]
        turned_to[pl.ds((part % 2) * TILE, TILE), pl.ds(0, row_count)] = (
            own_columns[part][...].astype(F32).T.astype(BF16)
        )

    def row_copy(j):
        window = (everything, everything, tile_of(j))
        return [
            remote(
                sent_out.at[window], came_out.at[window],
                row_send.at[0, j], row_recv.at[0, j], far_id,
            ),
            remote(
                down_sent.at[tile_of(j)], down_came.at[tile_of(j)],
                row_send.at[1, j], row_recv.at[1, j], far_id,
            ),
        ]

    def stores(j, slot):
        return [
            pltpu.make_async_copy(
                total.at[slot, pl.ds(0, 2), pl.ds(0, TILE)], sent_out.at[:, :, tile_of(j)],
                store_sem.at[slot, 0],
            ),
            pltpu.make_async_copy(
                total.at[slot, pl.ds(0, 2), pl.ds(TILE, TILE)], kept_out.at[:, :, tile_of(j)],
                store_sem.at[slot, 1],
            ),
            pltpu.make_async_copy(
                total.at[slot, 2, pl.ds(TILE, TILE)], down_kept.at[tile_of(j)],
                store_sem.at[slot, 3],
            ),
        ]

    def down_store(slot, into):
        return pltpu.make_async_copy(
            total.at[slot, 2, pl.ds(0, TILE)], into, store_sem.at[slot, 2]
        )

    def unit_loads(j):
        return [
            pltpu.make_async_copy(
                source.at[:, tile_of(j)], units.at[i, pl.ds(0, row_count)], unit_sem.at[i]
            )
            for i, source in enumerate((gg_ref, gu_ref, act_ref))
        ]

    def feed_forward_tile(j, first=False):
        slot = j % 2
        for load in weight_loads(j, slot):
            load.wait()

        if first:
            for load in weight_loads(1, 1):
                load.start()
        else:

            @pl.when(j + 1 < tiles)
            def _():
                for load in weight_loads(j + 1, 1 - slot):
                    load.start()

        for load in unit_loads(j):
            load.start()

        def block(m):
            rows = pl.ds(pl.multiple_of(m * 512, 512), 512)
            to = pl.ds(pl.multiple_of(row_count + m * 512, 512), 512)
            gate = jnp.dot(normed[rows, :], gate_w[slot], preferred_element_type=F32)
            up = jnp.dot(normed[rows, :], up_w[slot], preferred_element_type=F32)
            back = lax.dot_general(
                cot[rows, :], down_w[slot], transposed, preferred_element_type=F32
            )
            sigmoid = jax.nn.sigmoid(gate)
            swish = gate * sigmoid
            units[2, to, :] = (swish * up).astype(BF16)
            units[0, to, :] = (back * up * sigmoid * (1.0 + gate * (1.0 - sigmoid))).astype(BF16)
            units[1, to, :] = (back * swish).astype(BF16)

        if first:
            loop(2, block)
            for copy, later in zip(late_copies[:2], late_twins):
                copy.wait()
                later.start()
            branch_copy.start()
            for place in (8, 9):
                for load in piece_load(order[place], place % 2):
                    load.start()
            for place in range(8, 12):
                take_piece(place)
            block(2)
        else:
            loop(normed.shape[0] // 512, block)
        for load in unit_loads(j):
            load.wait()

        total[slot, 0] = jnp.dot(normed_t[...], units[0], preferred_element_type=F32)
        total[slot, 1] = jnp.dot(normed_t[...], units[1], preferred_element_type=F32)
        turned = jnp.dot(cot_t[...], units[2], preferred_element_type=F32)
        for part in range(2):
            total[slot, 2, pl.ds(part * TILE, TILE)] = turned[part * TILE : (part + 1) * TILE].T
        for store in stores(j, slot):
            store.start()
        here = j < tiles - LAST

        @pl.when(here)
        def _():
            store = down_store(slot, down_sent.at[tile_of(j)])
            store.start()
            store.wait()
            row_copy(j)[1].start()

        @pl.when(jnp.logical_not(here))
        def _():
            store = down_store(slot, down_last.at[tile_of(j - (tiles - LAST))])
            store.start()
            store.wait()

        for store in stores(j, slot):
            store.wait()
        row_copy(j)[0].start()

    def x_copies(slot):
        return [
            remote(out_part.at[0, slot], out_x.at[slot], x_send.at[0, slot],
                   x_recv.at[0, slot], x_id),
            remote(proj_part.at[0, slot], proj_x.at[slot], x_send.at[1, slot],
                   x_recv.at[1, slot], x_id),
        ]

    def attention_parts():
        for load in far_loads + loads[8:13]:
            load.wait()
        projected_copy.wait()

        def convert(r):
            window = pl.ds(pl.multiple_of(r * ROWS, ROWS), ROWS)
            block, rest = r // (run // ROWS), r % (run // ROWS)
            for s in range(2):
                which = core if s == 0 else 1 - core
                here = pl.ds(
                    pl.multiple_of(block * half + which * run + rest * ROWS, ROWS), ROWS
                )
                grad_attn[1, here, :] = staged[0, window, pl.ds(s * 1024, 1024)].astype(BF16)
                normed_one[1, here, :] = staged[1, window, pl.ds(s * 1024, 1024)].astype(BF16)
                there = pl.ds(pl.multiple_of(s * half + r * ROWS, ROWS), ROWS)
                projected[1, there, :] = far_staged[s, window, :].astype(BF16)
                heads[1, there, :] = far_heads[window, pl.ds(s * 512, 512)].astype(BF16)

        loop(half // ROWS, convert)
        for side in range(2):
            x_at = 1 - x_low if side == 0 else x_low
            for slot in range(2):
                z_at = 1 - z_high if slot == 0 else z_high
                columns = pl.ds(pl.multiple_of(z_at * 512 + x_at * 256, 256), 256)
                out_part[side, slot] = lax.dot_general(
                    heads[0], grad_attn[0, :, columns], over, preferred_element_type=F32
                ) + lax.dot_general(
                    heads[1], grad_attn[1, :, columns], over, preferred_element_type=F32
                )
                proj_part[side, slot] = lax.dot_general(
                    normed_one[0, :, columns], projected[0], over, preferred_element_type=F32
                ) + lax.dot_general(
                    normed_one[1, :, columns], projected[1], over, preferred_element_type=F32
                )
                if side == 0:
                    for copy in x_copies(slot):
                        copy.start()

    def core_copy(j):
        window = (everything, tile_of(j))
        return remote(
            staged.at[0].at[window], core_in.at[window], core_send.at[j], core_recv.at[j], twin_id
        )

    def y_copy(j):
        window = (everything, tile_of(j))
        return remote(
            staged.at[1].at[window], y_in.at[window], y_send.at[j], y_recv.at[j], y_id
        )

    def attention_sums():
        for load in loads[4:8] + loads[14:]:
            load.wait()

        def produce(j):
            product[...] = lax.dot_general(
                projected[0], w_proj[tile_of(j), :], transposed, preferred_element_type=F32
            )
            for block in range(2):
                for slot, which in ((0, 1 - core), (1, core)):
                    staged[slot, pl.ds(block * run, run), tile_of(j)] = product[
                        pl.ds(own_row(block, which), run), :
                    ]
            core_copy(j).start()

        def forward(j):
            core_copy(j).wait_recv()
            staged[1, :, tile_of(j)] = staged[1, :, tile_of(j)] + core_in[:, tile_of(j)]
            y_copy(j).start()

        produce(0)

        def step(j):
            produce(j + 1)
            forward(j)

        loop(tiles - 1, step)
        forward(tiles - 1)
        loop(tiles, lambda j: core_copy(j).wait_send())

    feed_forward_tile(0, first=True)
    for load in loads[4:13] + loads[14:]:
        load.start()
    far_loads = (
        [
            pltpu.make_async_copy(
                grad_attn_far_ref.at[s], staged.at[0, :, pl.ds(s * 1024, 1024)], piece_sem.at[s]
            )
            for s in range(2)
        ]
        + [
            pltpu.make_async_copy(
                normed_one_far_ref.at[s], staged.at[1, :, pl.ds(s * 1024, 1024)],
                piece_sem.at[2 + s],
            )
            for s in range(2)
        ]
        + [
            pltpu.make_async_copy(heads_far_ref, far_heads, piece_sem.at[5]),
        ]
    )
    for load in far_loads:
        load.start()


    def step(j):
        feed_forward_tile(j + 1)

        @pl.when(j == 0)
        def _():
            attention_parts()
            attention_sums()

    loop(tiles - 1, step)
    hidden_load = pltpu.make_async_copy(grad_hidden_ref, core_in, load_sem.at[0])
    hidden_load.start()

    def z_copies():
        return [
            remote(out_part.at[1, 0], out_came, z_send.at[0], z_recv.at[0], z_id),
            remote(proj_part.at[1, 0], proj_came, z_send.at[1], z_recv.at[1], z_id),
        ]

    for slot in range(2):
        for copy in x_copies(slot):
            copy.wait_recv()
        out_part[1, slot] = out_part[1, slot] + out_x[slot]
        proj_part[1, slot] = proj_part[1, slot] + proj_x[slot]
        if slot == 0:
            for copy in z_copies():
                copy.start()
    part_stores = [
        pltpu.make_async_copy(out_part.at[1, 1], out_mine, load_sem.at[1]),
        pltpu.make_async_copy(proj_part.at[1, 1], proj_mine, load_sem.at[2]),
    ]
    for store in part_stores:
        store.start()

    gain = gain_ref[...]
    gains[pl.ds(0, 1), :] = jnp.zeros_like(gain)
    gains[pl.ds(1, 1), :] = gain_two_ref[...]
    hidden_load.wait()
    loop(tiles, lambda j: y_copy(j).wait_recv())

    def norm_rows(i):
        window = pl.ds(pl.multiple_of(i * ROWS, ROWS), ROWS)
        incoming = staged[1, window, :] + y_in[window, :]
        values = tok[window, :].astype(F32)
        scale = lax.rsqrt(jnp.mean(values * values, axis=-1, keepdims=True) + EPSILON)
        weighted = incoming * gain
        inner = jnp.mean(weighted * values, axis=-1, keepdims=True)
        back = scale * weighted - values * (scale * scale * scale) * inner
        staged[0, window, :] = core_in[window, :] + back
        gains[pl.ds(0, 1), :] = gains[pl.ds(0, 1), :] + jnp.sum(
            incoming * values * scale, axis=0, keepdims=True
        )

    loop(half // ROWS, norm_rows)

    def to_rows(slot, out, sems, first):
        copies, kept = [], []
        for block in range(2):
            local, here = pl.ds(block * run, run), pl.ds(own_row(block, core), run)
            copies.append(remote(
                staged.at[slot, local], out.at[here],
                end_send.at[sems + block], end_recv.at[sems + block], twin_id,
            ))
            kept.append(pltpu.make_async_copy(
                staged.at[slot, local], out.at[here], load_sem.at[first + block]
            ))
        for copy in copies + kept:
            copy.start()
        return copies, kept

    input_copies, input_stores = to_rows(0, input_out, 3, 3)

    gain_twin = remote(gains, gains_came, gain_send.at[7], gain_recv.at[7], twin_id)
    gain_twin.start()

    loop(tiles, lambda j: y_copy(j).wait_send())
    branch_copy.wait()
    branch_loads = [
        pltpu.make_async_copy(branch_ref, staged.at[1], load_sem.at[5]),
        pltpu.make_async_copy(branch_came, y_in, load_sem.at[6]),
    ]
    for load in branch_loads:
        load.start()
    gain_twin.wait()
    gains[...] = gains[...] + gains_came[...]

    def gain_copy(m):
        return remote(
            gains.at[:, tile_of(peers[m])], gain_out.at[m], gain_send.at[m], gain_recv.at[m],
            (peers[m], tensor),
        )

    for m in range(7):
        gain_copy(m).start()
    gain_out[7] = gains[:, tile_of(dp)]
    for load in branch_loads:
        load.wait()

    def mixed_rows(i):
        window = pl.ds(pl.multiple_of(i * ROWS, ROWS), ROWS)
        staged[1, window, :] = staged[1, window, :] + y_in[window, :]

    loop(half // ROWS, mixed_rows)
    mixed_copy = remote(staged.at[1], core_in, end_send.at[5], end_recv.at[5], twin_id)
    mixed_copy.start()

    def put_mixed(source, which, first):
        def narrow(i):
            window = pl.ds(pl.multiple_of(i * ROWS, ROWS), ROWS)
            tok[window, :] = source[window, :].astype(BF16)

        loop(half // ROWS, narrow)
        copies = [
            pltpu.make_async_copy(
                tok.at[pl.ds(block * run, run)], mixed_out.at[pl.ds(own_row(block, which), run)],
                load_sem.at[first + block],
            )
            for block in range(2)
        ]
        for copy in copies:
            copy.start()
        for copy in copies:
            copy.wait()

    put_mixed(staged.at[1], core, 7)
    mixed_copy.wait()
    put_mixed(core_in, 1 - core, 9)

    for copy in part_stores + input_stores + input_copies:
        copy.wait()
    for m in range(7):
        gain_copy(m).wait()
    for slot in range(2):
        for copy in x_copies(slot):
            copy.wait_send()
    for copy in z_copies():
        copy.wait()
    loop(tiles, lambda j: row_copy(j)[0].wait())
    loop(tiles - LAST, lambda j: row_copy(j)[1].wait())


def last(
    normed_others, cot_others, normed, cot, act, gg, gu, w_gate, w_up, w_down,
    projected, branch, gain_two, w_query, w_key, w_value, heads, grad_attn, grad_attn_far,
    normed_one, normed_one_far, heads_far, grad_hidden, tokens, gain,
):
    row_count, width = tokens.shape
    half = row_count // 2
    tiles = width // TILE
    hidden_units = w_gate.shape[1]
    hbm = pl.BlockSpec(memory_space=pl.ANY)
    vmem = pl.BlockSpec(memory_space=pltpu.VMEM)
    wide = jax.ShapeDtypeStruct((half, width), F32)
    rows_pair = jax.ShapeDtypeStruct((2, TILE, hidden_units), F32)
    columns = jax.ShapeDtypeStruct((hidden_units, TILE), F32)
    out_block = jax.ShapeDtypeStruct((512, TILE), F32)
    proj_block = jax.ShapeDtypeStruct((TILE, 768), F32)
    dma = pltpu.SemaphoreType.DMA
    return pl.pallas_call(
        last_kernel,
        out_shape=(
            rows_pair, rows_pair, rows_pair, columns, columns, columns,
            jax.ShapeDtypeStruct((LAST * TILE, TILE), F32), out_block, out_block, proj_block, proj_block,
            jax.ShapeDtypeStruct((row_count, width), F32),
            jax.ShapeDtypeStruct((row_count, width), BF16),
            wide,
            jax.ShapeDtypeStruct((2, half, width), F32),
            jax.ShapeDtypeStruct((2, half, width), F32),
            jax.ShapeDtypeStruct((8, 2, TILE), F32),
        ),
        in_specs=[hbm] * 12 + [vmem] + [hbm] * 11 + [vmem],
        out_specs=(hbm,) * 16 + (vmem,),
        scratch_shapes=[
            pltpu.VMEM((6 * half, width), BF16),
            pltpu.VMEM((6 * half, width), BF16),
            pltpu.VMEM((2 * TILE, row_count + 6 * half), BF16),
            pltpu.VMEM((2 * TILE, row_count + 6 * half), BF16),
            pltpu.VMEM((3, row_count + 6 * half, TILE), BF16),
            pltpu.VMEM((2, width, TILE), BF16),
            pltpu.VMEM((2, width, TILE), BF16),
            pltpu.VMEM((2, TILE, width), BF16),
            pltpu.VMEM((2, 3, 2 * TILE, TILE), F32),
            pltpu.VMEM((2, half, width), F32),
            pltpu.VMEM((half, width), F32),
            pltpu.VMEM((half, width), F32),
            pltpu.VMEM((width, 768), BF16),
            pltpu.VMEM((half, width), BF16),
            pltpu.VMEM((2, row_count, 512), BF16),
            pltpu.VMEM((2, row_count, 1024), BF16),
            pltpu.VMEM((2, row_count, 1024), BF16),
            pltpu.VMEM((2, row_count, 768), BF16),
            pltpu.VMEM((2, 2, 512, TILE), F32),
            pltpu.VMEM((2, 2, TILE, 768), F32),
            pltpu.VMEM((2, 512, TILE), F32),
            pltpu.VMEM((2, TILE, 768), F32),
            pltpu.VMEM((2, half, 768), F32),
            pltpu.VMEM((half, 1024), F32),
            pltpu.VMEM((2, width), F32),
            pltpu.VMEM((2, width), F32),
            dma((15,)), dma((6,)), dma((2, 3)), dma((3,)), dma((2, 4)),
            dma((2, tiles)), dma((2, tiles)),
            dma((tiles,)), dma((tiles,)), dma((tiles,)), dma((tiles,)),
            dma((2, 2)), dma((2, 2)), dma((2,)), dma((2,)), dma((7,)), dma((7,)), dma((8,)), dma((8,)),
            dma((6,)), dma((6,)), pltpu.VMEM((row_count, TILE), F32),
        ],
        compiler_params=pltpu.CompilerParams(
            collective_id=1, has_side_effects=True, vmem_limit_bytes=64 * 1024 * 1024
        ),
        name="weight_gradients",
    )(
        normed_others, cot_others, normed, cot, act, gg, gu, w_gate, w_up, w_down,
        projected, branch, gain_two, w_query, w_key, w_value, heads, grad_attn, grad_attn_far,
        normed_one, normed_one_far, heads_far, grad_hidden, tokens, gain.reshape(1, width),
    )


def finish_kernel(
    kept, came, down_kept, down_came, out_mine, out_came, proj_mine, proj_came, input_in,
    mixed_in, gains, w_gate, w_up, w_down, w_out, w_query, w_key, w_value, grad_input, mixed,
    gain_one, gain_two,
):
    w_gate[...] = kept[0] + came[0]
    w_up[...] = kept[1] + came[1]
    w_down[...] = down_kept[...] + down_came[...]
    w_out[...] = out_mine[...] + out_came[...]
    queries, keys = w_query.shape[1], w_key.shape[1]
    w_query[...] = proj_mine[:, :queries] + proj_came[:, :queries]
    w_key[...] = proj_mine[:, queries : queries + keys] + proj_came[:, queries : queries + keys]
    w_value[...] = proj_mine[:, queries + keys :] + proj_came[:, queries + keys :]
    grad_input[...] = input_in[...]
    mixed[...] = mixed_in[...]
    total = jnp.sum(gains[...], axis=0)
    gain_one[...] = total[0:1]
    gain_two[...] = total[1:2]


def finish(*parts):
    steps = 4
    kept, down, out, proj, whole, gains = (parts[i] for i in (0, 2, 4, 6, 8, 10))
    rows, units = kept.shape[1:]

    def block(array, lead=()):
        size = array[len(lead) :]
        shape = lead + (size[0] // steps,) + size[1:]
        return pl.BlockSpec(shape, lambda i: (0,) * len(lead) + (i,) + (0,) * (len(size) - 1))

    fixed = lambda shape: pl.BlockSpec(shape, lambda i: (0,) * len(shape))
    outs = [
        (rows, units), (rows, units), down.shape, out.shape,
        (proj.shape[0], 512), (proj.shape[0], 128), (proj.shape[0], 128), whole.shape,
    ]
    return pl.pallas_call(
        finish_kernel,
        grid=(steps,),
        out_shape=[jax.ShapeDtypeStruct(shape, F32) for shape in outs]
        + [
            jax.ShapeDtypeStruct(whole.shape, BF16),
            jax.ShapeDtypeStruct((1, gains.shape[2]), F32),
            jax.ShapeDtypeStruct((1, gains.shape[2]), F32),
        ],
        in_specs=[block(kept.shape, (2,))] * 2
        + [block(part.shape) for part in parts[2:10]]
        + [fixed(gains.shape)],
        out_specs=[block(shape) for shape in outs]
        + [block(whole.shape)] + [fixed((1, gains.shape[2]))] * 2,
        compiler_params=pltpu.CompilerParams(vmem_limit_bytes=64 * 1024 * 1024),
        cost_estimate=pl.CostEstimate(
            flops=2_000_000, bytes_accessed=34_000_000, transcendentals=0
        ),
        name="last_sums",
    )(*parts)


def body(
    tokens,
    segments,
    positions,
    attn_gain,
    w_query,
    key_weight,
    value_weight,
    w_out,
    mlp_gain,
    w_gate,
    w_up,
    w_down,
    cotangent,
):
    groups = lax.axis_size("dp")
    place = lax.axis_index("dp")
    core = lax.axis_index("tensor") % 2
    all_bits = [1 << i for i in range(groups.bit_length() - 1)]
    shared_bits = [bit for bit in (4, 1) if bit < groups]
    split_bits = [bit for bit in all_bits if bit not in shared_bits]

    def blocks(matrix, offsets):
        width = matrix.shape[1] // groups
        return [
            lax.dynamic_slice_in_dim(matrix, (place ^ offset) * width, width, 1)
            for offset in offsets
        ]

    def offsets_of(bits):
        found = [0]
        for bit in bits:
            found = found + [offset + bit for offset in found]
        return found

    def reduced(matrix_of, bits):
        sent = None
        for bit in bits:
            rest = bits[bits.index(bit) + 1 :]
            offsets = offsets_of(rest)
            if sent is None:
                away = matrix_of([offset ^ bit for offset in offsets])
                home = matrix_of(offsets)
            else:
                away = [sent[offset ^ bit] for offset in offsets]
                home = [sent[offset] for offset in offsets]
            came = swap(away, "dp", bit)
            sent = {offset: h + c for offset, h, c in zip(offsets, home, came)}
        return sent[0]

    row_count, width = tokens.shape
    query_width, kv_width = w_query.shape[1], key_weight.shape[1]
    half_dim = HEAD_SIZE // 2
    frequency = 500000.0 ** (-(jnp.arange(half_dim).astype(F32) * 2.0 / HEAD_SIZE))
    frequency = jnp.tile(frequency, 4)
    (
        normed_one,
        head_outputs,
        _,
        _,
        _,
        normed_one_far,
        heads_far,
        grad_hidden,
        grad_attn,
        projected,
        grad_attn_far,
        branch,
        normed_two,
        activation,
        grad_gate_in,
        grad_up_in,
        gain_two_half,
        cotangent_others,
        normed_others,
    ) = middle(
        w_query, key_weight, value_weight, w_out, tokens, cotangent,
        attn_gain, mlp_gain, w_gate, w_up, w_down, segments, positions, frequency,
    )
    (
        kept,
        _,
        came,
        down_kept,
        _,
        down_came,
        down_last,
        out_mine,
        out_came,
        proj_mine,
        proj_came,
        grad_input,
        mixed,
        _,
        _,
        _,
        gains,
    ) = last(
        normed_others, cotangent_others, normed_two, cotangent, activation, grad_gate_in,
        grad_up_in, w_gate, w_up, w_down, projected, branch, gain_two_half, w_query, key_weight,
        value_weight, head_outputs, grad_attn, grad_attn_far, normed_one, normed_one_far,
        heads_far, grad_hidden, tokens, attn_gain,
    )
    pairs = [(i, i ^ 2) for i in range(lax.axis_size("dp"))]
    last_came = lax.ppermute(down_last, "dp", pairs)
    (
        grad_w_gate,
        grad_w_up,
        grad_w_down,
        grad_w_out,
        grad_w_query,
        grad_w_key,
        grad_w_value,
        grad_input,
        mixed,
        grad_attn_gain,
        grad_mlp_gain,
    ) = finish(
        kept, came, down_kept, down_came, out_mine, out_came, proj_mine, proj_came, grad_input,
        mixed, gains,
    )
    done = grad_w_down.shape[0] - LAST * TILE
    grad_w_down = lax.dynamic_update_slice(grad_w_down, down_kept[done:] + last_came, (done, 0))
    grad_attn_gain, grad_mlp_gain = grad_attn_gain[0], grad_mlp_gain[0]
    return (
        mixed,
        grad_input,
        grad_attn_gain,
        grad_w_query,
        grad_w_key,
        grad_w_value,
        grad_w_out,
        grad_mlp_gain,
        grad_w_gate,
        grad_w_up,
        grad_w_down,
    )


def product(left_matrix, right_matrix):
    return jnp.dot(left_matrix, right_matrix, preferred_element_type=F32)


def over_rows(left_matrix, right_matrix):
    return lax.dot_general(
        left_matrix, right_matrix, (((0,), (0,)), ((), ())), preferred_element_type=F32
    )


def against(gradient, weight):
    return lax.dot_general(
        gradient, weight, (((1,), (1,)), ((), ())), preferred_element_type=F32
    )


def narrowed(value):
    return jnp.where(value == value, value, 0.0).astype(BF16)


def swap(value, axis, bit):
    size = lax.axis_size(axis)
    return lax.ppermute(value, axis, [(i, i ^ bit) for i in range(size)])


def half_of(value, which, dim=0):
    size = value.shape[dim] // 2
    return lax.dynamic_slice_in_dim(value, which * size, size, dim)


def joined(mine, other, which):
    first = jnp.where(which == 0, mine, other)
    second = jnp.where(which == 0, other, mine)
    return jnp.concatenate([first, second], axis=0)


def tensor_sum_half(partial, core):
    total = half_of(partial, core) + swap(half_of(partial, 1 - core), "tensor", 1)
    bit = 2
    while bit < lax.axis_size("tensor"):
        total = total + swap(total, "tensor", bit)
        bit *= 2
    return total


def tables(places):
    half_dim = HEAD_SIZE // 2
    frequency = 500000.0 ** (-(jnp.arange(half_dim).astype(F32) * 2.0 / HEAD_SIZE))
    angles = places.astype(F32)[..., None] * frequency
    cosine_lookup = jnp.cos(angles)
    sine_lookup = jnp.sin(angles)
    return (
        jnp.concatenate([cosine_lookup, cosine_lookup], -1),
        jnp.concatenate([sine_lookup, sine_lookup], -1),
    )


def apply_rotary(field, cosine_lookup, sine_lookup):
    half_dim = HEAD_SIZE // 2
    turned = jnp.concatenate([-field[..., half_dim:], field[..., :half_dim]], -1)
    return field * cosine_lookup + turned * sine_lookup


def unrotate(gradient, cosine_lookup, sine_lookup):
    half_dim = HEAD_SIZE // 2
    sined = gradient * sine_lookup
    return gradient * cosine_lookup + jnp.concatenate(
        [sined[..., half_dim:], -sined[..., :half_dim]], -1
    )


def allowed_pairs(segment):
    spots = jnp.arange(segment.shape[0])
    return (spots[:, None] >= spots[None, :]) & (segment[:, None] == segment[None, :])


def scores(query_rotated, key_rotated, segment):
    raw_scores = jnp.einsum(
        "qhgd,khd->hgqk", query_rotated, key_rotated, preferred_element_type=F32
    ) * HEAD_SIZE ** (-0.5)
    return jnp.where(allowed_pairs(segment), raw_scores, MASKED)


def attend_forward(query_rotated, key_rotated, value_seq, segment):
    masked = scores(query_rotated, key_rotated, segment)
    row_peak = jnp.max(masked, axis=-1, keepdims=True)
    log_total = row_peak + jnp.log(jnp.sum(jnp.exp(masked - row_peak), axis=-1, keepdims=True))
    attention_probs = jnp.exp(masked - log_total).astype(BF16)
    combined_heads = jnp.einsum(
        "ojus,sov->uojv", attention_probs, value_seq, preferred_element_type=F32
    )
    return (combined_heads, log_total)


def attend_backward(query_rotated, key_rotated, value_seq, segment, log_total, grad_heads):
    masked = scores(query_rotated, key_rotated, segment)
    attention_probs = jnp.exp(masked - log_total)
    grad_probs = jnp.einsum("qhgd,khd->hgqk", grad_heads, value_seq, preferred_element_type=F32)
    row_sum = jnp.sum(attention_probs * grad_probs, axis=-1, keepdims=True)
    grad_raw = jnp.where(
        allowed_pairs(segment), attention_probs * (grad_probs - row_sum), 0.0
    ).astype(BF16)
    factor = HEAD_SIZE ** (-0.5)
    grad_query_rot = (
        jnp.einsum("ojus,sov->uojv", grad_raw, key_rotated, preferred_element_type=F32) * factor
    )
    grad_key_rot = (
        jnp.einsum("hgqk,qhgd->khd", grad_raw, query_rotated, preferred_element_type=F32) * factor
    )
    grad_value_rot = jnp.einsum(
        "hgqk,qhgd->khd", attention_probs.astype(BF16), grad_heads, preferred_element_type=F32
    )
    return (grad_query_rot, grad_key_rot, grad_value_rot)


def per_sequence(step, *fields):
    results = [step(*[field[s] for field in fields]) for s in range(fields[0].shape[0])]
    return [jnp.stack(parts) for parts in zip(*results)]


def general_body(
    tokens,
    segments,
    positions,
    attn_gain,
    w_query,
    key_weight,
    value_weight,
    w_out,
    mlp_gain,
    w_gate,
    w_up,
    w_down,
    cotangent,
):
    groups = lax.axis_size("dp")
    place = lax.axis_index("dp")
    core = lax.axis_index("tensor") % 2
    all_bits = [1 << i for i in range(groups.bit_length() - 1)]
    shared_bits = [bit for bit in (4, 1) if bit < groups]
    split_bits = [bit for bit in all_bits if bit not in shared_bits]

    def gathered(half):
        parts = [half]
        for bit in shared_bits:
            parts = parts + [swap(part, "dp", bit) for part in parts]
        others = parts[1:]
        twins = [swap(part, "tensor", 1) for part in others]
        return jnp.concatenate([narrowed(part) for part in others + twins], axis=0)

    def blocks(matrix, offsets):
        width = matrix.shape[1] // groups
        return [
            lax.dynamic_slice_in_dim(matrix, (place ^ offset) * width, width, 1)
            for offset in offsets
        ]

    def offsets_of(bits):
        found = [0]
        for bit in bits:
            found = found + [offset + bit for offset in found]
        return found

    def reduced(matrix_of, bits):
        sent = None
        for bit in bits:
            rest = bits[bits.index(bit) + 1 :]
            offsets = offsets_of(rest)
            if sent is None:
                away = matrix_of([offset ^ bit for offset in offsets])
                home = matrix_of(offsets)
            else:
                away = [sent[offset ^ bit] for offset in offsets]
                home = [sent[offset] for offset in offsets]
            came = swap(away, "dp", bit)
            sent = {offset: h + c for offset, h, c in zip(offsets, home, came)}
        return sent[0]

    inputs = tokens.astype(F32)
    row_count, width = inputs.shape
    seq_count, seq_len = segments.shape
    query_heads = w_query.shape[1] // HEAD_SIZE
    kv_heads = key_weight.shape[1] // HEAD_SIZE
    group_size = query_heads // kv_heads
    query_width, kv_width = w_query.shape[1], key_weight.shape[1]

    cotangent_half = half_of(cotangent, core).astype(F32)
    cotangent_others = gathered(cotangent_half)

    scale_one = lax.rsqrt(jnp.mean(inputs * inputs, axis=-1, keepdims=True) + EPSILON)
    normed_one = (inputs * scale_one * attn_gain).astype(BF16)
    cosine_lookup, sine_lookup = tables(positions.reshape(row_count))
    cosine_lookup = cosine_lookup[:, None, :]
    sine_lookup = sine_lookup[:, None, :]
    query_projected = product(normed_one, w_query).reshape(row_count, query_heads, HEAD_SIZE)
    key_projected = product(normed_one, key_weight).reshape(row_count, kv_heads, HEAD_SIZE)
    query_rotated = (
        apply_rotary(query_projected, cosine_lookup, sine_lookup)
        .astype(BF16)
        .reshape(seq_count, seq_len, kv_heads, group_size, HEAD_SIZE)
    )
    key_rotated = (
        apply_rotary(key_projected, cosine_lookup, sine_lookup)
        .astype(BF16)
        .reshape(seq_count, seq_len, kv_heads, HEAD_SIZE)
    )
    value_projected = (
        product(normed_one, value_weight)
        .astype(BF16)
        .reshape(seq_count, seq_len, kv_heads, HEAD_SIZE)
    )
    combined_heads, log_totals = per_sequence(
        attend_forward, query_rotated, key_rotated, value_projected, segments
    )
    head_outputs = combined_heads.reshape(row_count, query_width).astype(BF16)

    inputs_half = half_of(inputs, core)
    hidden = inputs_half + tensor_sum_half(product(head_outputs, w_out), core)
    scale_two = lax.rsqrt(jnp.mean(hidden * hidden, axis=-1, keepdims=True) + EPSILON)
    normed_half = (hidden * scale_two * mlp_gain).astype(BF16)
    normed_sent = normed_half.astype(F32)
    normed_twin = narrowed(swap(normed_sent, "tensor", 1))
    normed_two = joined(normed_half, normed_twin, core)
    normed_others = gathered(normed_sent)

    def feed_forward(normed, incoming):
        gate_proj = product(normed, w_gate)
        up_proj = product(normed, w_up)
        grad_activation = against(incoming, w_down)
        sigmoid_gate = jax.nn.sigmoid(gate_proj)
        swish_gate = gate_proj * sigmoid_gate
        activation = (swish_gate * up_proj).astype(BF16)
        grad_gate_in = (
            grad_activation * up_proj * sigmoid_gate * (1.0 + gate_proj * (1.0 - sigmoid_gate))
        ).astype(BF16)
        grad_up_in = (grad_activation * swish_gate).astype(BF16)
        return activation, grad_gate_in, grad_up_in

    activation, grad_gate_in, grad_up_in = feed_forward(normed_two, cotangent)
    grad_normed_two = tensor_sum_half(
        against(grad_gate_in, w_gate) + against(grad_up_in, w_up), core
    )
    mixed_half = hidden + tensor_sum_half(product(activation, w_down), core)
    mixed = joined(mixed_half.astype(BF16), narrowed(swap(mixed_half, "tensor", 1)), core)

    weighted = grad_normed_two * mlp_gain
    inner_mean = jnp.mean(weighted * hidden, axis=-1, keepdims=True)
    back_two = scale_two * weighted - hidden * (scale_two * scale_two * scale_two) * inner_mean
    gain_two_half = jnp.sum(grad_normed_two * hidden * scale_two, axis=0)
    grad_hidden = cotangent_half + back_two
    attn_half = grad_hidden.astype(BF16)
    attn_twin = narrowed(swap(grad_hidden, "tensor", 1))
    grad_attn = joined(attn_half, attn_twin, core)

    grad_heads = (
        against(grad_attn, w_out)
        .astype(BF16)
        .reshape(seq_count, seq_len, kv_heads, group_size, HEAD_SIZE)
    )
    grad_query_rot, grad_key_rot, grad_value_rot = per_sequence(
        attend_backward,
        query_rotated,
        key_rotated,
        value_projected,
        segments,
        log_totals,
        grad_heads,
    )
    grad_query_in = (
        unrotate(
            grad_query_rot.reshape(row_count, query_heads, HEAD_SIZE), cosine_lookup, sine_lookup
        )
        .reshape(row_count, query_width)
        .astype(BF16)
    )
    grad_key_in = (
        unrotate(grad_key_rot.reshape(row_count, kv_heads, HEAD_SIZE), cosine_lookup, sine_lookup)
        .reshape(row_count, kv_width)
        .astype(BF16)
    )
    grad_value_in = grad_value_rot.reshape(row_count, kv_width).astype(BF16)
    partial_one = (
        against(grad_query_in, w_query)
        + against(grad_key_in, key_weight)
        + against(grad_value_in, value_weight)
    )
    grad_normed_one = tensor_sum_half(partial_one, core)
    scale_one = half_of(scale_one, core)
    weighted = grad_normed_one * attn_gain
    inner_mean = jnp.mean(weighted * inputs_half, axis=-1, keepdims=True)
    back_one = scale_one * weighted - inputs_half * (scale_one * scale_one * scale_one) * inner_mean
    gain_one_half = jnp.sum(grad_normed_one * inputs_half * scale_one, axis=0)
    input_half = grad_hidden + back_one
    grad_input = joined(input_half, swap(input_half, "tensor", 1), core)

    activation_o, grad_gate_o, grad_up_o = feed_forward(normed_others, cotangent_others)

    def rows_of(left, left_others, right, right_others):
        def term(offsets):
            ours = blocks(left, offsets)
            theirs = blocks(left_others, offsets)
            return [
                over_rows(a, right) + over_rows(b, right_others) for a, b in zip(ours, theirs)
            ]

        return reduced(term, split_bits)

    def columns_of(left, left_others, right, right_others):
        def term(offsets):
            ours = blocks(right, offsets)
            theirs = blocks(right_others, offsets)
            return [
                over_rows(left, a) + over_rows(left_others, b) for a, b in zip(ours, theirs)
            ]

        return reduced(term, split_bits)

    grad_w_down = columns_of(activation, activation_o, cotangent, cotangent_others)
    grad_w_gate = rows_of(normed_two, normed_others, grad_gate_in, grad_gate_o)
    grad_w_up = rows_of(normed_two, normed_others, grad_up_in, grad_up_o)

    grad_w_out = reduced(
        lambda offsets: [over_rows(head_outputs, b) for b in blocks(grad_attn, offsets)], all_bits
    )
    projected = jnp.concatenate([grad_query_in, grad_key_in, grad_value_in], axis=1)
    grad_w_proj = reduced(
        lambda offsets: [over_rows(b, projected) for b in blocks(normed_one, offsets)], all_bits
    )
    grad_w_query = grad_w_proj[:, :query_width]
    grad_w_key = grad_w_proj[:, query_width : query_width + kv_width]
    grad_w_value = grad_w_proj[:, query_width + kv_width :]

    gains = jnp.stack([gain_one_half, gain_two_half])
    gains = gains + swap(gains, "tensor", 1)
    gains = reduced(lambda offsets: blocks(gains, offsets), all_bits)
    grad_attn_gain, grad_mlp_gain = gains[0], gains[1]
    return (
        mixed,
        grad_input,
        grad_attn_gain,
        grad_w_query,
        grad_w_key,
        grad_w_value,
        grad_w_out,
        grad_mlp_gain,
        grad_w_gate,
        grad_w_up,
        grad_w_down,
    )


def solution(mesh):
    placed = (
        P("dp", None),
        P("dp", None),
        P("dp", None),
        P(),
        P(None, "tensor"),
        P(None, "tensor"),
        P(None, "tensor"),
        P("tensor", None),
        P(),
        P(None, "tensor"),
        P(None, "tensor"),
        P("tensor", None),
        P("dp", None),
    )
    fits = mesh.shape["dp"] == 8 and mesh.shape["tensor"] == 4
    return jax.shard_map(
        body if fits else general_body,
        mesh=mesh,
        in_specs=placed,
        out_specs=(
            P("dp", None),
            P("dp", None),
            P("dp"),
            P("dp", "tensor"),
            P("dp", "tensor"),
            P("dp", "tensor"),
            P("tensor", "dp"),
            P("dp"),
            P("dp", "tensor"),
            P("dp", "tensor"),
            P("tensor", "dp"),
        ),
        check_vma=False,
    )
```

```python
import functools

import jax
import jax.numpy as jnp
import numpy as np
from jax import lax
from jax.experimental import pallas as pl
from jax.experimental.pallas import tpu as pltpu
from jax.sharding import PartitionSpec as P

HEAD_SIZE = 64
EPSILON = 1e-05
MASKED = -1e30
F32 = jnp.float32
BF16 = jnp.bfloat16


MESH = pl.DeviceIdType.MESH
CHUNKS = 4
TILE = 256
ROWS = 16


def flip(index, bit):
    return index + bit * (1 - 2 * ((index // bit) % 2))


def loop(count, step):
    lax.fori_loop(0, count, lambda i, carry: (step(i), carry)[1], 0)


def middle_kernel(
    w_query_ref,
    w_key_ref,
    w_value_ref,
    w_out_ref,
    tokens_ref,
    cot_ref,
    gain_one_ref,
    gain_ref,
    w_gate_ref,
    w_up_ref,
    w_down_ref,
    segment_ref,
    position_ref,
    frequency_ref,
    normed_one_out,
    heads_out,
    query_ref,
    keys_ref,
    values_ref,
    normed_one_far,
    heads_far,
    grad_hidden_out,
    grad_attn_out,
    projected_out,
    projected_wide,
    grad_attn_far,
    branch_out,
    normed_out,
    activation_out,
    grad_gate_out,
    grad_up_out,
    gain_out,
    cot_others,
    normed_others,
    gate_w,
    up_w,
    down_w,
    cot,
    cot_half,
    normed,
    normed_sent,
    normed_twin,
    act,
    gg,
    gu,
    away,
    mine,
    core_in,
    y_in,
    product,
    log_total_ref,
    segment_column,
    cosine_ref,
    sine_ref,
    local_sem,
    core_send,
    core_recv,
    y_send,
    y_recv,
    cot_send,
    cot_recv,
    n_send,
    n_recv,
    twin_send,
    twin_recv,
    hidden_send,
    hidden_recv,
    far_send,
    far_recv,
    free_sem,
):
    dp, tensor = lax.axis_index("dp"), lax.axis_index("tensor")
    core, y_bit = tensor % 2, (tensor // 2) % 2
    z_low = (dp // 2) % 2
    twin_id = (dp, flip(tensor, 1))
    y_id = (dp, flip(tensor, 2))
    x_id = (flip(dp, 1), tensor)
    z_id = (flip(dp, 4), tensor)
    far_id = (flip(dp, 2), tensor)
    half, width = cot_half.shape
    run = half // 2
    row_count = 2 * half
    hidden_units = gate_w.shape[1]
    query_width = w_query_ref.shape[1]
    tiles = width // TILE
    chunk = half // CHUNKS
    transposed = (((1,), (1,)), ((), ()))
    everything = slice(None)
    heads = gg.at[:, pl.ds(0, query_width)]
    tok = gu
    hidden = core_in.at[0]

    def own_row(block, which):
        return pl.multiple_of(block * half + which * run, run)

    def own_chunk(k, which):
        return own_row(k // 2, which) + (k % 2) * chunk

    def remote(src, dst, send, recv, device):
        return pltpu.make_async_remote_copy(
            src_ref=src, dst_ref=dst, send_sem=send, recv_sem=recv,
            device_id=device, device_id_type=MESH,
        )

    loads = {
        "tok": pltpu.make_async_copy(tokens_ref, tok, local_sem.at[0]),
        "query": pltpu.make_async_copy(
            w_query_ref, gate_w.at[:, pl.ds(0, query_width)], local_sem.at[1]
        ),
        "key": pltpu.make_async_copy(
            w_key_ref, gate_w.at[:, pl.ds(query_width, 128)], local_sem.at[2]
        ),
        "value": pltpu.make_async_copy(
            w_value_ref, gate_w.at[:, pl.ds(query_width + 128, 128)], local_sem.at[3]
        ),
        "w_out": pltpu.make_async_copy(w_out_ref, cot, local_sem.at[4]),
        "up": pltpu.make_async_copy(w_up_ref, up_w, local_sem.at[5]),
        "down": pltpu.make_async_copy(w_down_ref, down_w, local_sem.at[6]),
        "gate": pltpu.make_async_copy(w_gate_ref, gate_w, local_sem.at[7]),
        "cot": pltpu.make_async_copy(cot_ref, cot, local_sem.at[8]),
        "cot_0": pltpu.make_async_copy(
            cot_ref.at[pl.ds(own_row(0, core), run)], act.at[pl.ds(0, run)], local_sem.at[10]
        ),
        "cot_1": pltpu.make_async_copy(
            cot_ref.at[pl.ds(own_row(1, core), run)], act.at[pl.ds(run, run)], local_sem.at[11]
        ),
    }
    for name in ("cot_0", "cot_1", "tok", "query", "key", "value", "w_out", "up", "down"):
        loads[name].start()

    barrier = pltpu.get_barrier_semaphore()
    for device in (twin_id, y_id, x_id, z_id, far_id):
        pl.semaphore_signal(barrier, inc=1, device_id=device, device_id_type=MESH)
    loads["cot_0"].wait()
    loads["cot_1"].wait()

    def widen(i):
        window = pl.ds(pl.multiple_of(i * ROWS, ROWS), ROWS)
        cot_half[window, :] = act[window, :].astype(F32)

    loop(half // ROWS, widen)
    pl.semaphore_wait(barrier, 5)

    def rows(k):
        return pl.ds(pl.multiple_of(k * chunk, chunk), chunk)

    def from_x(source, slots, k, send, recv):
        return remote(source.at[rows(k)], slots.at[0, rows(k)], send.at[0, k], recv.at[0, k], x_id)

    def from_z(source, slots, k, send, recv):
        return remote(source.at[rows(k)], slots.at[1, rows(k)], send.at[1, k], recv.at[1, k], z_id)

    def from_zx(slots, k, send, recv):
        return remote(
            slots.at[1, rows(k)], slots.at[2, rows(k)], send.at[2, k], recv.at[2, k], x_id
        )

    def to_twin(slots, which, slot):
        return remote(
            slots.at[slot], slots.at[3 + slot],
            twin_send.at[which, slot], twin_recv.at[which, slot], twin_id,
        )

    half_chunk = pl.ds(pl.multiple_of((2 + y_bit) * chunk, chunk), chunk)

    def last_z():
        return remote(
            normed_sent.at[half_chunk], normed_others.at[1, half_chunk],
            n_send.at[1, 2], n_recv.at[1, 2], z_id,
        )

    def last_y():
        return remote(
            normed_others.at[1, half_chunk], normed_others.at[1, half_chunk],
            n_send.at[1, 3], n_recv.at[1, 3], y_id,
        )

    def half_to_twin(slots, which, part, window):
        return remote(
            slots.at[1, window], slots.at[4, window],
            twin_send.at[which, 1 + part], twin_recv.at[which, 1 + part], twin_id,
        )

    first_run, last_run = pl.ds(0, run), pl.ds(run, run)
    other_quarter = pl.ds(pl.multiple_of((1 - y_bit) * run, run), run)
    quarter = pl.ds(pl.multiple_of(y_bit * run, run), run)

    def quarter_z():
        return remote(
            cot_half.at[quarter], cot_others.at[1, quarter],
            cot_send.at[1, 0], cot_recv.at[1, 0], z_id,
        )

    def quarter_zx():
        return remote(
            cot_others.at[1, quarter], cot_others.at[2, quarter],
            cot_send.at[2, 0], cot_recv.at[2, 0], x_id,
        )

    def quarter_y():
        return remote(
            cot_others.at[1, quarter], cot_others.at[1, quarter],
            cot_send.at[1, 1], cot_recv.at[1, 1], y_id,
        )

    quarter_z().start()
    for k in range(CHUNKS):
        from_x(cot_half, cot_others, k, cot_send, cot_recv).start()

    def far_columns(b):
        return pl.ds(pl.multiple_of(b * 1024 + (1 - z_low) * 512, 512), 512)

    gain_one = gain_one_ref[...]
    segments = segment_ref[...].astype(F32)
    segment_column[...] = jnp.broadcast_to(segments, (8, row_count)).T
    loads["tok"].wait()

    def first_norm(block):
        def step(i):
            window = pl.ds(pl.multiple_of(block * half + i * ROWS, ROWS), ROWS)
            values = tok[window, :].astype(F32)
            scale = lax.rsqrt(jnp.mean(values * values, axis=-1, keepdims=True) + EPSILON)
            normed[window, :] = (values * scale * gain_one).astype(BF16)

        loop(half // ROWS, step)

    normed_one_store = pltpu.make_async_copy(normed, normed_one_out, local_sem.at[9])

    def stage_far(block):
        def step(i):
            window = pl.ds(pl.multiple_of(block * run + i * ROWS, ROWS), ROWS)
            here = pl.ds(pl.multiple_of(own_row(block, core) + i * ROWS, ROWS), ROWS)
            for b in range(2):
                core_in[2, window, pl.ds(b * 512, 512)] = normed[here, far_columns(b)].astype(F32)

        loop(run // ROWS, step)

    normed_one_copy = remote(
        core_in.at[2, :, pl.ds(0, 1024)], normed_one_far.at[0],
        far_send.at[0], far_recv.at[0], far_id,
    )

    places = jnp.broadcast_to(position_ref[...].astype(F32), (8, row_count)).T

    def make_tables(block):
        window = pl.ds(block * half, half)
        angles = places[block * half : (block + 1) * half, 0:1] * frequency_ref[...]
        cosine_ref[window, :] = jnp.cos(angles)
        sines = jnp.sin(angles)
        signs = lax.broadcasted_iota(jnp.int32, (half, 128), 1) % 64 < 32
        sine_ref[window, :] = jnp.where(signs, sines, -sines)

    lane = lax.broadcasted_iota(jnp.int32, (TILE, 128), 1)
    factor = HEAD_SIZE ** (-0.5)

    def turn(value):
        return jnp.where(lane % 64 < 32, pltpu.roll(value, 96, 1), pltpu.roll(value, 32, 1))

    def rotate_tile(value, window):
        return value * cosine_ref[window, :] - turn(value) * sine_ref[window, :]

    def unrotate_tile(value, window):
        return value * cosine_ref[window, :] + turn(value) * sine_ref[window, :]

    def project_in(block):
        window = pl.ds(block * TILE, TILE)

        def query_tile(j):
            projection = jnp.dot(
                normed[window, :],
                gate_w[:, pl.ds(pl.multiple_of(j * TILE, TILE), TILE)],
                preferred_element_type=F32,
            )
            for part in range(2):
                act[window, pl.ds(pl.multiple_of(j * TILE + part * 128, 128), 128)] = rotate_tile(
                    projection[:, part * 128 : (part + 1) * 128], window
                ).astype(BF16)

        loop(query_width // TILE, query_tile)
        projection = jnp.dot(
            normed[window, :], gate_w[:, pl.ds(query_width, TILE)], preferred_element_type=F32
        )
        for base, value in (
            (1024, rotate_tile(projection[:, :128], window)),
            (1536, projection[:, 128:]),
        ):
            other = pltpu.roll(value, 64, 1)
            halves_of = (
                jnp.where(lane < 64, value, 0.0),
                jnp.where(lane >= 64, other, 0.0),
                jnp.where(lane < 64, other, 0.0),
                jnp.where(lane >= 64, value, 0.0),
            )
            for i, padded in enumerate(halves_of):
                act[window, pl.ds(base + i * 128, 128)] = padded.astype(BF16)

    def allowed_of(block):
        keys_seen = (block + 1) * TILE
        window = pl.ds(block * TILE, TILE)
        key_place = lax.broadcasted_iota(jnp.int32, (keys_seen, TILE), 0)
        query_place = lax.broadcasted_iota(jnp.int32, (keys_seen, TILE), 1) + block * TILE
        return (key_place <= query_place) & (
            segment_column[pl.ds(0, keys_seen), pl.ds(0, 1)] == segments[:, block * TILE : (block + 1) * TILE]
        )

    def attend(block, p):
        kv = p // 2
        column = pl.multiple_of(p * 128, 128)
        window = pl.ds(block * TILE, TILE)
        seen = pl.ds(0, (block + 1) * TILE)
        queries = act[window, pl.ds(column, 128)]
        allowed = allowed_of(block)
        result = jnp.zeros((TILE, 128), F32)
        for side in range(2):
            padded = pl.multiple_of((kv * 2 + side) * 128, 128)
            keys = act[seen, pl.ds(pl.multiple_of(1024 + padded, 128), 128)]
            vals = act[seen, pl.ds(pl.multiple_of(1536 + padded, 128), 128)]
            raw = jnp.where(
                allowed,
                lax.dot_general(keys, queries, transposed, preferred_element_type=F32) * factor,
                MASKED,
            )
            peak = jnp.max(raw, axis=0, keepdims=True)
            lifted = jnp.exp(raw - peak)
            summed = jnp.sum(lifted, axis=0, keepdims=True)
            log_total_ref[pl.ds(2 * p + side, 1), window] = peak + jnp.log(summed)
            result = result + lax.dot_general(
                (lifted * (1.0 / summed)).astype(BF16), vals, (((0,), (0,)), ((), ())),
                preferred_element_type=F32,
            )
        heads[window, pl.ds(column, 128)] = result.astype(BF16)

    def core_copy(which, window, k):
        return remote(
            away.at[window], core_in.at[min(which, 1)].at[window],
            core_send.at[which, k], core_recv.at[which, k], twin_id,
        )

    def y_copy(which, window, k):
        return remote(
            mine.at[which].at[window], y_in.at[which].at[window],
            y_send.at[which, k], y_recv.at[which, k], y_id,
        )

    def split_tile(which, block, columns, value):
        product[...] = value
        local = pl.ds(block * run, run)
        away[local, columns] = product[pl.ds(pl.multiple_of((1 - core) * run, run), run), :]
        mine[which, local, columns] = product[pl.ds(pl.multiple_of(core * run, run), run), :]

    row_windows = [(rows(k), everything) for k in range(CHUNKS)]

    def tile_of(j):
        return pl.ds(pl.multiple_of(j * TILE, TILE), TILE)

    first_norm(0)
    first_norm(1)
    normed_one_store.start()
    stage_far(0)
    stage_far(1)
    normed_one_copy.start()
    for name in ("query", "key", "value", "w_out"):
        loads[name].wait()
    for block in range(2):
        make_tables(block)
        project_in(block)
        loop(query_width // 128, functools.partial(attend, block))

        def project(j, block=block):
            split_tile(0, block, tile_of(j), jnp.dot(
                heads[pl.ds(block * TILE, TILE), :], cot[:, tile_of(j)],
                preferred_element_type=F32,
            ))

        loop(tiles, project)
        for k in (2 * block, 2 * block + 1):
            core_copy(0, row_windows[k], k).start()
        for k in (2 * block, 2 * block + 1):
            core_copy(0, row_windows[k], k).wait_recv()

            def add(i, k=k):
                window = pl.ds(pl.multiple_of(k * chunk + i * ROWS, ROWS), ROWS)
                mine[0, window, :] = mine[0, window, :] + core_in[0, window, :]

            loop(chunk // ROWS, add)
            y_copy(0, row_windows[k], k).start()
    normed_one_store.wait()
    loads["gate"].start()
    loads["cot"].start()
    keeps = [
        pltpu.make_async_copy(act.at[:, pl.ds(0, 512)], query_ref, local_sem.at[0]),
        pltpu.make_async_copy(act.at[:, pl.ds(1024, 512)], keys_ref, local_sem.at[1]),
        pltpu.make_async_copy(act.at[:, pl.ds(1536, 512)], values_ref, local_sem.at[2]),
        pltpu.make_async_copy(heads, heads_out, local_sem.at[3]),
    ]
    for keep in keeps:
        keep.start()

    def stage_heads(i):
        window = pl.ds(pl.multiple_of(i * ROWS, ROWS), ROWS)
        for b in range(2):
            here = pl.ds(pl.multiple_of(b * half + i * ROWS, ROWS), ROWS)
            core_in[2, window, pl.ds(1024 + b * 512, 512)] = heads[here, :].astype(F32)

    loop(half // ROWS, stage_heads)
    heads_copy = remote(
        core_in.at[2, :, pl.ds(1024, 1024)], heads_far, far_send.at[1], far_recv.at[1], far_id
    )
    heads_copy.start()
    for keep in keeps:
        keep.wait()

    for name in ("cot", "up", "down"):
        loads[name].wait()

    def activation_grad(j):
        gg[:, tile_of(j)] = lax.dot_general(
            cot[...], down_w[tile_of(j), :], transposed, preferred_element_type=F32
        ).astype(BF16)

    loop(hidden_units // TILE, activation_grad)
    loads["gate"].wait()
    gain = gain_ref[...]

    def twin_copy(k):
        return remote(
            normed_sent.at[rows(k)], normed_twin.at[rows(k)],
            n_send.at[3, k], n_recv.at[3, k], twin_id,
        )

    def block_window(block, j):
        return (pl.ds(block * run, run), tile_of(j))

    for block in range(2):
        chunks = (2 * block, 2 * block + 1)
        for k in chunks:
            y_copy(0, row_windows[k], k).wait_recv()

            def normalize_rows(i, k=k):
                window = pl.ds(pl.multiple_of(k * chunk + i * ROWS, ROWS), ROWS)
                here = pl.ds(pl.multiple_of(own_chunk(k, core) + i * ROWS, ROWS), ROWS)
                values = tok[here, :].astype(F32) + (mine[0, window, :] + y_in[0, window, :])
                scale = lax.rsqrt(jnp.mean(values * values, axis=-1, keepdims=True) + EPSILON)
                rounded = (values * scale * gain).astype(BF16)
                hidden[window, :] = values
                normed[here, :] = rounded
                normed_sent[window, :] = rounded.astype(F32)

            loop(chunk // ROWS, normalize_rows)
            twin_copy(k).start()
            if block == 0:
                from_z(normed_sent, normed_others, k, n_send, n_recv).start()
            elif k == 3:
                last_z().start()
            from_x(normed_sent, normed_others, k, n_send, n_recv).start()
        for k in chunks:
            twin_copy(k).wait_recv()

            def take(i, k=k):
                here = pl.ds(pl.multiple_of(own_chunk(k, 1 - core) + i * ROWS, ROWS), ROWS)
                normed[here, :] = normed_twin[
                    pl.ds(pl.multiple_of(k * chunk + i * ROWS, ROWS), ROWS), :
                ].astype(BF16)

            loop(chunk // ROWS, take)
        window = pl.ds(block * TILE, TILE)

        def units(j, window=window):
            columns = tile_of(j)
            gate = jnp.dot(normed[window, :], gate_w[:, columns], preferred_element_type=F32)
            up = jnp.dot(normed[window, :], up_w[:, columns], preferred_element_type=F32)
            back = gg[window, columns].astype(F32)
            sigmoid = jax.nn.sigmoid(gate)
            swish = gate * sigmoid
            act[window, columns] = (swish * up).astype(BF16)
            gg[window, columns] = (
                back * up * sigmoid * (1.0 + gate * (1.0 - sigmoid))
            ).astype(BF16)
            gu[window, columns] = (back * swish).astype(BF16)

        if block == 0:
            loop(hidden_units // TILE, units)
            for k in range(CHUNKS):
                core_copy(0, row_windows[k], k).wait_send()
        else:
            loop(hidden_units // TILE, units)

        def produce(j, block=block, window=window):
            split_tile(1, block, tile_of(j), lax.dot_general(
                gg[window, :], gate_w[tile_of(j), :], transposed, preferred_element_type=F32
            ) + lax.dot_general(
                gu[window, :], up_w[tile_of(j), :], transposed, preferred_element_type=F32
            ))
            core_copy(1, block_window(block, j), block * tiles + j).start()

        def forward(j, block=block):
            where = block_window(block, j)
            core_copy(1, where, block * tiles + j).wait_recv()
            mine[(1,) + where] = mine[(1,) + where] + core_in[(1,) + where]
            y_copy(1, where, block * tiles + j).start()

        def step(j, produce=produce, forward=forward):
            produce(j + 1)
            forward(j)

        produce(0)
        loop(tiles - 1, step)
        forward(tiles - 1)
    stores = [
        pltpu.make_async_copy(normed, normed_out, local_sem.at[7]),
        pltpu.make_async_copy(act, activation_out, local_sem.at[8]),
        pltpu.make_async_copy(gg, grad_gate_out, local_sem.at[9]),
        pltpu.make_async_copy(gu, grad_up_out, local_sem.at[10]),
    ]
    for store in stores:
        store.start()
    pl.semaphore_signal(free_sem, inc=1, device_id=twin_id, device_id_type=MESH)
    quarter_z().wait()
    quarter_zx().start()
    half_to_twin(cot_others, 0, 0, quarter).start()

    for block in range(2):
        loop(tiles, lambda j: core_copy(1, block_window(block, j), block * tiles + j).wait_send())
    for k in range(CHUNKS):
        y_copy(0, row_windows[k], k).wait_send()

    def branch_produce(j):
        for block in range(2):
            split_tile(0, block, tile_of(j), jnp.dot(
                act[pl.ds(block * TILE, TILE), :], down_w[:, tile_of(j)],
                preferred_element_type=F32,
            ))
        core_copy(2, (everything, tile_of(j)), j).start()

    def branch_add(j):
        core_copy(2, (everything, tile_of(j)), j).wait_recv()
        mine[0, :, tile_of(j)] = mine[0, :, tile_of(j)] + core_in[1, :, tile_of(j)]

    def branch_step(j):
        branch_produce(j + 1)
        branch_add(j)

    pl.semaphore_wait(free_sem, 1)
    branch_produce(0)
    loop(tiles - 1, branch_step)
    branch_add(tiles - 1)
    first_y = (1 - y_bit).astype(F32)

    def add_hidden(i):
        window = pl.ds(pl.multiple_of(i * ROWS, ROWS), ROWS)
        mine[0, window, :] = mine[0, window, :] + hidden[window, :] * first_y

    loop(half // ROWS, add_hidden)
    branch_store = pltpu.make_async_copy(mine.at[0], branch_out, local_sem.at[12])
    branch_store.start()

    for store in stores:
        store.wait()
    operands = [
        pltpu.make_async_copy(query_ref, act.at[:, pl.ds(0, 512)], local_sem.at[0]),
        pltpu.make_async_copy(keys_ref, act.at[:, pl.ds(1024, 512)], local_sem.at[1]),
        pltpu.make_async_copy(values_ref, act.at[:, pl.ds(1536, 512)], local_sem.at[2]),
        pltpu.make_async_copy(w_out_ref, gate_w.at[pl.ds(0, 512)], local_sem.at[3]),
    ]
    for operand in operands:
        operand.start()
    for operand in operands:
        operand.wait()

    gain_out[...] = jnp.zeros_like(gain_out)
    sums = y_in.at[0]
    sums[:, pl.ds(0, 1024)] = jnp.zeros((TILE, 1024), F32)

    def hidden_copy(k):
        return remote(
            core_in.at[0, rows(k)], normed_twin.at[rows(k)],
            hidden_send.at[k], hidden_recv.at[k], twin_id,
        )

    def hidden_far(block, b):
        local = pl.ds(block * run, run)
        return remote(
            core_in.at[0, local, far_columns(b)],
            grad_attn_far.at[0, local, pl.ds(b * 512, 512)],
            far_send.at[3 + 2 * block + b], far_recv.at[3 + 2 * block + b], far_id,
        )

    def gather_into(offset, kv, value):
        for part in range(value.shape[0] // TILE):
            columns = pl.ds(pl.multiple_of(offset + kv * 256 + part * 128, 128), 128)
            sums[:, columns] = sums[:, columns] + value[part * TILE : (part + 1) * TILE]

    def put(block, column, value):
        rounded = value.astype(BF16)
        gu[pl.ds(block * TILE, TILE), pl.ds(column, 128)] = rounded
        core_in[1, :, pl.ds(block * 768 + column, 128)] = rounded.astype(F32)

    def attend_back(block, p):
        kv = p // 2
        column = pl.multiple_of(p * 128, 128)
        keys_seen = (block + 1) * TILE
        window = pl.ds(block * TILE, TILE)
        seen = pl.ds(0, keys_seen)
        queries = act[window, pl.ds(column, 128)]
        upstream = act[window, pl.ds(pl.multiple_of(512 + column, 128), 128)]
        allowed = allowed_of(block)
        query_grad = jnp.zeros((TILE, 128), F32)
        for side in range(2):
            padded = pl.multiple_of((kv * 2 + side) * 128, 128)
            keys = act[seen, pl.ds(pl.multiple_of(1024 + padded, 128), 128)]
            vals = act[seen, pl.ds(pl.multiple_of(1536 + padded, 128), 128)]
            raw = lax.dot_general(keys, queries, transposed, preferred_element_type=F32) * factor
            log_total = log_total_ref[pl.ds(2 * p + side, 1), window]
            probs = jnp.exp(jnp.where(allowed, raw - log_total, MASKED))
            grad_probs = lax.dot_general(
                vals, upstream, transposed, preferred_element_type=F32
            )
            row_sum = jnp.sum(probs * grad_probs, axis=0, keepdims=True)
            grad_raw = (probs * (grad_probs - row_sum)).astype(BF16)
            query_grad = query_grad + lax.dot_general(
                grad_raw, keys, (((0,), (0,)), ((), ())), preferred_element_type=F32
            )
            own = (lax.broadcasted_iota(jnp.int32, (keys_seen, 128), 1) // 64) == side
            gather_into(0, kv, jnp.where(
                own, jnp.dot(grad_raw, queries, preferred_element_type=F32), 0.0
            ))
            gather_into(512, kv, jnp.where(
                own, jnp.dot(probs.astype(BF16), upstream, preferred_element_type=F32), 0.0
            ))
        put(block, column, unrotate_tile(query_grad * factor, window))

    for block in range(2):
        loop(tiles, lambda j: y_copy(1, block_window(block, j), block * tiles + j).wait_recv())
        if block == 1:
            quarter_y().start()
        for k in (2 * block, 2 * block + 1):

            def norm_rows(i, k=k):
                window = pl.ds(pl.multiple_of(k * chunk + i * ROWS, ROWS), ROWS)
                here = pl.ds(pl.multiple_of(own_chunk(k, core) + i * ROWS, ROWS), ROWS)
                incoming = mine[1, window, :] + y_in[1, window, :]
                values = hidden[window, :]
                scale = lax.rsqrt(jnp.mean(values * values, axis=-1, keepdims=True) + EPSILON)
                weighted = incoming * gain
                inner = jnp.mean(weighted * values, axis=-1, keepdims=True)
                back = scale * weighted - values * (scale * scale * scale) * inner
                total = cot[here, :].astype(F32) + back
                core_in[0, window, :] = total
                normed[here, :] = total.astype(BF16)
                gain_out[...] = gain_out[...] + jnp.sum(
                    incoming * values * scale, axis=0, keepdims=True
                )

            loop(chunk // ROWS, norm_rows)
            hidden_copy(k).start()
        for b in range(2):
            hidden_far(block, b).start()
        for k in (2 * block, 2 * block + 1):
            hidden_copy(k).wait_recv()

            def take_hidden(i, k=k):
                here = pl.ds(pl.multiple_of(own_chunk(k, 1 - core) + i * ROWS, ROWS), ROWS)
                normed[here, :] = normed_twin[
                    pl.ds(pl.multiple_of(k * chunk + i * ROWS, ROWS), ROWS), :
                ].astype(BF16)

            loop(chunk // ROWS, take_hidden)

        def head_tile(j, block=block):
            window = pl.ds(block * TILE, TILE)
            act[window, pl.ds(pl.multiple_of(512 + j * TILE, TILE), TILE)] = lax.dot_general(
                normed[window, :], gate_w[tile_of(j), :], transposed, preferred_element_type=F32
            ).astype(BF16)

        loop(512 // TILE, head_tile)
        loop(query_width // 128, functools.partial(attend_back, block))
        if block == 0:
            for k in (0, 1):
                from_z(normed_sent, normed_others, k, n_send, n_recv).wait_recv()
                from_zx(normed_others, k, n_send, n_recv).start()
            half_to_twin(normed_others, 1, 0, first_run).start()
            for k in range(CHUNKS):
                from_x(cot_half, cot_others, k, cot_send, cot_recv).wait()
            to_twin(cot_others, 0, 0).start()

    grad_stores = [
        pltpu.make_async_copy(core_in.at[0], grad_hidden_out, local_sem.at[4]),
        pltpu.make_async_copy(normed, grad_attn_out, local_sem.at[5]),
    ]
    for store in grad_stores:
        store.start()

    def both(offset, block):
        def folded(kv):
            value = sums[:, pl.ds(offset + kv * 256 + block * 128, 128)]
            return value + pltpu.roll(value, 64, 1)

        return jnp.where(lane < 64, folded(0), folded(1))

    for block in range(2):
        window = pl.ds(block * TILE, TILE)
        put(block, 512, unrotate_tile(both(0, block) * factor, window))
        put(block, 640, both(512, block))
    projected_store = pltpu.make_async_copy(
        gu.at[:, pl.ds(0, 768)], projected_out, local_sem.at[6]
    )
    wide_stores = [
        pltpu.make_async_copy(
            core_in.at[1, :, pl.ds(b * 768, 768)], projected_wide.at[b], local_sem.at[b]
        )
        for b in range(2)
    ]
    for store in [projected_store] + wide_stores:
        store.start()

    last_z().wait()
    last_y().start()
    normed_one_copy.wait()
    normed_one_twin = remote(
        normed_one_far.at[0], normed_one_far.at[1], far_send.at[2], far_recv.at[2], twin_id
    )
    normed_one_twin.start()
    heads_copy.wait()
    for block in range(2):
        for b in range(2):
            hidden_far(block, b).wait()
    hidden_far_twin = remote(
        grad_attn_far.at[0], grad_attn_far.at[1], far_send.at[7], far_recv.at[7], twin_id
    )
    hidden_far_twin.start()
    for k in range(CHUNKS):
        from_x(normed_sent, normed_others, k, n_send, n_recv).wait_recv()
    to_twin(normed_others, 1, 0).start()
    quarter_y().wait()
    half_to_twin(cot_others, 0, 1, other_quarter).start()
    last_y().wait()
    half_to_twin(normed_others, 1, 1, last_run).start()

    for store in grad_stores + wide_stores + [projected_store, branch_store]:
        store.wait()
    for copy in (hidden_far_twin, normed_one_twin, quarter_zx()):
        copy.wait()
    for k in range(CHUNKS):
        hidden_copy(k).wait_send()
        twin_copy(k).wait_send()
        from_x(normed_sent, normed_others, k, n_send, n_recv).wait_send()
    for k in (0, 1):
        from_z(normed_sent, normed_others, k, n_send, n_recv).wait_send()
        from_zx(normed_others, k, n_send, n_recv).wait()
    for block in range(2):
        loop(tiles, lambda j: y_copy(1, block_window(block, j), block * tiles + j).wait_send())
    loop(tiles, lambda j: core_copy(2, (everything, tile_of(j)), j).wait_send())
    to_twin(cot_others, 0, 0).wait()
    to_twin(normed_others, 1, 0).wait()
    half_to_twin(cot_others, 0, 0, quarter).wait()
    half_to_twin(cot_others, 0, 1, other_quarter).wait()
    half_to_twin(normed_others, 1, 0, first_run).wait()
    half_to_twin(normed_others, 1, 1, last_run).wait()


def middle(
    w_query, w_key, w_value, w_out, tokens, cotangent, gain_one, gain,
    w_gate, w_up, w_down, segment, position, frequency,
):
    row_count, width = tokens.shape
    half = row_count // 2
    hidden_units = w_gate.shape[1]
    tiles = width // TILE
    hbm = pl.BlockSpec(memory_space=pl.ANY)
    vmem = pl.BlockSpec(memory_space=pltpu.VMEM)
    wide = jax.ShapeDtypeStruct((half, width), F32)
    units = jax.ShapeDtypeStruct((row_count, hidden_units), BF16)
    square = jax.ShapeDtypeStruct((row_count, 512), BF16)
    dma = pltpu.SemaphoreType.DMA
    return pl.pallas_call(
        middle_kernel,
        out_shape=(
            jax.ShapeDtypeStruct((row_count, width), BF16),
            square, square, square, square,
            jax.ShapeDtypeStruct((2, half, width // 2), F32),
            jax.ShapeDtypeStruct((half, width // 2), F32),
            wide,
            jax.ShapeDtypeStruct((row_count, width), BF16),
            jax.ShapeDtypeStruct((row_count, 768), BF16),
            jax.ShapeDtypeStruct((2, half, 768), F32),
            jax.ShapeDtypeStruct((2, half, width // 2), F32),
            wide,
            jax.ShapeDtypeStruct((row_count, width), BF16),
            units, units, units,
            jax.ShapeDtypeStruct((1, width), F32),
            jax.ShapeDtypeStruct((5, half, width), F32),
            jax.ShapeDtypeStruct((5, half, width), F32),
        ),
        in_specs=[hbm] * 6 + [vmem] * 2 + [hbm] * 3 + [vmem] * 3,
        out_specs=(hbm,) * 17 + (vmem,) + (hbm,) * 2,
        scratch_shapes=[
            pltpu.VMEM(w_gate.shape, BF16),
            pltpu.VMEM(w_up.shape, BF16),
            pltpu.VMEM(w_down.shape, BF16),
            pltpu.VMEM((row_count, width), BF16),
            pltpu.VMEM((half, width), F32),
            pltpu.VMEM((row_count, width), BF16),
            pltpu.VMEM((half, width), F32),
            pltpu.VMEM((half, width), F32),
            pltpu.VMEM((row_count, hidden_units), BF16),
            pltpu.VMEM((row_count, hidden_units), BF16),
            pltpu.VMEM((row_count, hidden_units), BF16),
            pltpu.VMEM((half, width), F32),
            pltpu.VMEM((2, half, width), F32),
            pltpu.VMEM((3, half, width), F32),
            pltpu.VMEM((2, half, width), F32),
            pltpu.VMEM((half, TILE), F32),
            pltpu.VMEM((8, row_count), F32),
            pltpu.VMEM((row_count, 8), F32),
            pltpu.VMEM((row_count, 128), F32),
            pltpu.VMEM((row_count, 128), F32),
            dma((13,)),
            dma((3, 2 * tiles)), dma((3, 2 * tiles)), dma((2, 2 * tiles)), dma((2, 2 * tiles)),
            dma((3, CHUNKS)), dma((3, CHUNKS)),
            dma((4, CHUNKS)), dma((4, CHUNKS)),
            dma((2, 3)), dma((2, 3)),
            dma((CHUNKS,)), dma((CHUNKS,)),
            dma((8,)), dma((8,)),
            pltpu.SemaphoreType.REGULAR,
        ],
        compiler_params=pltpu.CompilerParams(
            collective_id=0, has_side_effects=True, vmem_limit_bytes=64 * 1024 * 1024
        ),
        name="feed_forward",
    )(
        w_query, w_key, w_value, w_out, tokens, cotangent,
        gain_one.reshape(1, width), gain.reshape(1, width), w_gate, w_up, w_down,
        segment.reshape(1, row_count), position.reshape(1, row_count), jnp.asarray(frequency).reshape(1, 128),
    )


LAST = 2


def last_kernel(
    normed_others_ref,
    cot_others_ref,
    normed_ref,
    cot_ref,
    act_ref,
    gg_ref,
    gu_ref,
    w_gate_ref,
    w_up_ref,
    w_down_ref,
    projected_ref,
    projected_wide_ref,
    branch_ref,
    gain_two_ref,
    w_query_ref,
    w_key_ref,
    w_value_ref,
    heads_ref,
    grad_attn_ref,
    grad_attn_far_ref,
    normed_one_ref,
    normed_one_far_ref,
    heads_far_ref,
    grad_hidden_ref,
    tokens_ref,
    gain_ref,
    kept_out,
    sent_out,
    came_out,
    down_kept,
    down_sent,
    down_came,
    down_last,
    out_mine,
    out_came,
    proj_mine,
    proj_came,
    input_out,
    mixed_out,
    branch_came,
    normed_late,
    cot_late,
    gain_out,
    normed,
    cot,
    normed_t,
    cot_t,
    units,
    gate_w,
    up_w,
    down_w,
    total,
    staged,
    core_in,
    y_in,
    w_proj,
    tok,
    heads,
    grad_attn,
    normed_one,
    projected,
    out_part,
    proj_part,
    out_x,
    proj_x,
    far_staged,
    far_heads,
    gains,
    gains_came,
    load_sem,
    piece_sem,
    weight_sem,
    unit_sem,
    store_sem,
    row_send,
    row_recv,
    core_send,
    core_recv,
    y_send,
    y_recv,
    x_send,
    x_recv,
    z_send,
    z_recv,
    end_send,
    end_recv,
    gain_send,
    gain_recv,
    late_send,
    late_recv,
    product,
):
    dp, tensor = lax.axis_index("dp"), lax.axis_index("tensor")
    core = tensor % 2
    x_low, z_low, z_high = dp % 2, (dp // 2) % 2, dp // 4
    twin_id = (dp, flip(tensor, 1))
    y_id = (dp, flip(tensor, 2))
    x_id = (flip(dp, 1), tensor)
    z_id = (flip(dp, 4), tensor)
    far_id = (flip(dp, 2), tensor)
    half, width = tok.shape
    row_count = 2 * half
    tiles = width // TILE
    run = half // 2
    y_bit = (tensor // 2) % 2

    def own_row(block, which):
        return pl.multiple_of(block * half + which * run, run)

    everything = slice(None)
    transposed = (((1,), (1,)), ((), ()))
    over = (((0,), (0,)), ((), ()))

    def remote(src, dst, send, recv, device):
        return pltpu.make_async_remote_copy(
            src_ref=src, dst_ref=dst, send_sem=send, recv_sem=recv,
            device_id=device, device_id_type=MESH,
        )

    def tile_of(j):
        return pl.ds(pl.multiple_of(j * TILE, TILE), TILE)

    away_block = tile_of(flip(dp, 2))
    home_block = tile_of(dp)
    near = [
        pl.ds(pl.multiple_of(b * 1024 + z_low * 512, 512), 512) for b in range(2)
    ]
    own_columns = [units.at[0, pl.ds(i * row_count, row_count)] for i in range(4)]
    loads = [
        pltpu.make_async_copy(normed_ref.at[:, away_block], own_columns[0], load_sem.at[0]),
        pltpu.make_async_copy(normed_ref.at[:, home_block], own_columns[1], load_sem.at[1]),
        pltpu.make_async_copy(cot_ref.at[:, away_block], own_columns[2], load_sem.at[2]),
        pltpu.make_async_copy(cot_ref.at[:, home_block], own_columns[3], load_sem.at[3]),
        pltpu.make_async_copy(w_query_ref, w_proj.at[:, pl.ds(0, 512)], load_sem.at[4]),
        pltpu.make_async_copy(w_key_ref, w_proj.at[:, pl.ds(512, 128)], load_sem.at[5]),
        pltpu.make_async_copy(w_value_ref, w_proj.at[:, pl.ds(640, 128)], load_sem.at[6]),
        pltpu.make_async_copy(
            tokens_ref.at[pl.ds(own_row(0, core), run)], tok.at[pl.ds(0, run)], load_sem.at[7]
        ),
        pltpu.make_async_copy(heads_ref, heads.at[0], load_sem.at[8]),
        pltpu.make_async_copy(
            grad_attn_ref.at[:, near[0]], grad_attn.at[0, :, pl.ds(0, 512)], load_sem.at[9]
        ),
        pltpu.make_async_copy(
            grad_attn_ref.at[:, near[1]], grad_attn.at[0, :, pl.ds(512, 512)], load_sem.at[10]
        ),
        pltpu.make_async_copy(
            normed_one_ref.at[:, near[0]], normed_one.at[0, :, pl.ds(0, 512)], load_sem.at[11]
        ),
        pltpu.make_async_copy(
            normed_one_ref.at[:, near[1]], normed_one.at[0, :, pl.ds(512, 512)], load_sem.at[12]
        ),
        pltpu.make_async_copy(projected_ref, projected.at[0], load_sem.at[13]),
        pltpu.make_async_copy(
            tokens_ref.at[pl.ds(own_row(1, core), run)], tok.at[pl.ds(run, run)], load_sem.at[14]
        ),
    ]

    late_normed = pl.ds(run, run)
    early_normed = pl.ds(0, run)
    late_cot = pl.ds(pl.multiple_of((1 - y_bit) * run, run), run)
    early_cot = pl.ds(pl.multiple_of(y_bit * run, run), run)

    def piece_load(i, slot):
        which, part = i // 6, i % 6
        source = (normed_others_ref, cot_others_ref)[which]
        late = (normed_late, cot_late)[which]
        into = staged.at[slot]
        if part in (0, 1, 3, 4):
            return [pltpu.make_async_copy(source.at[part], into, piece_sem.at[slot])]
        if part == 5:
            return [pltpu.make_async_copy(late.at[1], into, piece_sem.at[slot])]
        early_rows = (early_normed, early_cot)[which]
        late_rows = (late_normed, late_cot)[which]
        return [
            pltpu.make_async_copy(
                source.at[2, early_rows], into.at[early_rows], piece_sem.at[slot]
            ),
            pltpu.make_async_copy(
                late.at[0, late_rows], into.at[late_rows], piece_sem.at[2 + slot]
            ),
        ]

    def weight_loads(j, slot):
        return [
            pltpu.make_async_copy(
                w_gate_ref.at[:, tile_of(j)], gate_w.at[slot], weight_sem.at[slot, 0]
            ),
            pltpu.make_async_copy(
                w_up_ref.at[:, tile_of(j)], up_w.at[slot], weight_sem.at[slot, 1]
            ),
            pltpu.make_async_copy(
                w_down_ref.at[tile_of(j), :], down_w.at[slot], weight_sem.at[slot, 2]
            ),
        ]

    order = [0, 1, 3, 4, 6, 7, 9, 10, 2, 8, 5, 11]
    for i in range(2):
        for load in piece_load(order[i], i):
            load.start()
    for load in loads[:4]:
        load.start()
    for load in weight_loads(0, 0):
        load.start()

    barrier = pltpu.get_barrier_semaphore()
    peers = []
    for m in range(1, 8):
        peer = dp
        for bit in (1, 2, 4):
            peer = flip(peer, bit) if m & bit else peer
        peers.append(peer)
    for device in [twin_id, y_id] + [(peer, tensor) for peer in peers]:
        pl.semaphore_signal(barrier, inc=1, device_id=device, device_id_type=MESH)
    pl.semaphore_wait(barrier, 9)
    projected_copy = remote(
        projected_wide_ref, far_staged, end_send.at[2], end_recv.at[2], far_id
    )
    projected_copy.start()
    late_copies = [
        remote(normed_others_ref.at[1, late_normed], normed_late.at[0, late_normed],
               late_send.at[0], late_recv.at[0], x_id),
        remote(cot_others_ref.at[2, early_cot], cot_late.at[0, early_cot],
               late_send.at[1], late_recv.at[1], y_id),
        remote(normed_others_ref.at[2, early_normed], normed_late.at[1, early_normed],
               late_send.at[2], late_recv.at[2], twin_id),
        remote(cot_others_ref.at[2, early_cot], cot_late.at[1, early_cot],
               late_send.at[3], late_recv.at[3], twin_id),
    ]
    for copy in late_copies:
        copy.start()
    branch_copy = remote(branch_ref, branch_came, end_send.at[1], end_recv.at[1], y_id)

    late_twins = [
        remote(normed_late.at[0, late_normed], normed_late.at[1, late_normed],
               late_send.at[4], late_recv.at[4], twin_id),
        remote(cot_late.at[0, late_cot], cot_late.at[1, late_cot],
               late_send.at[5], late_recv.at[5], twin_id),
    ]
    def take_piece(place):
        i, slot = order[place], place % 2
        for load in piece_load(i, slot):
            load.wait()
        rows_to, turned_to = (normed, normed_t) if i < 6 else (cot, cot_t)
        base = {0: 0, 1: 1, 3: 2, 4: 3, 2: 4, 5: 5}[i % 6] * half

        def convert(r, slot=slot, rows_to=rows_to, base=base):
            window = pl.ds(pl.multiple_of(r * ROWS, ROWS), ROWS)
            rows_to[pl.ds(pl.multiple_of(base + r * ROWS, ROWS), ROWS), :] = staged[
                slot, window, :
            ].astype(BF16)

        loop(half // ROWS, convert)
        for part, block in enumerate((away_block, home_block)):
            turned_to[pl.ds(part * TILE, TILE), pl.ds(row_count + base, half)] = (
                staged[slot, :, block].T.astype(BF16)
            )
        if place == 8:
            for copy in late_copies[2:] + late_twins:
                copy.wait()
        if place + 2 < 8 or 8 <= place < 10:
            for load in piece_load(order[place + 2], slot):
                load.start()
    for place in range(8):
        take_piece(place)
    for part in range(4):
        loads[part].wait()
        turned_to = (normed_t, cot_t)[part // 2]
        turned_to[pl.ds((part % 2) * TILE, TILE), pl.ds(0, row_count)] = (
            own_columns[part][...].astype(F32).T.astype(BF16)
        )

    def row_copy(j):
        window = (everything, everything, tile_of(j))
        return [
            remote(
                sent_out.at[window], came_out.at[window],
                row_send.at[0, j], row_recv.at[0, j], far_id,
            ),
            remote(
                down_sent.at[tile_of(j)], down_came.at[tile_of(j)],
                row_send.at[1, j], row_recv.at[1, j], far_id,
            ),
        ]

    def stores(j, slot):
        return [
            pltpu.make_async_copy(
                total.at[slot, pl.ds(0, 2), pl.ds(0, TILE)], sent_out.at[:, :, tile_of(j)],
                store_sem.at[slot, 0],
            ),
            pltpu.make_async_copy(
                total.at[slot, pl.ds(0, 2), pl.ds(TILE, TILE)], kept_out.at[:, :, tile_of(j)],
                store_sem.at[slot, 1],
            ),
            pltpu.make_async_copy(
                total.at[slot, 2, pl.ds(TILE, TILE)], down_kept.at[tile_of(j)],
                store_sem.at[slot, 3],
            ),
        ]

    def down_store(slot, into):
        return pltpu.make_async_copy(
            total.at[slot, 2, pl.ds(0, TILE)], into, store_sem.at[slot, 2]
        )

    def unit_loads(j):
        return [
            pltpu.make_async_copy(
                source.at[:, tile_of(j)], units.at[i, pl.ds(0, row_count)], unit_sem.at[i]
            )
            for i, source in enumerate((gg_ref, gu_ref, act_ref))
        ]

    def feed_forward_tile(j, first=False):
        slot = j % 2
        for load in weight_loads(j, slot):
            load.wait()

        if first:
            for load in weight_loads(1, 1):
                load.start()
        else:

            @pl.when(j + 1 < tiles)
            def _():
                for load in weight_loads(j + 1, 1 - slot):
                    load.start()

        for load in unit_loads(j):
            load.start()

        def block(m):
            rows = pl.ds(pl.multiple_of(m * 512, 512), 512)
            to = pl.ds(pl.multiple_of(row_count + m * 512, 512), 512)
            gate = jnp.dot(normed[rows, :], gate_w[slot], preferred_element_type=F32)
            up = jnp.dot(normed[rows, :], up_w[slot], preferred_element_type=F32)
            back = lax.dot_general(
                cot[rows, :], down_w[slot], transposed, preferred_element_type=F32
            )
            sigmoid = jax.nn.sigmoid(gate)
            swish = gate * sigmoid
            units[2, to, :] = (swish * up).astype(BF16)
            units[0, to, :] = (back * up * sigmoid * (1.0 + gate * (1.0 - sigmoid))).astype(BF16)
            units[1, to, :] = (back * swish).astype(BF16)

        if first:
            loop(2, block)
            for copy, later in zip(late_copies[:2], late_twins):
                copy.wait()
                later.start()
            branch_copy.start()
            for place in (8, 9):
                for load in piece_load(order[place], place % 2):
                    load.start()
            for place in range(8, 12):
                take_piece(place)
            block(2)
        else:
            loop(normed.shape[0] // 512, block)
        for load in unit_loads(j):
            load.wait()

        total[slot, 0] = jnp.dot(normed_t[...], units[0], preferred_element_type=F32)
        total[slot, 1] = jnp.dot(normed_t[...], units[1], preferred_element_type=F32)
        turned = jnp.dot(cot_t[...], units[2], preferred_element_type=F32)
        for part in range(2):
            total[slot, 2, pl.ds(part * TILE, TILE)] = turned[part * TILE : (part + 1) * TILE].T
        for store in stores(j, slot):
            store.start()
        here = j < tiles - LAST

        @pl.when(here)
        def _():
            store = down_store(slot, down_sent.at[tile_of(j)])
            store.start()
            store.wait()
            row_copy(j)[1].start()

        @pl.when(jnp.logical_not(here))
        def _():
            store = down_store(slot, down_last.at[tile_of(j - (tiles - LAST))])
            store.start()
            store.wait()

        for store in stores(j, slot):
            store.wait()
        row_copy(j)[0].start()

    def x_copies(slot):
        return [
            remote(out_part.at[0, slot], out_x.at[slot], x_send.at[0, slot],
                   x_recv.at[0, slot], x_id),
            remote(proj_part.at[0, slot], proj_x.at[slot], x_send.at[1, slot],
                   x_recv.at[1, slot], x_id),
        ]

    def attention_parts():
        for load in far_loads + loads[8:14]:
            load.wait()
        projected_copy.wait()

        def convert(r):
            window = pl.ds(pl.multiple_of(r * ROWS, ROWS), ROWS)
            block, rest = r // (run // ROWS), r % (run // ROWS)
            for s in range(2):
                which = core if s == 0 else 1 - core
                here = pl.ds(
                    pl.multiple_of(block * half + which * run + rest * ROWS, ROWS), ROWS
                )
                grad_attn[1, here, :] = staged[0, window, pl.ds(s * 1024, 1024)].astype(BF16)
                normed_one[1, here, :] = staged[1, window, pl.ds(s * 1024, 1024)].astype(BF16)
                there = pl.ds(pl.multiple_of(s * half + r * ROWS, ROWS), ROWS)
                projected[1, there, :] = far_staged[s, window, :].astype(BF16)
                heads[1, there, :] = far_heads[window, pl.ds(s * 512, 512)].astype(BF16)

        loop(half // ROWS, convert)
        for side in range(2):
            x_at = 1 - x_low if side == 0 else x_low
            for slot in range(2):
                z_at = 1 - z_high if slot == 0 else z_high
                columns = pl.ds(pl.multiple_of(z_at * 512 + x_at * 256, 256), 256)
                out_part[side, slot] = lax.dot_general(
                    heads[0], grad_attn[0, :, columns], over, preferred_element_type=F32
                ) + lax.dot_general(
                    heads[1], grad_attn[1, :, columns], over, preferred_element_type=F32
                )
                proj_part[side, slot] = lax.dot_general(
                    normed_one[0, :, columns], projected[0], over, preferred_element_type=F32
                ) + lax.dot_general(
                    normed_one[1, :, columns], projected[1], over, preferred_element_type=F32
                )
                if side == 0:
                    for copy in x_copies(slot):
                        copy.start()

    def core_copy(j):
        window = (everything, tile_of(j))
        return remote(
            staged.at[0].at[window], core_in.at[window], core_send.at[j], core_recv.at[j], twin_id
        )

    def y_copy(j):
        window = (everything, tile_of(j))
        return remote(
            staged.at[1].at[window], y_in.at[window], y_send.at[j], y_recv.at[j], y_id
        )

    def attention_sums():
        for load in loads[4:8] + loads[14:]:
            load.wait()

        def produce(j):
            product[...] = lax.dot_general(
                projected[0], w_proj[tile_of(j), :], transposed, preferred_element_type=F32
            )
            for block in range(2):
                for slot, which in ((0, 1 - core), (1, core)):
                    staged[slot, pl.ds(block * run, run), tile_of(j)] = product[
                        pl.ds(own_row(block, which), run), :
                    ]
            core_copy(j).start()

        def forward(j):
            core_copy(j).wait_recv()
            staged[1, :, tile_of(j)] = staged[1, :, tile_of(j)] + core_in[:, tile_of(j)]
            y_copy(j).start()

        produce(0)

        def step(j):
            produce(j + 1)
            forward(j)

        loop(tiles - 1, step)
        forward(tiles - 1)
        loop(tiles, lambda j: core_copy(j).wait_send())

    feed_forward_tile(0, first=True)
    for load in loads[4:]:
        load.start()
    far_loads = (
        [
            pltpu.make_async_copy(
                grad_attn_far_ref.at[s], staged.at[0, :, pl.ds(s * 1024, 1024)], piece_sem.at[s]
            )
            for s in range(2)
        ]
        + [
            pltpu.make_async_copy(
                normed_one_far_ref.at[s], staged.at[1, :, pl.ds(s * 1024, 1024)],
                piece_sem.at[2 + s],
            )
            for s in range(2)
        ]
        + [
            pltpu.make_async_copy(heads_far_ref, far_heads, piece_sem.at[5]),
        ]
    )
    for load in far_loads:
        load.start()


    def step(j):
        feed_forward_tile(j + 1)

        @pl.when(j == 0)
        def _():
            attention_parts()
            attention_sums()

    loop(tiles - 1, step)
    hidden_load = pltpu.make_async_copy(grad_hidden_ref, core_in, load_sem.at[0])
    hidden_load.start()

    def z_copies():
        return [
            remote(out_part.at[1, 0], out_came, z_send.at[0], z_recv.at[0], z_id),
            remote(proj_part.at[1, 0], proj_came, z_send.at[1], z_recv.at[1], z_id),
        ]

    for slot in range(2):
        for copy in x_copies(slot):
            copy.wait_recv()
        out_part[1, slot] = out_part[1, slot] + out_x[slot]
        proj_part[1, slot] = proj_part[1, slot] + proj_x[slot]
        if slot == 0:
            for copy in z_copies():
                copy.start()
    part_stores = [
        pltpu.make_async_copy(out_part.at[1, 1], out_mine, load_sem.at[1]),
        pltpu.make_async_copy(proj_part.at[1, 1], proj_mine, load_sem.at[2]),
    ]
    for store in part_stores:
        store.start()

    gain = gain_ref[...]
    gains[pl.ds(0, 1), :] = jnp.zeros_like(gain)
    gains[pl.ds(1, 1), :] = gain_two_ref[...]
    hidden_load.wait()
    loop(tiles, lambda j: y_copy(j).wait_recv())

    def norm_rows(i):
        window = pl.ds(pl.multiple_of(i * ROWS, ROWS), ROWS)
        incoming = staged[1, window, :] + y_in[window, :]
        values = tok[window, :].astype(F32)
        scale = lax.rsqrt(jnp.mean(values * values, axis=-1, keepdims=True) + EPSILON)
        weighted = incoming * gain
        inner = jnp.mean(weighted * values, axis=-1, keepdims=True)
        back = scale * weighted - values * (scale * scale * scale) * inner
        staged[0, window, :] = core_in[window, :] + back
        gains[pl.ds(0, 1), :] = gains[pl.ds(0, 1), :] + jnp.sum(
            incoming * values * scale, axis=0, keepdims=True
        )

    loop(half // ROWS, norm_rows)

    def to_rows(slot, out, sems, first):
        copies, kept = [], []
        for block in range(2):
            local, here = pl.ds(block * run, run), pl.ds(own_row(block, core), run)
            copies.append(remote(
                staged.at[slot, local], out.at[here],
                end_send.at[sems + block], end_recv.at[sems + block], twin_id,
            ))
            kept.append(pltpu.make_async_copy(
                staged.at[slot, local], out.at[here], load_sem.at[first + block]
            ))
        for copy in copies + kept:
            copy.start()
        return copies, kept

    input_copies, input_stores = to_rows(0, input_out, 3, 3)

    gain_twin = remote(gains, gains_came, gain_send.at[7], gain_recv.at[7], twin_id)
    gain_twin.start()

    loop(tiles, lambda j: y_copy(j).wait_send())
    branch_copy.wait()
    branch_loads = [
        pltpu.make_async_copy(branch_ref, staged.at[1], load_sem.at[5]),
        pltpu.make_async_copy(branch_came, y_in, load_sem.at[6]),
    ]
    for load in branch_loads:
        load.start()
    gain_twin.wait()
    gains[...] = gains[...] + gains_came[...]

    def gain_copy(m):
        return remote(
            gains.at[:, tile_of(peers[m])], gain_out.at[m], gain_send.at[m], gain_recv.at[m],
            (peers[m], tensor),
        )

    for m in range(7):
        gain_copy(m).start()
    gain_out[7] = gains[:, tile_of(dp)]
    for load in branch_loads:
        load.wait()

    def mixed_rows(i):
        window = pl.ds(pl.multiple_of(i * ROWS, ROWS), ROWS)
        staged[1, window, :] = staged[1, window, :] + y_in[window, :]

    loop(half // ROWS, mixed_rows)
    mixed_copy = remote(staged.at[1], core_in, end_send.at[5], end_recv.at[5], twin_id)
    mixed_copy.start()

    def put_mixed(source, which, first):
        def narrow(i):
            window = pl.ds(pl.multiple_of(i * ROWS, ROWS), ROWS)
            tok[window, :] = source[window, :].astype(BF16)

        loop(half // ROWS, narrow)
        copies = [
            pltpu.make_async_copy(
                tok.at[pl.ds(block * run, run)], mixed_out.at[pl.ds(own_row(block, which), run)],
                load_sem.at[first + block],
            )
            for block in range(2)
        ]
        for copy in copies:
            copy.start()
        for copy in copies:
            copy.wait()

    put_mixed(staged.at[1], core, 7)
    mixed_copy.wait()
    put_mixed(core_in, 1 - core, 9)

    for copy in part_stores + input_stores + input_copies:
        copy.wait()
    for m in range(7):
        gain_copy(m).wait()
    for slot in range(2):
        for copy in x_copies(slot):
            copy.wait_send()
    for copy in z_copies():
        copy.wait()
    loop(tiles, lambda j: row_copy(j)[0].wait())
    loop(tiles - LAST, lambda j: row_copy(j)[1].wait())


def last(
    normed_others, cot_others, normed, cot, act, gg, gu, w_gate, w_up, w_down,
    projected, projected_wide, branch, gain_two, w_query, w_key, w_value, heads, grad_attn, grad_attn_far,
    normed_one, normed_one_far, heads_far, grad_hidden, tokens, gain,
):
    row_count, width = tokens.shape
    half = row_count // 2
    tiles = width // TILE
    hidden_units = w_gate.shape[1]
    hbm = pl.BlockSpec(memory_space=pl.ANY)
    vmem = pl.BlockSpec(memory_space=pltpu.VMEM)
    wide = jax.ShapeDtypeStruct((half, width), F32)
    rows_pair = jax.ShapeDtypeStruct((2, TILE, hidden_units), F32)
    columns = jax.ShapeDtypeStruct((hidden_units, TILE), F32)
    out_block = jax.ShapeDtypeStruct((512, TILE), F32)
    proj_block = jax.ShapeDtypeStruct((TILE, 768), F32)
    dma = pltpu.SemaphoreType.DMA
    return pl.pallas_call(
        last_kernel,
        out_shape=(
            rows_pair, rows_pair, rows_pair, columns, columns, columns,
            jax.ShapeDtypeStruct((LAST * TILE, TILE), F32), out_block, out_block, proj_block, proj_block,
            jax.ShapeDtypeStruct((row_count, width), F32),
            jax.ShapeDtypeStruct((row_count, width), BF16),
            wide,
            jax.ShapeDtypeStruct((2, half, width), F32),
            jax.ShapeDtypeStruct((2, half, width), F32),
            jax.ShapeDtypeStruct((8, 2, TILE), F32),
        ),
        in_specs=[hbm] * 13 + [vmem] + [hbm] * 11 + [vmem],
        out_specs=(hbm,) * 16 + (vmem,),
        scratch_shapes=[
            pltpu.VMEM((6 * half, width), BF16),
            pltpu.VMEM((6 * half, width), BF16),
            pltpu.VMEM((2 * TILE, row_count + 6 * half), BF16),
            pltpu.VMEM((2 * TILE, row_count + 6 * half), BF16),
            pltpu.VMEM((3, row_count + 6 * half, TILE), BF16),
            pltpu.VMEM((2, width, TILE), BF16),
            pltpu.VMEM((2, width, TILE), BF16),
            pltpu.VMEM((2, TILE, width), BF16),
            pltpu.VMEM((2, 3, 2 * TILE, TILE), F32),
            pltpu.VMEM((2, half, width), F32),
            pltpu.VMEM((half, width), F32),
            pltpu.VMEM((half, width), F32),
            pltpu.VMEM((width, 768), BF16),
            pltpu.VMEM((half, width), BF16),
            pltpu.VMEM((2, row_count, 512), BF16),
            pltpu.VMEM((2, row_count, 1024), BF16),
            pltpu.VMEM((2, row_count, 1024), BF16),
            pltpu.VMEM((2, row_count, 768), BF16),
            pltpu.VMEM((2, 2, 512, TILE), F32),
            pltpu.VMEM((2, 2, TILE, 768), F32),
            pltpu.VMEM((2, 512, TILE), F32),
            pltpu.VMEM((2, TILE, 768), F32),
            pltpu.VMEM((2, half, 768), F32),
            pltpu.VMEM((half, 1024), F32),
            pltpu.VMEM((2, width), F32),
            pltpu.VMEM((2, width), F32),
            dma((15,)), dma((6,)), dma((2, 3)), dma((3,)), dma((2, 4)),
            dma((2, tiles)), dma((2, tiles)),
            dma((tiles,)), dma((tiles,)), dma((tiles,)), dma((tiles,)),
            dma((2, 2)), dma((2, 2)), dma((2,)), dma((2,)), dma((7,)), dma((7,)), dma((8,)), dma((8,)),
            dma((6,)), dma((6,)), pltpu.VMEM((row_count, TILE), F32),
        ],
        compiler_params=pltpu.CompilerParams(
            collective_id=1, has_side_effects=True, vmem_limit_bytes=64 * 1024 * 1024
        ),
        name="weight_gradients",
    )(
        normed_others, cot_others, normed, cot, act, gg, gu, w_gate, w_up, w_down,
        projected, projected_wide, branch, gain_two, w_query, w_key, w_value, heads, grad_attn, grad_attn_far,
        normed_one, normed_one_far, heads_far, grad_hidden, tokens, gain.reshape(1, width),
    )


def finish_kernel(
    kept, came, down_kept, down_came, out_mine, out_came, proj_mine, proj_came, input_in,
    mixed_in, gains, w_gate, w_up, w_down, w_out, w_query, w_key, w_value, grad_input, mixed,
    gain_one, gain_two,
):
    w_gate[...] = kept[0] + came[0]
    w_up[...] = kept[1] + came[1]
    w_down[...] = down_kept[...] + down_came[...]
    w_out[...] = out_mine[...] + out_came[...]
    queries, keys = w_query.shape[1], w_key.shape[1]
    w_query[...] = proj_mine[:, :queries] + proj_came[:, :queries]
    w_key[...] = proj_mine[:, queries : queries + keys] + proj_came[:, queries : queries + keys]
    w_value[...] = proj_mine[:, queries + keys :] + proj_came[:, queries + keys :]
    grad_input[...] = input_in[...]
    mixed[...] = mixed_in[...]
    total = jnp.sum(gains[...], axis=0)
    gain_one[...] = total[0:1]
    gain_two[...] = total[1:2]


def finish(*parts):
    steps = 4
    kept, down, out, proj, whole, gains = (parts[i] for i in (0, 2, 4, 6, 8, 10))
    rows, units = kept.shape[1:]

    def block(array, lead=()):
        size = array[len(lead) :]
        shape = lead + (size[0] // steps,) + size[1:]
        return pl.BlockSpec(shape, lambda i: (0,) * len(lead) + (i,) + (0,) * (len(size) - 1))

    fixed = lambda shape: pl.BlockSpec(shape, lambda i: (0,) * len(shape))
    outs = [
        (rows, units), (rows, units), down.shape, out.shape,
        (proj.shape[0], 512), (proj.shape[0], 128), (proj.shape[0], 128), whole.shape,
    ]
    return pl.pallas_call(
        finish_kernel,
        grid=(steps,),
        out_shape=[jax.ShapeDtypeStruct(shape, F32) for shape in outs]
        + [
            jax.ShapeDtypeStruct(whole.shape, BF16),
            jax.ShapeDtypeStruct((1, gains.shape[2]), F32),
            jax.ShapeDtypeStruct((1, gains.shape[2]), F32),
        ],
        in_specs=[block(kept.shape, (2,))] * 2
        + [block(part.shape) for part in parts[2:10]]
        + [fixed(gains.shape)],
        out_specs=[block(shape) for shape in outs]
        + [block(whole.shape)] + [fixed((1, gains.shape[2]))] * 2,
        compiler_params=pltpu.CompilerParams(vmem_limit_bytes=64 * 1024 * 1024),
        cost_estimate=pl.CostEstimate(
            flops=2_000_000, bytes_accessed=34_000_000, transcendentals=0
        ),
        name="last_sums",
    )(*parts)


def body(
    tokens,
    segments,
    positions,
    attn_gain,
    w_query,
    key_weight,
    value_weight,
    w_out,
    mlp_gain,
    w_gate,
    w_up,
    w_down,
    cotangent,
):
    row_count, width = tokens.shape
    half = row_count // 2
    hidden_units = w_gate.shape[1]
    tiles = width // TILE
    hbm = pl.BlockSpec(memory_space=pl.ANY)
    vmem = pl.BlockSpec(memory_space=pltpu.VMEM)
    wide = jax.ShapeDtypeStruct((half, width), F32)
    units = jax.ShapeDtypeStruct((row_count, hidden_units), BF16)
    square = jax.ShapeDtypeStruct((row_count, 512), BF16)
    dma = pltpu.SemaphoreType.DMA
    return pl.pallas_call(
        middle_kernel,
        out_shape=(
            jax.ShapeDtypeStruct((row_count, width), BF16),
            square, square, square, square,
            jax.ShapeDtypeStruct((2, half, width // 2), F32),
            jax.ShapeDtypeStruct((half, width // 2), F32),
            wide,
            jax.ShapeDtypeStruct((row_count, width), BF16),
            jax.ShapeDtypeStruct((row_count, 768), BF16),
            jax.ShapeDtypeStruct((2, half, 768), F32),
            jax.ShapeDtypeStruct((2, half, width // 2), F32),
            wide,
            jax.ShapeDtypeStruct((row_count, width), BF16),
            units, units, units,
            jax.ShapeDtypeStruct((1, width), F32),
            jax.ShapeDtypeStruct((5, half, width), F32),
            jax.ShapeDtypeStruct((5, half, width), F32),
        ),
        in_specs=[hbm] * 6 + [vmem] * 2 + [hbm] * 3 + [vmem] * 3,
        out_specs=(hbm,) * 17 + (vmem,) + (hbm,) * 2,
        scratch_shapes=[
            pltpu.VMEM(w_gate.shape, BF16),
            pltpu.VMEM(w_up.shape, BF16),
            pltpu.VMEM(w_down.shape, BF16),
            pltpu.VMEM((row_count, width), BF16),
            pltpu.VMEM((half, width), F32),
            pltpu.VMEM((row_count, width), BF16),
            pltpu.VMEM((half, width), F32),
            pltpu.VMEM((half, width), F32),
            pltpu.VMEM((row_count, hidden_units), BF16),
            pltpu.VMEM((row_count, hidden_units), BF16),
            pltpu.VMEM((row_count, hidden_units), BF16),
            pltpu.VMEM((half, width), F32),
            pltpu.VMEM((2, half, width), F32),
            pltpu.VMEM((3, half, width), F32),
            pltpu.VMEM((2, half, width), F32),
            pltpu.VMEM((half, TILE), F32),
            pltpu.VMEM((8, row_count), F32),
            pltpu.VMEM((row_count, 8), F32),
            pltpu.VMEM((row_count, 128), F32),
            pltpu.VMEM((row_count, 128), F32),
            dma((13,)),
            dma((3, 2 * tiles)), dma((3, 2 * tiles)), dma((2, 2 * tiles)), dma((2, 2 * tiles)),
            dma((3, CHUNKS)), dma((3, CHUNKS)),
            dma((4, CHUNKS)), dma((4, CHUNKS)),
            dma((2, 3)), dma((2, 3)),
            dma((CHUNKS,)), dma((CHUNKS,)),
            dma((8,)), dma((8,)),
            pltpu.SemaphoreType.REGULAR,
        ],
        compiler_params=pltpu.CompilerParams(
            collective_id=0, has_side_effects=True, vmem_limit_bytes=64 * 1024 * 1024
        ),
        name="feed_forward",
    )(
        w_query, w_key, w_value, w_out, tokens, cotangent,
        gain_one.reshape(1, width), gain.reshape(1, width), w_gate, w_up, w_down,
        segment.reshape(1, row_count), position.reshape(1, row_count), jnp.asarray(frequency).reshape(1, 128),
    )


LAST = 2


def last_kernel(
    normed_others_ref,
    cot_others_ref,
    normed_ref,
    cot_ref,
    act_ref,
    gg_ref,
    gu_ref,
    w_gate_ref,
    w_up_ref,
    w_down_ref,
    projected_ref,
    projected_wide_ref,
    branch_ref,
    gain_two_ref,
    w_query_ref,
    w_key_ref,
    w_value_ref,
    heads_ref,
    grad_attn_ref,
    grad_attn_far_ref,
    normed_one_ref,
    normed_one_far_ref,
    heads_far_ref,
    grad_hidden_ref,
    tokens_ref,
    gain_ref,
    kept_out,
    sent_out,
    came_out,
    down_kept,
    down_sent,
    down_came,
    down_last,
    out_mine,
    out_came,
    proj_mine,
    proj_came,
    input_out,
    mixed_out,
    branch_came,
    normed_late,
    cot_late,
    gain_out,
    normed,
    cot,
    normed_t,
    cot_t,
    units,
    gate_w,
    up_w,
    down_w,
    total,
    staged,
    core_in,
    y_in,
    w_proj,
    tok,
    heads,
    grad_attn,
    normed_one,
    projected,
    out_part,
    proj_part,
    out_x,
    proj_x,
    far_staged,
    far_heads,
    gains,
    gains_came,
    load_sem,
    piece_sem,
    weight_sem,
    unit_sem,
    store_sem,
    row_send,
    row_recv,
    core_send,
    core_recv,
    y_send,
    y_recv,
    x_send,
    x_recv,
    z_send,
    z_recv,
    end_send,
    end_recv,
    gain_send,
    gain_recv,
    late_send,
    late_recv,
    product,
):
    dp, tensor = lax.axis_index("dp"), lax.axis_index("tensor")
    core = tensor % 2
    x_low, z_low, z_high = dp % 2, (dp // 2) % 2, dp // 4
    twin_id = (dp, flip(tensor, 1))
    y_id = (dp, flip(tensor, 2))
    x_id = (flip(dp, 1), tensor)
    z_id = (flip(dp, 4), tensor)
    far_id = (flip(dp, 2), tensor)
    half, width = tok.shape
    row_count = 2 * half
    tiles = width // TILE
    run = half // 2
    y_bit = (tensor // 2) % 2

    def own_row(block, which):
        return pl.multiple_of(block * half + which * run, run)

    everything = slice(None)
    transposed = (((1,), (1,)), ((), ()))
    over = (((0,), (0,)), ((), ()))

    def remote(src, dst, send, recv, device):
        return pltpu.make_async_remote_copy(
            src_ref=src, dst_ref=dst, send_sem=send, recv_sem=recv,
            device_id=device, device_id_type=MESH,
        )

    def tile_of(j):
        return pl.ds(pl.multiple_of(j * TILE, TILE), TILE)

    away_block = tile_of(flip(dp, 2))
    home_block = tile_of(dp)
    near = [
        pl.ds(pl.multiple_of(b * 1024 + z_low * 512, 512), 512) for b in range(2)
    ]
    own_columns = [units.at[0, pl.ds(i * row_count, row_count)] for i in range(4)]
    loads = [
        pltpu.make_async_copy(normed_ref.at[:, away_block], own_columns[0], load_sem.at[0]),
        pltpu.make_async_copy(normed_ref.at[:, home_block], own_columns[1], load_sem.at[1]),
        pltpu.make_async_copy(cot_ref.at[:, away_block], own_columns[2], load_sem.at[2]),
        pltpu.make_async_copy(cot_ref.at[:, home_block], own_columns[3], load_sem.at[3]),
        pltpu.make_async_copy(w_query_ref, w_proj.at[:, pl.ds(0, 512)], load_sem.at[4]),
        pltpu.make_async_copy(w_key_ref, w_proj.at[:, pl.ds(512, 128)], load_sem.at[5]),
        pltpu.make_async_copy(w_value_ref, w_proj.at[:, pl.ds(640, 128)], load_sem.at[6]),
        pltpu.make_async_copy(
            tokens_ref.at[pl.ds(own_row(0, core), run)], tok.at[pl.ds(0, run)], load_sem.at[7]
        ),
        pltpu.make_async_copy(heads_ref, heads.at[0], load_sem.at[8]),
        pltpu.make_async_copy(
            grad_attn_ref.at[:, near[0]], grad_attn.at[0, :, pl.ds(0, 512)], load_sem.at[9]
        ),
        pltpu.make_async_copy(
            grad_attn_ref.at[:, near[1]], grad_attn.at[0, :, pl.ds(512, 512)], load_sem.at[10]
        ),
        pltpu.make_async_copy(
            normed_one_ref.at[:, near[0]], normed_one.at[0, :, pl.ds(0, 512)], load_sem.at[11]
        ),
        pltpu.make_async_copy(
            normed_one_ref.at[:, near[1]], normed_one.at[0, :, pl.ds(512, 512)], load_sem.at[12]
        ),
        pltpu.make_async_copy(projected_ref, projected.at[0], load_sem.at[13]),
        pltpu.make_async_copy(
            tokens_ref.at[pl.ds(own_row(1, core), run)], tok.at[pl.ds(run, run)], load_sem.at[14]
        ),
    ]

    late_normed = pl.ds(run, run)
    early_normed = pl.ds(0, run)
    late_cot = pl.ds(pl.multiple_of((1 - y_bit) * run, run), run)
    early_cot = pl.ds(pl.multiple_of(y_bit * run, run), run)

    def piece_load(i, slot):
        which, part = i // 6, i % 6
        source = (normed_others_ref, cot_others_ref)[which]
        late = (normed_late, cot_late)[which]
        into = staged.at[slot]
        if part in (0, 1, 3, 4):
            return [pltpu.make_async_copy(source.at[part], into, piece_sem.at[slot])]
        if part == 5:
            return [pltpu.make_async_copy(late.at[1], into, piece_sem.at[slot])]
        early_rows = (early_normed, early_cot)[which]
        late_rows = (late_normed, late_cot)[which]
        return [
            pltpu.make_async_copy(
                source.at[2, early_rows], into.at[early_rows], piece_sem.at[slot]
            ),
            pltpu.make_async_copy(
                late.at[0, late_rows], into.at[late_rows], piece_sem.at[2 + slot]
            ),
        ]

    def weight_loads(j, slot):
        return [
            pltpu.make_async_copy(
                w_gate_ref.at[:, tile_of(j)], gate_w.at[slot], weight_sem.at[slot, 0]
            ),
            pltpu.make_async_copy(
                w_up_ref.at[:, tile_of(j)], up_w.at[slot], weight_sem.at[slot, 1]
            ),
            pltpu.make_async_copy(
                w_down_ref.at[tile_of(j), :], down_w.at[slot], weight_sem.at[slot, 2]
            ),
        ]

    order = [0, 1, 3, 4, 6, 7, 9, 10, 2, 8, 5, 11]
    for i in range(2):
        for load in piece_load(order[i], i):
            load.start()
    for load in loads[:4]:
        load.start()
    for load in weight_loads(0, 0):
        load.start()

    barrier = pltpu.get_barrier_semaphore()
    peers = []
    for m in range(1, 8):
        peer = dp
        for bit in (1, 2, 4):
            peer = flip(peer, bit) if m & bit else peer
        peers.append(peer)
    for device in [twin_id, y_id] + [(peer, tensor) for peer in peers]:
        pl.semaphore_signal(barrier, inc=1, device_id=device, device_id_type=MESH)
    pl.semaphore_wait(barrier, 9)
    projected_copy = remote(
        projected_wide_ref, far_staged, end_send.at[2], end_recv.at[2], far_id
    )
    projected_copy.start()
    late_copies = [
        remote(normed_others_ref.at[1, late_normed], normed_late.at[0, late_normed],
               late_send.at[0], late_recv.at[0], x_id),
        remote(cot_others_ref.at[2, early_cot], cot_late.at[0, early_cot],
               late_send.at[1], late_recv.at[1], y_id),
        remote(normed_others_ref.at[2, early_normed], normed_late.at[1, early_normed],
               late_send.at[2], late_recv.at[2], twin_id),
        remote(cot_others_ref.at[2, early_cot], cot_late.at[1, early_cot],
               late_send.at[3], late_recv.at[3], twin_id),
    ]
    for copy in late_copies:
        copy.start()
    branch_copy = remote(branch_ref, branch_came, end_send.at[1], end_recv.at[1], y_id)

    late_twins = [
        remote(normed_late.at[0, late_normed], normed_late.at[1, late_normed],
               late_send.at[4], late_recv.at[4], twin_id),
        remote(cot_late.at[0, late_cot], cot_late.at[1, late_cot],
               late_send.at[5], late_recv.at[5], twin_id),
    ]
    def take_piece(place):
        i, slot = order[place], place % 2
        for load in piece_load(i, slot):
            load.wait()
        rows_to, turned_to = (normed, normed_t) if i < 6 else (cot, cot_t)
        base = {0: 0, 1: 1, 3: 2, 4: 3, 2: 4, 5: 5}[i % 6] * half

        def convert(r, slot=slot, rows_to=rows_to, base=base):
            window = pl.ds(pl.multiple_of(r * ROWS, ROWS), ROWS)
            rows_to[pl.ds(pl.multiple_of(base + r * ROWS, ROWS), ROWS), :] = staged[
                slot, window, :
            ].astype(BF16)

        loop(half // ROWS, convert)
        for part, block in enumerate((away_block, home_block)):
            turned_to[pl.ds(part * TILE, TILE), pl.ds(row_count + base, half)] = (
                staged[slot, :, block].T.astype(BF16)
            )
        if place == 8:
            for copy in late_copies[2:] + late_twins:
                copy.wait()
        if place + 2 < 8 or 8 <= place < 10:
            for load in piece_load(order[place + 2], slot):
                load.start()
    for place in range(8):
        take_piece(place)
    for part in range(4):
        loads[part].wait()
        turned_to = (normed_t, cot_t)[part // 2]
        turned_to[pl.ds((part % 2) * TILE, TILE), pl.ds(0, row_count)] = (
            own_columns[part][...].astype(F32).T.astype(BF16)
        )

    def row_copy(j):
        window = (everything, everything, tile_of(j))
        return [
            remote(
                sent_out.at[window], came_out.at[window],
                row_send.at[0, j], row_recv.at[0, j], far_id,
            ),
            remote(
                down_sent.at[tile_of(j)], down_came.at[tile_of(j)],
                row_send.at[1, j], row_recv.at[1, j], far_id,
            ),
        ]

    def stores(j, slot):
        return [
            pltpu.make_async_copy(
                total.at[slot, pl.ds(0, 2), pl.ds(0, TILE)], sent_out.at[:, :, tile_of(j)],
                store_sem.at[slot, 0],
            ),
            pltpu.make_async_copy(
                total.at[slot, pl.ds(0, 2), pl.ds(TILE, TILE)], kept_out.at[:, :, tile_of(j)],
                store_sem.at[slot, 1],
            ),
            pltpu.make_async_copy(
                total.at[slot, 2, pl.ds(TILE, TILE)], down_kept.at[tile_of(j)],
                store_sem.at[slot, 3],
            ),
        ]

    def down_store(slot, into):
        return pltpu.make_async_copy(
            total.at[slot, 2, pl.ds(0, TILE)], into, store_sem.at[slot, 2]
        )

    def unit_loads(j):
        return [
            pltpu.make_async_copy(
                source.at[:, tile_of(j)], units.at[i, pl.ds(0, row_count)], unit_sem.at[i]
            )
            for i, source in enumerate((gg_ref, gu_ref, act_ref))
        ]

    def feed_forward_tile(j, first=False):
        slot = j % 2
        for load in weight_loads(j, slot):
            load.wait()

        if first:
            for load in weight_loads(1, 1):
                load.start()
        else:

            @pl.when(j + 1 < tiles)
            def _():
                for load in weight_loads(j + 1, 1 - slot):
                    load.start()

        for load in unit_loads(j):
            load.start()

        def block(m):
            rows = pl.ds(pl.multiple_of(m * 512, 512), 512)
            to = pl.ds(pl.multiple_of(row_count + m * 512, 512), 512)
            gate = jnp.dot(normed[rows, :], gate_w[slot], preferred_element_type=F32)
            up = jnp.dot(normed[rows, :], up_w[slot], preferred_element_type=F32)
            back = lax.dot_general(
                cot[rows, :], down_w[slot], transposed, preferred_element_type=F32
            )
            sigmoid = jax.nn.sigmoid(gate)
            swish = gate * sigmoid
            units[2, to, :] = (swish * up).astype(BF16)
            units[0, to, :] = (back * up * sigmoid * (1.0 + gate * (1.0 - sigmoid))).astype(BF16)
            units[1, to, :] = (back * swish).astype(BF16)

        if first:
            loop(2, block)
            for copy, later in zip(late_copies[:2], late_twins):
                copy.wait()
                later.start()
            branch_copy.start()
            for place in (8, 9):
                for load in piece_load(order[place], place % 2):
                    load.start()
            for place in range(8, 12):
                take_piece(place)
            block(2)
        else:
            loop(normed.shape[0] // 512, block)
        for load in unit_loads(j):
            load.wait()

        total[slot, 0] = jnp.dot(normed_t[...], units[0], preferred_element_type=F32)
        total[slot, 1] = jnp.dot(normed_t[...], units[1], preferred_element_type=F32)
        turned = jnp.dot(cot_t[...], units[2], preferred_element_type=F32)
        for part in range(2):
            total[slot, 2, pl.ds(part * TILE, TILE)] = turned[part * TILE : (part + 1) * TILE].T
        for store in stores(j, slot):
            store.start()
        here = j < tiles - LAST

        @pl.when(here)
        def _():
            store = down_store(slot, down_sent.at[tile_of(j)])
            store.start()
            store.wait()
            row_copy(j)[1].start()

        @pl.when(jnp.logical_not(here))
        def _():
            store = down_store(slot, down_last.at[tile_of(j - (tiles - LAST))])
            store.start()
            store.wait()

        for store in stores(j, slot):
            store.wait()
        row_copy(j)[0].start()

    def x_copies(slot):
        return [
            remote(out_part.at[0, slot], out_x.at[slot], x_send.at[0, slot],
                   x_recv.at[0, slot], x_id),
            remote(proj_part.at[0, slot], proj_x.at[slot], x_send.at[1, slot],
                   x_recv.at[1, slot], x_id),
        ]

    def attention_parts():
        for load in far_loads + loads[8:14]:
            load.wait()
        projected_copy.wait()

        def convert(r):
            window = pl.ds(pl.multiple_of(r * ROWS, ROWS), ROWS)
            block, rest = r // (run // ROWS), r % (run // ROWS)
            for s in range(2):
                which = core if s == 0 else 1 - core
                here = pl.ds(
                    pl.multiple_of(block * half + which * run + rest * ROWS, ROWS), ROWS
                )
                grad_attn[1, here, :] = staged[0, window, pl.ds(s * 1024, 1024)].astype(BF16)
                normed_one[1, here, :] = staged[1, window, pl.ds(s * 1024, 1024)].astype(BF16)
                there = pl.ds(pl.multiple_of(s * half + r * ROWS, ROWS), ROWS)
                projected[1, there, :] = far_staged[s, window, :].astype(BF16)
                heads[1, there, :] = far_heads[window, pl.ds(s * 512, 512)].astype(BF16)

        loop(half // ROWS, convert)
        for side in range(2):
            x_at = 1 - x_low if side == 0 else x_low
            for slot in range(2):
                z_at = 1 - z_high if slot == 0 else z_high
                columns = pl.ds(pl.multiple_of(z_at * 512 + x_at * 256, 256), 256)
                out_part[side, slot] = lax.dot_general(
                    heads[0], grad_attn[0, :, columns], over, preferred_element_type=F32
                ) + lax.dot_general(
                    heads[1], grad_attn[1, :, columns], over, preferred_element_type=F32
                )
                proj_part[side, slot] = lax.dot_general(
                    normed_one[0, :, columns], projected[0], over, preferred_element_type=F32
                ) + lax.dot_general(
                    normed_one[1, :, columns], projected[1], over, preferred_element_type=F32
                )
                if side == 0:
                    for copy in x_copies(slot):
                        copy.start()

    def core_copy(j):
        window = (everything, tile_of(j))
        return remote(
            staged.at[0].at[window], core_in.at[window], core_send.at[j], core_recv.at[j], twin_id
        )

    def y_copy(j):
        window = (everything, tile_of(j))
        return remote(
            staged.at[1].at[window], y_in.at[window], y_send.at[j], y_recv.at[j], y_id
        )

    def attention_sums():
        for load in loads[4:8] + loads[14:]:
            load.wait()

        def produce(j):
            product[...] = lax.dot_general(
                projected[0], w_proj[tile_of(j), :], transposed, preferred_element_type=F32
            )
            for block in range(2):
                for slot, which in ((0, 1 - core), (1, core)):
                    staged[slot, pl.ds(block * run, run), tile_of(j)] = product[
                        pl.ds(own_row(block, which), run), :
                    ]
            core_copy(j).start()

        def forward(j):
            core_copy(j).wait_recv()
            staged[1, :, tile_of(j)] = staged[1, :, tile_of(j)] + core_in[:, tile_of(j)]
            y_copy(j).start()

        produce(0)

        def step(j):
            produce(j + 1)
            forward(j)

        loop(tiles - 1, step)
        forward(tiles - 1)
        loop(tiles, lambda j: core_copy(j).wait_send())

    feed_forward_tile(0, first=True)
    for load in loads[4:]:
        load.start()
    far_loads = (
        [
            pltpu.make_async_copy(
                grad_attn_far_ref.at[s], staged.at[0, :, pl.ds(s * 1024, 1024)], piece_sem.at[s]
            )
            for s in range(2)
        ]
        + [
            pltpu.make_async_copy(
                normed_one_far_ref.at[s], staged.at[1, :, pl.ds(s * 1024, 1024)],
                piece_sem.at[2 + s],
            )
            for s in range(2)
        ]
        + [
            pltpu.make_async_copy(heads_far_ref, far_heads, piece_sem.at[5]),
        ]
    )
    for load in far_loads:
        load.start()


    def step(j):
        feed_forward_tile(j + 1)

        @pl.when(j == 0)
        def _():
            attention_parts()
            attention_sums()

    loop(tiles - 1, step)
    hidden_load = pltpu.make_async_copy(grad_hidden_ref, core_in, load_sem.at[0])
    hidden_load.start()

    def z_copies():
        return [
            remote(out_part.at[1, 0], out_came, z_send.at[0], z_recv.at[0], z_id),
            remote(proj_part.at[1, 0], proj_came, z_send.at[1], z_recv.at[1], z_id),
        ]

    for slot in range(2):
        for copy in x_copies(slot):
            copy.wait_recv()
        out_part[1, slot] = out_part[1, slot] + out_x[slot]
        proj_part[1, slot] = proj_part[1, slot] + proj_x[slot]
        if slot == 0:
            for copy in z_copies():
                copy.start()
    part_stores = [
        pltpu.make_async_copy(out_part.at[1, 1], out_mine, load_sem.at[1]),
        pltpu.make_async_copy(proj_part.at[1, 1], proj_mine, load_sem.at[2]),
    ]
    for store in part_stores:
        store.start()

    gain = gain_ref[...]
    gains[pl.ds(0, 1), :] = jnp.zeros_like(gain)
    gains[pl.ds(1, 1), :] = gain_two_ref[...]
    hidden_load.wait()
    loop(tiles, lambda j: y_copy(j).wait_recv())

    def norm_rows(i):
        window = pl.ds(pl.multiple_of(i * ROWS, ROWS), ROWS)
        incoming = staged[1, window, :] + y_in[window, :]
        values = tok[window, :].astype(F32)
        scale = lax.rsqrt(jnp.mean(values * values, axis=-1, keepdims=True) + EPSILON)
        weighted = incoming * gain
        inner = jnp.mean(weighted * values, axis=-1, keepdims=True)
        back = scale * weighted - values * (scale * scale * scale) * inner
        staged[0, window, :] = core_in[window, :] + back
        gains[pl.ds(0, 1), :] = gains[pl.ds(0, 1), :] + jnp.sum(
            incoming * values * scale, axis=0, keepdims=True
        )

    loop(half // ROWS, norm_rows)

    def to_rows(slot, out, sems, first):
        copies, kept = [], []
        for block in range(2):
            local, here = pl.ds(block * run, run), pl.ds(own_row(block, core), run)
            copies.append(remote(
                staged.at[slot, local], out.at[here],
                end_send.at[sems + block], end_recv.at[sems + block], twin_id,
            ))
            kept.append(pltpu.make_async_copy(
                staged.at[slot, local], out.at[here], load_sem.at[first + block]
            ))
        for copy in copies + kept:
            copy.start()
        return copies, kept

    input_copies, input_stores = to_rows(0, input_out, 3, 3)

    gain_twin = remote(gains, gains_came, gain_send.at[7], gain_recv.at[7], twin_id)
    gain_twin.start()

    loop(tiles, lambda j: y_copy(j).wait_send())
    branch_copy.wait()
    branch_loads = [
        pltpu.make_async_copy(branch_ref, staged.at[1], load_sem.at[5]),
        pltpu.make_async_copy(branch_came, y_in, load_sem.at[6]),
    ]
    for load in branch_loads:
        load.start()
    gain_twin.wait()
    gains[...] = gains[...] + gains_came[...]

    def gain_copy(m):
        return remote(
            gains.at[:, tile_of(peers[m])], gain_out.at[m], gain_send.at[m], gain_recv.at[m],
            (peers[m], tensor),
        )

    for m in range(7):
        gain_copy(m).start()
    gain_out[7] = gains[:, tile_of(dp)]
    for load in branch_loads:
        load.wait()

    def mixed_rows(i):
        window = pl.ds(pl.multiple_of(i * ROWS, ROWS), ROWS)
        staged[1, window, :] = staged[1, window, :] + y_in[window, :]

    loop(half // ROWS, mixed_rows)
    mixed_copy = remote(staged.at[1], core_in, end_send.at[5], end_recv.at[5], twin_id)
    mixed_copy.start()

    def put_mixed(source, which, first):
        def narrow(i):
            window = pl.ds(pl.multiple_of(i * ROWS, ROWS), ROWS)
            tok[window, :] = source[window, :].astype(BF16)

        loop(half // ROWS, narrow)
        copies = [
            pltpu.make_async_copy(
                tok.at[pl.ds(block * run, run)], mixed_out.at[pl.ds(own_row(block, which), run)],
                load_sem.at[first + block],
            )
            for block in range(2)
        ]
        for copy in copies:
            copy.start()
        for copy in copies:
            copy.wait()

    put_mixed(staged.at[1], core, 7)
    mixed_copy.wait()
    put_mixed(core_in, 1 - core, 9)

    for copy in part_stores + input_stores + input_copies:
        copy.wait()
    for m in range(7):
        gain_copy(m).wait()
    for slot in range(2):
        for copy in x_copies(slot):
            copy.wait_send()
    for copy in z_copies():
        copy.wait()
    loop(tiles, lambda j: row_copy(j)[0].wait())
    loop(tiles - LAST, lambda j: row_copy(j)[1].wait())


def last(
    normed_others, cot_others, normed, cot, act, gg, gu, w_gate, w_up, w_down,
    projected, projected_wide, branch, gain_two, w_query, w_key, w_value, heads, grad_attn, grad_attn_far,
    normed_one, normed_one_far, heads_far, grad_hidden, tokens, gain,
):
    row_count, width = tokens.shape
    half = row_count // 2
    tiles = width // TILE
    hidden_units = w_gate.shape[1]
    hbm = pl.BlockSpec(memory_space=pl.ANY)
    vmem = pl.BlockSpec(memory_space=pltpu.VMEM)
    wide = jax.ShapeDtypeStruct((half, width), F32)
    rows_pair = jax.ShapeDtypeStruct((2, TILE, hidden_units), F32)
    columns = jax.ShapeDtypeStruct((hidden_units, TILE), F32)
    out_block = jax.ShapeDtypeStruct((512, TILE), F32)
    proj_block = jax.ShapeDtypeStruct((TILE, 768), F32)
    dma = pltpu.SemaphoreType.DMA
    return pl.pallas_call(
        last_kernel,
        out_shape=(
            rows_pair, rows_pair, rows_pair, columns, columns, columns,
            jax.ShapeDtypeStruct((LAST * TILE, TILE), F32), out_block, out_block, proj_block, proj_block,
            jax.ShapeDtypeStruct((row_count, width), F32),
            jax.ShapeDtypeStruct((row_count, width), BF16),
            wide,
            jax.ShapeDtypeStruct((2, half, width), F32),
            jax.ShapeDtypeStruct((2, half, width), F32),
            jax.ShapeDtypeStruct((8, 2, TILE), F32),
        ),
        in_specs=[hbm] * 13 + [vmem] + [hbm] * 11 + [vmem],
        out_specs=(hbm,) * 16 + (vmem,),
        scratch_shapes=[
            pltpu.VMEM((6 * half, width), BF16),
            pltpu.VMEM((6 * half, width), BF16),
            pltpu.VMEM((2 * TILE, row_count + 6 * half), BF16),
            pltpu.VMEM((2 * TILE, row_count + 6 * half), BF16),
            pltpu.VMEM((3, row_count + 6 * half, TILE), BF16),
            pltpu.VMEM((2, width, TILE), BF16),
            pltpu.VMEM((2, width, TILE), BF16),
            pltpu.VMEM((2, TILE, width), BF16),
            pltpu.VMEM((2, 3, 2 * TILE, TILE), F32),
            pltpu.VMEM((2, half, width), F32),
            pltpu.VMEM((half, width), F32),
            pltpu.VMEM((half, width), F32),
            pltpu.VMEM((width, 768), BF16),
            pltpu.VMEM((half, width), BF16),
            pltpu.VMEM((2, row_count, 512), BF16),
            pltpu.VMEM((2, row_count, 1024), BF16),
            pltpu.VMEM((2, row_count, 1024), BF16),
            pltpu.VMEM((2, row_count, 768), BF16),
            pltpu.VMEM((2, 2, 512, TILE), F32),
            pltpu.VMEM((2, 2, TILE, 768), F32),
            pltpu.VMEM((2, 512, TILE), F32),
            pltpu.VMEM((2, TILE, 768), F32),
            pltpu.VMEM((2, half, 768), F32),
            pltpu.VMEM((half, 1024), F32),
            pltpu.VMEM((2, width), F32),
            pltpu.VMEM((2, width), F32),
            dma((15,)), dma((6,)), dma((2, 3)), dma((3,)), dma((2, 4)),
            dma((2, tiles)), dma((2, tiles)),
            dma((tiles,)), dma((tiles,)), dma((tiles,)), dma((tiles,)),
            dma((2, 2)), dma((2, 2)), dma((2,)), dma((2,)), dma((7,)), dma((7,)), dma((8,)), dma((8,)),
            dma((6,)), dma((6,)), pltpu.VMEM((row_count, TILE), F32),
        ],
        compiler_params=pltpu.CompilerParams(
            collective_id=1, has_side_effects=True, vmem_limit_bytes=64 * 1024 * 1024
        ),
        name="weight_gradients",
    )(
        normed_others, cot_others, normed, cot, act, gg, gu, w_gate, w_up, w_down,
        projected, projected_wide, branch, gain_two, w_query, w_key, w_value, heads, grad_attn, grad_attn_far,
        normed_one, normed_one_far, heads_far, grad_hidden, tokens, gain.reshape(1, width),
    )


def finish_kernel(
    kept, came, down_kept, down_came, out_mine, out_came, proj_mine, proj_came, input_in,
    mixed_in, gains, w_gate, w_up, w_down, w_out, w_query, w_key, w_value, grad_input, mixed,
    gain_one, gain_two,
):
    w_gate[...] = kept[0] + came[0]
    w_up[...] = kept[1] + came[1]
    w_down[...] = down_kept[...] + down_came[...]
    w_out[...] = out_mine[...] + out_came[...]
    queries, keys = w_query.shape[1], w_key.shape[1]
    w_query[...] = proj_mine[:, :queries] + proj_came[:, :queries]
    w_key[...] = proj_mine[:, queries : queries + keys] + proj_came[:, queries : queries + keys]
    w_value[...] = proj_mine[:, queries + keys :] + proj_came[:, queries + keys :]
    grad_input[...] = input_in[...]
    mixed[...] = mixed_in[...]
    total = jnp.sum(gains[...], axis=0)
    gain_one[...] = total[0:1]
    gain_two[...] = total[1:2]


def finish(*parts):
    steps = 4
    kept, down, out, proj, whole, gains = (parts[i] for i in (0, 2, 4, 6, 8, 10))
    rows, units = kept.shape[1:]

    def block(array, lead=()):
        size = array[len(lead) :]
        shape = lead + (size[0] // steps,) + size[1:]
        return pl.BlockSpec(shape, lambda i: (0,) * len(lead) + (i,) + (0,) * (len(size) - 1))

    fixed = lambda shape: pl.BlockSpec(shape, lambda i: (0,) * len(shape))
    outs = [
        (rows, units), (rows, units), down.shape, out.shape,
        (proj.shape[0], 512), (proj.shape[0], 128), (proj.shape[0], 128), whole.shape,
    ]
    return pl.pallas_call(
        finish_kernel,
        grid=(steps,),
        out_shape=[jax.ShapeDtypeStruct(shape, F32) for shape in outs]
        + [
            jax.ShapeDtypeStruct(whole.shape, BF16),
            jax.ShapeDtypeStruct((1, gains.shape[2]), F32),
            jax.ShapeDtypeStruct((1, gains.shape[2]), F32),
        ],
        in_specs=[block(kept.shape, (2,))] * 2
        + [block(part.shape) for part in parts[2:10]]
        + [fixed(gains.shape)],
        out_specs=[block(shape) for shape in outs]
        + [block(whole.shape)] + [fixed((1, gains.shape[2]))] * 2,
        compiler_params=pltpu.CompilerParams(vmem_limit_bytes=64 * 1024 * 1024),
        cost_estimate=pl.CostEstimate(
            flops=2_000_000, bytes_accessed=34_000_000, transcendentals=0
        ),
        name="last_sums",
    )(*parts)


def body(
    tokens,
    segments,
    positions,
    attn_gain,
    w_query,
    key_weight,
    value_weight,
    w_out,
    mlp_gain,
    w_gate,
    w_up,
    w_down,
    cotangent,
):
    groups = lax.axis_size("dp")
    place = lax.axis_index("dp")
    core = lax.axis_index("tensor") % 2
    all_bits = [1 << i for i in range(groups.bit_length() - 1)]
    shared_bits = [bit for bit in (4, 1) if bit < groups]
    split_bits = [bit for bit in all_bits if bit not in shared_bits]

    def blocks(matrix, offsets):
        width = matrix.shape[1] // groups
        return [
            lax.dynamic_slice_in_dim(matrix, (place ^ offset) * width, width, 1)
            for offset in offsets
        ]

    def offsets_of(bits):
        found = [0]
        for bit in bits:
            found = found + [offset + bit for offset in found]
        return found

    def reduced(matrix_of, bits):
        sent = None
        for bit in bits:
            rest = bits[bits.index(bit) + 1 :]
            offsets = offsets_of(rest)
            if sent is None:
                away = matrix_of([offset ^ bit for offset in offsets])
                home = matrix_of(offsets)
            else:
                away = [sent[offset ^ bit] for offset in offsets]
                home = [sent[offset] for offset in offsets]
            came = swap(away, "dp", bit)
            sent = {offset: h + c for offset, h, c in zip(offsets, home, came)}
        return sent[0]

    row_count, width = tokens.shape
    query_width, kv_width = w_query.shape[1], key_weight.shape[1]
    half_dim = HEAD_SIZE // 2
    steps = np.arange(half_dim, dtype=np.float32) * 2.0 / HEAD_SIZE
    frequency = np.tile((500000.0 ** -steps).astype(np.float32), 4)
    (
        normed_one,
        head_outputs,
        _,
        _,
        _,
        normed_one_far,
        heads_far,
        grad_hidden,
        grad_attn,
        projected,
        projected_wide,
        grad_attn_far,
        branch,
        normed_two,
        activation,
        grad_gate_in,
        grad_up_in,
        gain_two_half,
        cotangent_others,
        normed_others,
    ) = middle(
        w_query, key_weight, value_weight, w_out, tokens, cotangent,
        attn_gain, mlp_gain, w_gate, w_up, w_down, segments, positions, frequency,
    )
    (
        kept,
        _,
        came,
        down_kept,
        _,
        down_came,
        down_last,
        out_mine,
        out_came,
        proj_mine,
        proj_came,
        grad_input,
        mixed,
        _,
        _,
        _,
        gains,
    ) = last(
        normed_others, cotangent_others, normed_two, cotangent, activation, grad_gate_in,
        grad_up_in, w_gate, w_up, w_down, projected, projected_wide, branch, gain_two_half, w_query, key_weight,
        value_weight, head_outputs, grad_attn, grad_attn_far, normed_one, normed_one_far,
        heads_far, grad_hidden, tokens, attn_gain,
    )
    pairs = [(i, i ^ 2) for i in range(lax.axis_size("dp"))]
    last_came = lax.ppermute(down_last, "dp", pairs)
    (
        grad_w_gate,
        grad_w_up,
        grad_w_down,
        grad_w_out,
        grad_w_query,
        grad_w_key,
        grad_w_value,
        grad_input,
        mixed,
        grad_attn_gain,
        grad_mlp_gain,
    ) = finish(
        kept, came, down_kept, down_came, out_mine, out_came, proj_mine, proj_came, grad_input,
        mixed, gains,
    )
    done = grad_w_down.shape[0] - LAST * TILE
    grad_w_down = lax.dynamic_update_slice(grad_w_down, down_kept[done:] + last_came, (done, 0))
    grad_attn_gain, grad_mlp_gain = grad_attn_gain[0], grad_mlp_gain[0]
    return (
        mixed,
        grad_input,
        grad_attn_gain,
        grad_w_query,
        grad_w_key,
        grad_w_value,
        grad_w_out,
        grad_mlp_gain,
        grad_w_gate,
        grad_w_up,
        grad_w_down,
    )


def product(left_matrix, right_matrix):
    return jnp.dot(left_matrix, right_matrix, preferred_element_type=F32)


def over_rows(left_matrix, right_matrix):
    return lax.dot_general(
        left_matrix, right_matrix, (((0,), (0,)), ((), ())), preferred_element_type=F32
    )


def against(gradient, weight):
    return lax.dot_general(
        gradient, weight, (((1,), (1,)), ((), ())), preferred_element_type=F32
    )


def narrowed(value):
    return jnp.where(value == value, value, 0.0).astype(BF16)


def swap(value, axis, bit):
    size = lax.axis_size(axis)
    return lax.ppermute(value, axis, [(i, i ^ bit) for i in range(size)])


def half_of(value, which, dim=0):
    size = value.shape[dim] // 2
    return lax.dynamic_slice_in_dim(value, which * size, size, dim)


def joined(mine, other, which):
    first = jnp.where(which == 0, mine, other)
    second = jnp.where(which == 0, other, mine)
    return jnp.concatenate([first, second], axis=0)


def tensor_sum_half(partial, core):
    total = half_of(partial, core) + swap(half_of(partial, 1 - core), "tensor", 1)
    bit = 2
    while bit < lax.axis_size("tensor"):
        total = total + swap(total, "tensor", bit)
        bit *= 2
    return total


def tables(places):
    half_dim = HEAD_SIZE // 2
    frequency = 500000.0 ** (-(jnp.arange(half_dim).astype(F32) * 2.0 / HEAD_SIZE))
    angles = places.astype(F32)[..., None] * frequency
    cosine_lookup = jnp.cos(angles)
    sine_lookup = jnp.sin(angles)
    return (
        jnp.concatenate([cosine_lookup, cosine_lookup], -1),
        jnp.concatenate([sine_lookup, sine_lookup], -1),
    )


def apply_rotary(field, cosine_lookup, sine_lookup):
    half_dim = HEAD_SIZE // 2
    turned = jnp.concatenate([-field[..., half_dim:], field[..., :half_dim]], -1)
    return field * cosine_lookup + turned * sine_lookup


def unrotate(gradient, cosine_lookup, sine_lookup):
    half_dim = HEAD_SIZE // 2
    sined = gradient * sine_lookup
    return gradient * cosine_lookup + jnp.concatenate(
        [sined[..., half_dim:], -sined[..., :half_dim]], -1
    )


def allowed_pairs(segment):
    spots = jnp.arange(segment.shape[0])
    return (spots[:, None] >= spots[None, :]) & (segment[:, None] == segment[None, :])


def scores(query_rotated, key_rotated, segment):
    raw_scores = jnp.einsum(
        "qhgd,khd->hgqk", query_rotated, key_rotated, preferred_element_type=F32
    ) * HEAD_SIZE ** (-0.5)
    return jnp.where(allowed_pairs(segment), raw_scores, MASKED)


def attend_forward(query_rotated, key_rotated, value_seq, segment):
    masked = scores(query_rotated, key_rotated, segment)
    row_peak = jnp.max(masked, axis=-1, keepdims=True)
    log_total = row_peak + jnp.log(jnp.sum(jnp.exp(masked - row_peak), axis=-1, keepdims=True))
    attention_probs = jnp.exp(masked - log_total).astype(BF16)
    combined_heads = jnp.einsum(
        "ojus,sov->uojv", attention_probs, value_seq, preferred_element_type=F32
    )
    return (combined_heads, log_total)


def attend_backward(query_rotated, key_rotated, value_seq, segment, log_total, grad_heads):
    masked = scores(query_rotated, key_rotated, segment)
    attention_probs = jnp.exp(masked - log_total)
    grad_probs = jnp.einsum("qhgd,khd->hgqk", grad_heads, value_seq, preferred_element_type=F32)
    row_sum = jnp.sum(attention_probs * grad_probs, axis=-1, keepdims=True)
    grad_raw = jnp.where(
        allowed_pairs(segment), attention_probs * (grad_probs - row_sum), 0.0
    ).astype(BF16)
    factor = HEAD_SIZE ** (-0.5)
    grad_query_rot = (
        jnp.einsum("ojus,sov->uojv", grad_raw, key_rotated, preferred_element_type=F32) * factor
    )
    grad_key_rot = (
        jnp.einsum("hgqk,qhgd->khd", grad_raw, query_rotated, preferred_element_type=F32) * factor
    )
    grad_value_rot = jnp.einsum(
        "hgqk,qhgd->khd", attention_probs.astype(BF16), grad_heads, preferred_element_type=F32
    )
    return (grad_query_rot, grad_key_rot, grad_value_rot)


def per_sequence(step, *fields):
    results = [step(*[field[s] for field in fields]) for s in range(fields[0].shape[0])]
    return [jnp.stack(parts) for parts in zip(*results)]


def general_body(
    tokens,
    segments,
    positions,
    attn_gain,
    w_query,
    key_weight,
    value_weight,
    w_out,
    mlp_gain,
    w_gate,
    w_up,
    w_down,
    cotangent,
):
    groups = lax.axis_size("dp")
    place = lax.axis_index("dp")
    core = lax.axis_index("tensor") % 2
    all_bits = [1 << i for i in range(groups.bit_length() - 1)]
    shared_bits = [bit for bit in (4, 1) if bit < groups]
    split_bits = [bit for bit in all_bits if bit not in shared_bits]

    def gathered(half):
        parts = [half]
        for bit in shared_bits:
            parts = parts + [swap(part, "dp", bit) for part in parts]
        others = parts[1:]
        twins = [swap(part, "tensor", 1) for part in others]
        return jnp.concatenate([narrowed(part) for part in others + twins], axis=0)

    def blocks(matrix, offsets):
        width = matrix.shape[1] // groups
        return [
            lax.dynamic_slice_in_dim(matrix, (place ^ offset) * width, width, 1)
            for offset in offsets
        ]

    def offsets_of(bits):
        found = [0]
        for bit in bits:
            found = found + [offset + bit for offset in found]
        return found

    def reduced(matrix_of, bits):
        sent = None
        for bit in bits:
            rest = bits[bits.index(bit) + 1 :]
            offsets = offsets_of(rest)
            if sent is None:
                away = matrix_of([offset ^ bit for offset in offsets])
                home = matrix_of(offsets)
            else:
                away = [sent[offset ^ bit] for offset in offsets]
                home = [sent[offset] for offset in offsets]
            came = swap(away, "dp", bit)
            sent = {offset: h + c for offset, h, c in zip(offsets, home, came)}
        return sent[0]

    inputs = tokens.astype(F32)
    row_count, width = inputs.shape
    seq_count, seq_len = segments.shape
    query_heads = w_query.shape[1] // HEAD_SIZE
    kv_heads = key_weight.shape[1] // HEAD_SIZE
    group_size = query_heads // kv_heads
    query_width, kv_width = w_query.shape[1], key_weight.shape[1]

    cotangent_half = half_of(cotangent, core).astype(F32)
    cotangent_others = gathered(cotangent_half)

    scale_one = lax.rsqrt(jnp.mean(inputs * inputs, axis=-1, keepdims=True) + EPSILON)
    normed_one = (inputs * scale_one * attn_gain).astype(BF16)
    cosine_lookup, sine_lookup = tables(positions.reshape(row_count))
    cosine_lookup = cosine_lookup[:, None, :]
    sine_lookup = sine_lookup[:, None, :]
    query_projected = product(normed_one, w_query).reshape(row_count, query_heads, HEAD_SIZE)
    key_projected = product(normed_one, key_weight).reshape(row_count, kv_heads, HEAD_SIZE)
    query_rotated = (
        apply_rotary(query_projected, cosine_lookup, sine_lookup)
        .astype(BF16)
        .reshape(seq_count, seq_len, kv_heads, group_size, HEAD_SIZE)
    )
    key_rotated = (
        apply_rotary(key_projected, cosine_lookup, sine_lookup)
        .astype(BF16)
        .reshape(seq_count, seq_len, kv_heads, HEAD_SIZE)
    )
    value_projected = (
        product(normed_one, value_weight)
        .astype(BF16)
        .reshape(seq_count, seq_len, kv_heads, HEAD_SIZE)
    )
    combined_heads, log_totals = per_sequence(
        attend_forward, query_rotated, key_rotated, value_projected, segments
    )
    head_outputs = combined_heads.reshape(row_count, query_width).astype(BF16)

    inputs_half = half_of(inputs, core)
    hidden = inputs_half + tensor_sum_half(product(head_outputs, w_out), core)
    scale_two = lax.rsqrt(jnp.mean(hidden * hidden, axis=-1, keepdims=True) + EPSILON)
    normed_half = (hidden * scale_two * mlp_gain).astype(BF16)
    normed_sent = normed_half.astype(F32)
    normed_twin = narrowed(swap(normed_sent, "tensor", 1))
    normed_two = joined(normed_half, normed_twin, core)
    normed_others = gathered(normed_sent)

    def feed_forward(normed, incoming):
        gate_proj = product(normed, w_gate)
        up_proj = product(normed, w_up)
        grad_activation = against(incoming, w_down)
        sigmoid_gate = jax.nn.sigmoid(gate_proj)
        swish_gate = gate_proj * sigmoid_gate
        activation = (swish_gate * up_proj).astype(BF16)
        grad_gate_in = (
            grad_activation * up_proj * sigmoid_gate * (1.0 + gate_proj * (1.0 - sigmoid_gate))
        ).astype(BF16)
        grad_up_in = (grad_activation * swish_gate).astype(BF16)
        return activation, grad_gate_in, grad_up_in

    activation, grad_gate_in, grad_up_in = feed_forward(normed_two, cotangent)
    grad_normed_two = tensor_sum_half(
        against(grad_gate_in, w_gate) + against(grad_up_in, w_up), core
    )
    mixed_half = hidden + tensor_sum_half(product(activation, w_down), core)
    mixed = joined(mixed_half.astype(BF16), narrowed(swap(mixed_half, "tensor", 1)), core)

    weighted = grad_normed_two * mlp_gain
    inner_mean = jnp.mean(weighted * hidden, axis=-1, keepdims=True)
    back_two = scale_two * weighted - hidden * (scale_two * scale_two * scale_two) * inner_mean
    gain_two_half = jnp.sum(grad_normed_two * hidden * scale_two, axis=0)
    grad_hidden = cotangent_half + back_two
    attn_half = grad_hidden.astype(BF16)
    attn_twin = narrowed(swap(grad_hidden, "tensor", 1))
    grad_attn = joined(attn_half, attn_twin, core)

    grad_heads = (
        against(grad_attn, w_out)
        .astype(BF16)
        .reshape(seq_count, seq_len, kv_heads, group_size, HEAD_SIZE)
    )
    grad_query_rot, grad_key_rot, grad_value_rot = per_sequence(
        attend_backward,
        query_rotated,
        key_rotated,
        value_projected,
        segments,
        log_totals,
        grad_heads,
    )
    grad_query_in = (
        unrotate(
            grad_query_rot.reshape(row_count, query_heads, HEAD_SIZE), cosine_lookup, sine_lookup
        )
        .reshape(row_count, query_width)
        .astype(BF16)
    )
    grad_key_in = (
        unrotate(grad_key_rot.reshape(row_count, kv_heads, HEAD_SIZE), cosine_lookup, sine_lookup)
        .reshape(row_count, kv_width)
        .astype(BF16)
    )
    grad_value_in = grad_value_rot.reshape(row_count, kv_width).astype(BF16)
    partial_one = (
        against(grad_query_in, w_query)
        + against(grad_key_in, key_weight)
        + against(grad_value_in, value_weight)
    )
    grad_normed_one = tensor_sum_half(partial_one, core)
    scale_one = half_of(scale_one, core)
    weighted = grad_normed_one * attn_gain
    inner_mean = jnp.mean(weighted * inputs_half, axis=-1, keepdims=True)
    back_one = scale_one * weighted - inputs_half * (scale_one * scale_one * scale_one) * inner_mean
    gain_one_half = jnp.sum(grad_normed_one * inputs_half * scale_one, axis=0)
    input_half = grad_hidden + back_one
    grad_input = joined(input_half, swap(input_half, "tensor", 1), core)

    activation_o, grad_gate_o, grad_up_o = feed_forward(normed_others, cotangent_others)

    def rows_of(left, left_others, right, right_others):
        def term(offsets):
            ours = blocks(left, offsets)
            theirs = blocks(left_others, offsets)
            return [
                over_rows(a, right) + over_rows(b, right_others) for a, b in zip(ours, theirs)
            ]

        return reduced(term, split_bits)

    def columns_of(left, left_others, right, right_others):
        def term(offsets):
            ours = blocks(right, offsets)
            theirs = blocks(right_others, offsets)
            return [
                over_rows(left, a) + over_rows(left_others, b) for a, b in zip(ours, theirs)
            ]

        return reduced(term, split_bits)

    grad_w_down = columns_of(activation, activation_o, cotangent, cotangent_others)
    grad_w_gate = rows_of(normed_two, normed_others, grad_gate_in, grad_gate_o)
    grad_w_up = rows_of(normed_two, normed_others, grad_up_in, grad_up_o)

    grad_w_out = reduced(
        lambda offsets: [over_rows(head_outputs, b) for b in blocks(grad_attn, offsets)], all_bits
    )
    projected = jnp.concatenate([grad_query_in, grad_key_in, grad_value_in], axis=1)
    grad_w_proj = reduced(
        lambda offsets: [over_rows(b, projected) for b in blocks(normed_one, offsets)], all_bits
    )
    grad_w_query = grad_w_proj[:, :query_width]
    grad_w_key = grad_w_proj[:, query_width : query_width + kv_width]
    grad_w_value = grad_w_proj[:, query_width + kv_width :]

    gains = jnp.stack([gain_one_half, gain_two_half])
    gains = gains + swap(gains, "tensor", 1)
    gains = reduced(lambda offsets: blocks(gains, offsets), all_bits)
    grad_attn_gain, grad_mlp_gain = gains[0], gains[1]
    return (
        mixed,
        grad_input,
        grad_attn_gain,
        grad_w_query,
        grad_w_key,
        grad_w_value,
        grad_w_out,
        grad_mlp_gain,
        grad_w_gate,
        grad_w_up,
        grad_w_down,
    )


def solution(mesh):
    placed = (
        P("dp", None),
        P("dp", None),
        P("dp", None),
        P(),
        P(None, "tensor"),
        P(None, "tensor"),
        P(None, "tensor"),
        P("tensor", None),
        P(),
        P(None, "tensor"),
        P(None, "tensor"),
        P("tensor", None),
        P("dp", None),
    )
    fits = mesh.shape["dp"] == 8 and mesh.shape["tensor"] == 4
    return jax.shard_map(
        body if fits else general_body,
        mesh=mesh,
        in_specs=placed,
        out_specs=(
            P("dp", None),
            P("dp", None),
            P("dp"),
            P("dp", "tensor"),
            P("dp", "tensor"),
            P("dp", "tensor"),
            P("tensor", "dp"),
            P("dp"),
            P("dp", "tensor"),
            P("dp", "tensor"),
            P("tensor", "dp"),
        ),
        check_vma=False,
    )
```
